32 devices in a mesh: dp: 4 (over z), fsdp: 8 (over y, x, core).
Axes of the slice: x: 2, y: 2, z: 4, core: 2. Of those that a mesh axis runs over, the one named last changes fastest.
Arguments:
- inputs: bfloat16 [32, 1024, 768], P(('dp', 'fsdp')), may hold values from -6 to 6
- cotangent: bfloat16 [32, 1024, 768], P(('dp', 'fsdp')), may hold values from -6 to 6
- weight_in: float32 [768, 3352], P(('dp', 'fsdp')), may hold values from -0.21875 to 0.21875
- weight_out: float32 [768, 1536], P(('dp', 'fsdp')), may hold values from -0.15625 to 0.15625
- small_params: float32 [11336], replicated, may hold values from -7 to 3, as said below
- moment_in: float32 [768, 3352], P(('dp', 'fsdp')), may hold values from -512 to 512
- moment_out: float32 [768, 1536], P(('dp', 'fsdp')), may hold values from -1024 to 1024
- moment_small: float32 [11336], replicated, may hold values from -112 to 112
Outputs:
- block_out: bfloat16 [32, 1024, 768], P(('dp', 'fsdp'))
- input_grad: float32 [32, 1024, 768], P(('dp', 'fsdp'))
- grad_in: float32 [768, 3352], P(('dp', 'fsdp'))
- grad_out: float32 [768, 1536], P(('dp', 'fsdp'))
- grad_small: float32 [11336], replicated
- new_moment_in: float32 [768, 3352], P(('dp', 'fsdp'))
- new_moment_out: float32 [768, 1536], P(('dp', 'fsdp'))
- new_moment_small: float32 [11336], replicated
- new_weight_in: float32 [768, 3352], P(('dp', 'fsdp'))
- new_weight_out: float32 [768, 1536], P(('dp', 'fsdp'))
- new_small: float32 [11336], replicated
The draws below stay inside these ranges and needn't reach their ends.
Inputs may be any that keep to these rules, and one draw needn't show every extreme that they name: `small_params`: norm gain, convolution taps and bias, step bias as inverse softplus of step sizes, log of rates, skip gains and gated norm gain laid end to end.
All inputs are finite; a program needn't handle non-finite values.
Results may differ from the reference program's by a relative error of at most 0.0017.
The reference program's roundings to bfloat16 on the way count: a program that leaves them out, or rounds other values in their place, can miss the bound.
Values may be sent and summed in bfloat16 or wider, within the bound.
A program may use at most 256 MiB of HBM per device.

```python
import math
import jax
import jax.numpy as jnp
from jax import lax

D = 768
HEADS = 24
HEAD_DIM = 64
NSTATE = 128
KCONV = 4
BLOCK = 256
LEN = 1024
ITERS = 5
INNER = 1536
CONVCH = 1792
IN_W = 3352
SMALL = 11336
SEQS = 32
TOKENS = 32768


def draw_small_params(key, part):
    key = jax.random.fold_in(key, 11)
    streams = jax.random.split(key, 7)
    place = jnp.arange(D, dtype=jnp.float32) / D
    norm_gain = (0.5 + 1.5 * place) * jax.random.uniform(streams[0], (D,), jnp.float32, 0.8, 1.2)
    conv_weight = jax.random.uniform(streams[1], (KCONV * CONVCH,), jnp.float32, -0.8, 0.8)
    conv_bias = jax.random.uniform(streams[2], (CONVCH,), jnp.float32, -0.5, 0.5)
    step_size = jnp.exp(jax.random.uniform(streams[3], (HEADS,), jnp.float32, math.log(0.001), math.log(0.1)))
    dt_bias = step_size + jnp.log(-jnp.expm1(-step_size))
    decay_log = jnp.log(jax.random.uniform(streams[4], (HEADS,), jnp.float32, 1.0, 16.0))
    skip_gain = jax.random.uniform(streams[5], (HEADS,), jnp.float32, 0.5, 1.5)
    inner_gain = jax.random.uniform(streams[6], (INNER,), jnp.float32, 0.6, 1.4)
    return jnp.concatenate([norm_gain, conv_weight, conv_bias, dt_bias, decay_log, skip_gain, inner_gain])


def steps_of(stream_key, dims, cuts, smallest, high):
    gain = 1.0
    for axis_at, blocks in cuts:
        steps = jax.random.uniform(jax.random.fold_in(jax.random.fold_in(stream_key, 6), axis_at), (blocks,), jnp.float32, smallest / len(cuts), high / len(cuts))
        gain = gain * jnp.repeat(jnp.exp(steps), dims[axis_at] // blocks).reshape((-1,) + (1,) * (len(dims) - 1 - axis_at))
    return gain


def centred(stream_key, dims, width, bound, pieces=(), kind=jnp.bfloat16):
    values = width * jax.random.normal(stream_key, dims, jnp.float32)
    if pieces:
        values = values * steps_of(stream_key, dims, pieces, -0.22, 0.18)
    return jnp.clip(values, -bound, bound).astype(kind)


def setup_inputs(seed: int = 0) -> dict:
    splits = jax.random.split(jax.random.key(seed), 9)
    return {
        "inputs": centred(splits[0], (SEQS, LEN, D), 1.0, 6.0, ((0, 32),)),
        "cotangent": centred(splits[1], (SEQS, LEN, D), 1.0, 6.0, ((0, 32),)),
        "weight_in": centred(splits[2], (D, IN_W), D ** -0.5, 0.21875, ((0, 32),), jnp.float32),
        "weight_out": centred(splits[3], (D, INNER), INNER ** -0.5, 0.15625, ((0, 32),), jnp.float32),
        "small_params": draw_small_params(jax.random.fold_in(splits[8], 71), 0),
        "moment_in": centred(splits[5], (D, IN_W), (0.5 * TOKENS ** 0.5), 512.0, ((0, 32),), jnp.float32),
        "moment_out": centred(splits[6], (D, INNER), (TOKENS ** 0.5), 1024.0, ((0, 32),), jnp.float32),
        "moment_small": centred(splits[7], (SMALL,), (0.1 * TOKENS ** 0.5), 112.0, (), jnp.float32),
    }


MOMENTUM = 0.95
MATRIX_RATE = 0.15
WEIGHT_DECAY = 0.1
SMALL_RATE = 0.01
EPSILON = 1e-05
COEF_A = 3.4445
COEF_B = -4.775
COEF_C = 2.0315

@jax.custom_vjp
def low(v):
    return lax.optimization_barrier(v.astype(jnp.bfloat16)).astype(jnp.float32)

@jax.custom_vjp
def low_back(v):
    return v

def low_keep(v):
    return (low(v), None)

def low_pass(kept, grad):
    return (grad,)

def back_keep(v):
    return (v, None)

def back_low(kept, grad):
    return (low(grad),)
low.defvjp(low_keep, low_pass)
low_back.defvjp(back_keep, back_low)

def unpack(params):
    offset = 0
    norm_gain = params[offset:offset + D]
    offset += D
    conv_weight = params[offset:offset + KCONV * CONVCH].reshape(KCONV, CONVCH)
    offset += KCONV * CONVCH
    conv_bias = params[offset:offset + CONVCH]
    offset += CONVCH
    dt_bias = params[offset:offset + HEADS]
    offset += HEADS
    decay_log = params[offset:offset + HEADS]
    offset += HEADS
    skip_gain = params[offset:offset + HEADS]
    offset += HEADS
    inner_gain = params[offset:offset + INNER]
    return (norm_gain, conv_weight, conv_bias, dt_bias, decay_log, skip_gain, inner_gain)

def scan_blocks(values, step_sizes, head_rates, in_map, out_map):
    highest = lax.Precision.HIGHEST
    blocks = LEN // BLOCK
    values = values.reshape(blocks, BLOCK, HEADS, HEAD_DIM)
    step_sizes = step_sizes.reshape(blocks, BLOCK, HEADS)
    in_map = in_map.reshape(blocks, BLOCK, NSTATE)
    out_map = out_map.reshape(blocks, BLOCK, NSTATE)
    cumlog = jnp.cumsum(step_sizes * head_rates, axis=1)
    causal = (jnp.arange(BLOCK)[:, None] >= jnp.arange(BLOCK)[None, :])[None, :, :, None]
    log_gaps = cumlog[:, :, None, :] - cumlog[:, None, :, :]
    decay_mat = jnp.where(causal, jnp.exp(jnp.where(causal, log_gaps, 0.0)), 0.0)
    scores = jnp.einsum('ctn,csn->cts', out_map, in_map, precision=highest)
    weights = scores[..., None] * decay_mat * step_sizes[:, None, :, :]
    inside = jnp.einsum('ctsh,cshp->cthp', weights, values, precision=highest)
    to_end = jnp.exp(cumlog[:, -1:, :] - cumlog) * step_sizes
    states = jnp.einsum('csh,cshp,csn->chpn', to_end, values, in_map, precision=highest)
    through = jnp.exp(cumlog[:, -1, :])

    def carry_step(carried, pair):
        factor, addend = pair
        return (factor[:, None, None] * carried + addend, carried)
    _, entering = lax.scan(carry_step, jnp.zeros((HEADS, HEAD_DIM, NSTATE), jnp.float32), (through, states))
    across = jnp.einsum('ctn,chpn->cthp', out_map, entering, precision=highest) * jnp.exp(cumlog)[..., None]
    return (inside + across).reshape(LEN, HEADS, HEAD_DIM)

def block(residual, weight_in, weight_out, params):
    highest = lax.Precision.HIGHEST
    norm_gain, conv_weight, conv_bias, dt_bias, decay_log, skip_gain, inner_gain = unpack(params)
    scaled = residual * lax.rsqrt(lax.optimization_barrier(jnp.mean(residual * residual, axis=-1, keepdims=True)) + EPSILON) * norm_gain
    project = low_back(jnp.dot(low(scaled), weight_in, precision=highest))
    gate_part = project[:, :INNER]
    conv_input = project[:, INNER:INNER + CONVCH]
    step_raw = project[:, INNER + CONVCH:]
    padded = jnp.pad(conv_input, ((KCONV - 1, 0), (0, 0)))
    convolved = conv_bias + jnp.zeros((LEN, CONVCH), jnp.float32)
    for tap_index in range(KCONV):
        convolved = convolved + padded[tap_index:tap_index + LEN] * conv_weight[tap_index]
    convolved = jax.nn.silu(convolved)
    values = convolved[:, :INNER].reshape(LEN, HEADS, HEAD_DIM)
    in_map = convolved[:, INNER:INNER + NSTATE]
    out_map = convolved[:, INNER + NSTATE:]
    step_sizes = jax.nn.softplus(step_raw + dt_bias)
    head_rates = -jnp.exp(decay_log)
    mixer = scan_blocks(values, step_sizes, head_rates, in_map, out_map) + skip_gain[:, None] * values
    gated = mixer.reshape(LEN, INNER) * jax.nn.silu(gate_part)
    normed = gated * lax.rsqrt(lax.optimization_barrier(jnp.mean(gated * gated, axis=-1, keepdims=True)) + EPSILON) * inner_gain
    branch = jnp.dot(low(normed), weight_out.T, precision=highest)
    return residual + branch

def forward(inputs, weight_in, weight_out, params):
    rounded_in = low(weight_in)
    rounded_out = low(weight_out)
    checked = jax.checkpoint(block)

    def one_sequence(sequence):
        return checked(sequence, rounded_in, rounded_out, params)
    return lax.map(one_sequence, inputs)

def orthogonalize(update):
    highest = lax.Precision.HIGHEST
    matrix = update / (jnp.sqrt(jnp.sum(update * update)) + 1e-07)
    for iteration in range(ITERS):
        gram = jnp.dot(matrix, matrix.T, precision=highest)
        once = jnp.dot(gram, matrix, precision=highest)
        twice = jnp.dot(gram, once, precision=highest)
        matrix = COEF_A * matrix + COEF_B * once + COEF_C * twice
    return matrix

def muon(gradient, moment, weight):
    fresh = MOMENTUM * moment + gradient
    direction = orthogonalize(gradient + MOMENTUM * fresh)
    factor = 0.2 * math.sqrt(max(weight.shape))
    return (fresh, weight * (1.0 - MATRIX_RATE * WEIGHT_DECAY) - MATRIX_RATE * factor * direction)

def reference(inputs, cotangent, weight_in, weight_out, small_params, moment_in, moment_out, moment_small):
    outputs, pull = jax.vjp(forward, inputs.astype(jnp.float32), weight_in, weight_out, small_params)
    input_grad, grad_in, grad_out, grad_small = pull(cotangent.astype(jnp.float32))
    new_moment_in, new_weight_in = muon(grad_in, moment_in, weight_in)
    new_moment_out, new_weight_out = muon(grad_out, moment_out, weight_out)
    new_moment_small = MOMENTUM * moment_small + grad_small
    new_small = small_params - SMALL_RATE * new_moment_small
    return (outputs.astype(jnp.bfloat16), input_grad, grad_in, grad_out, grad_small, new_moment_in, new_moment_out, new_moment_small, new_weight_in, new_weight_out, new_small)
```

```python
import math

import jax
import jax.numpy as jnp
from jax import lax
from jax.sharding import PartitionSpec as P

D = 768
HEADS = 24
HEAD_DIM = 64
NSTATE = 128
KCONV = 4
BLOCK = 256
LEN = 1024
ITERS = 5
INNER = 1536
CONVCH = 1792
IN_W = 3352


MOMENTUM = 0.95
MATRIX_RATE = 0.15
WEIGHT_DECAY = 0.1
SMALL_RATE = 0.01
EPSILON = 1e-05
COEF_A = 3.4445
COEF_B = -4.775
COEF_C = 2.0315


def unpack(params):
    offset = 0
    norm_gain = params[offset : offset + D]
    offset += D
    conv_weight = params[offset : offset + KCONV * CONVCH].reshape(KCONV, CONVCH)
    offset += KCONV * CONVCH
    conv_bias = params[offset : offset + CONVCH]
    offset += CONVCH
    dt_bias = params[offset : offset + HEADS]
    offset += HEADS
    decay_log = params[offset : offset + HEADS]
    offset += HEADS
    skip_gain = params[offset : offset + HEADS]
    offset += HEADS
    inner_gain = params[offset : offset + INNER]
    return (norm_gain, conv_weight, conv_bias, dt_bias, decay_log, skip_gain, inner_gain)


def scan_blocks(values, step_sizes, head_rates, in_map, out_map):
    highest = lax.Precision.HIGHEST
    blocks = LEN // BLOCK
    values = values.reshape(blocks, BLOCK, HEADS, HEAD_DIM)
    step_sizes = step_sizes.reshape(blocks, BLOCK, HEADS)
    in_map = in_map.reshape(blocks, BLOCK, NSTATE)
    out_map = out_map.reshape(blocks, BLOCK, NSTATE)
    cumlog = jnp.cumsum(step_sizes * head_rates, axis=1)
    causal = (jnp.arange(BLOCK)[:, None] >= jnp.arange(BLOCK)[None, :])[None, :, :, None]
    log_gaps = cumlog[:, :, None, :] - cumlog[:, None, :, :]
    decay_mat = jnp.where(causal, jnp.exp(jnp.where(causal, log_gaps, 0.0)), 0.0)
    scores = jnp.einsum("ctn,csn->cts", out_map, in_map, precision=highest)
    weights = scores[..., None] * decay_mat * step_sizes[:, None, :, :]
    inside = jnp.einsum("ctsh,cshp->cthp", weights, values, precision=highest)
    to_end = jnp.exp(cumlog[:, -1:, :] - cumlog) * step_sizes
    states = jnp.einsum("csh,cshp,csn->chpn", to_end, values, in_map, precision=highest)
    through = jnp.exp(cumlog[:, -1, :])

    def carry_step(carried, pair):
        factor, addend = pair
        return (factor[:, None, None] * carried + addend, carried)

    _, entering = lax.scan(
        carry_step, jnp.zeros((HEADS, HEAD_DIM, NSTATE), jnp.float32), (through, states)
    )
    across = (
        jnp.einsum("ctn,chpn->cthp", out_map, entering, precision=highest)
        * jnp.exp(cumlog)[..., None]
    )
    return (inside + across).reshape(LEN, HEADS, HEAD_DIM)


def norm_part(residual, params):
    norm_gain = params[:D]
    return (
        residual
        * lax.rsqrt(jnp.mean(residual * residual, axis=-1, keepdims=True) + EPSILON)
        * norm_gain
    )


def mixer_part(project, params):
    norm_gain, conv_weight, conv_bias, dt_bias, decay_log, skip_gain, inner_gain = unpack(params)
    gate_part = project[:, :INNER]
    conv_input = project[:, INNER : INNER + CONVCH]
    step_raw = project[:, INNER + CONVCH :]
    padded = jnp.pad(conv_input, ((KCONV - 1, 0), (0, 0)))
    convolved = conv_bias + jnp.zeros((LEN, CONVCH), jnp.float32)
    for tap_index in range(KCONV):
        convolved = convolved + padded[tap_index : tap_index + LEN] * conv_weight[tap_index]
    convolved = jax.nn.silu(convolved)
    values = convolved[:, :INNER].reshape(LEN, HEADS, HEAD_DIM)
    in_map = convolved[:, INNER : INNER + NSTATE]
    out_map = convolved[:, INNER + NSTATE :]
    step_sizes = jax.nn.softplus(step_raw + dt_bias)
    head_rates = -jnp.exp(decay_log)
    mixer = (
        scan_blocks(values, step_sizes, head_rates, in_map, out_map) + skip_gain[:, None] * values
    )
    gated = mixer.reshape(LEN, INNER) * jax.nn.silu(gate_part)
    return gated * lax.rsqrt(jnp.mean(gated * gated, axis=-1, keepdims=True) + EPSILON) * inner_gain


def forward_one(sequence, whole_in, whole_out, params):
    scaled = norm_part(sequence, params).astype(jnp.bfloat16)
    project = jnp.dot(scaled, whole_in, preferred_element_type=jnp.float32)
    normed = mixer_part(project, params).astype(jnp.bfloat16)
    branch = lax.dot_general(
        normed, whole_out, (((1,), (1,)), ((), ())), preferred_element_type=jnp.float32
    )
    return (sequence + branch, scaled, project, normed)


def backward_one(sequence, back, scaled, project, normed, whole_in, whole_out, params):
    back_low = back.astype(jnp.bfloat16)
    step_out = lax.dot_general(
        normed, back_low, (((0,), (0,)), ((), ())), preferred_element_type=jnp.float32
    )
    normed_grad = jnp.dot(back_low, whole_out, preferred_element_type=jnp.float32)
    _, pull_mixer = jax.vjp(mixer_part, project, params)
    project_grad, params_mixer = pull_mixer(normed_grad)
    project_low = project_grad.astype(jnp.bfloat16)
    step_in = lax.dot_general(
        project_low, scaled, (((0,), (0,)), ((), ())), preferred_element_type=jnp.float32
    )
    scaled_grad = lax.dot_general(
        project_low, whole_in, (((1,), (1,)), ((), ())), preferred_element_type=jnp.float32
    )
    _, pull_norm = jax.vjp(norm_part, sequence, params)
    sequence_grad, params_norm = pull_norm(scaled_grad)
    return (back + sequence_grad, step_in, step_out, params_mixer + params_norm)


def iterate(first_gram, slabs):
    high = lax.Precision.HIGH
    scale = 1.0 / (jnp.sqrt(jnp.trace(first_gram)) + 1e-07)
    gram = first_gram * (scale * scale)
    slabs = slabs * scale
    eye = jnp.eye(gram.shape[0], dtype=jnp.float32)
    for iteration in range(ITERS):
        if iteration == ITERS - 1:
            once = jnp.dot(slabs, gram, precision=high)
            twice = jnp.dot(once, gram, precision=high)
            slabs = COEF_A * slabs + COEF_B * once + COEF_C * twice
        else:
            square = jnp.dot(gram, gram, precision=high)
            factor = COEF_A * eye + COEF_B * gram + COEF_C * square
            slabs = jnp.dot(slabs, factor, precision=high)
            half = jnp.dot(factor, gram, precision=high)
            gram = jnp.dot(half, factor, precision=high)
    return slabs


def to_columns(rows, count):
    pieces = rows.T.reshape(count, -1, rows.shape[0])
    pieces = lax.all_to_all(pieces, ("dp", "fsdp"), split_axis=0, concat_axis=0, tiled=True)
    return pieces.transpose(1, 0, 2).reshape(pieces.shape[1], -1)


def to_rows(columns, count):
    pieces = columns.reshape(columns.shape[0], count, -1).transpose(1, 0, 2)
    pieces = lax.all_to_all(pieces, ("dp", "fsdp"), split_axis=0, concat_axis=0, tiled=True)
    return pieces.reshape(-1, pieces.shape[2]).T


def shards(
    inputs, cotangent, weight_in, weight_out, small_params, moment_in, moment_out, moment_small
):
    axes = ("dp", "fsdp")
    count = lax.axis_size("dp") * lax.axis_size("fsdp")
    me = lax.axis_index("dp") * lax.axis_size("fsdp") + lax.axis_index("fsdp")
    own = weight_in.shape[0]
    whole_in, whole_out = (
        lax.all_gather(weight_in.astype(jnp.bfloat16), axes, axis=0, tiled=True),
        lax.all_gather(weight_out.astype(jnp.bfloat16), axes, axis=0, tiled=True),
    )
    old_gate = to_columns(moment_in[:, :INNER], count)
    old_conv = to_columns(moment_in[:, INNER : INNER + CONVCH], count)
    old_out = to_columns(moment_out, count)
    old_step = lax.all_gather(moment_in[:, INNER + CONVCH :], axes, axis=0, tiled=True).T

    def one(totals, pair):
        sequence, back = pair
        result, scaled, project, normed = forward_one(sequence, whole_in, whole_out, small_params)
        seq_grad, step_in, step_out, step_small = backward_one(
            sequence, back, scaled, project, normed, whole_in, whole_out, small_params
        )
        return (
            (totals[0] + step_in, totals[1] + step_out, totals[2] + step_small),
            (result.astype(jnp.bfloat16), seq_grad),
        )

    start = (
        jnp.zeros((IN_W, D), jnp.float32),
        jnp.zeros((INNER, D), jnp.float32),
        jnp.zeros(small_params.shape, jnp.float32),
    )
    (part_in, part_out, part_small), (outputs, input_grad) = lax.scan(
        one, start, (inputs.astype(jnp.float32), cotangent.astype(jnp.float32))
    )

    def scatter(part):
        return lax.psum_scatter(part, axes, scatter_dimension=0, tiled=True)

    new_out = scatter(part_out)
    new_gate = scatter(part_in[:INNER])
    new_conv = scatter(part_in[INNER : INNER + CONVCH])
    grad_small, new_step = lax.psum((part_small, part_in[INNER + CONVCH :]), axes)

    def push(gradient, moment):
        return gradient + MOMENTUM * (MOMENTUM * moment + gradient)

    push_out = push(new_out, old_out)
    push_in = jnp.concatenate([push(new_gate, old_gate), push(new_conv, old_conv)], axis=0)
    push_step = push(new_step, old_step)

    def gram(slabs):
        return lax.dot_general(
            slabs, slabs, (((0,), (0,)), ((), ())), precision=lax.Precision.HIGH
        )

    gram_in, gram_out = lax.psum((gram(push_in), gram(push_out)), axes)
    ortho_out = iterate(gram_out, push_out)
    ortho_in = iterate(
        gram_in + gram(push_step), jnp.concatenate([push_in, push_step], axis=0)
    )
    gates, convs = INNER // count, CONVCH // count

    def rows_in(gate, conv, step):
        step_own = lax.dynamic_slice_in_dim(step, me * own, own, 1).T
        return jnp.concatenate([to_rows(gate, count), to_rows(conv, count), step_own], axis=1)

    grad_in = rows_in(new_gate, new_conv, new_step)
    grad_out = to_rows(new_out, count)
    direction_in = rows_in(
        ortho_in[:gates], ortho_in[gates : gates + convs], ortho_in[gates + convs :]
    )
    direction_out = to_rows(ortho_out, count)
    new_moment_in = MOMENTUM * moment_in + grad_in
    new_moment_out = MOMENTUM * moment_out + grad_out
    decay = 1.0 - MATRIX_RATE * WEIGHT_DECAY
    new_weight_in = weight_in * decay - MATRIX_RATE * 0.2 * math.sqrt(max(D, IN_W)) * direction_in
    new_weight_out = (
        weight_out * decay - MATRIX_RATE * 0.2 * math.sqrt(max(D, INNER)) * direction_out
    )
    new_moment_small = MOMENTUM * moment_small + grad_small
    new_small = small_params - SMALL_RATE * new_moment_small
    return (
        outputs,
        input_grad,
        grad_in,
        grad_out,
        grad_small,
        new_moment_in,
        new_moment_out,
        new_moment_small,
        new_weight_in,
        new_weight_out,
        new_small,
    )


def solution(mesh):
    return jax.shard_map(
        shards,
        mesh=mesh,
        in_specs=(
            P(("dp", "fsdp"), None, None),
            P(("dp", "fsdp"), None, None),
            P(("dp", "fsdp"), None),
            P(("dp", "fsdp"), None),
            P(),
            P(("dp", "fsdp"), None),
            P(("dp", "fsdp"), None),
            P(),
        ),
        out_specs=(
            P(("dp", "fsdp"), None, None),
            P(("dp", "fsdp"), None, None),
            P(("dp", "fsdp"), None),
            P(("dp", "fsdp"), None),
            P(),
            P(("dp", "fsdp"), None),
            P(("dp", "fsdp"), None),
            P(),
            P(("dp", "fsdp"), None),
            P(("dp", "fsdp"), None),
            P(),
        ),
        check_vma=False,
    )
```

```python
import functools
import math

import jax
import jax.numpy as jnp
from jax import lax
from jax.experimental import pallas as pl
from jax.experimental.pallas import tpu as pltpu
from jax.sharding import PartitionSpec as P

D = 768
HEADS = 24
HEAD_DIM = 64
NSTATE = 128
KCONV = 4
LEN = 1024
ITERS = 5
INNER = 1536
CONVCH = 1792
IN_W = 3352
WIDE = INNER + CONVCH
STEP = 32

MOMENTUM = 0.95
MATRIX_RATE = 0.15
WEIGHT_DECAY = 0.1
SMALL_RATE = 0.01
EPSILON = 1e-05
COEF_A = 3.4445
COEF_B = -4.775
COEF_C = 2.0315

F32 = jnp.float32
BF16 = jnp.bfloat16
CHUNK = 128
STRIP = 256
PER = STRIP // CHUNK
STRIPS = LEN // STRIP
GROUP = 4


def dot(a, b):
    return lax.dot_general(a, b, (((1,), (0,)), ((), ())), preferred_element_type=F32)


def dot_nt(a, b):
    return lax.dot_general(a, b, (((1,), (1,)), ((), ())), preferred_element_type=F32)


def dot_tn(a, b):
    return lax.dot_general(a, b, (((0,), (0,)), ((), ())), preferred_element_type=F32)


def split(v):
    high = v.astype(BF16)
    return high, (v - high.astype(F32)).astype(BF16)


def beside(*parts):
    return jnp.concatenate(parts, axis=1)


def above(*parts):
    return jnp.concatenate(parts, axis=0)


def right_pair(b):
    high, low = split(b)
    return above(beside(high, low), beside(high, jnp.zeros_like(low)))


def three_pass(a, pair):
    high, low = split(a)
    both = dot(beside(high, low), pair)
    half = both.shape[1] // 2
    return both[:, :half] + both[:, half:]


def exact_sum(a, ones):
    high = a.astype(BF16)
    rest = a - high.astype(F32)
    mid = rest.astype(BF16)
    low = (rest - mid.astype(F32)).astype(BF16)
    return dot(beside(high, mid, low), above(ones, ones, ones))


def stack_left(a):
    high, low = split(a)
    return above(beside(high, high), beside(low, jnp.zeros_like(low)))


def fold(rows):
    total = rows[0:8]
    for i in range(1, rows.shape[0] // 8):
        total = total + rows[8 * i : 8 * i + 8]
    return total


def row_sum(rows):
    return jnp.sum(fold(rows), axis=0, keepdims=True)


def upper():
    row = lax.broadcasted_iota(jnp.int32, (CHUNK, CHUNK), 0)
    col = lax.broadcasted_iota(jnp.int32, (CHUNK, CHUNK), 1)
    return col >= row


def softplus(v):
    return jnp.maximum(v, 0.0) + jnp.log1p(jnp.exp(-jnp.abs(v)))


def rates_of(raw, heads_ref, ones):
    steps = softplus(raw + heads_ref[0])
    logs = exact_sum(steps * heads_ref[1], ones)
    last = jnp.broadcast_to(logs[:, CHUNK - 1 : CHUNK], logs.shape)
    columns = above(logs, jnp.zeros((CHUNK - HEADS, CHUNK), F32)).T
    return steps, logs, columns, jnp.exp(logs), jnp.exp(last - logs), jnp.exp(last)


def wide(v):
    return beside(*([v] * PER))


def forward_kernel(
    x_ref, w_in_ref, w_step_ref, w_out_ref, gain_ref, taps_ref, heads_ref, inner_ref,
    out_ref, hb_ref, z_ref, cin_ref, c_ref, raw_ref, y_ref, s_ref, normed_ref, r_ref,
    act, gated, state, tail,
):
    @pl.when(pl.program_id(0) == 0)
    def _():
        state[...] = jnp.zeros_like(state)
        tail[...] = jnp.zeros_like(tail)

    x = x_ref[...].astype(F32)
    scaled = x * lax.rsqrt(jnp.mean(x * x, axis=-1, keepdims=True) + EPSILON) * gain_ref[...]
    hb = scaled.astype(BF16)
    hb_ref[...] = hb
    for i in range(INNER // 256):
        z_ref[256 * i : 256 * i + 256] = dot_nt(w_in_ref[256 * i : 256 * i + 256], hb)
    for i in range(CONVCH // 256):
        start = INNER + 256 * i
        cin_ref[256 * i : 256 * i + 256] = dot_nt(w_in_ref[start : start + 256], hb)
    raw_ref[...] = dot_nt(w_step_ref[...], hb)

    def conv_tile(i, carry):
        rows = pl.ds(pl.multiple_of(i * 64, 64), 64)
        cur = cin_ref[rows, :]
        ext = beside(tail[rows, :], cur)
        total = wide(taps_ref[KCONV, rows, :])
        for k in range(KCONV - 1):
            shifted = pltpu.roll(ext, KCONV - 1 - k, 1)[:, CHUNK:]
            total = total + shifted * wide(taps_ref[k, rows, :])
        total = total + cur * wide(taps_ref[KCONV - 1, rows, :])
        c_ref[rows, :] = total
        act[rows, :] = total * jax.nn.sigmoid(total)
        tail[rows, :] = cur[:, STRIP - CHUNK :]
        return carry

    lax.fori_loop(0, CONVCH // 64, conv_tile, 0)
    causal = upper()
    ones = causal.astype(F32).astype(BF16)

    def chunk(j, carry):
        cols = pl.ds(pl.multiple_of(j * CHUNK, CHUNK), CHUNK)
        steps, logs, columns, grown, to_end, through = rates_of(
            raw_ref[0:HEADS, cols], heads_ref, ones
        )
        in_map = act[INNER : INNER + NSTATE, cols].T
        in_pair = right_pair(in_map)
        out_pair = right_pair(act[INNER + NSTATE :, cols])
        scores = three_pass(in_map, out_pair)
        squares = jnp.zeros((8, CHUNK), F32)
        for g in range(HEADS // GROUP):
            rows = slice(g * GROUP * HEAD_DIM, (g + 1) * GROUP * HEAD_DIM)
            held = state[rows]
            s_ref[j, rows] = held
            across = three_pass(held, out_pair)
            ending, kept = [], []
            for q in range(GROUP):
                h = g * GROUP + q
                mine = slice(h * HEAD_DIM, (h + 1) * HEAD_DIM)
                values = act[mine, cols]
                fed = values * steps[h : h + 1]
                gaps = logs[h : h + 1] - jnp.broadcast_to(columns[:, h : h + 1], (CHUNK, CHUNK))
                weights = scores * jnp.where(causal, jnp.exp(gaps), 0.0)
                both = dot(stack_left(fed), above(*split(weights)))
                y = both[:HEAD_DIM] + both[HEAD_DIM:]
                y = y + across[q * HEAD_DIM : (q + 1) * HEAD_DIM] * grown[h : h + 1]
                y_ref[mine, cols] = y
                gate = z_ref[mine, cols]
                open_ = (y + heads_ref[2][h : h + 1] * values) * (gate * jax.nn.sigmoid(gate))
                gated[mine, cols] = open_
                squares = squares + fold(open_ * open_)
                ending.append(fed * to_end[h : h + 1])
                kept.append(jnp.broadcast_to(through[h : h + 1], (HEAD_DIM, CHUNK)))
            state[rows] = held * above(*kept) + three_pass(above(*ending), in_pair)
        mean = jnp.sum(squares, axis=0, keepdims=True) * (1.0 / INNER)
        r_ref[:, cols] = jnp.broadcast_to(lax.rsqrt(mean + EPSILON), (8, CHUNK))
        return carry

    lax.fori_loop(0, PER, chunk, 0)

    def norm_tile(i, carry):
        rows = pl.ds(pl.multiple_of(i * 64, 64), 64)
        scale = jnp.broadcast_to(r_ref[0:1, :], (64, STRIP))
        normed_ref[rows, :] = (gated[rows, :] * scale * wide(inner_ref[rows, :])).astype(BF16)
        return carry

    lax.fori_loop(0, INNER // 64, norm_tile, 0)
    for i in range(D // 256):
        part = slice(256 * i, 256 * i + 256)
        branch = dot(w_out_ref[part], normed_ref[...]).T
        out_ref[:, part] = (x_ref[:, part].astype(F32) + branch).astype(BF16)


def backward_kernel(
    x_ref, back_ref, w_in_ref, w_step_ref, w_out_ref, gain_ref, taps_ref, heads_ref, inner_ref,
    z_ref, cin_ref, c_ref, raw_ref, y_ref, s_ref, r_ref,
    dx_ref, dproj_ref, dstep_ref, dgain_ref, dtaps_ref, dheads_ref, dinner_ref,
    act, dact, dnormed, dy, dstate, flow, tail, dlogs, vdu_rows,
):
    first = pl.program_id(0) == 0

    @pl.when(first)
    def _():
        dstate[...] = jnp.zeros_like(dstate)
        flow[...] = jnp.zeros_like(flow)
        tail[...] = jnp.zeros_like(tail)
        dgain_ref[...] = jnp.zeros_like(dgain_ref)
        dtaps_ref[...] = jnp.zeros_like(dtaps_ref)
        dheads_ref[...] = jnp.zeros_like(dheads_ref)
        dinner_ref[...] = jnp.zeros_like(dinner_ref)

    back = back_ref[...]
    for i in range(INNER // 256):
        dnormed[256 * i : 256 * i + 256] = dot_nt(w_out_ref[256 * i : 256 * i + 256], back)

    def act_tile(i, carry):
        rows = pl.ds(pl.multiple_of(i * 64, 64), 64)
        c = c_ref[rows, :]
        act[rows, :] = c * jax.nn.sigmoid(c)
        return carry

    lax.fori_loop(0, CONVCH // 64, act_tile, 0)

    def mean_tile(h, total):
        rows = pl.ds(pl.multiple_of(h * HEAD_DIM, HEAD_DIM), HEAD_DIM)
        gate = z_ref[rows, :]
        skip = wide(heads_ref[2, pl.ds(h, 1), :])
        mixed = y_ref[rows, :] + skip * act[rows, :]
        opened = mixed * (gate * jax.nn.sigmoid(gate))
        return total + fold(dnormed[rows, :] * wide(inner_ref[rows, :]) * opened)

    inner_mean = lax.fori_loop(0, HEADS, mean_tile, jnp.zeros((8, STRIP), F32))
    inner_mean = jnp.sum(inner_mean, axis=0, keepdims=True) * (1.0 / INNER)

    def gate_tile(h, carry):
        rows = pl.ds(pl.multiple_of(h * HEAD_DIM, HEAD_DIM), HEAD_DIM)
        gate = z_ref[rows, :]
        skip = wide(heads_ref[2, pl.ds(h, 1), :])
        values = act[rows, :]
        y = y_ref[rows, :]
        mixed = y + skip * values
        sig = jax.nn.sigmoid(gate)
        sil = gate * sig
        opened = mixed * sil
        r = r_ref[0:1, :]
        dn = dnormed[rows, :]
        gained = dn * opened * r
        dinner_ref[rows, :] += gained[:, :CHUNK] + gained[:, CHUNK:]
        dopened = dn * wide(inner_ref[rows, :]) * r - opened * (r * r * r * inner_mean)
        dmixed = dopened * sil
        dy[rows, :] = dmixed
        dproj_ref[rows, :] = (dopened * mixed * (sig * (1.0 + gate * (1.0 - sig)))).astype(BF16)
        skipped = row_sum(dmixed * values)
        dheads_ref[2, pl.ds(h, 1), :] += skipped[:, :CHUNK] + skipped[:, CHUNK:]
        dlogs[pl.ds(h, 1), :] = row_sum(dmixed * y)
        return carry

    lax.fori_loop(0, HEADS, gate_tile, 0)
    causal = upper()
    ones = causal.astype(F32).astype(BF16)
    ones_back = jnp.logical_not(upper()).astype(F32).astype(BF16)
    row = lax.broadcasted_iota(jnp.int32, (CHUNK, CHUNK), 0)
    col = lax.broadcasted_iota(jnp.int32, (CHUNK, CHUNK), 1)
    ones_back = (row >= col).astype(F32).astype(BF16)

    def chunk(step, carry):
        j = PER - 1 - step
        cols = pl.ds(pl.multiple_of(j * CHUNK, CHUNK), CHUNK)
        raw = raw_ref[0:HEADS, cols]
        steps, logs, columns, grown, to_end, through = rates_of(raw, heads_ref, ones)
        in_turned = act[INNER : INNER + NSTATE, cols]
        out_turned = act[INNER + NSTATE :, cols]
        in_map = in_turned.T
        out_map = out_turned.T
        scores = three_pass(in_map, right_pair(out_turned))
        in_pair = right_pair(in_turned)
        out_pair = right_pair(out_map)
        dscores = jnp.zeros((CHUNK, CHUNK), F32)
        din = jnp.zeros((NSTATE, CHUNK), F32)
        dout = jnp.zeros((NSTATE, CHUNK), F32)
        for g in range(HEADS // GROUP):
            rows = slice(g * GROUP * HEAD_DIM, (g + 1) * GROUP * HEAD_DIM)
            leaving = dstate[rows]
            entering = s_ref[j, rows]
            from_state = three_pass(leaving, in_pair)
            ending, growing, kept = [], [], []
            for q in range(GROUP):
                h = g * GROUP + q
                mine = slice(h * HEAD_DIM, (h + 1) * HEAD_DIM)
                values = act[mine, cols]
                fed = values * steps[h : h + 1]
                dys = dy[mine, cols]
                gaps = logs[h : h + 1] - jnp.broadcast_to(columns[:, h : h + 1], (CHUNK, CHUNK))
                decay = jnp.where(causal, jnp.exp(gaps), 0.0)
                weights = scores * decay
                both = dot_nt(stack_left(dys), beside(*split(weights)))
                du = both[:HEAD_DIM] + both[HEAD_DIM:]
                du = du + from_state[q * HEAD_DIM : (q + 1) * HEAD_DIM] * to_end[h : h + 1]
                fed_high, fed_low = split(fed)
                dy_high, dy_low = split(dys)
                dweights = dot_tn(
                    above(fed_high, fed_low, fed_high), above(dy_high, dy_high, dy_low)
                )
                dscores = dscores + dweights * decay
                vdu_rows[h : h + 1, :] = row_sum(values * du)
                dact[mine, cols] = du * steps[h : h + 1] + heads_ref[2][h : h + 1] * dys
                ending.append(fed * to_end[h : h + 1])
                growing.append(dys * grown[h : h + 1])
                kept.append(jnp.broadcast_to(through[h : h + 1], (HEAD_DIM, CHUNK)))
            ending = above(*ending)
            growing = above(*growing)
            end_high, end_low = split(ending)
            grow_high, grow_low = split(growing)
            leave_high, leave_low = split(leaving)
            enter_high, enter_low = split(entering)
            din = din + dot_tn(
                above(leave_high, leave_low, leave_high), above(end_high, end_high, end_low)
            )
            dout = dout + dot_tn(
                above(enter_high, enter_low, enter_high), above(grow_high, grow_high, grow_low)
            )
            arrived = leaving * above(*kept) + three_pass(growing, out_pair)
            dstate[rows] = arrived
            meet = arrived * entering
            for q in range(GROUP):
                h = g * GROUP + q
                dheads_ref[3, h : h + 1, :] = row_sum(meet[q * HEAD_DIM : (q + 1) * HEAD_DIM])
        vdu = vdu_rows[...]
        dlog = dlogs[:, cols] - steps * vdu
        drate = exact_sum(dlog, ones_back) + flow[...]
        flow[...] = jnp.broadcast_to(
            jnp.sum(dheads_ref[3], axis=1, keepdims=True), (HEADS, CHUNK)
        )
        dsteps = vdu + heads_ref[1] * drate
        draw = dsteps * jax.nn.sigmoid(raw + heads_ref[0])
        dheads_ref[0] += draw
        dheads_ref[1] += drate * steps * heads_ref[1]
        dstep_ref[:, cols] = above(draw, jnp.zeros((STEP - HEADS, CHUNK), F32)).astype(BF16)
        score_high, score_low = split(dscores)
        both = dot_nt(stack_left(out_turned), beside(score_high, score_low))
        dact[INNER : INNER + NSTATE, cols] = din + both[:NSTATE] + both[NSTATE:]
        both = dot(stack_left(in_turned), above(score_high, score_low))
        dact[INNER + NSTATE :, cols] = dout + both[:NSTATE] + both[NSTATE:]
        return carry

    lax.fori_loop(0, PER, chunk, 0)

    def conv_tile(i, carry):
        rows = pl.ds(pl.multiple_of(i * 64, 64), 64)
        c = c_ref[rows, :]
        sig = jax.nn.sigmoid(c)
        dpre = dact[rows, :] * (sig * (1.0 + c * (1.0 - sig)))
        cin = cin_ref[rows, :]
        ext = beside(dpre, tail[rows, :])
        dcin = dpre * wide(taps_ref[KCONV - 1, rows, :])
        grad = cin * dpre
        dtaps_ref[KCONV - 1, rows, :] += grad[:, :CHUNK] + grad[:, CHUNK:]
        dtaps_ref[KCONV, rows, :] += dpre[:, :CHUNK] + dpre[:, CHUNK:]
        for k in range(KCONV - 1):
            ahead = KCONV - 1 - k
            shifted = pltpu.roll(ext, STRIP + CHUNK - ahead, 1)[:, :STRIP]
            dcin = dcin + shifted * wide(taps_ref[k, rows, :])
            grad = cin * shifted
            dtaps_ref[k, rows, :] += grad[:, :CHUNK] + grad[:, CHUNK:]
        tail[rows, :] = dpre[:, :CHUNK]
        out_rows = pl.ds(pl.multiple_of(INNER + i * 64, 64), 64)
        dproj_ref[out_rows, :] = dcin.astype(BF16)
        return carry

    lax.fori_loop(0, CONVCH // 64, conv_tile, 0)
    x = x_ref[...].astype(F32)
    r = lax.rsqrt(jnp.mean(x * x, axis=-1, keepdims=True) + EPSILON)
    parts = []
    for i in range(D // 256):
        part = slice(256 * i, 256 * i + 256)
        parts.append(
            (dot(w_in_ref[part], dproj_ref[...]) + dot(w_step_ref[part], dstep_ref[...])).T
        )
    dscaled = beside(*parts)
    plain = x * r
    dgain_ref[...] += fold(dscaled * plain)
    gained = dscaled * gain_ref[...]
    inner = jnp.mean(gained * plain, axis=-1, keepdims=True)
    dx_ref[...] = back.astype(F32) + (gained - plain * inner) * r


def whole(shape):
    return pl.BlockSpec(shape, lambda i: (0,) * len(shape), pipeline_mode=pl.Buffered(1))


def strip_rows(width):
    return pl.BlockSpec((STRIP, width), lambda i: (i, 0))


def strip_cols(height):
    return pl.BlockSpec((height, STRIP), lambda i: (0, i))


def shape(*dims, dtype=F32):
    return jax.ShapeDtypeStruct(dims, dtype)


def forward_call(x, w_in_t, w_step_t, w_out, gain, taps, heads, inner):
    return pl.pallas_call(
        forward_kernel,
        grid=(STRIPS,),
        in_specs=[
            strip_rows(D), whole((WIDE, D)), whole((STEP, D)), whole((D, INNER)), whole((1, D)),
            whole((KCONV + 1, CONVCH, CHUNK)), whole((3, HEADS, CHUNK)), whole((INNER, CHUNK)),
        ],
        out_specs=[
            strip_rows(D), strip_rows(D), strip_cols(INNER), strip_cols(CONVCH),
            strip_cols(CONVCH), strip_cols(STEP), strip_cols(INNER),
            pl.BlockSpec((PER, INNER, NSTATE), lambda i: (i, 0, 0)), strip_cols(INNER),
            strip_cols(8),
        ],
        out_shape=[
            shape(LEN, D, dtype=BF16), shape(LEN, D, dtype=BF16), shape(INNER, LEN),
            shape(CONVCH, LEN), shape(CONVCH, LEN), shape(STEP, LEN), shape(INNER, LEN),
            shape(LEN // CHUNK, INNER, NSTATE), shape(INNER, LEN, dtype=BF16), shape(8, LEN),
        ],
        scratch_shapes=[
            pltpu.VMEM((CONVCH, STRIP), F32), pltpu.VMEM((INNER, STRIP), F32),
            pltpu.VMEM((INNER, NSTATE), F32), pltpu.VMEM((CONVCH, CHUNK), F32),
        ],
        compiler_params=pltpu.CompilerParams(vmem_limit_bytes=56 * 2**20),
        name="mixer_forward",
    )(x, w_in_t, w_step_t, w_out, gain, taps, heads, inner)


def backward_call(x, back, w_in, w_step, w_out_t, gain, taps, heads, inner, kept):
    last = STRIPS - 1

    def rows(width):
        return pl.BlockSpec((STRIP, width), lambda i: (last - i, 0))

    def cols(height):
        return pl.BlockSpec((height, STRIP), lambda i: (0, last - i))

    z, cin, c, raw, y, states, r = kept
    return pl.pallas_call(
        backward_kernel,
        grid=(STRIPS,),
        in_specs=[
            rows(D), rows(D), whole((D, WIDE)), whole((D, STEP)), whole((INNER, D)),
            whole((1, D)), whole((KCONV + 1, CONVCH, CHUNK)), whole((3, HEADS, CHUNK)),
            whole((INNER, CHUNK)), cols(INNER), cols(CONVCH), cols(CONVCH), cols(STEP),
            cols(INNER), pl.BlockSpec((PER, INNER, NSTATE), lambda i: (last - i, 0, 0)), cols(8),
        ],
        out_specs=[
            rows(D), cols(WIDE), cols(STEP), whole((8, D)), whole((KCONV + 1, CONVCH, CHUNK)),
            whole((4, HEADS, CHUNK)), whole((INNER, CHUNK)),
        ],
        out_shape=[
            shape(LEN, D), shape(WIDE, LEN, dtype=BF16), shape(STEP, LEN, dtype=BF16),
            shape(8, D), shape(KCONV + 1, CONVCH, CHUNK), shape(4, HEADS, CHUNK),
            shape(INNER, CHUNK),
        ],
        scratch_shapes=[
            pltpu.VMEM((CONVCH, STRIP), F32), pltpu.VMEM((CONVCH, STRIP), F32),
            pltpu.VMEM((INNER, STRIP), F32), pltpu.VMEM((INNER, STRIP), F32),
            pltpu.VMEM((INNER, NSTATE), F32), pltpu.VMEM((HEADS, CHUNK), F32),
            pltpu.VMEM((CONVCH, CHUNK), F32), pltpu.VMEM((HEADS, STRIP), F32),
            pltpu.VMEM((HEADS, CHUNK), F32),
        ],
        compiler_params=pltpu.CompilerParams(vmem_limit_bytes=60 * 2**20),
        name="mixer_backward",
    )(x, back, w_in, w_step, w_out_t, gain, taps, heads, inner, z, cin, c, raw, y, states, r)


def lanes(vector):
    return jnp.broadcast_to(vector[..., None], vector.shape + (CHUNK,))


def parameters(params):
    gain = params[:D].reshape(1, D)
    at = D
    taps = lanes(params[at : at + (KCONV + 1) * CONVCH].reshape(KCONV + 1, CONVCH))
    at += (KCONV + 1) * CONVCH
    heads = params[at : at + 3 * HEADS].reshape(3, HEADS)
    heads = lanes(jnp.stack([heads[0], -jnp.exp(heads[1]), heads[2]]))
    inner = lanes(params[at + 3 * HEADS :])
    return gain, taps, heads, inner


def block_and_gradients(x, back, whole_in, whole_out, params):
    gain, taps, heads, inner = parameters(params)
    w_in = whole_in[:, :WIDE]
    w_step = jnp.pad(whole_in[:, WIDE:], ((0, 0), (0, STEP - HEADS)))
    out, hb, z, cin, c, raw, y, states, normed, r = forward_call(
        x, w_in.T, w_step.T, whole_out, gain, taps, heads, inner
    )
    dx, dproj, dstep, dgain, dtaps, dheads, dinner = backward_call(
        x, back, w_in, w_step, whole_out.T, gain, taps, heads, inner,
        (z, cin, c, raw, y, states, r),
    )
    grad_out = dot(normed, back)
    grad_in = dot(dproj, hb)
    grad_step = dot(dstep, hb)[:HEADS]
    small = jnp.concatenate(
        [
            jnp.sum(dgain, axis=0),
            jnp.sum(dtaps, axis=-1).reshape(-1),
            jnp.sum(dheads[:3], axis=-1).reshape(-1),
            jnp.sum(dinner, axis=-1),
        ]
    )
    return out, dx, grad_in, grad_step, grad_out, small


def iterate(first_gram, slabs):
    high = lax.Precision.HIGH
    scale = 1.0 / (jnp.sqrt(jnp.trace(first_gram)) + 1e-07)
    gram = first_gram * (scale * scale)
    slabs = slabs * scale
    eye = jnp.eye(gram.shape[0], dtype=jnp.float32)
    for iteration in range(ITERS):
        if iteration == ITERS - 1:
            once = jnp.dot(slabs, gram, precision=high)
            twice = jnp.dot(once, gram, precision=high)
            slabs = COEF_A * slabs + COEF_B * once + COEF_C * twice
        else:
            square = jnp.dot(gram, gram, precision=high)
            factor = COEF_A * eye + COEF_B * gram + COEF_C * square
            slabs = jnp.dot(slabs, factor, precision=high)
            half = jnp.dot(factor, gram, precision=high)
            gram = jnp.dot(half, factor, precision=high)
    return slabs


def to_columns(rows, count):
    pieces = rows.T.reshape(count, -1, rows.shape[0])
    pieces = lax.all_to_all(pieces, ("dp", "fsdp"), split_axis=0, concat_axis=0, tiled=True)
    return pieces.transpose(1, 0, 2).reshape(pieces.shape[1], -1)


def to_rows(columns, count):
    pieces = columns.reshape(columns.shape[0], count, -1).transpose(1, 0, 2)
    pieces = lax.all_to_all(pieces, ("dp", "fsdp"), split_axis=0, concat_axis=0, tiled=True)
    return pieces.reshape(-1, pieces.shape[2]).T


def shards(
    inputs, cotangent, weight_in, weight_out, small_params, moment_in, moment_out, moment_small
):
    axes = ("dp", "fsdp")
    count = lax.axis_size("dp") * lax.axis_size("fsdp")
    me = lax.axis_index("dp") * lax.axis_size("fsdp") + lax.axis_index("fsdp")
    own = weight_in.shape[0]
    whole_in, whole_out = (
        lax.all_gather(weight_in.astype(jnp.bfloat16), axes, axis=0, tiled=True),
        lax.all_gather(weight_out.astype(jnp.bfloat16), axes, axis=0, tiled=True),
    )
    old_gate = to_columns(moment_in[:, :INNER], count)
    old_conv = to_columns(moment_in[:, INNER : INNER + CONVCH], count)
    old_out = to_columns(moment_out, count)
    old_step = lax.all_gather(moment_in[:, INNER + CONVCH :], axes, axis=0, tiled=True).T
    output, dx, part_in, part_step, part_out, part_small = block_and_gradients(
        inputs[0], cotangent[0], whole_in, whole_out, small_params
    )
    outputs, input_grad = output[None], dx[None]

    def scatter(part):
        return lax.psum_scatter(part, axes, scatter_dimension=0, tiled=True)

    new_out = scatter(part_out)
    new_gate = scatter(part_in[:INNER])
    new_conv = scatter(part_in[INNER:])
    grad_small, new_step = lax.psum((part_small, part_step), axes)

    def push(gradient, moment):
        return gradient + MOMENTUM * (MOMENTUM * moment + gradient)

    push_out = push(new_out, old_out)
    push_in = jnp.concatenate([push(new_gate, old_gate), push(new_conv, old_conv)], axis=0)
    push_step = push(new_step, old_step)

    def gram(slabs):
        return lax.dot_general(
            slabs, slabs, (((0,), (0,)), ((), ())), precision=lax.Precision.HIGH
        )

    gram_in, gram_out = lax.psum((gram(push_in), gram(push_out)), axes)
    ortho_out = iterate(gram_out, push_out)
    ortho_in = iterate(
        gram_in + gram(push_step), jnp.concatenate([push_in, push_step], axis=0)
    )
    gates, convs = INNER // count, CONVCH // count

    def rows_in(gate, conv, step):
        step_own = lax.dynamic_slice_in_dim(step, me * own, own, 1).T
        return jnp.concatenate([to_rows(gate, count), to_rows(conv, count), step_own], axis=1)

    grad_in = rows_in(new_gate, new_conv, new_step)
    grad_out = to_rows(new_out, count)
    direction_in = rows_in(
        ortho_in[:gates], ortho_in[gates : gates + convs], ortho_in[gates + convs :]
    )
    direction_out = to_rows(ortho_out, count)
    new_moment_in = MOMENTUM * moment_in + grad_in
    new_moment_out = MOMENTUM * moment_out + grad_out
    decay = 1.0 - MATRIX_RATE * WEIGHT_DECAY
    new_weight_in = weight_in * decay - MATRIX_RATE * 0.2 * math.sqrt(max(D, IN_W)) * direction_in
    new_weight_out = (
        weight_out * decay - MATRIX_RATE * 0.2 * math.sqrt(max(D, INNER)) * direction_out
    )
    new_moment_small = MOMENTUM * moment_small + grad_small
    new_small = small_params - SMALL_RATE * new_moment_small
    return (
        outputs,
        input_grad,
        grad_in,
        grad_out,
        grad_small,
        new_moment_in,
        new_moment_out,
        new_moment_small,
        new_weight_in,
        new_weight_out,
        new_small,
    )


def solution(mesh):
    return jax.shard_map(
        shards,
        mesh=mesh,
        in_specs=(
            P(("dp", "fsdp"), None, None),
            P(("dp", "fsdp"), None, None),
            P(("dp", "fsdp"), None),
            P(("dp", "fsdp"), None),
            P(),
            P(("dp", "fsdp"), None),
            P(("dp", "fsdp"), None),
            P(),
        ),
        out_specs=(
            P(("dp", "fsdp"), None, None),
            P(("dp", "fsdp"), None, None),
            P(("dp", "fsdp"), None),
            P(("dp", "fsdp"), None),
            P(),
            P(("dp", "fsdp"), None),
            P(("dp", "fsdp"), None),
            P(),
            P(("dp", "fsdp"), None),
            P(("dp", "fsdp"), None),
            P(),
        ),
        check_vma=False,
    )
```

```python
import functools
import math

import jax
import jax.numpy as jnp
from jax import lax
from jax.experimental import pallas as pl
from jax.experimental.pallas import tpu as pltpu
from jax.sharding import PartitionSpec as P

D = 768
HEADS = 24
HEAD_DIM = 64
NSTATE = 128
KCONV = 4
LEN = 1024
ITERS = 5
INNER = 1536
CONVCH = 1792
IN_W = 3352
WIDE = INNER + CONVCH
STEP = 32

MOMENTUM = 0.95
MATRIX_RATE = 0.15
WEIGHT_DECAY = 0.1
SMALL_RATE = 0.01
EPSILON = 1e-05
COEF_A = 3.4445
COEF_B = -4.775
COEF_C = 2.0315

F32 = jnp.float32
BF16 = jnp.bfloat16
CHUNK = 128
STRIP = 256
PER = STRIP // CHUNK
STRIPS = LEN // STRIP
GROUP = 4


def dot(a, b):
    return lax.dot_general(a, b, (((1,), (0,)), ((), ())), preferred_element_type=F32)


def dot_nt(a, b):
    return lax.dot_general(a, b, (((1,), (1,)), ((), ())), preferred_element_type=F32)


def dot_tn(a, b):
    return lax.dot_general(a, b, (((0,), (0,)), ((), ())), preferred_element_type=F32)


def split(v):
    high = v.astype(BF16)
    return high, (v - high.astype(F32)).astype(BF16)


def beside(*parts):
    return jnp.concatenate(parts, axis=1)


def above(*parts):
    return jnp.concatenate(parts, axis=0)


def right_pair(b):
    high, low = split(b)
    return above(beside(high, low), beside(high, jnp.zeros_like(low)))


def three_pass(a, pair):
    high, low = split(a)
    both = dot(beside(high, low), pair)
    half = both.shape[1] // 2
    return both[:, :half] + both[:, half:]


def exact_sum(a, ones):
    high = a.astype(BF16)
    rest = a - high.astype(F32)
    mid = rest.astype(BF16)
    low = (rest - mid.astype(F32)).astype(BF16)
    return dot(beside(high, mid, low), above(ones, ones, ones))


def stack_left(a):
    high, low = split(a)
    return above(beside(high, high), beside(low, jnp.zeros_like(low)))


def fold(rows):
    total = rows[0:8]
    for i in range(1, rows.shape[0] // 8):
        total = total + rows[8 * i : 8 * i + 8]
    return total


def row_sum(rows):
    return jnp.sum(fold(rows), axis=0, keepdims=True)


def upper():
    row = lax.broadcasted_iota(jnp.int32, (CHUNK, CHUNK), 0)
    col = lax.broadcasted_iota(jnp.int32, (CHUNK, CHUNK), 1)
    return col >= row


def softplus(v):
    return jnp.maximum(v, 0.0) + jnp.log1p(jnp.exp(-jnp.abs(v)))


def rates_of(raw, heads_ref, ones):
    steps = softplus(raw + heads_ref[0])
    logs = exact_sum(steps * heads_ref[1], ones)
    last = jnp.broadcast_to(logs[:, CHUNK - 1 : CHUNK], logs.shape)
    columns = above(logs, jnp.zeros((CHUNK - HEADS, CHUNK), F32)).T
    return steps, logs, columns, jnp.exp(logs), jnp.exp(last - logs), jnp.exp(last)


def wide(v):
    return beside(*([v] * PER))


def forward_kernel(
    x_ref, w_in_ref, w_step_ref, w_out_ref, gain_ref, taps_ref, heads_ref, inner_ref,
    out_ref, hb_ref, z_ref, cin_ref, c_ref, raw_ref, y_ref, s_ref, normed_ref, r_ref,
    act, gated, state, tail,
):
    @pl.when(pl.program_id(0) == 0)
    def _():
        state[...] = jnp.zeros_like(state)
        tail[...] = jnp.zeros_like(tail)

    x = x_ref[...].astype(F32)
    scaled = x * lax.rsqrt(jnp.mean(x * x, axis=-1, keepdims=True) + EPSILON) * gain_ref[...]
    hb = scaled.astype(BF16)
    hb_ref[...] = hb
    for i in range(INNER // 256):
        z_ref[256 * i : 256 * i + 256] = dot_nt(w_in_ref[256 * i : 256 * i + 256], hb)
    for i in range(CONVCH // 256):
        start = INNER + 256 * i
        cin_ref[256 * i : 256 * i + 256] = dot_nt(w_in_ref[start : start + 256], hb)
    raw_ref[...] = dot_nt(w_step_ref[...], hb)

    def conv_tile(i, carry):
        rows = pl.ds(pl.multiple_of(i * 64, 64), 64)
        cur = cin_ref[rows, :]
        ext = beside(tail[rows, :], cur)
        total = wide(taps_ref[KCONV, rows, :])
        for k in range(KCONV - 1):
            shifted = pltpu.roll(ext, KCONV - 1 - k, 1)[:, CHUNK:]
            total = total + shifted * wide(taps_ref[k, rows, :])
        total = total + cur * wide(taps_ref[KCONV - 1, rows, :])
        c_ref[rows, :] = total
        act[rows, :] = total * jax.nn.sigmoid(total)
        tail[rows, :] = cur[:, STRIP - CHUNK :]
        return carry

    lax.fori_loop(0, CONVCH // 64, conv_tile, 0)
    causal = upper()
    ones = causal.astype(F32).astype(BF16)

    def chunk(j, carry):
        cols = pl.ds(pl.multiple_of(j * CHUNK, CHUNK), CHUNK)
        steps, logs, columns, grown, to_end, through = rates_of(
            raw_ref[0:HEADS, cols], heads_ref, ones
        )
        in_map = act[INNER : INNER + NSTATE, cols].T
        in_pair = right_pair(in_map)
        out_pair = right_pair(act[INNER + NSTATE :, cols])
        scores = three_pass(in_map, out_pair)
        squares = jnp.zeros((8, CHUNK), F32)
        for g in range(HEADS // GROUP):
            rows = slice(g * GROUP * HEAD_DIM, (g + 1) * GROUP * HEAD_DIM)
            held = state[rows]
            s_ref[j, rows] = held
            across = three_pass(held, out_pair)
            ending, kept = [], []
            for q in range(GROUP):
                h = g * GROUP + q
                mine = slice(h * HEAD_DIM, (h + 1) * HEAD_DIM)
                values = act[mine, cols]
                fed = values * steps[h : h + 1]
                gaps = logs[h : h + 1] - jnp.broadcast_to(columns[:, h : h + 1], (CHUNK, CHUNK))
                weights = scores * jnp.where(causal, jnp.exp(gaps), 0.0)
                both = dot(stack_left(fed), above(*split(weights)))
                y = both[:HEAD_DIM] + both[HEAD_DIM:]
                y = y + across[q * HEAD_DIM : (q + 1) * HEAD_DIM] * grown[h : h + 1]
                y_ref[mine, cols] = y
                gate = z_ref[mine, cols]
                open_ = (y + heads_ref[2][h : h + 1] * values) * (gate * jax.nn.sigmoid(gate))
                gated[mine, cols] = open_
                squares = squares + fold(open_ * open_)
                ending.append(fed * to_end[h : h + 1])
                kept.append(jnp.broadcast_to(through[h : h + 1], (HEAD_DIM, CHUNK)))
            state[rows] = held * above(*kept) + three_pass(above(*ending), in_pair)
        mean = jnp.sum(squares, axis=0, keepdims=True) * (1.0 / INNER)
        r_ref[:, cols] = jnp.broadcast_to(lax.rsqrt(mean + EPSILON), (8, CHUNK))
        return carry

    lax.fori_loop(0, PER, chunk, 0)

    def norm_tile(i, carry):
        rows = pl.ds(pl.multiple_of(i * 64, 64), 64)
        scale = jnp.broadcast_to(r_ref[0:1, :], (64, STRIP))
        normed_ref[rows, :] = (gated[rows, :] * scale * wide(inner_ref[rows, :])).astype(BF16)
        return carry

    lax.fori_loop(0, INNER // 64, norm_tile, 0)
    for i in range(D // 256):
        part = slice(256 * i, 256 * i + 256)
        branch = dot(w_out_ref[part], normed_ref[...]).T
        out_ref[:, part] = (x_ref[:, part].astype(F32) + branch).astype(BF16)


def backward_kernel(
    x_ref, back_ref, w_in_ref, w_step_ref, w_out_ref, gain_ref, taps_ref, heads_ref, inner_ref,
    z_ref, cin_ref, c_ref, raw_ref, y_ref, s_ref, r_ref,
    dx_ref, dgate_ref, dconv_ref, dstep_ref, dgain_ref, dtaps_ref, dheads_ref, dinner_ref,
    act, dact, dnormed, dy, dstate, flow, tail, dlogs, vdu_rows,
):
    first = pl.program_id(0) == 0

    @pl.when(first)
    def _():
        dstate[...] = jnp.zeros_like(dstate)
        flow[...] = jnp.zeros_like(flow)
        tail[...] = jnp.zeros_like(tail)
        dgain_ref[...] = jnp.zeros_like(dgain_ref)
        dtaps_ref[...] = jnp.zeros_like(dtaps_ref)
        dheads_ref[...] = jnp.zeros_like(dheads_ref)
        dinner_ref[...] = jnp.zeros_like(dinner_ref)

    back = back_ref[...]
    for i in range(INNER // 256):
        dnormed[256 * i : 256 * i + 256] = dot_nt(w_out_ref[256 * i : 256 * i + 256], back)

    def act_tile(i, carry):
        rows = pl.ds(pl.multiple_of(i * 64, 64), 64)
        c = c_ref[rows, :]
        act[rows, :] = c * jax.nn.sigmoid(c)
        return carry

    lax.fori_loop(0, CONVCH // 64, act_tile, 0)

    def mean_tile(h, total):
        rows = pl.ds(pl.multiple_of(h * HEAD_DIM, HEAD_DIM), HEAD_DIM)
        gate = z_ref[rows, :]
        skip = wide(heads_ref[2, pl.ds(h, 1), :])
        mixed = y_ref[rows, :] + skip * act[rows, :]
        opened = mixed * (gate * jax.nn.sigmoid(gate))
        return total + fold(dnormed[rows, :] * wide(inner_ref[rows, :]) * opened)

    inner_mean = lax.fori_loop(0, HEADS, mean_tile, jnp.zeros((8, STRIP), F32))
    inner_mean = jnp.sum(inner_mean, axis=0, keepdims=True) * (1.0 / INNER)

    def gate_tile(h, carry):
        rows = pl.ds(pl.multiple_of(h * HEAD_DIM, HEAD_DIM), HEAD_DIM)
        gate = z_ref[rows, :]
        skip = wide(heads_ref[2, pl.ds(h, 1), :])
        values = act[rows, :]
        y = y_ref[rows, :]
        mixed = y + skip * values
        sig = jax.nn.sigmoid(gate)
        sil = gate * sig
        opened = mixed * sil
        r = r_ref[0:1, :]
        dn = dnormed[rows, :]
        gained = dn * opened * r
        dinner_ref[rows, :] += gained[:, :CHUNK] + gained[:, CHUNK:]
        dopened = dn * wide(inner_ref[rows, :]) * r - opened * (r * r * r * inner_mean)
        dmixed = dopened * sil
        dy[rows, :] = dmixed
        dgate_ref[rows, :] = (dopened * mixed * (sig * (1.0 + gate * (1.0 - sig)))).astype(BF16)
        skipped = row_sum(dmixed * values)
        dheads_ref[2, pl.ds(h, 1), :] += skipped[:, :CHUNK] + skipped[:, CHUNK:]
        dlogs[pl.ds(h, 1), :] = row_sum(dmixed * y)
        return carry

    lax.fori_loop(0, HEADS, gate_tile, 0)
    causal = upper()
    ones = causal.astype(F32).astype(BF16)
    row = lax.broadcasted_iota(jnp.int32, (CHUNK, CHUNK), 0)
    col = lax.broadcasted_iota(jnp.int32, (CHUNK, CHUNK), 1)
    ones_back = (row >= col).astype(F32).astype(BF16)

    def chunk(step, carry):
        j = PER - 1 - step
        cols = pl.ds(pl.multiple_of(j * CHUNK, CHUNK), CHUNK)
        raw = raw_ref[0:HEADS, cols]
        steps, logs, columns, grown, to_end, through = rates_of(raw, heads_ref, ones)
        in_turned = act[INNER : INNER + NSTATE, cols]
        out_turned = act[INNER + NSTATE :, cols]
        in_map = in_turned.T
        out_map = out_turned.T
        scores = three_pass(in_map, right_pair(out_turned))
        in_pair = right_pair(in_turned)
        out_pair = right_pair(out_map)
        dscores = jnp.zeros((CHUNK, CHUNK), F32)
        din = jnp.zeros((NSTATE, CHUNK), F32)
        dout = jnp.zeros((NSTATE, CHUNK), F32)
        for g in range(HEADS // GROUP):
            rows = slice(g * GROUP * HEAD_DIM, (g + 1) * GROUP * HEAD_DIM)
            leaving = dstate[rows]
            entering = s_ref[j, rows]
            from_state = three_pass(leaving, in_pair)
            ending, growing, kept = [], [], []
            for q in range(GROUP):
                h = g * GROUP + q
                mine = slice(h * HEAD_DIM, (h + 1) * HEAD_DIM)
                values = act[mine, cols]
                fed = values * steps[h : h + 1]
                dys = dy[mine, cols]
                gaps = logs[h : h + 1] - jnp.broadcast_to(columns[:, h : h + 1], (CHUNK, CHUNK))
                decay = jnp.where(causal, jnp.exp(gaps), 0.0)
                weights = scores * decay
                both = dot_nt(stack_left(dys), beside(*split(weights)))
                du = both[:HEAD_DIM] + both[HEAD_DIM:]
                du = du + from_state[q * HEAD_DIM : (q + 1) * HEAD_DIM] * to_end[h : h + 1]
                fed_high, fed_low = split(fed)
                dy_high, dy_low = split(dys)
                dweights = dot_tn(
                    above(fed_high, fed_low, fed_high), above(dy_high, dy_high, dy_low)
                )
                dscores = dscores + dweights * decay
                vdu_rows[h : h + 1, :] = row_sum(values * du)
                dact[mine, cols] = du * steps[h : h + 1] + heads_ref[2][h : h + 1] * dys
                ending.append(fed * to_end[h : h + 1])
                growing.append(dys * grown[h : h + 1])
                kept.append(jnp.broadcast_to(through[h : h + 1], (HEAD_DIM, CHUNK)))
            ending = above(*ending)
            growing = above(*growing)
            end_high, end_low = split(ending)
            grow_high, grow_low = split(growing)
            leave_high, leave_low = split(leaving)
            enter_high, enter_low = split(entering)
            din = din + dot_tn(
                above(leave_high, leave_low, leave_high), above(end_high, end_high, end_low)
            )
            dout = dout + dot_tn(
                above(enter_high, enter_low, enter_high), above(grow_high, grow_high, grow_low)
            )
            arrived = leaving * above(*kept) + three_pass(growing, out_pair)
            dstate[rows] = arrived
            meet = arrived * entering
            for q in range(GROUP):
                h = g * GROUP + q
                dheads_ref[3, h : h + 1, :] = row_sum(meet[q * HEAD_DIM : (q + 1) * HEAD_DIM])
        vdu = vdu_rows[...]
        dlog = dlogs[:, cols] - steps * vdu
        drate = exact_sum(dlog, ones_back) + flow[...]
        flow[...] = jnp.broadcast_to(
            jnp.sum(dheads_ref[3], axis=1, keepdims=True), (HEADS, CHUNK)
        )
        dsteps = vdu + heads_ref[1] * drate
        draw = dsteps * jax.nn.sigmoid(raw + heads_ref[0])
        dheads_ref[0] += draw
        dheads_ref[1] += drate * steps * heads_ref[1]
        dstep_ref[:, cols] = above(draw, jnp.zeros((STEP - HEADS, CHUNK), F32)).astype(BF16)
        score_high, score_low = split(dscores)
        both = dot_nt(stack_left(out_turned), beside(score_high, score_low))
        dact[INNER : INNER + NSTATE, cols] = din + both[:NSTATE] + both[NSTATE:]
        both = dot(stack_left(in_turned), above(score_high, score_low))
        dact[INNER + NSTATE :, cols] = dout + both[:NSTATE] + both[NSTATE:]
        return carry

    lax.fori_loop(0, PER, chunk, 0)

    def conv_tile(i, carry):
        rows = pl.ds(pl.multiple_of(i * 64, 64), 64)
        c = c_ref[rows, :]
        sig = jax.nn.sigmoid(c)
        dpre = dact[rows, :] * (sig * (1.0 + c * (1.0 - sig)))
        cin = cin_ref[rows, :]
        ext = beside(dpre, tail[rows, :])
        dcin = dpre * wide(taps_ref[KCONV - 1, rows, :])
        grad = cin * dpre
        dtaps_ref[KCONV - 1, rows, :] += grad[:, :CHUNK] + grad[:, CHUNK:]
        dtaps_ref[KCONV, rows, :] += dpre[:, :CHUNK] + dpre[:, CHUNK:]
        for k in range(KCONV - 1):
            ahead = KCONV - 1 - k
            shifted = pltpu.roll(ext, STRIP + CHUNK - ahead, 1)[:, :STRIP]
            dcin = dcin + shifted * wide(taps_ref[k, rows, :])
            grad = cin * shifted
            dtaps_ref[k, rows, :] += grad[:, :CHUNK] + grad[:, CHUNK:]
        tail[rows, :] = dpre[:, :CHUNK]
        dconv_ref[rows, :] = dcin.astype(BF16)
        return carry

    lax.fori_loop(0, CONVCH // 64, conv_tile, 0)
    x = x_ref[...].astype(F32)
    r = lax.rsqrt(jnp.mean(x * x, axis=-1, keepdims=True) + EPSILON)
    parts = []
    for i in range(D // 256):
        part = slice(256 * i, 256 * i + 256)
        total = dot(w_in_ref[part, :INNER], dgate_ref[...])
        total = total + dot(w_in_ref[part, INNER:], dconv_ref[...])
        parts.append((total + dot(w_step_ref[part], dstep_ref[...])).T)
    dscaled = beside(*parts)
    plain = x * r
    dgain_ref[...] += fold(dscaled * plain)
    gained = dscaled * gain_ref[...]
    inner = jnp.mean(gained * plain, axis=-1, keepdims=True)
    dx_ref[...] = back.astype(F32) + (gained - plain * inner) * r


def whole(shape):
    return pl.BlockSpec(shape, lambda i: (0,) * len(shape), pipeline_mode=pl.Buffered(1))


def strip_rows(width):
    return pl.BlockSpec((STRIP, width), lambda i: (i, 0))


def strip_cols(height):
    return pl.BlockSpec((height, STRIP), lambda i: (0, i))


def shape(*dims, dtype=F32):
    return jax.ShapeDtypeStruct(dims, dtype)


def forward_call(x, w_in_t, w_step_t, w_out, gain, taps, heads, inner):
    return pl.pallas_call(
        forward_kernel,
        grid=(STRIPS,),
        in_specs=[
            strip_rows(D), whole((WIDE, D)), whole((STEP, D)), whole((D, INNER)), whole((1, D)),
            whole((KCONV + 1, CONVCH, CHUNK)), whole((3, HEADS, CHUNK)), whole((INNER, CHUNK)),
        ],
        out_specs=[
            strip_rows(D), strip_rows(D), strip_cols(INNER), strip_cols(CONVCH),
            strip_cols(CONVCH), strip_cols(STEP), strip_cols(INNER),
            pl.BlockSpec((PER, INNER, NSTATE), lambda i: (i, 0, 0)), strip_cols(INNER),
            strip_cols(8),
        ],
        out_shape=[
            shape(LEN, D, dtype=BF16), shape(LEN, D, dtype=BF16), shape(INNER, LEN),
            shape(CONVCH, LEN), shape(CONVCH, LEN), shape(STEP, LEN), shape(INNER, LEN),
            shape(LEN // CHUNK, INNER, NSTATE), shape(INNER, LEN, dtype=BF16), shape(8, LEN),
        ],
        scratch_shapes=[
            pltpu.VMEM((CONVCH, STRIP), F32), pltpu.VMEM((INNER, STRIP), F32),
            pltpu.VMEM((INNER, NSTATE), F32), pltpu.VMEM((CONVCH, CHUNK), F32),
        ],
        compiler_params=pltpu.CompilerParams(vmem_limit_bytes=56 * 2**20),
        name="mixer_forward",
    )(x, w_in_t, w_step_t, w_out, gain, taps, heads, inner)


def backward_call(x, back, w_in, w_step, w_out_t, gain, taps, heads, inner, kept):
    last = STRIPS - 1

    def rows(width):
        return pl.BlockSpec((STRIP, width), lambda i: (last - i, 0))

    def cols(height):
        return pl.BlockSpec((height, STRIP), lambda i: (0, last - i))

    z, cin, c, raw, y, states, r = kept
    return pl.pallas_call(
        backward_kernel,
        grid=(STRIPS,),
        in_specs=[
            rows(D), rows(D), whole((D, WIDE)), whole((D, STEP)), whole((INNER, D)),
            whole((1, D)), whole((KCONV + 1, CONVCH, CHUNK)), whole((3, HEADS, CHUNK)),
            whole((INNER, CHUNK)), cols(INNER), cols(CONVCH), cols(CONVCH), cols(STEP),
            cols(INNER), pl.BlockSpec((PER, INNER, NSTATE), lambda i: (last - i, 0, 0)), cols(8),
        ],
        out_specs=[
            rows(D), cols(INNER), cols(CONVCH), cols(STEP), whole((8, D)), whole((KCONV + 1, CONVCH, CHUNK)),
            whole((4, HEADS, CHUNK)), whole((INNER, CHUNK)),
        ],
        out_shape=[
            shape(LEN, D), shape(INNER, LEN, dtype=BF16), shape(CONVCH, LEN, dtype=BF16),
            shape(STEP, LEN, dtype=BF16),
            shape(8, D), shape(KCONV + 1, CONVCH, CHUNK), shape(4, HEADS, CHUNK),
            shape(INNER, CHUNK),
        ],
        scratch_shapes=[
            pltpu.VMEM((CONVCH, STRIP), F32), pltpu.VMEM((CONVCH, STRIP), F32),
            pltpu.VMEM((INNER, STRIP), F32), pltpu.VMEM((INNER, STRIP), F32),
            pltpu.VMEM((INNER, NSTATE), F32), pltpu.VMEM((HEADS, CHUNK), F32),
            pltpu.VMEM((CONVCH, CHUNK), F32), pltpu.VMEM((HEADS, STRIP), F32),
            pltpu.VMEM((HEADS, CHUNK), F32),
        ],
        compiler_params=pltpu.CompilerParams(vmem_limit_bytes=60 * 2**20),
        name="mixer_backward",
    )(x, back, w_in, w_step, w_out_t, gain, taps, heads, inner, z, cin, c, raw, y, states, r)


def lanes(vector):
    return jnp.broadcast_to(vector[..., None], vector.shape + (CHUNK,))


def parameters(params):
    gain = params[:D].reshape(1, D)
    at = D
    taps = lanes(params[at : at + (KCONV + 1) * CONVCH].reshape(KCONV + 1, CONVCH))
    at += (KCONV + 1) * CONVCH
    heads = params[at : at + 3 * HEADS].reshape(3, HEADS)
    heads = lanes(jnp.stack([heads[0], -jnp.exp(heads[1]), heads[2]]))
    inner = lanes(params[at + 3 * HEADS :])
    return gain, taps, heads, inner


def block_and_gradients(x, back, whole_in, whole_out, params):
    gain, taps, heads, inner = parameters(params)
    w_in = whole_in[:, :WIDE]
    w_step = jnp.pad(whole_in[:, WIDE:], ((0, 0), (0, STEP - HEADS)))
    out, hb, z, cin, c, raw, y, states, normed, r = forward_call(
        x, w_in.T, w_step.T, whole_out, gain, taps, heads, inner
    )
    dx, dgate, dconv, dstep, dgain, dtaps, dheads, dinner = backward_call(
        x, back, w_in, w_step, whole_out.T, gain, taps, heads, inner,
        (z, cin, c, raw, y, states, r),
    )
    grad_out = dot(normed, back)
    grad_gate = dot(dgate, hb)
    grad_conv = dot(dconv, hb)
    grad_step = dot(dstep, hb)[:HEADS]
    small = jnp.concatenate(
        [
            jnp.sum(dgain, axis=0),
            jnp.sum(dtaps, axis=-1).reshape(-1),
            jnp.sum(dheads[:3], axis=-1).reshape(-1),
            jnp.sum(dinner, axis=-1),
        ]
    )
    return out, dx, grad_gate, grad_conv, grad_step, grad_out, small


MESH = pl.DeviceIdType.MESH


class Place:
    def __init__(self, sizes):
        self.Z, self.F = sizes
        self.C, self.Y = 2, 2
        self.X = self.F // 4
        f = lax.axis_index("fsdp")
        self.z = lax.axis_index("dp")
        self.c = lax.rem(f, 2)
        self.x = lax.rem(f // 2, self.X)
        self.y = f // (2 * self.X)
        self.f = f

    def at(self, z=None, y=None, x=None, c=None):
        z = self.z if z is None else z
        y = self.y if y is None else y
        x = self.x if x is None else x
        c = self.c if c is None else c
        return (z, (y * self.X + x) * 2 + c)

    def other_x(self, step):
        return lax.rem(self.x + step, self.X)


def signal(device):
    pl.semaphore_signal(
        pltpu.get_barrier_semaphore(), inc=1, device_id=device, device_id_type=MESH
    )


def greet_all(place):
    count = place.Z * place.F
    me = place.z * place.F + place.f

    def step(i, carry):
        peer = lax.rem(me + i, count)
        signal((peer // place.F, lax.rem(peer, place.F)))
        return carry

    lax.fori_loop(1, count, step, 0)
    pl.semaphore_wait(pltpu.get_barrier_semaphore(), count - 1)


def remote(src, dst, send, recv, device):
    return pltpu.make_async_remote_copy(
        src_ref=src, dst_ref=dst, send_sem=send, recv_sem=recv, device_id=device,
        device_id_type=MESH,
    )


def add_blocks(dst, src, count):
    def step(i, carry):
        target = dst(i)
        target[...] = target[...] + src(i)[...]
        return carry

    lax.fori_loop(0, count, step, 0)


class Swap:
    def __init__(self, place, src, dst, send, recv, local):
        self.place, self.src, self.dst = place, src, dst
        self.send, self.recv, self.local = send, recv, local
        self.count = place.Z * place.F
        self.me = place.z * place.F + place.f

    def to(self, i):
        peer = lax.rem(self.me + i, self.count)
        return remote(
            self.src.at[peer], self.dst.at[self.me], self.send.at[i], self.recv.at[i],
            (peer // self.place.F, lax.rem(peer, self.place.F)),
        )

    def start(self):
        pltpu.make_async_copy(self.src.at[self.me], self.dst.at[self.me], self.local).start()

        def step(i, carry):
            self.to(i).start()
            return carry

        lax.fori_loop(1, self.count, step, 0)

    def wait(self):
        pltpu.make_async_copy(self.src.at[self.me], self.dst.at[self.me], self.local).wait()

        def step(i, carry):
            sender = lax.rem(self.me + self.count - i, self.count)
            self.to(i).wait_send()
            remote(
                self.src.at[sender], self.dst.at[sender], self.send.at[i], self.recv.at[i],
                (sender // self.place.F, lax.rem(sender, self.place.F)),
            ).wait_recv()
            return carry

        lax.fori_loop(1, self.count, step, 0)


def swap_kernel(sizes, src, dst, send, recv, local):
    place = Place(sizes)
    greet_all(place)
    swap = Swap(place, src, dst, send, recv, local)
    swap.start()
    swap.wait()


def swap_call(blocks, sizes, collective_id):
    count = sizes[0] * sizes[1]
    return pl.pallas_call(
        functools.partial(swap_kernel, sizes),
        out_shape=jax.ShapeDtypeStruct(blocks.shape, blocks.dtype),
        in_specs=[pl.BlockSpec(memory_space=pl.ANY)],
        out_specs=pl.BlockSpec(memory_space=pl.ANY),
        scratch_shapes=[
            pltpu.SemaphoreType.DMA((count,)), pltpu.SemaphoreType.DMA((count,)),
            pltpu.SemaphoreType.DMA,
        ],
        compiler_params=pltpu.CompilerParams(collective_id=collective_id, has_side_effects=True),
        name="swap",
    )(blocks)


class Plane:
    def __init__(self, place, acc, x1, y1, x2, y2, sems):
        self.p, self.acc = place, acc
        self.x1, self.y1, self.x2, self.y2, self.sems = x1, y1, x2, y2, sems
        self.h = place.Z // 2

    def copies(self, stage):
        p, acc, h = self.p, self.acc, self.h
        low, high = pl.ds(0, h), pl.ds(h, p.Z - h)
        out = []
        base = stage * p.X
        for s in range(1, p.X):
            x = p.other_x(s)
            if stage == 0:
                src, dst = acc.at[low, :, x], self.x1.at[s - 1]
            else:
                src, dst = acc.at[high, p.y, x], self.x2.at[s - 1]
            sem = self.sems.at[base + s]
            out.append(remote(src, dst, sem.at[0], sem.at[1], p.at(x=x)))
        if stage == 0:
            src, dst = acc.at[high, 1 - p.y], self.y1
        else:
            src, dst = acc.at[low, 1 - p.y, p.x], self.y2
        sem = self.sems.at[base]
        out.append(remote(src, dst, sem.at[0], sem.at[1], p.at(y=1 - p.y)))
        return out

    def start(self, stage):
        for copy in self.copies(stage):
            copy.start()

    def finish(self, stage):
        p, acc, h = self.p, self.acc, self.h
        for copy in self.copies(stage):
            copy.wait()
        for s in range(p.X - 1):
            if stage == 0:
                add_blocks(
                    lambda i: acc.at[i // p.Y, lax.rem(i, p.Y), p.x],
                    lambda i: self.x1.at[s, i // p.Y, lax.rem(i, p.Y)],
                    h * p.Y,
                )
            else:
                add_blocks(
                    lambda i: acc.at[h + i, p.y, p.x], lambda i: self.x2.at[s, i], p.Z - h
                )
        if stage == 0:
            add_blocks(
                lambda i: acc.at[h + i // p.X, p.y, lax.rem(i, p.X)],
                lambda i: self.y1.at[i // p.X, lax.rem(i, p.X)],
                (p.Z - h) * p.X,
            )
        else:
            add_blocks(lambda i: acc.at[i, p.y, p.x], lambda i: self.y2.at[i], h)


def plane_scratch(sizes, block):
    Z, X, Y = sizes[0], sizes[1] // 4, 2
    h = Z // 2
    return [
        pltpu.VMEM((Z, Y, X) + block, F32), pltpu.VMEM((X - 1, h, Y) + block, F32),
        pltpu.VMEM((Z - h, X) + block, F32), pltpu.VMEM((X - 1, Z - h) + block, F32),
        pltpu.VMEM((h,) + block, F32), pltpu.SemaphoreType.DMA((2 * X, 2)),
    ]


def scatter_kernel(sizes, parts, *refs):
    ins, outs, rest = refs[:parts], refs[parts : 2 * parts], refs[2 * parts :]
    p = Place(sizes)
    Z = p.Z
    work = [rest[10 * k : 10 * k + 10] for k in range(parts)]
    signal(p.at(c=1 - p.c))
    signal(p.at(y=1 - p.y))
    for s in range(1, p.X):
        signal(p.at(x=p.other_x(s)))

    for s in range(1, Z):
        signal(p.at(z=lax.rem(p.z + s, Z)))
    pl.semaphore_wait(pltpu.get_barrier_semaphore(), p.X + Z)

    def core_copies(k):
        acc, core, sems = work[k][0], work[k][6], work[k][7]
        return (
            remote(
                ins[k].at[:, :, :, 1 - p.c], core, sems.at[0], sems.at[1], p.at(c=1 - p.c)
            ),
            pltpu.make_async_copy(ins[k].at[:, :, :, p.c], acc, sems.at[2]),
        )

    for k in range(parts):
        for copy in core_copies(k):
            copy.start()
    planes = [Plane(p, *work[k][:6]) for k in range(parts)]
    for k in range(parts):
        for copy in core_copies(k):
            copy.wait()
        acc, core = work[k][0], work[k][6]

        def place_of(i):
            return i // (p.Y * p.X), lax.rem(i // p.X, p.Y), lax.rem(i, p.X)

        add_blocks(
            lambda i: acc.at[place_of(i)], lambda i: core.at[place_of(i)], Z * p.Y * p.X
        )
        planes[k].start(0)
    for k in range(parts):
        planes[k].finish(0)
        planes[k].start(1)

    def flow(k, t, right):
        acc, held, sems = work[k][0], work[k][8], work[k][9]
        side = 0 if right else 1
        target = p.z + 1 if right else p.z - 1
        sem = sems.at[side, t]
        return remote(
            acc.at[t, p.y, p.x], held.at[side, t], sem.at[0], sem.at[1], p.at(z=target)
        )

    def send(k, t, right):
        @pl.when(p.z < t if right else p.z > t)
        def _():
            flow(k, t, right).start()

    def receive(k, t, right):
        acc, held = work[k][0], work[k][8]

        @pl.when(jnp.logical_and(p.z > 0, p.z <= t) if right else
                 jnp.logical_and(p.z < Z - 1, p.z >= t))
        def _():
            flow(k, t, right).wait_recv()
            mine = acc.at[t, p.y, p.x]
            mine[...] = mine[...] + held[0 if right else 1, t]

    def pass_on(k, j, right):
        t = Z - 1 - j if right else j
        receive(k, t, right)

        @pl.when(p.z > 0 if right else p.z < Z - 1)
        def _():
            send(k, t, right)

    for k in range(parts):
        planes[k].finish(1)
        for j in range(Z - 1):
            @pl.when(p.z == 0)
            def _():
                send(k, Z - 1 - j, True)

            @pl.when(p.z == Z - 1)
            def _():
                send(k, j, False)

    for k in range(parts):
        for j in range(Z):
            @pl.when(p.z < Z // 2)
            def _():
                pass_on(k, j, True)
                pass_on(k, j, False)

            @pl.when(p.z >= Z // 2)
            def _():
                pass_on(k, j, False)
                pass_on(k, j, True)

        for j in range(Z):
            for right in (True, False):
                @pl.when(p.z < j if right else p.z > j)
                def _():
                    flow(k, j, right).wait_send()

        outs[k][...] = work[k][0][p.z, p.y, p.x]


def scatter_call(blocks, sizes, collective_id):
    Z, F = sizes
    X, Y = F // 4, 2
    ins = [b.reshape((Z, Y, X, 2) + b.shape[1:]) for b in blocks]
    scratch = []
    for b in blocks:
        block = b.shape[1:]
        scratch += plane_scratch(sizes, block)
        scratch += [
            pltpu.VMEM((Z, Y, X) + block, F32), pltpu.SemaphoreType.DMA((3,)),
            pltpu.VMEM((2, Z) + block, F32), pltpu.SemaphoreType.DMA((2, Z, 2)),
        ]
    return pl.pallas_call(
        functools.partial(scatter_kernel, sizes, len(blocks)),
        out_shape=[jax.ShapeDtypeStruct(b.shape[1:], F32) for b in blocks],
        in_specs=[pl.BlockSpec(memory_space=pl.ANY)] * len(blocks),
        out_specs=[pl.BlockSpec(memory_space=pltpu.VMEM)] * len(blocks),
        scratch_shapes=scratch,
        compiler_params=pltpu.CompilerParams(
            collective_id=collective_id, has_side_effects=True, vmem_limit_bytes=56 * 2**20
        ),
        name="scatter",
    )(*ins)


def sum_kernel(
    sizes, gram_ref, give_ref, blocks_ref, out_ref, given_ref, moved_ref,
    sum_ref, acc, x1, y1, x2, y2, sems, core, core_sems, held, z_sems, back_sems, swap_send, swap_recv, local,
):
    p = Place(sizes)
    Z, h = p.Z, p.Z // 2
    low, high = pl.ds(0, h), pl.ds(h, Z - h)
    greet_all(p)
    partner = p.at(c=1 - p.c)
    first = [
        remote(gram_ref.at[1 - p.c], core, core_sems.at[0], core_sems.at[1], partner),
        remote(give_ref, given_ref, core_sems.at[2], core_sems.at[3], partner),
        pltpu.make_async_copy(gram_ref.at[p.c], acc, core_sems.at[4]),
    ]
    for copy in first:
        copy.start()
    swap = Swap(p, blocks_ref, moved_ref, swap_send, swap_recv, local)
    for copy in first:
        copy.wait()

    def place_of(i):
        return i // (p.Y * p.X), lax.rem(i // p.X, p.Y), lax.rem(i, p.X)

    add_blocks(lambda i: acc.at[place_of(i)], lambda i: core.at[place_of(i)], Z * p.Y * p.X)
    plane = Plane(p, acc, x1, y1, x2, y2, sems)
    plane.start(0)
    plane.finish(0)
    plane.start(1)
    swap.start()
    plane.finish(1)

    def over(s):
        z = lax.rem(p.z + s, Z)
        return remote(
            acc.at[z, p.y, p.x], held.at[s - 1], z_sems.at[0, s, 0], z_sems.at[0, s, 1], p.at(z=z)
        )

    for s in range(1, Z):
        over(s).start()
    for s in range(1, Z):
        over(s).wait()
    total = acc[p.z, p.y, p.x]
    for s in range(1, Z):
        total = total + held[s - 1]
    sum_ref[p.z, p.y, p.x] = total

    def back(s):
        z = lax.rem(p.z + s, Z)
        mine = sum_ref.at[p.z, p.y, p.x]
        return remote(mine, mine, z_sems.at[1, s, 0], z_sems.at[1, s, 1], p.at(z=z))

    for s in range(1, Z):
        back(s).start()
    for s in range(1, Z):
        back(s).wait_send()
        z = lax.rem(p.z + Z - s, Z)
        theirs = sum_ref.at[z, p.y, p.x]
        remote(theirs, theirs, z_sems.at[1, s, 0], z_sems.at[1, s, 1], p.at(z=z)).wait_recv()

    def spread(stage, start):
        for s in range(1, p.X):
            sem = back_sems.at[stage * p.X + s]
            mine, theirs = (
                sum_ref.at[high, p.y, x] if stage == 0 else sum_ref.at[low, :, x]
                for x in (p.x, lax.rem(p.x + p.X - s, p.X))
            )
            copy = remote(mine, mine, sem.at[0], sem.at[1], p.at(x=p.other_x(s)))
            if start:
                copy.start()
            else:
                copy.wait_send()
                remote(theirs, theirs, sem.at[0], sem.at[1], p.at(x=p.other_x(s))).wait_recv()
        sem = back_sems.at[stage * p.X]
        mine, theirs = (
            sum_ref.at[low, y, p.x] if stage == 0 else sum_ref.at[high, y]
            for y in (p.y, 1 - p.y)
        )
        copy = remote(mine, mine, sem.at[0], sem.at[1], p.at(y=1 - p.y))
        if start:
            copy.start()
        else:
            copy.wait_send()
            remote(theirs, theirs, sem.at[0], sem.at[1], p.at(y=1 - p.y)).wait_recv()

    for stage in range(2):
        spread(stage, True)
        spread(stage, False)
    out_ref[...] = sum_ref[...]
    swap.wait()


def sum_call(grams, give, blocks, sizes, collective_id):
    Z, F = sizes
    X, Y = F // 4, 2
    block = grams.shape[2:]
    count = Z * F
    return pl.pallas_call(
        functools.partial(sum_kernel, sizes),
        out_shape=[
            jax.ShapeDtypeStruct((Z, Y, X) + block, F32), jax.ShapeDtypeStruct(give.shape, F32),
            jax.ShapeDtypeStruct(blocks.shape, F32),
        ],
        in_specs=[pl.BlockSpec(memory_space=pl.ANY)] * 3,
        out_specs=[
            pl.BlockSpec(memory_space=pltpu.VMEM), pl.BlockSpec(memory_space=pl.ANY),
            pl.BlockSpec(memory_space=pl.ANY),
        ],
        scratch_shapes=[pltpu.VMEM((Z, Y, X) + block, F32)]
        + plane_scratch(sizes, block)
        + [
            pltpu.VMEM((Z, Y, X) + block, F32), pltpu.SemaphoreType.DMA((5,)),
            pltpu.VMEM((Z - 1,) + block, F32), pltpu.SemaphoreType.DMA((2, Z, 2)),
            pltpu.SemaphoreType.DMA((2 * X, 2)), pltpu.SemaphoreType.DMA((count,)),
            pltpu.SemaphoreType.DMA((count,)), pltpu.SemaphoreType.DMA,
        ],
        compiler_params=pltpu.CompilerParams(
            collective_id=collective_id, has_side_effects=True, vmem_limit_bytes=56 * 2**20
        ),
        name="gram_sum",
    )(grams.reshape((2, Z, Y, X) + block), give, blocks)


def pack(gram):
    rows = []
    for i in range(D // 256):
        a, b = 128 * i, D - 128 * (i + 1)
        rows.append(beside(gram[a : a + 128, a:], gram[b : b + 128, b:]))
    return above(*rows)


def unpack(packed):
    rows = [None] * (D // 128)
    for i in range(D // 256):
        pair = packed[128 * i : 128 * i + 128]
        wide_part, j = D - 128 * i, D // 128 - 1 - i
        rows[i] = jnp.pad(pair[:, :wide_part], ((0, 0), (128 * i, 0)))
        rows[j] = jnp.pad(pair[:, wide_part:], ((0, 0), (128 * j, 0)))
    half = above(*rows)
    at = lax.broadcasted_iota(jnp.int32, (D, D), 0) // 128
    to = lax.broadcasted_iota(jnp.int32, (D, D), 1) // 128
    return jnp.where(at <= to, half, half.T)


def iterate(first_gram, slabs):
    high = lax.Precision.HIGH
    scale = 1.0 / (jnp.sqrt(jnp.trace(first_gram)) + 1e-07)
    gram = first_gram * (scale * scale)
    slabs = slabs * scale
    eye = jnp.eye(gram.shape[0], dtype=F32)
    for iteration in range(ITERS):
        if iteration == ITERS - 1:
            once = jnp.dot(slabs, gram, precision=high)
            twice = jnp.dot(once, gram, precision=high)
            slabs = COEF_A * slabs + COEF_B * once + COEF_C * twice
        else:
            square = jnp.dot(gram, gram, precision=high)
            factor = COEF_A * eye + COEF_B * gram + COEF_C * square
            slabs = jnp.dot(slabs, factor, precision=high)
            half = jnp.dot(factor, gram, precision=high)
            gram = jnp.dot(half, factor, precision=high)
    return slabs


def gram_of(slab):
    return lax.dot_general(slab, slab, (((0,), (0,)), ((), ())), precision=lax.Precision.HIGH)


def spread_columns(rows, count):
    return rows.reshape(rows.shape[0], count, -1).transpose(1, 0, 2)


def gather_columns(blocks):
    return blocks.transpose(1, 0, 2).reshape(blocks.shape[1], -1)


def lanes_256(blocks):
    return jnp.pad(blocks, ((0, 0), (0, 0), (0, 256 - blocks.shape[2])))


def shards(
    inputs, cotangent, weight_in, weight_out, small_params, moment_in, moment_out, moment_small
):
    axes = ("dp", "fsdp")
    sizes = (lax.axis_size("dp"), lax.axis_size("fsdp"))
    count = sizes[0] * sizes[1]
    in_core = lax.rem(lax.axis_index("fsdp"), 2) == 0
    own = weight_in.shape[0]
    gates, convs = INNER // count, CONVCH // count
    ins = gates + convs
    whole_in, whole_out = (
        lax.all_gather(weight_in.astype(BF16), axes, axis=0, tiled=True),
        lax.all_gather(weight_out.astype(BF16), axes, axis=0, tiled=True),
    )
    old = jnp.concatenate(
        [
            spread_columns(moment_in[:, :INNER], count),
            spread_columns(moment_in[:, INNER:WIDE], count),
            spread_columns(moment_out, count),
            jnp.broadcast_to(moment_in[:, WIDE:], (count, own, HEADS)),
        ],
        axis=2,
    )
    old = swap_call(lanes_256(old), sizes, 0)
    old = old.reshape(D, 256)[:, : ins + gates + HEADS].T
    output, dx, part_gate, part_conv, part_step, part_out, part_small = block_and_gradients(
        inputs[0], cotangent[0], whole_in, whole_out, small_params
    )
    outputs, input_grad = output[None], dx[None]

    per = -(-(small_params.shape[0] + HEADS * D) // D)
    part_small = jnp.concatenate([part_small, part_step.reshape(-1)])
    part_small = jnp.pad(part_small, (0, D * per - part_small.shape[0])).reshape(count, own * per)
    part_small = jnp.pad(part_small, ((0, 0), (0, 1024 - own * per))).reshape(count, 8, 128)
    new_out, new_gate, new_conv, new_small = scatter_call(
        [
            part_out.reshape(count, gates, D), part_gate.reshape(count, gates, D),
            part_conv.reshape(count, convs, D), part_small,
        ],
        sizes,
        1,
    )

    def push(gradient, moment):
        return gradient + MOMENTUM * (MOMENTUM * moment + gradient)

    new_in = above(new_gate, new_conv)
    push_in = push(new_in, old[:ins])
    push_out = push(new_out, old[ins : ins + gates])
    give = jnp.where(in_core, jnp.pad(push_out, ((0, ins - gates), (0, 0))), push_in)
    message = jnp.concatenate(
        [
            above(new_in, new_out).T.reshape(count, own, ins + gates),
            jnp.broadcast_to(
                new_small.reshape(-1)[: own * per].reshape(own, per), (count, own, per)
            ),
        ],
        axis=2,
    )
    grams = jnp.stack([pack(gram_of(push_in)), pack(gram_of(push_out))])
    grams = grams.reshape(2, count // 2, -1, grams.shape[2])
    gram, given, moved = sum_call(grams, give, lanes_256(message), sizes, 2)
    small = moved[:, :, ins + gates : ins + gates + per].reshape(-1)
    grad_small = small[: small_params.shape[0]]
    new_step = small[grad_small.shape[0] : grad_small.shape[0] + HEADS * D].reshape(HEADS, D)
    push_step = push(new_step, old[ins + gates :])
    gram = unpack(gram.reshape(-1, gram.shape[-1]))
    gram = gram + jnp.where(in_core, gram_of(push_step), 0.0)
    slab_in = above(push_in, given, push_step)
    slab_out = above(given[:gates], push_out, jnp.zeros((2 * convs + HEADS, D), F32))
    ortho = iterate(gram, jnp.where(in_core, slab_in, slab_out))
    spread = swap_call(lanes_256(ortho.T.reshape(count, own, -1)), sizes, 3)

    def rows_in(gate_blocks, conv_blocks, step_rows):
        return beside(gather_columns(gate_blocks), gather_columns(conv_blocks), step_rows)

    evens, odds = spread[0::2], spread[1::2]
    direction_in = rows_in(
        jnp.concatenate([evens[:, :, :gates], evens[:, :, ins : ins + gates]], axis=2),
        jnp.concatenate([evens[:, :, gates:ins], evens[:, :, ins + gates : 2 * ins]], axis=2),
        evens[0, :, 2 * ins : 2 * ins + HEADS],
    )
    direction_out = gather_columns(odds[:, :, : 2 * gates])
    first_row = (lax.axis_index("dp") * sizes[1] + lax.axis_index("fsdp")) * own
    grad_in = rows_in(
        moved[:, :, :gates],
        moved[:, :, gates:ins],
        lax.dynamic_slice_in_dim(new_step, first_row, own, 1).T,
    )
    grad_out = gather_columns(moved[:, :, ins : ins + gates])
    new_moment_in = MOMENTUM * moment_in + grad_in
    new_moment_out = MOMENTUM * moment_out + grad_out
    decay = 1.0 - MATRIX_RATE * WEIGHT_DECAY
    new_weight_in = weight_in * decay - MATRIX_RATE * 0.2 * math.sqrt(max(D, IN_W)) * direction_in
    new_weight_out = (
        weight_out * decay - MATRIX_RATE * 0.2 * math.sqrt(max(D, INNER)) * direction_out
    )
    new_moment_small = MOMENTUM * moment_small + grad_small
    new_small_params = small_params - SMALL_RATE * new_moment_small
    return (
        outputs,
        input_grad,
        grad_in,
        grad_out,
        grad_small,
        new_moment_in,
        new_moment_out,
        new_moment_small,
        new_weight_in,
        new_weight_out,
        new_small_params,
    )


def solution(mesh):
    return jax.shard_map(
        shards,
        mesh=mesh,
        in_specs=(
            P(("dp", "fsdp"), None, None),
            P(("dp", "fsdp"), None, None),
            P(("dp", "fsdp"), None),
            P(("dp", "fsdp"), None),
            P(),
            P(("dp", "fsdp"), None),
            P(("dp", "fsdp"), None),
            P(),
        ),
        out_specs=(
            P(("dp", "fsdp"), None, None),
            P(("dp", "fsdp"), None, None),
            P(("dp", "fsdp"), None),
            P(("dp", "fsdp"), None),
            P(),
            P(("dp", "fsdp"), None),
            P(("dp", "fsdp"), None),
            P(),
            P(("dp", "fsdp"), None),
            P(("dp", "fsdp"), None),
            P(),
        ),
        check_vma=False,
    )
```

```python
import functools
import math

import jax
import jax.numpy as jnp
from jax import lax
from jax.experimental import pallas as pl
from jax.experimental.pallas import tpu as pltpu
from jax.sharding import PartitionSpec as P

D = 768
HEADS = 24
HEAD_DIM = 64
NSTATE = 128
KCONV = 4
LEN = 1024
ITERS = 5
INNER = 1536
CONVCH = 1792
IN_W = 3352
WIDE = INNER + CONVCH
STEP = 32
HALF = 2560
OUT_AT = WIDE - HALF
STEP_AT = OUT_AT + INNER

MOMENTUM = 0.95
MATRIX_RATE = 0.15
WEIGHT_DECAY = 0.1
SMALL_RATE = 0.01
EPSILON = 1e-05
COEF_A = 3.4445
COEF_B = -4.775
COEF_C = 2.0315

F32 = jnp.float32
BF16 = jnp.bfloat16
CHUNK = 128
STRIP = 256
PER = STRIP // CHUNK
STRIPS = LEN // STRIP
GROUP = 4


def dot(a, b):
    return lax.dot_general(a, b, (((1,), (0,)), ((), ())), preferred_element_type=F32)


def dot_nt(a, b):
    return lax.dot_general(a, b, (((1,), (1,)), ((), ())), preferred_element_type=F32)


def dot_tn(a, b):
    return lax.dot_general(a, b, (((0,), (0,)), ((), ())), preferred_element_type=F32)


def split(v):
    high = v.astype(BF16)
    return high, (v - high.astype(F32)).astype(BF16)


def beside(*parts):
    return jnp.concatenate(parts, axis=1)


def above(*parts):
    return jnp.concatenate(parts, axis=0)


def right_pair(b):
    high, low = split(b)
    return above(beside(high, low), beside(high, jnp.zeros_like(low)))


def three_pass(a, pair):
    high, low = split(a)
    both = dot(beside(high, low), pair)
    half = both.shape[1] // 2
    return both[:, :half] + both[:, half:]


def exact_sum(a, ones):
    high = a.astype(BF16)
    rest = a - high.astype(F32)
    mid = rest.astype(BF16)
    low = (rest - mid.astype(F32)).astype(BF16)
    return dot(beside(high, mid, low), above(ones, ones, ones))


def stack_left(a):
    high, low = split(a)
    return above(beside(high, high), beside(low, jnp.zeros_like(low)))


def fold(rows):
    total = rows[0:8]
    for i in range(1, rows.shape[0] // 8):
        total = total + rows[8 * i : 8 * i + 8]
    return total


def row_sum(rows):
    return jnp.sum(fold(rows), axis=0, keepdims=True)


def upper():
    row = lax.broadcasted_iota(jnp.int32, (CHUNK, CHUNK), 0)
    col = lax.broadcasted_iota(jnp.int32, (CHUNK, CHUNK), 1)
    return col >= row


def softplus(v):
    return jnp.maximum(v, 0.0) + jnp.log1p(jnp.exp(-jnp.abs(v)))


def rates_of(raw, heads_ref, ones):
    steps = softplus(raw + heads_ref[0])
    logs = exact_sum(steps * heads_ref[1], ones)
    last = jnp.broadcast_to(logs[:, CHUNK - 1 : CHUNK], logs.shape)
    columns = above(logs, jnp.zeros((CHUNK - HEADS, CHUNK), F32)).T
    return steps, logs, columns, jnp.exp(logs), jnp.exp(last - logs), jnp.exp(last)


def wide(v):
    return beside(*([v] * PER))


def forward_kernel(
    x_ref, first_t_ref, second_t_ref, second_ref, gain_ref, taps_ref, heads_ref, inner_ref,
    out_ref, hb_ref, z_ref, cin_ref, c_ref, raw_ref, y_ref, s_ref, normed_ref, r_ref,
    act, gated, state, tail,
):
    @pl.when(pl.program_id(0) == 0)
    def _():
        state[...] = jnp.zeros_like(state)
        tail[...] = jnp.zeros_like(tail)

    x = x_ref[...].astype(F32)
    scaled = x * lax.rsqrt(jnp.mean(x * x, axis=-1, keepdims=True) + EPSILON) * gain_ref[...]
    hb = scaled.astype(BF16)
    hb_ref[...] = hb
    for i in range(INNER // 256):
        z_ref[256 * i : 256 * i + 256] = dot_nt(first_t_ref[256 * i : 256 * i + 256], hb)
    for i in range(CONVCH // 256):
        start = INNER + 256 * i
        if start < HALF:
            rows = first_t_ref[start : start + 256]
        else:
            rows = second_t_ref[start - HALF : start - HALF + 256]
        cin_ref[256 * i : 256 * i + 256] = dot_nt(rows, hb)
    raw_ref[...] = dot_nt(second_t_ref[STEP_AT : STEP_AT + STEP], hb)

    def conv_tile(i, carry):
        rows = pl.ds(pl.multiple_of(i * 64, 64), 64)
        cur = cin_ref[rows, :]
        ext = beside(tail[rows, :], cur)
        total = wide(taps_ref[KCONV, rows, :])
        for k in range(KCONV - 1):
            shifted = pltpu.roll(ext, KCONV - 1 - k, 1)[:, CHUNK:]
            total = total + shifted * wide(taps_ref[k, rows, :])
        total = total + cur * wide(taps_ref[KCONV - 1, rows, :])
        c_ref[rows, :] = total
        act[rows, :] = total * jax.nn.sigmoid(total)
        tail[rows, :] = cur[:, STRIP - CHUNK :]
        return carry

    lax.fori_loop(0, CONVCH // 64, conv_tile, 0)
    causal = upper()
    ones = causal.astype(F32).astype(BF16)

    def chunk(j, carry):
        cols = pl.ds(pl.multiple_of(j * CHUNK, CHUNK), CHUNK)
        steps, logs, columns, grown, to_end, through = rates_of(
            raw_ref[0:HEADS, cols], heads_ref, ones
        )
        in_map = act[INNER : INNER + NSTATE, cols].T
        in_pair = right_pair(in_map)
        out_pair = right_pair(act[INNER + NSTATE :, cols])
        scores = three_pass(in_map, out_pair)
        squares = jnp.zeros((8, CHUNK), F32)
        for g in range(HEADS // GROUP):
            rows = slice(g * GROUP * HEAD_DIM, (g + 1) * GROUP * HEAD_DIM)
            held = state[rows]
            s_ref[j, rows] = held
            across = three_pass(held, out_pair)
            ending, kept = [], []
            for q in range(GROUP):
                h = g * GROUP + q
                mine = slice(h * HEAD_DIM, (h + 1) * HEAD_DIM)
                values = act[mine, cols]
                fed = values * steps[h : h + 1]
                gaps = logs[h : h + 1] - jnp.broadcast_to(columns[:, h : h + 1], (CHUNK, CHUNK))
                weights = scores * jnp.where(causal, jnp.exp(gaps), 0.0)
                both = dot(stack_left(fed), above(*split(weights)))
                y = both[:HEAD_DIM] + both[HEAD_DIM:]
                y = y + across[q * HEAD_DIM : (q + 1) * HEAD_DIM] * grown[h : h + 1]
                y_ref[mine, cols] = y
                gate = z_ref[mine, cols]
                open_ = (y + heads_ref[2][h : h + 1] * values) * (gate * jax.nn.sigmoid(gate))
                gated[mine, cols] = open_
                squares = squares + fold(open_ * open_)
                ending.append(fed * to_end[h : h + 1])
                kept.append(jnp.broadcast_to(through[h : h + 1], (HEAD_DIM, CHUNK)))
            state[rows] = held * above(*kept) + three_pass(above(*ending), in_pair)
        mean = jnp.sum(squares, axis=0, keepdims=True) * (1.0 / INNER)
        r_ref[:, cols] = jnp.broadcast_to(lax.rsqrt(mean + EPSILON), (8, CHUNK))
        return carry

    lax.fori_loop(0, PER, chunk, 0)

    def norm_tile(i, carry):
        rows = pl.ds(pl.multiple_of(i * 64, 64), 64)
        scale = jnp.broadcast_to(r_ref[0:1, :], (64, STRIP))
        normed_ref[rows, :] = (gated[rows, :] * scale * wide(inner_ref[rows, :])).astype(BF16)
        return carry

    lax.fori_loop(0, INNER // 64, norm_tile, 0)
    for i in range(D // 256):
        part = slice(256 * i, 256 * i + 256)
        branch = dot(second_ref[part, OUT_AT:STEP_AT], normed_ref[...]).T
        out_ref[:, part] = (x_ref[:, part].astype(F32) + branch).astype(BF16)


def backward_kernel(
    x_ref, back_ref, first_ref, second_ref, second_t_ref, gain_ref, taps_ref, heads_ref, inner_ref,
    z_ref, cin_ref, c_ref, raw_ref, y_ref, s_ref, r_ref,
    dx_ref, dgate_ref, dconv_ref, dstep_ref, dgain_ref, dtaps_ref, dheads_ref, dinner_ref,
    act, dact, dnormed, dy, dstate, flow, tail, dlogs, vdu_rows,
):
    first = pl.program_id(0) == 0

    @pl.when(first)
    def _():
        dstate[...] = jnp.zeros_like(dstate)
        flow[...] = jnp.zeros_like(flow)
        tail[...] = jnp.zeros_like(tail)
        dgain_ref[...] = jnp.zeros_like(dgain_ref)
        dtaps_ref[...] = jnp.zeros_like(dtaps_ref)
        dheads_ref[...] = jnp.zeros_like(dheads_ref)
        dinner_ref[...] = jnp.zeros_like(dinner_ref)

    back = back_ref[...]
    for i in range(INNER // 256):
        dnormed[256 * i : 256 * i + 256] = dot_nt(
            second_t_ref[OUT_AT + 256 * i : OUT_AT + 256 * i + 256], back
        )

    def act_tile(i, carry):
        rows = pl.ds(pl.multiple_of(i * 64, 64), 64)
        c = c_ref[rows, :]
        act[rows, :] = c * jax.nn.sigmoid(c)
        return carry

    lax.fori_loop(0, CONVCH // 64, act_tile, 0)

    def mean_tile(h, total):
        rows = pl.ds(pl.multiple_of(h * HEAD_DIM, HEAD_DIM), HEAD_DIM)
        gate = z_ref[rows, :]
        skip = wide(heads_ref[2, pl.ds(h, 1), :])
        mixed = y_ref[rows, :] + skip * act[rows, :]
        opened = mixed * (gate * jax.nn.sigmoid(gate))
        return total + fold(dnormed[rows, :] * wide(inner_ref[rows, :]) * opened)

    inner_mean = lax.fori_loop(0, HEADS, mean_tile, jnp.zeros((8, STRIP), F32))
    inner_mean = jnp.sum(inner_mean, axis=0, keepdims=True) * (1.0 / INNER)

    def gate_tile(h, carry):
        rows = pl.ds(pl.multiple_of(h * HEAD_DIM, HEAD_DIM), HEAD_DIM)
        gate = z_ref[rows, :]
        skip = wide(heads_ref[2, pl.ds(h, 1), :])
        values = act[rows, :]
        y = y_ref[rows, :]
        mixed = y + skip * values
        sig = jax.nn.sigmoid(gate)
        sil = gate * sig
        opened = mixed * sil
        r = r_ref[0:1, :]
        dn = dnormed[rows, :]
        gained = dn * opened * r
        dinner_ref[rows, :] += gained[:, :CHUNK] + gained[:, CHUNK:]
        dopened = dn * wide(inner_ref[rows, :]) * r - opened * (r * r * r * inner_mean)
        dmixed = dopened * sil
        dy[rows, :] = dmixed
        dgate_ref[rows, :] = (dopened * mixed * (sig * (1.0 + gate * (1.0 - sig)))).astype(BF16)
        skipped = row_sum(dmixed * values)
        dheads_ref[2, pl.ds(h, 1), :] += skipped[:, :CHUNK] + skipped[:, CHUNK:]
        dlogs[pl.ds(h, 1), :] = row_sum(dmixed * y)
        return carry

    lax.fori_loop(0, HEADS, gate_tile, 0)
    causal = upper()
    ones = causal.astype(F32).astype(BF16)
    row = lax.broadcasted_iota(jnp.int32, (CHUNK, CHUNK), 0)
    col = lax.broadcasted_iota(jnp.int32, (CHUNK, CHUNK), 1)
    ones_back = (row >= col).astype(F32).astype(BF16)

    def chunk(step, carry):
        j = PER - 1 - step
        cols = pl.ds(pl.multiple_of(j * CHUNK, CHUNK), CHUNK)
        raw = raw_ref[0:HEADS, cols]
        steps, logs, columns, grown, to_end, through = rates_of(raw, heads_ref, ones)
        in_turned = act[INNER : INNER + NSTATE, cols]
        out_turned = act[INNER + NSTATE :, cols]
        in_map = in_turned.T
        out_map = out_turned.T
        scores = three_pass(in_map, right_pair(out_turned))
        in_pair = right_pair(in_turned)
        out_pair = right_pair(out_map)
        dscores = jnp.zeros((CHUNK, CHUNK), F32)
        din = jnp.zeros((NSTATE, CHUNK), F32)
        dout = jnp.zeros((NSTATE, CHUNK), F32)
        for g in range(HEADS // GROUP):
            rows = slice(g * GROUP * HEAD_DIM, (g + 1) * GROUP * HEAD_DIM)
            leaving = dstate[rows]
            entering = s_ref[j, rows]
            from_state = three_pass(leaving, in_pair)
            ending, growing, kept = [], [], []
            for q in range(GROUP):
                h = g * GROUP + q
                mine = slice(h * HEAD_DIM, (h + 1) * HEAD_DIM)
                values = act[mine, cols]
                fed = values * steps[h : h + 1]
                dys = dy[mine, cols]
                gaps = logs[h : h + 1] - jnp.broadcast_to(columns[:, h : h + 1], (CHUNK, CHUNK))
                decay = jnp.where(causal, jnp.exp(gaps), 0.0)
                weights = scores * decay
                both = dot_nt(stack_left(dys), beside(*split(weights)))
                du = both[:HEAD_DIM] + both[HEAD_DIM:]
                du = du + from_state[q * HEAD_DIM : (q + 1) * HEAD_DIM] * to_end[h : h + 1]
                fed_high, fed_low = split(fed)
                dy_high, dy_low = split(dys)
                dweights = dot_tn(
                    above(fed_high, fed_low, fed_high), above(dy_high, dy_high, dy_low)
                )
                dscores = dscores + dweights * decay
                vdu_rows[h : h + 1, :] = row_sum(values * du)
                dact[mine, cols] = du * steps[h : h + 1] + heads_ref[2][h : h + 1] * dys
                ending.append(fed * to_end[h : h + 1])
                growing.append(dys * grown[h : h + 1])
                kept.append(jnp.broadcast_to(through[h : h + 1], (HEAD_DIM, CHUNK)))
            ending = above(*ending)
            growing = above(*growing)
            end_high, end_low = split(ending)
            grow_high, grow_low = split(growing)
            leave_high, leave_low = split(leaving)
            enter_high, enter_low = split(entering)
            din = din + dot_tn(
                above(leave_high, leave_low, leave_high), above(end_high, end_high, end_low)
            )
            dout = dout + dot_tn(
                above(enter_high, enter_low, enter_high), above(grow_high, grow_high, grow_low)
            )
            arrived = leaving * above(*kept) + three_pass(growing, out_pair)
            dstate[rows] = arrived
            meet = arrived * entering
            for q in range(GROUP):
                h = g * GROUP + q
                dheads_ref[3, h : h + 1, :] = row_sum(meet[q * HEAD_DIM : (q + 1) * HEAD_DIM])
        vdu = vdu_rows[...]
        dlog = dlogs[:, cols] - steps * vdu
        drate = exact_sum(dlog, ones_back) + flow[...]
        flow[...] = jnp.broadcast_to(
            jnp.sum(dheads_ref[3], axis=1, keepdims=True), (HEADS, CHUNK)
        )
        dsteps = vdu + heads_ref[1] * drate
        draw = dsteps * jax.nn.sigmoid(raw + heads_ref[0])
        dheads_ref[0] += draw
        dheads_ref[1] += drate * steps * heads_ref[1]
        dstep_ref[:, cols] = above(draw, jnp.zeros((STEP - HEADS, CHUNK), F32)).astype(BF16)
        score_high, score_low = split(dscores)
        both = dot_nt(stack_left(out_turned), beside(score_high, score_low))
        dact[INNER : INNER + NSTATE, cols] = din + both[:NSTATE] + both[NSTATE:]
        both = dot(stack_left(in_turned), above(score_high, score_low))
        dact[INNER + NSTATE :, cols] = dout + both[:NSTATE] + both[NSTATE:]
        return carry

    lax.fori_loop(0, PER, chunk, 0)

    def conv_tile(i, carry):
        rows = pl.ds(pl.multiple_of(i * 64, 64), 64)
        c = c_ref[rows, :]
        sig = jax.nn.sigmoid(c)
        dpre = dact[rows, :] * (sig * (1.0 + c * (1.0 - sig)))
        cin = cin_ref[rows, :]
        ext = beside(dpre, tail[rows, :])
        dcin = dpre * wide(taps_ref[KCONV - 1, rows, :])
        grad = cin * dpre
        dtaps_ref[KCONV - 1, rows, :] += grad[:, :CHUNK] + grad[:, CHUNK:]
        dtaps_ref[KCONV, rows, :] += dpre[:, :CHUNK] + dpre[:, CHUNK:]
        for k in range(KCONV - 1):
            ahead = KCONV - 1 - k
            shifted = pltpu.roll(ext, STRIP + CHUNK - ahead, 1)[:, :STRIP]
            dcin = dcin + shifted * wide(taps_ref[k, rows, :])
            grad = cin * shifted
            dtaps_ref[k, rows, :] += grad[:, :CHUNK] + grad[:, CHUNK:]
        tail[rows, :] = dpre[:, :CHUNK]
        dconv_ref[rows, :] = dcin.astype(BF16)
        return carry

    lax.fori_loop(0, CONVCH // 64, conv_tile, 0)
    x = x_ref[...].astype(F32)
    r = lax.rsqrt(jnp.mean(x * x, axis=-1, keepdims=True) + EPSILON)
    parts = []
    for i in range(D // 256):
        part = slice(256 * i, 256 * i + 256)
        total = dot(first_ref[part, :INNER], dgate_ref[...])
        total = total + dot(first_ref[part, INNER:], dconv_ref[: HALF - INNER])
        total = total + dot(second_ref[part, :OUT_AT], dconv_ref[HALF - INNER :])
        step = second_ref[part, STEP_AT : STEP_AT + STEP]
        parts.append((total + dot(step, dstep_ref[...])).T)
    dscaled = beside(*parts)
    plain = x * r
    dgain_ref[...] += fold(dscaled * plain)
    gained = dscaled * gain_ref[...]
    inner = jnp.mean(gained * plain, axis=-1, keepdims=True)
    dx_ref[...] = back.astype(F32) + (gained - plain * inner) * r


def whole(shape):
    return pl.BlockSpec(shape, lambda i: (0,) * len(shape), pipeline_mode=pl.Buffered(1))


def strip_rows(width):
    return pl.BlockSpec((STRIP, width), lambda i: (i, 0))


def strip_cols(height):
    return pl.BlockSpec((height, STRIP), lambda i: (0, i))


def shape(*dims, dtype=F32):
    return jax.ShapeDtypeStruct(dims, dtype)


def half(k, *dims):
    return pl.BlockSpec((None,) + dims, lambda i: (k, 0, 0), pipeline_mode=pl.Buffered(1))


def forward_call(x, weights, weights_t, gain, taps, heads, inner):
    return pl.pallas_call(
        forward_kernel,
        grid=(STRIPS,),
        in_specs=[
            strip_rows(D), half(0, HALF, D), half(1, HALF, D), half(1, D, HALF), whole((1, D)),
            whole((KCONV + 1, CONVCH, CHUNK)), whole((3, HEADS, CHUNK)), whole((INNER, CHUNK)),
        ],
        out_specs=[
            strip_rows(D), strip_rows(D), strip_cols(INNER), strip_cols(CONVCH),
            strip_cols(CONVCH), strip_cols(STEP), strip_cols(INNER),
            pl.BlockSpec((PER, INNER, NSTATE), lambda i: (i, 0, 0)), strip_cols(INNER),
            strip_cols(8),
        ],
        out_shape=[
            shape(LEN, D, dtype=BF16), shape(LEN, D, dtype=BF16), shape(INNER, LEN),
            shape(CONVCH, LEN), shape(CONVCH, LEN), shape(STEP, LEN), shape(INNER, LEN),
            shape(LEN // CHUNK, INNER, NSTATE), shape(INNER, LEN, dtype=BF16), shape(8, LEN),
        ],
        scratch_shapes=[
            pltpu.VMEM((CONVCH, STRIP), F32), pltpu.VMEM((INNER, STRIP), F32),
            pltpu.VMEM((INNER, NSTATE), F32), pltpu.VMEM((CONVCH, CHUNK), F32),
        ],
        compiler_params=pltpu.CompilerParams(vmem_limit_bytes=56 * 2**20),
        name="mixer_forward",
    )(x, weights_t, weights_t, weights, gain, taps, heads, inner)


def backward_call(x, back, weights, weights_t, gain, taps, heads, inner, kept):
    last = STRIPS - 1

    def rows(width):
        return pl.BlockSpec((STRIP, width), lambda i: (last - i, 0))

    def cols(height):
        return pl.BlockSpec((height, STRIP), lambda i: (0, last - i))

    z, cin, c, raw, y, states, r = kept
    return pl.pallas_call(
        backward_kernel,
        grid=(STRIPS,),
        in_specs=[
            rows(D), rows(D), half(0, D, HALF), half(1, D, HALF), half(1, HALF, D),
            whole((1, D)), whole((KCONV + 1, CONVCH, CHUNK)), whole((3, HEADS, CHUNK)),
            whole((INNER, CHUNK)), cols(INNER), cols(CONVCH), cols(CONVCH), cols(STEP),
            cols(INNER), pl.BlockSpec((PER, INNER, NSTATE), lambda i: (last - i, 0, 0)), cols(8),
        ],
        out_specs=[
            rows(D), cols(INNER), cols(CONVCH), cols(STEP), whole((8, D)), whole((KCONV + 1, CONVCH, CHUNK)),
            whole((4, HEADS, CHUNK)), whole((INNER, CHUNK)),
        ],
        out_shape=[
            shape(LEN, D), shape(INNER, LEN, dtype=BF16), shape(CONVCH, LEN, dtype=BF16),
            shape(STEP, LEN, dtype=BF16),
            shape(8, D), shape(KCONV + 1, CONVCH, CHUNK), shape(4, HEADS, CHUNK),
            shape(INNER, CHUNK),
        ],
        scratch_shapes=[
            pltpu.VMEM((CONVCH, STRIP), F32), pltpu.VMEM((CONVCH, STRIP), F32),
            pltpu.VMEM((INNER, STRIP), F32), pltpu.VMEM((INNER, STRIP), F32),
            pltpu.VMEM((INNER, NSTATE), F32), pltpu.VMEM((HEADS, CHUNK), F32),
            pltpu.VMEM((CONVCH, CHUNK), F32), pltpu.VMEM((HEADS, STRIP), F32),
            pltpu.VMEM((HEADS, CHUNK), F32),
        ],
        compiler_params=pltpu.CompilerParams(vmem_limit_bytes=60 * 2**20),
        name="mixer_backward",
    )(x, back, weights, weights, weights_t, gain, taps, heads, inner, z, cin, c, raw, y, states, r)


def lanes(vector):
    return jnp.broadcast_to(vector[..., None], vector.shape + (CHUNK,))


def parameters(params):
    gain = params[:D].reshape(1, D)
    at = D
    taps = lanes(params[at : at + (KCONV + 1) * CONVCH].reshape(KCONV + 1, CONVCH))
    at += (KCONV + 1) * CONVCH
    heads = params[at : at + 3 * HEADS].reshape(3, HEADS)
    heads = lanes(jnp.stack([heads[0], -jnp.exp(heads[1]), heads[2]]))
    inner = lanes(params[at + 3 * HEADS :])
    return gain, taps, heads, inner


def block_and_gradients(x, back, weights, params):
    gain, taps, heads, inner = parameters(params)
    weights_t = weights.transpose(0, 2, 1)
    out, hb, z, cin, c, raw, y, states, normed, r = forward_call(
        x, weights, weights_t, gain, taps, heads, inner
    )
    dx, dgate, dconv, dstep, dgain, dtaps, dheads, dinner = backward_call(
        x, back, weights, weights_t, gain, taps, heads, inner, (z, cin, c, raw, y, states, r)
    )
    grad_out = dot(normed, back)
    grad_gate = dot(dgate, hb)
    grad_conv = dot(dconv, hb)
    grad_step = dot(dstep, hb)[:HEADS]
    small = jnp.concatenate(
        [
            jnp.sum(dgain, axis=0),
            jnp.sum(dtaps, axis=-1).reshape(-1),
            jnp.sum(dheads[:3], axis=-1).reshape(-1),
            jnp.sum(dinner, axis=-1),
        ]
    )
    return out, dx, grad_gate, grad_conv, grad_step, grad_out, small


MESH = pl.DeviceIdType.MESH


class Place:
    def __init__(self, sizes):
        self.Z, self.F = sizes
        self.C, self.Y = 2, 2
        self.X = self.F // 4
        f = lax.axis_index("fsdp")
        self.z = lax.axis_index("dp")
        self.c = lax.rem(f, 2)
        self.x = lax.rem(f // 2, self.X)
        self.y = f // (2 * self.X)
        self.f = f

    def at(self, z=None, y=None, x=None, c=None):
        z = self.z if z is None else z
        y = self.y if y is None else y
        x = self.x if x is None else x
        c = self.c if c is None else c
        return (z, (y * self.X + x) * 2 + c)

    def other_x(self, step):
        return lax.rem(self.x + step, self.X)


def signal(device):
    pl.semaphore_signal(
        pltpu.get_barrier_semaphore(), inc=1, device_id=device, device_id_type=MESH
    )


def greet_all(place):
    count = place.Z * place.F
    me = place.z * place.F + place.f

    def step(i, carry):
        peer = lax.rem(me + i, count)
        signal((peer // place.F, lax.rem(peer, place.F)))
        return carry

    lax.fori_loop(1, count, step, 0)
    pl.semaphore_wait(pltpu.get_barrier_semaphore(), count - 1)


def remote(src, dst, send, recv, device):
    return pltpu.make_async_remote_copy(
        src_ref=src, dst_ref=dst, send_sem=send, recv_sem=recv, device_id=device,
        device_id_type=MESH,
    )


def add_blocks(dst, src, count):
    def step(i, carry):
        target = dst(i)
        target[...] = target[...] + src(i)[...]
        return carry

    lax.fori_loop(0, count, step, 0)


class Swap:
    def __init__(self, place, src, dst, send, recv, local):
        self.place, self.src, self.dst = place, src, dst
        self.send, self.recv, self.local = send, recv, local
        self.count = place.Z * place.F
        self.me = place.z * place.F + place.f

    def to(self, i):
        peer = lax.rem(self.me + i, self.count)
        return remote(
            self.src.at[peer], self.dst.at[self.me], self.send.at[i], self.recv.at[i],
            (peer // self.place.F, lax.rem(peer, self.place.F)),
        )

    def start(self):
        pltpu.make_async_copy(self.src.at[self.me], self.dst.at[self.me], self.local).start()

        def step(i, carry):
            self.to(i).start()
            return carry

        lax.fori_loop(1, self.count, step, 0)

    def wait(self):
        pltpu.make_async_copy(self.src.at[self.me], self.dst.at[self.me], self.local).wait()

        def step(i, carry):
            sender = lax.rem(self.me + self.count - i, self.count)
            self.to(i).wait_send()
            remote(
                self.src.at[sender], self.dst.at[sender], self.send.at[i], self.recv.at[i],
                (sender // self.place.F, lax.rem(sender, self.place.F)),
            ).wait_recv()
            return carry

        lax.fori_loop(1, self.count, step, 0)


def swap_kernel(sizes, src, dst, send, recv, local):
    place = Place(sizes)
    greet_all(place)
    swap = Swap(place, src, dst, send, recv, local)
    swap.start()
    swap.wait()


def swap_call(blocks, sizes, collective_id):
    count = sizes[0] * sizes[1]
    return pl.pallas_call(
        functools.partial(swap_kernel, sizes),
        out_shape=jax.ShapeDtypeStruct(blocks.shape, blocks.dtype),
        in_specs=[pl.BlockSpec(memory_space=pl.ANY)],
        out_specs=pl.BlockSpec(memory_space=pl.ANY),
        scratch_shapes=[
            pltpu.SemaphoreType.DMA((count,)), pltpu.SemaphoreType.DMA((count,)),
            pltpu.SemaphoreType.DMA,
        ],
        compiler_params=pltpu.CompilerParams(collective_id=collective_id, has_side_effects=True),
        name="swap",
    )(blocks)


class Plane:
    def __init__(self, place, acc, x1, y1, x2, y2, sems):
        self.p, self.acc = place, acc
        self.x1, self.y1, self.x2, self.y2, self.sems = x1, y1, x2, y2, sems
        self.h = place.Z // 2

    def copies(self, stage):
        p, acc, h = self.p, self.acc, self.h
        low, high = pl.ds(0, h), pl.ds(h, p.Z - h)
        out = []
        base = stage * p.X
        for s in range(1, p.X):
            x = p.other_x(s)
            if stage == 0:
                src, dst = acc.at[low, :, x], self.x1.at[s - 1]
            else:
                src, dst = acc.at[high, p.y, x], self.x2.at[s - 1]
            sem = self.sems.at[base + s]
            out.append(remote(src, dst, sem.at[0], sem.at[1], p.at(x=x)))
        if stage == 0:
            src, dst = acc.at[high, 1 - p.y], self.y1
        else:
            src, dst = acc.at[low, 1 - p.y, p.x], self.y2
        sem = self.sems.at[base]
        out.append(remote(src, dst, sem.at[0], sem.at[1], p.at(y=1 - p.y)))
        return out

    def start(self, stage):
        for copy in self.copies(stage):
            copy.start()

    def finish(self, stage):
        p, acc, h = self.p, self.acc, self.h
        for copy in self.copies(stage):
            copy.wait()
        for s in range(p.X - 1):
            if stage == 0:
                add_blocks(
                    lambda i: acc.at[i // p.Y, lax.rem(i, p.Y), p.x],
                    lambda i: self.x1.at[s, i // p.Y, lax.rem(i, p.Y)],
                    h * p.Y,
                )
            else:
                add_blocks(
                    lambda i: acc.at[h + i, p.y, p.x], lambda i: self.x2.at[s, i], p.Z - h
                )
        if stage == 0:
            add_blocks(
                lambda i: acc.at[h + i // p.X, p.y, lax.rem(i, p.X)],
                lambda i: self.y1.at[i // p.X, lax.rem(i, p.X)],
                (p.Z - h) * p.X,
            )
        else:
            add_blocks(lambda i: acc.at[i, p.y, p.x], lambda i: self.y2.at[i], h)


def plane_scratch(sizes, block):
    Z, X, Y = sizes[0], sizes[1] // 4, 2
    h = Z // 2
    return [
        pltpu.VMEM((Z, Y, X) + block, F32), pltpu.VMEM((X - 1, h, Y) + block, F32),
        pltpu.VMEM((Z - h, X) + block, F32), pltpu.VMEM((X - 1, Z - h) + block, F32),
        pltpu.VMEM((h,) + block, F32), pltpu.SemaphoreType.DMA((2 * X, 2)),
    ]


def scatter_kernel(sizes, parts, *refs):
    ins, outs, rest = refs[:parts], refs[parts : 2 * parts], refs[2 * parts :]
    p = Place(sizes)
    Z = p.Z
    work = [rest[10 * k : 10 * k + 10] for k in range(parts)]
    signal(p.at(c=1 - p.c))
    signal(p.at(y=1 - p.y))
    for s in range(1, p.X):
        signal(p.at(x=p.other_x(s)))

    for s in range(1, Z):
        signal(p.at(z=lax.rem(p.z + s, Z)))
    pl.semaphore_wait(pltpu.get_barrier_semaphore(), p.X + Z)

    def core_copies(k):
        acc, core, sems = work[k][0], work[k][6], work[k][7]
        return (
            remote(
                ins[k].at[:, :, :, 1 - p.c], core, sems.at[0], sems.at[1], p.at(c=1 - p.c)
            ),
            pltpu.make_async_copy(ins[k].at[:, :, :, p.c], acc, sems.at[2]),
        )

    for k in range(parts):
        for copy in core_copies(k):
            copy.start()
    planes = [Plane(p, *work[k][:6]) for k in range(parts)]
    for k in range(parts):
        for copy in core_copies(k):
            copy.wait()
        acc, core = work[k][0], work[k][6]

        def place_of(i):
            return i // (p.Y * p.X), lax.rem(i // p.X, p.Y), lax.rem(i, p.X)

        add_blocks(
            lambda i: acc.at[place_of(i)], lambda i: core.at[place_of(i)], Z * p.Y * p.X
        )
        planes[k].start(0)
    for k in range(parts):
        planes[k].finish(0)
        planes[k].start(1)

    def flow(k, t, right):
        acc, held, sems = work[k][0], work[k][8], work[k][9]
        side = 0 if right else 1
        target = p.z + 1 if right else p.z - 1
        sem = sems.at[side, t]
        return remote(
            acc.at[t, p.y, p.x], held.at[side, t], sem.at[0], sem.at[1], p.at(z=target)
        )

    def send(k, t, right):
        @pl.when(p.z < t if right else p.z > t)
        def _():
            flow(k, t, right).start()

    def receive(k, t, right):
        acc, held = work[k][0], work[k][8]

        @pl.when(jnp.logical_and(p.z > 0, p.z <= t) if right else
                 jnp.logical_and(p.z < Z - 1, p.z >= t))
        def _():
            flow(k, t, right).wait_recv()
            mine = acc.at[t, p.y, p.x]
            mine[...] = mine[...] + held[0 if right else 1, t]

    def pass_on(k, j, right):
        t = Z - 1 - j if right else j
        receive(k, t, right)

        @pl.when(p.z > 0 if right else p.z < Z - 1)
        def _():
            send(k, t, right)

    for k in range(parts):
        planes[k].finish(1)
        for j in range(Z - 1):
            @pl.when(p.z == 0)
            def _():
                send(k, Z - 1 - j, True)

            @pl.when(p.z == Z - 1)
            def _():
                send(k, j, False)

    for k in range(parts):
        for j in range(Z):
            @pl.when(p.z < Z // 2)
            def _():
                pass_on(k, j, True)
                pass_on(k, j, False)

            @pl.when(p.z >= Z // 2)
            def _():
                pass_on(k, j, False)
                pass_on(k, j, True)

        for j in range(Z):
            for right in (True, False):
                @pl.when(p.z < j if right else p.z > j)
                def _():
                    flow(k, j, right).wait_send()

        outs[k][...] = work[k][0][p.z, p.y, p.x]


def scatter_call(blocks, sizes, collective_id):
    Z, F = sizes
    X, Y = F // 4, 2
    ins = [b.reshape((Z, Y, X, 2) + b.shape[1:]) for b in blocks]
    scratch = []
    for b in blocks:
        block = b.shape[1:]
        scratch += plane_scratch(sizes, block)
        scratch += [
            pltpu.VMEM((Z, Y, X) + block, F32), pltpu.SemaphoreType.DMA((3,)),
            pltpu.VMEM((2, Z) + block, F32), pltpu.SemaphoreType.DMA((2, Z, 2)),
        ]
    return pl.pallas_call(
        functools.partial(scatter_kernel, sizes, len(blocks)),
        out_shape=[jax.ShapeDtypeStruct(b.shape[1:], F32) for b in blocks],
        in_specs=[pl.BlockSpec(memory_space=pl.ANY)] * len(blocks),
        out_specs=[pl.BlockSpec(memory_space=pltpu.VMEM)] * len(blocks),
        scratch_shapes=scratch,
        compiler_params=pltpu.CompilerParams(
            collective_id=collective_id, has_side_effects=True, vmem_limit_bytes=56 * 2**20
        ),
        name="scatter",
    )(*ins)


def sum_kernel(
    sizes, gram_ref, give_ref, blocks_ref, out_ref, given_ref, moved_ref,
    sum_ref, acc, x1, y1, x2, y2, sems, core, core_sems, held, z_sems, back_sems, swap_send, swap_recv, local,
):
    p = Place(sizes)
    Z, h = p.Z, p.Z // 2
    low, high = pl.ds(0, h), pl.ds(h, Z - h)
    greet_all(p)
    partner = p.at(c=1 - p.c)
    first = [
        remote(gram_ref.at[1 - p.c], core, core_sems.at[0], core_sems.at[1], partner),
        remote(give_ref, given_ref, core_sems.at[2], core_sems.at[3], partner),
        pltpu.make_async_copy(gram_ref.at[p.c], acc, core_sems.at[4]),
    ]
    for copy in first:
        copy.start()
    swap = Swap(p, blocks_ref, moved_ref, swap_send, swap_recv, local)
    for copy in first:
        copy.wait()

    def place_of(i):
        return i // (p.Y * p.X), lax.rem(i // p.X, p.Y), lax.rem(i, p.X)

    add_blocks(lambda i: acc.at[place_of(i)], lambda i: core.at[place_of(i)], Z * p.Y * p.X)
    plane = Plane(p, acc, x1, y1, x2, y2, sems)
    plane.start(0)
    plane.finish(0)
    plane.start(1)
    swap.start()
    plane.finish(1)

    def over(s):
        z = lax.rem(p.z + s, Z)
        return remote(
            acc.at[z, p.y, p.x], held.at[s - 1], z_sems.at[0, s, 0], z_sems.at[0, s, 1], p.at(z=z)
        )

    for s in range(1, Z):
        over(s).start()
    for s in range(1, Z):
        over(s).wait()
    total = acc[p.z, p.y, p.x]
    for s in range(1, Z):
        total = total + held[s - 1]
    sum_ref[p.z, p.y, p.x] = total

    def back(s):
        z = lax.rem(p.z + s, Z)
        mine = sum_ref.at[p.z, p.y, p.x]
        return remote(mine, mine, z_sems.at[1, s, 0], z_sems.at[1, s, 1], p.at(z=z))

    for s in range(1, Z):
        back(s).start()
    for s in range(1, Z):
        back(s).wait_send()
        z = lax.rem(p.z + Z - s, Z)
        theirs = sum_ref.at[z, p.y, p.x]
        remote(theirs, theirs, z_sems.at[1, s, 0], z_sems.at[1, s, 1], p.at(z=z)).wait_recv()

    def spread(stage, start):
        for s in range(1, p.X):
            sem = back_sems.at[stage * p.X + s]
            mine, theirs = (
                sum_ref.at[high, p.y, x] if stage == 0 else sum_ref.at[low, :, x]
                for x in (p.x, lax.rem(p.x + p.X - s, p.X))
            )
            copy = remote(mine, mine, sem.at[0], sem.at[1], p.at(x=p.other_x(s)))
            if start:
                copy.start()
            else:
                copy.wait_send()
                remote(theirs, theirs, sem.at[0], sem.at[1], p.at(x=p.other_x(s))).wait_recv()
        sem = back_sems.at[stage * p.X]
        mine, theirs = (
            sum_ref.at[low, y, p.x] if stage == 0 else sum_ref.at[high, y]
            for y in (p.y, 1 - p.y)
        )
        copy = remote(mine, mine, sem.at[0], sem.at[1], p.at(y=1 - p.y))
        if start:
            copy.start()
        else:
            copy.wait_send()
            remote(theirs, theirs, sem.at[0], sem.at[1], p.at(y=1 - p.y)).wait_recv()

    for stage in range(2):
        spread(stage, True)
        spread(stage, False)
    out_ref[...] = sum_ref[...]
    swap.wait()


def sum_call(grams, give, blocks, sizes, collective_id):
    Z, F = sizes
    X, Y = F // 4, 2
    block = grams.shape[2:]
    count = Z * F
    return pl.pallas_call(
        functools.partial(sum_kernel, sizes),
        out_shape=[
            jax.ShapeDtypeStruct((Z, Y, X) + block, F32), jax.ShapeDtypeStruct(give.shape, F32),
            jax.ShapeDtypeStruct(blocks.shape, F32),
        ],
        in_specs=[pl.BlockSpec(memory_space=pl.ANY)] * 3,
        out_specs=[
            pl.BlockSpec(memory_space=pltpu.VMEM), pl.BlockSpec(memory_space=pl.ANY),
            pl.BlockSpec(memory_space=pl.ANY),
        ],
        scratch_shapes=[pltpu.VMEM((Z, Y, X) + block, F32)]
        + plane_scratch(sizes, block)
        + [
            pltpu.VMEM((Z, Y, X) + block, F32), pltpu.SemaphoreType.DMA((5,)),
            pltpu.VMEM((Z - 1,) + block, F32), pltpu.SemaphoreType.DMA((2, Z, 2)),
            pltpu.SemaphoreType.DMA((2 * X, 2)), pltpu.SemaphoreType.DMA((count,)),
            pltpu.SemaphoreType.DMA((count,)), pltpu.SemaphoreType.DMA,
        ],
        compiler_params=pltpu.CompilerParams(
            collective_id=collective_id, has_side_effects=True, vmem_limit_bytes=56 * 2**20
        ),
        name="gram_sum",
    )(grams.reshape((2, Z, Y, X) + block), give, blocks)


def gather_kernel(
    sizes, w_in_ref, w_out_ref, blocks_ref, all_ref, moved_ref,
    both, mine, core_sems, z_sems, near, far, across, swap_send, swap_recv, local,
):
    p = Place(sizes)
    Z, h = p.Z, p.Z // 2
    greet_all(p)
    own = both.shape[1]
    both[p.c, :, :WIDE] = w_in_ref[:, :WIDE]
    both[p.c, :, WIDE : WIDE + INNER] = w_out_ref[...]
    both[p.c, :, WIDE + INNER :] = jnp.concatenate(
        [w_in_ref[:, WIDE:], jnp.zeros((own, 2 * HALF - IN_W - INNER), F32)], axis=1
    )
    partner = p.at(c=1 - p.c)
    pair = remote(
        both.at[p.c], both.at[p.c], core_sems.at[0], core_sems.at[1], partner
    )
    pair.start()
    pair.wait_send()
    other = both.at[1 - p.c]
    remote(other, other, core_sems.at[0], core_sems.at[1], partner).wait_recv()
    for k in range(2):
        cols = slice(k * HALF, k * HALF + HALF)
        mine[k] = above(both[0, :, cols], both[1, :, cols]).astype(BF16)
    keeps = [
        pltpu.make_async_copy(mine.at[k], all_ref.at[k, p.z, p.y, p.x], core_sems.at[2 + k])
        for k in range(2)
    ]
    for keep in keeps:
        keep.start()

    def spot(z, y, x):
        return all_ref.at[p.c, z, y, x]

    def copy(src, dst, sem, device):
        return remote(src, dst, sem.at[0], sem.at[1], device)

    def along_z(z, right, src=None):
        here = spot(z, p.y, p.x)
        target = p.at(z=p.z + 1 if right else p.z - 1)
        return copy(here if src is None else src, here, z_sems.at[0 if right else 1, z], target)

    def near_copies(z, src=None):
        here = spot(z, p.y, p.x)
        src = here if src is None else src
        found = [copy(src, here, near.at[z, 0], p.at(y=1 - p.y))]
        for s in range(1, p.X):
            found.append(copy(src, here, near.at[z, s], p.at(x=p.other_x(s))))
        return found

    def near_arrivals(z):
        found = [(z, 1 - p.y, p.x, near.at[z, 0])]
        for s in range(1, p.X):
            found.append((z, p.y, lax.rem(p.x + p.X - s, p.X), near.at[z, s]))
        return found

    def far_copies(z):
        low, high = [], []
        for s in range(1, p.X):
            x = p.other_x(s)
            there = spot(z, p.y, x)
            low.append(copy(there, there, far.at[z, s], p.at(y=1 - p.y)))
            there = spot(z, 1 - p.y, p.x)
            high.append(copy(there, there, far.at[z, s], p.at(x=x)))
        return low, high

    def far_arrivals(z):
        low = [(z, 1 - p.y, p.other_x(s), far.at[z, s]) for s in range(1, p.X)]
        high = [
            (z, 1 - p.y, lax.rem(p.x + p.X - s, p.X), far.at[z, s]) for s in range(1, p.X)
        ]
        return low, high

    def to_partner(z, y, x):
        here = spot(z, y, x)
        return copy(here, here, across.at[z, y, x], partner)

    def await_block(z, y, x, sem):
        here = spot(z, y, x)
        copy(here, here, sem, partner).wait_recv()
        to_partner(z, y, x).start()

    def start_all(copies):
        for c in copies:
            c.start()

    @pl.when(p.z < Z - 1)
    def _():
        along_z(p.z, True, mine.at[p.c]).start()

    @pl.when(p.z > 0)
    def _():
        along_z(p.z, False, mine.at[p.c]).start()

    start_all(near_copies(p.z, mine.at[p.c]))
    swap = Swap(p, blocks_ref, moved_ref, swap_send, swap_recv, local)
    swap.start()

    def visit(right, z):
        await_block(z, p.y, p.x, z_sems.at[0 if right else 1, z])

        @pl.when(p.z < Z - 1 if right else p.z > 0)
        def _():
            along_z(z, right).start()

        start_all(near_copies(z))

    def by_distance(low, high):
        for j in range(1, Z):
            @pl.when(p.z - j >= 0)
            def _():
                low(p.z - j)

            @pl.when(p.z + j < Z)
            def _():
                high(p.z + j)

    by_distance(lambda z: visit(True, z), lambda z: visit(False, z))

    def relay(z):
        for block in near_arrivals(z):
            await_block(*block)
        low, high = far_copies(z)

        @pl.when(z < h)
        def _():
            start_all(low)

        @pl.when(z >= h)
        def _():
            start_all(high)

    relay(p.z)
    by_distance(relay, relay)

    def settle(z):
        low, high = far_arrivals(z)

        @pl.when(z < h)
        def _():
            for block in low:
                await_block(*block)

        @pl.when(z >= h)
        def _():
            for block in high:
                await_block(*block)

    settle(p.z)
    by_distance(settle, settle)
    for keep in keeps:
        keep.wait()

    def finish(z, carry):
        for c in near_copies(z):
            c.wait_send()
        low, high = far_copies(z)

        @pl.when(z < h)
        def _():
            for c in low:
                c.wait_send()

        @pl.when(z >= h)
        def _():
            for c in high:
                c.wait_send()

        @pl.when(jnp.logical_and(z <= p.z, p.z < Z - 1))
        def _():
            along_z(z, True).wait_send()

        @pl.when(jnp.logical_and(z >= p.z, p.z > 0))
        def _():
            along_z(z, False).wait_send()

        for y in range(p.Y):
            for x in range(p.X):
                @pl.when(jnp.logical_not(jnp.logical_and(
                    z == p.z, jnp.logical_and(p.y == y, p.x == x))))
                def _():
                    to_partner(z, y, x).wait_send()
                    theirs = all_ref.at[1 - p.c, z, y, x]
                    copy(theirs, theirs, across.at[z, y, x], partner).wait_recv()

        return carry

    lax.fori_loop(0, Z, finish, 0)
    swap.wait()


def gather_call(weight_in, weight_out, blocks, sizes, collective_id):
    Z, F = sizes
    X, Y = F // 4, 2
    own = weight_in.shape[0]
    count = Z * F
    vmem = pl.BlockSpec(memory_space=pltpu.VMEM)
    hbm = pl.BlockSpec(memory_space=pl.ANY)
    whole_weights, moved = pl.pallas_call(
        functools.partial(gather_kernel, sizes),
        out_shape=[
            jax.ShapeDtypeStruct((2, Z, Y, X, 2 * own, HALF), BF16),
            jax.ShapeDtypeStruct(blocks.shape, F32),
        ],
        in_specs=[vmem, vmem, hbm],
        out_specs=[hbm, hbm],
        scratch_shapes=[
            pltpu.VMEM((2, own, 2 * HALF), F32), pltpu.VMEM((2, 2 * own, HALF), BF16),
            pltpu.SemaphoreType.DMA((4,)), pltpu.SemaphoreType.DMA((2, Z, 2)),
            pltpu.SemaphoreType.DMA((Z, X, 2)), pltpu.SemaphoreType.DMA((Z, X, 2)),
            pltpu.SemaphoreType.DMA((Z, Y, X, 2)), pltpu.SemaphoreType.DMA((count,)),
            pltpu.SemaphoreType.DMA((count,)), pltpu.SemaphoreType.DMA,
        ],
        compiler_params=pltpu.CompilerParams(
            collective_id=collective_id, has_side_effects=True, vmem_limit_bytes=40 * 2**20
        ),
        name="weights_gather",
    )(weight_in, weight_out, blocks)
    return whole_weights.reshape(2, D, HALF), moved


def pack(gram):
    rows = []
    for i in range(D // 256):
        a, b = 128 * i, D - 128 * (i + 1)
        rows.append(beside(gram[a : a + 128, a:], gram[b : b + 128, b:]))
    return above(*rows)


def unpack(packed):
    rows = [None] * (D // 128)
    for i in range(D // 256):
        pair = packed[128 * i : 128 * i + 128]
        wide_part, j = D - 128 * i, D // 128 - 1 - i
        rows[i] = jnp.pad(pair[:, :wide_part], ((0, 0), (128 * i, 0)))
        rows[j] = jnp.pad(pair[:, wide_part:], ((0, 0), (128 * j, 0)))
    half = above(*rows)
    at = lax.broadcasted_iota(jnp.int32, (D, D), 0) // 128
    to = lax.broadcasted_iota(jnp.int32, (D, D), 1) // 128
    return jnp.where(at <= to, half, half.T)


def iterate(first_gram, slabs):
    high = lax.Precision.HIGH
    scale = 1.0 / (jnp.sqrt(jnp.trace(first_gram)) + 1e-07)
    gram = first_gram * (scale * scale)
    slabs = slabs * scale
    eye = jnp.eye(gram.shape[0], dtype=F32)
    for iteration in range(ITERS):
        if iteration == ITERS - 1:
            once = jnp.dot(slabs, gram, precision=high)
            twice = jnp.dot(once, gram, precision=high)
            slabs = COEF_A * slabs + COEF_B * once + COEF_C * twice
        else:
            square = jnp.dot(gram, gram, precision=high)
            factor = COEF_A * eye + COEF_B * gram + COEF_C * square
            slabs = jnp.dot(slabs, factor, precision=high)
            half = jnp.dot(factor, gram, precision=high)
            gram = jnp.dot(half, factor, precision=high)
    return slabs


def gram_of(slab):
    return lax.dot_general(slab, slab, (((0,), (0,)), ((), ())), precision=lax.Precision.HIGH)


def spread_columns(rows, count):
    return rows.reshape(rows.shape[0], count, -1).transpose(1, 0, 2)


def gather_columns(blocks):
    return blocks.transpose(1, 0, 2).reshape(blocks.shape[1], -1)


def lanes_256(blocks):
    return jnp.pad(blocks, ((0, 0), (0, 0), (0, 256 - blocks.shape[2])))


def shards(
    inputs, cotangent, weight_in, weight_out, small_params, moment_in, moment_out, moment_small
):
    sizes = (lax.axis_size("dp"), lax.axis_size("fsdp"))
    count = sizes[0] * sizes[1]
    in_core = lax.rem(lax.axis_index("fsdp"), 2) == 0
    own = weight_in.shape[0]
    gates, convs = INNER // count, CONVCH // count
    ins = gates + convs
    old = jnp.concatenate(
        [
            spread_columns(moment_in[:, :INNER], count),
            spread_columns(moment_in[:, INNER:WIDE], count),
            spread_columns(moment_out, count),
            jnp.broadcast_to(moment_in[:, WIDE:], (count, own, HEADS)),
        ],
        axis=2,
    )
    weights, old = gather_call(weight_in, weight_out, lanes_256(old), sizes, 0)
    old = old.reshape(D, 256)[:, : ins + gates + HEADS].T
    output, dx, part_gate, part_conv, part_step, part_out, part_small = block_and_gradients(
        inputs[0], cotangent[0], weights, small_params
    )
    outputs, input_grad = output[None], dx[None]

    per = -(-(small_params.shape[0] + HEADS * D) // D)
    part_small = jnp.concatenate([part_small, part_step.reshape(-1)])
    part_small = jnp.pad(part_small, (0, D * per - part_small.shape[0])).reshape(count, own * per)
    part_small = jnp.pad(part_small, ((0, 0), (0, 1024 - own * per))).reshape(count, 8, 128)
    new_out, new_gate, new_conv, new_small = scatter_call(
        [
            part_out.reshape(count, gates, D), part_gate.reshape(count, gates, D),
            part_conv.reshape(count, convs, D), part_small,
        ],
        sizes,
        1,
    )

    def push(gradient, moment):
        return gradient + MOMENTUM * (MOMENTUM * moment + gradient)

    new_in = above(new_gate, new_conv)
    push_in = push(new_in, old[:ins])
    push_out = push(new_out, old[ins : ins + gates])
    give = jnp.where(in_core, jnp.pad(push_out, ((0, ins - gates), (0, 0))), push_in)
    message = jnp.concatenate(
        [
            above(new_in, new_out).T.reshape(count, own, ins + gates),
            jnp.broadcast_to(
                new_small.reshape(-1)[: own * per].reshape(own, per), (count, own, per)
            ),
        ],
        axis=2,
    )
    grams = jnp.stack([pack(gram_of(push_in)), pack(gram_of(push_out))])
    grams = grams.reshape(2, count // 2, -1, grams.shape[2])
    gram, given, moved = sum_call(grams, give, lanes_256(message), sizes, 2)
    small = moved[:, :, ins + gates : ins + gates + per].reshape(-1)
    grad_small = small[: small_params.shape[0]]
    new_step = small[grad_small.shape[0] : grad_small.shape[0] + HEADS * D].reshape(HEADS, D)
    push_step = push(new_step, old[ins + gates :])
    gram = unpack(gram.reshape(-1, gram.shape[-1]))
    gram = gram + jnp.where(in_core, gram_of(push_step), 0.0)
    slab_in = above(push_in, given, push_step)
    slab_out = above(given[:gates], push_out, jnp.zeros((2 * convs + HEADS, D), F32))
    ortho = iterate(gram, jnp.where(in_core, slab_in, slab_out))
    spread = swap_call(lanes_256(ortho.T.reshape(count, own, -1)), sizes, 3)

    def rows_in(gate_blocks, conv_blocks, step_rows):
        return beside(gather_columns(gate_blocks), gather_columns(conv_blocks), step_rows)

    evens, odds = spread[0::2], spread[1::2]
    direction_in = rows_in(
        jnp.concatenate([evens[:, :, :gates], evens[:, :, ins : ins + gates]], axis=2),
        jnp.concatenate([evens[:, :, gates:ins], evens[:, :, ins + gates : 2 * ins]], axis=2),
        evens[0, :, 2 * ins : 2 * ins + HEADS],
    )
    direction_out = gather_columns(odds[:, :, : 2 * gates])
    first_row = (lax.axis_index("dp") * sizes[1] + lax.axis_index("fsdp")) * own
    grad_in = rows_in(
        moved[:, :, :gates],
        moved[:, :, gates:ins],
        lax.dynamic_slice_in_dim(new_step, first_row, own, 1).T,
    )
    grad_out = gather_columns(moved[:, :, ins : ins + gates])
    new_moment_in = MOMENTUM * moment_in + grad_in
    new_moment_out = MOMENTUM * moment_out + grad_out
    decay = 1.0 - MATRIX_RATE * WEIGHT_DECAY
    new_weight_in = weight_in * decay - MATRIX_RATE * 0.2 * math.sqrt(max(D, IN_W)) * direction_in
    new_weight_out = (
        weight_out * decay - MATRIX_RATE * 0.2 * math.sqrt(max(D, INNER)) * direction_out
    )
    new_moment_small = MOMENTUM * moment_small + grad_small
    new_small_params = small_params - SMALL_RATE * new_moment_small
    return (
        outputs,
        input_grad,
        grad_in,
        grad_out,
        grad_small,
        new_moment_in,
        new_moment_out,
        new_moment_small,
        new_weight_in,
        new_weight_out,
        new_small_params,
    )


def solution(mesh):
    return jax.shard_map(
        shards,
        mesh=mesh,
        in_specs=(
            P(("dp", "fsdp"), None, None),
            P(("dp", "fsdp"), None, None),
            P(("dp", "fsdp"), None),
            P(("dp", "fsdp"), None),
            P(),
            P(("dp", "fsdp"), None),
            P(("dp", "fsdp"), None),
            P(),
        ),
        out_specs=(
            P(("dp", "fsdp"), None, None),
            P(("dp", "fsdp"), None, None),
            P(("dp", "fsdp"), None),
            P(("dp", "fsdp"), None),
            P(),
            P(("dp", "fsdp"), None),
            P(("dp", "fsdp"), None),
            P(),
            P(("dp", "fsdp"), None),
            P(("dp", "fsdp"), None),
            P(),
        ),
        check_vma=False,
    )
```

```python
import functools
import math

import jax
import jax.numpy as jnp
from jax import lax
from jax.experimental import pallas as pl
from jax.experimental.pallas import tpu as pltpu
from jax.sharding import PartitionSpec as P

D = 768
HEADS = 24
HEAD_DIM = 64
NSTATE = 128
KCONV = 4
LEN = 1024
ITERS = 5
INNER = 1536
CONVCH = 1792
IN_W = 3352
WIDE = INNER + CONVCH
STEP = 32
HALF = 2560
OUT_AT = WIDE - HALF
STEP_AT = OUT_AT + INNER

MOMENTUM = 0.95
MATRIX_RATE = 0.15
WEIGHT_DECAY = 0.1
SMALL_RATE = 0.01
EPSILON = 1e-05
COEF_A = 3.4445
COEF_B = -4.775
COEF_C = 2.0315

F32 = jnp.float32
BF16 = jnp.bfloat16
CHUNK = 128
STRIP = 256
PER = STRIP // CHUNK
STRIPS = LEN // STRIP
GROUP = 4


def dot(a, b):
    return lax.dot_general(a, b, (((1,), (0,)), ((), ())), preferred_element_type=F32)


def dot_nt(a, b):
    return lax.dot_general(a, b, (((1,), (1,)), ((), ())), preferred_element_type=F32)


def dot_tn(a, b):
    return lax.dot_general(a, b, (((0,), (0,)), ((), ())), preferred_element_type=F32)


def split(v):
    high = v.astype(BF16)
    return high, (v - high.astype(F32)).astype(BF16)


def beside(*parts):
    return jnp.concatenate(parts, axis=1)


def above(*parts):
    return jnp.concatenate(parts, axis=0)


def right_pair(b):
    high, low = split(b)
    return above(beside(high, low), beside(high, jnp.zeros_like(low)))


def three_pass(a, pair):
    high, low = split(a)
    both = dot(beside(high, low), pair)
    half = both.shape[1] // 2
    return both[:, :half] + both[:, half:]


def exact_sum(a, ones):
    high = a.astype(BF16)
    rest = a - high.astype(F32)
    mid = rest.astype(BF16)
    low = (rest - mid.astype(F32)).astype(BF16)
    return dot(beside(high, mid, low), above(ones, ones, ones))


def stack_left(a):
    high, low = split(a)
    return above(beside(high, high), beside(low, jnp.zeros_like(low)))


def fold(rows):
    total = rows[0:8]
    for i in range(1, rows.shape[0] // 8):
        total = total + rows[8 * i : 8 * i + 8]
    return total


def row_sum(rows):
    return jnp.sum(fold(rows), axis=0, keepdims=True)


def upper():
    row = lax.broadcasted_iota(jnp.int32, (CHUNK, CHUNK), 0)
    col = lax.broadcasted_iota(jnp.int32, (CHUNK, CHUNK), 1)
    return col >= row


def softplus(v):
    return jnp.maximum(v, 0.0) + jnp.log1p(jnp.exp(-jnp.abs(v)))


def rates_of(raw, heads_ref, ones):
    steps = softplus(raw + heads_ref[0])
    logs = exact_sum(steps * heads_ref[1], ones)
    last = jnp.broadcast_to(logs[:, CHUNK - 1 : CHUNK], logs.shape)
    columns = above(logs, jnp.zeros((CHUNK - HEADS, CHUNK), F32)).T
    return steps, logs, columns, jnp.exp(logs), jnp.exp(last - logs), jnp.exp(last)


def wide(v):
    return beside(*([v] * PER))


def forward_kernel(
    x_ref, back_ref, first_ref, second_ref, gain_ref, taps_ref, heads_ref, inner_ref,
    out_ref, hb_ref, cin_ref, c_ref, raw_ref, s_ref, normed_ref,
    dy_ref, dgate_ref, dlogs_ref, dskip_ref, dinner_ref,
    act, z, mixed, dnormed, state, tail, turned,
):
    @pl.when(pl.program_id(0) == 0)
    def _():
        state[...] = jnp.zeros_like(state)
        tail[...] = jnp.zeros_like(tail)
        dskip_ref[...] = jnp.zeros_like(dskip_ref)
        dinner_ref[...] = jnp.zeros_like(dinner_ref)
        for i in range(HALF // 256):
            part = slice(256 * i, 256 * i + 256)
            turned[0, part] = first_ref[:, part].T
            turned[1, part] = second_ref[:, part].T

    x = x_ref[...].astype(F32)
    scaled = x * lax.rsqrt(jnp.mean(x * x, axis=-1, keepdims=True) + EPSILON) * gain_ref[...]
    hb = scaled.astype(BF16)
    hb_ref[...] = hb
    back = back_ref[...]
    for i in range(INNER // 256):
        part = slice(256 * i, 256 * i + 256)
        z[part] = dot_nt(turned[0, part], hb)
        dnormed[part] = dot_nt(turned[1, OUT_AT + 256 * i : OUT_AT + 256 * i + 256], back)
    for i in range(CONVCH // 256):
        start = INNER + 256 * i
        rows = turned[start // HALF, start % HALF : start % HALF + 256]
        cin_ref[256 * i : 256 * i + 256] = dot_nt(rows, hb)
    raw_ref[...] = dot_nt(turned[1, STEP_AT : STEP_AT + STEP], hb)

    lane = lax.broadcasted_iota(jnp.int32, (64, CHUNK), 1)

    def later(cols, steps, before):
        turned_cols = [before] + [pltpu.roll(col, steps, 1) for col in cols]
        pairs = zip(turned_cols[:-1], turned_cols[1:])
        return [jnp.where(lane < steps, a, b) for a, b in pairs], turned_cols[-1]

    def conv_tile(i, carry):
        rows = pl.ds(pl.multiple_of(i * 64, 64), 64)
        cur = cin_ref[rows, :]
        cols = [cur[:, CHUNK * j : CHUNK * j + CHUNK] for j in range(PER)]
        taps = [taps_ref[k, rows, :] for k in range(KCONV + 1)]
        ones_late, tail[0, rows, :] = later(cols, 1, tail[0, rows, :])
        early = [taps[1] * a + taps[0] * b for a, b in zip(cols, ones_late)]
        twos_late, tail[1, rows, :] = later(early, 2, tail[1, rows, :])
        total = beside(*[
            taps[4] + c + taps[2] * b + taps[3] * a for a, b, c in zip(cols, ones_late, twos_late)
        ])
        c_ref[rows, :] = total
        act[rows, :] = total * jax.nn.sigmoid(total)
        return carry

    lax.fori_loop(0, CONVCH // 64, conv_tile, 0, unroll=4)
    causal = upper()
    ones = causal.astype(F32).astype(BF16)

    def chunk(j, carry):
        cols = pl.ds(pl.multiple_of(j * CHUNK, CHUNK), CHUNK)
        steps, logs, columns, grown, to_end, through = rates_of(
            raw_ref[0:HEADS, cols], heads_ref, ones
        )
        in_map = act[INNER : INNER + NSTATE, cols].T
        in_pair = right_pair(in_map)
        out_pair = right_pair(act[INNER + NSTATE :, cols])
        scores = three_pass(in_map, out_pair)
        for g in range(HEADS // GROUP):
            rows = slice(g * GROUP * HEAD_DIM, (g + 1) * GROUP * HEAD_DIM)
            held = state[rows]
            s_ref[j, rows] = held
            across = three_pass(held, out_pair)
            ending, kept = [], []
            for q in range(GROUP):
                h = g * GROUP + q
                mine = slice(h * HEAD_DIM, (h + 1) * HEAD_DIM)
                values = act[mine, cols]
                fed = values * steps[h : h + 1]
                gaps = logs[h : h + 1] - jnp.broadcast_to(columns[:, h : h + 1], (CHUNK, CHUNK))
                weights = scores * jnp.where(causal, jnp.exp(gaps), 0.0)
                both = dot(stack_left(fed), above(*split(weights)))
                y = both[:HEAD_DIM] + both[HEAD_DIM:]
                y = y + across[q * HEAD_DIM : (q + 1) * HEAD_DIM] * grown[h : h + 1]
                mixed[mine, cols] = y + heads_ref[2][h : h + 1] * values
                ending.append(fed * to_end[h : h + 1])
                kept.append(jnp.broadcast_to(through[h : h + 1], (HEAD_DIM, CHUNK)))
            state[rows] = held * above(*kept) + three_pass(above(*ending), in_pair)
        return carry

    lax.fori_loop(0, PER, chunk, 0)

    def mean_tile(h, totals):
        rows = pl.ds(pl.multiple_of(h * HEAD_DIM, HEAD_DIM), HEAD_DIM)
        gate = z[rows, :]
        opened = mixed[rows, :] * (gate * jax.nn.sigmoid(gate))
        gained = dnormed[rows, :] * wide(inner_ref[rows, :]) * opened
        return totals[0] + fold(opened * opened), totals[1] + fold(gained)

    nothing = jnp.zeros((8, STRIP), F32)
    squares, gains = lax.fori_loop(0, HEADS, mean_tile, (nothing, nothing))
    mean = jnp.sum(squares, axis=0, keepdims=True) * (1.0 / INNER)
    r = lax.rsqrt(mean + EPSILON)
    pulled = jnp.sum(gains, axis=0, keepdims=True) * (1.0 / INNER) * (r * r * r)

    def gate_tile(h, carry):
        rows = pl.ds(pl.multiple_of(h * HEAD_DIM, HEAD_DIM), HEAD_DIM)
        gate = z[rows, :]
        skip = wide(heads_ref[2, pl.ds(h, 1), :])
        mix = mixed[rows, :]
        sig = jax.nn.sigmoid(gate)
        sil = gate * sig
        opened = mix * sil
        normed = opened * r
        inner = wide(inner_ref[rows, :])
        normed_ref[rows, :] = (normed * inner).astype(BF16)
        dn = dnormed[rows, :]
        gained = dn * normed
        dinner_ref[rows, :] += gained[:, :CHUNK] + gained[:, CHUNK:]
        dopened = dn * inner * r - opened * pulled
        dmixed = dopened * sil
        dy_ref[rows, :] = dmixed
        dgate_ref[rows, :] = (dopened * mix * (sig * (1.0 + gate * (1.0 - sig)))).astype(BF16)
        skipped = row_sum(dmixed * act[rows, :])
        dskip_ref[pl.ds(h, 1), :] += skipped[:, :CHUNK] + skipped[:, CHUNK:]
        dlogs_ref[pl.ds(h, 1), :] = row_sum(dmixed * mix) - skip * skipped
        return carry

    lax.fori_loop(0, HEADS, gate_tile, 0)
    for i in range(D // 256):
        part = slice(256 * i, 256 * i + 256)
        branch = dot(second_ref[part, OUT_AT:STEP_AT], normed_ref[...]).T
        out_ref[:, part] = (x_ref[:, part].astype(F32) + branch).astype(BF16)


def backward_kernel(
    x_ref, back_ref, first_ref, second_ref, gain_ref, taps_ref, heads_ref,
    cin_ref, c_ref, raw_ref, s_ref, dy, dgate_ref, dlogs,
    dx_ref, dconv_ref, dstep_ref, dgain_ref, dtaps_ref, dheads_ref,
    act, dact, dstate, flow, tail, meets, vdu_rows,
):
    first = pl.program_id(0) == 0

    @pl.when(first)
    def _():
        dstate[...] = jnp.zeros_like(dstate)
        flow[...] = jnp.zeros_like(flow)
        tail[...] = jnp.zeros_like(tail)
        dgain_ref[...] = jnp.zeros_like(dgain_ref)
        dtaps_ref[...] = jnp.zeros_like(dtaps_ref)
        dheads_ref[...] = jnp.zeros_like(dheads_ref)

    back = back_ref[...]

    def act_tile(i, carry):
        rows = pl.ds(pl.multiple_of(i * 64, 64), 64)
        c = c_ref[rows, :]
        act[rows, :] = c * jax.nn.sigmoid(c)
        return carry

    lax.fori_loop(0, CONVCH // 64, act_tile, 0)
    causal = upper()
    ones = causal.astype(F32).astype(BF16)
    row = lax.broadcasted_iota(jnp.int32, (CHUNK, CHUNK), 0)
    col = lax.broadcasted_iota(jnp.int32, (CHUNK, CHUNK), 1)
    ones_back = (row >= col).astype(F32).astype(BF16)

    def chunk(step, carry):
        j = PER - 1 - step
        cols = pl.ds(pl.multiple_of(j * CHUNK, CHUNK), CHUNK)
        raw = raw_ref[0:HEADS, cols]
        steps, logs, columns, grown, to_end, through = rates_of(raw, heads_ref, ones)
        in_turned = act[INNER : INNER + NSTATE, cols]
        out_turned = act[INNER + NSTATE :, cols]
        in_map = in_turned.T
        out_map = out_turned.T
        scores = three_pass(in_map, right_pair(out_turned))
        in_pair = right_pair(in_turned)
        out_pair = right_pair(out_map)
        dscores = jnp.zeros((CHUNK, CHUNK), F32)
        din = jnp.zeros((NSTATE, CHUNK), F32)
        dout = jnp.zeros((NSTATE, CHUNK), F32)
        for g in range(HEADS // GROUP):
            rows = slice(g * GROUP * HEAD_DIM, (g + 1) * GROUP * HEAD_DIM)
            leaving = dstate[rows]
            entering = s_ref[j, rows]
            from_state = three_pass(leaving, in_pair)
            ending, growing, kept = [], [], []
            for q in range(GROUP):
                h = g * GROUP + q
                mine = slice(h * HEAD_DIM, (h + 1) * HEAD_DIM)
                values = act[mine, cols]
                fed = values * steps[h : h + 1]
                dys = dy[mine, cols]
                gaps = logs[h : h + 1] - jnp.broadcast_to(columns[:, h : h + 1], (CHUNK, CHUNK))
                decay = jnp.where(causal, jnp.exp(gaps), 0.0)
                weights = scores * decay
                both = dot_nt(stack_left(dys), beside(*split(weights)))
                du = both[:HEAD_DIM] + both[HEAD_DIM:]
                du = du + from_state[q * HEAD_DIM : (q + 1) * HEAD_DIM] * to_end[h : h + 1]
                fed_high, fed_low = split(fed)
                dy_high, dy_low = split(dys)
                dweights = dot_tn(
                    above(fed_high, fed_low, fed_high), above(dy_high, dy_high, dy_low)
                )
                dscores = dscores + dweights * decay
                vdu_rows[h : h + 1, :] = row_sum(values * du)
                dact[mine, cols] = du * steps[h : h + 1] + heads_ref[2][h : h + 1] * dys
                ending.append(fed * to_end[h : h + 1])
                growing.append(dys * grown[h : h + 1])
                kept.append(jnp.broadcast_to(through[h : h + 1], (HEAD_DIM, CHUNK)))
            ending = above(*ending)
            growing = above(*growing)
            end_high, end_low = split(ending)
            grow_high, grow_low = split(growing)
            leave_high, leave_low = split(leaving)
            enter_high, enter_low = split(entering)
            din = din + dot_tn(
                above(leave_high, leave_low, leave_high), above(end_high, end_high, end_low)
            )
            dout = dout + dot_tn(
                above(enter_high, enter_low, enter_high), above(grow_high, grow_high, grow_low)
            )
            arrived = leaving * above(*kept) + three_pass(growing, out_pair)
            dstate[rows] = arrived
            meet = arrived * entering
            for q in range(GROUP):
                h = g * GROUP + q
                meets[h : h + 1, :] = row_sum(meet[q * HEAD_DIM : (q + 1) * HEAD_DIM])
        vdu = vdu_rows[...]
        dlog = dlogs[:, cols] - steps * vdu
        drate = exact_sum(dlog, ones_back) + flow[...]
        flow[...] = jnp.broadcast_to(
            jnp.sum(meets[...], axis=1, keepdims=True), (HEADS, CHUNK)
        )
        dsteps = vdu + heads_ref[1] * drate
        draw = dsteps * jax.nn.sigmoid(raw + heads_ref[0])
        dheads_ref[0] += draw
        dheads_ref[1] += drate * steps * heads_ref[1]
        dstep_ref[:, cols] = above(draw, jnp.zeros((STEP - HEADS, CHUNK), F32)).astype(BF16)
        score_high, score_low = split(dscores)
        both = dot_nt(stack_left(out_turned), beside(score_high, score_low))
        dact[INNER : INNER + NSTATE, cols] = din + both[:NSTATE] + both[NSTATE:]
        both = dot(stack_left(in_turned), above(score_high, score_low))
        dact[INNER + NSTATE :, cols] = dout + both[:NSTATE] + both[NSTATE:]
        return carry

    lax.fori_loop(0, PER, chunk, 0)

    lane = lax.broadcasted_iota(jnp.int32, (64, CHUNK), 1)

    def conv_tile(i, carry):
        rows = pl.ds(pl.multiple_of(i * 64, 64), 64)
        c = c_ref[rows, :]
        sig = jax.nn.sigmoid(c)
        dpre = dact[rows, :] * (sig * (1.0 + c * (1.0 - sig)))
        cin = cin_ref[rows, :]
        cols = [dpre[:, CHUNK * j : CHUNK * j + CHUNK] for j in range(PER)]
        dcin = dpre * wide(taps_ref[KCONV - 1, rows, :])
        grad = cin * dpre
        dtaps_ref[KCONV - 1, rows, :] += grad[:, :CHUNK] + grad[:, CHUNK:]
        dtaps_ref[KCONV, rows, :] += dpre[:, :CHUNK] + dpre[:, CHUNK:]
        for k in range(KCONV - 1):
            ahead = KCONV - 1 - k
            turned = [pltpu.roll(col, CHUNK - ahead, 1) for col in cols] + [tail[k, rows, :]]
            tail[k, rows, :] = turned[0]
            pairs = zip(turned[:-1], turned[1:])
            shifted = beside(*[jnp.where(lane < CHUNK - ahead, a, b) for a, b in pairs])
            dcin = dcin + shifted * wide(taps_ref[k, rows, :])
            grad = cin * shifted
            dtaps_ref[k, rows, :] += grad[:, :CHUNK] + grad[:, CHUNK:]
        dconv_ref[rows, :] = dcin.astype(BF16)
        return carry

    lax.fori_loop(0, CONVCH // 64, conv_tile, 0, unroll=4)
    x = x_ref[...].astype(F32)
    r = lax.rsqrt(jnp.mean(x * x, axis=-1, keepdims=True) + EPSILON)
    parts = []
    for i in range(D // 256):
        part = slice(256 * i, 256 * i + 256)
        total = dot(first_ref[part, :INNER], dgate_ref[...])
        total = total + dot(first_ref[part, INNER:], dconv_ref[: HALF - INNER])
        total = total + dot(second_ref[part, :OUT_AT], dconv_ref[HALF - INNER :])
        step = second_ref[part, STEP_AT : STEP_AT + STEP]
        parts.append((total + dot(step, dstep_ref[...])).T)
    dscaled = beside(*parts)
    plain = x * r
    dgain_ref[...] += fold(dscaled * plain)
    gained = dscaled * gain_ref[...]
    inner = jnp.mean(gained * plain, axis=-1, keepdims=True)
    dx_ref[...] = back.astype(F32) + (gained - plain * inner) * r


def whole(shape):
    return pl.BlockSpec(shape, lambda i: (0,) * len(shape), pipeline_mode=pl.Buffered(1))


def strip_rows(width):
    return pl.BlockSpec((STRIP, width), lambda i: (i, 0))


def strip_cols(height):
    return pl.BlockSpec((height, STRIP), lambda i: (0, i))


def shape(*dims, dtype=F32):
    return jax.ShapeDtypeStruct(dims, dtype)


def half(k, *dims):
    return pl.BlockSpec((None,) + dims, lambda i: (k, 0, 0), pipeline_mode=pl.Buffered(1))


def forward_call(x, back, weights, gain, taps, heads, inner):
    return pl.pallas_call(
        forward_kernel,
        grid=(STRIPS,),
        in_specs=[
            strip_rows(D), strip_rows(D), half(0, D, HALF), half(1, D, HALF), whole((1, D)),
            whole((KCONV + 1, CONVCH, CHUNK)), whole((3, HEADS, CHUNK)), whole((INNER, CHUNK)),
        ],
        out_specs=[
            strip_rows(D), strip_rows(D), strip_cols(CONVCH), strip_cols(CONVCH),
            strip_cols(STEP), pl.BlockSpec((PER, INNER, NSTATE), lambda i: (i, 0, 0)),
            strip_cols(INNER), strip_cols(INNER), strip_cols(INNER), strip_cols(HEADS),
            whole((HEADS, CHUNK)), whole((INNER, CHUNK)),
        ],
        out_shape=[
            shape(LEN, D, dtype=BF16), shape(LEN, D, dtype=BF16), shape(CONVCH, LEN),
            shape(CONVCH, LEN), shape(STEP, LEN), shape(LEN // CHUNK, INNER, NSTATE),
            shape(INNER, LEN, dtype=BF16), shape(INNER, LEN), shape(INNER, LEN, dtype=BF16),
            shape(HEADS, LEN), shape(HEADS, CHUNK), shape(INNER, CHUNK),
        ],
        scratch_shapes=[
            pltpu.VMEM((CONVCH, STRIP), F32), pltpu.VMEM((INNER, STRIP), F32),
            pltpu.VMEM((INNER, STRIP), F32), pltpu.VMEM((INNER, STRIP), F32),
            pltpu.VMEM((INNER, NSTATE), F32), pltpu.VMEM((2, CONVCH, CHUNK), F32),
            pltpu.VMEM((2, HALF, D), BF16),
        ],
        compiler_params=pltpu.CompilerParams(vmem_limit_bytes=60 * 2**20),
        name="mixer_forward",
    )(x, back, weights, weights, gain, taps, heads, inner)


def backward_call(x, back, weights, gain, taps, heads, kept):
    last = STRIPS - 1

    def rows(width):
        return pl.BlockSpec((STRIP, width), lambda i: (last - i, 0))

    def cols(height):
        return pl.BlockSpec((height, STRIP), lambda i: (0, last - i))

    return pl.pallas_call(
        backward_kernel,
        grid=(STRIPS,),
        in_specs=[
            rows(D), rows(D), half(0, D, HALF), half(1, D, HALF), whole((1, D)),
            whole((KCONV + 1, CONVCH, CHUNK)), whole((3, HEADS, CHUNK)), cols(CONVCH),
            cols(CONVCH), cols(STEP),
            pl.BlockSpec((PER, INNER, NSTATE), lambda i: (last - i, 0, 0)), cols(INNER),
            cols(INNER), cols(HEADS),
        ],
        out_specs=[
            rows(D), cols(CONVCH), cols(STEP), whole((8, D)),
            whole((KCONV + 1, CONVCH, CHUNK)), whole((2, HEADS, CHUNK)),
        ],
        out_shape=[
            shape(LEN, D), shape(CONVCH, LEN, dtype=BF16), shape(STEP, LEN, dtype=BF16),
            shape(8, D), shape(KCONV + 1, CONVCH, CHUNK), shape(2, HEADS, CHUNK),
        ],
        scratch_shapes=[
            pltpu.VMEM((CONVCH, STRIP), F32), pltpu.VMEM((CONVCH, STRIP), F32),
            pltpu.VMEM((INNER, NSTATE), F32), pltpu.VMEM((HEADS, CHUNK), F32),
            pltpu.VMEM((KCONV - 1, CONVCH, CHUNK), F32), pltpu.VMEM((HEADS, CHUNK), F32),
            pltpu.VMEM((HEADS, CHUNK), F32),
        ],
        compiler_params=pltpu.CompilerParams(vmem_limit_bytes=60 * 2**20),
        name="mixer_backward",
    )(x, back, weights, weights, gain, taps, heads, *kept)


def lanes(vector):
    return jnp.broadcast_to(vector[..., None], vector.shape + (CHUNK,))


def parameters(params):
    gain = params[:D].reshape(1, D)
    at = D
    taps = lanes(params[at : at + (KCONV + 1) * CONVCH].reshape(KCONV + 1, CONVCH))
    at += (KCONV + 1) * CONVCH
    heads = params[at : at + 3 * HEADS].reshape(3, HEADS)
    heads = lanes(jnp.stack([heads[0], -jnp.exp(heads[1]), heads[2]]))
    inner = lanes(params[at + 3 * HEADS :])
    return gain, taps, heads, inner


def block_and_gradients(x, back, weights, params):
    gain, taps, heads, inner = parameters(params)
    out, hb, cin, c, raw, states, normed, dy, dgate, dlogs, dskip, dinner = forward_call(
        x, back, weights, gain, taps, heads, inner
    )
    dx, dconv, dstep, dgain, dtaps, dheads = backward_call(
        x, back, weights, gain, taps, heads, (cin, c, raw, states, dy, dgate, dlogs)
    )
    grad_out = dot(normed, back)
    grad_gate = dot(dgate, hb)
    grad_conv = dot(dconv, hb)
    grad_step = dot(dstep, hb)[:HEADS]
    small = jnp.concatenate(
        [
            jnp.sum(dgain, axis=0),
            jnp.sum(dtaps, axis=-1).reshape(-1),
            jnp.sum(dheads, axis=-1).reshape(-1),
            jnp.sum(dskip, axis=-1),
            jnp.sum(dinner, axis=-1),
        ]
    )
    return out, dx, grad_gate, grad_conv, grad_step, grad_out, small


MESH = pl.DeviceIdType.MESH


class Place:
    def __init__(self, sizes):
        self.Z, self.F = sizes
        self.C, self.Y = 2, 2
        self.X = self.F // 4
        f = lax.axis_index("fsdp")
        self.z = lax.axis_index("dp")
        self.c = lax.rem(f, 2)
        self.x = lax.rem(f // 2, self.X)
        self.y = f // (2 * self.X)
        self.f = f

    def at(self, z=None, y=None, x=None, c=None):
        z = self.z if z is None else z
        y = self.y if y is None else y
        x = self.x if x is None else x
        c = self.c if c is None else c
        return (z, (y * self.X + x) * 2 + c)

    def other_x(self, step):
        return lax.rem(self.x + step, self.X)


def signal(device):
    pl.semaphore_signal(
        pltpu.get_barrier_semaphore(), inc=1, device_id=device, device_id_type=MESH
    )


def greet_all(place):
    count = place.Z * place.F
    me = place.z * place.F + place.f

    def step(i, carry):
        peer = lax.rem(me + i, count)
        signal((peer // place.F, lax.rem(peer, place.F)))
        return carry

    lax.fori_loop(1, count, step, 0)
    pl.semaphore_wait(pltpu.get_barrier_semaphore(), count - 1)


def remote(src, dst, send, recv, device):
    return pltpu.make_async_remote_copy(
        src_ref=src, dst_ref=dst, send_sem=send, recv_sem=recv, device_id=device,
        device_id_type=MESH,
    )


def add_blocks(dst, src, count):
    def step(i, carry):
        target = dst(i)
        target[...] = target[...] + src(i)[...]
        return carry

    lax.fori_loop(0, count, step, 0)


class Swap:
    def __init__(self, place, src, dst, send, recv, local, same=False):
        self.place, self.src, self.dst, self.same = place, src, dst, same
        self.send, self.recv, self.local = send, recv, local
        self.count = place.Z * place.F
        self.me = place.z * place.F + place.f

    def to(self, i):
        peer = lax.rem(self.me + i, self.count)
        return remote(
            self.block(peer), self.dst.at[self.me], self.send.at[i], self.recv.at[i],
            (peer // self.place.F, lax.rem(peer, self.place.F)),
        )

    def block(self, peer):
        return self.src if self.same else self.src.at[peer]

    def start(self):
        pltpu.make_async_copy(self.block(self.me), self.dst.at[self.me], self.local).start()

        def step(i, carry):
            self.to(i).start()
            return carry

        lax.fori_loop(1, self.count, step, 0)

    def wait(self):
        pltpu.make_async_copy(self.block(self.me), self.dst.at[self.me], self.local).wait()

        def step(i, carry):
            sender = lax.rem(self.me + self.count - i, self.count)
            self.to(i).wait_send()
            remote(
                self.block(sender), self.dst.at[sender], self.send.at[i], self.recv.at[i],
                (sender // self.place.F, lax.rem(sender, self.place.F)),
            ).wait_recv()
            return carry

        lax.fori_loop(1, self.count, step, 0)


class Plane:
    def __init__(self, place, acc, x1, y1, x2, y2, sems):
        self.p, self.acc = place, acc
        self.x1, self.y1, self.x2, self.y2, self.sems = x1, y1, x2, y2, sems
        self.h = place.Z // 2

    def copies(self, stage):
        p, acc, h = self.p, self.acc, self.h
        low, high = pl.ds(0, h), pl.ds(h, p.Z - h)
        out = []
        base = stage * p.X
        for s in range(1, p.X):
            x = p.other_x(s)
            if stage == 0:
                src, dst = acc.at[low, :, x], self.x1.at[s - 1]
            else:
                src, dst = acc.at[high, p.y, x], self.x2.at[s - 1]
            sem = self.sems.at[base + s]
            out.append(remote(src, dst, sem.at[0], sem.at[1], p.at(x=x)))
        if stage == 0:
            src, dst = acc.at[high, 1 - p.y], self.y1
        else:
            src, dst = acc.at[low, 1 - p.y, p.x], self.y2
        sem = self.sems.at[base]
        out.append(remote(src, dst, sem.at[0], sem.at[1], p.at(y=1 - p.y)))
        return out

    def start(self, stage):
        for copy in self.copies(stage):
            copy.start()

    def finish(self, stage):
        p, acc, h = self.p, self.acc, self.h
        for copy in self.copies(stage):
            copy.wait()
        for s in range(p.X - 1):
            if stage == 0:
                add_blocks(
                    lambda i: acc.at[i // p.Y, lax.rem(i, p.Y), p.x],
                    lambda i: self.x1.at[s, i // p.Y, lax.rem(i, p.Y)],
                    h * p.Y,
                )
            else:
                add_blocks(
                    lambda i: acc.at[h + i, p.y, p.x], lambda i: self.x2.at[s, i], p.Z - h
                )
        if stage == 0:
            add_blocks(
                lambda i: acc.at[h + i // p.X, p.y, lax.rem(i, p.X)],
                lambda i: self.y1.at[i // p.X, lax.rem(i, p.X)],
                (p.Z - h) * p.X,
            )
        else:
            add_blocks(lambda i: acc.at[i, p.y, p.x], lambda i: self.y2.at[i], h)


def plane_scratch(sizes, block):
    Z, X, Y = sizes[0], sizes[1] // 4, 2
    h = Z // 2
    return [
        pltpu.VMEM((Z, Y, X) + block, F32), pltpu.VMEM((X - 1, h, Y) + block, F32),
        pltpu.VMEM((Z - h, X) + block, F32), pltpu.VMEM((X - 1, Z - h) + block, F32),
        pltpu.VMEM((h,) + block, F32), pltpu.SemaphoreType.DMA((2 * X, 2)),
    ]


def scatter_kernel(sizes, parts, *refs):
    ins, outs, rest = refs[:parts], refs[parts : 2 * parts], refs[2 * parts :]
    p = Place(sizes)
    Z = p.Z
    work = [rest[10 * k : 10 * k + 10] for k in range(parts)]
    signal(p.at(c=1 - p.c))
    signal(p.at(y=1 - p.y))
    for s in range(1, p.X):
        signal(p.at(x=p.other_x(s)))

    for s in range(1, Z):
        signal(p.at(z=lax.rem(p.z + s, Z)))
    pl.semaphore_wait(pltpu.get_barrier_semaphore(), p.X + Z)

    def core_copies(k):
        acc, core, sems = work[k][0], work[k][6], work[k][7]
        return (
            remote(
                ins[k].at[:, :, :, 1 - p.c], core, sems.at[0], sems.at[1], p.at(c=1 - p.c)
            ),
            pltpu.make_async_copy(ins[k].at[:, :, :, p.c], acc, sems.at[2]),
        )

    for k in range(parts):
        for copy in core_copies(k):
            copy.start()
    planes = [Plane(p, *work[k][:6]) for k in range(parts)]
    for k in range(parts):
        for copy in core_copies(k):
            copy.wait()
        acc, core = work[k][0], work[k][6]

        def place_of(i):
            return i // (p.Y * p.X), lax.rem(i // p.X, p.Y), lax.rem(i, p.X)

        add_blocks(
            lambda i: acc.at[place_of(i)], lambda i: core.at[place_of(i)], Z * p.Y * p.X
        )
        planes[k].start(0)
    for k in range(parts):
        planes[k].finish(0)
        planes[k].start(1)

    def flow(k, t, right):
        acc, held, sems = work[k][0], work[k][8], work[k][9]
        side = 0 if right else 1
        target = p.z + 1 if right else p.z - 1
        sem = sems.at[side, t]
        return remote(
            acc.at[t, p.y, p.x], held.at[side, t], sem.at[0], sem.at[1], p.at(z=target)
        )

    def send(k, t, right):
        @pl.when(p.z < t if right else p.z > t)
        def _():
            flow(k, t, right).start()

    def receive(k, t, right):
        acc, held = work[k][0], work[k][8]

        @pl.when(jnp.logical_and(p.z > 0, p.z <= t) if right else
                 jnp.logical_and(p.z < Z - 1, p.z >= t))
        def _():
            flow(k, t, right).wait_recv()
            mine = acc.at[t, p.y, p.x]
            mine[...] = mine[...] + held[0 if right else 1, t]

    def pass_on(k, j, right):
        t = Z - 1 - j if right else j
        receive(k, t, right)

        @pl.when(p.z > 0 if right else p.z < Z - 1)
        def _():
            send(k, t, right)

    for k in range(parts):
        planes[k].finish(1)
        for j in range(Z - 1):
            @pl.when(p.z == 0)
            def _():
                send(k, Z - 1 - j, True)

            @pl.when(p.z == Z - 1)
            def _():
                send(k, j, False)

    for k in range(parts):
        for j in range(Z):
            @pl.when(p.z < Z // 2)
            def _():
                pass_on(k, j, True)
                pass_on(k, j, False)

            @pl.when(p.z >= Z // 2)
            def _():
                pass_on(k, j, False)
                pass_on(k, j, True)

        for j in range(Z):
            for right in (True, False):
                @pl.when(p.z < j if right else p.z > j)
                def _():
                    flow(k, j, right).wait_send()

        outs[k][...] = work[k][0][p.z, p.y, p.x]


def scatter_call(blocks, sizes, collective_id):
    Z, F = sizes
    X, Y = F // 4, 2
    ins = [b.reshape((Z, Y, X, 2) + b.shape[1:]) for b in blocks]
    scratch = []
    for b in blocks:
        block = b.shape[1:]
        scratch += plane_scratch(sizes, block)
        scratch += [
            pltpu.VMEM((Z, Y, X) + block, F32), pltpu.SemaphoreType.DMA((3,)),
            pltpu.VMEM((2, Z) + block, F32), pltpu.SemaphoreType.DMA((2, Z, 2)),
        ]
    return pl.pallas_call(
        functools.partial(scatter_kernel, sizes, len(blocks)),
        out_shape=[jax.ShapeDtypeStruct(b.shape[1:], F32) for b in blocks],
        in_specs=[pl.BlockSpec(memory_space=pl.ANY)] * len(blocks),
        out_specs=[pl.BlockSpec(memory_space=pltpu.VMEM)] * len(blocks),
        scratch_shapes=scratch,
        compiler_params=pltpu.CompilerParams(
            collective_id=collective_id, has_side_effects=True, vmem_limit_bytes=56 * 2**20
        ),
        name="scatter",
    )(*ins)


def gather_kernel(
    sizes, w_in_ref, w_out_ref, blocks_ref, all_ref, moved_ref,
    both, mine, core_sems, z_sems, near, far, across, swap_send, swap_recv, local,
):
    p = Place(sizes)
    Z, h = p.Z, p.Z // 2
    greet_all(p)
    own = both.shape[1]
    both[p.c, :, :WIDE] = w_in_ref[:, :WIDE]
    both[p.c, :, WIDE : WIDE + INNER] = w_out_ref[...]
    both[p.c, :, WIDE + INNER :] = jnp.concatenate(
        [w_in_ref[:, WIDE:], jnp.zeros((own, 2 * HALF - IN_W - INNER), F32)], axis=1
    )
    partner = p.at(c=1 - p.c)
    pair = remote(
        both.at[p.c], both.at[p.c], core_sems.at[0], core_sems.at[1], partner
    )
    pair.start()
    pair.wait_send()
    other = both.at[1 - p.c]
    remote(other, other, core_sems.at[0], core_sems.at[1], partner).wait_recv()
    for k in range(2):
        cols = slice(k * HALF, k * HALF + HALF)
        mine[k] = above(both[0, :, cols], both[1, :, cols]).astype(BF16)
    keeps = [
        pltpu.make_async_copy(mine.at[k], all_ref.at[k, p.z, p.y, p.x], core_sems.at[2 + k])
        for k in range(2)
    ]
    for keep in keeps:
        keep.start()

    def spot(z, y, x):
        return all_ref.at[p.c, z, y, x]

    def copy(src, dst, sem, device):
        return remote(src, dst, sem.at[0], sem.at[1], device)

    def along_z(z, right, src=None):
        here = spot(z, p.y, p.x)
        target = p.at(z=p.z + 1 if right else p.z - 1)
        return copy(here if src is None else src, here, z_sems.at[0 if right else 1, z], target)

    def near_copies(z, src=None):
        here = spot(z, p.y, p.x)
        src = here if src is None else src
        found = [copy(src, here, near.at[z, 0], p.at(y=1 - p.y))]
        for s in range(1, p.X):
            found.append(copy(src, here, near.at[z, s], p.at(x=p.other_x(s))))
        return found

    def near_arrivals(z):
        found = [(z, 1 - p.y, p.x, near.at[z, 0])]
        for s in range(1, p.X):
            found.append((z, p.y, lax.rem(p.x + p.X - s, p.X), near.at[z, s]))
        return found

    def far_copies(z):
        low, high = [], []
        for s in range(1, p.X):
            x = p.other_x(s)
            there = spot(z, p.y, x)
            low.append(copy(there, there, far.at[z, s], p.at(y=1 - p.y)))
            there = spot(z, 1 - p.y, p.x)
            high.append(copy(there, there, far.at[z, s], p.at(x=x)))
        return low, high

    def far_arrivals(z):
        low = [(z, 1 - p.y, p.other_x(s), far.at[z, s]) for s in range(1, p.X)]
        high = [
            (z, 1 - p.y, lax.rem(p.x + p.X - s, p.X), far.at[z, s]) for s in range(1, p.X)
        ]
        return low, high

    def to_partner(z, y, x):
        here = spot(z, y, x)
        return copy(here, here, across.at[z, y, x], partner)

    def await_block(z, y, x, sem):
        here = spot(z, y, x)
        copy(here, here, sem, partner).wait_recv()
        to_partner(z, y, x).start()

    def start_all(copies):
        for c in copies:
            c.start()

    @pl.when(p.z < Z - 1)
    def _():
        along_z(p.z, True, mine.at[p.c]).start()

    @pl.when(p.z > 0)
    def _():
        along_z(p.z, False, mine.at[p.c]).start()

    start_all(near_copies(p.z, mine.at[p.c]))
    swap = Swap(p, blocks_ref, moved_ref, swap_send, swap_recv, local)
    swap.start()

    def visit(right, z):
        await_block(z, p.y, p.x, z_sems.at[0 if right else 1, z])

        @pl.when(p.z < Z - 1 if right else p.z > 0)
        def _():
            along_z(z, right).start()

        start_all(near_copies(z))

    def by_distance(low, high):
        for j in range(1, Z):
            @pl.when(p.z - j >= 0)
            def _():
                low(p.z - j)

            @pl.when(p.z + j < Z)
            def _():
                high(p.z + j)

    by_distance(lambda z: visit(True, z), lambda z: visit(False, z))

    def relay(z):
        for block in near_arrivals(z):
            await_block(*block)
        low, high = far_copies(z)

        @pl.when(z < h)
        def _():
            start_all(low)

        @pl.when(z >= h)
        def _():
            start_all(high)

    relay(p.z)
    by_distance(relay, relay)

    def settle(z):
        low, high = far_arrivals(z)

        @pl.when(z < h)
        def _():
            for block in low:
                await_block(*block)

        @pl.when(z >= h)
        def _():
            for block in high:
                await_block(*block)

    settle(p.z)
    by_distance(settle, settle)
    for keep in keeps:
        keep.wait()

    def finish(z, carry):
        for c in near_copies(z):
            c.wait_send()
        low, high = far_copies(z)

        @pl.when(z < h)
        def _():
            for c in low:
                c.wait_send()

        @pl.when(z >= h)
        def _():
            for c in high:
                c.wait_send()

        @pl.when(jnp.logical_and(z <= p.z, p.z < Z - 1))
        def _():
            along_z(z, True).wait_send()

        @pl.when(jnp.logical_and(z >= p.z, p.z > 0))
        def _():
            along_z(z, False).wait_send()

        for y in range(p.Y):
            for x in range(p.X):
                @pl.when(jnp.logical_not(jnp.logical_and(
                    z == p.z, jnp.logical_and(p.y == y, p.x == x))))
                def _():
                    to_partner(z, y, x).wait_send()
                    theirs = all_ref.at[1 - p.c, z, y, x]
                    copy(theirs, theirs, across.at[z, y, x], partner).wait_recv()

        return carry

    lax.fori_loop(0, Z, finish, 0)
    swap.wait()


def gather_call(weight_in, weight_out, blocks, sizes, collective_id):
    Z, F = sizes
    X, Y = F // 4, 2
    own = weight_in.shape[0]
    count = Z * F
    vmem = pl.BlockSpec(memory_space=pltpu.VMEM)
    hbm = pl.BlockSpec(memory_space=pl.ANY)
    whole_weights, moved = pl.pallas_call(
        functools.partial(gather_kernel, sizes),
        out_shape=[
            jax.ShapeDtypeStruct((2, Z, Y, X, 2 * own, HALF), BF16),
            jax.ShapeDtypeStruct(blocks.shape, F32),
        ],
        in_specs=[vmem, vmem, hbm],
        out_specs=[hbm, hbm],
        scratch_shapes=[
            pltpu.VMEM((2, own, 2 * HALF), F32), pltpu.VMEM((2, 2 * own, HALF), BF16),
            pltpu.SemaphoreType.DMA((4,)), pltpu.SemaphoreType.DMA((2, Z, 2)),
            pltpu.SemaphoreType.DMA((Z, X, 2)), pltpu.SemaphoreType.DMA((Z, X, 2)),
            pltpu.SemaphoreType.DMA((Z, Y, X, 2)), pltpu.SemaphoreType.DMA((count,)),
            pltpu.SemaphoreType.DMA((count,)), pltpu.SemaphoreType.DMA,
        ],
        compiler_params=pltpu.CompilerParams(
            collective_id=collective_id, has_side_effects=True, vmem_limit_bytes=40 * 2**20
        ),
        name="weights_gather",
    )(weight_in, weight_out, blocks)
    return whole_weights.reshape(2, D, HALF), moved


def gram_rows(slab, row):
    high, low = split(slab)
    left = above(high, low, high)[:, 128 * row : 128 * row + 128]
    return dot_tn(left, above(high, high, low)[:, 128 * row :])


def pack_gram(target, slab):
    Z, Y, X, per, _ = target.shape
    rows = above(*[
        beside(gram_rows(slab, i), gram_rows(slab, D // 128 - 1 - i)) for i in range(D // 256)
    ])
    rows = above(rows, jnp.zeros((Z * Y * X * per - rows.shape[0], rows.shape[1]), F32)) if (
        Z * Y * X * per > rows.shape[0]) else rows
    for i in range(Z * Y * X):
        target[i // (Y * X), i // X % Y, i % X] = rows[per * i : per * i + per]


def unpack_gram(gram, packed):
    Z, Y, X, per, _ = packed.shape
    rows = above(*[packed[i // (Y * X), i // X % Y, i % X] for i in range(Z * Y * X)])
    for i in range(D // 256):
        pair = rows[128 * i : 128 * i + 128]
        wide_part, j = D - 128 * i, D // 128 - 1 - i
        for row, part in ((i, pair[:, :wide_part]), (j, pair[:, wide_part:])):
            gram[128 * row : 128 * row + 128, 128 * row :] = part
            for k in range(row + 1, D // 128):
                at = 128 * (k - row)
                gram[128 * k : 128 * k + 128, 128 * row : 128 * row + 128] = part[
                    :, at : at + 128
                ].T


def put_left(left, value, rows):
    high, low = split(value)
    left[rows] = beside(high, low, high)


def put_right(right, value, row):
    high, low = split(value)
    size = value.shape[0]
    right[row : row + size] = high
    right[D + row : D + row + size] = high
    right[2 * D + row : 2 * D + row + size] = low


TILE = 256


def symmetric_product(target, left, right):
    for i in range(D // TILE):
        rows = slice(TILE * i, TILE * i + TILE)
        part = dot(left[rows], right[:, TILE * i :])
        target[rows, TILE * i :] = part
        for j in range(i + 1, D // TILE):
            at = TILE * (j - i)
            target[TILE * j : TILE * j + TILE, rows] = part[:, at : at + TILE].T


def iterate(gram, square, factor, left, right, slab, slab_left):
    tiles = [slice(TILE * i, TILE * i + TILE) for i in range(D // TILE)]
    row = lax.broadcasted_iota(jnp.int32, (TILE, D), 0)
    col = lax.broadcasted_iota(jnp.int32, (TILE, D), 1)
    diagonals = [(row + TILE * i == col) for i in range(D // TILE)]
    trace = jnp.zeros((8, D), F32)
    for rows, diagonal in zip(tiles, diagonals):
        trace = trace + fold(jnp.where(diagonal, gram[rows], 0.0))
    trace = jnp.sum(jnp.sum(trace, axis=0, keepdims=True), axis=1, keepdims=True)
    scale = 1.0 / (jnp.sqrt(trace) + 1e-07)
    for rows in tiles:
        gram[rows] = gram[rows] * (scale * scale)
    slab[...] = slab[...] * scale

    def step(iteration, carry):
        for i, rows in enumerate(tiles):
            value = gram[rows]
            put_left(left, value, rows)
            put_right(right, value, TILE * i)
        symmetric_product(square, left, right)
        for i, rows in enumerate(tiles):
            value = COEF_B * gram[rows] + COEF_C * square[rows]
            put_right(right, value + jnp.where(diagonals[i], COEF_A, 0.0), TILE * i)
        put_left(slab_left, slab[...], slice(None))
        slab[...] = dot(slab_left[...], right[...])
        symmetric_product(factor, left, right)
        for rows in tiles:
            put_left(left, factor[rows], rows)
        symmetric_product(gram, left, right)
        return carry

    lax.fori_loop(0, ITERS - 1, step, 0)
    for i, rows in enumerate(tiles):
        put_right(right, gram[rows], TILE * i)
    first = slab[...]
    put_left(slab_left, first, slice(None))
    once = dot(slab_left[...], right[...])
    put_left(slab_left, once, slice(None))
    slab[...] = COEF_A * first + COEF_B * once + COEF_C * dot(slab_left[...], right[...])


def update_kernel(
    sizes, gate_ref, conv_ref, out_ref, small_ref, old_ref, moved_ref, smalls_ref, spread_ref,
    acc, x1, y1, x2, y2, sems, total, core, core_sems, held, z_sems, back_sems, give, given,
    messages, smalls, gram, square, factor, left, right, slab, slab_left,
    swap_send, swap_recv, local,
):
    p = Place(sizes)
    Z, h = p.Z, p.Z // 2
    low, high = pl.ds(0, h), pl.ds(h, Z - h)
    count = Z * p.F
    own = D // count
    gates, convs = gate_ref.shape[0], conv_ref.shape[0]
    ins = gates + convs
    greet_all(p)
    swaps = [
        Swap(p, src, dst, swap_send.at[k], swap_recv.at[k], local.at[k], same)
        for k, (src, dst, same) in enumerate([
            (small_ref, smalls, True), (messages.at[0], moved_ref, False),
            (messages.at[1], spread_ref, False),
        ])
    ]
    swaps[0].start()
    old = old_ref[...].T
    new_in = above(gate_ref[...], conv_ref[...])
    new_out = out_ref[...]

    def push(gradient, moment):
        return gradient + MOMENTUM * (MOMENTUM * moment + gradient)

    push_in = push(new_in, old[:ins])
    push_out = above(push(new_out, old[ins : ins + gates]), jnp.zeros((ins - gates, D), F32))
    in_core = p.c == 0
    give[...] = jnp.where(in_core, push_out, push_in)
    slab[:ins] = jnp.where(in_core, push_in, push_out)
    partner = p.at(c=1 - p.c)
    pack_gram(total, give[...])
    first = [
        remote(total, core, core_sems.at[0], core_sems.at[1], partner),
        remote(give, given, core_sems.at[2], core_sems.at[3], partner),
    ]
    for copy in first:
        copy.start()
    pack_gram(acc, slab[:ins])

    def store_messages(k, turned):
        turned = beside(turned, jnp.zeros((D, 256 - turned.shape[1]), F32)) if (
            turned.shape[1] < 256) else turned
        for d in range(count):
            messages[k, d] = turned[own * d : own * d + own]

    for copy in first:
        copy.wait()

    def place_of(i):
        return i // (p.Y * p.X), lax.rem(i // p.X, p.Y), lax.rem(i, p.X)

    add_blocks(lambda i: acc.at[place_of(i)], lambda i: core.at[place_of(i)], Z * p.Y * p.X)
    plane = Plane(p, acc, x1, y1, x2, y2, sems)
    plane.start(0)
    store_messages(0, above(new_in, new_out).T)
    plane.finish(0)
    plane.start(1)
    plane.finish(1)

    def over(s):
        z = lax.rem(p.z + s, Z)
        return remote(
            acc.at[z, p.y, p.x], held.at[s - 1], z_sems.at[0, s, 0], z_sems.at[0, s, 1], p.at(z=z)
        )

    for s in range(1, Z):
        over(s).start()
    for s in range(1, Z):
        over(s).wait()
    result = acc[p.z, p.y, p.x]
    for s in range(1, Z):
        result = result + held[s - 1]
    total[p.z, p.y, p.x] = result

    def back(s):
        z = lax.rem(p.z + s, Z)
        here = total.at[p.z, p.y, p.x]
        return remote(here, here, z_sems.at[1, s, 0], z_sems.at[1, s, 1], p.at(z=z))

    for s in range(1, Z):
        back(s).start()
    for s in range(1, Z):
        back(s).wait_send()
        z = lax.rem(p.z + Z - s, Z)
        theirs = total.at[z, p.y, p.x]
        remote(theirs, theirs, z_sems.at[1, s, 0], z_sems.at[1, s, 1], p.at(z=z)).wait_recv()

    def spread(stage):
        pairs = []
        for s in range(1, p.X):
            sem = back_sems.at[stage * p.X + s]
            here, theirs = (
                total.at[high, p.y, x] if stage == 0 else total.at[low, :, x]
                for x in (p.x, lax.rem(p.x + p.X - s, p.X))
            )
            device = p.at(x=p.other_x(s))
            pairs.append([remote(ref, ref, sem.at[0], sem.at[1], device) for ref in (here, theirs)])
        sem = back_sems.at[stage * p.X]
        here, theirs = (
            total.at[low, y, p.x] if stage == 0 else total.at[high, y] for y in (p.y, 1 - p.y)
        )
        device = p.at(y=1 - p.y)
        pairs.append([remote(ref, ref, sem.at[0], sem.at[1], device) for ref in (here, theirs)])
        for mine, _ in pairs:
            mine.start()
        for mine, other in pairs:
            mine.wait_send()
            other.wait_recv()

    for stage in range(2):
        spread(stage)
    swaps[0].wait()
    swaps[1].start()
    smalls_ref[...] = smalls[...]
    rows = smalls[...].reshape(-1, 128)
    new_step = beside(*[rows[HEADS * j : HEADS * j + HEADS] for j in range(D // 128)])
    push_step = push(new_step, old_ref[...].T[ins + gates : ins + gates + HEADS])
    push_step = jnp.where(in_core, push_step, 0.0)
    mine, theirs = slab[:ins], given[...]
    slab_in = above(mine, theirs, push_step)
    slab_out = above(theirs[:gates], mine[:gates], jnp.zeros((2 * convs + HEADS, D), F32))
    slab[: 2 * ins + HEADS] = jnp.where(in_core, slab_in, slab_out)
    slab[2 * ins + HEADS :] = jnp.zeros((slab.shape[0] - 2 * ins - HEADS, D), F32)
    unpack_gram(gram, total)
    step_high, step_low = split(push_step)
    step_left = above(step_high, step_low, step_high)
    gram[...] = gram[...] + dot_tn(step_left, above(step_high, step_high, step_low))
    iterate(gram, square, factor, left, right, slab, slab_left)
    store_messages(1, slab[...].T)
    swaps[2].start()
    swaps[1].wait()
    swaps[2].wait()


def update_call(parts, small, old, sizes, collective_id):
    Z, F = sizes
    X, Y = F // 4, 2
    count = Z * F
    own = D // count
    chips = count // 2
    gate, conv, out = parts
    ins = gate.shape[0] + conv.shape[0]
    per = -(-(D // 2) // (8 * chips)) * 8
    block = (per, D + 128)
    vmem = pl.BlockSpec(memory_space=pltpu.VMEM)
    hbm = pl.BlockSpec(memory_space=pl.ANY)
    dma = pltpu.SemaphoreType.DMA
    return pl.pallas_call(
        functools.partial(update_kernel, sizes),
        out_shape=[
            shape(count, own, 256), shape(count, *small.shape), shape(count, own, 256),
        ],
        in_specs=[vmem] * 5,
        out_specs=[hbm, vmem, hbm],
        scratch_shapes=plane_scratch(sizes, block)
        + [
            pltpu.VMEM((Z, Y, X) + block, F32), pltpu.VMEM((Z, Y, X) + block, F32), dma((4,)),
            pltpu.VMEM((Z - 1,) + block, F32), dma((2, Z, 2)), dma((2 * X, 2)),
            pltpu.VMEM((ins, D), F32), pltpu.VMEM((ins, D), F32),
            pltpu.VMEM((2, count, own, 256), F32), pltpu.VMEM((count,) + small.shape, F32),
            pltpu.VMEM((D, D), F32), pltpu.VMEM((D, D), F32), pltpu.VMEM((D, D), F32),
            pltpu.VMEM((D, 3 * D), BF16), pltpu.VMEM((3 * D, D), BF16),
            pltpu.VMEM((256, D), F32), pltpu.VMEM((256, 3 * D), BF16),
            dma((3, count)), dma((3, count)), dma((3,)),
        ],
        compiler_params=pltpu.CompilerParams(
            collective_id=collective_id, has_side_effects=True, vmem_limit_bytes=56 * 2**20
        ),
        name="update",
    )(gate, conv, out, small, old)


def spread_columns(rows, count):
    return rows.reshape(rows.shape[0], count, -1).transpose(1, 0, 2)


def gather_columns(blocks):
    return blocks.transpose(1, 0, 2).reshape(blocks.shape[1], -1)


def lanes_256(blocks):
    return jnp.pad(blocks, ((0, 0), (0, 0), (0, 256 - blocks.shape[2])))


def shards(
    inputs, cotangent, weight_in, weight_out, small_params, moment_in, moment_out, moment_small
):
    sizes = (lax.axis_size("dp"), lax.axis_size("fsdp"))
    count = sizes[0] * sizes[1]
    own = weight_in.shape[0]
    gates, convs = INNER // count, CONVCH // count
    ins = gates + convs
    old = jnp.concatenate(
        [
            spread_columns(moment_in[:, :INNER], count),
            spread_columns(moment_in[:, INNER:WIDE], count),
            spread_columns(moment_out, count),
            jnp.broadcast_to(moment_in[:, WIDE:], (count, own, HEADS)),
        ],
        axis=2,
    )
    weights, old = gather_call(weight_in, weight_out, lanes_256(old), sizes, 0)
    output, dx, part_gate, part_conv, part_step, part_out, part_small = block_and_gradients(
        inputs[0], cotangent[0], weights, small_params
    )
    outputs, input_grad = output[None], dx[None]

    flat = [
        part_step.reshape(HEADS, D // 128, 128).transpose(1, 0, 2).reshape(-1), part_small,
    ]
    flat = jnp.concatenate(flat)
    lines = -(-flat.shape[0] // (1024 * count)) * 8
    flat = jnp.pad(flat, (0, count * lines * 128 - flat.shape[0])).reshape(count, lines, 128)
    new_out, new_gate, new_conv, new_small = scatter_call(
        [
            part_out.reshape(count, gates, D), part_gate.reshape(count, gates, D),
            part_conv.reshape(count, convs, D), flat,
        ],
        sizes,
        1,
    )
    moved, smalls, spread = update_call(
        (new_gate, new_conv, new_out), new_small, old.reshape(D, 256), sizes, 2
    )
    smalls = smalls.reshape(-1)
    grad_small = smalls[HEADS * D : HEADS * D + small_params.shape[0]]
    new_step = smalls[: HEADS * D].reshape(D // 128, HEADS, 128).transpose(1, 0, 2)
    new_step = new_step.reshape(HEADS, D)

    def rows_in(gate_blocks, conv_blocks, step_rows):
        return beside(gather_columns(gate_blocks), gather_columns(conv_blocks), step_rows)

    evens, odds = spread[0::2], spread[1::2]
    direction_in = rows_in(
        jnp.concatenate([evens[:, :, :gates], evens[:, :, ins : ins + gates]], axis=2),
        jnp.concatenate([evens[:, :, gates:ins], evens[:, :, ins + gates : 2 * ins]], axis=2),
        evens[0, :, 2 * ins : 2 * ins + HEADS],
    )
    direction_out = gather_columns(odds[:, :, : 2 * gates])
    first_row = (lax.axis_index("dp") * sizes[1] + lax.axis_index("fsdp")) * own
    grad_in = rows_in(
        moved[:, :, :gates],
        moved[:, :, gates:ins],
        lax.dynamic_slice_in_dim(new_step, first_row, own, 1).T,
    )
    grad_out = gather_columns(moved[:, :, ins : ins + gates])
    new_moment_in = MOMENTUM * moment_in + grad_in
    new_moment_out = MOMENTUM * moment_out + grad_out
    decay = 1.0 - MATRIX_RATE * WEIGHT_DECAY
    new_weight_in = weight_in * decay - MATRIX_RATE * 0.2 * math.sqrt(max(D, IN_W)) * direction_in
    new_weight_out = (
        weight_out * decay - MATRIX_RATE * 0.2 * math.sqrt(max(D, INNER)) * direction_out
    )
    new_moment_small = MOMENTUM * moment_small + grad_small
    new_small_params = small_params - SMALL_RATE * new_moment_small
    return (
        outputs,
        input_grad,
        grad_in,
        grad_out,
        grad_small,
        new_moment_in,
        new_moment_out,
        new_moment_small,
        new_weight_in,
        new_weight_out,
        new_small_params,
    )


def solution(mesh):
    return jax.shard_map(
        shards,
        mesh=mesh,
        in_specs=(
            P(("dp", "fsdp"), None, None),
            P(("dp", "fsdp"), None, None),
            P(("dp", "fsdp"), None),
            P(("dp", "fsdp"), None),
            P(),
            P(("dp", "fsdp"), None),
            P(("dp", "fsdp"), None),
            P(),
        ),
        out_specs=(
            P(("dp", "fsdp"), None, None),
            P(("dp", "fsdp"), None, None),
            P(("dp", "fsdp"), None),
            P(("dp", "fsdp"), None),
            P(),
            P(("dp", "fsdp"), None),
            P(("dp", "fsdp"), None),
            P(),
            P(("dp", "fsdp"), None),
            P(("dp", "fsdp"), None),
            P(),
        ),
        check_vma=False,
    )
```

```python
import functools
import math

import jax
import jax.numpy as jnp
from jax import lax
from jax.experimental import pallas as pl
from jax.experimental.pallas import tpu as pltpu
from jax.sharding import PartitionSpec as P

D = 768
HEADS = 24
HEAD_DIM = 64
NSTATE = 128
KCONV = 4
LEN = 1024
ITERS = 5
INNER = 1536
CONVCH = 1792
IN_W = 3352
WIDE = INNER + CONVCH
STEP = 32
HALF = 2560
OUT_AT = WIDE - HALF
STEP_AT = OUT_AT + INNER

MOMENTUM = 0.95
MATRIX_RATE = 0.15
WEIGHT_DECAY = 0.1
SMALL_RATE = 0.01
EPSILON = 1e-05
COEF_A = 3.4445
COEF_B = -4.775
COEF_C = 2.0315

F32 = jnp.float32
BF16 = jnp.bfloat16
CHUNK = 128
STRIP = 256
PER = STRIP // CHUNK
STRIPS = LEN // STRIP
GROUP = 4


def dot(a, b):
    return lax.dot_general(a, b, (((1,), (0,)), ((), ())), preferred_element_type=F32)


def dot_nt(a, b):
    return lax.dot_general(a, b, (((1,), (1,)), ((), ())), preferred_element_type=F32)


def dot_tn(a, b):
    return lax.dot_general(a, b, (((0,), (0,)), ((), ())), preferred_element_type=F32)


def split(v):
    high = v.astype(BF16)
    return high, (v - high.astype(F32)).astype(BF16)


def beside(*parts):
    return jnp.concatenate(parts, axis=1)


def above(*parts):
    return jnp.concatenate(parts, axis=0)


def right_pair(b):
    high, low = split(b)
    return above(beside(high, low), beside(high, jnp.zeros_like(low)))


def three_pass(a, pair):
    high, low = split(a)
    both = dot(beside(high, low), pair)
    half = both.shape[1] // 2
    return both[:, :half] + both[:, half:]


def exact_sum(a, ones):
    high = a.astype(BF16)
    rest = a - high.astype(F32)
    mid = rest.astype(BF16)
    low = (rest - mid.astype(F32)).astype(BF16)
    return dot(beside(high, mid, low), above(ones, ones, ones))


def stack_left(a):
    high, low = split(a)
    return above(beside(high, high), beside(low, jnp.zeros_like(low)))


def fold(rows):
    total = rows[0:8]
    for i in range(1, rows.shape[0] // 8):
        total = total + rows[8 * i : 8 * i + 8]
    return total


def row_sum(rows):
    return jnp.sum(fold(rows), axis=0, keepdims=True)


def upper():
    row = lax.broadcasted_iota(jnp.int32, (CHUNK, CHUNK), 0)
    col = lax.broadcasted_iota(jnp.int32, (CHUNK, CHUNK), 1)
    return col >= row


def softplus(v):
    return jnp.maximum(v, 0.0) + jnp.log1p(jnp.exp(-jnp.abs(v)))


def rates_of(raw, heads_ref, ones):
    steps = softplus(raw + heads_ref[0])
    logs = exact_sum(steps * heads_ref[1], ones)
    last = jnp.broadcast_to(logs[:, CHUNK - 1 : CHUNK], logs.shape)
    columns = above(logs, jnp.zeros((CHUNK - HEADS, CHUNK), F32)).T
    return steps, logs, columns, jnp.exp(logs), jnp.exp(last - logs), jnp.exp(last)


def silu(v):
    return v * jax.nn.sigmoid(v)


def wide(v):
    return beside(*([v] * PER))


def forward_kernel(
    sizes, x_ref, back_ref, first_ref, second_ref, gain_ref, taps_ref, heads_ref, inner_ref,
    blocks_ref, out_ref, hb_ref, cin_ref, c_ref, raw_ref, s_ref, normed_ref,
    dy_ref, dgate_ref, dlogs_ref, dskip_ref, dinner_ref, moved_ref,
    act, z, mixed, dnormed, state, tail, turned, *work,
):
    p = Place(sizes)
    swap = Swap(p, blocks_ref, moved_ref, *work)

    @pl.when(pl.program_id(0) == 0)
    def _():
        greet_all(p)
        swap.start()
        state[...] = jnp.zeros_like(state)
        tail[...] = jnp.zeros_like(tail)
        dskip_ref[...] = jnp.zeros_like(dskip_ref)
        dinner_ref[...] = jnp.zeros_like(dinner_ref)
        for i in range(HALF // 256):
            part = slice(256 * i, 256 * i + 256)
            turned[0, part] = first_ref[:, part].T
            turned[1, part] = second_ref[:, part].T

    x = x_ref[...].astype(F32)
    scaled = x * lax.rsqrt(jnp.mean(x * x, axis=-1, keepdims=True) + EPSILON) * gain_ref[...]
    hb = scaled.astype(BF16)
    hb_ref[...] = hb
    back = back_ref[...]
    for i in range(INNER // 256):
        part = slice(256 * i, 256 * i + 256)
        z[part] = dot_nt(turned[0, part], hb)
        dnormed[part] = dot_nt(turned[1, OUT_AT + 256 * i : OUT_AT + 256 * i + 256], back)
    for i in range(CONVCH // 256):
        start = INNER + 256 * i
        rows = turned[start // HALF, start % HALF : start % HALF + 256]
        cin_ref[256 * i : 256 * i + 256] = dot_nt(rows, hb)
    raw_ref[...] = dot_nt(turned[1, STEP_AT : STEP_AT + STEP], hb)

    lane = lax.broadcasted_iota(jnp.int32, (64, CHUNK), 1)

    def later(cols, steps, before):
        turned_cols = [before] + [pltpu.roll(col, steps, 1) for col in cols]
        pairs = zip(turned_cols[:-1], turned_cols[1:])
        return [jnp.where(lane < steps, a, b) for a, b in pairs], turned_cols[-1]

    def conv_tile(i, carry):
        rows = pl.ds(pl.multiple_of(i * 64, 64), 64)
        cur = cin_ref[rows, :]
        cols = [cur[:, CHUNK * j : CHUNK * j + CHUNK] for j in range(PER)]
        taps = [taps_ref[k, rows, :] for k in range(KCONV + 1)]
        ones_late, tail[0, rows, :] = later(cols, 1, tail[0, rows, :])
        early = [taps[1] * a + taps[0] * b for a, b in zip(cols, ones_late)]
        twos_late, tail[1, rows, :] = later(early, 2, tail[1, rows, :])
        total = beside(*[
            taps[4] + c + taps[2] * b + taps[3] * a for a, b, c in zip(cols, ones_late, twos_late)
        ])
        c_ref[rows, :] = total
        act[rows, :] = total * jax.nn.sigmoid(total)
        return carry

    lax.fori_loop(0, CONVCH // 64, conv_tile, 0, unroll=4)
    causal = upper()
    ones = causal.astype(F32).astype(BF16)

    def chunk(j, carry):
        cols = pl.ds(pl.multiple_of(j * CHUNK, CHUNK), CHUNK)
        steps, logs, columns, grown, to_end, through = rates_of(
            raw_ref[0:HEADS, cols], heads_ref, ones
        )
        in_map = act[INNER : INNER + NSTATE, cols].T
        in_pair = right_pair(in_map)
        out_pair = right_pair(act[INNER + NSTATE :, cols])
        scores = three_pass(in_map, out_pair)
        for g in range(HEADS // GROUP):
            rows = slice(g * GROUP * HEAD_DIM, (g + 1) * GROUP * HEAD_DIM)
            held = state[rows]
            s_ref[j, rows] = held
            across = three_pass(held, out_pair)
            ending, kept = [], []
            for q in range(GROUP):
                h = g * GROUP + q
                mine = slice(h * HEAD_DIM, (h + 1) * HEAD_DIM)
                values = act[mine, cols]
                fed = values * steps[h : h + 1]
                gaps = logs[h : h + 1] - jnp.broadcast_to(columns[:, h : h + 1], (CHUNK, CHUNK))
                weights = scores * jnp.where(causal, jnp.exp(gaps), 0.0)
                both = dot(stack_left(fed), above(*split(weights)))
                y = both[:HEAD_DIM] + both[HEAD_DIM:]
                y = y + across[q * HEAD_DIM : (q + 1) * HEAD_DIM] * grown[h : h + 1]
                mixed[mine, cols] = y + heads_ref[2][h : h + 1] * values
                ending.append(fed * to_end[h : h + 1])
                kept.append(jnp.broadcast_to(through[h : h + 1], (HEAD_DIM, CHUNK)))
            state[rows] = held * above(*kept) + three_pass(above(*ending), in_pair)
        return carry

    lax.fori_loop(0, PER, chunk, 0)

    def mean_tile(h, totals):
        rows = pl.ds(pl.multiple_of(h * HEAD_DIM, HEAD_DIM), HEAD_DIM)
        gate = z[rows, :]
        opened = mixed[rows, :] * (gate * jax.nn.sigmoid(gate))
        gained = dnormed[rows, :] * wide(inner_ref[rows, :]) * opened
        return totals[0] + fold(opened * opened), totals[1] + fold(gained)

    nothing = jnp.zeros((8, STRIP), F32)
    squares, gains = lax.fori_loop(0, HEADS, mean_tile, (nothing, nothing))
    mean = jnp.sum(squares, axis=0, keepdims=True) * (1.0 / INNER)
    r = lax.rsqrt(mean + EPSILON)
    pulled = jnp.sum(gains, axis=0, keepdims=True) * (1.0 / INNER) * (r * r * r)

    def gate_tile(h, carry):
        rows = pl.ds(pl.multiple_of(h * HEAD_DIM, HEAD_DIM), HEAD_DIM)
        gate = z[rows, :]
        skip = wide(heads_ref[2, pl.ds(h, 1), :])
        mix = mixed[rows, :]
        sig = jax.nn.sigmoid(gate)
        sil = gate * sig
        opened = mix * sil
        normed = opened * r
        inner = wide(inner_ref[rows, :])
        normed_ref[rows, :] = (normed * inner).astype(BF16)
        dn = dnormed[rows, :]
        gained = dn * normed
        dinner_ref[rows, :] += gained[:, :CHUNK] + gained[:, CHUNK:]
        dopened = dn * inner * r - opened * pulled
        dmixed = dopened * sil
        dy_ref[rows, :] = dmixed
        dgate_ref[rows, :] = (dopened * mix * (sig * (1.0 + gate * (1.0 - sig)))).astype(BF16)
        skipped = row_sum(dmixed * act[rows, :])
        dskip_ref[pl.ds(h, 1), :] += skipped[:, :CHUNK] + skipped[:, CHUNK:]
        dlogs_ref[pl.ds(h, 1), :] = row_sum(dmixed * mix) - skip * skipped
        return carry

    lax.fori_loop(0, HEADS, gate_tile, 0)
    for i in range(D // 256):
        part = slice(256 * i, 256 * i + 256)
        branch = dot(second_ref[part, OUT_AT:STEP_AT], normed_ref[...]).T
        out_ref[:, part] = (x_ref[:, part].astype(F32) + branch).astype(BF16)

    @pl.when(pl.program_id(0) == STRIPS - 1)
    def _():
        swap.wait()


def backward_kernel(
    sizes, x_ref, back_ref, first_ref, second_ref, gain_ref, taps_ref, heads_ref,
    cin_ref, c_ref, raw_ref, s_ref, dy, dgate_ref, dlogs, out_part, gate_part,
    dx_ref, dconv_ref, dstep_ref, dgain_ref, dtaps_ref, dheads_ref, out_column, gate_column,
    dact, dstate, flow, tail, meets, vdu_rows, *work,
):
    step_now = pl.program_id(0)
    p = Place(sizes)
    sums = [
        PlaneSum(p, part, work[8 * k : 8 * k + 8]) for k, part in enumerate((out_part, gate_part))
    ]

    @pl.when(step_now == 0)
    def _():
        greet_near(p, False)
        sums[0].begin()

    @pl.when(step_now == 1)
    def _():
        sums[1].pair()

    @pl.when(step_now == 0)
    def _():
        dstate[...] = jnp.zeros_like(dstate)
        flow[...] = jnp.zeros_like(flow)
        tail[...] = jnp.zeros_like(tail)
        dgain_ref[...] = jnp.zeros_like(dgain_ref)
        dtaps_ref[...] = jnp.zeros_like(dtaps_ref)
        dheads_ref[...] = jnp.zeros_like(dheads_ref)

    back = back_ref[...]

    causal = upper()
    ones = causal.astype(F32).astype(BF16)
    row = lax.broadcasted_iota(jnp.int32, (CHUNK, CHUNK), 0)
    col = lax.broadcasted_iota(jnp.int32, (CHUNK, CHUNK), 1)
    ones_back = (row >= col).astype(F32).astype(BF16)

    def chunk(step, carry):
        j = PER - 1 - step
        cols = pl.ds(pl.multiple_of(j * CHUNK, CHUNK), CHUNK)
        raw = raw_ref[0:HEADS, cols]
        steps, logs, columns, grown, to_end, through = rates_of(raw, heads_ref, ones)
        in_turned = silu(c_ref[INNER : INNER + NSTATE, cols])
        out_turned = silu(c_ref[INNER + NSTATE :, cols])
        in_map = in_turned.T
        out_map = out_turned.T
        scores = three_pass(in_map, right_pair(out_turned))
        in_pair = right_pair(in_turned)
        out_pair = right_pair(out_map)
        dscores = jnp.zeros((CHUNK, CHUNK), F32)
        din = jnp.zeros((NSTATE, CHUNK), F32)
        dout = jnp.zeros((NSTATE, CHUNK), F32)
        for g in range(HEADS // GROUP):
            rows = slice(g * GROUP * HEAD_DIM, (g + 1) * GROUP * HEAD_DIM)
            leaving = dstate[rows]
            entering = s_ref[j, rows]
            from_state = three_pass(leaving, in_pair)
            ending, growing, kept = [], [], []
            for q in range(GROUP):
                h = g * GROUP + q
                mine = slice(h * HEAD_DIM, (h + 1) * HEAD_DIM)
                values = silu(c_ref[mine, cols])
                fed = values * steps[h : h + 1]
                dys = dy[mine, cols]
                gaps = logs[h : h + 1] - jnp.broadcast_to(columns[:, h : h + 1], (CHUNK, CHUNK))
                decay = jnp.where(causal, jnp.exp(gaps), 0.0)
                weights = scores * decay
                both = dot_nt(stack_left(dys), beside(*split(weights)))
                du = both[:HEAD_DIM] + both[HEAD_DIM:]
                du = du + from_state[q * HEAD_DIM : (q + 1) * HEAD_DIM] * to_end[h : h + 1]
                fed_high, fed_low = split(fed)
                dy_high, dy_low = split(dys)
                dweights = dot_tn(
                    above(fed_high, fed_low, fed_high), above(dy_high, dy_high, dy_low)
                )
                dscores = dscores + dweights * decay
                vdu_rows[h : h + 1, :] = row_sum(values * du)
                dact[mine, cols] = du * steps[h : h + 1] + heads_ref[2][h : h + 1] * dys
                ending.append(fed * to_end[h : h + 1])
                growing.append(dys * grown[h : h + 1])
                kept.append(jnp.broadcast_to(through[h : h + 1], (HEAD_DIM, CHUNK)))
            ending = above(*ending)
            growing = above(*growing)
            end_high, end_low = split(ending)
            grow_high, grow_low = split(growing)
            leave_high, leave_low = split(leaving)
            enter_high, enter_low = split(entering)
            din = din + dot_tn(
                above(leave_high, leave_low, leave_high), above(end_high, end_high, end_low)
            )
            dout = dout + dot_tn(
                above(enter_high, enter_low, enter_high), above(grow_high, grow_high, grow_low)
            )
            arrived = leaving * above(*kept) + three_pass(growing, out_pair)
            dstate[rows] = arrived
            meet = arrived * entering
            for q in range(GROUP):
                h = g * GROUP + q
                meets[h : h + 1, :] = row_sum(meet[q * HEAD_DIM : (q + 1) * HEAD_DIM])
        vdu = vdu_rows[...]
        dlog = dlogs[:, cols] - steps * vdu
        drate = exact_sum(dlog, ones_back) + flow[...]
        flow[...] = jnp.broadcast_to(
            jnp.sum(meets[...], axis=1, keepdims=True), (HEADS, CHUNK)
        )
        dsteps = vdu + heads_ref[1] * drate
        draw = dsteps * jax.nn.sigmoid(raw + heads_ref[0])
        dheads_ref[0] += draw
        dheads_ref[1] += drate * steps * heads_ref[1]
        dstep_ref[:, cols] = above(draw, jnp.zeros((STEP - HEADS, CHUNK), F32)).astype(BF16)
        score_high, score_low = split(dscores)
        both = dot_nt(stack_left(out_turned), beside(score_high, score_low))
        dact[INNER : INNER + NSTATE, cols] = din + both[:NSTATE] + both[NSTATE:]
        both = dot(stack_left(in_turned), above(score_high, score_low))
        dact[INNER + NSTATE :, cols] = dout + both[:NSTATE] + both[NSTATE:]
        return carry

    lax.fori_loop(0, PER, chunk, 0)

    @pl.when(step_now == 0)
    def _():
        sums[0].pair()
        sums[0].plane.start(0)
        sums[1].begin()

    @pl.when(step_now == 1)
    def _():
        sums[0].plane.finish(0)
        sums[1].plane.start(0)

    @pl.when(step_now == 2)
    def _():
        sums[1].plane.finish(0)
        sums[0].plane.start(1)
        sums[1].plane.start(1)

    lane = lax.broadcasted_iota(jnp.int32, (64, CHUNK), 1)

    def conv_tile(i, carry):
        rows = pl.ds(pl.multiple_of(i * 64, 64), 64)
        c = c_ref[rows, :]
        sig = jax.nn.sigmoid(c)
        dpre = dact[rows, :] * (sig * (1.0 + c * (1.0 - sig)))
        cin = cin_ref[rows, :]
        cols = [dpre[:, CHUNK * j : CHUNK * j + CHUNK] for j in range(PER)]
        dcin = dpre * wide(taps_ref[KCONV - 1, rows, :])
        grad = cin * dpre
        dtaps_ref[KCONV - 1, rows, :] += grad[:, :CHUNK] + grad[:, CHUNK:]
        dtaps_ref[KCONV, rows, :] += dpre[:, :CHUNK] + dpre[:, CHUNK:]
        for k in range(KCONV - 1):
            ahead = KCONV - 1 - k
            turned = [pltpu.roll(col, CHUNK - ahead, 1) for col in cols] + [tail[k, rows, :]]
            tail[k, rows, :] = turned[0]
            pairs = zip(turned[:-1], turned[1:])
            shifted = beside(*[jnp.where(lane < CHUNK - ahead, a, b) for a, b in pairs])
            dcin = dcin + shifted * wide(taps_ref[k, rows, :])
            grad = cin * shifted
            dtaps_ref[k, rows, :] += grad[:, :CHUNK] + grad[:, CHUNK:]
        dconv_ref[rows, :] = dcin.astype(BF16)
        return carry

    lax.fori_loop(0, CONVCH // 64, conv_tile, 0, unroll=4)
    x = x_ref[...].astype(F32)
    r = lax.rsqrt(jnp.mean(x * x, axis=-1, keepdims=True) + EPSILON)
    parts = []
    for i in range(D // 256):
        part = slice(256 * i, 256 * i + 256)
        total = dot(first_ref[part, :INNER], dgate_ref[...])
        total = total + dot(first_ref[part, INNER:], dconv_ref[: HALF - INNER])
        total = total + dot(second_ref[part, :OUT_AT], dconv_ref[HALF - INNER :])
        step = second_ref[part, STEP_AT : STEP_AT + STEP]
        parts.append((total + dot(step, dstep_ref[...])).T)
    dscaled = beside(*parts)
    plain = x * r
    dgain_ref[...] += fold(dscaled * plain)
    gained = dscaled * gain_ref[...]
    inner = jnp.mean(gained * plain, axis=-1, keepdims=True)
    dx_ref[...] = back.astype(F32) + (gained - plain * inner) * r

    @pl.when(step_now == STRIPS - 1)
    def _():
        for part, column in zip(sums, (out_column, gate_column)):
            part.plane.finish(1)
            column[...] = part.column()


def whole(shape):
    return pl.BlockSpec(shape, lambda i: (0,) * len(shape), pipeline_mode=pl.Buffered(1))


def strip_rows(width):
    return pl.BlockSpec((STRIP, width), lambda i: (i, 0))


def strip_cols(height):
    return pl.BlockSpec((height, STRIP), lambda i: (0, i))


def shape(*dims, dtype=F32):
    return jax.ShapeDtypeStruct(dims, dtype)


def half(k, *dims):
    return pl.BlockSpec((None,) + dims, lambda i: (k, 0, 0), pipeline_mode=pl.Buffered(1))


def forward_call(x, back, weights, gain, taps, heads, inner, blocks, sizes, collective_id):
    count = sizes[0] * sizes[1]
    dma = pltpu.SemaphoreType.DMA
    hbm = pl.BlockSpec(memory_space=pl.ANY)
    return pl.pallas_call(
        functools.partial(forward_kernel, sizes),
        grid=(STRIPS,),
        in_specs=[
            strip_rows(D), strip_rows(D), half(0, D, HALF), half(1, D, HALF), whole((1, D)),
            whole((KCONV + 1, CONVCH, CHUNK)), whole((3, HEADS, CHUNK)), whole((INNER, CHUNK)),
            hbm,
        ],
        out_specs=[
            strip_rows(D), strip_rows(D), strip_cols(CONVCH), strip_cols(CONVCH),
            strip_cols(STEP), pl.BlockSpec((PER, INNER, NSTATE), lambda i: (i, 0, 0)),
            strip_cols(INNER), strip_cols(INNER), strip_cols(INNER), strip_cols(HEADS),
            whole((HEADS, CHUNK)), whole((INNER, CHUNK)), hbm,
        ],
        out_shape=[
            shape(LEN, D, dtype=BF16), shape(LEN, D, dtype=BF16), shape(CONVCH, LEN),
            shape(CONVCH, LEN), shape(STEP, LEN), shape(LEN // CHUNK, INNER, NSTATE),
            shape(INNER, LEN, dtype=BF16), shape(INNER, LEN), shape(INNER, LEN, dtype=BF16),
            shape(HEADS, LEN), shape(HEADS, CHUNK), shape(INNER, CHUNK), shape(*blocks.shape),
        ],
        scratch_shapes=[
            pltpu.VMEM((CONVCH, STRIP), F32), pltpu.VMEM((INNER, STRIP), F32),
            pltpu.VMEM((INNER, STRIP), F32), pltpu.VMEM((INNER, STRIP), F32),
            pltpu.VMEM((INNER, NSTATE), F32), pltpu.VMEM((2, CONVCH, CHUNK), F32),
            pltpu.VMEM((2, HALF, D), BF16), dma((count,)), dma((count,)), dma,
        ],
        compiler_params=pltpu.CompilerParams(
            vmem_limit_bytes=60 * 2**20, collective_id=collective_id, has_side_effects=True
        ),
        name="mixer_forward",
    )(x, back, weights, weights, gain, taps, heads, inner, blocks)


def backward_call(x, back, weights, gain, taps, heads, kept, parts, sizes, collective_id):
    last = STRIPS - 1

    def rows(width):
        return pl.BlockSpec((STRIP, width), lambda i: (last - i, 0))

    def cols(height):
        return pl.BlockSpec((height, STRIP), lambda i: (0, last - i))

    Z = sizes[0]
    size = (parts[0].shape[1], D)
    dma = pltpu.SemaphoreType.DMA
    hbm = pl.BlockSpec(memory_space=pl.ANY)
    return pl.pallas_call(
        functools.partial(backward_kernel, sizes),
        grid=(STRIPS,),
        in_specs=[
            rows(D), rows(D), half(0, D, HALF), half(1, D, HALF), whole((1, D)),
            whole((KCONV, CONVCH, CHUNK)), whole((3, HEADS, CHUNK)), cols(CONVCH),
            cols(CONVCH), cols(STEP),
            pl.BlockSpec((PER, INNER, NSTATE), lambda i: (last - i, 0, 0)), cols(INNER),
            cols(INNER), cols(HEADS), hbm, hbm,
        ],
        out_specs=[
            rows(D), cols(CONVCH), cols(STEP), whole((8, D)),
            whole((KCONV + 1, CONVCH, CHUNK)), whole((2, HEADS, CHUNK)), whole((Z,) + size),
            whole((Z,) + size),
        ],
        out_shape=[
            shape(LEN, D), shape(CONVCH, LEN, dtype=BF16), shape(STEP, LEN, dtype=BF16),
            shape(8, D), shape(KCONV + 1, CONVCH, CHUNK), shape(2, HEADS, CHUNK),
            shape(Z, *size), shape(Z, *size),
        ],
        scratch_shapes=[
            pltpu.VMEM((CONVCH, STRIP), F32),
            pltpu.VMEM((INNER, NSTATE), F32), pltpu.VMEM((HEADS, CHUNK), F32),
            pltpu.VMEM((KCONV - 1, CONVCH, CHUNK), F32), pltpu.VMEM((HEADS, CHUNK), F32),
            pltpu.VMEM((HEADS, CHUNK), F32),
        ]
        + 2 * sum_scratch(sizes, size),
        compiler_params=pltpu.CompilerParams(
            vmem_limit_bytes=63 * 2**20, collective_id=collective_id, has_side_effects=True
        ),
        name="mixer_backward",
    )(
        x, back, weights, weights, gain, taps, heads, *kept,
        *(by_place(part, sizes) for part in parts),
    )


def lanes(vector):
    return jnp.broadcast_to(vector[..., None], vector.shape + (CHUNK,))


def parameters(params):
    gain = params[:D].reshape(1, D)
    at = D
    taps = lanes(params[at : at + (KCONV + 1) * CONVCH].reshape(KCONV + 1, CONVCH))
    at += (KCONV + 1) * CONVCH
    heads = params[at : at + 3 * HEADS].reshape(3, HEADS)
    heads = lanes(jnp.stack([heads[0], -jnp.exp(heads[1]), heads[2]]))
    inner = lanes(params[at + 3 * HEADS :])
    return gain, taps, heads, inner


def block_and_gradients(x, back, weights, params, blocks, sizes, collective_ids):
    count = sizes[0] * sizes[1]
    gain, taps, heads, inner = parameters(params)
    out, hb, cin, c, raw, states, normed, dy, dgate, dlogs, dskip, dinner, moved = forward_call(
        x, back, weights, gain, taps, heads, inner, blocks, sizes, collective_ids[0]
    )
    parts = [dot(normed, back).reshape(count, -1, D), dot(dgate, hb).reshape(count, -1, D)]
    dx, dconv, dstep, dgain, dtaps, dheads, out_column, gate_column = backward_call(
        x, back, weights, gain, taps, heads, (cin, c, raw, states, dy, dgate, dlogs), parts,
        sizes, collective_ids[1],
    )
    grad_conv = dot(dconv, hb)
    grad_step = dot(dstep, hb)[:HEADS]
    small = jnp.concatenate(
        [
            jnp.sum(dgain, axis=0),
            jnp.sum(dtaps, axis=-1).reshape(-1),
            jnp.sum(dheads, axis=-1).reshape(-1),
            jnp.sum(dskip, axis=-1),
            jnp.sum(dinner, axis=-1),
        ]
    )
    return out, dx, (out_column, gate_column), grad_conv, grad_step, small, moved


MESH = pl.DeviceIdType.MESH


class Place:
    def __init__(self, sizes):
        self.Z, self.F = sizes
        self.C, self.Y = 2, 2
        self.X = self.F // 4
        f = lax.axis_index("fsdp")
        self.z = lax.axis_index("dp")
        self.c = lax.rem(f, 2)
        self.x = lax.rem(f // 2, self.X)
        self.y = f // (2 * self.X)
        self.f = f

    def at(self, z=None, y=None, x=None, c=None):
        z = self.z if z is None else z
        y = self.y if y is None else y
        x = self.x if x is None else x
        c = self.c if c is None else c
        return (z, (y * self.X + x) * 2 + c)

    def other_x(self, step):
        return lax.rem(self.x + step, self.X)


def signal(device):
    pl.semaphore_signal(
        pltpu.get_barrier_semaphore(), inc=1, device_id=device, device_id_type=MESH
    )


def greet_all(place):
    count = place.Z * place.F
    me = place.z * place.F + place.f

    def step(i, carry):
        peer = lax.rem(me + i, count)
        signal((peer // place.F, lax.rem(peer, place.F)))
        return carry

    lax.fori_loop(1, count, step, 0)
    pl.semaphore_wait(pltpu.get_barrier_semaphore(), count - 1)


def remote(src, dst, send, recv, device):
    return pltpu.make_async_remote_copy(
        src_ref=src, dst_ref=dst, send_sem=send, recv_sem=recv, device_id=device,
        device_id_type=MESH,
    )


def add_blocks(dst, src, count):
    def step(i, carry):
        target = dst(i)
        target[...] = target[...] + src(i)[...]
        return carry

    lax.fori_loop(0, count, step, 0)


class Swap:
    def __init__(self, place, src, dst, send, recv, local, same=False, narrow=None):
        self.place, self.src, self.dst, self.same, self.narrow = place, src, dst, same, narrow
        self.send, self.recv, self.local = send, recv, local
        self.count = place.Z * place.F
        self.me = place.z * place.F + place.f

    def block(self, peer):
        return self.src if self.same else self.src.at[peer]

    def cut(self, ref, odd):
        return ref.at[:, pl.ds(0, self.narrow)] if odd else ref

    def each(self, sender, act):
        if self.narrow is None:
            act(False)
        else:
            @pl.when(lax.rem(sender, 2) == 0)
            def _():
                act(False)

            @pl.when(lax.rem(sender, 2) == 1)
            def _():
                act(True)

    def to(self, i, odd):
        peer = lax.rem(self.me + i, self.count)
        return remote(
            self.cut(self.block(peer), odd), self.cut(self.dst.at[self.me], odd),
            self.send.at[i], self.recv.at[i],
            (peer // self.place.F, lax.rem(peer, self.place.F)),
        )

    def keep(self):
        return pltpu.make_async_copy(self.block(self.me), self.dst.at[self.me], self.local)

    def start(self):
        self.keep().start()

        def step(i, carry):
            self.each(self.me, lambda odd: self.to(i, odd).start())
            return carry

        lax.fori_loop(1, self.count, step, 0)

    def wait(self):
        self.keep().wait()

        def step(i, carry):
            sender = lax.rem(self.me + self.count - i, self.count)
            self.each(self.me, lambda odd: self.to(i, odd).wait_send())
            self.each(sender, lambda odd: remote(
                self.cut(self.block(sender), odd), self.cut(self.dst.at[sender], odd),
                self.send.at[i], self.recv.at[i],
                (sender // self.place.F, lax.rem(sender, self.place.F)),
            ).wait_recv())
            return carry

        lax.fori_loop(1, self.count, step, 0)


def greet_near(place, along_z):
    signal(place.at(c=1 - place.c))
    signal(place.at(y=1 - place.y))
    for s in range(1, place.X):
        signal(place.at(x=place.other_x(s)))
    if along_z:
        for s in range(1, place.Z):
            signal(place.at(z=lax.rem(place.z + s, place.Z)))
    pl.semaphore_wait(
        pltpu.get_barrier_semaphore(), place.X + 1 + (place.Z - 1 if along_z else 0)
    )


class Plane:
    def __init__(self, place, acc, x1, y1, x2, y2, sems):
        self.p, self.acc = place, acc
        self.x1, self.y1, self.x2, self.y2, self.sems = x1, y1, x2, y2, sems
        self.h = place.Z // 2

    def copies(self, stage):
        p, acc, h = self.p, self.acc, self.h
        low, high = pl.ds(0, h), pl.ds(h, p.Z - h)
        out = []
        base = stage * p.X
        for s in range(1, p.X):
            x = p.other_x(s)
            if stage == 0:
                src, dst = acc.at[low, :, x], self.x1.at[s - 1]
            else:
                src, dst = acc.at[high, p.y, x], self.x2.at[s - 1]
            sem = self.sems.at[base + s]
            out.append(remote(src, dst, sem.at[0], sem.at[1], p.at(x=x)))
        if stage == 0:
            src, dst = acc.at[high, 1 - p.y], self.y1
        else:
            src, dst = acc.at[low, 1 - p.y, p.x], self.y2
        sem = self.sems.at[base]
        out.append(remote(src, dst, sem.at[0], sem.at[1], p.at(y=1 - p.y)))
        return out

    def start(self, stage):
        for copy in self.copies(stage):
            copy.start()

    def finish(self, stage):
        p, acc, h = self.p, self.acc, self.h
        for copy in self.copies(stage):
            copy.wait()
        for s in range(p.X - 1):
            if stage == 0:
                add_blocks(
                    lambda i: acc.at[i // p.Y, lax.rem(i, p.Y), p.x],
                    lambda i: self.x1.at[s, i // p.Y, lax.rem(i, p.Y)],
                    h * p.Y,
                )
            else:
                add_blocks(
                    lambda i: acc.at[h + i, p.y, p.x], lambda i: self.x2.at[s, i], p.Z - h
                )
        if stage == 0:
            add_blocks(
                lambda i: acc.at[h + i // p.X, p.y, lax.rem(i, p.X)],
                lambda i: self.y1.at[i // p.X, lax.rem(i, p.X)],
                (p.Z - h) * p.X,
            )
        else:
            add_blocks(lambda i: acc.at[i, p.y, p.x], lambda i: self.y2.at[i], h)


def plane_scratch(sizes, block):
    Z, X, Y = sizes[0], sizes[1] // 4, 2
    h = Z // 2
    return [
        pltpu.VMEM((Z, Y, X) + block, F32), pltpu.VMEM((X - 1, h, Y) + block, F32),
        pltpu.VMEM((Z - h, X) + block, F32), pltpu.VMEM((X - 1, Z - h) + block, F32),
        pltpu.VMEM((h,) + block, F32), pltpu.SemaphoreType.DMA((2 * X, 2)),
    ]


def sum_scratch(sizes, block):
    Z, X, Y = sizes[0], sizes[1] // 4, 2
    return plane_scratch(sizes, block) + [
        pltpu.VMEM((Z, Y, X) + block, F32), pltpu.SemaphoreType.DMA((3,)),
    ]


def by_place(blocks, sizes):
    return blocks.reshape((sizes[0], 2, sizes[1] // 4, 2) + blocks.shape[1:])


class PlaneSum:
    def __init__(self, place, part, work):
        self.p, self.part = place, part
        self.acc, self.core, self.sems = work[0], work[6], work[7]
        self.plane = Plane(place, *work[:6])

    def copies(self):
        p = self.p
        return (
            remote(
                self.part.at[:, :, :, 1 - p.c], self.core, self.sems.at[0], self.sems.at[1],
                p.at(c=1 - p.c),
            ),
            pltpu.make_async_copy(self.part.at[:, :, :, p.c], self.acc, self.sems.at[2]),
        )

    def begin(self):
        for copy in self.copies():
            copy.start()

    def pair(self):
        p = self.p
        for copy in self.copies():
            copy.wait()

        def place_of(i):
            return i // (p.Y * p.X), lax.rem(i // p.X, p.Y), lax.rem(i, p.X)

        add_blocks(
            lambda i: self.acc.at[place_of(i)], lambda i: self.core.at[place_of(i)],
            p.Z * p.Y * p.X,
        )

    def block(self, z):
        return self.acc.at[z, self.p.y, self.p.x]

    def column(self):
        return self.acc[:, self.p.y, self.p.x]


class Column:
    def __init__(self, part, acc, sem):
        self.copy = pltpu.make_async_copy(part, acc, sem)
        self.acc = acc

    def block(self, z):
        return self.acc.at[z]


class Chain:
    def __init__(self, place, part, held, sems):
        self.p, self.part, self.held, self.sems = place, part, held, sems

    def flow(self, t, right):
        p, side = self.p, 0 if right else 1
        sem = self.sems.at[side, t]
        target = p.at(z=p.z + 1 if right else p.z - 1)
        return remote(self.part.block(t), self.held.at[side, t], sem.at[0], sem.at[1], target)

    def send(self, t, right):
        @pl.when(self.p.z < t if right else self.p.z > t)
        def _():
            self.flow(t, right).start()

    def first(self):
        p = self.p
        for j in range(p.Z - 1):
            @pl.when(p.z == 0)
            def _():
                self.send(p.Z - 1 - j, True)

            @pl.when(p.z == p.Z - 1)
            def _():
                self.send(j, False)

    def receive(self, t, right):
        p = self.p

        @pl.when(jnp.logical_and(p.z > 0, p.z <= t) if right else
                 jnp.logical_and(p.z < p.Z - 1, p.z >= t))
        def _():
            self.flow(t, right).wait_recv()
            mine = self.part.block(t)
            mine[...] = mine[...] + self.held[0 if right else 1, t]

    def pass_on(self, j, right):
        p = self.p
        t = p.Z - 1 - j if right else j
        self.receive(t, right)

        @pl.when(p.z > 0 if right else p.z < p.Z - 1)
        def _():
            self.send(t, right)

    def run(self):
        p = self.p
        for j in range(p.Z):
            @pl.when(p.z < p.Z // 2)
            def _():
                self.pass_on(j, True)
                self.pass_on(j, False)

            @pl.when(p.z >= p.Z // 2)
            def _():
                self.pass_on(j, False)
                self.pass_on(j, True)

    def finish(self):
        p = self.p
        for t in range(p.Z):
            for right in (True, False):
                @pl.when(p.z < t if right else p.z > t)
                def _():
                    self.flow(t, right).wait_send()


def scatter_kernel(sizes, columns, parts, *refs):
    total = columns + parts
    ins, outs, rest = refs[:total], refs[total : 2 * total], list(refs[2 * total :])
    p = Place(sizes)
    found, chains = [], []
    for k in range(total):
        if k < columns:
            found.append(Column(ins[k], *rest[:2]))
            rest = rest[2:]
        else:
            found.append(PlaneSum(p, ins[k], rest[:8]))
            rest = rest[8:]
        chains.append(Chain(p, found[k], *rest[:2]))
        rest = rest[2:]
    greet_near(p, True)
    for column in found[:columns]:
        column.copy.start()
    for part in found[columns:]:
        part.begin()
    for k in range(columns):
        found[k].copy.wait()
        chains[k].first()
    for part in found[columns:]:
        part.pair()
        part.plane.start(0)
    for k in range(columns):
        chains[k].run()
    for part in found[columns:]:
        part.plane.finish(0)
        part.plane.start(1)
    for k in range(columns, total):
        found[k].plane.finish(1)
        chains[k].first()
    for k in range(columns, total):
        chains[k].run()
    for k in range(total):
        chains[k].finish()
        outs[k][...] = found[k].block(p.z)[...]


def scatter_call(columns, parts, sizes, collective_id):
    Z = sizes[0]
    scratch = []
    for k, b in enumerate(columns + parts):
        block = b.shape[1:]
        if k < len(columns):
            scratch += [pltpu.VMEM(b.shape, F32), pltpu.SemaphoreType.DMA]
        else:
            scratch += sum_scratch(sizes, block)
        scratch += [pltpu.VMEM((2, Z) + block, F32), pltpu.SemaphoreType.DMA((2, Z, 2))]
    total = len(columns) + len(parts)
    return pl.pallas_call(
        functools.partial(scatter_kernel, sizes, len(columns), len(parts)),
        out_shape=[jax.ShapeDtypeStruct(b.shape[1:], F32) for b in columns + parts],
        in_specs=[pl.BlockSpec(memory_space=pl.ANY)] * total,
        out_specs=[pl.BlockSpec(memory_space=pltpu.VMEM)] * total,
        scratch_shapes=scratch,
        compiler_params=pltpu.CompilerParams(
            collective_id=collective_id, has_side_effects=True, vmem_limit_bytes=56 * 2**20
        ),
        name="scatter",
    )(*columns, *(by_place(b, sizes) for b in parts))


def gather_kernel(
    sizes, w_in_ref, w_out_ref, all_ref, both, mine, core_sems, z_sems, near, far, across,
):
    p = Place(sizes)
    Z, h = p.Z, p.Z // 2
    greet_all(p)
    own = both.shape[1]
    both[p.c, :, :WIDE] = w_in_ref[:, :WIDE]
    both[p.c, :, WIDE : WIDE + INNER] = w_out_ref[...]
    both[p.c, :, WIDE + INNER :] = jnp.concatenate(
        [w_in_ref[:, WIDE:], jnp.zeros((own, 2 * HALF - IN_W - INNER), F32)], axis=1
    )
    partner = p.at(c=1 - p.c)
    pair = remote(
        both.at[p.c], both.at[p.c], core_sems.at[0], core_sems.at[1], partner
    )
    pair.start()
    pair.wait_send()
    other = both.at[1 - p.c]
    remote(other, other, core_sems.at[0], core_sems.at[1], partner).wait_recv()
    for k in range(2):
        cols = slice(k * HALF, k * HALF + HALF)
        mine[k] = above(both[0, :, cols], both[1, :, cols]).astype(BF16)
    keeps = [
        pltpu.make_async_copy(mine.at[k], all_ref.at[k, p.z, p.y, p.x], core_sems.at[2 + k])
        for k in range(2)
    ]
    for keep in keeps:
        keep.start()

    def spot(z, y, x):
        return all_ref.at[p.c, z, y, x]

    def copy(src, dst, sem, device):
        return remote(src, dst, sem.at[0], sem.at[1], device)

    def along_z(z, right, src=None):
        here = spot(z, p.y, p.x)
        target = p.at(z=p.z + 1 if right else p.z - 1)
        return copy(here if src is None else src, here, z_sems.at[0 if right else 1, z], target)

    def near_copies(z, src=None):
        here = spot(z, p.y, p.x)
        src = here if src is None else src
        found = [copy(src, here, near.at[z, 0], p.at(y=1 - p.y))]
        for s in range(1, p.X):
            found.append(copy(src, here, near.at[z, s], p.at(x=p.other_x(s))))
        return found

    def near_arrivals(z):
        found = [(z, 1 - p.y, p.x, near.at[z, 0])]
        for s in range(1, p.X):
            found.append((z, p.y, lax.rem(p.x + p.X - s, p.X), near.at[z, s]))
        return found

    def far_copies(z):
        low, high = [], []
        for s in range(1, p.X):
            x = p.other_x(s)
            there = spot(z, p.y, x)
            low.append(copy(there, there, far.at[z, s], p.at(y=1 - p.y)))
            there = spot(z, 1 - p.y, p.x)
            high.append(copy(there, there, far.at[z, s], p.at(x=x)))
        return low, high

    def far_arrivals(z):
        low = [(z, 1 - p.y, p.other_x(s), far.at[z, s]) for s in range(1, p.X)]
        high = [
            (z, 1 - p.y, lax.rem(p.x + p.X - s, p.X), far.at[z, s]) for s in range(1, p.X)
        ]
        return low, high

    def to_partner(z, y, x):
        here = spot(z, y, x)
        return copy(here, here, across.at[z, y, x], partner)

    def await_block(z, y, x, sem):
        here = spot(z, y, x)
        copy(here, here, sem, partner).wait_recv()
        to_partner(z, y, x).start()

    def start_all(copies):
        for c in copies:
            c.start()

    @pl.when(p.z < Z - 1)
    def _():
        along_z(p.z, True, mine.at[p.c]).start()

    @pl.when(p.z > 0)
    def _():
        along_z(p.z, False, mine.at[p.c]).start()

    start_all(near_copies(p.z, mine.at[p.c]))

    def visit(right, z):
        await_block(z, p.y, p.x, z_sems.at[0 if right else 1, z])

        @pl.when(p.z < Z - 1 if right else p.z > 0)
        def _():
            along_z(z, right).start()

        start_all(near_copies(z))

    def by_distance(low, high):
        for j in range(1, Z):
            @pl.when(p.z - j >= 0)
            def _():
                low(p.z - j)

            @pl.when(p.z + j < Z)
            def _():
                high(p.z + j)

    by_distance(lambda z: visit(True, z), lambda z: visit(False, z))

    def relay(z):
        for block in near_arrivals(z):
            await_block(*block)
        low, high = far_copies(z)

        @pl.when(z < h)
        def _():
            start_all(low)

        @pl.when(z >= h)
        def _():
            start_all(high)

    relay(p.z)
    by_distance(relay, relay)

    def settle(z):
        low, high = far_arrivals(z)

        @pl.when(z < h)
        def _():
            for block in low:
                await_block(*block)

        @pl.when(z >= h)
        def _():
            for block in high:
                await_block(*block)

    settle(p.z)
    by_distance(settle, settle)
    for keep in keeps:
        keep.wait()

    def finish(z, carry):
        for c in near_copies(z):
            c.wait_send()
        low, high = far_copies(z)

        @pl.when(z < h)
        def _():
            for c in low:
                c.wait_send()

        @pl.when(z >= h)
        def _():
            for c in high:
                c.wait_send()

        @pl.when(jnp.logical_and(z <= p.z, p.z < Z - 1))
        def _():
            along_z(z, True).wait_send()

        @pl.when(jnp.logical_and(z >= p.z, p.z > 0))
        def _():
            along_z(z, False).wait_send()

        for y in range(p.Y):
            for x in range(p.X):
                @pl.when(jnp.logical_not(jnp.logical_and(
                    z == p.z, jnp.logical_and(p.y == y, p.x == x))))
                def _():
                    to_partner(z, y, x).wait_send()
                    theirs = all_ref.at[1 - p.c, z, y, x]
                    copy(theirs, theirs, across.at[z, y, x], partner).wait_recv()

        return carry

    lax.fori_loop(0, Z, finish, 0)


def gather_call(weight_in, weight_out, sizes, collective_id):
    Z, F = sizes
    X, Y = F // 4, 2
    own = weight_in.shape[0]
    vmem = pl.BlockSpec(memory_space=pltpu.VMEM)
    hbm = pl.BlockSpec(memory_space=pl.ANY)
    whole_weights = pl.pallas_call(
        functools.partial(gather_kernel, sizes),
        out_shape=jax.ShapeDtypeStruct((2, Z, Y, X, 2 * own, HALF), BF16),
        in_specs=[vmem, vmem],
        out_specs=hbm,
        scratch_shapes=[
            pltpu.VMEM((2, own, 2 * HALF), F32), pltpu.VMEM((2, 2 * own, HALF), BF16),
            pltpu.SemaphoreType.DMA((4,)), pltpu.SemaphoreType.DMA((2, Z, 2)),
            pltpu.SemaphoreType.DMA((Z, X, 2)), pltpu.SemaphoreType.DMA((Z, X, 2)),
            pltpu.SemaphoreType.DMA((Z, Y, X, 2)),
        ],
        compiler_params=pltpu.CompilerParams(
            collective_id=collective_id, has_side_effects=True, vmem_limit_bytes=40 * 2**20
        ),
        name="weights_gather",
    )(weight_in, weight_out)
    return whole_weights.reshape(2, D, HALF)


def gram_rows(slab, row):
    high, low = split(slab)
    left = above(high, low, high)[:, 128 * row : 128 * row + 128]
    return dot_tn(left, above(high, high, low)[:, 128 * row :])


def pack_gram(targets, slab):
    Z, Y, X, per, _ = targets[0].shape
    rows = above(*[
        beside(gram_rows(slab, i), gram_rows(slab, D // 128 - 1 - i)) for i in range(D // 256)
    ])
    if Z * Y * X * per > rows.shape[0]:
        rows = above(rows, jnp.zeros((Z * Y * X * per - rows.shape[0], rows.shape[1]), F32))
    at = 0
    for target in targets:
        cols = slice(at, at + target.shape[4])
        for i in range(Z * Y * X):
            target[i // (Y * X), i // X % Y, i % X] = rows[per * i : per * i + per, cols]
        at += target.shape[4]


def unpack_gram(gram, packed):
    Z, Y, X, _, _ = packed[0].shape
    rows = beside(*[
        above(*[part[i // (Y * X), i // X % Y, i % X] for i in range(Z * Y * X)])
        for part in packed
    ])
    for i in range(D // 256):
        pair = rows[128 * i : 128 * i + 128]
        wide_part, j = D - 128 * i, D // 128 - 1 - i
        for row, part in ((i, pair[:, :wide_part]), (j, pair[:, wide_part:])):
            gram[128 * row : 128 * row + 128, 128 * row :] = part
            for k in range(row + 1, D // 128):
                at = 128 * (k - row)
                gram[128 * k : 128 * k + 128, 128 * row : 128 * row + 128] = part[
                    :, at : at + 128
                ].T


class AllSum:
    def __init__(self, place, work):
        self.p = place
        self.total, self.acc, self.core, self.core_sems = work[0], work[1], work[7], work[8]
        self.held, self.z_sems, self.back_sems = work[9:12]
        self.plane = Plane(place, *work[1:7])
        self.steps = [
            self.pair, self.second, self.cross, self.turn, self.spread, self.spread_on, self.done,
        ]

    def to_core(self):
        p = self.p
        return remote(
            self.total, self.core, self.core_sems.at[0], self.core_sems.at[1], p.at(c=1 - p.c)
        )

    def pair(self):
        p = self.p
        self.to_core().wait()

        def place_of(i):
            return i // (p.Y * p.X), lax.rem(i // p.X, p.Y), lax.rem(i, p.X)

        add_blocks(
            lambda i: self.acc.at[place_of(i)], lambda i: self.core.at[place_of(i)],
            p.Z * p.Y * p.X,
        )
        self.plane.start(0)

    def second(self):
        self.plane.finish(0)
        self.plane.start(1)

    def over(self, s):
        p = self.p
        z = lax.rem(p.z + s, p.Z)
        sem = self.z_sems.at[0, s]
        return remote(
            self.acc.at[z, p.y, p.x], self.held.at[s - 1], sem.at[0], sem.at[1], p.at(z=z)
        )

    def cross(self):
        self.plane.finish(1)
        for s in range(1, self.p.Z):
            self.over(s).start()

    def back(self, s, mine):
        p = self.p
        sem = self.z_sems.at[1, s]
        z = p.z if mine else lax.rem(p.z + p.Z - s, p.Z)
        ref = self.total.at[z, p.y, p.x]
        return remote(ref, ref, sem.at[0], sem.at[1], p.at(z=lax.rem(p.z + s, p.Z)))

    def turn(self):
        p = self.p
        for s in range(1, p.Z):
            self.over(s).wait()
        result = self.acc[p.z, p.y, p.x]
        for s in range(1, p.Z):
            result = result + self.held[s - 1]
        self.total[p.z, p.y, p.x] = result
        for s in range(1, p.Z):
            self.back(s, True).start()

    def planes(self, stage, mine):
        p, total, h = self.p, self.total, self.p.Z // 2
        low, high = pl.ds(0, h), pl.ds(h, p.Z - h)
        found = []
        for s in range(1, p.X):
            sem = self.back_sems.at[stage * p.X + s]
            x = p.x if mine else lax.rem(p.x + p.X - s, p.X)
            ref = total.at[high, p.y, x] if stage == 0 else total.at[low, :, x]
            found.append(remote(ref, ref, sem.at[0], sem.at[1], p.at(x=p.other_x(s))))
        sem = self.back_sems.at[stage * p.X]
        y = p.y if mine else 1 - p.y
        ref = total.at[low, y, p.x] if stage == 0 else total.at[high, y]
        found.append(remote(ref, ref, sem.at[0], sem.at[1], p.at(y=1 - p.y)))
        return found

    def arrive(self, copies):
        for mine, theirs in copies:
            mine.wait_send()
            theirs.wait_recv()

    def spread(self):
        self.arrive([(self.back(s, True), self.back(s, False)) for s in range(1, self.p.Z)])
        for copy in self.planes(0, True):
            copy.start()

    def spread_on(self):
        self.arrive(zip(self.planes(0, True), self.planes(0, False)))
        for copy in self.planes(1, True):
            copy.start()

    def done(self):
        self.arrive(zip(self.planes(1, True), self.planes(1, False)))


def all_sum_scratch(sizes, block):
    Z, X, Y = sizes[0], sizes[1] // 4, 2
    dma = pltpu.SemaphoreType.DMA
    return [pltpu.VMEM((Z, Y, X) + block, F32)] + plane_scratch(sizes, block) + [
        pltpu.VMEM((Z, Y, X) + block, F32), dma((2,)), pltpu.VMEM((Z - 1,) + block, F32),
        dma((2, Z, 2)), dma((2 * X, 2)),
    ]


def put_left(left, value, rows):
    high, low = split(value)
    left[rows] = beside(high, low, high)


def put_right(right, value, row):
    high, low = split(value)
    size = value.shape[0]
    right[row : row + size] = high
    right[D + row : D + row + size] = high
    right[2 * D + row : 2 * D + row + size] = low


TILE = 256


def symmetric_product(target, left, right):
    for i in range(D // TILE):
        rows = slice(TILE * i, TILE * i + TILE)
        part = dot(left[rows], right[:, TILE * i :])
        target[rows, TILE * i :] = part
        for j in range(i + 1, D // TILE):
            at = TILE * (j - i)
            target[TILE * j : TILE * j + TILE, rows] = part[:, at : at + TILE].T


def iterate(gram, square, factor, left, right, slab, slab_left):
    tiles = [slice(TILE * i, TILE * i + TILE) for i in range(D // TILE)]
    row = lax.broadcasted_iota(jnp.int32, (TILE, D), 0)
    col = lax.broadcasted_iota(jnp.int32, (TILE, D), 1)
    diagonals = [(row + TILE * i == col) for i in range(D // TILE)]
    trace = jnp.zeros((8, D), F32)
    for rows, diagonal in zip(tiles, diagonals):
        trace = trace + fold(jnp.where(diagonal, gram[rows], 0.0))
    trace = jnp.sum(jnp.sum(trace, axis=0, keepdims=True), axis=1, keepdims=True)
    scale = 1.0 / (jnp.sqrt(trace) + 1e-07)
    for rows in tiles:
        gram[rows] = gram[rows] * (scale * scale)
    slab[...] = slab[...] * scale

    def step(iteration, carry):
        for i, rows in enumerate(tiles):
            value = gram[rows]
            put_left(left, value, rows)
            put_right(right, value, TILE * i)
        symmetric_product(square, left, right)
        for i, rows in enumerate(tiles):
            value = COEF_B * gram[rows] + COEF_C * square[rows]
            put_right(right, value + jnp.where(diagonals[i], COEF_A, 0.0), TILE * i)
        put_left(slab_left, slab[...], slice(None))
        slab[...] = dot(slab_left[...], right[...])
        symmetric_product(factor, left, right)
        for rows in tiles:
            put_left(left, factor[rows], rows)
        symmetric_product(gram, left, right)
        return carry

    lax.fori_loop(0, ITERS - 1, step, 0)
    for i, rows in enumerate(tiles):
        put_right(right, gram[rows], TILE * i)
    first = slab[...]
    put_left(slab_left, first, slice(None))
    once = dot(slab_left[...], right[...])
    put_left(slab_left, once, slice(None))
    slab[...] = COEF_A * first + COEF_B * once + COEF_C * dot(slab_left[...], right[...])


def update_kernel(
    sizes, gate_ref, conv_ref, out_ref, small_ref, old_ref, moved_ref, smalls_ref, spread_ref,
    give, given, give_sems, messages, smalls, gram, square, factor, left, right, slab, slab_left,
    swap_send, swap_recv, local, *work,
):
    p = Place(sizes)
    count = p.Z * p.F
    own = D // count
    gates, convs = gate_ref.shape[0], conv_ref.shape[0]
    ins = gates + convs
    greet_all(p)
    swaps = [
        Swap(p, src, dst, swap_send.at[k], swap_recv.at[k], local.at[k], same, narrow)
        for k, (src, dst, same, narrow) in enumerate([
            (small_ref, smalls, True, None), (messages.at[0], moved_ref, False, None),
            (messages.at[1], spread_ref, False, -(-2 * gates // 128) * 128),
        ])
    ]
    swaps[0].start()
    old = old_ref[...].T
    new_in = above(gate_ref[...], conv_ref[...])
    new_out = out_ref[...]

    def push(gradient, moment):
        return gradient + MOMENTUM * (MOMENTUM * moment + gradient)

    push_in = push(new_in, old[:ins])
    push_out = above(push(new_out, old[ins : ins + gates]), jnp.zeros((ins - gates, D), F32))
    in_core = p.c == 0
    give[...] = jnp.where(in_core, push_out, push_in)
    slab[:ins] = jnp.where(in_core, push_in, push_out)
    partner = p.at(c=1 - p.c)
    pieces = [AllSum(p, work[:12]), AllSum(p, work[12:])]
    pack_gram([piece.total for piece in pieces], give[...])
    for piece in pieces:
        piece.to_core().start()
    exchange = remote(give, given, give_sems.at[0], give_sems.at[1], partner)
    exchange.start()
    pack_gram([piece.acc for piece in pieces], slab[:ins])

    def store_messages(k, turned):
        turned = beside(turned, jnp.zeros((D, 256 - turned.shape[1]), F32)) if (
            turned.shape[1] < 256) else turned
        for d in range(count):
            messages[k, d] = turned[own * d : own * d + own]

    for k in range(len(pieces[0].steps)):
        for piece in pieces:
            piece.steps[k]()
        if k == 0:
            store_messages(0, above(new_in, new_out).T)
    exchange.wait()
    swaps[0].wait()
    swaps[1].start()
    smalls_ref[...] = smalls[...]
    rows = smalls[...].reshape(-1, 128)
    new_step = beside(*[rows[HEADS * j : HEADS * j + HEADS] for j in range(D // 128)])
    push_step = push(new_step, old_ref[...].T[ins + gates : ins + gates + HEADS])
    push_step = jnp.where(in_core, push_step, 0.0)
    mine, theirs = slab[:ins], given[...]
    slab_in = above(mine, theirs, push_step)
    slab_out = above(theirs[:gates], mine[:gates], jnp.zeros((2 * convs + HEADS, D), F32))
    slab[: 2 * ins + HEADS] = jnp.where(in_core, slab_in, slab_out)
    slab[2 * ins + HEADS :] = jnp.zeros((slab.shape[0] - 2 * ins - HEADS, D), F32)
    unpack_gram(gram, [piece.total for piece in pieces])
    step_high, step_low = split(push_step)
    step_left = above(step_high, step_low, step_high)
    gram[...] = gram[...] + dot_tn(step_left, above(step_high, step_high, step_low))
    iterate(gram, square, factor, left, right, slab, slab_left)
    store_messages(1, slab[...].T)
    swaps[2].start()
    swaps[1].wait()
    swaps[2].wait()


def update_call(parts, small, old, sizes, collective_id):
    count = sizes[0] * sizes[1]
    own = D // count
    chips = count // 2
    gate, conv, out = parts
    ins = gate.shape[0] + conv.shape[0]
    per = -(-(D // 2) // (8 * chips)) * 8
    blocks = [(per, 512), (per, D + 128 - 512)]
    vmem = pl.BlockSpec(memory_space=pltpu.VMEM)
    hbm = pl.BlockSpec(memory_space=pl.ANY)
    dma = pltpu.SemaphoreType.DMA
    return pl.pallas_call(
        functools.partial(update_kernel, sizes),
        out_shape=[
            shape(count, own, 256), shape(count, *small.shape), shape(count, own, 256),
        ],
        in_specs=[vmem] * 5,
        out_specs=[hbm, vmem, hbm],
        scratch_shapes=[
            pltpu.VMEM((ins, D), F32), pltpu.VMEM((ins, D), F32), dma((2,)),
            pltpu.VMEM((2, count, own, 256), F32), pltpu.VMEM((count,) + small.shape, F32),
            pltpu.VMEM((D, D), F32), pltpu.VMEM((D, D), F32), pltpu.VMEM((D, D), F32),
            pltpu.VMEM((D, 3 * D), BF16), pltpu.VMEM((3 * D, D), BF16),
            pltpu.VMEM((256, D), F32), pltpu.VMEM((256, 3 * D), BF16),
            dma((3, count)), dma((3, count)), dma((3,)),
        ]
        + all_sum_scratch(sizes, blocks[0])
        + all_sum_scratch(sizes, blocks[1]),
        compiler_params=pltpu.CompilerParams(
            collective_id=collective_id, has_side_effects=True, vmem_limit_bytes=56 * 2**20
        ),
        name="update",
    )(gate, conv, out, small, old)


def spread_columns(rows, count):
    return rows.reshape(rows.shape[0], count, -1).transpose(1, 0, 2)


def gather_columns(blocks):
    return blocks.transpose(1, 0, 2).reshape(blocks.shape[1], -1)


def lanes_256(blocks):
    return jnp.pad(blocks, ((0, 0), (0, 0), (0, 256 - blocks.shape[2])))


def shards(
    inputs, cotangent, weight_in, weight_out, small_params, moment_in, moment_out, moment_small
):
    sizes = (lax.axis_size("dp"), lax.axis_size("fsdp"))
    count = sizes[0] * sizes[1]
    own = weight_in.shape[0]
    gates, convs = INNER // count, CONVCH // count
    ins = gates + convs
    old = jnp.concatenate(
        [
            spread_columns(moment_in[:, :INNER], count),
            spread_columns(moment_in[:, INNER:WIDE], count),
            spread_columns(moment_out, count),
            jnp.broadcast_to(moment_in[:, WIDE:], (count, own, HEADS)),
        ],
        axis=2,
    )
    weights = gather_call(weight_in, weight_out, sizes, 0)
    output, dx, columns, part_conv, part_step, part_small, old = block_and_gradients(
        inputs[0], cotangent[0], weights, small_params, lanes_256(old), sizes, (3, 4)
    )
    outputs, input_grad = output[None], dx[None]

    flat = [
        part_step.reshape(HEADS, D // 128, 128).transpose(1, 0, 2).reshape(-1), part_small,
    ]
    flat = jnp.concatenate(flat)
    lines = -(-flat.shape[0] // (1024 * count)) * 8
    flat = jnp.pad(flat, (0, count * lines * 128 - flat.shape[0])).reshape(count, lines, 128)
    new_out, new_gate, new_conv, new_small = scatter_call(
        list(columns), [part_conv.reshape(count, convs, D), flat], sizes, 1
    )
    moved, smalls, spread = update_call(
        (new_gate, new_conv, new_out), new_small, old.reshape(D, 256), sizes, 2
    )
    smalls = smalls.reshape(-1)
    grad_small = smalls[HEADS * D : HEADS * D + small_params.shape[0]]
    new_step = smalls[: HEADS * D].reshape(D // 128, HEADS, 128).transpose(1, 0, 2)
    new_step = new_step.reshape(HEADS, D)

    def rows_in(gate_blocks, conv_blocks, step_rows):
        return beside(gather_columns(gate_blocks), gather_columns(conv_blocks), step_rows)

    evens, odds = spread[0::2], spread[1::2]
    direction_in = rows_in(
        jnp.concatenate([evens[:, :, :gates], evens[:, :, ins : ins + gates]], axis=2),
        jnp.concatenate([evens[:, :, gates:ins], evens[:, :, ins + gates : 2 * ins]], axis=2),
        evens[0, :, 2 * ins : 2 * ins + HEADS],
    )
    direction_out = gather_columns(odds[:, :, : 2 * gates])
    first_row = (lax.axis_index("dp") * sizes[1] + lax.axis_index("fsdp")) * own
    grad_in = rows_in(
        moved[:, :, :gates],
        moved[:, :, gates:ins],
        lax.dynamic_slice_in_dim(new_step, first_row, own, 1).T,
    )
    grad_out = gather_columns(moved[:, :, ins : ins + gates])
    new_moment_in = MOMENTUM * moment_in + grad_in
    new_moment_out = MOMENTUM * moment_out + grad_out
    decay = 1.0 - MATRIX_RATE * WEIGHT_DECAY
    new_weight_in = weight_in * decay - MATRIX_RATE * 0.2 * math.sqrt(max(D, IN_W)) * direction_in
    new_weight_out = (
        weight_out * decay - MATRIX_RATE * 0.2 * math.sqrt(max(D, INNER)) * direction_out
    )
    new_moment_small = MOMENTUM * moment_small + grad_small
    new_small_params = small_params - SMALL_RATE * new_moment_small
    return (
        outputs,
        input_grad,
        grad_in,
        grad_out,
        grad_small,
        new_moment_in,
        new_moment_out,
        new_moment_small,
        new_weight_in,
        new_weight_out,
        new_small_params,
    )


def solution(mesh):
    return jax.shard_map(
        shards,
        mesh=mesh,
        in_specs=(
            P(("dp", "fsdp"), None, None),
            P(("dp", "fsdp"), None, None),
            P(("dp", "fsdp"), None),
            P(("dp", "fsdp"), None),
            P(),
            P(("dp", "fsdp"), None),
            P(("dp", "fsdp"), None),
            P(),
        ),
        out_specs=(
            P(("dp", "fsdp"), None, None),
            P(("dp", "fsdp"), None, None),
            P(("dp", "fsdp"), None),
            P(("dp", "fsdp"), None),
            P(),
            P(("dp", "fsdp"), None),
            P(("dp", "fsdp"), None),
            P(),
            P(("dp", "fsdp"), None),
            P(("dp", "fsdp"), None),
            P(),
        ),
        check_vma=False,
    )
```

```python
import functools
import math

import jax
import jax.numpy as jnp
from jax import lax
from jax.experimental import pallas as pl
from jax.experimental.pallas import tpu as pltpu
from jax.sharding import PartitionSpec as P

D = 768
HEADS = 24
HEAD_DIM = 64
NSTATE = 128
KCONV = 4
LEN = 1024
ITERS = 5
INNER = 1536
CONVCH = 1792
IN_W = 3352
SMALL = 11336
WIDE = INNER + CONVCH
TAIL_SUMS = 1664 - 2 * HEADS
STEP = 32
CONV_A = 768
HALF = 2560
OUT_AT = WIDE - HALF
STEP_AT = OUT_AT + INNER

MOMENTUM = 0.95
MATRIX_RATE = 0.15
WEIGHT_DECAY = 0.1
SMALL_RATE = 0.01
EPSILON = 1e-05
COEF_A = 3.4445
COEF_B = -4.775
COEF_C = 2.0315

F32 = jnp.float32
BF16 = jnp.bfloat16
CHUNK = 128
STRIP = 256
PER = STRIP // CHUNK
STRIPS = LEN // STRIP
GRAD_TILE = 768
GROUP = 4


def dot(a, b):
    return lax.dot_general(a, b, (((1,), (0,)), ((), ())), preferred_element_type=F32)


def dot_nt(a, b):
    return lax.dot_general(a, b, (((1,), (1,)), ((), ())), preferred_element_type=F32)


def dot_tn(a, b):
    return lax.dot_general(a, b, (((0,), (0,)), ((), ())), preferred_element_type=F32)


def split(v):
    high = v.astype(BF16)
    return high, (v - high.astype(F32)).astype(BF16)


def beside(*parts):
    return jnp.concatenate(parts, axis=1)


def above(*parts):
    return jnp.concatenate(parts, axis=0)


def right_pair(b):
    high, low = split(b)
    return above(beside(high, low), beside(high, jnp.zeros_like(low)))


def three_pass(a, pair):
    high, low = split(a)
    both = dot(beside(high, low), pair)
    half = both.shape[1] // 2
    return both[:, :half] + both[:, half:]


def exact_sum(a, ones):
    high = a.astype(BF16)
    rest = a - high.astype(F32)
    mid = rest.astype(BF16)
    low = (rest - mid.astype(F32)).astype(BF16)
    return dot(beside(high, mid, low), above(ones, ones, ones))


def lane_sums(a):
    high = a.astype(BF16)
    rest = a - high.astype(F32)
    mid = rest.astype(BF16)
    low = (rest - mid.astype(F32)).astype(BF16)
    parts = beside(high, mid, low)
    return dot_nt(jnp.ones((8, parts.shape[1]), BF16), parts)


def stack_left(a):
    high, low = split(a)
    return above(beside(high, high), beside(low, jnp.zeros_like(low)))


def fold(rows):
    total = rows[0:8]
    for i in range(1, rows.shape[0] // 8):
        total = total + rows[8 * i : 8 * i + 8]
    return total


def row_sum(rows):
    return jnp.sum(fold(rows), axis=0, keepdims=True)


def upper():
    row = lax.broadcasted_iota(jnp.int32, (CHUNK, CHUNK), 0)
    col = lax.broadcasted_iota(jnp.int32, (CHUNK, CHUNK), 1)
    return col >= row


def softplus(v):
    return jnp.maximum(v, 0.0) + jnp.log1p(jnp.exp(-jnp.abs(v)))


def rates_of(raw, heads_ref, ones):
    steps = softplus(raw + heads_ref[0])
    logs = exact_sum(steps * heads_ref[1], ones)
    last = jnp.broadcast_to(logs[:, CHUNK - 1 : CHUNK], logs.shape)
    columns = above(logs, jnp.zeros((CHUNK - HEADS, CHUNK), F32)).T
    return steps, logs, columns, jnp.exp(logs), jnp.exp(last - logs), jnp.exp(last)


def silu(v):
    return v * jax.nn.sigmoid(v)


def wide(v):
    return beside(*([v] * PER))


def forward_kernel(
    sizes, x_ref, back_ref, first_ref, second_ref, gain_ref, taps_ref, heads_ref, inner_ref,
    blocks_ref, out_ref, hb_ref, cin_ref, c_ref, raw_ref, s_ref, normed_ref,
    dy_ref, dgate_ref, dlogs_ref, tail_sums_ref, moved_ref,
    act, z, mixed, dnormed, state, tail, turned, dskip, dinner, *work,
):
    p = Place(sizes)
    swap = Swap(p, blocks_ref, moved_ref, *work)

    @pl.when(pl.program_id(0) == 0)
    def _():
        greet_all(p)
        swap.start()
        state[...] = jnp.zeros_like(state)
        tail[...] = jnp.zeros_like(tail)
        dskip[...] = jnp.zeros_like(dskip)
        dinner[...] = jnp.zeros_like(dinner)
        for i in range(HALF // 256):
            part = slice(256 * i, 256 * i + 256)
            turned[0, part] = first_ref[:, part].T
            turned[1, part] = second_ref[:, part].T

    x = x_ref[...].astype(F32)
    scaled = x * lax.rsqrt(jnp.mean(x * x, axis=-1, keepdims=True) + EPSILON) * gain_ref[...]
    hb = scaled.astype(BF16)
    hb_ref[...] = hb
    back = back_ref[...]
    for i in range(INNER // 256):
        part = slice(256 * i, 256 * i + 256)
        z[part] = dot_nt(turned[0, part], hb)
        dnormed[part] = dot_nt(turned[1, OUT_AT + 256 * i : OUT_AT + 256 * i + 256], back)
    for i in range(CONVCH // 256):
        start = INNER + 256 * i
        rows = turned[start // HALF, start % HALF : start % HALF + 256]
        cin_ref[256 * i : 256 * i + 256] = dot_nt(rows, hb)
    raw_ref[...] = dot_nt(turned[1, STEP_AT : STEP_AT + STEP], hb)

    lane = lax.broadcasted_iota(jnp.int32, (64, CHUNK), 1)

    def later(cols, steps, before):
        turned_cols = [before] + [pltpu.roll(col, steps, 1) for col in cols]
        pairs = zip(turned_cols[:-1], turned_cols[1:])
        return [jnp.where(lane < steps, a, b) for a, b in pairs], turned_cols[-1]

    def conv_tile(i, carry):
        rows = pl.ds(pl.multiple_of(i * 64, 64), 64)
        cur = cin_ref[rows, :]
        cols = [cur[:, CHUNK * j : CHUNK * j + CHUNK] for j in range(PER)]
        taps = [taps_ref[k, rows, :] for k in range(KCONV + 1)]
        ones_late, tail[0, rows, :] = later(cols, 1, tail[0, rows, :])
        early = [taps[1] * a + taps[0] * b for a, b in zip(cols, ones_late)]
        twos_late, tail[1, rows, :] = later(early, 2, tail[1, rows, :])
        total = beside(*[
            taps[4] + c + taps[2] * b + taps[3] * a for a, b, c in zip(cols, ones_late, twos_late)
        ])
        c_ref[rows, :] = total
        act[rows, :] = total * jax.nn.sigmoid(total)
        return carry

    lax.fori_loop(0, CONVCH // 64, conv_tile, 0, unroll=4)
    causal = upper()
    ones = causal.astype(F32).astype(BF16)

    def chunk(j, carry):
        cols = pl.ds(pl.multiple_of(j * CHUNK, CHUNK), CHUNK)
        steps, logs, columns, grown, to_end, through = rates_of(
            raw_ref[0:HEADS, cols], heads_ref, ones
        )
        in_map = act[INNER : INNER + NSTATE, cols].T
        in_pair = right_pair(in_map)
        out_pair = right_pair(act[INNER + NSTATE :, cols])
        scores = three_pass(in_map, out_pair)
        for g in range(HEADS // GROUP):
            rows = slice(g * GROUP * HEAD_DIM, (g + 1) * GROUP * HEAD_DIM)
            held = state[rows]
            s_ref[j, rows] = held
            across = three_pass(held, out_pair)
            ending, kept = [], []
            for q in range(GROUP):
                h = g * GROUP + q
                mine = slice(h * HEAD_DIM, (h + 1) * HEAD_DIM)
                values = act[mine, cols]
                fed = values * steps[h : h + 1]
                gaps = logs[h : h + 1] - jnp.broadcast_to(columns[:, h : h + 1], (CHUNK, CHUNK))
                weights = scores * jnp.where(causal, jnp.exp(gaps), 0.0)
                both = dot(stack_left(fed), above(*split(weights)))
                y = both[:HEAD_DIM] + both[HEAD_DIM:]
                y = y + across[q * HEAD_DIM : (q + 1) * HEAD_DIM] * grown[h : h + 1]
                mixed[mine, cols] = y + heads_ref[2][h : h + 1] * values
                ending.append(fed * to_end[h : h + 1])
                kept.append(jnp.broadcast_to(through[h : h + 1], (HEAD_DIM, CHUNK)))
            state[rows] = held * above(*kept) + three_pass(above(*ending), in_pair)
        return carry

    lax.fori_loop(0, PER, chunk, 0)

    def mean_tile(h, totals):
        rows = pl.ds(pl.multiple_of(h * HEAD_DIM, HEAD_DIM), HEAD_DIM)
        gate = z[rows, :]
        opened = mixed[rows, :] * (gate * jax.nn.sigmoid(gate))
        gained = dnormed[rows, :] * wide(inner_ref[rows, :]) * opened
        return totals[0] + fold(opened * opened), totals[1] + fold(gained)

    nothing = jnp.zeros((8, STRIP), F32)
    squares, gains = lax.fori_loop(0, HEADS, mean_tile, (nothing, nothing))
    mean = jnp.sum(squares, axis=0, keepdims=True) * (1.0 / INNER)
    r = lax.rsqrt(mean + EPSILON)
    pulled = jnp.sum(gains, axis=0, keepdims=True) * (1.0 / INNER) * (r * r * r)

    def gate_tile(h, carry):
        rows = pl.ds(pl.multiple_of(h * HEAD_DIM, HEAD_DIM), HEAD_DIM)
        gate = z[rows, :]
        skip = wide(heads_ref[2, pl.ds(h, 1), :])
        mix = mixed[rows, :]
        sig = jax.nn.sigmoid(gate)
        sil = gate * sig
        opened = mix * sil
        normed = opened * r
        inner = wide(inner_ref[rows, :])
        normed_ref[rows, :] = (normed * inner).astype(BF16)
        dn = dnormed[rows, :]
        gained = dn * normed
        dinner[rows, :] += gained[:, :CHUNK] + gained[:, CHUNK:]
        dopened = dn * inner * r - opened * pulled
        dmixed = dopened * sil
        dy_ref[rows, :] = dmixed
        dgate_ref[rows, :] = (dopened * mix * (sig * (1.0 + gate * (1.0 - sig)))).astype(BF16)
        skipped = row_sum(dmixed * act[rows, :])
        dskip[pl.ds(h, 1), :] += skipped[:, :CHUNK] + skipped[:, CHUNK:]
        dlogs_ref[pl.ds(h, 1), :] = row_sum(dmixed * mix) - skip * skipped
        return carry

    lax.fori_loop(0, HEADS, gate_tile, 0)
    for i in range(D // 256):
        part = slice(256 * i, 256 * i + 256)
        branch = dot(second_ref[part, OUT_AT:STEP_AT], normed_ref[...]).T
        out_ref[:, part] = (x_ref[:, part].astype(F32) + branch).astype(BF16)

    @pl.when(pl.program_id(0) == STRIPS - 1)
    def _():
        tail_sums_ref[...] = beside(
            lane_sums(dskip[...]), lane_sums(dinner[...]),
            jnp.zeros((8, tail_sums_ref.shape[1] - HEADS - INNER), F32),
        )
        swap.wait()


def backward_kernel(
    sizes, x_ref, back_ref, w_in_ref, step_in_ref, gain_ref, taps_ref, heads_ref,
    cin_ref, c_ref, raw_ref, s_ref, dy, dgate_ref, dlogs, tail_sums_ref, out_part, gate_part,
    dx_ref, dconv_a_ref, dconv_b_ref, flat_ref, out_column, gate_column,
    dact, dstate, flow, tail, meets, vdu_rows, dstep_ref, dstep_sum, dgain, dtaps_ref, dheads_ref,
    *work,
):
    step_now = pl.program_id(0)
    p = Place(sizes)
    sums = [
        PlaneSum(p, part, work[8 * k : 8 * k + 8]) for k, part in enumerate((out_part, gate_part))
    ]

    @pl.when(step_now == 0)
    def _():
        greet_near(p, False)
        sums[0].begin()

    @pl.when(step_now == 1)
    def _():
        sums[1].pair()

    @pl.when(step_now == 2)
    def _():
        sums[0].plane.finish(0)
        sums[0].plane.start(1)

    @pl.when(step_now == 3)
    def _():
        sums[1].plane.finish(0)
        sums[1].plane.start(1)

    @pl.when(step_now == 0)
    def _():
        dstate[...] = jnp.zeros_like(dstate)
        flow[...] = jnp.zeros_like(flow)
        tail[...] = jnp.zeros_like(tail)
        dgain[...] = jnp.zeros_like(dgain)
        dstep_sum[...] = jnp.zeros_like(dstep_sum)
        dtaps_ref[...] = jnp.zeros_like(dtaps_ref)
        dheads_ref[...] = jnp.zeros_like(dheads_ref)

    back = back_ref[...]

    causal = upper()
    ones = causal.astype(F32).astype(BF16)
    row = lax.broadcasted_iota(jnp.int32, (CHUNK, CHUNK), 0)
    col = lax.broadcasted_iota(jnp.int32, (CHUNK, CHUNK), 1)
    ones_back = (row >= col).astype(F32).astype(BF16)

    def chunk(step, carry):
        j = PER - 1 - step
        cols = pl.ds(pl.multiple_of(j * CHUNK, CHUNK), CHUNK)
        raw = raw_ref[0:HEADS, cols]
        steps, logs, columns, grown, to_end, through = rates_of(raw, heads_ref, ones)
        in_turned = silu(c_ref[INNER : INNER + NSTATE, cols])
        out_turned = silu(c_ref[INNER + NSTATE :, cols])
        in_map = in_turned.T
        out_map = out_turned.T
        scores = three_pass(in_map, right_pair(out_turned))
        in_pair = right_pair(in_turned)
        out_pair = right_pair(out_map)
        dscores = jnp.zeros((CHUNK, CHUNK), F32)
        din = jnp.zeros((NSTATE, CHUNK), F32)
        dout = jnp.zeros((NSTATE, CHUNK), F32)
        for g in range(HEADS // GROUP):
            rows = slice(g * GROUP * HEAD_DIM, (g + 1) * GROUP * HEAD_DIM)
            leaving = dstate[rows]
            entering = s_ref[j, rows]
            from_state = three_pass(leaving, in_pair)
            ending, growing, kept = [], [], []
            for q in range(GROUP):
                h = g * GROUP + q
                mine = slice(h * HEAD_DIM, (h + 1) * HEAD_DIM)
                values = silu(c_ref[mine, cols])
                fed = values * steps[h : h + 1]
                dys = dy[mine, cols]
                gaps = logs[h : h + 1] - jnp.broadcast_to(columns[:, h : h + 1], (CHUNK, CHUNK))
                decay = jnp.where(causal, jnp.exp(gaps), 0.0)
                weights = scores * decay
                both = dot_nt(stack_left(dys), beside(*split(weights)))
                du = both[:HEAD_DIM] + both[HEAD_DIM:]
                du = du + from_state[q * HEAD_DIM : (q + 1) * HEAD_DIM] * to_end[h : h + 1]
                fed_high, fed_low = split(fed)
                dy_high, dy_low = split(dys)
                dweights = dot_tn(
                    above(fed_high, fed_low, fed_high), above(dy_high, dy_high, dy_low)
                )
                dscores = dscores + dweights * decay
                vdu_rows[h : h + 1, :] = row_sum(values * du)
                dact[mine, cols] = du * steps[h : h + 1] + heads_ref[2][h : h + 1] * dys
                ending.append(fed * to_end[h : h + 1])
                growing.append(dys * grown[h : h + 1])
                kept.append(jnp.broadcast_to(through[h : h + 1], (HEAD_DIM, CHUNK)))
            ending = above(*ending)
            growing = above(*growing)
            end_high, end_low = split(ending)
            grow_high, grow_low = split(growing)
            leave_high, leave_low = split(leaving)
            enter_high, enter_low = split(entering)
            din = din + dot_tn(
                above(leave_high, leave_low, leave_high), above(end_high, end_high, end_low)
            )
            dout = dout + dot_tn(
                above(enter_high, enter_low, enter_high), above(grow_high, grow_high, grow_low)
            )
            arrived = leaving * above(*kept) + three_pass(growing, out_pair)
            dstate[rows] = arrived
            meet = arrived * entering
            for q in range(GROUP):
                h = g * GROUP + q
                meets[h : h + 1, :] = row_sum(meet[q * HEAD_DIM : (q + 1) * HEAD_DIM])
        vdu = vdu_rows[...]
        dlog = dlogs[:, cols] - steps * vdu
        drate = exact_sum(dlog, ones_back) + flow[...]
        flow[...] = jnp.broadcast_to(
            jnp.sum(meets[...], axis=1, keepdims=True), (HEADS, CHUNK)
        )
        dsteps = vdu + heads_ref[1] * drate
        draw = dsteps * jax.nn.sigmoid(raw + heads_ref[0])
        dheads_ref[0] += draw
        dheads_ref[1] += drate * steps * heads_ref[1]
        dstep_ref[:, cols] = above(draw, jnp.zeros((STEP - HEADS, CHUNK), F32)).astype(BF16)
        score_high, score_low = split(dscores)
        both = dot_nt(stack_left(out_turned), beside(score_high, score_low))
        dact[INNER : INNER + NSTATE, cols] = din + both[:NSTATE] + both[NSTATE:]
        both = dot(stack_left(in_turned), above(score_high, score_low))
        dact[INNER + NSTATE :, cols] = dout + both[:NSTATE] + both[NSTATE:]
        return carry

    lax.fori_loop(0, PER, chunk, 0)

    @pl.when(step_now == 0)
    def _():
        sums[0].pair()
        sums[0].plane.start(0)
        sums[1].begin()

    @pl.when(step_now == 1)
    def _():
        sums[1].plane.start(0)

    lane = lax.broadcasted_iota(jnp.int32, (64, CHUNK), 1)

    def conv_tile(target, start, i, carry):
        rows = pl.ds(pl.multiple_of(start + i * 64, 64), 64)
        c = c_ref[rows, :]
        sig = jax.nn.sigmoid(c)
        dpre = dact[rows, :] * (sig * (1.0 + c * (1.0 - sig)))
        cin = cin_ref[rows, :]
        cols = [dpre[:, CHUNK * j : CHUNK * j + CHUNK] for j in range(PER)]
        dcin = dpre * wide(taps_ref[KCONV - 1, rows, :])
        grad = cin * dpre
        dtaps_ref[KCONV - 1, rows, :] += grad[:, :CHUNK] + grad[:, CHUNK:]
        dtaps_ref[KCONV, rows, :] += dpre[:, :CHUNK] + dpre[:, CHUNK:]
        for k in range(KCONV - 1):
            ahead = KCONV - 1 - k
            turned = [pltpu.roll(col, CHUNK - ahead, 1) for col in cols] + [tail[k, rows, :]]
            tail[k, rows, :] = turned[0]
            pairs = zip(turned[:-1], turned[1:])
            shifted = beside(*[jnp.where(lane < CHUNK - ahead, a, b) for a, b in pairs])
            dcin = dcin + shifted * wide(taps_ref[k, rows, :])
            grad = cin * shifted
            dtaps_ref[k, rows, :] += grad[:, :CHUNK] + grad[:, CHUNK:]
        target[pl.ds(pl.multiple_of(i * 64, 64), 64), :] = dcin.astype(BF16)
        return carry

    for target, start in ((dconv_a_ref, 0), (dconv_b_ref, CONV_A)):
        lax.fori_loop(
            0, target.shape[0] // 64, functools.partial(conv_tile, target, start), 0, unroll=4
        )
    x = x_ref[...].astype(F32)
    r = lax.rsqrt(jnp.mean(x * x, axis=-1, keepdims=True) + EPSILON)
    parts = []
    for i in range(D // 256):
        part = slice(256 * i, 256 * i + 256)
        total = dot(w_in_ref[part, :INNER], dgate_ref[...])
        total = total + dot(w_in_ref[part, INNER : INNER + CONV_A], dconv_a_ref[...])
        total = total + dot(w_in_ref[part, INNER + CONV_A :], dconv_b_ref[...])
        step = step_in_ref[part, :STEP]
        parts.append((total + dot(step, dstep_ref[...])).T)
    dscaled = beside(*parts)
    plain = x * r
    dgain[...] += fold(dscaled * plain)
    dstep_sum[...] += dot(dstep_ref[...], (plain * gain_ref[...]).astype(BF16))
    gained = dscaled * gain_ref[...]
    inner = jnp.mean(gained * plain, axis=-1, keepdims=True)
    dx_ref[...] = back.astype(F32) + (gained - plain * inner) * r

    @pl.when(step_now == STRIPS - 1)
    def _():
        for part, column in zip(sums, (out_column, gate_column)):
            part.plane.finish(1)
            column[...] = part.column()
        store_flat(flat_ref, dstep_sum, dgain, dtaps_ref, dheads_ref, tail_sums_ref)


def store_flat(flat_ref, dstep_sum, dgain, dtaps, dheads, tail_sums_ref):
    flat_ref[...] = jnp.zeros_like(flat_ref)
    for j in range(D // 128):
        flat_ref[HEADS * j : HEADS * j + HEADS] = dstep_sum[:HEADS, 128 * j : 128 * j + 128]
    last = beside(
        lane_sums(dheads[0])[:1], lane_sums(dheads[1])[:1], tail_sums_ref[:1],
    )
    rows = [jnp.sum(dgain[...], axis=0, keepdims=True)]
    rows += [lane_sums(dtaps[k])[:1] for k in range(KCONV + 1)]
    at = HEADS * (D // 128)
    for row in rows + [last]:
        for j in range(row.shape[1] // 128):
            flat_ref[at + j : at + j + 1] = row[:, 128 * j : 128 * j + 128]
        at += row.shape[1] // 128


def whole(shape):
    return pl.BlockSpec(shape, lambda i: (0,) * len(shape), pipeline_mode=pl.Buffered(1))


def strip_rows(width):
    return pl.BlockSpec((STRIP, width), lambda i: (i, 0))


def strip_cols(height):
    return pl.BlockSpec((height, STRIP), lambda i: (0, i))


def shape(*dims, dtype=F32):
    return jax.ShapeDtypeStruct(dims, dtype)


def columns(width, at):
    return pl.BlockSpec((D, width), lambda i: (0, at), pipeline_mode=pl.Buffered(1))


def forward_call(x, back, weights, gain, taps, heads, inner, blocks, sizes, collective_id):
    count = sizes[0] * sizes[1]
    dma = pltpu.SemaphoreType.DMA
    hbm = pl.BlockSpec(memory_space=pl.ANY)
    return pl.pallas_call(
        functools.partial(forward_kernel, sizes),
        grid=(STRIPS,),
        in_specs=[
            strip_rows(D), strip_rows(D), columns(HALF, 0), columns(HALF, 1), whole((1, D)),
            whole((KCONV + 1, CONVCH, CHUNK)), whole((3, HEADS, CHUNK)), whole((INNER, CHUNK)),
            hbm,
        ],
        out_specs=[
            strip_rows(D), strip_rows(D), strip_cols(CONVCH), strip_cols(CONVCH),
            strip_cols(STEP), pl.BlockSpec((PER, INNER, NSTATE), lambda i: (i, 0, 0)),
            strip_cols(INNER), strip_cols(INNER), strip_cols(INNER), strip_cols(HEADS),
            whole((8, TAIL_SUMS)), hbm,
        ],
        out_shape=[
            shape(LEN, D, dtype=BF16), shape(LEN, D, dtype=BF16), shape(CONVCH, LEN),
            shape(CONVCH, LEN), shape(STEP, LEN), shape(LEN // CHUNK, INNER, NSTATE),
            shape(INNER, LEN, dtype=BF16), shape(INNER, LEN), shape(INNER, LEN, dtype=BF16),
            shape(HEADS, LEN), shape(8, TAIL_SUMS), shape(*blocks.shape),
        ],
        scratch_shapes=[
            pltpu.VMEM((CONVCH, STRIP), F32), pltpu.VMEM((INNER, STRIP), F32),
            pltpu.VMEM((INNER, STRIP), F32), pltpu.VMEM((INNER, STRIP), F32),
            pltpu.VMEM((INNER, NSTATE), F32), pltpu.VMEM((2, CONVCH, CHUNK), F32),
            pltpu.VMEM((2, HALF, D), BF16), pltpu.VMEM((HEADS, CHUNK), F32),
            pltpu.VMEM((INNER, CHUNK), F32), dma((count,)), dma((count,)), dma,
        ],
        compiler_params=pltpu.CompilerParams(
            vmem_limit_bytes=60 * 2**20, collective_id=collective_id, has_side_effects=True
        ),
        name="mixer_forward",
    )(x, back, weights, weights, gain, taps, heads, inner, blocks)


def backward_call(x, back, weights, gain, taps, heads, kept, tail_sums, parts, sizes,
                  collective_id):
    last = STRIPS - 1

    def rows(width):
        return pl.BlockSpec((STRIP, width), lambda i: (last - i, 0))

    def cols(height):
        return pl.BlockSpec((height, STRIP), lambda i: (0, last - i))

    Z = sizes[0]
    lines = flat_lines(sizes[0] * sizes[1])
    size = (parts[0].shape[1], D)
    dma = pltpu.SemaphoreType.DMA
    hbm = pl.BlockSpec(memory_space=pl.ANY)
    return pl.pallas_call(
        functools.partial(backward_kernel, sizes),
        grid=(STRIPS,),
        in_specs=[
            rows(D), rows(D), columns(WIDE, 0),
            columns(256, (HALF + STEP_AT) // 256), whole((1, D)),
            whole((KCONV, CONVCH, CHUNK)), whole((3, HEADS, CHUNK)), cols(CONVCH),
            cols(CONVCH), cols(STEP),
            pl.BlockSpec((PER, INNER, NSTATE), lambda i: (last - i, 0, 0)), cols(INNER),
            cols(INNER), cols(HEADS), whole((8, TAIL_SUMS)), hbm, hbm,
        ],
        out_specs=[
            rows(D), cols(CONV_A), cols(CONVCH - CONV_A), whole((lines, 128)),
            whole((Z,) + size), whole((Z,) + size),
        ],
        out_shape=[
            shape(LEN, D), shape(CONV_A, LEN, dtype=BF16),
            shape(CONVCH - CONV_A, LEN, dtype=BF16), shape(lines, 128),
            shape(Z, *size), shape(Z, *size),
        ],
        scratch_shapes=[
            pltpu.VMEM((CONVCH, STRIP), F32),
            pltpu.VMEM((INNER, NSTATE), F32), pltpu.VMEM((HEADS, CHUNK), F32),
            pltpu.VMEM((KCONV - 1, CONVCH, CHUNK), F32), pltpu.VMEM((HEADS, CHUNK), F32),
            pltpu.VMEM((HEADS, CHUNK), F32), pltpu.VMEM((STEP, STRIP), BF16),
            pltpu.VMEM((STEP, D), F32), pltpu.VMEM((8, D), F32),
            pltpu.VMEM((KCONV + 1, CONVCH, CHUNK), F32), pltpu.VMEM((2, HEADS, CHUNK), F32),
        ]
        + 2 * sum_scratch(sizes, size),
        compiler_params=pltpu.CompilerParams(
            vmem_limit_bytes=63 * 2**20, collective_id=collective_id, has_side_effects=True
        ),
        name="mixer_backward",
    )(
        x, back, weights, weights, gain, taps, heads, *kept, tail_sums,
        *(by_place(part, sizes) for part in parts),
    )


def grads_kernel(normed_ref, dgate_ref, back_ref, hb_ref, out_ref, gate_ref):
    step = pl.program_id(0)

    @pl.when(step < INNER // GRAD_TILE)
    def _():
        out_ref[...] = dot(normed_ref[...], back_ref[...])

    @pl.when(step >= INNER // GRAD_TILE)
    def _():
        gate_ref[...] = dot(dgate_ref[...], hb_ref[...])


def grads_call(normed, dgate, back, hb):
    tiles = INNER // GRAD_TILE
    first = lambda i: (jnp.minimum(i, tiles - 1), 0)
    second = lambda i: (jnp.maximum(i - tiles, 0), 0)
    return pl.pallas_call(
        grads_kernel,
        grid=(2 * tiles,),
        in_specs=[
            pl.BlockSpec((GRAD_TILE, LEN), first), pl.BlockSpec((GRAD_TILE, LEN), second),
            whole((LEN, D)), whole((LEN, D)),
        ],
        out_specs=[pl.BlockSpec((GRAD_TILE, D), first), pl.BlockSpec((GRAD_TILE, D), second)],
        out_shape=[shape(INNER, D), shape(INNER, D)],
        compiler_params=pltpu.CompilerParams(vmem_limit_bytes=60 * 2**20),
        name="grads",
    )(normed, dgate, back, hb)


def flat_lines(count):
    return -(-(HEADS * D + SMALL) // (1024 * count)) * 8 * count


def block_and_gradients(x, back, weights, vectors, blocks, sizes, collective_ids):
    count = sizes[0] * sizes[1]
    gain, taps, heads, inner = vectors
    out, hb, cin, c, raw, states, normed, dy, dgate, dlogs, tail_sums, moved = forward_call(
        x, back, weights, gain, taps, heads, inner, blocks, sizes, collective_ids[0]
    )
    parts = [part.reshape(count, -1, D) for part in grads_call(normed, dgate, back, hb)]
    dx, dconv_a, dconv_b, flat, out_column, gate_column = backward_call(
        x, back, weights, gain, taps, heads, (cin, c, raw, states, dy, dgate, dlogs), tail_sums,
        parts, sizes, collective_ids[1],
    )
    parts = [dot(part, hb).reshape(count, -1, D) for part in (dconv_a, dconv_b)]
    return out, dx, [out_column, gate_column], parts + [flat.reshape(count, -1, 128)], moved


MESH = pl.DeviceIdType.MESH


class Place:
    def __init__(self, sizes):
        self.Z, self.F = sizes
        self.C, self.Y = 2, 2
        self.X = self.F // 4
        f = lax.axis_index("fsdp")
        self.z = lax.axis_index("dp")
        self.c = lax.rem(f, 2)
        self.x = lax.rem(f // 2, self.X)
        self.y = f // (2 * self.X)
        self.f = f

    def at(self, z=None, y=None, x=None, c=None):
        z = self.z if z is None else z
        y = self.y if y is None else y
        x = self.x if x is None else x
        c = self.c if c is None else c
        return (z, (y * self.X + x) * 2 + c)

    def other_x(self, step):
        return lax.rem(self.x + step, self.X)


def signal(device):
    pl.semaphore_signal(
        pltpu.get_barrier_semaphore(), inc=1, device_id=device, device_id_type=MESH
    )


def greet_all(place):
    count = place.Z * place.F
    me = place.z * place.F + place.f

    def step(i, carry):
        peer = lax.rem(me + i, count)
        signal((peer // place.F, lax.rem(peer, place.F)))
        return carry

    lax.fori_loop(1, count, step, 0)
    pl.semaphore_wait(pltpu.get_barrier_semaphore(), count - 1)


def remote(src, dst, send, recv, device):
    return pltpu.make_async_remote_copy(
        src_ref=src, dst_ref=dst, send_sem=send, recv_sem=recv, device_id=device,
        device_id_type=MESH,
    )


def add_blocks(dst, src, count):
    def step(i, carry):
        target = dst(i)
        target[...] = target[...] + src(i)[...]
        return carry

    lax.fori_loop(0, count, step, 0)


class Swap:
    def __init__(self, place, src, dst, send, recv, local, same=False, narrow=None):
        self.place, self.src, self.dst, self.same, self.narrow = place, src, dst, same, narrow
        self.send, self.recv, self.local = send, recv, local
        self.count = place.Z * place.F
        self.me = place.z * place.F + place.f

    def block(self, peer):
        return self.src if self.same else self.src.at[peer]

    def cut(self, ref, odd):
        return ref.at[:, pl.ds(0, self.narrow)] if odd else ref

    def each(self, sender, act):
        if self.narrow is None:
            act(False)
        else:
            @pl.when(lax.rem(sender, 2) == 0)
            def _():
                act(False)

            @pl.when(lax.rem(sender, 2) == 1)
            def _():
                act(True)

    def to(self, i, odd):
        peer = lax.rem(self.me + i, self.count)
        return remote(
            self.cut(self.block(peer), odd), self.cut(self.dst.at[self.me], odd),
            self.send.at[i], self.recv.at[i],
            (peer // self.place.F, lax.rem(peer, self.place.F)),
        )

    def keep(self):
        return pltpu.make_async_copy(self.block(self.me), self.dst.at[self.me], self.local)

    def start(self):
        self.keep().start()

        def step(i, carry):
            self.each(self.me, lambda odd: self.to(i, odd).start())
            return carry

        lax.fori_loop(1, self.count, step, 0)

    def wait(self):
        self.keep().wait()

        def step(i, carry):
            sender = lax.rem(self.me + self.count - i, self.count)
            self.each(self.me, lambda odd: self.to(i, odd).wait_send())
            self.each(sender, lambda odd: remote(
                self.cut(self.block(sender), odd), self.cut(self.dst.at[sender], odd),
                self.send.at[i], self.recv.at[i],
                (sender // self.place.F, lax.rem(sender, self.place.F)),
            ).wait_recv())
            return carry

        lax.fori_loop(1, self.count, step, 0)


def greet_near(place, along_z):
    signal(place.at(c=1 - place.c))
    signal(place.at(y=1 - place.y))
    for s in range(1, place.X):
        signal(place.at(x=place.other_x(s)))
    if along_z:
        for s in range(1, place.Z):
            signal(place.at(z=lax.rem(place.z + s, place.Z)))
    pl.semaphore_wait(
        pltpu.get_barrier_semaphore(), place.X + 1 + (place.Z - 1 if along_z else 0)
    )


class Plane:
    def __init__(self, place, acc, x1, y1, x2, y2, sems):
        self.p, self.acc = place, acc
        self.x1, self.y1, self.x2, self.y2, self.sems = x1, y1, x2, y2, sems
        self.h = place.Z // 2

    def copies(self, stage):
        p, acc, h = self.p, self.acc, self.h
        low, high = pl.ds(0, h), pl.ds(h, p.Z - h)
        out = []
        base = stage * p.X
        for s in range(1, p.X):
            x = p.other_x(s)
            if stage == 0:
                src, dst = acc.at[low, :, x], self.x1.at[s - 1]
            else:
                src, dst = acc.at[high, p.y, x], self.x2.at[s - 1]
            sem = self.sems.at[base + s]
            out.append(remote(src, dst, sem.at[0], sem.at[1], p.at(x=x)))
        if stage == 0:
            src, dst = acc.at[high, 1 - p.y], self.y1
        else:
            src, dst = acc.at[low, 1 - p.y, p.x], self.y2
        sem = self.sems.at[base]
        out.append(remote(src, dst, sem.at[0], sem.at[1], p.at(y=1 - p.y)))
        return out

    def start(self, stage):
        for copy in self.copies(stage):
            copy.start()

    def finish(self, stage):
        p, acc, h = self.p, self.acc, self.h
        for copy in self.copies(stage):
            copy.wait()
        for s in range(p.X - 1):
            if stage == 0:
                add_blocks(
                    lambda i: acc.at[i // p.Y, lax.rem(i, p.Y), p.x],
                    lambda i: self.x1.at[s, i // p.Y, lax.rem(i, p.Y)],
                    h * p.Y,
                )
            else:
                add_blocks(
                    lambda i: acc.at[h + i, p.y, p.x], lambda i: self.x2.at[s, i], p.Z - h
                )
        if stage == 0:
            add_blocks(
                lambda i: acc.at[h + i // p.X, p.y, lax.rem(i, p.X)],
                lambda i: self.y1.at[i // p.X, lax.rem(i, p.X)],
                (p.Z - h) * p.X,
            )
        else:
            add_blocks(lambda i: acc.at[i, p.y, p.x], lambda i: self.y2.at[i], h)


def plane_scratch(sizes, block):
    Z, X, Y = sizes[0], sizes[1] // 4, 2
    h = Z // 2
    return [
        pltpu.VMEM((Z, Y, X) + block, F32), pltpu.VMEM((X - 1, h, Y) + block, F32),
        pltpu.VMEM((Z - h, X) + block, F32), pltpu.VMEM((X - 1, Z - h) + block, F32),
        pltpu.VMEM((h,) + block, F32), pltpu.SemaphoreType.DMA((2 * X, 2)),
    ]


def sum_scratch(sizes, block):
    Z, X, Y = sizes[0], sizes[1] // 4, 2
    return plane_scratch(sizes, block) + [
        pltpu.VMEM((Z, Y, X) + block, F32), pltpu.SemaphoreType.DMA((3,)),
    ]


def by_place(blocks, sizes):
    return blocks.reshape((sizes[0], 2, sizes[1] // 4, 2) + blocks.shape[1:])


class PlaneSum:
    def __init__(self, place, part, work):
        self.p, self.part = place, part
        self.acc, self.core, self.sems = work[0], work[6], work[7]
        self.plane = Plane(place, *work[:6])

    def copies(self):
        p = self.p
        return (
            remote(
                self.part.at[:, :, :, 1 - p.c], self.core, self.sems.at[0], self.sems.at[1],
                p.at(c=1 - p.c),
            ),
            pltpu.make_async_copy(self.part.at[:, :, :, p.c], self.acc, self.sems.at[2]),
        )

    def begin(self):
        for copy in self.copies():
            copy.start()

    def pair(self):
        p = self.p
        for copy in self.copies():
            copy.wait()

        def place_of(i):
            return i // (p.Y * p.X), lax.rem(i // p.X, p.Y), lax.rem(i, p.X)

        add_blocks(
            lambda i: self.acc.at[place_of(i)], lambda i: self.core.at[place_of(i)],
            p.Z * p.Y * p.X,
        )

    def block(self, z):
        return self.acc.at[z, self.p.y, self.p.x]

    def column(self):
        return self.acc[:, self.p.y, self.p.x]


class Column:
    def __init__(self, part, acc, sem):
        self.copy = pltpu.make_async_copy(part, acc, sem)
        self.acc = acc

    def block(self, z):
        return self.acc.at[z]


class Chain:
    def __init__(self, place, part, held, sems):
        self.p, self.part, self.held, self.sems = place, part, held, sems

    def flow(self, t, right):
        p, side = self.p, 0 if right else 1
        sem = self.sems.at[side, t]
        target = p.at(z=p.z + 1 if right else p.z - 1)
        return remote(self.part.block(t), self.held.at[side, t], sem.at[0], sem.at[1], target)

    def send(self, t, right):
        @pl.when(self.p.z < t if right else self.p.z > t)
        def _():
            self.flow(t, right).start()

    def first(self):
        p = self.p
        for j in range(p.Z - 1):
            @pl.when(p.z == 0)
            def _():
                self.send(p.Z - 1 - j, True)

            @pl.when(p.z == p.Z - 1)
            def _():
                self.send(j, False)

    def receive(self, t, right):
        self.flow(t, right).wait_recv()
        mine = self.part.block(t)
        mine[...] = mine[...] + self.held[0 if right else 1, t]

    def forward(self, j):
        p = self.p
        for right in (True, False):
            t = p.Z - 1 - j if right else j

            @pl.when(jnp.logical_and(p.z > 0, p.z < t) if right else
                     jnp.logical_and(p.z < p.Z - 1, p.z > t))
            def _():
                self.receive(t, right)
                self.flow(t, right).start()

    def last(self):
        p = self.p

        @pl.when(p.z > 0)
        def _():
            self.receive(p.z, True)

        @pl.when(p.z < p.Z - 1)
        def _():
            self.receive(p.z, False)

    def finish(self):
        p = self.p
        for t in range(p.Z):
            for right in (True, False):
                @pl.when(p.z < t if right else p.z > t)
                def _():
                    self.flow(t, right).wait_send()


class Direct:
    def __init__(self, place, part, held, sems):
        self.p, self.part, self.held, self.sems = place, part, held, sems

    def over(self, s):
        p = self.p
        z = lax.rem(p.z + s, p.Z)
        sem = self.sems.at[s]
        return remote(self.part.block(z), self.held.at[s - 1], sem.at[0], sem.at[1], p.at(z=z))

    def start(self):
        for s in range(1, self.p.Z):
            self.over(s).start()

    def last(self):
        mine = self.part.block(self.p.z)
        total = mine[...]
        for s in range(1, self.p.Z):
            self.over(s).wait()
            total = total + self.held[s - 1]
        mine[...] = total


def scatter_kernel(sizes, columns, parts, *refs):
    total = columns + parts
    ins, outs, rest = refs[:total], refs[total : 2 * total], list(refs[2 * total :])
    p = Place(sizes)
    found, chains = [], []
    for k in range(total):
        if k < columns:
            found.append(Column(ins[k], *rest[:2]))
            rest = rest[2:]
        else:
            found.append(PlaneSum(p, ins[k], rest[:8]))
            rest = rest[8:]
        chains.append((Chain if k < columns else Direct)(p, found[k], *rest[:2]))
        rest = rest[2:]
    greet_near(p, True)
    for column in found[:columns]:
        column.copy.start()
    for part in found[columns:]:
        part.begin()
    for k in range(columns):
        found[k].copy.wait()
        chains[k].first()
    hops = p.Z - 2

    def forward(j):
        if j < hops:
            for chain in chains[:columns]:
                chain.forward(j)

    queue = list(zip(found[columns:], chains[columns:]))
    stages = [
        lambda part, chain: (part.pair(), part.plane.start(0)),
        lambda part, chain: (part.plane.finish(0), part.plane.start(1)),
        lambda part, chain: (part.plane.finish(1), chain.start()),
    ]
    for k in range(len(queue) + len(stages) - 1):
        for j in range(len(stages)):
            if 0 <= k - j < len(queue):
                stages[j](*queue[k - j])
        forward(k)
    for k in range(len(queue) + len(stages) - 1, hops):
        forward(k)
    for k in range(columns):
        chains[k].last()
        chains[k].finish()
    for _, chain in queue:
        chain.last()
    for k in range(total):
        outs[k][...] = found[k].block(p.z)[...]


def scatter_call(columns, parts, sizes, collective_id):
    Z = sizes[0]
    scratch = []
    for k, b in enumerate(columns + parts):
        block = b.shape[1:]
        if k < len(columns):
            scratch += [pltpu.VMEM(b.shape, F32), pltpu.SemaphoreType.DMA]
        else:
            scratch += sum_scratch(sizes, block)
        if k < len(columns):
            scratch += [pltpu.VMEM((2, Z) + block, F32), pltpu.SemaphoreType.DMA((2, Z, 2))]
        else:
            scratch += [pltpu.VMEM((Z - 1,) + block, F32), pltpu.SemaphoreType.DMA((Z, 2))]
    total = len(columns) + len(parts)
    return pl.pallas_call(
        functools.partial(scatter_kernel, sizes, len(columns), len(parts)),
        out_shape=[jax.ShapeDtypeStruct(b.shape[1:], F32) for b in columns + parts],
        in_specs=[pl.BlockSpec(memory_space=pl.ANY)] * total,
        out_specs=[pl.BlockSpec(memory_space=pltpu.VMEM)] * total,
        scratch_shapes=scratch,
        compiler_params=pltpu.CompilerParams(
            collective_id=collective_id, has_side_effects=True, vmem_limit_bytes=56 * 2**20
        ),
        name="scatter",
    )(*columns, *(by_place(b, sizes) for b in parts))


def gather_kernel(
    sizes, w_in_ref, w_out_ref, m_in_ref, m_out_ref, params_ref, inner_rows_ref,
    all_ref, blocks_ref, gain_ref, taps_ref, heads_ref, inner_ref,
    mine, keep_sem, z_sems, near, far, across,
):
    p = Place(sizes)
    Z, h = p.Z, p.Z // 2
    greet_near(p, True)
    own = mine.shape[0]
    partner = p.at(c=1 - p.c)
    mine[:, :WIDE] = w_in_ref[:, :WIDE].astype(BF16)
    mine[:, WIDE : WIDE + INNER] = w_out_ref[...].astype(BF16)
    mine[:, WIDE + INNER :] = jnp.concatenate(
        [w_in_ref[:, WIDE:], jnp.zeros((own, 2 * HALF - IN_W - INNER), F32)], axis=1
    ).astype(BF16)
    keep = pltpu.make_async_copy(mine, all_ref.at[p.z, p.y, p.x, p.c], keep_sem)
    keep.start()

    def spot(z, y, x):
        return all_ref.at[z, y, x, p.c]

    def copy(src, dst, sem, device):
        return remote(src, dst, sem.at[0], sem.at[1], device)

    def along_z(z, right, src=None):
        here = spot(z, p.y, p.x)
        target = p.at(z=p.z + 1 if right else p.z - 1)
        return copy(here if src is None else src, here, z_sems.at[0 if right else 1, z], target)

    def near_copies(z, src=None):
        here = spot(z, p.y, p.x)
        src = here if src is None else src
        found = [copy(src, here, near.at[z, 0], p.at(y=1 - p.y))]
        for s in range(1, p.X):
            found.append(copy(src, here, near.at[z, s], p.at(x=p.other_x(s))))
        return found

    def near_arrivals(z):
        found = [(z, 1 - p.y, p.x, near.at[z, 0])]
        for s in range(1, p.X):
            found.append((z, p.y, lax.rem(p.x + p.X - s, p.X), near.at[z, s]))
        return found

    def far_copies(z):
        low, high = [], []
        for s in range(1, p.X):
            x = p.other_x(s)
            there = spot(z, p.y, x)
            low.append(copy(there, there, far.at[z, s], p.at(y=1 - p.y)))
            there = spot(z, 1 - p.y, p.x)
            high.append(copy(there, there, far.at[z, s], p.at(x=x)))
        return low, high

    def far_arrivals(z):
        low = [(z, 1 - p.y, p.other_x(s), far.at[z, s]) for s in range(1, p.X)]
        high = [
            (z, 1 - p.y, lax.rem(p.x + p.X - s, p.X), far.at[z, s]) for s in range(1, p.X)
        ]
        return low, high

    def to_partner(z, y, x, src=None):
        here = spot(z, y, x)
        return copy(here if src is None else src, here, across.at[z, y, x], partner)

    def await_block(z, y, x, sem):
        here = spot(z, y, x)
        copy(here, here, sem, partner).wait_recv()
        to_partner(z, y, x).start()

    def start_all(copies):
        for c in copies:
            c.start()

    @pl.when(p.z < Z - 1)
    def _():
        along_z(p.z, True, mine).start()

    @pl.when(p.z > 0)
    def _():
        along_z(p.z, False, mine).start()

    start_all(near_copies(p.z, mine))
    to_partner(p.z, p.y, p.x, mine).start()
    spread_vectors(params_ref, inner_rows_ref, gain_ref, taps_ref, heads_ref, inner_ref)
    spread_moments(m_in_ref, m_out_ref, blocks_ref)

    def visit(right, z):
        await_block(z, p.y, p.x, z_sems.at[0 if right else 1, z])

        @pl.when(p.z < Z - 1 if right else p.z > 0)
        def _():
            along_z(z, right).start()

        start_all(near_copies(z))

    def by_distance(low, high):
        for j in range(1, Z):
            @pl.when(p.z - j >= 0)
            def _():
                low(p.z - j)

            @pl.when(p.z + j < Z)
            def _():
                high(p.z + j)

    by_distance(lambda z: visit(True, z), lambda z: visit(False, z))

    def relay(z):
        for block in near_arrivals(z):
            await_block(*block)
        low, high = far_copies(z)

        @pl.when(z < h)
        def _():
            start_all(low)

        @pl.when(z >= h)
        def _():
            start_all(high)

    relay(p.z)
    by_distance(relay, relay)

    def settle(z):
        low, high = far_arrivals(z)

        @pl.when(z < h)
        def _():
            for block in low:
                await_block(*block)

        @pl.when(z >= h)
        def _():
            for block in high:
                await_block(*block)

    settle(p.z)
    by_distance(settle, settle)
    keep.wait()

    def finish(z, carry):
        for c in near_copies(z):
            c.wait_send()
        low, high = far_copies(z)

        @pl.when(z < h)
        def _():
            for c in low:
                c.wait_send()

        @pl.when(z >= h)
        def _():
            for c in high:
                c.wait_send()

        @pl.when(jnp.logical_and(z <= p.z, p.z < Z - 1))
        def _():
            along_z(z, True).wait_send()

        @pl.when(jnp.logical_and(z >= p.z, p.z > 0))
        def _():
            along_z(z, False).wait_send()

        for y in range(p.Y):
            for x in range(p.X):
                to_partner(z, y, x).wait_send()
                theirs = all_ref.at[z, y, x, 1 - p.c]
                copy(theirs, theirs, across.at[z, y, x], partner).wait_recv()

        return carry

    lax.fori_loop(0, Z, finish, 0)


def column_of(row):
    return jnp.broadcast_to(row, (128, 128)).T


def spread_vectors(params_ref, inner_rows_ref, gain_ref, taps_ref, heads_ref, inner_ref):
    row = D // 128
    gain_ref[...] = beside(*[params_ref[j : j + 1] for j in range(row)])
    for k in range(KCONV + 1):
        for j in range(CONVCH // 128):
            taps_ref[k, 128 * j : 128 * j + 128] = column_of(params_ref[row : row + 1])
            row += 1
    heads = column_of(params_ref[row : row + 1])
    heads_ref[0] = heads[:HEADS]
    heads_ref[1] = -jnp.exp(heads[HEADS : 2 * HEADS])
    heads_ref[2] = heads[2 * HEADS : 3 * HEADS]
    for j in range(INNER // 128):
        inner_ref[128 * j : 128 * j + 128] = column_of(inner_rows_ref[j : j + 1])


def cuts_of(count):
    widths = [(0, INNER), (INNER, CONV_A), (INNER + CONV_A, CONVCH - CONV_A)]
    return [(start, width // count) for start, width in widths], INNER // count


def spread_moments(m_in_ref, m_out_ref, blocks_ref):
    count, own, lanes_in_block = blocks_ref.shape
    ins, outs = cuts_of(count)
    step = m_in_ref[:, WIDE:]
    used = sum(width for _, width in ins) + outs + HEADS
    for d in range(count):
        pieces = [m_in_ref[:, start + width * d : start + width * (d + 1)] for start, width in ins]
        pieces += [m_out_ref[:, outs * d : outs * (d + 1)], step]
        blocks_ref[d] = beside(*pieces, jnp.zeros((own, lanes_in_block - used), F32))


def gather_call(weight_in, weight_out, moment_in, moment_out, params, sizes, collective_id):
    Z, F = sizes
    X, Y = F // 4, 2
    own = weight_in.shape[0]
    count = Z * F
    inner_rows = params[-INNER:].reshape(-1, 128)
    params = jnp.pad(params, (0, -params.shape[0] % 128)).reshape(-1, 128)
    vmem = pl.BlockSpec(memory_space=pltpu.VMEM)
    hbm = pl.BlockSpec(memory_space=pl.ANY)
    whole_weights, blocks, *vectors = pl.pallas_call(
        functools.partial(gather_kernel, sizes),
        out_shape=[
            shape(Z, Y, X, 2, own, 2 * HALF, dtype=BF16), shape(count, own, 256), shape(1, D),
            shape(KCONV + 1, CONVCH, CHUNK), shape(3, HEADS, CHUNK), shape(INNER, CHUNK),
        ],
        in_specs=[vmem] * 6,
        out_specs=[hbm] + [vmem] * 5,
        scratch_shapes=[
            pltpu.VMEM((own, 2 * HALF), BF16), pltpu.SemaphoreType.DMA, pltpu.SemaphoreType.DMA((2, Z, 2)),
            pltpu.SemaphoreType.DMA((Z, X, 2)), pltpu.SemaphoreType.DMA((Z, X, 2)),
            pltpu.SemaphoreType.DMA((Z, Y, X, 2)),
        ],
        compiler_params=pltpu.CompilerParams(
            collective_id=collective_id, has_side_effects=True, vmem_limit_bytes=60 * 2**20
        ),
        name="weights_gather",
    )(weight_in, weight_out, moment_in, moment_out, params, inner_rows)
    return whole_weights.reshape(D, 2 * HALF), blocks, vectors


def gram_rows(slab, row):
    high, low = split(slab)
    left = above(high, low, high)[:, 128 * row : 128 * row + 128]
    return dot_tn(left, above(high, high, low)[:, 128 * row :])


def pack_gram(targets, slab):
    Z, Y, X, per, _ = targets[0].shape
    rows = above(*[
        beside(gram_rows(slab, i), gram_rows(slab, D // 128 - 1 - i)) for i in range(D // 256)
    ])
    if Z * Y * X * per > rows.shape[0]:
        rows = above(rows, jnp.zeros((Z * Y * X * per - rows.shape[0], rows.shape[1]), F32))
    at = 0
    for target in targets:
        cols = slice(at, at + target.shape[4])
        for i in range(Z * Y * X):
            target[i // (Y * X), i // X % Y, i % X] = rows[per * i : per * i + per, cols]
        at += target.shape[4]


def unpack_gram(gram, packed):
    Z, Y, X, _, _ = packed[0].shape
    rows = beside(*[
        above(*[part[i // (Y * X), i // X % Y, i % X] for i in range(Z * Y * X)])
        for part in packed
    ])
    for i in range(D // 256):
        pair = rows[128 * i : 128 * i + 128]
        wide_part, j = D - 128 * i, D // 128 - 1 - i
        for row, part in ((i, pair[:, :wide_part]), (j, pair[:, wide_part:])):
            gram[128 * row : 128 * row + 128, 128 * row :] = part
            for k in range(row + 1, D // 128):
                at = 128 * (k - row)
                gram[128 * k : 128 * k + 128, 128 * row : 128 * row + 128] = part[
                    :, at : at + 128
                ].T


BEHIND = 2


class AllSum:
    def __init__(self, place, work):
        self.p = place
        self.total, self.acc, self.core, self.core_sems = work[0], work[1], work[7], work[8]
        self.held, self.z_sems, self.back_sems = work[9:12]
        self.plane = Plane(place, *work[1:7])
        self.steps = [
            self.pair, self.second, self.cross, self.turn, self.spread, self.spread_on, self.done,
        ]

    def to_core(self):
        p = self.p
        return remote(
            self.total, self.core, self.core_sems.at[0], self.core_sems.at[1], p.at(c=1 - p.c)
        )

    def pair(self):
        p = self.p
        self.to_core().wait()

        def place_of(i):
            return i // (p.Y * p.X), lax.rem(i // p.X, p.Y), lax.rem(i, p.X)

        add_blocks(
            lambda i: self.acc.at[place_of(i)], lambda i: self.core.at[place_of(i)],
            p.Z * p.Y * p.X,
        )
        self.plane.start(0)

    def second(self):
        self.plane.finish(0)
        self.plane.start(1)

    def over(self, s):
        p = self.p
        z = lax.rem(p.z + s, p.Z)
        sem = self.z_sems.at[0, s]
        return remote(
            self.acc.at[z, p.y, p.x], self.held.at[s - 1], sem.at[0], sem.at[1], p.at(z=z)
        )

    def cross(self):
        self.plane.finish(1)
        for s in range(1, self.p.Z):
            self.over(s).start()

    def back(self, s, mine):
        p = self.p
        sem = self.z_sems.at[1, s]
        z = p.z if mine else lax.rem(p.z + p.Z - s, p.Z)
        ref = self.total.at[z, p.y, p.x]
        return remote(ref, ref, sem.at[0], sem.at[1], p.at(z=lax.rem(p.z + s, p.Z)))

    def turn(self):
        p = self.p
        for s in range(1, p.Z):
            self.over(s).wait()
        result = self.acc[p.z, p.y, p.x]
        for s in range(1, p.Z):
            result = result + self.held[s - 1]
        self.total[p.z, p.y, p.x] = result
        for s in range(1, p.Z):
            self.back(s, True).start()

    def planes(self, stage, mine):
        p, total, h = self.p, self.total, self.p.Z // 2
        low, high = pl.ds(0, h), pl.ds(h, p.Z - h)
        found = []
        for s in range(1, p.X):
            sem = self.back_sems.at[stage * p.X + s]
            x = p.x if mine else lax.rem(p.x + p.X - s, p.X)
            ref = total.at[high, p.y, x] if stage == 0 else total.at[low, :, x]
            found.append(remote(ref, ref, sem.at[0], sem.at[1], p.at(x=p.other_x(s))))
        sem = self.back_sems.at[stage * p.X]
        y = p.y if mine else 1 - p.y
        ref = total.at[low, y, p.x] if stage == 0 else total.at[high, y]
        found.append(remote(ref, ref, sem.at[0], sem.at[1], p.at(y=1 - p.y)))
        return found

    def arrive(self, copies):
        for mine, theirs in copies:
            mine.wait_send()
            theirs.wait_recv()

    def spread(self):
        self.arrive([(self.back(s, True), self.back(s, False)) for s in range(1, self.p.Z)])
        for copy in self.planes(0, True):
            copy.start()

    def spread_on(self):
        self.arrive(zip(self.planes(0, True), self.planes(0, False)))
        for copy in self.planes(1, True):
            copy.start()

    def done(self):
        self.arrive(zip(self.planes(1, True), self.planes(1, False)))


def all_sum_scratch(sizes, block):
    Z, X, Y = sizes[0], sizes[1] // 4, 2
    dma = pltpu.SemaphoreType.DMA
    return [pltpu.VMEM((Z, Y, X) + block, F32)] + plane_scratch(sizes, block) + [
        pltpu.VMEM((Z, Y, X) + block, F32), dma((2,)), pltpu.VMEM((Z - 1,) + block, F32),
        dma((2, Z, 2)), dma((2 * X, 2)),
    ]


def put_left(left, value, rows):
    high, low = split(value)
    left[rows] = beside(high, low, high)


def put_right(right, value, row):
    high, low = split(value)
    size = value.shape[0]
    right[row : row + size] = high
    right[D + row : D + row + size] = high
    right[2 * D + row : 2 * D + row + size] = low


TILE = 256


def symmetric_product(target, left, right):
    for i in range(D // TILE):
        rows = slice(TILE * i, TILE * i + TILE)
        part = dot(left[rows], right[:, TILE * i :])
        target[rows, TILE * i :] = part
        for j in range(i + 1, D // TILE):
            at = TILE * (j - i)
            target[TILE * j : TILE * j + TILE, rows] = part[:, at : at + TILE].T


def iterate(gram, square, factor, left, right, slab, slab_left):
    tiles = [slice(TILE * i, TILE * i + TILE) for i in range(D // TILE)]
    row = lax.broadcasted_iota(jnp.int32, (TILE, D), 0)
    col = lax.broadcasted_iota(jnp.int32, (TILE, D), 1)
    diagonals = [(row + TILE * i == col) for i in range(D // TILE)]
    trace = jnp.zeros((8, D), F32)
    for rows, diagonal in zip(tiles, diagonals):
        trace = trace + fold(jnp.where(diagonal, gram[rows], 0.0))
    trace = jnp.sum(jnp.sum(trace, axis=0, keepdims=True), axis=1, keepdims=True)
    scale = 1.0 / (jnp.sqrt(trace) + 1e-07)
    for rows in tiles:
        gram[rows] = gram[rows] * (scale * scale)
    slab[...] = slab[...] * scale

    def step(iteration, carry):
        for i, rows in enumerate(tiles):
            value = gram[rows]
            put_left(left, value, rows)
            put_right(right, value, TILE * i)
        symmetric_product(square, left, right)
        for i, rows in enumerate(tiles):
            value = COEF_B * gram[rows] + COEF_C * square[rows]
            put_right(right, value + jnp.where(diagonals[i], COEF_A, 0.0), TILE * i)
        put_left(slab_left, slab[...], slice(None))
        slab[...] = dot(slab_left[...], right[...])
        symmetric_product(factor, left, right)
        for rows in tiles:
            put_left(left, factor[rows], rows)
        symmetric_product(gram, left, right)
        return carry

    lax.fori_loop(0, ITERS - 1, step, 0)
    for i, rows in enumerate(tiles):
        put_right(right, gram[rows], TILE * i)
    first = slab[...]
    put_left(slab_left, first, slice(None))
    once = dot(slab_left[...], right[...])
    put_left(slab_left, once, slice(None))
    slab[...] = COEF_A * first + COEF_B * once + COEF_C * dot(slab_left[...], right[...])


def update_kernel(
    sizes, gate_ref, conv_a_ref, conv_b_ref, out_ref, small_ref, old_ref, moved_ref, smalls_ref, spread_ref,
    give, given, give_sems, messages, smalls, gram, square, factor, left, right, slab, slab_left,
    swap_send, swap_recv, local, *work,
):
    p = Place(sizes)
    count = p.Z * p.F
    own = D // count
    gates = gate_ref.shape[0]
    ins = gates + conv_a_ref.shape[0] + conv_b_ref.shape[0]
    greet_all(p)
    swaps = [
        Swap(p, src, dst, swap_send.at[k], swap_recv.at[k], local.at[k], same, narrow)
        for k, (src, dst, same, narrow) in enumerate([
            (small_ref, smalls, True, None), (messages.at[0], moved_ref, False, None),
            (messages.at[1], spread_ref, False, -(-2 * gates // 128) * 128),
        ])
    ]
    swaps[0].start()
    old = old_ref[...].T
    new_in = above(gate_ref[...], conv_a_ref[...], conv_b_ref[...])
    new_out = out_ref[...]

    def push(gradient, moment):
        return gradient + MOMENTUM * (MOMENTUM * moment + gradient)

    push_in = push(new_in, old[:ins])
    push_out = above(push(new_out, old[ins : ins + gates]), jnp.zeros((ins - gates, D), F32))
    in_core = p.c == 0
    give[...] = jnp.where(in_core, push_out, push_in)
    slab[:ins] = jnp.where(in_core, push_in, push_out)
    partner = p.at(c=1 - p.c)
    pieces = [AllSum(p, work[:12]), AllSum(p, work[12:])]
    pack_gram([piece.total for piece in pieces], give[...])
    for piece in pieces:
        piece.to_core().start()
    exchange = remote(give, given, give_sems.at[0], give_sems.at[1], partner)
    exchange.start()
    pack_gram([piece.acc for piece in pieces], slab[:ins])

    def store_messages(k, turned):
        turned = beside(turned, jnp.zeros((D, 256 - turned.shape[1]), F32)) if (
            turned.shape[1] < 256) else turned
        for d in range(count):
            messages[k, d] = turned[own * d : own * d + own]

    steps = len(pieces[0].steps)
    for k in range(steps + BEHIND):
        for which, piece in enumerate(pieces):
            if 0 <= k - BEHIND * which < steps:
                piece.steps[k - BEHIND * which]()
        if k == 0:
            store_messages(0, above(new_in, new_out).T)
    exchange.wait()
    swaps[0].wait()
    swaps[1].start()
    smalls_ref[...] = smalls[...]
    rows = smalls[...].reshape(-1, 128)
    new_step = beside(*[rows[HEADS * j : HEADS * j + HEADS] for j in range(D // 128)])
    push_step = push(new_step, old_ref[...].T[ins + gates : ins + gates + HEADS])
    push_step = jnp.where(in_core, push_step, 0.0)
    mine, theirs = slab[:ins], given[...]
    slab_in = above(mine, theirs, push_step)
    slab_out = above(theirs[:gates], mine[:gates], jnp.zeros((2 * (ins - gates) + HEADS, D), F32))
    slab[: 2 * ins + HEADS] = jnp.where(in_core, slab_in, slab_out)
    slab[2 * ins + HEADS :] = jnp.zeros((slab.shape[0] - 2 * ins - HEADS, D), F32)
    unpack_gram(gram, [piece.total for piece in pieces])
    step_high, step_low = split(push_step)
    step_left = above(step_high, step_low, step_high)
    gram[...] = gram[...] + dot_tn(step_left, above(step_high, step_high, step_low))
    iterate(gram, square, factor, left, right, slab, slab_left)
    store_messages(1, slab[...].T)
    swaps[2].start()
    swaps[1].wait()
    swaps[2].wait()


def update_call(parts, small, old, sizes, collective_id):
    count = sizes[0] * sizes[1]
    own = D // count
    chips = count // 2
    ins = sum(part.shape[0] for part in parts[:3])
    per = -(-(D // 2) // (8 * chips)) * 8
    blocks = [(per, 512), (per, D + 128 - 512)]
    vmem = pl.BlockSpec(memory_space=pltpu.VMEM)
    hbm = pl.BlockSpec(memory_space=pl.ANY)
    dma = pltpu.SemaphoreType.DMA
    return pl.pallas_call(
        functools.partial(update_kernel, sizes),
        out_shape=[
            shape(count, own, 256), shape(count, *small.shape), shape(count, own, 256),
        ],
        in_specs=[vmem] * 6,
        out_specs=[hbm, vmem, hbm],
        scratch_shapes=[
            pltpu.VMEM((ins, D), F32), pltpu.VMEM((ins, D), F32), dma((2,)),
            pltpu.VMEM((2, count, own, 256), F32), pltpu.VMEM((count,) + small.shape, F32),
            pltpu.VMEM((D, D), F32), pltpu.VMEM((D, D), F32), pltpu.VMEM((D, D), F32),
            pltpu.VMEM((D, 3 * D), BF16), pltpu.VMEM((3 * D, D), BF16),
            pltpu.VMEM((256, D), F32), pltpu.VMEM((256, 3 * D), BF16),
            dma((3, count)), dma((3, count)), dma((3,)),
        ]
        + all_sum_scratch(sizes, blocks[0])
        + all_sum_scratch(sizes, blocks[1]),
        compiler_params=pltpu.CompilerParams(
            collective_id=collective_id, has_side_effects=True, vmem_limit_bytes=56 * 2**20
        ),
        name="update",
    )(*parts, small, old)


def finish_kernel(
    moved_ref, spread_ref, step_ref, w_in_ref, w_out_ref, m_in_ref, m_out_ref,
    g_in_ref, g_out_ref, new_m_in_ref, new_m_out_ref, new_w_in_ref, new_w_out_ref,
):
    count = moved_ref.shape[0]
    cuts, outs = cuts_of(count)
    ins = sum(width for _, width in cuts)
    decay = 1.0 - MATRIX_RATE * WEIGHT_DECAY
    at = 0
    for start, width in cuts:
        cols = slice(start, start + width * count)
        g_in_ref[:, cols] = beside(*[moved_ref[d, :, at : at + width] for d in range(count)])
        new_w_in_ref[:, cols] = beside(*[
            spread_ref[d - d % 2, :, ins * (d % 2) + at : ins * (d % 2) + at + width]
            for d in range(count)
        ])
        at += width
    g_in_ref[:, WIDE:] = step_ref[...]
    new_w_in_ref[:, WIDE:] = spread_ref[0, :, 2 * ins : 2 * ins + HEADS]
    g_out_ref[...] = beside(*[moved_ref[d, :, ins : ins + outs] for d in range(count)])
    new_w_out_ref[...] = beside(*[spread_ref[d, :, : 2 * outs] for d in range(1, count, 2)])
    for wide_side, g_ref, m_ref, w_ref, new_m_ref, new_w_ref in (
        (IN_W, g_in_ref, m_in_ref, w_in_ref, new_m_in_ref, new_w_in_ref),
        (INNER, g_out_ref, m_out_ref, w_out_ref, new_m_out_ref, new_w_out_ref),
    ):
        new_m_ref[...] = MOMENTUM * m_ref[...] + g_ref[...]
        rate = MATRIX_RATE * 0.2 * math.sqrt(max(D, wide_side))
        new_w_ref[...] = w_ref[...] * decay - rate * new_w_ref[...]


def finish_call(moved, spread, step_rows, weight_in, weight_out, moment_in, moment_out):
    vmem = pl.BlockSpec(memory_space=pltpu.VMEM)
    return pl.pallas_call(
        finish_kernel,
        out_shape=[shape(*weight_in.shape), shape(*weight_out.shape)] * 3,
        in_specs=[vmem] * 7,
        out_specs=[vmem] * 6,
        name="finish",
    )(moved, spread, step_rows, weight_in, weight_out, moment_in, moment_out)


def shards(
    inputs, cotangent, weight_in, weight_out, small_params, moment_in, moment_out, moment_small
):
    sizes = (lax.axis_size("dp"), lax.axis_size("fsdp"))
    own = weight_in.shape[0]
    weights, blocks, vectors = gather_call(
        weight_in, weight_out, moment_in, moment_out, small_params, sizes, 0
    )
    output, dx, columns, parts, old = block_and_gradients(
        inputs[0], cotangent[0], weights, vectors, blocks, sizes, (3, 4)
    )
    new_out, new_gate, new_conv_a, new_conv_b, new_small = scatter_call(columns, parts, sizes, 1)
    moved, smalls, spread = update_call(
        (new_gate, new_conv_a, new_conv_b, new_out), new_small, old.reshape(D, 256), sizes, 2
    )
    smalls = smalls.reshape(-1)
    grad_small = smalls[HEADS * D : HEADS * D + SMALL]
    new_step = smalls[: HEADS * D].reshape(D // 128, HEADS, 128).transpose(1, 0, 2)
    first_row = (lax.axis_index("dp") * sizes[1] + lax.axis_index("fsdp")) * own
    step_rows = lax.dynamic_slice_in_dim(new_step.reshape(HEADS, D), first_row, own, 1).T
    grad_in, grad_out, new_moment_in, new_moment_out, new_weight_in, new_weight_out = finish_call(
        moved, spread, step_rows, weight_in, weight_out, moment_in, moment_out
    )
    new_moment_small = MOMENTUM * moment_small + grad_small
    new_small_params = small_params - SMALL_RATE * new_moment_small
    return (
        output[None],
        dx[None],
        grad_in,
        grad_out,
        grad_small,
        new_moment_in,
        new_moment_out,
        new_moment_small,
        new_weight_in,
        new_weight_out,
        new_small_params,
    )


def solution(mesh):
    return jax.shard_map(
        shards,
        mesh=mesh,
        in_specs=(
            P(("dp", "fsdp"), None, None),
            P(("dp", "fsdp"), None, None),
            P(("dp", "fsdp"), None),
            P(("dp", "fsdp"), None),
            P(),
            P(("dp", "fsdp"), None),
            P(("dp", "fsdp"), None),
            P(),
        ),
        out_specs=(
            P(("dp", "fsdp"), None, None),
            P(("dp", "fsdp"), None, None),
            P(("dp", "fsdp"), None),
            P(("dp", "fsdp"), None),
            P(),
            P(("dp", "fsdp"), None),
            P(("dp", "fsdp"), None),
            P(),
            P(("dp", "fsdp"), None),
            P(("dp", "fsdp"), None),
            P(),
        ),
        check_vma=False,
    )
```

```python
import functools
import math

import jax
import jax.numpy as jnp
from jax import lax
from jax.experimental import pallas as pl
from jax.experimental.pallas import tpu as pltpu
from jax.sharding import PartitionSpec as P

D = 768
HEADS = 24
HEAD_DIM = 64
NSTATE = 128
KCONV = 4
LEN = 1024
ITERS = 5
INNER = 1536
CONVCH = 1792
IN_W = 3352
SMALL = 11336
WIDE = INNER + CONVCH
TAIL_SUMS = 1664 - 2 * HEADS
STEP = 32
CONV_A = 768
HALF = 2560
OUT_AT = WIDE - HALF
STEP_AT = OUT_AT + INNER

MOMENTUM = 0.95
MATRIX_RATE = 0.15
WEIGHT_DECAY = 0.1
SMALL_RATE = 0.01
EPSILON = 1e-05
COEF_A = 3.4445
COEF_B = -4.775
COEF_C = 2.0315

F32 = jnp.float32
BF16 = jnp.bfloat16
CHUNK = 128
STRIP = 256
PER = STRIP // CHUNK
STRIPS = LEN // STRIP
GRAD_TILE = 768
GROUP = 4


def dot(a, b):
    return lax.dot_general(a, b, (((1,), (0,)), ((), ())), preferred_element_type=F32)


def dot_nt(a, b):
    return lax.dot_general(a, b, (((1,), (1,)), ((), ())), preferred_element_type=F32)


def dot_tn(a, b):
    return lax.dot_general(a, b, (((0,), (0,)), ((), ())), preferred_element_type=F32)


def split(v):
    high = v.astype(BF16)
    return high, (v - high.astype(F32)).astype(BF16)


def beside(*parts):
    return jnp.concatenate(parts, axis=1)


def above(*parts):
    return jnp.concatenate(parts, axis=0)


def right_pair(b):
    high, low = split(b)
    return above(beside(high, low), beside(high, jnp.zeros_like(low)))


def three_pass(a, pair):
    high, low = split(a)
    both = dot(beside(high, low), pair)
    half = both.shape[1] // 2
    return both[:, :half] + both[:, half:]


def exact_sum(a, ones):
    high = a.astype(BF16)
    rest = a - high.astype(F32)
    mid = rest.astype(BF16)
    low = (rest - mid.astype(F32)).astype(BF16)
    return dot(beside(high, mid, low), above(ones, ones, ones))


def lane_sums(a):
    high = a.astype(BF16)
    rest = a - high.astype(F32)
    mid = rest.astype(BF16)
    low = (rest - mid.astype(F32)).astype(BF16)
    parts = beside(high, mid, low)
    return dot_nt(jnp.ones((8, parts.shape[1]), BF16), parts)


def stack_left(a):
    high, low = split(a)
    return above(beside(high, high), beside(low, jnp.zeros_like(low)))


def fold(rows):
    total = rows[0:8]
    for i in range(1, rows.shape[0] // 8):
        total = total + rows[8 * i : 8 * i + 8]
    return total


def row_sum(rows):
    return jnp.sum(fold(rows), axis=0, keepdims=True)


def upper():
    row = lax.broadcasted_iota(jnp.int32, (CHUNK, CHUNK), 0)
    col = lax.broadcasted_iota(jnp.int32, (CHUNK, CHUNK), 1)
    return col >= row


def softplus(v):
    return jnp.maximum(v, 0.0) + jnp.log1p(jnp.exp(-jnp.abs(v)))


def rates_of(raw, heads_ref, ones):
    steps = softplus(raw + heads_ref[0])
    logs = exact_sum(steps * heads_ref[1], ones)
    last = jnp.broadcast_to(logs[:, CHUNK - 1 : CHUNK], logs.shape)
    columns = above(logs, jnp.zeros((CHUNK - HEADS, CHUNK), F32)).T
    return steps, logs, columns, jnp.exp(logs), jnp.exp(last - logs), jnp.exp(last)


def silu(v):
    return v * jax.nn.sigmoid(v)


def wide(v):
    return beside(*([v] * PER))


def strip_at(s):
    return pl.ds(pl.multiple_of(s * STRIP, STRIP), STRIP)


def half_rows(rows, c):
    return pl.ds(pl.multiple_of(c * (rows // 2), rows // 2), rows // 2)


class Box:
    def __init__(self, box, dst, sems, partner):
        self.box, self.dst, self.sems, self.partner = box, dst, sems, partner

    def copy(self, s):
        sem = self.sems.at[s]
        return remote(self.box, self.dst(s), sem.at[0], sem.at[1], self.partner)

    def fill(self, s, value, before=None):
        @pl.when(pl.program_id(0) > 0)
        def _():
            self.copy(s - 1 if before is None else before).wait_send()

        self.box[...] = value
        self.copy(s).start()

    def finish(self, last=STRIPS - 1):
        self.copy(last).wait_send()
        for s in range(STRIPS):
            self.copy(s).wait_recv()


def forward_kernel(
    sizes, x_ref, back_ref, first_ref, second_ref, gain_ref, taps_ref, heads_ref, inner_ref,
    blocks_ref, whole_back_ref,
    out_ref, hb_ref, cin_ref, c_ref, raw_ref, s_ref, own_normed_ref,
    dy_ref, dgate_ref, own_dgate_ref, dlogs_ref, tail_sums_ref, moved_ref,
    peer_normed_ref, peer_dgate_ref, peer_hb_ref, peer_back_ref,
    act, z, mixed, dnormed, state, tail, turned, dskip, dinner, normed_ref,
    box_normed, box_dgate, box_hb, box_sems, back_sems, *work,
):
    p = Place(sizes)
    swap = Swap(p, blocks_ref, moved_ref, *work)
    partner = p.at(c=1 - p.c)
    strip = pl.program_id(0)
    back_copy = remote(
        whole_back_ref, peer_back_ref, back_sems.at[0], back_sems.at[1], partner
    )
    boxes = [
        Box(box, lambda s, ref=ref: ref.at[:, strip_at(s)], box_sems.at[k], partner)
        for k, (box, ref) in enumerate(
            [(box_normed, peer_normed_ref), (box_dgate, peer_dgate_ref)]
        )
    ]
    boxes.append(Box(box_hb, lambda s: peer_hb_ref.at[strip_at(s)], box_sems.at[2], partner))

    @pl.when(strip == 0)
    def _():
        greet_all(p)
        back_copy.start()
        swap.start()
        state[...] = jnp.zeros_like(state)
        tail[...] = jnp.zeros_like(tail)
        dskip[...] = jnp.zeros_like(dskip)
        dinner[...] = jnp.zeros_like(dinner)
        for i in range(HALF // 256):
            part = slice(256 * i, 256 * i + 256)
            turned[0, part] = first_ref[:, part].T
            turned[1, part] = second_ref[:, part].T

    x = x_ref[...].astype(F32)
    scaled = x * lax.rsqrt(jnp.mean(x * x, axis=-1, keepdims=True) + EPSILON) * gain_ref[...]
    hb = scaled.astype(BF16)
    hb_ref[...] = hb
    boxes[2].fill(strip, hb)
    back = back_ref[...]
    raw_ref[...] = dot_nt(turned[1, STEP_AT : STEP_AT + STEP], hb)

    lane = lax.broadcasted_iota(jnp.int32, (64, CHUNK), 1)

    def later(cols, steps, before):
        turned_cols = [before] + [pltpu.roll(col, steps, 1) for col in cols]
        pairs = zip(turned_cols[:-1], turned_cols[1:])
        return [jnp.where(lane < steps, a, b) for a, b in pairs], turned_cols[-1]

    def conv_tile(i):
        rows = slice(64 * i, 64 * i + 64)
        cur = cin_ref[rows]
        cols = [cur[:, CHUNK * j : CHUNK * j + CHUNK] for j in range(PER)]
        taps = [taps_ref[k, rows] for k in range(KCONV + 1)]
        ones_late, tail[0, rows] = later(cols, 1, tail[0, rows])
        early = [taps[1] * a + taps[0] * b for a, b in zip(cols, ones_late)]
        twos_late, tail[1, rows] = later(early, 2, tail[1, rows])
        total = beside(*[
            taps[4] + c + taps[2] * b + taps[3] * a for a, b, c in zip(cols, ones_late, twos_late)
        ])
        c_ref[rows] = total
        act[rows] = total * jax.nn.sigmoid(total)

    def project(i):
        start = INNER + 256 * i
        rows = turned[start // HALF, start % HALF : start % HALF + 256]
        cin_ref[256 * i : 256 * i + 256] = dot_nt(rows, hb)

    project(0)
    for i in range(CONVCH // 256):
        if i + 1 < CONVCH // 256:
            project(i + 1)
        if i < INNER // 256:
            part = slice(256 * i, 256 * i + 256)
            z[part] = dot_nt(turned[0, part], hb)
            dnormed[part] = dot_nt(turned[1, OUT_AT + 256 * i : OUT_AT + 256 * i + 256], back)
        for q in range(4):
            conv_tile(4 * i + q)
    causal = upper()
    ones = causal.astype(F32).astype(BF16)

    def chunk(j, carry):
        cols = pl.ds(pl.multiple_of(j * CHUNK, CHUNK), CHUNK)
        steps, logs, columns, grown, to_end, through = rates_of(
            raw_ref[0:HEADS, cols], heads_ref, ones
        )
        in_map = act[INNER : INNER + NSTATE, cols].T
        in_pair = right_pair(in_map)
        out_pair = right_pair(act[INNER + NSTATE :, cols])
        scores = three_pass(in_map, out_pair)
        for g in range(HEADS // GROUP):
            rows = slice(g * GROUP * HEAD_DIM, (g + 1) * GROUP * HEAD_DIM)
            held = state[rows]
            s_ref[j, rows] = held
            across = three_pass(held, out_pair)
            ending, kept = [], []
            for q in range(GROUP):
                h = g * GROUP + q
                mine = slice(h * HEAD_DIM, (h + 1) * HEAD_DIM)
                values = act[mine, cols]
                fed = values * steps[h : h + 1]
                gaps = logs[h : h + 1] - jnp.broadcast_to(columns[:, h : h + 1], (CHUNK, CHUNK))
                weights = scores * jnp.where(causal, jnp.exp(gaps), 0.0)
                both = dot(stack_left(fed), above(*split(weights)))
                y = both[:HEAD_DIM] + both[HEAD_DIM:]
                y = y + across[q * HEAD_DIM : (q + 1) * HEAD_DIM] * grown[h : h + 1]
                mixed[mine, cols] = y + heads_ref[2][h : h + 1] * values
                ending.append(fed * to_end[h : h + 1])
                kept.append(jnp.broadcast_to(through[h : h + 1], (HEAD_DIM, CHUNK)))
            state[rows] = held * above(*kept) + three_pass(above(*ending), in_pair)
        return carry

    lax.fori_loop(0, PER, chunk, 0)

    def mean_tile(h, totals):
        rows = pl.ds(pl.multiple_of(h * HEAD_DIM, HEAD_DIM), HEAD_DIM)
        gate = z[rows, :]
        opened = mixed[rows, :] * (gate * jax.nn.sigmoid(gate))
        gained = dnormed[rows, :] * wide(inner_ref[rows, :]) * opened
        return totals[0] + fold(opened * opened), totals[1] + fold(gained)

    nothing = jnp.zeros((8, STRIP), F32)
    squares, gains = lax.fori_loop(0, HEADS, mean_tile, (nothing, nothing))
    mean = jnp.sum(squares, axis=0, keepdims=True) * (1.0 / INNER)
    r = lax.rsqrt(mean + EPSILON)
    pulled = jnp.sum(gains, axis=0, keepdims=True) * (1.0 / INNER) * (r * r * r)

    def gate_tile(h, carry):
        rows = pl.ds(pl.multiple_of(h * HEAD_DIM, HEAD_DIM), HEAD_DIM)
        gate = z[rows, :]
        skip = wide(heads_ref[2, pl.ds(h, 1), :])
        mix = mixed[rows, :]
        sig = jax.nn.sigmoid(gate)
        sil = gate * sig
        opened = mix * sil
        normed = opened * r
        inner = wide(inner_ref[rows, :])
        normed_ref[rows, :] = (normed * inner).astype(BF16)
        dn = dnormed[rows, :]
        gained = dn * normed
        dinner[rows, :] += gained[:, :CHUNK] + gained[:, CHUNK:]
        dopened = dn * inner * r - opened * pulled
        dmixed = dopened * sil
        dy_ref[rows, :] = dmixed
        dgate_ref[rows, :] = (dopened * mix * (sig * (1.0 + gate * (1.0 - sig)))).astype(BF16)
        skipped = row_sum(dmixed * act[rows, :])
        dskip[pl.ds(h, 1), :] += skipped[:, :CHUNK] + skipped[:, CHUNK:]
        dlogs_ref[pl.ds(h, 1), :] = row_sum(dmixed * mix) - skip * skipped
        return carry

    lax.fori_loop(0, HEADS, gate_tile, 0)
    for box, own, ref in (
        (boxes[0], own_normed_ref, normed_ref), (boxes[1], own_dgate_ref, dgate_ref),
    ):
        own[...] = ref[half_rows(INNER, p.c), :]
        box.fill(strip, ref[half_rows(INNER, 1 - p.c), :])
    for i in range(D // 256):
        part = slice(256 * i, 256 * i + 256)
        branch = dot(second_ref[part, OUT_AT:STEP_AT], normed_ref[...]).T
        out_ref[:, part] = (x_ref[:, part].astype(F32) + branch).astype(BF16)

    @pl.when(pl.program_id(0) == STRIPS - 1)
    def _():
        tail_sums_ref[...] = beside(
            lane_sums(dskip[...]), lane_sums(dinner[...]),
            jnp.zeros((8, tail_sums_ref.shape[1] - HEADS - INNER), F32),
        )
        swap.wait()
        back_copy.wait()
        for box in boxes:
            box.finish()


def backward_kernel(
    sizes, x_ref, back_ref, w_in_ref, step_in_ref, gain_ref, taps_ref, heads_ref,
    cin_ref, c_ref, raw_ref, s_ref, dy, dgate_ref, dlogs, tail_sums_ref, out_part, gate_part,
    dx_ref, own_a_ref, own_b_ref, flat_ref, out_column, gate_column, peer_a_ref, peer_b_ref,
    dconv_a_ref, dconv_b_ref, box_a, box_b, box_sems, dact, dstate, flow, tail, meets, vdu_rows, dstep_ref, dstep_sum, dgain, dtaps_ref, dheads_ref,
    dscaled_turned, *work,
):
    step_now = pl.program_id(0)
    p = Place(sizes)
    partner = p.at(c=1 - p.c)
    strip = STRIPS - 1 - step_now
    boxes = [
        Box(box, lambda s, ref=ref: ref.at[:, strip_at(s)], box_sems.at[k], partner)
        for k, (box, ref) in enumerate([(box_a, peer_a_ref), (box_b, peer_b_ref)])
    ]
    sums = [
        PlaneSum(p, part, work[7 * k : 7 * k + 7]) for k, part in enumerate((out_part, gate_part))
    ]

    @pl.when(step_now == 0)
    def _():
        greet_near(p, False)
        for part in sums:
            part.begin()
        sums[0].start()

    @pl.when(step_now == 2)
    def _():
        sums[0].plane.finish(0)
        sums[0].plane.start(1)

    @pl.when(step_now == 0)
    def _():
        dstate[...] = jnp.zeros_like(dstate)
        flow[...] = jnp.zeros_like(flow)
        tail[...] = jnp.zeros_like(tail)
        dgain[...] = jnp.zeros_like(dgain)
        dstep_sum[...] = jnp.zeros_like(dstep_sum)
        dtaps_ref[...] = jnp.zeros_like(dtaps_ref)
        dheads_ref[...] = jnp.zeros_like(dheads_ref)

    back = back_ref[...]

    causal = upper()
    ones = causal.astype(F32).astype(BF16)
    row = lax.broadcasted_iota(jnp.int32, (CHUNK, CHUNK), 0)
    col = lax.broadcasted_iota(jnp.int32, (CHUNK, CHUNK), 1)
    ones_back = (row >= col).astype(F32).astype(BF16)

    def chunk(step, carry):
        j = PER - 1 - step
        cols = pl.ds(pl.multiple_of(j * CHUNK, CHUNK), CHUNK)
        raw = raw_ref[0:HEADS, cols]
        steps, logs, columns, grown, to_end, through = rates_of(raw, heads_ref, ones)
        in_turned = silu(c_ref[INNER : INNER + NSTATE, cols])
        out_turned = silu(c_ref[INNER + NSTATE :, cols])
        in_map = in_turned.T
        out_map = out_turned.T
        scores = three_pass(in_map, right_pair(out_turned))
        in_pair = right_pair(in_turned)
        out_pair = right_pair(out_map)
        dscores = jnp.zeros((CHUNK, CHUNK), F32)
        din = jnp.zeros((NSTATE, CHUNK), F32)
        dout = jnp.zeros((NSTATE, CHUNK), F32)
        for g in range(HEADS // GROUP):
            rows = slice(g * GROUP * HEAD_DIM, (g + 1) * GROUP * HEAD_DIM)
            leaving = dstate[rows]
            entering = s_ref[j, rows]
            from_state = three_pass(leaving, in_pair)
            ending, growing, kept = [], [], []
            for q in range(GROUP):
                h = g * GROUP + q
                mine = slice(h * HEAD_DIM, (h + 1) * HEAD_DIM)
                values = silu(c_ref[mine, cols])
                fed = values * steps[h : h + 1]
                dys = dy[mine, cols]
                gaps = logs[h : h + 1] - jnp.broadcast_to(columns[:, h : h + 1], (CHUNK, CHUNK))
                decay = jnp.where(causal, jnp.exp(gaps), 0.0)
                weights = scores * decay
                both = dot_nt(stack_left(dys), beside(*split(weights)))
                du = both[:HEAD_DIM] + both[HEAD_DIM:]
                du = du + from_state[q * HEAD_DIM : (q + 1) * HEAD_DIM] * to_end[h : h + 1]
                fed_high, fed_low = split(fed)
                dy_high, dy_low = split(dys)
                dweights = dot_tn(
                    above(fed_high, fed_low, fed_high), above(dy_high, dy_high, dy_low)
                )
                dscores = dscores + dweights * decay
                vdu_rows[h : h + 1, :] = row_sum(values * du)
                dact[mine, cols] = du * steps[h : h + 1] + heads_ref[2][h : h + 1] * dys
                ending.append(fed * to_end[h : h + 1])
                growing.append(dys * grown[h : h + 1])
                kept.append(jnp.broadcast_to(through[h : h + 1], (HEAD_DIM, CHUNK)))
            ending = above(*ending)
            growing = above(*growing)
            end_high, end_low = split(ending)
            grow_high, grow_low = split(growing)
            leave_high, leave_low = split(leaving)
            enter_high, enter_low = split(entering)
            din = din + dot_tn(
                above(leave_high, leave_low, leave_high), above(end_high, end_high, end_low)
            )
            dout = dout + dot_tn(
                above(enter_high, enter_low, enter_high), above(grow_high, grow_high, grow_low)
            )
            arrived = leaving * above(*kept) + three_pass(growing, out_pair)
            dstate[rows] = arrived
            meet = arrived * entering
            for q in range(GROUP):
                h = g * GROUP + q
                meets[h : h + 1, :] = row_sum(meet[q * HEAD_DIM : (q + 1) * HEAD_DIM])
        vdu = vdu_rows[...]
        dlog = dlogs[:, cols] - steps * vdu
        drate = exact_sum(dlog, ones_back) + flow[...]
        flow[...] = jnp.broadcast_to(
            jnp.sum(meets[...], axis=1, keepdims=True), (HEADS, CHUNK)
        )
        dsteps = vdu + heads_ref[1] * drate
        draw = dsteps * jax.nn.sigmoid(raw + heads_ref[0])
        dheads_ref[0] += draw
        dheads_ref[1] += drate * steps * heads_ref[1]
        dstep_ref[:, cols] = above(draw, jnp.zeros((STEP - HEADS, CHUNK), F32)).astype(BF16)
        score_high, score_low = split(dscores)
        both = dot_nt(stack_left(out_turned), beside(score_high, score_low))
        dact[INNER : INNER + NSTATE, cols] = din + both[:NSTATE] + both[NSTATE:]
        both = dot(stack_left(in_turned), above(score_high, score_low))
        dact[INNER + NSTATE :, cols] = dout + both[:NSTATE] + both[NSTATE:]
        return carry

    lax.fori_loop(0, PER, chunk, 0)

    @pl.when(step_now == 0)
    def _():
        sums[1].start()

    @pl.when(step_now == 2)
    def _():
        sums[1].plane.finish(0)
        sums[1].plane.start(1)

    lane = lax.broadcasted_iota(jnp.int32, (64, CHUNK), 1)

    def conv_tile(target, start, i):
        rows = slice(start + 64 * i, start + 64 * i + 64)
        c = c_ref[rows]
        sig = jax.nn.sigmoid(c)
        dpre = dact[rows] * (sig * (1.0 + c * (1.0 - sig)))
        cin = cin_ref[rows]
        cols = [dpre[:, CHUNK * j : CHUNK * j + CHUNK] for j in range(PER)]
        dcin = dpre * wide(taps_ref[KCONV - 1, rows])
        grad = cin * dpre
        dtaps_ref[KCONV - 1, rows] += grad[:, :CHUNK] + grad[:, CHUNK:]
        dtaps_ref[KCONV, rows] += dpre[:, :CHUNK] + dpre[:, CHUNK:]
        for k in range(KCONV - 1):
            ahead = KCONV - 1 - k
            turned = [pltpu.roll(col, CHUNK - ahead, 1) for col in cols] + [tail[k, rows]]
            tail[k, rows] = turned[0]
            pairs = zip(turned[:-1], turned[1:])
            shifted = beside(*[jnp.where(lane < CHUNK - ahead, a, b) for a, b in pairs])
            dcin = dcin + shifted * wide(taps_ref[k, rows])
            grad = cin * shifted
            dtaps_ref[k, rows] += grad[:, :CHUNK] + grad[:, CHUNK:]
        target[64 * i : 64 * i + 64] = dcin.astype(BF16)

    thirds = [slice(256 * i, 256 * i + 256) for i in range(D // 256)]
    conv_at = INNER + CONV_A
    tiles = CONV_A // 64
    for i in range(tiles):
        conv_tile(dconv_a_ref, 0, i)
        if i % 4 == 0:
            part = thirds[i // 4]
            dscaled_turned[part] = dot(w_in_ref[part, :INNER], dgate_ref[...])
    for i in range((CONVCH - CONV_A) // 64):
        conv_tile(dconv_b_ref, CONV_A, i)
        if i % 4 == 0 and i // 4 < len(thirds):
            part = thirds[i // 4]
            dscaled_turned[part] += dot(w_in_ref[part, INNER:conv_at], dconv_a_ref[...])
    for box, own, ref in (
        (boxes[0], own_a_ref, dconv_a_ref), (boxes[1], own_b_ref, dconv_b_ref),
    ):
        own[...] = ref[half_rows(ref.shape[0], p.c), :]
        box.fill(strip, ref[half_rows(ref.shape[0], 1 - p.c), :], strip + 1)
    x = x_ref[...].astype(F32)
    r = lax.rsqrt(jnp.mean(x * x, axis=-1, keepdims=True) + EPSILON)
    parts = []
    for part in thirds:
        total = dscaled_turned[part] + dot(w_in_ref[part, conv_at:], dconv_b_ref[...])
        parts.append((total + dot(step_in_ref[part, :STEP], dstep_ref[...])).T)
    dscaled = beside(*parts)
    plain = x * r
    dgain[...] += fold(dscaled * plain)
    dstep_sum[...] += dot(dstep_ref[...], (plain * gain_ref[...]).astype(BF16))
    gained = dscaled * gain_ref[...]
    inner = jnp.mean(gained * plain, axis=-1, keepdims=True)
    dx_ref[...] = back.astype(F32) + (gained - plain * inner) * r

    @pl.when(step_now == STRIPS - 1)
    def _():
        for part, column in zip(sums, (out_column, gate_column)):
            part.plane.finish(1)
            column[...] = part.column()
        for box in boxes:
            box.finish(0)
        store_flat(flat_ref, dstep_sum, dgain, dtaps_ref, dheads_ref, tail_sums_ref)


def store_flat(flat_ref, dstep_sum, dgain, dtaps, dheads, tail_sums_ref):
    flat_ref[...] = jnp.zeros_like(flat_ref)
    for j in range(D // 128):
        flat_ref[HEADS * j : HEADS * j + HEADS] = dstep_sum[:HEADS, 128 * j : 128 * j + 128]
    last = beside(
        lane_sums(dheads[0])[:1], lane_sums(dheads[1])[:1], tail_sums_ref[:1],
    )
    rows = [jnp.sum(dgain[...], axis=0, keepdims=True)]
    rows += [lane_sums(dtaps[k])[:1] for k in range(KCONV + 1)]
    at = HEADS * (D // 128)
    for row in rows + [last]:
        for j in range(row.shape[1] // 128):
            flat_ref[at + j : at + j + 1] = row[:, 128 * j : 128 * j + 128]
        at += row.shape[1] // 128


def whole(shape):
    return pl.BlockSpec(shape, lambda i: (0,) * len(shape), pipeline_mode=pl.Buffered(1))


def strip_rows(width):
    return pl.BlockSpec((STRIP, width), lambda i: (i, 0))


def strip_cols(height):
    return pl.BlockSpec((height, STRIP), lambda i: (0, i))


def shape(*dims, dtype=F32):
    return jax.ShapeDtypeStruct(dims, dtype)


def columns(width, at):
    return pl.BlockSpec((D, width), lambda i: (0, at), pipeline_mode=pl.Buffered(1))


def forward_call(x, back, weights, gain, taps, heads, inner, blocks, sizes, collective_id):
    count = sizes[0] * sizes[1]
    dma = pltpu.SemaphoreType.DMA
    hbm = pl.BlockSpec(memory_space=pl.ANY)
    return pl.pallas_call(
        functools.partial(forward_kernel, sizes),
        grid=(STRIPS,),
        in_specs=[
            strip_rows(D), strip_rows(D), columns(HALF, 0), columns(HALF, 1), whole((1, D)),
            whole((KCONV + 1, CONVCH, CHUNK)), whole((3, HEADS, CHUNK)), whole((INNER, CHUNK)),
            hbm, hbm,
        ],
        out_specs=[
            strip_rows(D), strip_rows(D), strip_cols(CONVCH), strip_cols(CONVCH),
            strip_cols(STEP), pl.BlockSpec((PER, INNER, NSTATE), lambda i: (i, 0, 0)),
            strip_cols(INNER // 2), strip_cols(INNER), strip_cols(INNER), strip_cols(INNER // 2),
            strip_cols(HEADS), whole((8, TAIL_SUMS)), hbm, hbm, hbm, hbm, hbm,
        ],
        out_shape=[
            shape(LEN, D, dtype=BF16), shape(LEN, D, dtype=BF16), shape(CONVCH, LEN),
            shape(CONVCH, LEN), shape(STEP, LEN), shape(LEN // CHUNK, INNER, NSTATE),
            shape(INNER // 2, LEN, dtype=BF16), shape(INNER, LEN), shape(INNER, LEN, dtype=BF16),
            shape(INNER // 2, LEN, dtype=BF16), shape(HEADS, LEN), shape(8, TAIL_SUMS),
            shape(*blocks.shape), shape(INNER // 2, LEN, dtype=BF16),
            shape(INNER // 2, LEN, dtype=BF16), shape(LEN, D, dtype=BF16),
            shape(LEN, D, dtype=BF16),
        ],
        scratch_shapes=[
            pltpu.VMEM((CONVCH, STRIP), F32), pltpu.VMEM((INNER, STRIP), F32),
            pltpu.VMEM((INNER, STRIP), F32), pltpu.VMEM((INNER, STRIP), F32),
            pltpu.VMEM((INNER, NSTATE), F32), pltpu.VMEM((2, CONVCH, CHUNK), F32),
            pltpu.VMEM((2, HALF, D), BF16), pltpu.VMEM((HEADS, CHUNK), F32),
            pltpu.VMEM((INNER, CHUNK), F32), pltpu.VMEM((INNER, STRIP), BF16),
            pltpu.VMEM((INNER // 2, STRIP), BF16), pltpu.VMEM((INNER // 2, STRIP), BF16),
            pltpu.VMEM((STRIP, D), BF16), dma((3, STRIPS, 2)), dma((2,)),
            dma((count,)), dma((count,)), dma,
        ],
        compiler_params=pltpu.CompilerParams(
            vmem_limit_bytes=60 * 2**20, collective_id=collective_id, has_side_effects=True
        ),
        name="mixer_forward",
    )(x, back, weights, weights, gain, taps, heads, inner, blocks, back)


def backward_call(x, back, weights, gain, taps, heads, kept, tail_sums, parts, sizes,
                  collective_id):
    last = STRIPS - 1

    def rows(width):
        return pl.BlockSpec((STRIP, width), lambda i: (last - i, 0))

    def cols(height):
        return pl.BlockSpec((height, STRIP), lambda i: (0, last - i))

    Z = sizes[0]
    lines = flat_lines(sizes[0] * sizes[1])
    size = (parts[0].shape[1], D)
    dma = pltpu.SemaphoreType.DMA
    hbm = pl.BlockSpec(memory_space=pl.ANY)
    return pl.pallas_call(
        functools.partial(backward_kernel, sizes),
        grid=(STRIPS,),
        in_specs=[
            rows(D), rows(D), columns(WIDE, 0),
            columns(256, (HALF + STEP_AT) // 256), whole((1, D)),
            whole((KCONV, CONVCH, CHUNK)), whole((3, HEADS, CHUNK)), cols(CONVCH),
            cols(CONVCH), cols(STEP),
            pl.BlockSpec((PER, INNER, NSTATE), lambda i: (last - i, 0, 0)), cols(INNER),
            cols(INNER), cols(HEADS), whole((8, TAIL_SUMS)), hbm, hbm,
        ],
        out_specs=[
            rows(D), cols(CONV_A // 2), cols((CONVCH - CONV_A) // 2), whole((lines, 128)),
            whole((Z,) + size), whole((Z,) + size), hbm, hbm,
        ],
        out_shape=[
            shape(LEN, D), shape(CONV_A // 2, LEN, dtype=BF16),
            shape((CONVCH - CONV_A) // 2, LEN, dtype=BF16), shape(lines, 128),
            shape(Z, *size), shape(Z, *size), shape(CONV_A // 2, LEN, dtype=BF16),
            shape((CONVCH - CONV_A) // 2, LEN, dtype=BF16),
        ],
        scratch_shapes=[
            pltpu.VMEM((CONV_A, STRIP), BF16), pltpu.VMEM((CONVCH - CONV_A, STRIP), BF16),
            pltpu.VMEM((CONV_A // 2, STRIP), BF16),
            pltpu.VMEM(((CONVCH - CONV_A) // 2, STRIP), BF16), dma((2, STRIPS, 2)),
            pltpu.VMEM((CONVCH, STRIP), F32),
            pltpu.VMEM((INNER, NSTATE), F32), pltpu.VMEM((HEADS, CHUNK), F32),
            pltpu.VMEM((KCONV - 1, CONVCH, CHUNK), F32), pltpu.VMEM((HEADS, CHUNK), F32),
            pltpu.VMEM((HEADS, CHUNK), F32), pltpu.VMEM((STEP, STRIP), BF16),
            pltpu.VMEM((STEP, D), F32), pltpu.VMEM((8, D), F32),
            pltpu.VMEM((KCONV + 1, CONVCH, CHUNK), F32), pltpu.VMEM((2, HEADS, CHUNK), F32),
            pltpu.VMEM((D, STRIP), F32),
        ]
        + 2 * (plane_scratch(sizes, size) + [dma]),
        compiler_params=pltpu.CompilerParams(
            vmem_limit_bytes=63 * 2**20, collective_id=collective_id, has_side_effects=True
        ),
        name="mixer_backward",
    )(
        x, back, weights, weights, gain, taps, heads, *kept, tail_sums,
        *(by_chip(part, sizes) for part in parts),
    )


def grads_kernel(*refs):
    ins, outs, (sides, others, results, sems, out_sems) = refs[:8], refs[8:10], refs[10:]
    copies = []
    for k in range(4):
        copies.append([
            pltpu.make_async_copy(ins[2 * k], sides.at[k], sems.at[2 * k]),
            pltpu.make_async_copy(ins[2 * k + 1], others.at[k], sems.at[2 * k + 1]),
        ])
        for copy in copies[k]:
            copy.start()
    stores = []
    for k in range(2):
        for half in (0, 1):
            for copy in copies[2 * k + half]:
                copy.wait()
            part = dot(sides[2 * k + half], others[2 * k + half])
            if half == 0:
                results[k] = part
            else:
                results[k] += part
        stores.append(pltpu.make_async_copy(results.at[k], outs[k], out_sems.at[k]))
        stores[k].start()
    for store in stores:
        store.wait()


def grads_call(own_normed, peer_normed, own_dgate, peer_dgate, backs, hbs):
    rows = INNER // 2
    hbm = pl.BlockSpec(memory_space=pl.ANY)
    return pl.pallas_call(
        grads_kernel,
        in_specs=[hbm] * 8,
        out_specs=[hbm] * 2,
        out_shape=[shape(rows, D)] * 2,
        scratch_shapes=[
            pltpu.VMEM((4, rows, LEN), BF16), pltpu.VMEM((4, LEN, D), BF16),
            pltpu.VMEM((2, rows, D), F32), pltpu.SemaphoreType.DMA((8,)),
            pltpu.SemaphoreType.DMA((2,)),
        ],
        compiler_params=pltpu.CompilerParams(vmem_limit_bytes=60 * 2**20),
        name="grads",
    )(own_normed, backs[0], peer_normed, backs[1], own_dgate, hbs[0], peer_dgate, hbs[1])


def flat_lines(count):
    return -(-(HEADS * D + SMALL) // (1024 * count)) * 8 * count


def block_and_gradients(x, back, weights, vectors, blocks, sizes, collective_ids):
    count = sizes[0] * sizes[1]
    gain, taps, heads, inner = vectors
    (
        out, hb, cin, c, raw, states, own_normed, dy, dgate, own_dgate, dlogs, tail_sums, moved,
        peer_normed, peer_dgate, peer_hb, peer_back,
    ) = forward_call(
        x, back, weights, gain, taps, heads, inner, blocks, sizes, collective_ids[0]
    )
    parts = grads_call(
        own_normed, peer_normed, own_dgate, peer_dgate, (back, peer_back), (hb, peer_hb)
    )
    parts = [part.reshape(count // 2, -1, D) for part in parts]
    dx, own_a, own_b, flat, out_column, gate_column, peer_a, peer_b = backward_call(
        x, back, weights, gain, taps, heads, (cin, c, raw, states, dy, dgate, dlogs), tail_sums,
        parts, sizes, collective_ids[1],
    )
    factors = (own_a, peer_a, own_b, peer_b, hb, peer_hb)
    return out, dx, [out_column, gate_column], factors, flat.reshape(count, -1, 128), moved


MESH = pl.DeviceIdType.MESH


class Place:
    def __init__(self, sizes):
        self.Z, self.F = sizes
        self.C, self.Y = 2, 2
        self.X = self.F // 4
        f = lax.axis_index("fsdp")
        self.z = lax.axis_index("dp")
        self.c = lax.rem(f, 2)
        self.x = lax.rem(f // 2, self.X)
        self.y = f // (2 * self.X)
        self.f = f

    def at(self, z=None, y=None, x=None, c=None):
        z = self.z if z is None else z
        y = self.y if y is None else y
        x = self.x if x is None else x
        c = self.c if c is None else c
        return (z, (y * self.X + x) * 2 + c)

    def other_x(self, step):
        return lax.rem(self.x + step, self.X)


def signal(device):
    pl.semaphore_signal(
        pltpu.get_barrier_semaphore(), inc=1, device_id=device, device_id_type=MESH
    )


def greet_all(place):
    count = place.Z * place.F
    me = place.z * place.F + place.f

    def step(i, carry):
        peer = lax.rem(me + i, count)
        signal((peer // place.F, lax.rem(peer, place.F)))
        return carry

    lax.fori_loop(1, count, step, 0)
    pl.semaphore_wait(pltpu.get_barrier_semaphore(), count - 1)


def remote(src, dst, send, recv, device):
    return pltpu.make_async_remote_copy(
        src_ref=src, dst_ref=dst, send_sem=send, recv_sem=recv, device_id=device,
        device_id_type=MESH,
    )


def add_blocks(dst, src, count):
    def step(i, carry):
        target = dst(i)
        target[...] = target[...] + src(i)[...]
        return carry

    lax.fori_loop(0, count, step, 0)


class Swap:
    def __init__(self, place, src, dst, send, recv, local, same=False, narrow=None):
        self.place, self.src, self.dst, self.same, self.narrow = place, src, dst, same, narrow
        self.send, self.recv, self.local = send, recv, local
        self.count = place.Z * place.F
        self.me = place.z * place.F + place.f

    def block(self, peer):
        return self.src if self.same else self.src.at[peer]

    def cut(self, ref, odd):
        return ref.at[:, pl.ds(0, self.narrow)] if odd else ref

    def each(self, sender, act):
        if self.narrow is None:
            act(False)
        else:
            @pl.when(lax.rem(sender, 2) == 0)
            def _():
                act(False)

            @pl.when(lax.rem(sender, 2) == 1)
            def _():
                act(True)

    def to(self, i, odd):
        peer = lax.rem(self.me + i, self.count)
        return remote(
            self.cut(self.block(peer), odd), self.cut(self.dst.at[self.me], odd),
            self.send.at[i], self.recv.at[i],
            (peer // self.place.F, lax.rem(peer, self.place.F)),
        )

    def keep(self):
        return pltpu.make_async_copy(self.block(self.me), self.dst.at[self.me], self.local)

    def start(self):
        self.keep().start()

        def step(i, carry):
            self.each(self.me, lambda odd: self.to(i, odd).start())
            return carry

        lax.fori_loop(1, self.count, step, 0)

    def wait(self):
        self.keep().wait()

        def step(i, carry):
            sender = lax.rem(self.me + self.count - i, self.count)
            self.each(self.me, lambda odd: self.to(i, odd).wait_send())
            self.each(sender, lambda odd: remote(
                self.cut(self.block(sender), odd), self.cut(self.dst.at[sender], odd),
                self.send.at[i], self.recv.at[i],
                (sender // self.place.F, lax.rem(sender, self.place.F)),
            ).wait_recv())
            return carry

        lax.fori_loop(1, self.count, step, 0)


def greet_near(place, along_z):
    signal(place.at(c=1 - place.c))
    signal(place.at(y=1 - place.y))
    for s in range(1, place.X):
        signal(place.at(x=place.other_x(s)))
    if along_z:
        for s in range(1, place.Z):
            signal(place.at(z=lax.rem(place.z + s, place.Z)))
    pl.semaphore_wait(
        pltpu.get_barrier_semaphore(), place.X + 1 + (place.Z - 1 if along_z else 0)
    )


class Plane:
    def __init__(self, place, acc, x1, y1, x2, y2, sems):
        self.p, self.acc = place, acc
        self.x1, self.y1, self.x2, self.y2, self.sems = x1, y1, x2, y2, sems
        self.h = place.Z // 2

    def copies(self, stage):
        p, acc, h = self.p, self.acc, self.h
        low, high = pl.ds(0, h), pl.ds(h, p.Z - h)
        out = []
        base = stage * p.X
        for s in range(1, p.X):
            x = p.other_x(s)
            if stage == 0:
                src, dst = acc.at[low, :, x], self.x1.at[s - 1]
            else:
                src, dst = acc.at[high, p.y, x], self.x2.at[s - 1]
            sem = self.sems.at[base + s]
            out.append(remote(src, dst, sem.at[0], sem.at[1], p.at(x=x)))
        if stage == 0:
            src, dst = acc.at[high, 1 - p.y], self.y1
        else:
            src, dst = acc.at[low, 1 - p.y, p.x], self.y2
        sem = self.sems.at[base]
        out.append(remote(src, dst, sem.at[0], sem.at[1], p.at(y=1 - p.y)))
        return out

    def start(self, stage):
        for copy in self.copies(stage):
            copy.start()

    def finish(self, stage):
        p, acc, h = self.p, self.acc, self.h
        for copy in self.copies(stage):
            copy.wait()
        for s in range(p.X - 1):
            if stage == 0:
                add_blocks(
                    lambda i: acc.at[i // p.Y, lax.rem(i, p.Y), p.x],
                    lambda i: self.x1.at[s, i // p.Y, lax.rem(i, p.Y)],
                    h * p.Y,
                )
            else:
                add_blocks(
                    lambda i: acc.at[h + i, p.y, p.x], lambda i: self.x2.at[s, i], p.Z - h
                )
        if stage == 0:
            add_blocks(
                lambda i: acc.at[h + i // p.X, p.y, lax.rem(i, p.X)],
                lambda i: self.y1.at[i // p.X, lax.rem(i, p.X)],
                (p.Z - h) * p.X,
            )
        else:
            add_blocks(lambda i: acc.at[i, p.y, p.x], lambda i: self.y2.at[i], h)


def plane_scratch(sizes, block):
    Z, X, Y = sizes[0], sizes[1] // 4, 2
    h = Z // 2
    return [
        pltpu.VMEM((Z, Y, X) + block, F32), pltpu.VMEM((X - 1, h, Y) + block, F32),
        pltpu.VMEM((Z - h, X) + block, F32), pltpu.VMEM((X - 1, Z - h) + block, F32),
        pltpu.VMEM((h,) + block, F32), pltpu.SemaphoreType.DMA((2 * X, 2)),
    ]


def by_place(blocks, sizes):
    return blocks.reshape((sizes[0], 2, sizes[1] // 4, 2) + blocks.shape[1:])


def by_chip(blocks, sizes):
    return blocks.reshape((sizes[0], 2, sizes[1] // 4) + blocks.shape[1:])


class PlaneSum:
    def __init__(self, place, part, work):
        self.p, self.part, self.acc, self.sem = place, part, work[0], work[6]
        self.plane = Plane(place, *work[:6])

    def copy(self):
        return pltpu.make_async_copy(self.part, self.acc, self.sem)

    def begin(self):
        self.copy().start()

    def start(self):
        self.copy().wait()
        self.plane.start(0)

    def block(self, z):
        return self.acc.at[z, self.p.y, self.p.x]

    def column(self):
        return self.acc[:, self.p.y, self.p.x]


class Product(PlaneSum):
    def __init__(self, place, factors, work):
        super().__init__(place, None, work)
        self.factors = factors

    def begin(self):
        pass

    def start(self):
        own, peer, right, peer_right = self.factors
        value = dot(own[...], right[...]) + dot(peer[...], peer_right[...])
        Z, Y, X, per, _ = self.acc.shape
        for i in range(Z * Y * X):
            self.acc[i // (Y * X), i // X % Y, i % X] = value[per * i : per * i + per]
        self.plane.start(0)


class PairSum(PlaneSum):
    def __init__(self, place, part, work):
        super().__init__(place, part, work)
        self.core, self.sems = work[7], work[8]

    def copies(self):
        p = self.p
        return (
            remote(
                self.part.at[:, :, :, 1 - p.c], self.core, self.sems.at[0], self.sems.at[1],
                p.at(c=1 - p.c),
            ),
            pltpu.make_async_copy(self.part.at[:, :, :, p.c], self.acc, self.sem),
        )

    def begin(self):
        for copy in self.copies():
            copy.start()

    def start(self):
        p = self.p
        for copy in self.copies():
            copy.wait()

        def place_of(i):
            return i // (p.Y * p.X), lax.rem(i // p.X, p.Y), lax.rem(i, p.X)

        add_blocks(
            lambda i: self.acc.at[place_of(i)], lambda i: self.core.at[place_of(i)],
            p.Z * p.Y * p.X,
        )
        self.plane.start(0)


class Column:
    def __init__(self, part, acc, sem):
        self.copy = pltpu.make_async_copy(part, acc, sem)
        self.acc = acc

    def block(self, z):
        return self.acc.at[z]


class Chain:
    def __init__(self, place, part, held, sems):
        self.p, self.part, self.held, self.sems = place, part, held, sems

    def flow(self, t, right):
        p, side = self.p, 0 if right else 1
        sem = self.sems.at[side, t]
        target = p.at(z=p.z + 1 if right else p.z - 1)
        return remote(self.part.block(t), self.held.at[side, t], sem.at[0], sem.at[1], target)

    def send(self, t, right):
        @pl.when(self.p.z < t if right else self.p.z > t)
        def _():
            self.flow(t, right).start()

    def first(self):
        p = self.p
        for j in range(p.Z - 1):
            @pl.when(p.z == 0)
            def _():
                self.send(p.Z - 1 - j, True)

            @pl.when(p.z == p.Z - 1)
            def _():
                self.send(j, False)

    def receive(self, t, right):
        self.flow(t, right).wait_recv()
        mine = self.part.block(t)
        mine[...] = mine[...] + self.held[0 if right else 1, t]

    def forward(self, j):
        p = self.p
        for right in (True, False):
            t = p.Z - 1 - j if right else j

            @pl.when(jnp.logical_and(p.z > 0, p.z < t) if right else
                     jnp.logical_and(p.z < p.Z - 1, p.z > t))
            def _():
                self.receive(t, right)
                self.flow(t, right).start()

    def last(self):
        p = self.p

        @pl.when(p.z > 0)
        def _():
            self.receive(p.z, True)

        @pl.when(p.z < p.Z - 1)
        def _():
            self.receive(p.z, False)

    def finish(self):
        p = self.p
        for t in range(p.Z):
            for right in (True, False):
                @pl.when(p.z < t if right else p.z > t)
                def _():
                    self.flow(t, right).wait_send()


class Direct:
    def __init__(self, place, part, held, sems):
        self.p, self.part, self.held, self.sems = place, part, held, sems

    def over(self, s):
        p = self.p
        z = lax.rem(p.z + s, p.Z)
        sem = self.sems.at[s]
        return remote(self.part.block(z), self.held.at[s - 1], sem.at[0], sem.at[1], p.at(z=z))

    def start(self):
        for s in range(1, self.p.Z):
            self.over(s).start()

    def last(self):
        mine = self.part.block(self.p.z)
        total = mine[...]
        for s in range(1, self.p.Z):
            self.over(s).wait()
            total = total + self.held[s - 1]
        mine[...] = total


def scatter_kernel(sizes, *refs):
    columns_in, factors, small_in, outs, rest = (
        refs[:2], refs[2:8], refs[8], refs[9:14], list(refs[14:])
    )

    def take(n):
        taken = rest[:n]
        del rest[:n]
        return taken

    p = Place(sizes)
    columns = [Column(ref, *take(2)) for ref in columns_in]
    chains = [Chain(p, column, *take(2)) for column in columns]
    own_a, peer_a, own_b, peer_b, hb, peer_hb = factors
    queue = [
        Product(p, (own_a, peer_a, hb, peer_hb), take(7)),
        Product(p, (own_b, peer_b, hb, peer_hb), take(7)),
        PairSum(p, small_in, take(9)),
    ]
    queue = [(part, Direct(p, part, *take(2))) for part in queue]
    greet_near(p, True)
    for column in columns:
        column.copy.start()
    for part, _ in queue:
        part.begin()
    for column, chain in zip(columns, chains):
        column.copy.wait()
        chain.first()
    hops = p.Z - 2

    def forward(j):
        if j < hops:
            for chain in chains:
                chain.forward(j)

    stages = [
        lambda part, direct: part.start(),
        lambda part, direct: (part.plane.finish(0), part.plane.start(1)),
        lambda part, direct: (part.plane.finish(1), direct.start()),
    ]
    steps = len(queue) + len(stages) - 1
    for k in range(max(steps, hops)):
        for j in range(len(stages)):
            if 0 <= k - j < len(queue):
                stages[j](*queue[k - j])
        forward(k)
    for chain in chains:
        chain.last()
        chain.finish()
    for _, direct in queue:
        direct.last()
    for part, out in zip(columns + [part for part, _ in queue], outs):
        out[...] = part.block(p.z)[...]


def scatter_call(columns, factors, small, sizes, collective_id):
    Z, F = sizes
    X, Y = F // 4, 2
    chips = Z * X * Y
    dma = pltpu.SemaphoreType.DMA
    parts = [(factors[0].shape[0] // chips, D), (factors[2].shape[0] // chips, D)]
    parts.append(small.shape[1:])
    scratch = []
    for column in columns:
        scratch += [pltpu.VMEM(column.shape, F32), dma]
    for column in columns:
        scratch += [pltpu.VMEM((2, Z) + column.shape[1:], F32), dma((2, Z, 2))]
    for block in parts:
        scratch += plane_scratch(sizes, block) + [dma]
    scratch += [pltpu.VMEM((Z, Y, X) + parts[2], F32), dma((2,))]
    for block in parts:
        scratch += [pltpu.VMEM((Z - 1,) + block, F32), dma((Z, 2))]
    hbm = pl.BlockSpec(memory_space=pl.ANY)
    vmem = pl.BlockSpec(memory_space=pltpu.VMEM)
    return pl.pallas_call(
        functools.partial(scatter_kernel, sizes),
        out_shape=[shape(*block) for block in [column.shape[1:] for column in columns] + parts],
        in_specs=[hbm] * 2 + [vmem] * 6 + [hbm],
        out_specs=[vmem] * 5,
        scratch_shapes=scratch,
        compiler_params=pltpu.CompilerParams(
            collective_id=collective_id, has_side_effects=True, vmem_limit_bytes=60 * 2**20
        ),
        name="scatter",
    )(*columns, *factors, by_place(small, sizes))


def gather_kernel(
    sizes, w_in_ref, w_out_ref, m_in_ref, m_out_ref, params_ref, inner_rows_ref,
    all_ref, blocks_ref, gain_ref, taps_ref, heads_ref, inner_ref,
    mine, keep_sem, z_sems, near, far, across,
):
    p = Place(sizes)
    Z, h = p.Z, p.Z // 2
    greet_near(p, True)
    own = mine.shape[0]
    partner = p.at(c=1 - p.c)
    mine[:, :WIDE] = w_in_ref[:, :WIDE].astype(BF16)
    mine[:, WIDE : WIDE + INNER] = w_out_ref[...].astype(BF16)
    mine[:, WIDE + INNER :] = jnp.concatenate(
        [w_in_ref[:, WIDE:], jnp.zeros((own, 2 * HALF - IN_W - INNER), F32)], axis=1
    ).astype(BF16)
    keep = pltpu.make_async_copy(mine, all_ref.at[p.z, p.y, p.x, p.c], keep_sem)
    keep.start()

    def spot(z, y, x):
        return all_ref.at[z, y, x, p.c]

    def copy(src, dst, sem, device):
        return remote(src, dst, sem.at[0], sem.at[1], device)

    def along_z(z, right, src=None):
        here = spot(z, p.y, p.x)
        target = p.at(z=p.z + 1 if right else p.z - 1)
        return copy(here if src is None else src, here, z_sems.at[0 if right else 1, z], target)

    def near_copies(z, src=None):
        here = spot(z, p.y, p.x)
        src = here if src is None else src
        found = [copy(src, here, near.at[z, 0], p.at(y=1 - p.y))]
        for s in range(1, p.X):
            found.append(copy(src, here, near.at[z, s], p.at(x=p.other_x(s))))
        return found

    def near_arrivals(z):
        found = [(z, 1 - p.y, p.x, near.at[z, 0])]
        for s in range(1, p.X):
            found.append((z, p.y, lax.rem(p.x + p.X - s, p.X), near.at[z, s]))
        return found

    def far_copies(z):
        low, high = [], []
        for s in range(1, p.X):
            x = p.other_x(s)
            there = spot(z, p.y, x)
            low.append(copy(there, there, far.at[z, s], p.at(y=1 - p.y)))
            there = spot(z, 1 - p.y, p.x)
            high.append(copy(there, there, far.at[z, s], p.at(x=x)))
        return low, high

    def far_arrivals(z):
        low = [(z, 1 - p.y, p.other_x(s), far.at[z, s]) for s in range(1, p.X)]
        high = [
            (z, 1 - p.y, lax.rem(p.x + p.X - s, p.X), far.at[z, s]) for s in range(1, p.X)
        ]
        return low, high

    def to_partner(z, y, x, src=None):
        here = spot(z, y, x)
        return copy(here if src is None else src, here, across.at[z, y, x], partner)

    def await_block(z, y, x, sem):
        here = spot(z, y, x)
        copy(here, here, sem, partner).wait_recv()
        to_partner(z, y, x).start()

    def start_all(copies):
        for c in copies:
            c.start()

    @pl.when(p.z < Z - 1)
    def _():
        along_z(p.z, True, mine).start()

    @pl.when(p.z > 0)
    def _():
        along_z(p.z, False, mine).start()

    start_all(near_copies(p.z, mine))
    to_partner(p.z, p.y, p.x, mine).start()
    spread_vectors(params_ref, inner_rows_ref, gain_ref, taps_ref, heads_ref, inner_ref)
    spread_moments(m_in_ref, m_out_ref, blocks_ref)

    def visit(right, z):
        await_block(z, p.y, p.x, z_sems.at[0 if right else 1, z])

        @pl.when(p.z < Z - 1 if right else p.z > 0)
        def _():
            along_z(z, right).start()

        start_all(near_copies(z))

    def by_distance(low, high):
        for j in range(1, Z):
            @pl.when(p.z - j >= 0)
            def _():
                low(p.z - j)

            @pl.when(p.z + j < Z)
            def _():
                high(p.z + j)

    by_distance(lambda z: visit(True, z), lambda z: visit(False, z))

    def relay(z):
        for block in near_arrivals(z):
            await_block(*block)
        low, high = far_copies(z)

        @pl.when(z < h)
        def _():
            start_all(low)

        @pl.when(z >= h)
        def _():
            start_all(high)

    relay(p.z)
    by_distance(relay, relay)

    def settle(z):
        low, high = far_arrivals(z)

        @pl.when(z < h)
        def _():
            for block in low:
                await_block(*block)

        @pl.when(z >= h)
        def _():
            for block in high:
                await_block(*block)

    settle(p.z)
    by_distance(settle, settle)
    keep.wait()

    def finish(z, carry):
        for c in near_copies(z):
            c.wait_send()
        low, high = far_copies(z)

        @pl.when(z < h)
        def _():
            for c in low:
                c.wait_send()

        @pl.when(z >= h)
        def _():
            for c in high:
                c.wait_send()

        @pl.when(jnp.logical_and(z <= p.z, p.z < Z - 1))
        def _():
            along_z(z, True).wait_send()

        @pl.when(jnp.logical_and(z >= p.z, p.z > 0))
        def _():
            along_z(z, False).wait_send()

        for y in range(p.Y):
            for x in range(p.X):
                to_partner(z, y, x).wait_send()
                theirs = all_ref.at[z, y, x, 1 - p.c]
                copy(theirs, theirs, across.at[z, y, x], partner).wait_recv()

        return carry

    lax.fori_loop(0, Z, finish, 0)


def column_of(row):
    return jnp.broadcast_to(row, (128, 128)).T


def spread_vectors(params_ref, inner_rows_ref, gain_ref, taps_ref, heads_ref, inner_ref):
    row = D // 128
    gain_ref[...] = beside(*[params_ref[j : j + 1] for j in range(row)])
    for k in range(KCONV + 1):
        for j in range(CONVCH // 128):
            taps_ref[k, 128 * j : 128 * j + 128] = column_of(params_ref[row : row + 1])
            row += 1
    heads = column_of(params_ref[row : row + 1])
    heads_ref[0] = heads[:HEADS]
    heads_ref[1] = -jnp.exp(heads[HEADS : 2 * HEADS])
    heads_ref[2] = heads[2 * HEADS : 3 * HEADS]
    for j in range(INNER // 128):
        inner_ref[128 * j : 128 * j + 128] = column_of(inner_rows_ref[j : j + 1])


def cuts_of(count):
    widths = [(0, INNER), (INNER, CONV_A), (INNER + CONV_A, CONVCH - CONV_A)]
    return [(start, width, width // count) for start, width in widths], INNER // count


def first_of(d, width, count):
    return d % 2 * (width // 2) + d // 2 * (width // count)


def spread_moments(m_in_ref, m_out_ref, blocks_ref):
    count, own, lanes_in_block = blocks_ref.shape
    ins, outs = cuts_of(count)
    step = m_in_ref[:, WIDE:]
    used = sum(each for _, _, each in ins) + outs + HEADS
    for d in range(count):
        pieces = []
        for start, width, each in ins:
            at = start + first_of(d, width, count)
            pieces.append(m_in_ref[:, at : at + each])
        at = first_of(d, INNER, count)
        pieces += [m_out_ref[:, at : at + outs], step]
        blocks_ref[d] = beside(*pieces, jnp.zeros((own, lanes_in_block - used), F32))


def gather_call(weight_in, weight_out, moment_in, moment_out, params, sizes, collective_id):
    Z, F = sizes
    X, Y = F // 4, 2
    own = weight_in.shape[0]
    count = Z * F
    inner_rows = params[-INNER:].reshape(-1, 128)
    params = jnp.pad(params, (0, -params.shape[0] % 128)).reshape(-1, 128)
    vmem = pl.BlockSpec(memory_space=pltpu.VMEM)
    hbm = pl.BlockSpec(memory_space=pl.ANY)
    whole_weights, blocks, *vectors = pl.pallas_call(
        functools.partial(gather_kernel, sizes),
        out_shape=[
            shape(Z, Y, X, 2, own, 2 * HALF, dtype=BF16), shape(count, own, 256), shape(1, D),
            shape(KCONV + 1, CONVCH, CHUNK), shape(3, HEADS, CHUNK), shape(INNER, CHUNK),
        ],
        in_specs=[vmem] * 6,
        out_specs=[hbm] + [vmem] * 5,
        scratch_shapes=[
            pltpu.VMEM((own, 2 * HALF), BF16), pltpu.SemaphoreType.DMA, pltpu.SemaphoreType.DMA((2, Z, 2)),
            pltpu.SemaphoreType.DMA((Z, X, 2)), pltpu.SemaphoreType.DMA((Z, X, 2)),
            pltpu.SemaphoreType.DMA((Z, Y, X, 2)),
        ],
        compiler_params=pltpu.CompilerParams(
            collective_id=collective_id, has_side_effects=True, vmem_limit_bytes=60 * 2**20
        ),
        name="weights_gather",
    )(weight_in, weight_out, moment_in, moment_out, params, inner_rows)
    return whole_weights.reshape(D, 2 * HALF), blocks, vectors


def gram_rows(slab, row):
    high, low = split(slab)
    left = above(high, low, high)[:, 128 * row : 128 * row + 128]
    return dot_tn(left, above(high, high, low)[:, 128 * row :])


def pack_gram(targets, slab):
    Z, Y, X, per, _ = targets[0].shape
    rows = above(*[
        beside(gram_rows(slab, i), gram_rows(slab, D // 128 - 1 - i)) for i in range(D // 256)
    ])
    if Z * Y * X * per > rows.shape[0]:
        rows = above(rows, jnp.zeros((Z * Y * X * per - rows.shape[0], rows.shape[1]), F32))
    at = 0
    for target in targets:
        cols = slice(at, at + target.shape[4])
        for i in range(Z * Y * X):
            target[i // (Y * X), i // X % Y, i % X] = rows[per * i : per * i + per, cols]
        at += target.shape[4]


def unpack_gram(gram, packed):
    Z, Y, X, _, _ = packed[0].shape
    rows = beside(*[
        above(*[part[i // (Y * X), i // X % Y, i % X] for i in range(Z * Y * X)])
        for part in packed
    ])
    for i in range(D // 256):
        pair = rows[128 * i : 128 * i + 128]
        wide_part, j = D - 128 * i, D // 128 - 1 - i
        for row, part in ((i, pair[:, :wide_part]), (j, pair[:, wide_part:])):
            gram[128 * row : 128 * row + 128, 128 * row :] = part
            for k in range(row + 1, D // 128):
                at = 128 * (k - row)
                gram[128 * k : 128 * k + 128, 128 * row : 128 * row + 128] = part[
                    :, at : at + 128
                ].T


BEHIND = 2


class AllSum:
    def __init__(self, place, work):
        self.p = place
        self.total, self.acc, self.core, self.core_sems = work[0], work[1], work[7], work[8]
        self.held, self.z_sems, self.back_sems = work[9:12]
        self.plane = Plane(place, *work[1:7])
        self.steps = [
            self.pair, self.second, self.cross, self.turn, self.spread, self.spread_on, self.done,
        ]

    def to_core(self):
        p = self.p
        return remote(
            self.total, self.core, self.core_sems.at[0], self.core_sems.at[1], p.at(c=1 - p.c)
        )

    def pair(self):
        p = self.p
        self.to_core().wait()

        def place_of(i):
            return i // (p.Y * p.X), lax.rem(i // p.X, p.Y), lax.rem(i, p.X)

        add_blocks(
            lambda i: self.acc.at[place_of(i)], lambda i: self.core.at[place_of(i)],
            p.Z * p.Y * p.X,
        )
        self.plane.start(0)

    def second(self):
        self.plane.finish(0)
        self.plane.start(1)

    def over(self, s):
        p = self.p
        z = lax.rem(p.z + s, p.Z)
        sem = self.z_sems.at[0, s]
        return remote(
            self.acc.at[z, p.y, p.x], self.held.at[s - 1], sem.at[0], sem.at[1], p.at(z=z)
        )

    def cross(self):
        self.plane.finish(1)
        for s in range(1, self.p.Z):
            self.over(s).start()

    def back(self, s, mine):
        p = self.p
        sem = self.z_sems.at[1, s]
        z = p.z if mine else lax.rem(p.z + p.Z - s, p.Z)
        ref = self.total.at[z, p.y, p.x]
        return remote(ref, ref, sem.at[0], sem.at[1], p.at(z=lax.rem(p.z + s, p.Z)))

    def turn(self):
        p = self.p
        for s in range(1, p.Z):
            self.over(s).wait()
        result = self.acc[p.z, p.y, p.x]
        for s in range(1, p.Z):
            result = result + self.held[s - 1]
        self.total[p.z, p.y, p.x] = result
        for s in range(1, p.Z):
            self.back(s, True).start()

    def planes(self, stage, mine):
        p, total, h = self.p, self.total, self.p.Z // 2
        low, high = pl.ds(0, h), pl.ds(h, p.Z - h)
        found = []
        for s in range(1, p.X):
            sem = self.back_sems.at[stage * p.X + s]
            x = p.x if mine else lax.rem(p.x + p.X - s, p.X)
            ref = total.at[high, p.y, x] if stage == 0 else total.at[low, :, x]
            found.append(remote(ref, ref, sem.at[0], sem.at[1], p.at(x=p.other_x(s))))
        sem = self.back_sems.at[stage * p.X]
        y = p.y if mine else 1 - p.y
        ref = total.at[low, y, p.x] if stage == 0 else total.at[high, y]
        found.append(remote(ref, ref, sem.at[0], sem.at[1], p.at(y=1 - p.y)))
        return found

    def arrive(self, copies):
        for mine, theirs in copies:
            mine.wait_send()
            theirs.wait_recv()

    def spread(self):
        self.arrive([(self.back(s, True), self.back(s, False)) for s in range(1, self.p.Z)])
        for copy in self.planes(0, True):
            copy.start()

    def spread_on(self):
        self.arrive(zip(self.planes(0, True), self.planes(0, False)))
        for copy in self.planes(1, True):
            copy.start()

    def done(self):
        self.arrive(zip(self.planes(1, True), self.planes(1, False)))


def all_sum_scratch(sizes, block):
    Z, X, Y = sizes[0], sizes[1] // 4, 2
    dma = pltpu.SemaphoreType.DMA
    return [pltpu.VMEM((Z, Y, X) + block, F32)] + plane_scratch(sizes, block) + [
        pltpu.VMEM((Z, Y, X) + block, F32), dma((2,)), pltpu.VMEM((Z - 1,) + block, F32),
        dma((2, Z, 2)), dma((2 * X, 2)),
    ]


def put_left(left, value, rows):
    high, low = split(value)
    left[rows] = beside(high, low, high)


def put_right(right, value, row):
    high, low = split(value)
    size = value.shape[0]
    right[row : row + size] = high
    right[D + row : D + row + size] = high
    right[2 * D + row : 2 * D + row + size] = low


TILE = 256


def symmetric_product(target, left, right):
    for i in range(D // TILE):
        rows = slice(TILE * i, TILE * i + TILE)
        part = dot(left[rows], right[:, TILE * i :])
        target[rows, TILE * i :] = part
        for j in range(i + 1, D // TILE):
            at = TILE * (j - i)
            target[TILE * j : TILE * j + TILE, rows] = part[:, at : at + TILE].T


def iterate(gram, square, factor, left, right, slab, slab_left):
    tiles = [slice(TILE * i, TILE * i + TILE) for i in range(D // TILE)]
    row = lax.broadcasted_iota(jnp.int32, (TILE, D), 0)
    col = lax.broadcasted_iota(jnp.int32, (TILE, D), 1)
    diagonals = [(row + TILE * i == col) for i in range(D // TILE)]
    trace = jnp.zeros((8, D), F32)
    for rows, diagonal in zip(tiles, diagonals):
        trace = trace + fold(jnp.where(diagonal, gram[rows], 0.0))
    trace = jnp.sum(jnp.sum(trace, axis=0, keepdims=True), axis=1, keepdims=True)
    scale = 1.0 / (jnp.sqrt(trace) + 1e-07)
    for rows in tiles:
        gram[rows] = gram[rows] * (scale * scale)
    slab[...] = slab[...] * scale

    def step(iteration, carry):
        for i, rows in enumerate(tiles):
            value = gram[rows]
            put_left(left, value, rows)
            put_right(right, value, TILE * i)
        symmetric_product(square, left, right)
        for i, rows in enumerate(tiles):
            value = COEF_B * gram[rows] + COEF_C * square[rows]
            put_right(right, value + jnp.where(diagonals[i], COEF_A, 0.0), TILE * i)
        put_left(slab_left, slab[...], slice(None))
        slab[...] = dot(slab_left[...], right[...])
        symmetric_product(factor, left, right)
        for rows in tiles:
            put_left(left, factor[rows], rows)
        symmetric_product(gram, left, right)
        return carry

    lax.fori_loop(0, ITERS - 1, step, 0)
    for i, rows in enumerate(tiles):
        put_right(right, gram[rows], TILE * i)
    first = slab[...]
    put_left(slab_left, first, slice(None))
    once = dot(slab_left[...], right[...])
    put_left(slab_left, once, slice(None))
    slab[...] = COEF_A * first + COEF_B * once + COEF_C * dot(slab_left[...], right[...])


def update_kernel(
    sizes, gate_ref, conv_a_ref, conv_b_ref, out_ref, small_ref, old_ref, moved_ref, smalls_ref, spread_ref,
    give, given, give_sems, messages, smalls, gram, square, factor, left, right, slab, slab_left,
    swap_send, swap_recv, local, *work,
):
    p = Place(sizes)
    count = p.Z * p.F
    own = D // count
    gates = gate_ref.shape[0]
    ins = gates + conv_a_ref.shape[0] + conv_b_ref.shape[0]
    greet_all(p)
    swaps = [
        Swap(p, src, dst, swap_send.at[k], swap_recv.at[k], local.at[k], same, narrow)
        for k, (src, dst, same, narrow) in enumerate([
            (small_ref, smalls, True, None), (messages.at[0], moved_ref, False, None),
            (messages.at[1], spread_ref, False, -(-2 * gates // 128) * 128),
        ])
    ]
    swaps[0].start()
    old = old_ref[...].T
    new_in = above(gate_ref[...], conv_a_ref[...], conv_b_ref[...])
    new_out = out_ref[...]

    def push(gradient, moment):
        return gradient + MOMENTUM * (MOMENTUM * moment + gradient)

    push_in = push(new_in, old[:ins])
    push_out = above(push(new_out, old[ins : ins + gates]), jnp.zeros((ins - gates, D), F32))
    in_core = p.c == 0
    give[...] = jnp.where(in_core, push_out, push_in)
    slab[:ins] = jnp.where(in_core, push_in, push_out)
    partner = p.at(c=1 - p.c)
    pieces = [AllSum(p, work[:12]), AllSum(p, work[12:])]
    pack_gram([piece.total for piece in pieces], give[...])
    for piece in pieces:
        piece.to_core().start()
    exchange = remote(give, given, give_sems.at[0], give_sems.at[1], partner)
    exchange.start()
    pack_gram([piece.acc for piece in pieces], slab[:ins])

    def store_messages(k, turned):
        turned = beside(turned, jnp.zeros((D, 256 - turned.shape[1]), F32)) if (
            turned.shape[1] < 256) else turned
        for d in range(count):
            messages[k, d] = turned[own * d : own * d + own]

    steps = len(pieces[0].steps)
    for k in range(steps + BEHIND):
        for which, piece in enumerate(pieces):
            if 0 <= k - BEHIND * which < steps:
                piece.steps[k - BEHIND * which]()
        if k == 0:
            store_messages(0, above(new_in, new_out).T)
    exchange.wait()
    swaps[0].wait()
    swaps[1].start()
    smalls_ref[...] = smalls[...]
    rows = smalls[...].reshape(-1, 128)
    new_step = beside(*[rows[HEADS * j : HEADS * j + HEADS] for j in range(D // 128)])
    push_step = push(new_step, old_ref[...].T[ins + gates : ins + gates + HEADS])
    push_step = jnp.where(in_core, push_step, 0.0)
    mine, theirs = slab[:ins], given[...]
    slab_in = above(mine, theirs, push_step)
    slab_out = above(theirs[:gates], mine[:gates], jnp.zeros((2 * (ins - gates) + HEADS, D), F32))
    slab[: 2 * ins + HEADS] = jnp.where(in_core, slab_in, slab_out)
    slab[2 * ins + HEADS :] = jnp.zeros((slab.shape[0] - 2 * ins - HEADS, D), F32)
    unpack_gram(gram, [piece.total for piece in pieces])
    step_high, step_low = split(push_step)
    step_left = above(step_high, step_low, step_high)
    gram[...] = gram[...] + dot_tn(step_left, above(step_high, step_high, step_low))
    iterate(gram, square, factor, left, right, slab, slab_left)
    store_messages(1, slab[...].T)
    swaps[2].start()
    swaps[1].wait()
    swaps[2].wait()


def update_call(parts, small, old, sizes, collective_id):
    count = sizes[0] * sizes[1]
    own = D // count
    chips = count // 2
    ins = sum(part.shape[0] for part in parts[:3])
    per = -(-(D // 2) // (8 * chips)) * 8
    blocks = [(per, 512), (per, D + 128 - 512)]
    vmem = pl.BlockSpec(memory_space=pltpu.VMEM)
    hbm = pl.BlockSpec(memory_space=pl.ANY)
    dma = pltpu.SemaphoreType.DMA
    return pl.pallas_call(
        functools.partial(update_kernel, sizes),
        out_shape=[
            shape(count, own, 256), shape(count, *small.shape), shape(count, own, 256),
        ],
        in_specs=[vmem] * 6,
        out_specs=[hbm, vmem, hbm],
        scratch_shapes=[
            pltpu.VMEM((ins, D), F32), pltpu.VMEM((ins, D), F32), dma((2,)),
            pltpu.VMEM((2, count, own, 256), F32), pltpu.VMEM((count,) + small.shape, F32),
            pltpu.VMEM((D, D), F32), pltpu.VMEM((D, D), F32), pltpu.VMEM((D, D), F32),
            pltpu.VMEM((D, 3 * D), BF16), pltpu.VMEM((3 * D, D), BF16),
            pltpu.VMEM((256, D), F32), pltpu.VMEM((256, 3 * D), BF16),
            dma((3, count)), dma((3, count)), dma((3,)),
        ]
        + all_sum_scratch(sizes, blocks[0])
        + all_sum_scratch(sizes, blocks[1]),
        compiler_params=pltpu.CompilerParams(
            collective_id=collective_id, has_side_effects=True, vmem_limit_bytes=56 * 2**20
        ),
        name="update",
    )(*parts, small, old)


def finish_kernel(
    moved_ref, spread_ref, step_ref, w_in_ref, w_out_ref, m_in_ref, m_out_ref,
    g_in_ref, g_out_ref, new_m_in_ref, new_m_out_ref, new_w_in_ref, new_w_out_ref,
):
    count = moved_ref.shape[0]
    cuts, outs = cuts_of(count)
    ins = sum(each for _, _, each in cuts)
    decay = 1.0 - MATRIX_RATE * WEIGHT_DECAY
    order = [(2 * chip + core, core) for core in range(2) for chip in range(count // 2)]
    at = 0
    for start, width, each in cuts:
        cols = slice(start, start + width)
        g_in_ref[:, cols] = beside(*[moved_ref[d, :, at : at + each] for d, _ in order])
        new_w_in_ref[:, cols] = beside(*[
            spread_ref[d - core, :, ins * core + at : ins * core + at + each] for d, core in order
        ])
        at += each
    g_in_ref[:, WIDE:] = step_ref[...]
    new_w_in_ref[:, WIDE:] = spread_ref[0, :, 2 * ins : 2 * ins + HEADS]
    g_out_ref[...] = beside(*[moved_ref[d, :, ins : ins + outs] for d, _ in order])
    new_w_out_ref[...] = beside(*[
        spread_ref[d - core + 1, :, outs * core : outs * core + outs] for d, core in order
    ])
    for wide_side, g_ref, m_ref, w_ref, new_m_ref, new_w_ref in (
        (IN_W, g_in_ref, m_in_ref, w_in_ref, new_m_in_ref, new_w_in_ref),
        (INNER, g_out_ref, m_out_ref, w_out_ref, new_m_out_ref, new_w_out_ref),
    ):
        new_m_ref[...] = MOMENTUM * m_ref[...] + g_ref[...]
        rate = MATRIX_RATE * 0.2 * math.sqrt(max(D, wide_side))
        new_w_ref[...] = w_ref[...] * decay - rate * new_w_ref[...]


def finish_call(moved, spread, step_rows, weight_in, weight_out, moment_in, moment_out):
    vmem = pl.BlockSpec(memory_space=pltpu.VMEM)
    return pl.pallas_call(
        finish_kernel,
        out_shape=[shape(*weight_in.shape), shape(*weight_out.shape)] * 3,
        in_specs=[vmem] * 7,
        out_specs=[vmem] * 6,
        name="finish",
    )(moved, spread, step_rows, weight_in, weight_out, moment_in, moment_out)


def shards(
    inputs, cotangent, weight_in, weight_out, small_params, moment_in, moment_out, moment_small
):
    sizes = (lax.axis_size("dp"), lax.axis_size("fsdp"))
    own = weight_in.shape[0]
    weights, blocks, vectors = gather_call(
        weight_in, weight_out, moment_in, moment_out, small_params, sizes, 0
    )
    output, dx, columns, factors, small, old = block_and_gradients(
        inputs[0], cotangent[0], weights, vectors, blocks, sizes, (3, 4)
    )
    new_out, new_gate, new_conv_a, new_conv_b, new_small = scatter_call(
        columns, factors, small, sizes, 1
    )
    moved, smalls, spread = update_call(
        (new_gate, new_conv_a, new_conv_b, new_out), new_small, old.reshape(D, 256), sizes, 2
    )
    smalls = smalls.reshape(-1)
    grad_small = smalls[HEADS * D : HEADS * D + SMALL]
    new_step = smalls[: HEADS * D].reshape(D // 128, HEADS, 128).transpose(1, 0, 2)
    first_row = (lax.axis_index("dp") * sizes[1] + lax.axis_index("fsdp")) * own
    step_rows = lax.dynamic_slice_in_dim(new_step.reshape(HEADS, D), first_row, own, 1).T
    grad_in, grad_out, new_moment_in, new_moment_out, new_weight_in, new_weight_out = finish_call(
        moved, spread, step_rows, weight_in, weight_out, moment_in, moment_out
    )
    new_moment_small = MOMENTUM * moment_small + grad_small
    new_small_params = small_params - SMALL_RATE * new_moment_small
    return (
        output[None],
        dx[None],
        grad_in,
        grad_out,
        grad_small,
        new_moment_in,
        new_moment_out,
        new_moment_small,
        new_weight_in,
        new_weight_out,
        new_small_params,
    )


def solution(mesh):
    return jax.shard_map(
        shards,
        mesh=mesh,
        in_specs=(
            P(("dp", "fsdp"), None, None),
            P(("dp", "fsdp"), None, None),
            P(("dp", "fsdp"), None),
            P(("dp", "fsdp"), None),
            P(),
            P(("dp", "fsdp"), None),
            P(("dp", "fsdp"), None),
            P(),
        ),
        out_specs=(
            P(("dp", "fsdp"), None, None),
            P(("dp", "fsdp"), None, None),
            P(("dp", "fsdp"), None),
            P(("dp", "fsdp"), None),
            P(),
            P(("dp", "fsdp"), None),
            P(("dp", "fsdp"), None),
            P(),
            P(("dp", "fsdp"), None),
            P(("dp", "fsdp"), None),
            P(),
        ),
        check_vma=False,
    )
```

```python
import functools
import math

import jax
import jax.numpy as jnp
from jax import lax
from jax.experimental import pallas as pl
from jax.experimental.pallas import tpu as pltpu
from jax.sharding import PartitionSpec as P

D = 768
HEADS = 24
HEAD_DIM = 64
NSTATE = 128
KCONV = 4
LEN = 1024
ITERS = 5
INNER = 1536
CONVCH = 1792
IN_W = 3352
SMALL = 11336
WIDE = INNER + CONVCH
TAIL_SUMS = 1664 - 2 * HEADS
STEP = 32
CONV_A = 768
HALF = 2560
OUT_AT = WIDE - HALF
STEP_AT = OUT_AT + INNER

MOMENTUM = 0.95
MATRIX_RATE = 0.15
WEIGHT_DECAY = 0.1
SMALL_RATE = 0.01
EPSILON = 1e-05
COEF_A = 3.4445
COEF_B = -4.775
COEF_C = 2.0315

F32 = jnp.float32
BF16 = jnp.bfloat16
CHUNK = 128
STRIP = 256
PER = STRIP // CHUNK
STRIPS = LEN // STRIP
GRAD_TILE = 256
GROUP = 4


def dot(a, b):
    return lax.dot_general(a, b, (((1,), (0,)), ((), ())), preferred_element_type=F32)


def dot_nt(a, b):
    return lax.dot_general(a, b, (((1,), (1,)), ((), ())), preferred_element_type=F32)


def dot_tn(a, b):
    return lax.dot_general(a, b, (((0,), (0,)), ((), ())), preferred_element_type=F32)


def split(v):
    high = v.astype(BF16)
    return high, (v - high.astype(F32)).astype(BF16)


def beside(*parts):
    return jnp.concatenate(parts, axis=1)


def above(*parts):
    return jnp.concatenate(parts, axis=0)


def right_pair(b):
    high, low = split(b)
    return above(beside(high, low), beside(high, jnp.zeros_like(low)))


def three_pass(a, pair):
    high, low = split(a)
    both = dot(beside(high, low), pair)
    half = both.shape[1] // 2
    return both[:, :half] + both[:, half:]


def exact_sum(a, ones):
    high = a.astype(BF16)
    rest = a - high.astype(F32)
    mid = rest.astype(BF16)
    low = (rest - mid.astype(F32)).astype(BF16)
    return dot(beside(high, mid, low), above(ones, ones, ones))


def lane_sums(a):
    high = a.astype(BF16)
    rest = a - high.astype(F32)
    mid = rest.astype(BF16)
    low = (rest - mid.astype(F32)).astype(BF16)
    parts = beside(high, mid, low)
    return dot_nt(jnp.ones((8, parts.shape[1]), BF16), parts)


def stack_left(a):
    high, low = split(a)
    return above(beside(high, high), beside(low, jnp.zeros_like(low)))


def fold(rows):
    total = rows[0:8]
    for i in range(1, rows.shape[0] // 8):
        total = total + rows[8 * i : 8 * i + 8]
    return total


def row_sum(rows):
    return jnp.sum(fold(rows), axis=0, keepdims=True)


def upper():
    row = lax.broadcasted_iota(jnp.int32, (CHUNK, CHUNK), 0)
    col = lax.broadcasted_iota(jnp.int32, (CHUNK, CHUNK), 1)
    return col >= row


def softplus(v):
    return jnp.maximum(v, 0.0) + jnp.log1p(jnp.exp(-jnp.abs(v)))


def rates_of(raw, heads_ref, ones):
    steps = softplus(raw + heads_ref[0])
    logs = exact_sum(steps * heads_ref[1], ones)
    last = jnp.broadcast_to(logs[:, CHUNK - 1 : CHUNK], logs.shape)
    columns = above(logs, jnp.zeros((CHUNK - HEADS, CHUNK), F32)).T
    return steps, logs, columns, jnp.exp(logs), jnp.exp(last - logs), jnp.exp(last)


def silu(v):
    return v * jax.nn.sigmoid(v)


def wide(v):
    return beside(*([v] * PER))


def strip_at(s):
    return pl.ds(pl.multiple_of(s * STRIP, STRIP), STRIP)


def half_rows(rows, c):
    return pl.ds(pl.multiple_of(c * (rows // 2), rows // 2), rows // 2)


class Box:
    def __init__(self, box, dst, sems, partner):
        self.box, self.dst, self.sems, self.partner = box, dst, sems, partner

    def copy(self, s):
        sem = self.sems.at[s]
        return remote(
            self.box.at[lax.rem(s, 2)], self.dst(s), sem.at[0], sem.at[1], self.partner
        )

    def fill(self, s, value, back=False):
        @pl.when(pl.program_id(0) > 1)
        def _():
            self.copy(s + 2 if back else s - 2).wait_send()

        self.box[lax.rem(s, 2)] = value
        self.copy(s).start()

    def finish(self, back=False):
        for s in range(2):
            self.copy(s if back else STRIPS - 1 - s).wait_send()
        for s in range(STRIPS):
            self.copy(s).wait_recv()


def forward_kernel(
    sizes, x_ref, back_ref, first_ref, second_ref, gain_ref, taps_ref, heads_ref, inner_ref,
    blocks_ref, whole_back_ref,
    out_ref, hb_ref, cin_ref, c_ref, raw_ref, s_ref, own_normed_ref,
    dy_ref, dgate_ref, own_dgate_ref, dlogs_ref, tail_sums_ref, moved_ref,
    peer_normed_ref, peer_dgate_ref, peer_hb_ref, peer_back_ref,
    act, z, mixed, dnormed, state, tail, turned, dskip, dinner, normed_ref,
    box_normed, box_dgate, box_hb, box_sems, back_sems, *work,
):
    p = Place(sizes)
    swap = Swap(p, blocks_ref, moved_ref, *work)
    partner = p.at(c=1 - p.c)
    strip = pl.program_id(0)
    back_copy = remote(
        whole_back_ref, peer_back_ref, back_sems.at[0], back_sems.at[1], partner
    )
    boxes = [
        Box(box, lambda s, ref=ref: ref.at[:, strip_at(s)], box_sems.at[k], partner)
        for k, (box, ref) in enumerate(
            [(box_normed, peer_normed_ref), (box_dgate, peer_dgate_ref)]
        )
    ]
    boxes.append(Box(box_hb, lambda s: peer_hb_ref.at[strip_at(s)], box_sems.at[2], partner))

    @pl.when(strip == 0)
    def _():
        greet_all(p)
        back_copy.start()
        swap.start()
        state[...] = jnp.zeros_like(state)
        tail[...] = jnp.zeros_like(tail)
        dskip[...] = jnp.zeros_like(dskip)
        dinner[...] = jnp.zeros_like(dinner)
        for i in range(HALF // 256):
            part = slice(256 * i, 256 * i + 256)
            turned[0, part] = first_ref[:, part].T
            turned[1, part] = second_ref[:, part].T

    x = x_ref[...].astype(F32)
    scaled = x * lax.rsqrt(jnp.mean(x * x, axis=-1, keepdims=True) + EPSILON) * gain_ref[...]
    hb = scaled.astype(BF16)
    hb_ref[...] = hb
    boxes[2].fill(strip, hb)
    back = back_ref[...]
    raw_ref[...] = dot_nt(turned[1, STEP_AT : STEP_AT + STEP], hb)

    lane = lax.broadcasted_iota(jnp.int32, (64, CHUNK), 1)

    def later(cols, steps, before):
        turned_cols = [before] + [pltpu.roll(col, steps, 1) for col in cols]
        pairs = zip(turned_cols[:-1], turned_cols[1:])
        return [jnp.where(lane < steps, a, b) for a, b in pairs], turned_cols[-1]

    def conv_tile(i):
        rows = slice(64 * i, 64 * i + 64)
        cur = cin_ref[rows]
        cols = [cur[:, CHUNK * j : CHUNK * j + CHUNK] for j in range(PER)]
        taps = [taps_ref[k, rows] for k in range(KCONV + 1)]
        ones_late, tail[0, rows] = later(cols, 1, tail[0, rows])
        early = [taps[1] * a + taps[0] * b for a, b in zip(cols, ones_late)]
        twos_late, tail[1, rows] = later(early, 2, tail[1, rows])
        total = beside(*[
            taps[4] + c + taps[2] * b + taps[3] * a for a, b, c in zip(cols, ones_late, twos_late)
        ])
        c_ref[rows] = total
        act[rows] = total * jax.nn.sigmoid(total)

    def project(i):
        start = INNER + 256 * i
        rows = turned[start // HALF, start % HALF : start % HALF + 256]
        cin_ref[256 * i : 256 * i + 256] = dot_nt(rows, hb)

    project(0)
    for i in range(CONVCH // 256):
        if i + 1 < CONVCH // 256:
            project(i + 1)
        if i < INNER // 256:
            part = slice(256 * i, 256 * i + 256)
            z[part] = dot_nt(turned[0, part], hb)
            dnormed[part] = dot_nt(turned[1, OUT_AT + 256 * i : OUT_AT + 256 * i + 256], back)
        for q in range(4):
            conv_tile(4 * i + q)
    causal = upper()
    ones = causal.astype(F32).astype(BF16)

    def chunk(j, carry):
        cols = pl.ds(pl.multiple_of(j * CHUNK, CHUNK), CHUNK)
        steps, logs, columns, grown, to_end, through = rates_of(
            raw_ref[0:HEADS, cols], heads_ref, ones
        )
        in_map = act[INNER : INNER + NSTATE, cols].T
        in_pair = right_pair(in_map)
        out_pair = right_pair(act[INNER + NSTATE :, cols])
        scores = three_pass(in_map, out_pair)
        for g in range(HEADS // GROUP):
            rows = slice(g * GROUP * HEAD_DIM, (g + 1) * GROUP * HEAD_DIM)
            held = state[rows]
            s_ref[j, rows] = held
            across = three_pass(held, out_pair)
            ending, kept = [], []
            for q in range(GROUP):
                h = g * GROUP + q
                mine = slice(h * HEAD_DIM, (h + 1) * HEAD_DIM)
                values = act[mine, cols]
                fed = values * steps[h : h + 1]
                gaps = logs[h : h + 1] - jnp.broadcast_to(columns[:, h : h + 1], (CHUNK, CHUNK))
                weights = scores * jnp.where(causal, jnp.exp(gaps), 0.0)
                both = dot(stack_left(fed), above(*split(weights)))
                y = both[:HEAD_DIM] + both[HEAD_DIM:]
                y = y + across[q * HEAD_DIM : (q + 1) * HEAD_DIM] * grown[h : h + 1]
                mixed[mine, cols] = y + heads_ref[2][h : h + 1] * values
                ending.append(fed * to_end[h : h + 1])
                kept.append(jnp.broadcast_to(through[h : h + 1], (HEAD_DIM, CHUNK)))
            state[rows] = held * above(*kept) + three_pass(above(*ending), in_pair)
        return carry

    lax.fori_loop(0, PER, chunk, 0)

    def mean_tile(h, totals):
        rows = pl.ds(pl.multiple_of(h * HEAD_DIM, HEAD_DIM), HEAD_DIM)
        gate = z[rows, :]
        opened = mixed[rows, :] * (gate * jax.nn.sigmoid(gate))
        gained = dnormed[rows, :] * wide(inner_ref[rows, :]) * opened
        return totals[0] + fold(opened * opened), totals[1] + fold(gained)

    nothing = jnp.zeros((8, STRIP), F32)
    squares, gains = lax.fori_loop(0, HEADS, mean_tile, (nothing, nothing))
    mean = jnp.sum(squares, axis=0, keepdims=True) * (1.0 / INNER)
    r = lax.rsqrt(mean + EPSILON)
    pulled = jnp.sum(gains, axis=0, keepdims=True) * (1.0 / INNER) * (r * r * r)

    def gate_tile(h, carry):
        rows = pl.ds(pl.multiple_of(h * HEAD_DIM, HEAD_DIM), HEAD_DIM)
        gate = z[rows, :]
        skip = wide(heads_ref[2, pl.ds(h, 1), :])
        mix = mixed[rows, :]
        sig = jax.nn.sigmoid(gate)
        sil = gate * sig
        opened = mix * sil
        normed = opened * r
        inner = wide(inner_ref[rows, :])
        normed_ref[rows, :] = (normed * inner).astype(BF16)
        dn = dnormed[rows, :]
        gained = dn * normed
        dinner[rows, :] += gained[:, :CHUNK] + gained[:, CHUNK:]
        dopened = dn * inner * r - opened * pulled
        dmixed = dopened * sil
        dy_ref[rows, :] = dmixed
        dgate_ref[rows, :] = (dopened * mix * (sig * (1.0 + gate * (1.0 - sig)))).astype(BF16)
        skipped = row_sum(dmixed * act[rows, :])
        dskip[pl.ds(h, 1), :] += skipped[:, :CHUNK] + skipped[:, CHUNK:]
        dlogs_ref[pl.ds(h, 1), :] = row_sum(dmixed * mix) - skip * skipped
        return carry

    lax.fori_loop(0, HEADS, gate_tile, 0)
    for box, own, ref in (
        (boxes[0], own_normed_ref, normed_ref), (boxes[1], own_dgate_ref, dgate_ref),
    ):
        own[...] = ref[half_rows(INNER, p.c), :]
        box.fill(strip, ref[half_rows(INNER, 1 - p.c), :])
    for i in range(D // 256):
        part = slice(256 * i, 256 * i + 256)
        branch = dot(second_ref[part, OUT_AT:STEP_AT], normed_ref[...]).T
        out_ref[:, part] = (x_ref[:, part].astype(F32) + branch).astype(BF16)

    @pl.when(pl.program_id(0) == STRIPS - 1)
    def _():
        tail_sums_ref[...] = beside(
            lane_sums(dskip[...]), lane_sums(dinner[...]),
            jnp.zeros((8, tail_sums_ref.shape[1] - HEADS - INNER), F32),
        )
        swap.wait()
        back_copy.wait()
        for box in boxes:
            box.finish()


def backward_kernel(
    sizes, x_ref, back_ref, w_in_ref, step_in_ref, gain_ref, taps_ref, heads_ref,
    cin_ref, c_ref, raw_ref, s_ref, dy, dgate_ref, dlogs, tail_sums_ref, out_part, gate_part,
    dx_ref, own_a_ref, own_b_ref, flat_ref, out_column, gate_column, peer_a_ref, peer_b_ref,
    dconv_a_ref, dconv_b_ref, box_a, box_b, box_sems, dact, dstate, flow, tail, meets, vdu_rows, dstep_ref, dstep_sum, dgain, dtaps_ref, dheads_ref,
    dscaled_turned, *work,
):
    step_now = pl.program_id(0)
    p = Place(sizes)
    partner = p.at(c=1 - p.c)
    strip = STRIPS - 1 - step_now
    boxes = [
        Box(box, lambda s, ref=ref: ref.at[:, strip_at(s)], box_sems.at[k], partner)
        for k, (box, ref) in enumerate([(box_a, peer_a_ref), (box_b, peer_b_ref)])
    ]
    sums = [
        PlaneSum(p, part, work[7 * k : 7 * k + 7]) for k, part in enumerate((out_part, gate_part))
    ]

    @pl.when(step_now == 0)
    def _():
        greet_near(p, False)
        for part in sums:
            part.begin()
        sums[0].start()

    @pl.when(step_now == 3)
    def _():
        sums[1].plane.finish(0)
        sums[1].plane.start(1)

    @pl.when(step_now == 0)
    def _():
        dstate[...] = jnp.zeros_like(dstate)
        flow[...] = jnp.zeros_like(flow)
        tail[...] = jnp.zeros_like(tail)
        dgain[...] = jnp.zeros_like(dgain)
        dstep_sum[...] = jnp.zeros_like(dstep_sum)
        dtaps_ref[...] = jnp.zeros_like(dtaps_ref)
        dheads_ref[...] = jnp.zeros_like(dheads_ref)

    back = back_ref[...]

    causal = upper()
    ones = causal.astype(F32).astype(BF16)
    row = lax.broadcasted_iota(jnp.int32, (CHUNK, CHUNK), 0)
    col = lax.broadcasted_iota(jnp.int32, (CHUNK, CHUNK), 1)
    ones_back = (row >= col).astype(F32).astype(BF16)

    def chunk(step, carry):
        j = PER - 1 - step
        cols = pl.ds(pl.multiple_of(j * CHUNK, CHUNK), CHUNK)
        raw = raw_ref[0:HEADS, cols]
        steps, logs, columns, grown, to_end, through = rates_of(raw, heads_ref, ones)
        in_turned = silu(c_ref[INNER : INNER + NSTATE, cols])
        out_turned = silu(c_ref[INNER + NSTATE :, cols])
        in_map = in_turned.T
        out_map = out_turned.T
        scores = three_pass(in_map, right_pair(out_turned))
        in_pair = right_pair(in_turned)
        out_pair = right_pair(out_map)
        dscores = jnp.zeros((CHUNK, CHUNK), F32)
        din = jnp.zeros((NSTATE, CHUNK), F32)
        dout = jnp.zeros((NSTATE, CHUNK), F32)
        for g in range(HEADS // GROUP):
            rows = slice(g * GROUP * HEAD_DIM, (g + 1) * GROUP * HEAD_DIM)
            leaving = dstate[rows]
            entering = s_ref[j, rows]
            from_state = three_pass(leaving, in_pair)
            ending, growing, kept = [], [], []
            for q in range(GROUP):
                h = g * GROUP + q
                mine = slice(h * HEAD_DIM, (h + 1) * HEAD_DIM)
                values = silu(c_ref[mine, cols])
                fed = values * steps[h : h + 1]
                dys = dy[mine, cols]
                gaps = logs[h : h + 1] - jnp.broadcast_to(columns[:, h : h + 1], (CHUNK, CHUNK))
                decay = jnp.where(causal, jnp.exp(gaps), 0.0)
                weights = scores * decay
                both = dot_nt(stack_left(dys), beside(*split(weights)))
                du = both[:HEAD_DIM] + both[HEAD_DIM:]
                du = du + from_state[q * HEAD_DIM : (q + 1) * HEAD_DIM] * to_end[h : h + 1]
                fed_high, fed_low = split(fed)
                dy_high, dy_low = split(dys)
                dweights = dot_tn(
                    above(fed_high, fed_low, fed_high), above(dy_high, dy_high, dy_low)
                )
                dscores = dscores + dweights * decay
                vdu_rows[h : h + 1, :] = row_sum(values * du)
                dact[mine, cols] = du * steps[h : h + 1] + heads_ref[2][h : h + 1] * dys
                ending.append(fed * to_end[h : h + 1])
                growing.append(dys * grown[h : h + 1])
                kept.append(jnp.broadcast_to(through[h : h + 1], (HEAD_DIM, CHUNK)))
            ending = above(*ending)
            growing = above(*growing)
            end_high, end_low = split(ending)
            grow_high, grow_low = split(growing)
            leave_high, leave_low = split(leaving)
            enter_high, enter_low = split(entering)
            din = din + dot_tn(
                above(leave_high, leave_low, leave_high), above(end_high, end_high, end_low)
            )
            dout = dout + dot_tn(
                above(enter_high, enter_low, enter_high), above(grow_high, grow_high, grow_low)
            )
            arrived = leaving * above(*kept) + three_pass(growing, out_pair)
            dstate[rows] = arrived
            meet = arrived * entering
            for q in range(GROUP):
                h = g * GROUP + q
                meets[h : h + 1, :] = row_sum(meet[q * HEAD_DIM : (q + 1) * HEAD_DIM])
        vdu = vdu_rows[...]
        dlog = dlogs[:, cols] - steps * vdu
        drate = exact_sum(dlog, ones_back) + flow[...]
        flow[...] = jnp.broadcast_to(
            jnp.sum(meets[...], axis=1, keepdims=True), (HEADS, CHUNK)
        )
        dsteps = vdu + heads_ref[1] * drate
        draw = dsteps * jax.nn.sigmoid(raw + heads_ref[0])
        dheads_ref[0] += draw
        dheads_ref[1] += drate * steps * heads_ref[1]
        dstep_ref[:, cols] = above(draw, jnp.zeros((STEP - HEADS, CHUNK), F32)).astype(BF16)
        score_high, score_low = split(dscores)
        both = dot_nt(stack_left(out_turned), beside(score_high, score_low))
        dact[INNER : INNER + NSTATE, cols] = din + both[:NSTATE] + both[NSTATE:]
        both = dot(stack_left(in_turned), above(score_high, score_low))
        dact[INNER + NSTATE :, cols] = dout + both[:NSTATE] + both[NSTATE:]
        return carry

    lax.fori_loop(0, PER, chunk, 0)

    @pl.when(step_now == 0)
    def _():
        sums[1].start()

    @pl.when(step_now == 2)
    def _():
        sums[0].plane.finish(0)
        sums[0].plane.start(1)

    lane = lax.broadcasted_iota(jnp.int32, (64, CHUNK), 1)

    def conv_tile(target, start, i):
        rows = slice(start + 64 * i, start + 64 * i + 64)
        c = c_ref[rows]
        sig = jax.nn.sigmoid(c)
        dpre = dact[rows] * (sig * (1.0 + c * (1.0 - sig)))
        cin = cin_ref[rows]
        cols = [dpre[:, CHUNK * j : CHUNK * j + CHUNK] for j in range(PER)]
        dcin = dpre * wide(taps_ref[KCONV - 1, rows])
        grad = cin * dpre
        dtaps_ref[KCONV - 1, rows] += grad[:, :CHUNK] + grad[:, CHUNK:]
        dtaps_ref[KCONV, rows] += dpre[:, :CHUNK] + dpre[:, CHUNK:]
        for k in range(KCONV - 1):
            ahead = KCONV - 1 - k
            turned = [pltpu.roll(col, CHUNK - ahead, 1) for col in cols] + [tail[k, rows]]
            tail[k, rows] = turned[0]
            pairs = zip(turned[:-1], turned[1:])
            shifted = beside(*[jnp.where(lane < CHUNK - ahead, a, b) for a, b in pairs])
            dcin = dcin + shifted * wide(taps_ref[k, rows])
            grad = cin * shifted
            dtaps_ref[k, rows] += grad[:, :CHUNK] + grad[:, CHUNK:]
        target[64 * i : 64 * i + 64] = dcin.astype(BF16)

    thirds = [slice(256 * i, 256 * i + 256) for i in range(D // 256)]
    conv_at = INNER + CONV_A
    tiles = CONV_A // 64
    for i in range(tiles):
        conv_tile(dconv_a_ref, 0, i)
        if i % 4 == 0:
            part = thirds[i // 4]
            dscaled_turned[part] = dot(w_in_ref[part, :INNER], dgate_ref[...])
    for i in range((CONVCH - CONV_A) // 64):
        conv_tile(dconv_b_ref, CONV_A, i)
        if i % 4 == 0 and i // 4 < len(thirds):
            part = thirds[i // 4]
            dscaled_turned[part] += dot(w_in_ref[part, INNER:conv_at], dconv_a_ref[...])
    for box, own, ref in (
        (boxes[0], own_a_ref, dconv_a_ref), (boxes[1], own_b_ref, dconv_b_ref),
    ):
        own[...] = ref[half_rows(ref.shape[0], p.c), :]
        box.fill(strip, ref[half_rows(ref.shape[0], 1 - p.c), :], True)
    x = x_ref[...].astype(F32)
    r = lax.rsqrt(jnp.mean(x * x, axis=-1, keepdims=True) + EPSILON)
    parts = []
    for part in thirds:
        total = dscaled_turned[part] + dot(w_in_ref[part, conv_at:], dconv_b_ref[...])
        parts.append((total + dot(step_in_ref[part, :STEP], dstep_ref[...])).T)
    dscaled = beside(*parts)
    plain = x * r
    dgain[...] += fold(dscaled * plain)
    dstep_sum[...] += dot(dstep_ref[...], (plain * gain_ref[...]).astype(BF16))
    gained = dscaled * gain_ref[...]
    inner = jnp.mean(gained * plain, axis=-1, keepdims=True)
    dx_ref[...] = back.astype(F32) + (gained - plain * inner) * r

    @pl.when(step_now == STRIPS - 1)
    def _():
        for part, column in zip(sums, (out_column, gate_column)):
            part.plane.finish(1)
            column[...] = part.column()
        for box in boxes:
            box.finish(True)
        store_flat(flat_ref, dstep_sum, dgain, dtaps_ref, dheads_ref, tail_sums_ref)


def store_flat(flat_ref, dstep_sum, dgain, dtaps, dheads, tail_sums_ref):
    flat_ref[...] = jnp.zeros_like(flat_ref)
    for j in range(D // 128):
        flat_ref[HEADS * j : HEADS * j + HEADS] = dstep_sum[:HEADS, 128 * j : 128 * j + 128]
    last = beside(
        lane_sums(dheads[0])[:1], lane_sums(dheads[1])[:1], tail_sums_ref[:1],
    )
    rows = [jnp.sum(dgain[...], axis=0, keepdims=True)]
    rows += [lane_sums(dtaps[k])[:1] for k in range(KCONV + 1)]
    at = HEADS * (D // 128)
    for row in rows + [last]:
        for j in range(row.shape[1] // 128):
            flat_ref[at + j : at + j + 1] = row[:, 128 * j : 128 * j + 128]
        at += row.shape[1] // 128


def whole(shape):
    return pl.BlockSpec(shape, lambda i: (0,) * len(shape), pipeline_mode=pl.Buffered(1))


def strip_rows(width):
    return pl.BlockSpec((STRIP, width), lambda i: (i, 0))


def strip_cols(height):
    return pl.BlockSpec((height, STRIP), lambda i: (0, i))


def shape(*dims, dtype=F32):
    return jax.ShapeDtypeStruct(dims, dtype)


def columns(width, at):
    return pl.BlockSpec((D, width), lambda i: (0, at), pipeline_mode=pl.Buffered(1))


def forward_call(x, back, weights, gain, taps, heads, inner, blocks, sizes, collective_id):
    count = sizes[0] * sizes[1]
    dma = pltpu.SemaphoreType.DMA
    hbm = pl.BlockSpec(memory_space=pl.ANY)
    return pl.pallas_call(
        functools.partial(forward_kernel, sizes),
        grid=(STRIPS,),
        in_specs=[
            strip_rows(D), strip_rows(D), columns(HALF, 0), columns(HALF, 1), whole((1, D)),
            whole((KCONV + 1, CONVCH, CHUNK)), whole((3, HEADS, CHUNK)), whole((INNER, CHUNK)),
            hbm, hbm,
        ],
        out_specs=[
            strip_rows(D), strip_rows(D), strip_cols(CONVCH), strip_cols(CONVCH),
            strip_cols(STEP), pl.BlockSpec((PER, INNER, NSTATE), lambda i: (i, 0, 0)),
            strip_cols(INNER // 2), strip_cols(INNER), strip_cols(INNER), strip_cols(INNER // 2),
            strip_cols(HEADS), whole((8, TAIL_SUMS)), hbm, hbm, hbm, hbm, hbm,
        ],
        out_shape=[
            shape(LEN, D, dtype=BF16), shape(LEN, D, dtype=BF16), shape(CONVCH, LEN),
            shape(CONVCH, LEN), shape(STEP, LEN), shape(LEN // CHUNK, INNER, NSTATE),
            shape(INNER // 2, LEN, dtype=BF16), shape(INNER, LEN), shape(INNER, LEN, dtype=BF16),
            shape(INNER // 2, LEN, dtype=BF16), shape(HEADS, LEN), shape(8, TAIL_SUMS),
            shape(*blocks.shape), shape(INNER // 2, LEN, dtype=BF16),
            shape(INNER // 2, LEN, dtype=BF16), shape(LEN, D, dtype=BF16),
            shape(LEN, D, dtype=BF16),
        ],
        scratch_shapes=[
            pltpu.VMEM((CONVCH, STRIP), F32), pltpu.VMEM((INNER, STRIP), F32),
            pltpu.VMEM((INNER, STRIP), F32), pltpu.VMEM((INNER, STRIP), F32),
            pltpu.VMEM((INNER, NSTATE), F32), pltpu.VMEM((2, CONVCH, CHUNK), F32),
            pltpu.VMEM((2, HALF, D), BF16), pltpu.VMEM((HEADS, CHUNK), F32),
            pltpu.VMEM((INNER, CHUNK), F32), pltpu.VMEM((INNER, STRIP), BF16),
            pltpu.VMEM((2, INNER // 2, STRIP), BF16), pltpu.VMEM((2, INNER // 2, STRIP), BF16),
            pltpu.VMEM((2, STRIP, D), BF16), dma((3, STRIPS, 2)), dma((2,)),
            dma((count,)), dma((count,)), dma,
        ],
        compiler_params=pltpu.CompilerParams(
            vmem_limit_bytes=60 * 2**20, collective_id=collective_id, has_side_effects=True
        ),
        name="mixer_forward",
    )(x, back, weights, weights, gain, taps, heads, inner, blocks, back)


def backward_call(x, back, weights, gain, taps, heads, kept, tail_sums, parts, sizes,
                  collective_id):
    last = STRIPS - 1

    def rows(width):
        return pl.BlockSpec((STRIP, width), lambda i: (last - i, 0))

    def cols(height):
        return pl.BlockSpec((height, STRIP), lambda i: (0, last - i))

    Z = sizes[0]
    lines = flat_lines(sizes[0] * sizes[1])
    size = (parts[0].shape[1], D)
    dma = pltpu.SemaphoreType.DMA
    hbm = pl.BlockSpec(memory_space=pl.ANY)
    return pl.pallas_call(
        functools.partial(backward_kernel, sizes),
        grid=(STRIPS,),
        in_specs=[
            rows(D), rows(D), columns(WIDE, 0),
            columns(256, (HALF + STEP_AT) // 256), whole((1, D)),
            whole((KCONV, CONVCH, CHUNK)), whole((3, HEADS, CHUNK)), cols(CONVCH),
            cols(CONVCH), cols(STEP),
            pl.BlockSpec((PER, INNER, NSTATE), lambda i: (last - i, 0, 0)), cols(INNER),
            cols(INNER), cols(HEADS), whole((8, TAIL_SUMS)), hbm, hbm,
        ],
        out_specs=[
            rows(D), cols(CONV_A // 2), cols((CONVCH - CONV_A) // 2), whole((lines, 128)),
            whole((Z,) + size), whole((Z,) + size), hbm, hbm,
        ],
        out_shape=[
            shape(LEN, D), shape(CONV_A // 2, LEN, dtype=BF16),
            shape((CONVCH - CONV_A) // 2, LEN, dtype=BF16), shape(lines, 128),
            shape(Z, *size), shape(Z, *size), shape(CONV_A // 2, LEN, dtype=BF16),
            shape((CONVCH - CONV_A) // 2, LEN, dtype=BF16),
        ],
        scratch_shapes=[
            pltpu.VMEM((CONV_A, STRIP), BF16), pltpu.VMEM((CONVCH - CONV_A, STRIP), BF16),
            pltpu.VMEM((2, CONV_A // 2, STRIP), BF16),
            pltpu.VMEM((2, (CONVCH - CONV_A) // 2, STRIP), BF16), dma((2, STRIPS, 2)),
            pltpu.VMEM((CONVCH, STRIP), F32),
            pltpu.VMEM((INNER, NSTATE), F32), pltpu.VMEM((HEADS, CHUNK), F32),
            pltpu.VMEM((KCONV - 1, CONVCH, CHUNK), F32), pltpu.VMEM((HEADS, CHUNK), F32),
            pltpu.VMEM((HEADS, CHUNK), F32), pltpu.VMEM((STEP, STRIP), BF16),
            pltpu.VMEM((STEP, D), F32), pltpu.VMEM((8, D), F32),
            pltpu.VMEM((KCONV + 1, CONVCH, CHUNK), F32), pltpu.VMEM((2, HEADS, CHUNK), F32),
            pltpu.VMEM((D, STRIP), F32),
        ]
        + 2 * (plane_scratch(sizes, size) + [dma]),
        compiler_params=pltpu.CompilerParams(
            vmem_limit_bytes=63 * 2**20, collective_id=collective_id, has_side_effects=True
        ),
        name="mixer_backward",
    )(
        x, back, weights, weights, gain, taps, heads, *kept, tail_sums,
        *(by_chip(part, sizes) for part in parts),
    )


def grads_kernel(*refs):
    ins, outs, (sides, others, results, sems, out_sems) = refs[:8], refs[8:10], refs[10:]
    copies = []
    for k in range(4):
        copies.append([
            pltpu.make_async_copy(ins[2 * k], sides.at[k], sems.at[2 * k]),
            pltpu.make_async_copy(ins[2 * k + 1], others.at[k], sems.at[2 * k + 1]),
        ])
        for copy in copies[k]:
            copy.start()
    stores = []
    for k in range(2):
        for half in (0, 1):
            for copy in copies[2 * k + half]:
                copy.wait()
            side, other = sides.at[2 * k + half], others.at[2 * k + half]

            def tile(i, carry, k=k, half=half, side=side, other=other):
                rows = pl.ds(pl.multiple_of(i * GRAD_TILE, GRAD_TILE), GRAD_TILE)
                part = dot(side[rows, :], other[...])
                results[k, rows, :] = part if half == 0 else results[k, rows, :] + part
                return carry

            lax.fori_loop(0, INNER // 2 // GRAD_TILE, tile, 0)
        stores.append(pltpu.make_async_copy(results.at[k], outs[k], out_sems.at[k]))
        stores[k].start()
    for store in stores:
        store.wait()


def grads_call(own_normed, peer_normed, own_dgate, peer_dgate, backs, hbs):
    rows = INNER // 2
    hbm = pl.BlockSpec(memory_space=pl.ANY)
    return pl.pallas_call(
        grads_kernel,
        in_specs=[hbm] * 8,
        out_specs=[hbm] * 2,
        out_shape=[shape(rows, D)] * 2,
        scratch_shapes=[
            pltpu.VMEM((4, rows, LEN), BF16), pltpu.VMEM((4, LEN, D), BF16),
            pltpu.VMEM((2, rows, D), F32), pltpu.SemaphoreType.DMA((8,)),
            pltpu.SemaphoreType.DMA((2,)),
        ],
        compiler_params=pltpu.CompilerParams(vmem_limit_bytes=60 * 2**20),
        name="grads",
    )(own_normed, backs[0], peer_normed, backs[1], own_dgate, hbs[0], peer_dgate, hbs[1])


def flat_lines(count):
    return -(-(HEADS * D + SMALL) // (1024 * count)) * 8 * count


def block_and_gradients(x, back, weights, vectors, blocks, sizes, collective_ids):
    count = sizes[0] * sizes[1]
    gain, taps, heads, inner = vectors
    (
        out, hb, cin, c, raw, states, own_normed, dy, dgate, own_dgate, dlogs, tail_sums, moved,
        peer_normed, peer_dgate, peer_hb, peer_back,
    ) = forward_call(
        x, back, weights, gain, taps, heads, inner, blocks, sizes, collective_ids[0]
    )
    parts = grads_call(
        own_normed, peer_normed, own_dgate, peer_dgate, (back, peer_back), (hb, peer_hb)
    )
    parts = [part.reshape(count // 2, -1, D) for part in parts]
    dx, own_a, own_b, flat, out_column, gate_column, peer_a, peer_b = backward_call(
        x, back, weights, gain, taps, heads, (cin, c, raw, states, dy, dgate, dlogs), tail_sums,
        parts, sizes, collective_ids[1],
    )
    factors = (own_a, peer_a, own_b, peer_b, hb, peer_hb)
    return out, dx, [out_column, gate_column], factors, flat.reshape(count, -1, 128), moved


MESH = pl.DeviceIdType.MESH


class Place:
    def __init__(self, sizes):
        self.Z, self.F = sizes
        self.C, self.Y = 2, 2
        self.X = self.F // 4
        f = lax.axis_index("fsdp")
        self.z = lax.axis_index("dp")
        self.c = lax.rem(f, 2)
        self.x = lax.rem(f // 2, self.X)
        self.y = f // (2 * self.X)
        self.f = f

    def at(self, z=None, y=None, x=None, c=None):
        z = self.z if z is None else z
        y = self.y if y is None else y
        x = self.x if x is None else x
        c = self.c if c is None else c
        return (z, (y * self.X + x) * 2 + c)

    def other_x(self, step):
        return lax.rem(self.x + step, self.X)


def signal(device):
    pl.semaphore_signal(
        pltpu.get_barrier_semaphore(), inc=1, device_id=device, device_id_type=MESH
    )


def greet_all(place):
    count = place.Z * place.F
    me = place.z * place.F + place.f

    def step(i, carry):
        peer = lax.rem(me + i, count)
        signal((peer // place.F, lax.rem(peer, place.F)))
        return carry

    lax.fori_loop(1, count, step, 0)
    pl.semaphore_wait(pltpu.get_barrier_semaphore(), count - 1)


def remote(src, dst, send, recv, device):
    return pltpu.make_async_remote_copy(
        src_ref=src, dst_ref=dst, send_sem=send, recv_sem=recv, device_id=device,
        device_id_type=MESH,
    )


def add_blocks(dst, src, count):
    def step(i, carry):
        target = dst(i)
        target[...] = target[...] + src(i)[...]
        return carry

    lax.fori_loop(0, count, step, 0)


class Swap:
    def __init__(self, place, src, dst, send, recv, local, same=False, narrow=None):
        self.place, self.src, self.dst, self.same, self.narrow = place, src, dst, same, narrow
        self.send, self.recv, self.local = send, recv, local
        self.count = place.Z * place.F
        self.me = place.z * place.F + place.f

    def block(self, peer):
        return self.src if self.same else self.src.at[peer]

    def cut(self, ref, odd):
        return ref.at[:, pl.ds(0, self.narrow)] if odd else ref

    def each(self, sender, act):
        if self.narrow is None:
            act(False)
        else:
            @pl.when(lax.rem(sender, 2) == 0)
            def _():
                act(False)

            @pl.when(lax.rem(sender, 2) == 1)
            def _():
                act(True)

    def to(self, i, odd):
        peer = lax.rem(self.me + i, self.count)
        return remote(
            self.cut(self.block(peer), odd), self.cut(self.dst.at[self.me], odd),
            self.send.at[i], self.recv.at[i],
            (peer // self.place.F, lax.rem(peer, self.place.F)),
        )

    def keep(self):
        return pltpu.make_async_copy(self.block(self.me), self.dst.at[self.me], self.local)

    def start(self):
        self.keep().start()

        def step(i, carry):
            self.each(self.me, lambda odd: self.to(i, odd).start())
            return carry

        lax.fori_loop(1, self.count, step, 0)

    def wait(self):
        self.keep().wait()

        def step(i, carry):
            sender = lax.rem(self.me + self.count - i, self.count)
            self.each(self.me, lambda odd: self.to(i, odd).wait_send())
            self.each(sender, lambda odd: remote(
                self.cut(self.block(sender), odd), self.cut(self.dst.at[sender], odd),
                self.send.at[i], self.recv.at[i],
                (sender // self.place.F, lax.rem(sender, self.place.F)),
            ).wait_recv())
            return carry

        lax.fori_loop(1, self.count, step, 0)


def greet_near(place, along_z):
    signal(place.at(c=1 - place.c))
    signal(place.at(y=1 - place.y))
    for s in range(1, place.X):
        signal(place.at(x=place.other_x(s)))
    if along_z:
        for s in range(1, place.Z):
            signal(place.at(z=lax.rem(place.z + s, place.Z)))
    pl.semaphore_wait(
        pltpu.get_barrier_semaphore(), place.X + 1 + (place.Z - 1 if along_z else 0)
    )


class Plane:
    def __init__(self, place, acc, x1, y1, x2, y2, sems):
        self.p, self.acc = place, acc
        self.x1, self.y1, self.x2, self.y2, self.sems = x1, y1, x2, y2, sems
        self.h = place.Z // 2

    def copies(self, stage):
        p, acc, h = self.p, self.acc, self.h
        low, high = pl.ds(0, h), pl.ds(h, p.Z - h)
        out = []
        base = stage * p.X
        for s in range(1, p.X):
            x = p.other_x(s)
            if stage == 0:
                src, dst = acc.at[low, :, x], self.x1.at[s - 1]
            else:
                src, dst = acc.at[high, p.y, x], self.x2.at[s - 1]
            sem = self.sems.at[base + s]
            out.append(remote(src, dst, sem.at[0], sem.at[1], p.at(x=x)))
        if stage == 0:
            src, dst = acc.at[high, 1 - p.y], self.y1
        else:
            src, dst = acc.at[low, 1 - p.y, p.x], self.y2
        sem = self.sems.at[base]
        out.append(remote(src, dst, sem.at[0], sem.at[1], p.at(y=1 - p.y)))
        return out

    def start(self, stage):
        for copy in self.copies(stage):
            copy.start()

    def finish(self, stage):
        p, acc, h = self.p, self.acc, self.h
        for copy in self.copies(stage):
            copy.wait()
        for s in range(p.X - 1):
            if stage == 0:
                add_blocks(
                    lambda i: acc.at[i // p.Y, lax.rem(i, p.Y), p.x],
                    lambda i: self.x1.at[s, i // p.Y, lax.rem(i, p.Y)],
                    h * p.Y,
                )
            else:
                add_blocks(
                    lambda i: acc.at[h + i, p.y, p.x], lambda i: self.x2.at[s, i], p.Z - h
                )
        if stage == 0:
            add_blocks(
                lambda i: acc.at[h + i // p.X, p.y, lax.rem(i, p.X)],
                lambda i: self.y1.at[i // p.X, lax.rem(i, p.X)],
                (p.Z - h) * p.X,
            )
        else:
            add_blocks(lambda i: acc.at[i, p.y, p.x], lambda i: self.y2.at[i], h)


def plane_scratch(sizes, block):
    Z, X, Y = sizes[0], sizes[1] // 4, 2
    h = Z // 2
    return [
        pltpu.VMEM((Z, Y, X) + block, F32), pltpu.VMEM((X - 1, h, Y) + block, F32),
        pltpu.VMEM((Z - h, X) + block, F32), pltpu.VMEM((X - 1, Z - h) + block, F32),
        pltpu.VMEM((h,) + block, F32), pltpu.SemaphoreType.DMA((2 * X, 2)),
    ]


def by_place(blocks, sizes):
    return blocks.reshape((sizes[0], 2, sizes[1] // 4, 2) + blocks.shape[1:])


def by_chip(blocks, sizes):
    return blocks.reshape((sizes[0], 2, sizes[1] // 4) + blocks.shape[1:])


class PlaneSum:
    def __init__(self, place, part, work):
        self.p, self.part, self.acc, self.sem = place, part, work[0], work[6]
        self.plane = Plane(place, *work[:6])

    def copy(self):
        return pltpu.make_async_copy(self.part, self.acc, self.sem)

    def begin(self):
        self.copy().start()

    def start(self):
        self.copy().wait()
        self.plane.start(0)

    def block(self, z):
        return self.acc.at[z, self.p.y, self.p.x]

    def column(self):
        return self.acc[:, self.p.y, self.p.x]


class Product(PlaneSum):
    def __init__(self, place, factors, work):
        super().__init__(place, None, work)
        self.factors = factors

    def begin(self):
        pass

    def start(self):
        own, peer, right, peer_right = self.factors
        Z, Y, X, per, _ = self.acc.shape
        h = Z // 2
        size = h * Y * X * per

        def half(k, carry):
            rows = pl.ds(pl.multiple_of(k * size, size), size)
            value = dot(own[rows, :], right[...]) + dot(peer[rows, :], peer_right[...])
            for i in range(h * Y * X):
                place = (k * h + i // (Y * X), i // X % Y, i % X)
                self.acc[place] = value[per * i : per * i + per]
            return carry

        lax.fori_loop(0, Z // h, half, 0)
        self.plane.start(0)


class PairSum(PlaneSum):
    def __init__(self, place, part, work):
        super().__init__(place, part, work)
        self.core, self.sems = work[7], work[8]

    def copies(self):
        p = self.p
        return (
            remote(
                self.part.at[:, :, :, 1 - p.c], self.core, self.sems.at[0], self.sems.at[1],
                p.at(c=1 - p.c),
            ),
            pltpu.make_async_copy(self.part.at[:, :, :, p.c], self.acc, self.sem),
        )

    def begin(self):
        for copy in self.copies():
            copy.start()

    def start(self):
        p = self.p
        for copy in self.copies():
            copy.wait()

        def place_of(i):
            return i // (p.Y * p.X), lax.rem(i // p.X, p.Y), lax.rem(i, p.X)

        add_blocks(
            lambda i: self.acc.at[place_of(i)], lambda i: self.core.at[place_of(i)],
            p.Z * p.Y * p.X,
        )
        self.plane.start(0)


class Column:
    def __init__(self, part, acc, sem):
        self.copy = pltpu.make_async_copy(part, acc, sem)
        self.acc = acc

    def block(self, z):
        return self.acc.at[z]


class Chain:
    def __init__(self, place, part, held, sems):
        self.p, self.part, self.held, self.sems = place, part, held, sems

    def flow(self, t, right):
        p, side = self.p, 0 if right else 1
        sem = self.sems.at[side, t]
        target = p.at(z=p.z + 1 if right else p.z - 1)
        return remote(self.part.block(t), self.held.at[side, t], sem.at[0], sem.at[1], target)

    def send(self, t, right):
        @pl.when(self.p.z < t if right else self.p.z > t)
        def _():
            self.flow(t, right).start()

    def first(self):
        p = self.p
        for j in range(p.Z - 1):
            @pl.when(p.z == 0)
            def _():
                self.send(p.Z - 1 - j, True)

            @pl.when(p.z == p.Z - 1)
            def _():
                self.send(j, False)

    def receive(self, t, right):
        self.flow(t, right).wait_recv()
        mine = self.part.block(t)
        mine[...] = mine[...] + self.held[0 if right else 1, t]

    def forward(self, j):
        p = self.p
        for right in (True, False):
            t = p.Z - 1 - j if right else j

            @pl.when(jnp.logical_and(p.z > 0, p.z < t) if right else
                     jnp.logical_and(p.z < p.Z - 1, p.z > t))
            def _():
                self.receive(t, right)
                self.flow(t, right).start()

    def last(self):
        p = self.p

        @pl.when(p.z > 0)
        def _():
            self.receive(p.z, True)

        @pl.when(p.z < p.Z - 1)
        def _():
            self.receive(p.z, False)

    def finish(self):
        p = self.p
        for t in range(p.Z):
            for right in (True, False):
                @pl.when(p.z < t if right else p.z > t)
                def _():
                    self.flow(t, right).wait_send()


class Direct:
    def __init__(self, place, part, held, sems):
        self.p, self.part, self.held, self.sems = place, part, held, sems

    def over(self, s):
        p = self.p
        z = lax.rem(p.z + s, p.Z)
        sem = self.sems.at[s]
        return remote(self.part.block(z), self.held.at[s - 1], sem.at[0], sem.at[1], p.at(z=z))

    def start(self):
        for s in range(1, self.p.Z):
            self.over(s).start()

    def last(self):
        mine = self.part.block(self.p.z)
        total = mine[...]
        for s in range(1, self.p.Z):
            self.over(s).wait()
            total = total + self.held[s - 1]
        mine[...] = total


def scatter_kernel(sizes, *refs):
    columns_in, factors, small_in, outs, rest = (
        refs[:2], refs[2:8], refs[8], refs[9:14], list(refs[14:])
    )

    def take(n):
        taken = rest[:n]
        del rest[:n]
        return taken

    p = Place(sizes)
    columns = [Column(ref, *take(2)) for ref in columns_in]
    chains = [Chain(p, column, *take(2)) for column in columns]
    own_a, peer_a, own_b, peer_b, hb, peer_hb = factors
    queue = [
        Product(p, (own_a, peer_a, hb, peer_hb), take(7)),
        Product(p, (own_b, peer_b, hb, peer_hb), take(7)),
        PairSum(p, small_in, take(9)),
    ]
    queue = [(part, Direct(p, part, *take(2))) for part in queue]
    greet_near(p, True)
    for column in columns:
        column.copy.start()
    for part, _ in queue:
        part.begin()
    for column, chain in zip(columns, chains):
        column.copy.wait()
        chain.first()
    hops = p.Z - 2

    def forward(j):
        if j < hops:
            for chain in chains:
                chain.forward(j)

    stages = [
        lambda part, direct: part.start(),
        lambda part, direct: (part.plane.finish(0), part.plane.start(1)),
        lambda part, direct: (part.plane.finish(1), direct.start()),
    ]
    for k, stage in enumerate(stages):
        for part, direct in queue:
            stage(part, direct)
        forward(k)
    for k in range(len(stages), hops):
        forward(k)
    for chain in chains:
        chain.last()
        chain.finish()
    for _, direct in queue:
        direct.last()
    for part, out in zip(columns + [part for part, _ in queue], outs):
        out[...] = part.block(p.z)[...]


def scatter_call(columns, factors, small, sizes, collective_id):
    Z, F = sizes
    X, Y = F // 4, 2
    chips = Z * X * Y
    dma = pltpu.SemaphoreType.DMA
    parts = [(factors[0].shape[0] // chips, D), (factors[2].shape[0] // chips, D)]
    parts.append(small.shape[1:])
    scratch = []
    for column in columns:
        scratch += [pltpu.VMEM(column.shape, F32), dma]
    for column in columns:
        scratch += [pltpu.VMEM((2, Z) + column.shape[1:], F32), dma((2, Z, 2))]
    for block in parts:
        scratch += plane_scratch(sizes, block) + [dma]
    scratch += [pltpu.VMEM((Z, Y, X) + parts[2], F32), dma((2,))]
    for block in parts:
        scratch += [pltpu.VMEM((Z - 1,) + block, F32), dma((Z, 2))]
    hbm = pl.BlockSpec(memory_space=pl.ANY)
    vmem = pl.BlockSpec(memory_space=pltpu.VMEM)
    return pl.pallas_call(
        functools.partial(scatter_kernel, sizes),
        out_shape=[shape(*block) for block in [column.shape[1:] for column in columns] + parts],
        in_specs=[hbm] * 2 + [vmem] * 6 + [hbm],
        out_specs=[vmem] * 5,
        scratch_shapes=scratch,
        compiler_params=pltpu.CompilerParams(
            collective_id=collective_id, has_side_effects=True, vmem_limit_bytes=60 * 2**20
        ),
        name="scatter",
    )(*columns, *factors, by_place(small, sizes))


def gather_kernel(
    sizes, w_in_ref, w_out_ref, m_in_ref, m_out_ref, params_ref, inner_rows_ref,
    all_ref, blocks_ref, gain_ref, taps_ref, heads_ref, inner_ref,
    mine, keep_sem, z_sems, near, far, across,
):
    p = Place(sizes)
    Z, h = p.Z, p.Z // 2
    greet_near(p, True)
    own = mine.shape[0]
    partner = p.at(c=1 - p.c)
    mine[:, :WIDE] = w_in_ref[:, :WIDE].astype(BF16)
    mine[:, WIDE : WIDE + INNER] = w_out_ref[...].astype(BF16)
    mine[:, WIDE + INNER :] = jnp.concatenate(
        [w_in_ref[:, WIDE:], jnp.zeros((own, 2 * HALF - IN_W - INNER), F32)], axis=1
    ).astype(BF16)
    keep = pltpu.make_async_copy(mine, all_ref.at[p.z, p.y, p.x, p.c], keep_sem)
    keep.start()

    def spot(z, y, x):
        return all_ref.at[z, y, x, p.c]

    def copy(src, dst, sem, device):
        return remote(src, dst, sem.at[0], sem.at[1], device)

    def along_z(z, right, src=None):
        here = spot(z, p.y, p.x)
        target = p.at(z=p.z + 1 if right else p.z - 1)
        return copy(here if src is None else src, here, z_sems.at[0 if right else 1, z], target)

    def near_copies(z, src=None):
        here = spot(z, p.y, p.x)
        src = here if src is None else src
        found = [copy(src, here, near.at[z, 0], p.at(y=1 - p.y))]
        for s in range(1, p.X):
            found.append(copy(src, here, near.at[z, s], p.at(x=p.other_x(s))))
        return found

    def near_arrivals(z):
        found = [(z, 1 - p.y, p.x, near.at[z, 0])]
        for s in range(1, p.X):
            found.append((z, p.y, lax.rem(p.x + p.X - s, p.X), near.at[z, s]))
        return found

    def far_copies(z):
        low, high = [], []
        for s in range(1, p.X):
            x = p.other_x(s)
            there = spot(z, p.y, x)
            low.append(copy(there, there, far.at[z, s], p.at(y=1 - p.y)))
            there = spot(z, 1 - p.y, p.x)
            high.append(copy(there, there, far.at[z, s], p.at(x=x)))
        return low, high

    def far_arrivals(z):
        low = [(z, 1 - p.y, p.other_x(s), far.at[z, s]) for s in range(1, p.X)]
        high = [
            (z, 1 - p.y, lax.rem(p.x + p.X - s, p.X), far.at[z, s]) for s in range(1, p.X)
        ]
        return low, high

    def to_partner(z, y, x, src=None):
        here = spot(z, y, x)
        return copy(here if src is None else src, here, across.at[z, y, x], partner)

    def await_block(z, y, x, sem):
        here = spot(z, y, x)
        copy(here, here, sem, partner).wait_recv()
        to_partner(z, y, x).start()

    def start_all(copies):
        for c in copies:
            c.start()

    @pl.when(p.z < Z - 1)
    def _():
        along_z(p.z, True, mine).start()

    @pl.when(p.z > 0)
    def _():
        along_z(p.z, False, mine).start()

    start_all(near_copies(p.z, mine))
    to_partner(p.z, p.y, p.x, mine).start()
    spread_vectors(params_ref, inner_rows_ref, gain_ref, taps_ref, heads_ref, inner_ref)
    spread_moments(m_in_ref, m_out_ref, blocks_ref)

    def visit(right, z):
        await_block(z, p.y, p.x, z_sems.at[0 if right else 1, z])

        @pl.when(p.z < Z - 1 if right else p.z > 0)
        def _():
            along_z(z, right).start()

        start_all(near_copies(z))

    def by_distance(low, high):
        for j in range(1, Z):
            @pl.when(p.z - j >= 0)
            def _():
                low(p.z - j)

            @pl.when(p.z + j < Z)
            def _():
                high(p.z + j)

    by_distance(lambda z: visit(True, z), lambda z: visit(False, z))

    def relay(z):
        for block in near_arrivals(z):
            await_block(*block)
        low, high = far_copies(z)

        @pl.when(z < h)
        def _():
            start_all(low)

        @pl.when(z >= h)
        def _():
            start_all(high)

    relay(p.z)
    by_distance(relay, relay)

    def settle(z):
        low, high = far_arrivals(z)

        @pl.when(z < h)
        def _():
            for block in low:
                await_block(*block)

        @pl.when(z >= h)
        def _():
            for block in high:
                await_block(*block)

    settle(p.z)
    by_distance(settle, settle)
    keep.wait()

    def finish(z, carry):
        for c in near_copies(z):
            c.wait_send()
        low, high = far_copies(z)

        @pl.when(z < h)
        def _():
            for c in low:
                c.wait_send()

        @pl.when(z >= h)
        def _():
            for c in high:
                c.wait_send()

        @pl.when(jnp.logical_and(z <= p.z, p.z < Z - 1))
        def _():
            along_z(z, True).wait_send()

        @pl.when(jnp.logical_and(z >= p.z, p.z > 0))
        def _():
            along_z(z, False).wait_send()

        for y in range(p.Y):
            for x in range(p.X):
                to_partner(z, y, x).wait_send()
                theirs = all_ref.at[z, y, x, 1 - p.c]
                copy(theirs, theirs, across.at[z, y, x], partner).wait_recv()

        return carry

    lax.fori_loop(0, Z, finish, 0)


def column_of(row):
    return jnp.broadcast_to(row, (128, 128)).T


def spread_vectors(params_ref, inner_rows_ref, gain_ref, taps_ref, heads_ref, inner_ref):
    row = D // 128
    gain_ref[...] = beside(*[params_ref[j : j + 1] for j in range(row)])
    for k in range(KCONV + 1):
        for j in range(CONVCH // 128):
            taps_ref[k, 128 * j : 128 * j + 128] = column_of(params_ref[row : row + 1])
            row += 1
    heads = column_of(params_ref[row : row + 1])
    heads_ref[0] = heads[:HEADS]
    heads_ref[1] = -jnp.exp(heads[HEADS : 2 * HEADS])
    heads_ref[2] = heads[2 * HEADS : 3 * HEADS]
    for j in range(INNER // 128):
        inner_ref[128 * j : 128 * j + 128] = column_of(inner_rows_ref[j : j + 1])


def cuts_of(count):
    widths = [(0, INNER), (INNER, CONV_A), (INNER + CONV_A, CONVCH - CONV_A)]
    return [(start, width, width // count) for start, width in widths], INNER // count


def first_of(d, width, count):
    return d % 2 * (width // 2) + d // 2 * (width // count)


def spread_moments(m_in_ref, m_out_ref, blocks_ref):
    count, own, lanes_in_block = blocks_ref.shape
    ins, outs = cuts_of(count)
    step = m_in_ref[:, WIDE:]
    used = sum(each for _, _, each in ins) + outs + HEADS
    for d in range(count):
        pieces = []
        for start, width, each in ins:
            at = start + first_of(d, width, count)
            pieces.append(m_in_ref[:, at : at + each])
        at = first_of(d, INNER, count)
        pieces += [m_out_ref[:, at : at + outs], step]
        blocks_ref[d] = beside(*pieces, jnp.zeros((own, lanes_in_block - used), F32))


def gather_call(weight_in, weight_out, moment_in, moment_out, params, sizes, collective_id):
    Z, F = sizes
    X, Y = F // 4, 2
    own = weight_in.shape[0]
    count = Z * F
    inner_rows = params[-INNER:].reshape(-1, 128)
    params = jnp.pad(params, (0, -params.shape[0] % 128)).reshape(-1, 128)
    vmem = pl.BlockSpec(memory_space=pltpu.VMEM)
    hbm = pl.BlockSpec(memory_space=pl.ANY)
    whole_weights, blocks, *vectors = pl.pallas_call(
        functools.partial(gather_kernel, sizes),
        out_shape=[
            shape(Z, Y, X, 2, own, 2 * HALF, dtype=BF16), shape(count, own, 256), shape(1, D),
            shape(KCONV + 1, CONVCH, CHUNK), shape(3, HEADS, CHUNK), shape(INNER, CHUNK),
        ],
        in_specs=[vmem] * 6,
        out_specs=[hbm] + [vmem] * 5,
        scratch_shapes=[
            pltpu.VMEM((own, 2 * HALF), BF16), pltpu.SemaphoreType.DMA, pltpu.SemaphoreType.DMA((2, Z, 2)),
            pltpu.SemaphoreType.DMA((Z, X, 2)), pltpu.SemaphoreType.DMA((Z, X, 2)),
            pltpu.SemaphoreType.DMA((Z, Y, X, 2)),
        ],
        compiler_params=pltpu.CompilerParams(
            collective_id=collective_id, has_side_effects=True, vmem_limit_bytes=60 * 2**20
        ),
        name="weights_gather",
    )(weight_in, weight_out, moment_in, moment_out, params, inner_rows)
    return whole_weights.reshape(D, 2 * HALF), blocks, vectors


def gram_rows(slab, row):
    high, low = split(slab)
    left = above(high, low, high)[:, 128 * row : 128 * row + 128]
    return dot_tn(left, above(high, high, low)[:, 128 * row :])


def pack_gram(targets, slab):
    Z, Y, X, per, _ = targets[0].shape
    rows = above(*[
        beside(gram_rows(slab, i), gram_rows(slab, D // 128 - 1 - i)) for i in range(D // 256)
    ])
    if Z * Y * X * per > rows.shape[0]:
        rows = above(rows, jnp.zeros((Z * Y * X * per - rows.shape[0], rows.shape[1]), F32))
    at = 0
    for target in targets:
        cols = slice(at, at + target.shape[4])
        for i in range(Z * Y * X):
            target[i // (Y * X), i // X % Y, i % X] = rows[per * i : per * i + per, cols]
        at += target.shape[4]


def unpack_gram(gram, packed):
    Z, Y, X, _, _ = packed[0].shape
    rows = beside(*[
        above(*[part[i // (Y * X), i // X % Y, i % X] for i in range(Z * Y * X)])
        for part in packed
    ])
    for i in range(D // 256):
        pair = rows[128 * i : 128 * i + 128]
        wide_part, j = D - 128 * i, D // 128 - 1 - i
        for row, part in ((i, pair[:, :wide_part]), (j, pair[:, wide_part:])):
            gram[128 * row : 128 * row + 128, 128 * row :] = part
            for k in range(row + 1, D // 128):
                at = 128 * (k - row)
                gram[128 * k : 128 * k + 128, 128 * row : 128 * row + 128] = part[
                    :, at : at + 128
                ].T


BEHIND = 2


class AllSum:
    def __init__(self, place, work):
        self.p = place
        self.total, self.acc, self.core, self.core_sems = work[0], work[1], work[7], work[8]
        self.held, self.z_sems, self.back_sems = work[9:12]
        self.plane = Plane(place, *work[1:7])
        self.steps = [
            self.pair, self.second, self.cross, self.turn, self.spread, self.spread_on, self.done,
        ]

    def to_core(self):
        p = self.p
        return remote(
            self.total, self.core, self.core_sems.at[0], self.core_sems.at[1], p.at(c=1 - p.c)
        )

    def pair(self):
        p = self.p
        self.to_core().wait()

        def place_of(i):
            return i // (p.Y * p.X), lax.rem(i // p.X, p.Y), lax.rem(i, p.X)

        add_blocks(
            lambda i: self.acc.at[place_of(i)], lambda i: self.core.at[place_of(i)],
            p.Z * p.Y * p.X,
        )
        self.plane.start(0)

    def second(self):
        self.plane.finish(0)
        self.plane.start(1)

    def over(self, s):
        p = self.p
        z = lax.rem(p.z + s, p.Z)
        sem = self.z_sems.at[0, s]
        return remote(
            self.acc.at[z, p.y, p.x], self.held.at[s - 1], sem.at[0], sem.at[1], p.at(z=z)
        )

    def cross(self):
        self.plane.finish(1)
        for s in range(1, self.p.Z):
            self.over(s).start()

    def back(self, s, mine):
        p = self.p
        sem = self.z_sems.at[1, s]
        z = p.z if mine else lax.rem(p.z + p.Z - s, p.Z)
        ref = self.total.at[z, p.y, p.x]
        return remote(ref, ref, sem.at[0], sem.at[1], p.at(z=lax.rem(p.z + s, p.Z)))

    def turn(self):
        p = self.p
        for s in range(1, p.Z):
            self.over(s).wait()
        result = self.acc[p.z, p.y, p.x]
        for s in range(1, p.Z):
            result = result + self.held[s - 1]
        self.total[p.z, p.y, p.x] = result
        for s in range(1, p.Z):
            self.back(s, True).start()

    def planes(self, stage, mine):
        p, total, h = self.p, self.total, self.p.Z // 2
        low, high = pl.ds(0, h), pl.ds(h, p.Z - h)
        found = []
        for s in range(1, p.X):
            sem = self.back_sems.at[stage * p.X + s]
            x = p.x if mine else lax.rem(p.x + p.X - s, p.X)
            ref = total.at[high, p.y, x] if stage == 0 else total.at[low, :, x]
            found.append(remote(ref, ref, sem.at[0], sem.at[1], p.at(x=p.other_x(s))))
        sem = self.back_sems.at[stage * p.X]
        y = p.y if mine else 1 - p.y
        ref = total.at[low, y, p.x] if stage == 0 else total.at[high, y]
        found.append(remote(ref, ref, sem.at[0], sem.at[1], p.at(y=1 - p.y)))
        return found

    def arrive(self, copies):
        for mine, theirs in copies:
            mine.wait_send()
            theirs.wait_recv()

    def spread(self):
        self.arrive([(self.back(s, True), self.back(s, False)) for s in range(1, self.p.Z)])
        for copy in self.planes(0, True):
            copy.start()

    def spread_on(self):
        self.arrive(zip(self.planes(0, True), self.planes(0, False)))
        for copy in self.planes(1, True):
            copy.start()

    def done(self):
        self.arrive(zip(self.planes(1, True), self.planes(1, False)))


def all_sum_scratch(sizes, block):
    Z, X, Y = sizes[0], sizes[1] // 4, 2
    dma = pltpu.SemaphoreType.DMA
    return [pltpu.VMEM((Z, Y, X) + block, F32)] + plane_scratch(sizes, block) + [
        pltpu.VMEM((Z, Y, X) + block, F32), dma((2,)), pltpu.VMEM((Z - 1,) + block, F32),
        dma((2, Z, 2)), dma((2 * X, 2)),
    ]


def put_left(left, value, rows):
    high, low = split(value)
    left[rows] = beside(high, low, high)


def put_right(right, value, row):
    high, low = split(value)
    size = value.shape[0]
    right[row : row + size] = high
    right[D + row : D + row + size] = high
    right[2 * D + row : 2 * D + row + size] = low


TILE = 256


def symmetric_product(target, left, right):
    for i in range(D // TILE):
        rows = slice(TILE * i, TILE * i + TILE)
        part = dot(left[rows], right[:, TILE * i :])
        target[rows, TILE * i :] = part
        for j in range(i + 1, D // TILE):
            at = TILE * (j - i)
            target[TILE * j : TILE * j + TILE, rows] = part[:, at : at + TILE].T


def iterate(gram, square, factor, left, right, slab, slab_left):
    tiles = [slice(TILE * i, TILE * i + TILE) for i in range(D // TILE)]
    row = lax.broadcasted_iota(jnp.int32, (TILE, D), 0)
    col = lax.broadcasted_iota(jnp.int32, (TILE, D), 1)
    diagonals = [(row + TILE * i == col) for i in range(D // TILE)]
    trace = jnp.zeros((8, D), F32)
    for rows, diagonal in zip(tiles, diagonals):
        trace = trace + fold(jnp.where(diagonal, gram[rows], 0.0))
    trace = jnp.sum(jnp.sum(trace, axis=0, keepdims=True), axis=1, keepdims=True)
    scale = 1.0 / (jnp.sqrt(trace) + 1e-07)
    for rows in tiles:
        gram[rows] = gram[rows] * (scale * scale)
    slab[...] = slab[...] * scale

    def step(iteration, carry):
        for i, rows in enumerate(tiles):
            value = gram[rows]
            put_left(left, value, rows)
            put_right(right, value, TILE * i)
        symmetric_product(square, left, right)
        for i, rows in enumerate(tiles):
            value = COEF_B * gram[rows] + COEF_C * square[rows]
            put_right(right, value + jnp.where(diagonals[i], COEF_A, 0.0), TILE * i)
        put_left(slab_left, slab[...], slice(None))
        slab[...] = dot(slab_left[...], right[...])
        symmetric_product(factor, left, right)
        for rows in tiles:
            put_left(left, factor[rows], rows)
        symmetric_product(gram, left, right)
        return carry

    lax.fori_loop(0, ITERS - 1, step, 0)
    for i, rows in enumerate(tiles):
        put_right(right, gram[rows], TILE * i)
    first = slab[...]
    put_left(slab_left, first, slice(None))
    once = dot(slab_left[...], right[...])
    put_left(slab_left, once, slice(None))
    slab[...] = COEF_A * first + COEF_B * once + COEF_C * dot(slab_left[...], right[...])


def update_kernel(
    sizes, gate_ref, conv_a_ref, conv_b_ref, out_ref, small_ref, old_ref, moved_ref, smalls_ref, spread_ref,
    give, given, give_sems, messages, smalls, mats, left, right, slab, slab_left,
    swap_send, swap_recv, local, *work,
):
    p = Place(sizes)
    count = p.Z * p.F
    own = D // count
    gates = gate_ref.shape[0]
    ins = gates + conv_a_ref.shape[0] + conv_b_ref.shape[0]
    greet_all(p)
    swaps = [
        Swap(p, src, dst, swap_send.at[k], swap_recv.at[k], local.at[k], same, narrow)
        for k, (src, dst, same, narrow) in enumerate([
            (small_ref, smalls, True, None), (messages.at[0], moved_ref, False, None),
            (messages.at[1], spread_ref, False, -(-2 * gates // 128) * 128),
        ])
    ]
    swaps[0].start()
    old = old_ref[...].T
    new_in = above(gate_ref[...], conv_a_ref[...], conv_b_ref[...])
    new_out = out_ref[...]

    def push(gradient, moment):
        return gradient + MOMENTUM * (MOMENTUM * moment + gradient)

    push_in = push(new_in, old[:ins])
    push_out = above(push(new_out, old[ins : ins + gates]), jnp.zeros((ins - gates, D), F32))
    in_core = p.c == 0
    give[...] = jnp.where(in_core, push_out, push_in)
    slab[:ins] = jnp.where(in_core, push_in, push_out)
    partner = p.at(c=1 - p.c)
    pieces = [AllSum(p, work[:12]), AllSum(p, work[12:])]
    pack_gram([piece.total for piece in pieces], give[...])
    for piece in pieces:
        piece.to_core().start()
    exchange = remote(give, given, give_sems.at[0], give_sems.at[1], partner)
    exchange.start()
    pack_gram([piece.acc for piece in pieces], slab[:ins])

    def store_messages(k, turned):
        turned = beside(turned, jnp.zeros((D, 256 - turned.shape[1]), F32)) if (
            turned.shape[1] < 256) else turned
        for d in range(count):
            messages[k, d] = turned[own * d : own * d + own]

    steps = len(pieces[0].steps)
    for k in range(steps + BEHIND):
        for which, piece in enumerate(pieces):
            if 0 <= k - BEHIND * which < steps:
                piece.steps[k - BEHIND * which]()
        if k == 0:
            store_messages(0, above(new_in, new_out).T)
    exchange.wait()
    swaps[0].wait()
    swaps[1].start()
    smalls_ref[...] = smalls[...]
    rows = smalls[...].reshape(-1, 128)
    new_step = beside(*[rows[HEADS * j : HEADS * j + HEADS] for j in range(D // 128)])
    push_step = push(new_step, old_ref[...].T[ins + gates : ins + gates + HEADS])
    push_step = jnp.where(in_core, push_step, 0.0)
    mine, theirs = slab[:ins], given[...]
    slab_in = above(mine, theirs, push_step)
    slab_out = above(theirs[:gates], mine[:gates], jnp.zeros((2 * (ins - gates) + HEADS, D), F32))
    slab[: 2 * ins + HEADS] = jnp.where(in_core, slab_in, slab_out)
    slab[2 * ins + HEADS :] = jnp.zeros((slab.shape[0] - 2 * ins - HEADS, D), F32)
    gram = mats.at[0]
    unpack_gram(gram, [piece.total for piece in pieces])
    step_high, step_low = split(push_step)
    step_left = above(step_high, step_low, step_high)
    gram[...] = gram[...] + dot_tn(step_left, above(step_high, step_high, step_low))
    iterate(gram, mats.at[1], mats.at[2], left, right, slab, slab_left)
    store_messages(1, slab[...].T)
    swaps[2].start()
    swaps[1].wait()
    swaps[2].wait()


def update_call(parts, small, old, sizes, collective_id):
    count = sizes[0] * sizes[1]
    own = D // count
    chips = count // 2
    ins = sum(part.shape[0] for part in parts[:3])
    per = -(-(D // 2) // (8 * chips)) * 8
    blocks = [(per, 512), (per, D + 128 - 512)]
    vmem = pl.BlockSpec(memory_space=pltpu.VMEM)
    hbm = pl.BlockSpec(memory_space=pl.ANY)
    dma = pltpu.SemaphoreType.DMA
    return pl.pallas_call(
        functools.partial(update_kernel, sizes),
        out_shape=[
            shape(count, own, 256), shape(count, *small.shape), shape(count, own, 256),
        ],
        in_specs=[vmem] * 6,
        out_specs=[hbm, vmem, hbm],
        scratch_shapes=[
            pltpu.VMEM((ins, D), F32), pltpu.VMEM((ins, D), F32), dma((2,)),
            pltpu.VMEM((2, count, own, 256), F32), pltpu.VMEM((count,) + small.shape, F32),
            pltpu.VMEM((3, D, D), F32),
            pltpu.VMEM((D, 3 * D), BF16), pltpu.VMEM((3 * D, D), BF16),
            pltpu.VMEM((256, D), F32), pltpu.VMEM((256, 3 * D), BF16),
            dma((3, count)), dma((3, count)), dma((3,)),
        ]
        + all_sum_scratch(sizes, blocks[0])
        + all_sum_scratch(sizes, blocks[1]),
        compiler_params=pltpu.CompilerParams(
            collective_id=collective_id, has_side_effects=True, vmem_limit_bytes=56 * 2**20
        ),
        name="update",
    )(*parts, small, old)


def finish_kernel(
    moved_ref, spread_ref, step_ref, w_in_ref, w_out_ref, m_in_ref, m_out_ref,
    g_in_ref, g_out_ref, new_m_in_ref, new_m_out_ref, new_w_in_ref, new_w_out_ref,
):
    count = moved_ref.shape[0]
    cuts, outs = cuts_of(count)
    ins = sum(each for _, _, each in cuts)
    decay = 1.0 - MATRIX_RATE * WEIGHT_DECAY
    order = [(2 * chip + core, core) for core in range(2) for chip in range(count // 2)]
    at = 0
    for start, width, each in cuts:
        cols = slice(start, start + width)
        g_in_ref[:, cols] = beside(*[moved_ref[d, :, at : at + each] for d, _ in order])
        new_w_in_ref[:, cols] = beside(*[
            spread_ref[d - core, :, ins * core + at : ins * core + at + each] for d, core in order
        ])
        at += each
    g_in_ref[:, WIDE:] = step_ref[...]
    new_w_in_ref[:, WIDE:] = spread_ref[0, :, 2 * ins : 2 * ins + HEADS]
    g_out_ref[...] = beside(*[moved_ref[d, :, ins : ins + outs] for d, _ in order])
    new_w_out_ref[...] = beside(*[
        spread_ref[d - core + 1, :, outs * core : outs * core + outs] for d, core in order
    ])
    for wide_side, g_ref, m_ref, w_ref, new_m_ref, new_w_ref in (
        (IN_W, g_in_ref, m_in_ref, w_in_ref, new_m_in_ref, new_w_in_ref),
        (INNER, g_out_ref, m_out_ref, w_out_ref, new_m_out_ref, new_w_out_ref),
    ):
        new_m_ref[...] = MOMENTUM * m_ref[...] + g_ref[...]
        rate = MATRIX_RATE * 0.2 * math.sqrt(max(D, wide_side))
        new_w_ref[...] = w_ref[...] * decay - rate * new_w_ref[...]


def finish_call(moved, spread, step_rows, weight_in, weight_out, moment_in, moment_out):
    vmem = pl.BlockSpec(memory_space=pltpu.VMEM)
    return pl.pallas_call(
        finish_kernel,
        out_shape=[shape(*weight_in.shape), shape(*weight_out.shape)] * 3,
        in_specs=[vmem] * 7,
        out_specs=[vmem] * 6,
        name="finish",
    )(moved, spread, step_rows, weight_in, weight_out, moment_in, moment_out)


def shards(
    inputs, cotangent, weight_in, weight_out, small_params, moment_in, moment_out, moment_small
):
    sizes = (lax.axis_size("dp"), lax.axis_size("fsdp"))
    own = weight_in.shape[0]
    weights, blocks, vectors = gather_call(
        weight_in, weight_out, moment_in, moment_out, small_params, sizes, 0
    )
    output, dx, columns, factors, small, old = block_and_gradients(
        inputs[0], cotangent[0], weights, vectors, blocks, sizes, (3, 4)
    )
    new_out, new_gate, new_conv_a, new_conv_b, new_small = scatter_call(
        columns, factors, small, sizes, 1
    )
    moved, smalls, spread = update_call(
        (new_gate, new_conv_a, new_conv_b, new_out), new_small, old.reshape(D, 256), sizes, 2
    )
    smalls = smalls.reshape(-1)
    grad_small = smalls[HEADS * D : HEADS * D + SMALL]
    new_step = smalls[: HEADS * D].reshape(D // 128, HEADS, 128).transpose(1, 0, 2)
    first_row = (lax.axis_index("dp") * sizes[1] + lax.axis_index("fsdp")) * own
    step_rows = lax.dynamic_slice_in_dim(new_step.reshape(HEADS, D), first_row, own, 1).T
    grad_in, grad_out, new_moment_in, new_moment_out, new_weight_in, new_weight_out = finish_call(
        moved, spread, step_rows, weight_in, weight_out, moment_in, moment_out
    )
    new_moment_small = MOMENTUM * moment_small + grad_small
    new_small_params = small_params - SMALL_RATE * new_moment_small
    return (
        output[None],
        dx[None],
        grad_in,
        grad_out,
        grad_small,
        new_moment_in,
        new_moment_out,
        new_moment_small,
        new_weight_in,
        new_weight_out,
        new_small_params,
    )


def solution(mesh):
    return jax.shard_map(
        shards,
        mesh=mesh,
        in_specs=(
            P(("dp", "fsdp"), None, None),
            P(("dp", "fsdp"), None, None),
            P(("dp", "fsdp"), None),
            P(("dp", "fsdp"), None),
            P(),
            P(("dp", "fsdp"), None),
            P(("dp", "fsdp"), None),
            P(),
        ),
        out_specs=(
            P(("dp", "fsdp"), None, None),
            P(("dp", "fsdp"), None, None),
            P(("dp", "fsdp"), None),
            P(("dp", "fsdp"), None),
            P(),
            P(("dp", "fsdp"), None),
            P(("dp", "fsdp"), None),
            P(),
            P(("dp", "fsdp"), None),
            P(("dp", "fsdp"), None),
            P(),
        ),
        check_vma=False,
    )
```

```python
import functools
import math

import jax
import jax.numpy as jnp
from jax import lax
from jax.experimental import pallas as pl
from jax.experimental.pallas import tpu as pltpu
from jax.sharding import PartitionSpec as P

D = 768
HEADS = 24
HEAD_DIM = 64
NSTATE = 128
KCONV = 4
LEN = 1024
ITERS = 5
INNER = 1536
CONVCH = 1792
IN_W = 3352
SMALL = 11336
WIDE = INNER + CONVCH
TAIL_SUMS = 1664 - 2 * HEADS
STEP = 32
CONV_A = 768
HALF = 2560
OUT_AT = WIDE - HALF
STEP_AT = OUT_AT + INNER

MOMENTUM = 0.95
MATRIX_RATE = 0.15
WEIGHT_DECAY = 0.1
SMALL_RATE = 0.01
EPSILON = 1e-05
COEF_A = 3.4445
COEF_B = -4.775
COEF_C = 2.0315

F32 = jnp.float32
BF16 = jnp.bfloat16
CHUNK = 128
STRIP = 256
PER = STRIP // CHUNK
STRIPS = LEN // STRIP
GRAD_TILE = 256
GROUP = 4


def dot(a, b):
    return lax.dot_general(a, b, (((1,), (0,)), ((), ())), preferred_element_type=F32)


def dot_nt(a, b):
    return lax.dot_general(a, b, (((1,), (1,)), ((), ())), preferred_element_type=F32)


def dot_tn(a, b):
    return lax.dot_general(a, b, (((0,), (0,)), ((), ())), preferred_element_type=F32)


def split(v):
    high = v.astype(BF16)
    return high, (v - high.astype(F32)).astype(BF16)


def beside(*parts):
    return jnp.concatenate(parts, axis=1)


def above(*parts):
    return jnp.concatenate(parts, axis=0)


def right_pair(b):
    high, low = split(b)
    return above(beside(high, low), beside(high, jnp.zeros_like(low)))


def three_pass(a, pair):
    high, low = split(a)
    both = dot(beside(high, low), pair)
    half = both.shape[1] // 2
    return both[:, :half] + both[:, half:]


def exact_sum(a, ones):
    high = a.astype(BF16)
    rest = a - high.astype(F32)
    mid = rest.astype(BF16)
    low = (rest - mid.astype(F32)).astype(BF16)
    return dot(beside(high, mid, low), above(ones, ones, ones))


def lane_sums(a):
    high = a.astype(BF16)
    rest = a - high.astype(F32)
    mid = rest.astype(BF16)
    low = (rest - mid.astype(F32)).astype(BF16)
    parts = beside(high, mid, low)
    return dot_nt(jnp.ones((8, parts.shape[1]), BF16), parts)


def stack_left(a):
    high, low = split(a)
    return above(beside(high, high), beside(low, jnp.zeros_like(low)))


def fold(rows):
    total = rows[0:8]
    for i in range(1, rows.shape[0] // 8):
        total = total + rows[8 * i : 8 * i + 8]
    return total


def row_sum(rows):
    return jnp.sum(fold(rows), axis=0, keepdims=True)


def upper():
    row = lax.broadcasted_iota(jnp.int32, (CHUNK, CHUNK), 0)
    col = lax.broadcasted_iota(jnp.int32, (CHUNK, CHUNK), 1)
    return col >= row


def softplus(v):
    return jnp.maximum(v, 0.0) + jnp.log1p(jnp.exp(-jnp.abs(v)))


def rates_of(raw, heads_ref, ones):
    steps = softplus(raw + heads_ref[0])
    logs = exact_sum(steps * heads_ref[1], ones)
    last = jnp.broadcast_to(logs[:, CHUNK - 1 : CHUNK], logs.shape)
    columns = above(logs, jnp.zeros((CHUNK - HEADS, CHUNK), F32)).T
    return steps, logs, columns, jnp.exp(logs), jnp.exp(last - logs), jnp.exp(last)


def silu(v):
    return v * jax.nn.sigmoid(v)


def wide(v):
    return beside(*([v] * PER))


def strip_at(s):
    return pl.ds(pl.multiple_of(s * STRIP, STRIP), STRIP)


def half_rows(rows, c):
    return pl.ds(pl.multiple_of(c * (rows // 2), rows // 2), rows // 2)


class Box:
    def __init__(self, box, dst, sems, partner):
        self.box, self.dst, self.sems, self.partner = box, dst, sems, partner

    def copy(self, s):
        sem = self.sems.at[s]
        return remote(
            self.box.at[lax.rem(s, 2)], self.dst(s), sem.at[0], sem.at[1], self.partner
        )

    def fill(self, s, value, back=False):
        @pl.when(pl.program_id(0) > 1)
        def _():
            self.copy(s + 2 if back else s - 2).wait_send()

        self.box[lax.rem(s, 2)] = value
        self.copy(s).start()

    def finish(self, back=False):
        for s in range(2):
            self.copy(s if back else STRIPS - 1 - s).wait_send()
        for s in range(STRIPS):
            self.copy(s).wait_recv()


def forward_kernel(
    sizes, x_ref, back_ref, first_ref, second_ref, gain_ref, taps_in, heads_ref, inner_in,
    blocks_ref, whole_back_ref,
    out_ref, hb_ref, cin_ref, c_ref, raw_ref, s_ref, own_normed_ref,
    dy_ref, dgate_ref, own_dgate_ref, dlogs_ref, tail_sums_ref, moved_ref,
    peer_normed_ref, peer_dgate_ref, peer_hb_ref, peer_back_ref,
    act, z, mixed, dnormed, state, tail, turned, dskip, dinner, normed_ref,
    taps_ref, inner_ref, load_sems, box_normed, box_dgate, box_hb, box_sems, back_sems, *work,
):
    p = Place(sizes)
    swap = Swap(p, blocks_ref, moved_ref, *work)
    partner = p.at(c=1 - p.c)
    strip = pl.program_id(0)
    back_copy = remote(
        whole_back_ref, peer_back_ref, back_sems.at[0], back_sems.at[1], partner
    )
    boxes = [
        Box(box, lambda s, ref=ref: ref.at[:, strip_at(s)], box_sems.at[k], partner)
        for k, (box, ref) in enumerate(
            [(box_normed, peer_normed_ref), (box_dgate, peer_dgate_ref)]
        )
    ]
    boxes.append(Box(box_hb, lambda s: peer_hb_ref.at[strip_at(s)], box_sems.at[2], partner))

    @pl.when(strip == 0)
    def _():
        loads = [
            pltpu.make_async_copy(taps_in, taps_ref, load_sems.at[0]),
            pltpu.make_async_copy(inner_in, inner_ref, load_sems.at[1]),
        ]
        for load in loads:
            load.start()
        greet_all(p)
        back_copy.start()
        swap.start()
        state[...] = jnp.zeros_like(state)
        tail[...] = jnp.zeros_like(tail)
        dskip[...] = jnp.zeros_like(dskip)
        dinner[...] = jnp.zeros_like(dinner)
        for i in range(HALF // 256):
            part = slice(256 * i, 256 * i + 256)
            turned[0, part] = first_ref[:, part].T
            turned[1, part] = second_ref[:, part].T
        for load in loads:
            load.wait()

    x = x_ref[...].astype(F32)
    scaled = x * lax.rsqrt(jnp.mean(x * x, axis=-1, keepdims=True) + EPSILON) * gain_ref[...]
    hb = scaled.astype(BF16)
    hb_ref[...] = hb
    boxes[2].fill(strip, hb)
    back = back_ref[...]
    raw_ref[...] = dot_nt(turned[1, STEP_AT : STEP_AT + STEP], hb)

    lane = lax.broadcasted_iota(jnp.int32, (64, CHUNK), 1)

    def later(cols, steps, before):
        turned_cols = [before] + [pltpu.roll(col, steps, 1) for col in cols]
        pairs = zip(turned_cols[:-1], turned_cols[1:])
        return [jnp.where(lane < steps, a, b) for a, b in pairs], turned_cols[-1]

    def conv_tile(i):
        rows = slice(64 * i, 64 * i + 64)
        cur = cin_ref[rows]
        cols = [cur[:, CHUNK * j : CHUNK * j + CHUNK] for j in range(PER)]
        taps = [taps_ref[k, rows] for k in range(KCONV + 1)]
        ones_late, tail[0, rows] = later(cols, 1, tail[0, rows])
        early = [taps[1] * a + taps[0] * b for a, b in zip(cols, ones_late)]
        twos_late, tail[1, rows] = later(early, 2, tail[1, rows])
        total = beside(*[
            taps[4] + c + taps[2] * b + taps[3] * a for a, b, c in zip(cols, ones_late, twos_late)
        ])
        c_ref[rows] = total
        act[rows] = total * jax.nn.sigmoid(total)

    def project(i):
        start = INNER + 256 * i
        rows = turned[start // HALF, start % HALF : start % HALF + 256]
        cin_ref[256 * i : 256 * i + 256] = dot_nt(rows, hb)

    project(0)
    for i in range(CONVCH // 256):
        if i + 1 < CONVCH // 256:
            project(i + 1)
        if i < INNER // 256:
            part = slice(256 * i, 256 * i + 256)
            z[part] = dot_nt(turned[0, part], hb)
            dnormed[part] = dot_nt(turned[1, OUT_AT + 256 * i : OUT_AT + 256 * i + 256], back)
        for q in range(4):
            conv_tile(4 * i + q)
    causal = upper()
    ones = causal.astype(F32).astype(BF16)

    def chunk(j, carry):
        cols = pl.ds(pl.multiple_of(j * CHUNK, CHUNK), CHUNK)
        steps, logs, columns, grown, to_end, through = rates_of(
            raw_ref[0:HEADS, cols], heads_ref, ones
        )
        in_map = act[INNER : INNER + NSTATE, cols].T
        in_pair = right_pair(in_map)
        out_pair = right_pair(act[INNER + NSTATE :, cols])
        scores = three_pass(in_map, out_pair)
        for g in range(HEADS // GROUP):
            rows = slice(g * GROUP * HEAD_DIM, (g + 1) * GROUP * HEAD_DIM)
            held = state[rows]
            s_ref[j, rows] = held
            across = three_pass(held, out_pair)
            ending, kept = [], []
            for q in range(GROUP):
                h = g * GROUP + q
                mine = slice(h * HEAD_DIM, (h + 1) * HEAD_DIM)
                values = act[mine, cols]
                fed = values * steps[h : h + 1]
                gaps = logs[h : h + 1] - jnp.broadcast_to(columns[:, h : h + 1], (CHUNK, CHUNK))
                weights = scores * jnp.where(causal, jnp.exp(gaps), 0.0)
                both = dot(stack_left(fed), above(*split(weights)))
                y = both[:HEAD_DIM] + both[HEAD_DIM:]
                y = y + across[q * HEAD_DIM : (q + 1) * HEAD_DIM] * grown[h : h + 1]
                mixed[mine, cols] = y + heads_ref[2][h : h + 1] * values
                ending.append(fed * to_end[h : h + 1])
                kept.append(jnp.broadcast_to(through[h : h + 1], (HEAD_DIM, CHUNK)))
            state[rows] = held * above(*kept) + three_pass(above(*ending), in_pair)
        return carry

    lax.fori_loop(0, PER, chunk, 0)

    def mean_tile(h, totals):
        rows = pl.ds(pl.multiple_of(h * HEAD_DIM, HEAD_DIM), HEAD_DIM)
        gate = z[rows, :]
        opened = mixed[rows, :] * (gate * jax.nn.sigmoid(gate))
        gained = dnormed[rows, :] * wide(inner_ref[rows, :]) * opened
        return totals[0] + fold(opened * opened), totals[1] + fold(gained)

    nothing = jnp.zeros((8, STRIP), F32)
    squares, gains = lax.fori_loop(0, HEADS, mean_tile, (nothing, nothing))
    mean = jnp.sum(squares, axis=0, keepdims=True) * (1.0 / INNER)
    r = lax.rsqrt(mean + EPSILON)
    pulled = jnp.sum(gains, axis=0, keepdims=True) * (1.0 / INNER) * (r * r * r)

    def gate_tile(h, carry):
        rows = pl.ds(pl.multiple_of(h * HEAD_DIM, HEAD_DIM), HEAD_DIM)
        gate = z[rows, :]
        skip = wide(heads_ref[2, pl.ds(h, 1), :])
        mix = mixed[rows, :]
        sig = jax.nn.sigmoid(gate)
        sil = gate * sig
        opened = mix * sil
        normed = opened * r
        inner = wide(inner_ref[rows, :])
        normed_ref[rows, :] = (normed * inner).astype(BF16)
        dn = dnormed[rows, :]
        gained = dn * normed
        dinner[rows, :] += gained[:, :CHUNK] + gained[:, CHUNK:]
        dopened = dn * inner * r - opened * pulled
        dmixed = dopened * sil
        dy_ref[rows, :] = dmixed
        dgate_ref[rows, :] = (dopened * mix * (sig * (1.0 + gate * (1.0 - sig)))).astype(BF16)
        skipped = row_sum(dmixed * act[rows, :])
        dskip[pl.ds(h, 1), :] += skipped[:, :CHUNK] + skipped[:, CHUNK:]
        dlogs_ref[pl.ds(h, 1), :] = row_sum(dmixed * mix) - skip * skipped
        return carry

    lax.fori_loop(0, HEADS, gate_tile, 0)
    for box, own, ref in (
        (boxes[0], own_normed_ref, normed_ref), (boxes[1], own_dgate_ref, dgate_ref),
    ):
        own[...] = ref[half_rows(INNER, p.c), :]
        box.fill(strip, ref[half_rows(INNER, 1 - p.c), :])
    for i in range(D // 256):
        part = slice(256 * i, 256 * i + 256)
        branch = dot(second_ref[part, OUT_AT:STEP_AT], normed_ref[...]).T
        out_ref[:, part] = (x_ref[:, part].astype(F32) + branch).astype(BF16)

    @pl.when(pl.program_id(0) == STRIPS - 1)
    def _():
        tail_sums_ref[...] = beside(
            lane_sums(dskip[...]), lane_sums(dinner[...]),
            jnp.zeros((8, tail_sums_ref.shape[1] - HEADS - INNER), F32),
        )
        swap.wait()
        back_copy.wait()
        for box in boxes:
            box.finish()


def backward_kernel(
    sizes, x_ref, back_ref, w_in_ref, step_in_ref, gain_ref, taps_ref, heads_ref,
    cin_ref, c_ref, raw_ref, s_ref, dy, dgate_ref, dlogs, tail_sums_ref, out_part, gate_part,
    dx_ref, own_a_ref, own_b_ref, flat_ref, out_column, gate_column, peer_a_ref, peer_b_ref,
    dconv_a_ref, dconv_b_ref, box_a, box_b, box_sems, dact, dstate, flow, tail, meets, vdu_rows, dstep_ref, dstep_sum, dgain, dtaps_ref, dheads_ref,
    dscaled_turned, *work,
):
    step_now = pl.program_id(0)
    p = Place(sizes)
    partner = p.at(c=1 - p.c)
    strip = STRIPS - 1 - step_now
    boxes = [
        Box(box, lambda s, ref=ref: ref.at[:, strip_at(s)], box_sems.at[k], partner)
        for k, (box, ref) in enumerate([(box_a, peer_a_ref), (box_b, peer_b_ref)])
    ]
    sums = [
        PlaneSum(p, part, work[7 * k : 7 * k + 7]) for k, part in enumerate((out_part, gate_part))
    ]

    @pl.when(step_now == 0)
    def _():
        sums[0].begin()
        greet_near(p, False)
        sums[0].start()
        sums[1].begin()

    @pl.when(step_now == 3)
    def _():
        sums[1].plane.finish(0)
        sums[1].plane.start(1)

    @pl.when(step_now == 0)
    def _():
        dstate[...] = jnp.zeros_like(dstate)
        flow[...] = jnp.zeros_like(flow)
        tail[...] = jnp.zeros_like(tail)
        dgain[...] = jnp.zeros_like(dgain)
        dstep_sum[...] = jnp.zeros_like(dstep_sum)
        dtaps_ref[...] = jnp.zeros_like(dtaps_ref)
        dheads_ref[...] = jnp.zeros_like(dheads_ref)

    back = back_ref[...]

    causal = upper()
    ones = causal.astype(F32).astype(BF16)
    row = lax.broadcasted_iota(jnp.int32, (CHUNK, CHUNK), 0)
    col = lax.broadcasted_iota(jnp.int32, (CHUNK, CHUNK), 1)
    ones_back = (row >= col).astype(F32).astype(BF16)

    def chunk(step, carry):
        j = PER - 1 - step
        cols = pl.ds(pl.multiple_of(j * CHUNK, CHUNK), CHUNK)
        raw = raw_ref[0:HEADS, cols]
        steps, logs, columns, grown, to_end, through = rates_of(raw, heads_ref, ones)
        in_turned = silu(c_ref[INNER : INNER + NSTATE, cols])
        out_turned = silu(c_ref[INNER + NSTATE :, cols])
        in_map = in_turned.T
        out_map = out_turned.T
        scores = three_pass(in_map, right_pair(out_turned))
        in_pair = right_pair(in_turned)
        out_pair = right_pair(out_map)
        dscores = jnp.zeros((CHUNK, CHUNK), F32)
        din = jnp.zeros((NSTATE, CHUNK), F32)
        dout = jnp.zeros((NSTATE, CHUNK), F32)
        for g in range(HEADS // GROUP):
            rows = slice(g * GROUP * HEAD_DIM, (g + 1) * GROUP * HEAD_DIM)
            leaving = dstate[rows]
            entering = s_ref[j, rows]
            from_state = three_pass(leaving, in_pair)
            ending, growing, kept = [], [], []
            for q in range(GROUP):
                h = g * GROUP + q
                mine = slice(h * HEAD_DIM, (h + 1) * HEAD_DIM)
                values = silu(c_ref[mine, cols])
                fed = values * steps[h : h + 1]
                dys = dy[mine, cols]
                gaps = logs[h : h + 1] - jnp.broadcast_to(columns[:, h : h + 1], (CHUNK, CHUNK))
                decay = jnp.where(causal, jnp.exp(gaps), 0.0)
                weights = scores * decay
                both = dot_nt(stack_left(dys), beside(*split(weights)))
                du = both[:HEAD_DIM] + both[HEAD_DIM:]
                du = du + from_state[q * HEAD_DIM : (q + 1) * HEAD_DIM] * to_end[h : h + 1]
                fed_high, fed_low = split(fed)
                dy_high, dy_low = split(dys)
                dweights = dot_tn(
                    above(fed_high, fed_low, fed_high), above(dy_high, dy_high, dy_low)
                )
                dscores = dscores + dweights * decay
                vdu_rows[h : h + 1, :] = row_sum(values * du)
                dact[mine, cols] = du * steps[h : h + 1] + heads_ref[2][h : h + 1] * dys
                ending.append(fed * to_end[h : h + 1])
                growing.append(dys * grown[h : h + 1])
                kept.append(jnp.broadcast_to(through[h : h + 1], (HEAD_DIM, CHUNK)))
            ending = above(*ending)
            growing = above(*growing)
            end_high, end_low = split(ending)
            grow_high, grow_low = split(growing)
            leave_high, leave_low = split(leaving)
            enter_high, enter_low = split(entering)
            din = din + dot_tn(
                above(leave_high, leave_low, leave_high), above(end_high, end_high, end_low)
            )
            dout = dout + dot_tn(
                above(enter_high, enter_low, enter_high), above(grow_high, grow_high, grow_low)
            )
            arrived = leaving * above(*kept) + three_pass(growing, out_pair)
            dstate[rows] = arrived
            meet = arrived * entering
            for q in range(GROUP):
                h = g * GROUP + q
                meets[h : h + 1, :] = row_sum(meet[q * HEAD_DIM : (q + 1) * HEAD_DIM])
        vdu = vdu_rows[...]
        dlog = dlogs[:, cols] - steps * vdu
        drate = exact_sum(dlog, ones_back) + flow[...]
        flow[...] = jnp.broadcast_to(
            jnp.sum(meets[...], axis=1, keepdims=True), (HEADS, CHUNK)
        )
        dsteps = vdu + heads_ref[1] * drate
        draw = dsteps * jax.nn.sigmoid(raw + heads_ref[0])
        dheads_ref[0] += draw
        dheads_ref[1] += drate * steps * heads_ref[1]
        dstep_ref[:, cols] = above(draw, jnp.zeros((STEP - HEADS, CHUNK), F32)).astype(BF16)
        score_high, score_low = split(dscores)
        both = dot_nt(stack_left(out_turned), beside(score_high, score_low))
        dact[INNER : INNER + NSTATE, cols] = din + both[:NSTATE] + both[NSTATE:]
        both = dot(stack_left(in_turned), above(score_high, score_low))
        dact[INNER + NSTATE :, cols] = dout + both[:NSTATE] + both[NSTATE:]
        return carry

    lax.fori_loop(0, PER, chunk, 0)

    @pl.when(step_now == 0)
    def _():
        sums[1].start()

    @pl.when(step_now == 2)
    def _():
        sums[0].plane.finish(0)
        sums[0].plane.start(1)

    lane = lax.broadcasted_iota(jnp.int32, (64, CHUNK), 1)

    def conv_tile(target, start, i):
        rows = slice(start + 64 * i, start + 64 * i + 64)
        c = c_ref[rows]
        sig = jax.nn.sigmoid(c)
        dpre = dact[rows] * (sig * (1.0 + c * (1.0 - sig)))
        cin = cin_ref[rows]
        cols = [dpre[:, CHUNK * j : CHUNK * j + CHUNK] for j in range(PER)]
        dcin = dpre * wide(taps_ref[KCONV - 1, rows])
        grad = cin * dpre
        dtaps_ref[KCONV - 1, rows] += grad[:, :CHUNK] + grad[:, CHUNK:]
        dtaps_ref[KCONV, rows] += dpre[:, :CHUNK] + dpre[:, CHUNK:]
        for k in range(KCONV - 1):
            ahead = KCONV - 1 - k
            turned = [pltpu.roll(col, CHUNK - ahead, 1) for col in cols] + [tail[k, rows]]
            tail[k, rows] = turned[0]
            pairs = zip(turned[:-1], turned[1:])
            shifted = beside(*[jnp.where(lane < CHUNK - ahead, a, b) for a, b in pairs])
            dcin = dcin + shifted * wide(taps_ref[k, rows])
            grad = cin * shifted
            dtaps_ref[k, rows] += grad[:, :CHUNK] + grad[:, CHUNK:]
        target[64 * i : 64 * i + 64] = dcin.astype(BF16)

    thirds = [slice(256 * i, 256 * i + 256) for i in range(D // 256)]
    conv_at = INNER + CONV_A
    tiles = CONV_A // 64
    for i in range(tiles):
        conv_tile(dconv_a_ref, 0, i)
        if i % 4 == 0:
            part = thirds[i // 4]
            dscaled_turned[part] = dot(w_in_ref[part, :INNER], dgate_ref[...])
    for i in range((CONVCH - CONV_A) // 64):
        conv_tile(dconv_b_ref, CONV_A, i)
        if i % 4 == 0 and i // 4 < len(thirds):
            part = thirds[i // 4]
            dscaled_turned[part] += dot(w_in_ref[part, INNER:conv_at], dconv_a_ref[...])
    for box, own, ref in (
        (boxes[0], own_a_ref, dconv_a_ref), (boxes[1], own_b_ref, dconv_b_ref),
    ):
        own[...] = ref[half_rows(ref.shape[0], p.c), :]
        box.fill(strip, ref[half_rows(ref.shape[0], 1 - p.c), :], True)
    x = x_ref[...].astype(F32)
    r = lax.rsqrt(jnp.mean(x * x, axis=-1, keepdims=True) + EPSILON)
    parts = []
    for part in thirds:
        total = dscaled_turned[part] + dot(w_in_ref[part, conv_at:], dconv_b_ref[...])
        parts.append((total + dot(step_in_ref[part, :STEP], dstep_ref[...])).T)
    dscaled = beside(*parts)
    plain = x * r
    dgain[...] += fold(dscaled * plain)
    dstep_sum[...] += dot(dstep_ref[...], (plain * gain_ref[...]).astype(BF16))
    gained = dscaled * gain_ref[...]
    inner = jnp.mean(gained * plain, axis=-1, keepdims=True)
    dx_ref[...] = back.astype(F32) + (gained - plain * inner) * r

    @pl.when(step_now == STRIPS - 1)
    def _():
        for part, column in zip(sums, (out_column, gate_column)):
            part.plane.finish(1)
            column[...] = part.column()
        for box in boxes:
            box.finish(True)
        store_flat(flat_ref, dstep_sum, dgain, dtaps_ref, dheads_ref, tail_sums_ref)


def store_flat(flat_ref, dstep_sum, dgain, dtaps, dheads, tail_sums_ref):
    flat_ref[...] = jnp.zeros_like(flat_ref)
    for j in range(D // 128):
        flat_ref[HEADS * j : HEADS * j + HEADS] = dstep_sum[:HEADS, 128 * j : 128 * j + 128]
    last = beside(
        lane_sums(dheads[0])[:1], lane_sums(dheads[1])[:1], tail_sums_ref[:1],
    )
    rows = [jnp.sum(dgain[...], axis=0, keepdims=True)]
    rows += [lane_sums(dtaps[k])[:1] for k in range(KCONV + 1)]
    at = HEADS * (D // 128)
    for row in rows + [last]:
        for j in range(row.shape[1] // 128):
            flat_ref[at + j : at + j + 1] = row[:, 128 * j : 128 * j + 128]
        at += row.shape[1] // 128


def whole(shape):
    return pl.BlockSpec(shape, lambda i: (0,) * len(shape), pipeline_mode=pl.Buffered(1))


def strip_rows(width):
    return pl.BlockSpec((STRIP, width), lambda i: (i, 0))


def strip_cols(height):
    return pl.BlockSpec((height, STRIP), lambda i: (0, i))


def shape(*dims, dtype=F32):
    return jax.ShapeDtypeStruct(dims, dtype)


def columns(width, at):
    return pl.BlockSpec((D, width), lambda i: (0, at), pipeline_mode=pl.Buffered(1))


def forward_call(x, back, weights, gain, taps, heads, inner, blocks, sizes, collective_id):
    count = sizes[0] * sizes[1]
    dma = pltpu.SemaphoreType.DMA
    hbm = pl.BlockSpec(memory_space=pl.ANY)
    return pl.pallas_call(
        functools.partial(forward_kernel, sizes),
        grid=(STRIPS,),
        in_specs=[
            strip_rows(D), strip_rows(D), columns(HALF, 0), columns(HALF, 1), whole((1, D)),
            hbm, whole((3, HEADS, CHUNK)), hbm, hbm, hbm,
        ],
        out_specs=[
            strip_rows(D), strip_rows(D), strip_cols(CONVCH), strip_cols(CONVCH),
            strip_cols(STEP), pl.BlockSpec((PER, INNER, NSTATE), lambda i: (i, 0, 0)),
            strip_cols(INNER // 2), strip_cols(INNER), strip_cols(INNER), strip_cols(INNER // 2),
            strip_cols(HEADS), whole((8, TAIL_SUMS)), hbm, hbm, hbm, hbm, hbm,
        ],
        out_shape=[
            shape(LEN, D, dtype=BF16), shape(LEN, D, dtype=BF16), shape(CONVCH, LEN),
            shape(CONVCH, LEN), shape(STEP, LEN), shape(LEN // CHUNK, INNER, NSTATE),
            shape(INNER // 2, LEN, dtype=BF16), shape(INNER, LEN), shape(INNER, LEN, dtype=BF16),
            shape(INNER // 2, LEN, dtype=BF16), shape(HEADS, LEN), shape(8, TAIL_SUMS),
            shape(*blocks.shape), shape(INNER // 2, LEN, dtype=BF16),
            shape(INNER // 2, LEN, dtype=BF16), shape(LEN, D, dtype=BF16),
            shape(LEN, D, dtype=BF16),
        ],
        scratch_shapes=[
            pltpu.VMEM((CONVCH, STRIP), F32), pltpu.VMEM((INNER, STRIP), F32),
            pltpu.VMEM((INNER, STRIP), F32), pltpu.VMEM((INNER, STRIP), F32),
            pltpu.VMEM((INNER, NSTATE), F32), pltpu.VMEM((2, CONVCH, CHUNK), F32),
            pltpu.VMEM((2, HALF, D), BF16), pltpu.VMEM((HEADS, CHUNK), F32),
            pltpu.VMEM((INNER, CHUNK), F32), pltpu.VMEM((INNER, STRIP), BF16),
            pltpu.VMEM((KCONV + 1, CONVCH, CHUNK), F32), pltpu.VMEM((INNER, CHUNK), F32), dma((2,)),
            pltpu.VMEM((2, INNER // 2, STRIP), BF16), pltpu.VMEM((2, INNER // 2, STRIP), BF16),
            pltpu.VMEM((2, STRIP, D), BF16), dma((3, STRIPS, 2)), dma((2,)),
            dma((count,)), dma((count,)), dma,
        ],
        compiler_params=pltpu.CompilerParams(
            vmem_limit_bytes=60 * 2**20, collective_id=collective_id, has_side_effects=True
        ),
        name="mixer_forward",
    )(x, back, weights, weights, gain, taps, heads, inner, blocks, back)


def backward_call(x, back, weights, gain, taps, heads, kept, tail_sums, parts, sizes,
                  collective_id):
    last = STRIPS - 1

    def rows(width):
        return pl.BlockSpec((STRIP, width), lambda i: (last - i, 0))

    def cols(height):
        return pl.BlockSpec((height, STRIP), lambda i: (0, last - i))

    Z = sizes[0]
    lines = flat_lines(sizes[0] * sizes[1])
    size = (parts[0].shape[1], D)
    dma = pltpu.SemaphoreType.DMA
    hbm = pl.BlockSpec(memory_space=pl.ANY)
    return pl.pallas_call(
        functools.partial(backward_kernel, sizes),
        grid=(STRIPS,),
        in_specs=[
            rows(D), rows(D), columns(WIDE, 0),
            columns(256, (HALF + STEP_AT) // 256), whole((1, D)),
            whole((KCONV, CONVCH, CHUNK)), whole((3, HEADS, CHUNK)), cols(CONVCH),
            cols(CONVCH), cols(STEP),
            pl.BlockSpec((PER, INNER, NSTATE), lambda i: (last - i, 0, 0)), cols(INNER),
            cols(INNER), cols(HEADS), whole((8, TAIL_SUMS)), hbm, hbm,
        ],
        out_specs=[
            rows(D), cols(CONV_A // 2), cols((CONVCH - CONV_A) // 2), whole((lines, 128)),
            whole((Z,) + size), whole((Z,) + size), hbm, hbm,
        ],
        out_shape=[
            shape(LEN, D), shape(CONV_A // 2, LEN, dtype=BF16),
            shape((CONVCH - CONV_A) // 2, LEN, dtype=BF16), shape(lines, 128),
            shape(Z, *size), shape(Z, *size), shape(CONV_A // 2, LEN, dtype=BF16),
            shape((CONVCH - CONV_A) // 2, LEN, dtype=BF16),
        ],
        scratch_shapes=[
            pltpu.VMEM((CONV_A, STRIP), BF16), pltpu.VMEM((CONVCH - CONV_A, STRIP), BF16),
            pltpu.VMEM((2, CONV_A // 2, STRIP), BF16),
            pltpu.VMEM((2, (CONVCH - CONV_A) // 2, STRIP), BF16), dma((2, STRIPS, 2)),
            pltpu.VMEM((CONVCH, STRIP), F32),
            pltpu.VMEM((INNER, NSTATE), F32), pltpu.VMEM((HEADS, CHUNK), F32),
            pltpu.VMEM((KCONV - 1, CONVCH, CHUNK), F32), pltpu.VMEM((HEADS, CHUNK), F32),
            pltpu.VMEM((HEADS, CHUNK), F32), pltpu.VMEM((STEP, STRIP), BF16),
            pltpu.VMEM((STEP, D), F32), pltpu.VMEM((8, D), F32),
            pltpu.VMEM((KCONV + 1, CONVCH, CHUNK), F32), pltpu.VMEM((2, HEADS, CHUNK), F32),
            pltpu.VMEM((D, STRIP), F32),
        ]
        + 2 * (plane_scratch(sizes, size) + [dma]),
        compiler_params=pltpu.CompilerParams(
            vmem_limit_bytes=63 * 2**20, collective_id=collective_id, has_side_effects=True
        ),
        name="mixer_backward",
    )(
        x, back, weights, weights, gain, taps, heads, *kept, tail_sums,
        *(by_chip(part, sizes) for part in parts),
    )


def grads_kernel(*refs):
    ins, outs, (sides, others, results, sems, out_sems) = refs[:8], refs[8:10], refs[10:]
    copies = []
    for k in range(4):
        copies.append([
            pltpu.make_async_copy(ins[2 * k], sides.at[k], sems.at[2 * k]),
            pltpu.make_async_copy(ins[2 * k + 1], others.at[k], sems.at[2 * k + 1]),
        ])
        for copy in copies[k]:
            copy.start()
    stores = []
    for k in range(2):
        for half in (0, 1):
            for copy in copies[2 * k + half]:
                copy.wait()
            side, other = sides.at[2 * k + half], others.at[2 * k + half]

            def tile(i, carry, k=k, half=half, side=side, other=other):
                rows = pl.ds(pl.multiple_of(i * GRAD_TILE, GRAD_TILE), GRAD_TILE)
                part = dot(side[rows, :], other[...])
                results[k, rows, :] = part if half == 0 else results[k, rows, :] + part
                return carry

            lax.fori_loop(0, INNER // 2 // GRAD_TILE, tile, 0)
        stores.append(pltpu.make_async_copy(results.at[k], outs[k], out_sems.at[k]))
        stores[k].start()
    for store in stores:
        store.wait()


def grads_call(own_normed, peer_normed, own_dgate, peer_dgate, backs, hbs):
    rows = INNER // 2
    hbm = pl.BlockSpec(memory_space=pl.ANY)
    return pl.pallas_call(
        grads_kernel,
        in_specs=[hbm] * 8,
        out_specs=[hbm] * 2,
        out_shape=[shape(rows, D)] * 2,
        scratch_shapes=[
            pltpu.VMEM((4, rows, LEN), BF16), pltpu.VMEM((4, LEN, D), BF16),
            pltpu.VMEM((2, rows, D), F32), pltpu.SemaphoreType.DMA((8,)),
            pltpu.SemaphoreType.DMA((2,)),
        ],
        compiler_params=pltpu.CompilerParams(vmem_limit_bytes=60 * 2**20),
        name="grads",
    )(own_normed, backs[0], peer_normed, backs[1], own_dgate, hbs[0], peer_dgate, hbs[1])


def flat_lines(count):
    return -(-(HEADS * D + SMALL) // (1024 * count)) * 8 * count


def block_and_gradients(x, back, weights, vectors, blocks, sizes, collective_ids):
    count = sizes[0] * sizes[1]
    gain, taps, heads, inner = vectors
    (
        out, hb, cin, c, raw, states, own_normed, dy, dgate, own_dgate, dlogs, tail_sums, moved,
        peer_normed, peer_dgate, peer_hb, peer_back,
    ) = forward_call(
        x, back, weights, gain, taps, heads, inner, blocks, sizes, collective_ids[0]
    )
    parts = grads_call(
        own_normed, peer_normed, own_dgate, peer_dgate, (back, peer_back), (hb, peer_hb)
    )
    parts = [part.reshape(count // 2, -1, D) for part in parts]
    dx, own_a, own_b, flat, out_column, gate_column, peer_a, peer_b = backward_call(
        x, back, weights, gain, taps, heads, (cin, c, raw, states, dy, dgate, dlogs), tail_sums,
        parts, sizes, collective_ids[1],
    )
    factors = (own_a, peer_a, own_b, peer_b, hb, peer_hb)
    return out, dx, [out_column, gate_column], factors, flat.reshape(count, -1, 128), moved


MESH = pl.DeviceIdType.MESH


class Place:
    def __init__(self, sizes):
        self.Z, self.F = sizes
        self.C, self.Y = 2, 2
        self.X = self.F // 4
        f = lax.axis_index("fsdp")
        self.z = lax.axis_index("dp")
        self.c = lax.rem(f, 2)
        self.x = lax.rem(f // 2, self.X)
        self.y = f // (2 * self.X)
        self.f = f

    def at(self, z=None, y=None, x=None, c=None):
        z = self.z if z is None else z
        y = self.y if y is None else y
        x = self.x if x is None else x
        c = self.c if c is None else c
        return (z, (y * self.X + x) * 2 + c)

    def other_x(self, step):
        return lax.rem(self.x + step, self.X)


def signal(device):
    pl.semaphore_signal(
        pltpu.get_barrier_semaphore(), inc=1, device_id=device, device_id_type=MESH
    )


def greet_all(place, wait=True):
    count = place.Z * place.F
    me = place.z * place.F + place.f

    def step(i, carry):
        peer = lax.rem(me + i, count)
        signal((peer // place.F, lax.rem(peer, place.F)))
        return carry

    lax.fori_loop(1, count, step, 0)
    if wait:
        await_all(place)


def await_all(place):
    pl.semaphore_wait(pltpu.get_barrier_semaphore(), place.Z * place.F - 1)


def remote(src, dst, send, recv, device):
    return pltpu.make_async_remote_copy(
        src_ref=src, dst_ref=dst, send_sem=send, recv_sem=recv, device_id=device,
        device_id_type=MESH,
    )


def add_blocks(dst, src, count):
    def step(i, carry):
        target = dst(i)
        target[...] = target[...] + src(i)[...]
        return carry

    lax.fori_loop(0, count, step, 0)


class Swap:
    def __init__(self, place, src, dst, send, recv, local, same=False, narrow=None):
        self.place, self.src, self.dst, self.same, self.narrow = place, src, dst, same, narrow
        self.send, self.recv, self.local = send, recv, local
        self.count = place.Z * place.F
        self.me = place.z * place.F + place.f

    def block(self, peer):
        return self.src if self.same else self.src.at[peer]

    def cut(self, ref, odd):
        return ref.at[:, pl.ds(0, self.narrow)] if odd else ref

    def each(self, sender, act):
        if self.narrow is None:
            act(False)
        else:
            @pl.when(lax.rem(sender, 2) == 0)
            def _():
                act(False)

            @pl.when(lax.rem(sender, 2) == 1)
            def _():
                act(True)

    def to(self, i, odd):
        peer = lax.rem(self.me + i, self.count)
        return remote(
            self.cut(self.block(peer), odd), self.cut(self.dst.at[self.me], odd),
            self.send.at[i], self.recv.at[i],
            (peer // self.place.F, lax.rem(peer, self.place.F)),
        )

    def keep(self):
        return pltpu.make_async_copy(self.block(self.me), self.dst.at[self.me], self.local)

    def start(self):
        self.keep().start()

        def step(i, carry):
            self.each(self.me, lambda odd: self.to(i, odd).start())
            return carry

        lax.fori_loop(1, self.count, step, 0)

    def wait(self):
        self.keep().wait()

        def step(i, carry):
            sender = lax.rem(self.me + self.count - i, self.count)
            self.each(self.me, lambda odd: self.to(i, odd).wait_send())
            self.each(sender, lambda odd: remote(
                self.cut(self.block(sender), odd), self.cut(self.dst.at[sender], odd),
                self.send.at[i], self.recv.at[i],
                (sender // self.place.F, lax.rem(sender, self.place.F)),
            ).wait_recv())
            return carry

        lax.fori_loop(1, self.count, step, 0)


def greet_near(place, along_z, wait=True):
    signal(place.at(c=1 - place.c))
    signal(place.at(y=1 - place.y))
    for s in range(1, place.X):
        signal(place.at(x=place.other_x(s)))
    if along_z:
        for s in range(1, place.Z):
            signal(place.at(z=lax.rem(place.z + s, place.Z)))
    if wait:
        await_near(place, along_z)


def await_near(place, along_z):
    pl.semaphore_wait(
        pltpu.get_barrier_semaphore(), place.X + 1 + (place.Z - 1 if along_z else 0)
    )


class Plane:
    def __init__(self, place, acc, x1, y1, x2, y2, sems):
        self.p, self.acc = place, acc
        self.x1, self.y1, self.x2, self.y2, self.sems = x1, y1, x2, y2, sems
        self.h = place.Z // 2

    def copies(self, stage):
        p, acc, h = self.p, self.acc, self.h
        low, high = pl.ds(0, h), pl.ds(h, p.Z - h)
        out = []
        base = stage * p.X
        for s in range(1, p.X):
            x = p.other_x(s)
            if stage == 0:
                src, dst = acc.at[low, :, x], self.x1.at[s - 1]
            else:
                src, dst = acc.at[high, p.y, x], self.x2.at[s - 1]
            sem = self.sems.at[base + s]
            out.append(remote(src, dst, sem.at[0], sem.at[1], p.at(x=x)))
        if stage == 0:
            src, dst = acc.at[high, 1 - p.y], self.y1
        else:
            src, dst = acc.at[low, 1 - p.y, p.x], self.y2
        sem = self.sems.at[base]
        out.append(remote(src, dst, sem.at[0], sem.at[1], p.at(y=1 - p.y)))
        return out

    def start(self, stage):
        for copy in self.copies(stage):
            copy.start()

    def finish(self, stage):
        p, acc, h = self.p, self.acc, self.h
        for copy in self.copies(stage):
            copy.wait()
        for s in range(p.X - 1):
            if stage == 0:
                add_blocks(
                    lambda i: acc.at[i // p.Y, lax.rem(i, p.Y), p.x],
                    lambda i: self.x1.at[s, i // p.Y, lax.rem(i, p.Y)],
                    h * p.Y,
                )
            else:
                add_blocks(
                    lambda i: acc.at[h + i, p.y, p.x], lambda i: self.x2.at[s, i], p.Z - h
                )
        if stage == 0:
            add_blocks(
                lambda i: acc.at[h + i // p.X, p.y, lax.rem(i, p.X)],
                lambda i: self.y1.at[i // p.X, lax.rem(i, p.X)],
                (p.Z - h) * p.X,
            )
        else:
            add_blocks(lambda i: acc.at[i, p.y, p.x], lambda i: self.y2.at[i], h)


def plane_scratch(sizes, block):
    Z, X, Y = sizes[0], sizes[1] // 4, 2
    h = Z // 2
    return [
        pltpu.VMEM((Z, Y, X) + block, F32), pltpu.VMEM((X - 1, h, Y) + block, F32),
        pltpu.VMEM((Z - h, X) + block, F32), pltpu.VMEM((X - 1, Z - h) + block, F32),
        pltpu.VMEM((h,) + block, F32), pltpu.SemaphoreType.DMA((2 * X, 2)),
    ]


def by_place(blocks, sizes):
    return blocks.reshape((sizes[0], 2, sizes[1] // 4, 2) + blocks.shape[1:])


def by_chip(blocks, sizes):
    return blocks.reshape((sizes[0], 2, sizes[1] // 4) + blocks.shape[1:])


class PlaneSum:
    def __init__(self, place, part, work):
        self.p, self.part, self.acc, self.sem = place, part, work[0], work[6]
        self.plane = Plane(place, *work[:6])

    def copy(self):
        return pltpu.make_async_copy(self.part, self.acc, self.sem)

    def begin(self):
        self.copy().start()

    def start(self):
        self.copy().wait()
        self.plane.start(0)

    def block(self, z):
        return self.acc.at[z, self.p.y, self.p.x]

    def column(self):
        return self.acc[:, self.p.y, self.p.x]


class Product(PlaneSum):
    def __init__(self, place, factors, work):
        super().__init__(place, None, work)
        self.factors, self.formed = factors, False

    def begin(self):
        pass

    def start(self):
        if not self.formed:
            self.form()
        self.plane.start(0)

    def form(self):
        self.formed = True
        own, peer, right, peer_right = self.factors
        Z, Y, X, per, _ = self.acc.shape
        h = Z // 2
        size = h * Y * X * per

        def half(k, carry):
            rows = pl.ds(pl.multiple_of(k * size, size), size)
            value = dot(own[rows, :], right[...]) + dot(peer[rows, :], peer_right[...])
            for i in range(h * Y * X):
                place = (k * h + i // (Y * X), i // X % Y, i % X)
                self.acc[place] = value[per * i : per * i + per]
            return carry

        lax.fori_loop(0, Z // h, half, 0)


class PairSum(PlaneSum):
    def __init__(self, place, part, work):
        super().__init__(place, part, work)
        self.core, self.sems = work[7], work[8]

    def copies(self):
        p = self.p
        return (
            remote(
                self.part.at[:, :, :, 1 - p.c], self.core, self.sems.at[0], self.sems.at[1],
                p.at(c=1 - p.c),
            ),
            pltpu.make_async_copy(self.part.at[:, :, :, p.c], self.acc, self.sem),
        )

    def begin(self):
        for copy in self.copies():
            copy.start()

    def start(self):
        p = self.p
        for copy in self.copies():
            copy.wait()

        def place_of(i):
            return i // (p.Y * p.X), lax.rem(i // p.X, p.Y), lax.rem(i, p.X)

        add_blocks(
            lambda i: self.acc.at[place_of(i)], lambda i: self.core.at[place_of(i)],
            p.Z * p.Y * p.X,
        )
        self.plane.start(0)


class Column:
    def __init__(self, part, acc, sem):
        self.copy = pltpu.make_async_copy(part, acc, sem)
        self.acc = acc

    def block(self, z):
        return self.acc.at[z]


class Chain:
    def __init__(self, place, part, held, sems):
        self.p, self.part, self.held, self.sems = place, part, held, sems

    def flow(self, t, side):
        p = self.p
        sem = self.sems.at[side, t]
        target = p.at(z=p.z + 1 - 2 * side)
        return remote(self.part.block(t), self.held.at[side, t], sem.at[0], sem.at[1], target)

    def first(self):
        p = self.p
        for j in range(p.Z - 1):
            @pl.when(p.z == 0)
            def _():
                self.flow(p.Z - 1 - j, 0).start()

            @pl.when(p.z == p.Z - 1)
            def _():
                self.flow(j, 1).start()

    def receive(self, t, side):
        self.flow(t, side).wait_recv()
        mine = self.part.block(t)
        mine[...] = mine[...] + self.held[side, t]

    def forward(self, j):
        p = self.p

        def turn(k, carry):
            side = lax.rem(k + p.z // (p.Z // 2), 2)
            t = (1 - side) * (p.Z - 1 - j) + side * j
            inside = jnp.logical_and(p.z > 0, p.z < p.Z - 1)

            @pl.when(jnp.logical_and(inside, (1 - 2 * side) * (t - p.z) > 0))
            def _():
                self.receive(t, side)
                self.flow(t, side).start()

            return carry

        lax.fori_loop(0, 2, turn, 0)

    def last(self):
        p = self.p

        @pl.when(p.z > 0)
        def _():
            self.receive(p.z, 0)

        @pl.when(p.z < p.Z - 1)
        def _():
            self.receive(p.z, 1)

    def finish(self):
        p = self.p
        for t in range(p.Z):
            for side in (0, 1):
                @pl.when(p.z < t if side == 0 else p.z > t)
                def _():
                    self.flow(t, side).wait_send()


class Direct:
    def __init__(self, place, part, held, sems):
        self.p, self.part, self.held, self.sems = place, part, held, sems

    def over(self, s):
        p = self.p
        z = lax.rem(p.z + s, p.Z)
        sem = self.sems.at[s]
        return remote(self.part.block(z), self.held.at[s - 1], sem.at[0], sem.at[1], p.at(z=z))

    def start(self):
        for s in range(1, self.p.Z):
            self.over(s).start()

    def last(self):
        mine = self.part.block(self.p.z)
        total = mine[...]
        for s in range(1, self.p.Z):
            self.over(s).wait()
            total = total + self.held[s - 1]
        mine[...] = total


def scatter_kernel(sizes, *refs):
    columns_in, factors, small_in, outs, rest = (
        refs[:2], refs[2:8], refs[8], refs[9:14], list(refs[14:])
    )

    def take(n):
        taken = rest[:n]
        del rest[:n]
        return taken

    p = Place(sizes)
    columns = [Column(ref, *take(2)) for ref in columns_in]
    chains = [Chain(p, column, *take(2)) for column in columns]
    own_a, peer_a, own_b, peer_b, hb, peer_hb = factors
    queue = [
        Product(p, (own_a, peer_a, hb, peer_hb), take(7)),
        Product(p, (own_b, peer_b, hb, peer_hb), take(7)),
        PairSum(p, small_in, take(9)),
    ]
    queue = [(part, Direct(p, part, *take(2))) for part in queue]
    greet_near(p, True, False)
    for column in columns:
        column.copy.start()
    queue[0][0].form()
    await_near(p, True)
    for part, _ in queue:
        part.begin()
    for column, chain in zip(columns, chains):
        column.copy.wait()
        chain.first()
    hops = p.Z - 2

    def forward(j):
        if j < hops:
            for chain in chains:
                chain.forward(j)

    stages = [
        lambda part, direct: part.start(),
        lambda part, direct: (part.plane.finish(0), part.plane.start(1)),
        lambda part, direct: (part.plane.finish(1), direct.start()),
    ]
    for k, stage in enumerate(stages):
        for part, direct in queue:
            stage(part, direct)
        forward(k)
    for k in range(len(stages), hops):
        forward(k)
    for chain in chains:
        chain.last()
        chain.finish()
    for _, direct in queue:
        direct.last()
    for part, out in zip(columns + [part for part, _ in queue], outs):
        out[...] = part.block(p.z)[...]


def scatter_call(columns, factors, small, sizes, collective_id):
    Z, F = sizes
    X, Y = F // 4, 2
    chips = Z * X * Y
    dma = pltpu.SemaphoreType.DMA
    parts = [(factors[0].shape[0] // chips, D), (factors[2].shape[0] // chips, D)]
    parts.append(small.shape[1:])
    scratch = []
    for column in columns:
        scratch += [pltpu.VMEM(column.shape, F32), dma]
    for column in columns:
        scratch += [pltpu.VMEM((2, Z) + column.shape[1:], F32), dma((2, Z, 2))]
    for block in parts:
        scratch += plane_scratch(sizes, block) + [dma]
    scratch += [pltpu.VMEM((Z, Y, X) + parts[2], F32), dma((2,))]
    for block in parts:
        scratch += [pltpu.VMEM((Z - 1,) + block, F32), dma((Z, 2))]
    hbm = pl.BlockSpec(memory_space=pl.ANY)
    vmem = pl.BlockSpec(memory_space=pltpu.VMEM)
    return pl.pallas_call(
        functools.partial(scatter_kernel, sizes),
        out_shape=[shape(*block) for block in [column.shape[1:] for column in columns] + parts],
        in_specs=[hbm] * 2 + [vmem] * 6 + [hbm],
        out_specs=[vmem] * 5,
        scratch_shapes=scratch,
        compiler_params=pltpu.CompilerParams(
            collective_id=collective_id, has_side_effects=True, vmem_limit_bytes=60 * 2**20
        ),
        name="scatter",
    )(*columns, *factors, by_place(small, sizes))


def gather_kernel(
    sizes, w_in_ref, w_out_ref, m_in_ref, m_out_ref, params_ref, inner_rows_ref,
    all_ref, blocks_ref, gain_ref, taps_ref, heads_ref, inner_ref,
    mine, keep_sem, z_sems, near, far, across,
):
    p = Place(sizes)
    Z, h = p.Z, p.Z // 2
    greet_near(p, True)
    own = mine.shape[0]
    partner = p.at(c=1 - p.c)
    mine[:, :WIDE] = w_in_ref[:, :WIDE].astype(BF16)
    mine[:, WIDE : WIDE + INNER] = w_out_ref[...].astype(BF16)
    mine[:, WIDE + INNER :] = jnp.concatenate(
        [w_in_ref[:, WIDE:], jnp.zeros((own, 2 * HALF - IN_W - INNER), F32)], axis=1
    ).astype(BF16)
    keep = pltpu.make_async_copy(mine, all_ref.at[p.z, p.y, p.x, p.c], keep_sem)
    keep.start()

    def spot(z, y, x):
        return all_ref.at[z, y, x, p.c]

    def copy(src, dst, sem, device):
        return remote(src, dst, sem.at[0], sem.at[1], device)

    def along_z(z, right, src=None):
        here = spot(z, p.y, p.x)
        target = p.at(z=p.z + 1 if right else p.z - 1)
        return copy(here if src is None else src, here, z_sems.at[0 if right else 1, z], target)

    def near_copies(z, src=None):
        here = spot(z, p.y, p.x)
        src = here if src is None else src
        found = [copy(src, here, near.at[z, 0], p.at(y=1 - p.y))]
        for s in range(1, p.X):
            found.append(copy(src, here, near.at[z, s], p.at(x=p.other_x(s))))
        return found

    def near_arrivals(z):
        found = [(z, 1 - p.y, p.x, near.at[z, 0])]
        for s in range(1, p.X):
            found.append((z, p.y, lax.rem(p.x + p.X - s, p.X), near.at[z, s]))
        return found

    def far_copies(z):
        low, high = [], []
        for s in range(1, p.X):
            x = p.other_x(s)
            there = spot(z, p.y, x)
            low.append(copy(there, there, far.at[z, s], p.at(y=1 - p.y)))
            there = spot(z, 1 - p.y, p.x)
            high.append(copy(there, there, far.at[z, s], p.at(x=x)))
        return low, high

    def far_arrivals(z):
        low = [(z, 1 - p.y, p.other_x(s), far.at[z, s]) for s in range(1, p.X)]
        high = [
            (z, 1 - p.y, lax.rem(p.x + p.X - s, p.X), far.at[z, s]) for s in range(1, p.X)
        ]
        return low, high

    def to_partner(z, y, x, src=None):
        here = spot(z, y, x)
        return copy(here if src is None else src, here, across.at[z, y, x], partner)

    def await_block(z, y, x, sem):
        here = spot(z, y, x)
        copy(here, here, sem, partner).wait_recv()
        to_partner(z, y, x).start()

    def start_all(copies):
        for c in copies:
            c.start()

    @pl.when(p.z < Z - 1)
    def _():
        along_z(p.z, True, mine).start()

    @pl.when(p.z > 0)
    def _():
        along_z(p.z, False, mine).start()

    start_all(near_copies(p.z, mine))
    to_partner(p.z, p.y, p.x, mine).start()
    spread_vectors(params_ref, inner_rows_ref, gain_ref, taps_ref, heads_ref, inner_ref)
    spread_moments(m_in_ref, m_out_ref, blocks_ref)

    def visit(right, z):
        await_block(z, p.y, p.x, z_sems.at[0 if right else 1, z])

        @pl.when(p.z < Z - 1 if right else p.z > 0)
        def _():
            along_z(z, right).start()

        start_all(near_copies(z))

    def by_distance(low, high):
        for j in range(1, Z):
            @pl.when(p.z - j >= 0)
            def _():
                low(p.z - j)

            @pl.when(p.z + j < Z)
            def _():
                high(p.z + j)

    by_distance(lambda z: visit(True, z), lambda z: visit(False, z))

    def relay(z):
        for block in near_arrivals(z):
            await_block(*block)
        low, high = far_copies(z)

        @pl.when(z < h)
        def _():
            start_all(low)

        @pl.when(z >= h)
        def _():
            start_all(high)

    relay(p.z)
    by_distance(relay, relay)

    def settle(z):
        low, high = far_arrivals(z)

        @pl.when(z < h)
        def _():
            for block in low:
                await_block(*block)

        @pl.when(z >= h)
        def _():
            for block in high:
                await_block(*block)

    settle(p.z)
    by_distance(settle, settle)
    keep.wait()

    def finish(z, carry):
        for c in near_copies(z):
            c.wait_send()
        low, high = far_copies(z)

        @pl.when(z < h)
        def _():
            for c in low:
                c.wait_send()

        @pl.when(z >= h)
        def _():
            for c in high:
                c.wait_send()

        @pl.when(jnp.logical_and(z <= p.z, p.z < Z - 1))
        def _():
            along_z(z, True).wait_send()

        @pl.when(jnp.logical_and(z >= p.z, p.z > 0))
        def _():
            along_z(z, False).wait_send()

        for y in range(p.Y):
            for x in range(p.X):
                to_partner(z, y, x).wait_send()
                theirs = all_ref.at[z, y, x, 1 - p.c]
                copy(theirs, theirs, across.at[z, y, x], partner).wait_recv()

        return carry

    lax.fori_loop(0, Z, finish, 0)


def column_of(row):
    return jnp.broadcast_to(row, (128, 128)).T


def spread_vectors(params_ref, inner_rows_ref, gain_ref, taps_ref, heads_ref, inner_ref):
    row = D // 128
    gain_ref[...] = beside(*[params_ref[j : j + 1] for j in range(row)])
    for k in range(KCONV + 1):
        for j in range(CONVCH // 128):
            taps_ref[k, 128 * j : 128 * j + 128] = column_of(params_ref[row : row + 1])
            row += 1
    heads = column_of(params_ref[row : row + 1])
    heads_ref[0] = heads[:HEADS]
    heads_ref[1] = -jnp.exp(heads[HEADS : 2 * HEADS])
    heads_ref[2] = heads[2 * HEADS : 3 * HEADS]
    for j in range(INNER // 128):
        inner_ref[128 * j : 128 * j + 128] = column_of(inner_rows_ref[j : j + 1])


def cuts_of(count):
    widths = [(0, INNER), (INNER, CONV_A), (INNER + CONV_A, CONVCH - CONV_A)]
    return [(start, width, width // count) for start, width in widths], INNER // count


def first_of(d, width, count):
    return d % 2 * (width // 2) + d // 2 * (width // count)


def spread_moments(m_in_ref, m_out_ref, blocks_ref):
    count, own, lanes_in_block = blocks_ref.shape
    ins, outs = cuts_of(count)
    step = m_in_ref[:, WIDE:]
    used = sum(each for _, _, each in ins) + outs + HEADS
    for d in range(count):
        pieces = []
        for start, width, each in ins:
            at = start + first_of(d, width, count)
            pieces.append(m_in_ref[:, at : at + each])
        at = first_of(d, INNER, count)
        pieces += [m_out_ref[:, at : at + outs], step]
        blocks_ref[d] = beside(*pieces, jnp.zeros((own, lanes_in_block - used), F32))


def gather_call(weight_in, weight_out, moment_in, moment_out, params, sizes, collective_id):
    Z, F = sizes
    X, Y = F // 4, 2
    own = weight_in.shape[0]
    count = Z * F
    inner_rows = params[-INNER:].reshape(-1, 128)
    params = jnp.pad(params, (0, -params.shape[0] % 128)).reshape(-1, 128)
    vmem = pl.BlockSpec(memory_space=pltpu.VMEM)
    hbm = pl.BlockSpec(memory_space=pl.ANY)
    whole_weights, blocks, *vectors = pl.pallas_call(
        functools.partial(gather_kernel, sizes),
        out_shape=[
            shape(Z, Y, X, 2, own, 2 * HALF, dtype=BF16), shape(count, own, 256), shape(1, D),
            shape(KCONV + 1, CONVCH, CHUNK), shape(3, HEADS, CHUNK), shape(INNER, CHUNK),
        ],
        in_specs=[vmem] * 6,
        out_specs=[hbm] + [vmem] * 5,
        scratch_shapes=[
            pltpu.VMEM((own, 2 * HALF), BF16), pltpu.SemaphoreType.DMA, pltpu.SemaphoreType.DMA((2, Z, 2)),
            pltpu.SemaphoreType.DMA((Z, X, 2)), pltpu.SemaphoreType.DMA((Z, X, 2)),
            pltpu.SemaphoreType.DMA((Z, Y, X, 2)),
        ],
        compiler_params=pltpu.CompilerParams(
            collective_id=collective_id, has_side_effects=True, vmem_limit_bytes=60 * 2**20
        ),
        name="weights_gather",
    )(weight_in, weight_out, moment_in, moment_out, params, inner_rows)
    return whole_weights.reshape(D, 2 * HALF), blocks, vectors


def gram_rows(slab, row):
    high, low = split(slab)
    left = above(high, low, high)[:, 128 * row : 128 * row + 128]
    return dot_tn(left, above(high, high, low)[:, 128 * row :])


def pack_gram(targets, slab):
    Z, Y, X, per, _ = targets[0].shape
    rows = above(*[
        beside(gram_rows(slab, i), gram_rows(slab, D // 128 - 1 - i)) for i in range(D // 256)
    ])
    if Z * Y * X * per > rows.shape[0]:
        rows = above(rows, jnp.zeros((Z * Y * X * per - rows.shape[0], rows.shape[1]), F32))
    at = 0
    for target in targets:
        cols = slice(at, at + target.shape[4])
        for i in range(Z * Y * X):
            target[i // (Y * X), i // X % Y, i % X] = rows[per * i : per * i + per, cols]
        at += target.shape[4]


def unpack_gram(gram, packed):
    Z, Y, X, _, _ = packed[0].shape
    rows = beside(*[
        above(*[part[i // (Y * X), i // X % Y, i % X] for i in range(Z * Y * X)])
        for part in packed
    ])
    for i in range(D // 256):
        pair = rows[128 * i : 128 * i + 128]
        wide_part, j = D - 128 * i, D // 128 - 1 - i
        for row, part in ((i, pair[:, :wide_part]), (j, pair[:, wide_part:])):
            gram[128 * row : 128 * row + 128, 128 * row :] = part
            for k in range(row + 1, D // 128):
                at = 128 * (k - row)
                gram[128 * k : 128 * k + 128, 128 * row : 128 * row + 128] = part[
                    :, at : at + 128
                ].T


BEHIND = 2


class AllSum:
    def __init__(self, place, work):
        self.p = place
        self.total, self.acc, self.core, self.core_sems = work[0], work[1], work[7], work[8]
        self.held, self.z_sems, self.back_sems = work[9:12]
        self.plane = Plane(place, *work[1:7])
        self.steps = [
            self.pair, self.second, self.cross, self.turn, self.spread, self.spread_on, self.done,
        ]

    def to_core(self):
        p = self.p
        return remote(
            self.total, self.core, self.core_sems.at[0], self.core_sems.at[1], p.at(c=1 - p.c)
        )

    def pair(self):
        p = self.p
        self.to_core().wait()

        def place_of(i):
            return i // (p.Y * p.X), lax.rem(i // p.X, p.Y), lax.rem(i, p.X)

        add_blocks(
            lambda i: self.acc.at[place_of(i)], lambda i: self.core.at[place_of(i)],
            p.Z * p.Y * p.X,
        )
        self.plane.start(0)

    def second(self):
        self.plane.finish(0)
        self.plane.start(1)

    def over(self, s):
        p = self.p
        z = lax.rem(p.z + s, p.Z)
        sem = self.z_sems.at[0, s]
        return remote(
            self.acc.at[z, p.y, p.x], self.held.at[s - 1], sem.at[0], sem.at[1], p.at(z=z)
        )

    def cross(self):
        self.plane.finish(1)
        for s in range(1, self.p.Z):
            self.over(s).start()

    def back(self, s, mine):
        p = self.p
        sem = self.z_sems.at[1, s]
        z = p.z if mine else lax.rem(p.z + p.Z - s, p.Z)
        ref = self.total.at[z, p.y, p.x]
        return remote(ref, ref, sem.at[0], sem.at[1], p.at(z=lax.rem(p.z + s, p.Z)))

    def turn(self):
        p = self.p
        for s in range(1, p.Z):
            self.over(s).wait()
        result = self.acc[p.z, p.y, p.x]
        for s in range(1, p.Z):
            result = result + self.held[s - 1]
        self.total[p.z, p.y, p.x] = result
        for s in range(1, p.Z):
            self.back(s, True).start()

    def planes(self, stage, mine):
        p, total, h = self.p, self.total, self.p.Z // 2
        low, high = pl.ds(0, h), pl.ds(h, p.Z - h)
        found = []
        for s in range(1, p.X):
            sem = self.back_sems.at[stage * p.X + s]
            x = p.x if mine else lax.rem(p.x + p.X - s, p.X)
            ref = total.at[high, p.y, x] if stage == 0 else total.at[low, :, x]
            found.append(remote(ref, ref, sem.at[0], sem.at[1], p.at(x=p.other_x(s))))
        sem = self.back_sems.at[stage * p.X]
        y = p.y if mine else 1 - p.y
        ref = total.at[low, y, p.x] if stage == 0 else total.at[high, y]
        found.append(remote(ref, ref, sem.at[0], sem.at[1], p.at(y=1 - p.y)))
        return found

    def arrive(self, copies):
        for mine, theirs in copies:
            mine.wait_send()
            theirs.wait_recv()

    def spread(self):
        self.arrive([(self.back(s, True), self.back(s, False)) for s in range(1, self.p.Z)])
        for copy in self.planes(0, True):
            copy.start()

    def spread_on(self):
        self.arrive(zip(self.planes(0, True), self.planes(0, False)))
        for copy in self.planes(1, True):
            copy.start()

    def done(self):
        self.arrive(zip(self.planes(1, True), self.planes(1, False)))


def all_sum_scratch(sizes, block):
    Z, X, Y = sizes[0], sizes[1] // 4, 2
    dma = pltpu.SemaphoreType.DMA
    return [pltpu.VMEM((Z, Y, X) + block, F32)] + plane_scratch(sizes, block) + [
        pltpu.VMEM((Z, Y, X) + block, F32), dma((2,)), pltpu.VMEM((Z - 1,) + block, F32),
        dma((2, Z, 2)), dma((2 * X, 2)),
    ]


def put_left(left, value, rows):
    high, low = split(value)
    left[rows] = beside(high, low, high)


def put_right(right, value, row):
    high, low = split(value)
    size = value.shape[0]
    right[row : row + size] = high
    right[D + row : D + row + size] = high
    right[2 * D + row : 2 * D + row + size] = low


TILE = 256


def symmetric_product(target, left, right):
    for i in range(D // TILE):
        rows = slice(TILE * i, TILE * i + TILE)
        part = dot(left[rows], right[:, TILE * i :])
        target[rows, TILE * i :] = part
        for j in range(i + 1, D // TILE):
            at = TILE * (j - i)
            target[TILE * j : TILE * j + TILE, rows] = part[:, at : at + TILE].T


def iterate(gram, square, factor, left, right, slab, slab_left):
    tiles = [slice(TILE * i, TILE * i + TILE) for i in range(D // TILE)]
    row = lax.broadcasted_iota(jnp.int32, (TILE, D), 0)
    col = lax.broadcasted_iota(jnp.int32, (TILE, D), 1)
    diagonals = [(row + TILE * i == col) for i in range(D // TILE)]
    trace = jnp.zeros((8, D), F32)
    for rows, diagonal in zip(tiles, diagonals):
        trace = trace + fold(jnp.where(diagonal, gram[rows], 0.0))
    trace = jnp.sum(jnp.sum(trace, axis=0, keepdims=True), axis=1, keepdims=True)
    scale = 1.0 / (jnp.sqrt(trace) + 1e-07)
    for rows in tiles:
        gram[rows] = gram[rows] * (scale * scale)
    slab[...] = slab[...] * scale

    def step(iteration, carry):
        for i, rows in enumerate(tiles):
            value = gram[rows]
            put_left(left, value, rows)
            put_right(right, value, TILE * i)
        symmetric_product(square, left, right)
        for i, rows in enumerate(tiles):
            value = COEF_B * gram[rows] + COEF_C * square[rows]
            put_right(right, value + jnp.where(diagonals[i], COEF_A, 0.0), TILE * i)
        put_left(slab_left, slab[...], slice(None))
        slab[...] = dot(slab_left[...], right[...])
        symmetric_product(factor, left, right)
        for rows in tiles:
            put_left(left, factor[rows], rows)
        symmetric_product(gram, left, right)
        return carry

    lax.fori_loop(0, ITERS - 1, step, 0)
    for i, rows in enumerate(tiles):
        put_right(right, gram[rows], TILE * i)
    first = slab[...]
    put_left(slab_left, first, slice(None))
    once = dot(slab_left[...], right[...])
    put_left(slab_left, once, slice(None))
    slab[...] = COEF_A * first + COEF_B * once + COEF_C * dot(slab_left[...], right[...])


def update_kernel(
    sizes, gate_ref, conv_a_ref, conv_b_ref, out_ref, small_ref, old_ref, moved_ref, smalls_ref, spread_ref,
    give, given, give_sems, messages, smalls, mats, left, right, slab, slab_left,
    swap_send, swap_recv, local, *work,
):
    p = Place(sizes)
    count = p.Z * p.F
    own = D // count
    gates = gate_ref.shape[0]
    ins = gates + conv_a_ref.shape[0] + conv_b_ref.shape[0]
    greet_all(p, False)
    swaps = [
        Swap(p, src, dst, swap_send.at[k], swap_recv.at[k], local.at[k], same, narrow)
        for k, (src, dst, same, narrow) in enumerate([
            (small_ref, smalls, True, None), (messages.at[0], moved_ref, False, None),
            (messages.at[1], spread_ref, False, -(-2 * gates // 128) * 128),
        ])
    ]
    old = old_ref[...].T
    new_in = above(gate_ref[...], conv_a_ref[...], conv_b_ref[...])
    new_out = out_ref[...]

    def push(gradient, moment):
        return gradient + MOMENTUM * (MOMENTUM * moment + gradient)

    push_in = push(new_in, old[:ins])
    push_out = above(push(new_out, old[ins : ins + gates]), jnp.zeros((ins - gates, D), F32))
    in_core = p.c == 0
    give[...] = jnp.where(in_core, push_out, push_in)
    slab[:ins] = jnp.where(in_core, push_in, push_out)
    partner = p.at(c=1 - p.c)
    pieces = [AllSum(p, work[:12]), AllSum(p, work[12:])]
    pack_gram([piece.total for piece in pieces], give[...])
    await_all(p)
    for piece in pieces:
        piece.to_core().start()
    exchange = remote(give, given, give_sems.at[0], give_sems.at[1], partner)
    exchange.start()
    swaps[0].start()
    pack_gram([piece.acc for piece in pieces], slab[:ins])

    def store_messages(k, turned):
        turned = beside(turned, jnp.zeros((D, 256 - turned.shape[1]), F32)) if (
            turned.shape[1] < 256) else turned
        for d in range(count):
            messages[k, d] = turned[own * d : own * d + own]

    steps = len(pieces[0].steps)
    for k in range(steps + BEHIND):
        for which, piece in enumerate(pieces):
            if 0 <= k - BEHIND * which < steps:
                piece.steps[k - BEHIND * which]()
        if k == 0:
            store_messages(0, above(new_in, new_out).T)
    exchange.wait()
    swaps[0].wait()
    swaps[1].start()
    smalls_ref[...] = smalls[...]
    rows = smalls[...].reshape(-1, 128)
    new_step = beside(*[rows[HEADS * j : HEADS * j + HEADS] for j in range(D // 128)])
    push_step = push(new_step, old_ref[...].T[ins + gates : ins + gates + HEADS])
    push_step = jnp.where(in_core, push_step, 0.0)
    mine, theirs = slab[:ins], given[...]
    slab_in = above(mine, theirs, push_step)
    slab_out = above(theirs[:gates], mine[:gates], jnp.zeros((2 * (ins - gates) + HEADS, D), F32))
    slab[: 2 * ins + HEADS] = jnp.where(in_core, slab_in, slab_out)
    slab[2 * ins + HEADS :] = jnp.zeros((slab.shape[0] - 2 * ins - HEADS, D), F32)
    gram = mats.at[0]
    unpack_gram(gram, [piece.total for piece in pieces])
    step_high, step_low = split(push_step)
    step_left = above(step_high, step_low, step_high)
    gram[...] = gram[...] + dot_tn(step_left, above(step_high, step_high, step_low))
    iterate(gram, mats.at[1], mats.at[2], left, right, slab, slab_left)
    store_messages(1, slab[...].T)
    swaps[2].start()
    swaps[1].wait()
    swaps[2].wait()


def update_call(parts, small, old, sizes, collective_id):
    count = sizes[0] * sizes[1]
    own = D // count
    chips = count // 2
    ins = sum(part.shape[0] for part in parts[:3])
    per = -(-(D // 2) // (8 * chips)) * 8
    blocks = [(per, 512), (per, D + 128 - 512)]
    vmem = pl.BlockSpec(memory_space=pltpu.VMEM)
    hbm = pl.BlockSpec(memory_space=pl.ANY)
    dma = pltpu.SemaphoreType.DMA
    return pl.pallas_call(
        functools.partial(update_kernel, sizes),
        out_shape=[
            shape(count, own, 256), shape(count, *small.shape), shape(count, own, 256),
        ],
        in_specs=[vmem] * 6,
        out_specs=[hbm, vmem, hbm],
        scratch_shapes=[
            pltpu.VMEM((ins, D), F32), pltpu.VMEM((ins, D), F32), dma((2,)),
            pltpu.VMEM((2, count, own, 256), F32), pltpu.VMEM((count,) + small.shape, F32),
            pltpu.VMEM((3, D, D), F32),
            pltpu.VMEM((D, 3 * D), BF16), pltpu.VMEM((3 * D, D), BF16),
            pltpu.VMEM((256, D), F32), pltpu.VMEM((256, 3 * D), BF16),
            dma((3, count)), dma((3, count)), dma((3,)),
        ]
        + all_sum_scratch(sizes, blocks[0])
        + all_sum_scratch(sizes, blocks[1]),
        compiler_params=pltpu.CompilerParams(
            collective_id=collective_id, has_side_effects=True, vmem_limit_bytes=56 * 2**20
        ),
        name="update",
    )(*parts, small, old)


def finish_kernel(
    moved_ref, spread_ref, step_ref, w_in_ref, w_out_ref, m_in_ref, m_out_ref,
    g_in_ref, g_out_ref, new_m_in_ref, new_m_out_ref, new_w_in_ref, new_w_out_ref,
):
    count = moved_ref.shape[0]
    cuts, outs = cuts_of(count)
    ins = sum(each for _, _, each in cuts)
    decay = 1.0 - MATRIX_RATE * WEIGHT_DECAY
    order = [(2 * chip + core, core) for core in range(2) for chip in range(count // 2)]
    at = 0
    for start, width, each in cuts:
        cols = slice(start, start + width)
        g_in_ref[:, cols] = beside(*[moved_ref[d, :, at : at + each] for d, _ in order])
        new_w_in_ref[:, cols] = beside(*[
            spread_ref[d - core, :, ins * core + at : ins * core + at + each] for d, core in order
        ])
        at += each
    g_in_ref[:, WIDE:] = step_ref[...]
    new_w_in_ref[:, WIDE:] = spread_ref[0, :, 2 * ins : 2 * ins + HEADS]
    g_out_ref[...] = beside(*[moved_ref[d, :, ins : ins + outs] for d, _ in order])
    new_w_out_ref[...] = beside(*[
        spread_ref[d - core + 1, :, outs * core : outs * core + outs] for d, core in order
    ])
    for wide_side, g_ref, m_ref, w_ref, new_m_ref, new_w_ref in (
        (IN_W, g_in_ref, m_in_ref, w_in_ref, new_m_in_ref, new_w_in_ref),
        (INNER, g_out_ref, m_out_ref, w_out_ref, new_m_out_ref, new_w_out_ref),
    ):
        new_m_ref[...] = MOMENTUM * m_ref[...] + g_ref[...]
        rate = MATRIX_RATE * 0.2 * math.sqrt(max(D, wide_side))
        new_w_ref[...] = w_ref[...] * decay - rate * new_w_ref[...]


def finish_call(moved, spread, step_rows, weight_in, weight_out, moment_in, moment_out):
    vmem = pl.BlockSpec(memory_space=pltpu.VMEM)
    return pl.pallas_call(
        finish_kernel,
        out_shape=[shape(*weight_in.shape), shape(*weight_out.shape)] * 3,
        in_specs=[vmem] * 7,
        out_specs=[vmem] * 6,
        name="finish",
    )(moved, spread, step_rows, weight_in, weight_out, moment_in, moment_out)


def shards(
    inputs, cotangent, weight_in, weight_out, small_params, moment_in, moment_out, moment_small
):
    sizes = (lax.axis_size("dp"), lax.axis_size("fsdp"))
    own = weight_in.shape[0]
    weights, blocks, vectors = gather_call(
        weight_in, weight_out, moment_in, moment_out, small_params, sizes, 0
    )
    output, dx, columns, factors, small, old = block_and_gradients(
        inputs[0], cotangent[0], weights, vectors, blocks, sizes, (3, 4)
    )
    new_out, new_gate, new_conv_a, new_conv_b, new_small = scatter_call(
        columns, factors, small, sizes, 1
    )
    moved, smalls, spread = update_call(
        (new_gate, new_conv_a, new_conv_b, new_out), new_small, old.reshape(D, 256), sizes, 2
    )
    smalls = smalls.reshape(-1)
    grad_small = smalls[HEADS * D : HEADS * D + SMALL]
    new_step = smalls[: HEADS * D].reshape(D // 128, HEADS, 128).transpose(1, 0, 2)
    first_row = (lax.axis_index("dp") * sizes[1] + lax.axis_index("fsdp")) * own
    step_rows = lax.dynamic_slice_in_dim(new_step.reshape(HEADS, D), first_row, own, 1).T
    grad_in, grad_out, new_moment_in, new_moment_out, new_weight_in, new_weight_out = finish_call(
        moved, spread, step_rows, weight_in, weight_out, moment_in, moment_out
    )
    new_moment_small = MOMENTUM * moment_small + grad_small
    new_small_params = small_params - SMALL_RATE * new_moment_small
    return (
        output[None],
        dx[None],
        grad_in,
        grad_out,
        grad_small,
        new_moment_in,
        new_moment_out,
        new_moment_small,
        new_weight_in,
        new_weight_out,
        new_small_params,
    )


def solution(mesh):
    return jax.shard_map(
        shards,
        mesh=mesh,
        in_specs=(
            P(("dp", "fsdp"), None, None),
            P(("dp", "fsdp"), None, None),
            P(("dp", "fsdp"), None),
            P(("dp", "fsdp"), None),
            P(),
            P(("dp", "fsdp"), None),
            P(("dp", "fsdp"), None),
            P(),
        ),
        out_specs=(
            P(("dp", "fsdp"), None, None),
            P(("dp", "fsdp"), None, None),
            P(("dp", "fsdp"), None),
            P(("dp", "fsdp"), None),
            P(),
            P(("dp", "fsdp"), None),
            P(("dp", "fsdp"), None),
            P(),
            P(("dp", "fsdp"), None),
            P(("dp", "fsdp"), None),
            P(),
        ),
        check_vma=False,
    )
```

```python
import functools
import math

import jax
import jax.numpy as jnp
from jax import lax
from jax.experimental import pallas as pl
from jax.experimental.pallas import tpu as pltpu
from jax.sharding import PartitionSpec as P

D = 768
HEADS = 24
HEAD_DIM = 64
NSTATE = 128
KCONV = 4
LEN = 1024
ITERS = 5
INNER = 1536
CONVCH = 1792
IN_W = 3352
SMALL = 11336
WIDE = INNER + CONVCH
TAIL_SUMS = 1664 - 2 * HEADS
STEP = 32
CONV_A = 768
HALF = 2560
OUT_AT = WIDE - HALF
STEP_AT = OUT_AT + INNER

MOMENTUM = 0.95
MATRIX_RATE = 0.15
WEIGHT_DECAY = 0.1
SMALL_RATE = 0.01
EPSILON = 1e-05
COEF_A = 3.4445
COEF_B = -4.775
COEF_C = 2.0315

F32 = jnp.float32
BF16 = jnp.bfloat16
CHUNK = 128
STRIP = 256
PER = STRIP // CHUNK
STRIPS = LEN // STRIP
GRAD_TILE = 256
GROUP = 4


def dot(a, b):
    return lax.dot_general(a, b, (((1,), (0,)), ((), ())), preferred_element_type=F32)


def dot_nt(a, b):
    return lax.dot_general(a, b, (((1,), (1,)), ((), ())), preferred_element_type=F32)


def dot_tn(a, b):
    return lax.dot_general(a, b, (((0,), (0,)), ((), ())), preferred_element_type=F32)


def split(v):
    high = v.astype(BF16)
    return high, (v - high.astype(F32)).astype(BF16)


def beside(*parts):
    return jnp.concatenate(parts, axis=1)


def above(*parts):
    return jnp.concatenate(parts, axis=0)


def right_pair(b):
    high, low = split(b)
    return above(beside(high, low), beside(high, jnp.zeros_like(low)))


def three_pass(a, pair):
    high, low = split(a)
    both = dot(beside(high, low), pair)
    half = both.shape[1] // 2
    return both[:, :half] + both[:, half:]


def exact_sum(a, ones):
    high = a.astype(BF16)
    rest = a - high.astype(F32)
    mid = rest.astype(BF16)
    low = (rest - mid.astype(F32)).astype(BF16)
    return dot(beside(high, mid, low), above(ones, ones, ones))


def lane_sums(a):
    high = a.astype(BF16)
    rest = a - high.astype(F32)
    mid = rest.astype(BF16)
    low = (rest - mid.astype(F32)).astype(BF16)
    parts = beside(high, mid, low)
    return dot_nt(jnp.ones((8, parts.shape[1]), BF16), parts)


def stack_left(a):
    high, low = split(a)
    return above(beside(high, high), beside(low, jnp.zeros_like(low)))


def fold(rows):
    total = rows[0:8]
    for i in range(1, rows.shape[0] // 8):
        total = total + rows[8 * i : 8 * i + 8]
    return total


def row_sum(rows):
    return jnp.sum(fold(rows), axis=0, keepdims=True)


def upper():
    row = lax.broadcasted_iota(jnp.int32, (CHUNK, CHUNK), 0)
    col = lax.broadcasted_iota(jnp.int32, (CHUNK, CHUNK), 1)
    return col >= row


def softplus(v):
    return jnp.maximum(v, 0.0) + jnp.log1p(jnp.exp(-jnp.abs(v)))


def rates_of(raw, heads_ref, ones):
    steps = softplus(raw + heads_ref[0])
    logs = exact_sum(steps * heads_ref[1], ones)
    last = jnp.broadcast_to(logs[:, CHUNK - 1 : CHUNK], logs.shape)
    columns = above(logs, jnp.zeros((CHUNK - HEADS, CHUNK), F32)).T
    return steps, logs, columns, jnp.exp(logs), jnp.exp(last - logs), jnp.exp(last)


def silu(v):
    return v * jax.nn.sigmoid(v)


def wide(v):
    return beside(*([v] * PER))


def strip_at(s):
    return pl.ds(pl.multiple_of(s * STRIP, STRIP), STRIP)


def half_rows(rows, c):
    return pl.ds(pl.multiple_of(c * (rows // 2), rows // 2), rows // 2)


class Box:
    def __init__(self, box, dst, sems, partner):
        self.box, self.dst, self.sems, self.partner = box, dst, sems, partner

    def copy(self, s):
        sem = self.sems.at[s]
        return remote(
            self.box.at[lax.rem(s, 2)], self.dst(s), sem.at[0], sem.at[1], self.partner
        )

    def fill(self, s, value, back=False):
        @pl.when(pl.program_id(0) > 1)
        def _():
            self.copy(s + 2 if back else s - 2).wait_send()

        self.box[lax.rem(s, 2)] = value
        self.copy(s).start()

    def finish(self, back=False):
        for s in range(2):
            self.copy(s if back else STRIPS - 1 - s).wait_send()
        for s in range(STRIPS):
            self.copy(s).wait_recv()


def forward_kernel(
    sizes, x_ref, back_ref, first_ref, second_ref, gain_ref, taps_in, heads_ref, inner_in,
    blocks_ref, whole_back_ref,
    out_ref, hb_ref, cin_ref, c_ref, raw_ref, s_ref, own_normed_ref,
    dy_ref, dgate_ref, own_dgate_ref, dlogs_ref, tail_sums_ref, moved_ref,
    peer_normed_ref, peer_dgate_ref, peer_hb_ref, peer_back_ref,
    act, z, mixed, dnormed, state, tail, turned, dskip, dinner, normed_ref,
    taps_ref, inner_ref, load_sems, box_normed, box_dgate, box_hb, box_sems, back_sems, *work,
):
    p = Place(sizes)
    swap = Swap(p, blocks_ref, moved_ref, *work)
    partner = p.at(c=1 - p.c)
    strip = pl.program_id(0)
    back_copy = remote(
        whole_back_ref, peer_back_ref, back_sems.at[0], back_sems.at[1], partner
    )
    boxes = [
        Box(box, lambda s, ref=ref: ref.at[:, strip_at(s)], box_sems.at[k], partner)
        for k, (box, ref) in enumerate(
            [(box_normed, peer_normed_ref), (box_dgate, peer_dgate_ref)]
        )
    ]
    boxes.append(Box(box_hb, lambda s: peer_hb_ref.at[strip_at(s)], box_sems.at[2], partner))

    @pl.when(strip == 0)
    def _():
        loads = [
            pltpu.make_async_copy(taps_in, taps_ref, load_sems.at[0]),
            pltpu.make_async_copy(inner_in, inner_ref, load_sems.at[1]),
        ]
        for load in loads:
            load.start()
        greet_all(p)
        back_copy.start()
        swap.start()
        state[...] = jnp.zeros_like(state)
        tail[...] = jnp.zeros_like(tail)
        dskip[...] = jnp.zeros_like(dskip)
        dinner[...] = jnp.zeros_like(dinner)
        for i in range(HALF // 256):
            part = slice(256 * i, 256 * i + 256)
            turned[0, part] = first_ref[:, part].T
            turned[1, part] = second_ref[:, part].T
        for load in loads:
            load.wait()

    x = x_ref[...].astype(F32)
    scaled = x * lax.rsqrt(jnp.mean(x * x, axis=-1, keepdims=True) + EPSILON) * gain_ref[...]
    hb = scaled.astype(BF16)
    hb_ref[...] = hb
    boxes[2].fill(strip, hb)
    back = back_ref[...]
    raw_ref[...] = dot_nt(turned[1, STEP_AT : STEP_AT + STEP], hb)

    lane = lax.broadcasted_iota(jnp.int32, (64, CHUNK), 1)

    def later(cols, steps, before):
        turned_cols = [before] + [pltpu.roll(col, steps, 1) for col in cols]
        pairs = zip(turned_cols[:-1], turned_cols[1:])
        return [jnp.where(lane < steps, a, b) for a, b in pairs], turned_cols[-1]

    def conv_tile(i):
        rows = slice(64 * i, 64 * i + 64)
        cur = cin_ref[rows]
        cols = [cur[:, CHUNK * j : CHUNK * j + CHUNK] for j in range(PER)]
        taps = [taps_ref[k, rows] for k in range(KCONV + 1)]
        ones_late, tail[0, rows] = later(cols, 1, tail[0, rows])
        early = [taps[1] * a + taps[0] * b for a, b in zip(cols, ones_late)]
        twos_late, tail[1, rows] = later(early, 2, tail[1, rows])
        total = beside(*[
            taps[4] + c + taps[2] * b + taps[3] * a for a, b, c in zip(cols, ones_late, twos_late)
        ])
        c_ref[rows] = total
        act[rows] = total * jax.nn.sigmoid(total)

    def project(i):
        start = INNER + 256 * i
        rows = turned[start // HALF, start % HALF : start % HALF + 256]
        cin_ref[256 * i : 256 * i + 256] = dot_nt(rows, hb)

    project(0)
    for i in range(CONVCH // 256):
        if i + 1 < CONVCH // 256:
            project(i + 1)
        if i < INNER // 256:
            part = slice(256 * i, 256 * i + 256)
            z[part] = dot_nt(turned[0, part], hb)
            dnormed[part] = dot_nt(turned[1, OUT_AT + 256 * i : OUT_AT + 256 * i + 256], back)
        for q in range(4):
            conv_tile(4 * i + q)
    causal = upper()
    ones = causal.astype(F32).astype(BF16)

    def chunk(j, carry):
        cols = pl.ds(pl.multiple_of(j * CHUNK, CHUNK), CHUNK)
        steps, logs, columns, grown, to_end, through = rates_of(
            raw_ref[0:HEADS, cols], heads_ref, ones
        )
        in_map = act[INNER : INNER + NSTATE, cols].T
        in_pair = right_pair(in_map)
        out_pair = right_pair(act[INNER + NSTATE :, cols])
        scores = three_pass(in_map, out_pair)
        for g in range(HEADS // GROUP):
            rows = slice(g * GROUP * HEAD_DIM, (g + 1) * GROUP * HEAD_DIM)
            held = state[rows]
            s_ref[j, rows] = held
            across = three_pass(held, out_pair)
            ending, kept = [], []
            for q in range(GROUP):
                h = g * GROUP + q
                mine = slice(h * HEAD_DIM, (h + 1) * HEAD_DIM)
                values = act[mine, cols]
                fed = values * steps[h : h + 1]
                gaps = logs[h : h + 1] - jnp.broadcast_to(columns[:, h : h + 1], (CHUNK, CHUNK))
                weights = scores * jnp.where(causal, jnp.exp(gaps), 0.0)
                both = dot(stack_left(fed), above(*split(weights)))
                y = both[:HEAD_DIM] + both[HEAD_DIM:]
                y = y + across[q * HEAD_DIM : (q + 1) * HEAD_DIM] * grown[h : h + 1]
                mixed[mine, cols] = y + heads_ref[2][h : h + 1] * values
                ending.append(fed * to_end[h : h + 1])
                kept.append(jnp.broadcast_to(through[h : h + 1], (HEAD_DIM, CHUNK)))
            state[rows] = held * above(*kept) + three_pass(above(*ending), in_pair)
        return carry

    lax.fori_loop(0, PER, chunk, 0)

    def mean_tile(h, totals):
        rows = pl.ds(pl.multiple_of(h * HEAD_DIM, HEAD_DIM), HEAD_DIM)
        gate = z[rows, :]
        opened = mixed[rows, :] * (gate * jax.nn.sigmoid(gate))
        gained = dnormed[rows, :] * wide(inner_ref[rows, :]) * opened
        return totals[0] + fold(opened * opened), totals[1] + fold(gained)

    nothing = jnp.zeros((8, STRIP), F32)
    squares, gains = lax.fori_loop(0, HEADS, mean_tile, (nothing, nothing))
    mean = jnp.sum(squares, axis=0, keepdims=True) * (1.0 / INNER)
    r = lax.rsqrt(mean + EPSILON)
    pulled = jnp.sum(gains, axis=0, keepdims=True) * (1.0 / INNER) * (r * r * r)

    def gate_tile(h, carry):
        rows = pl.ds(pl.multiple_of(h * HEAD_DIM, HEAD_DIM), HEAD_DIM)
        gate = z[rows, :]
        skip = wide(heads_ref[2, pl.ds(h, 1), :])
        mix = mixed[rows, :]
        sig = jax.nn.sigmoid(gate)
        sil = gate * sig
        opened = mix * sil
        normed = opened * r
        inner = wide(inner_ref[rows, :])
        normed_ref[rows, :] = (normed * inner).astype(BF16)
        dn = dnormed[rows, :]
        gained = dn * normed
        dinner[rows, :] += gained[:, :CHUNK] + gained[:, CHUNK:]
        dopened = dn * inner * r - opened * pulled
        dmixed = dopened * sil
        dy_ref[rows, :] = dmixed
        dgate_ref[rows, :] = (dopened * mix * (sig * (1.0 + gate * (1.0 - sig)))).astype(BF16)
        skipped = row_sum(dmixed * act[rows, :])
        dskip[pl.ds(h, 1), :] += skipped[:, :CHUNK] + skipped[:, CHUNK:]
        dlogs_ref[pl.ds(h, 1), :] = row_sum(dmixed * mix) - skip * skipped
        return carry

    lax.fori_loop(0, HEADS, gate_tile, 0)
    for box, own, ref in (
        (boxes[0], own_normed_ref, normed_ref), (boxes[1], own_dgate_ref, dgate_ref),
    ):
        own[...] = ref[half_rows(INNER, p.c), :]
        box.fill(strip, ref[half_rows(INNER, 1 - p.c), :])
    for i in range(D // 256):
        part = slice(256 * i, 256 * i + 256)
        branch = dot(second_ref[part, OUT_AT:STEP_AT], normed_ref[...]).T
        out_ref[:, part] = (x_ref[:, part].astype(F32) + branch).astype(BF16)

    @pl.when(pl.program_id(0) == STRIPS - 1)
    def _():
        tail_sums_ref[...] = beside(
            lane_sums(dskip[...]), lane_sums(dinner[...]),
            jnp.zeros((8, tail_sums_ref.shape[1] - HEADS - INNER), F32),
        )
        swap.wait()
        back_copy.wait()
        for box in boxes:
            box.finish()


def backward_kernel(
    sizes, x_ref, back_ref, w_in_ref, step_in_ref, gain_ref, taps_ref, heads_ref,
    cin_ref, c_ref, raw_ref, s_ref, dy, dgate_ref, dlogs, tail_sums_ref, out_part, gate_part,
    dx_ref, own_a_ref, own_b_ref, flat_ref, out_column, gate_column, peer_a_ref, peer_b_ref,
    dconv_a_ref, dconv_b_ref, box_a, box_b, box_sems, dact, dstate, flow, tail, meets, vdu_rows, dstep_ref, dstep_sum, dgain, dtaps_ref, dheads_ref,
    dscaled_turned, *work,
):
    step_now = pl.program_id(0)
    p = Place(sizes)
    partner = p.at(c=1 - p.c)
    strip = STRIPS - 1 - step_now
    boxes = [
        Box(box, lambda s, ref=ref: ref.at[:, strip_at(s)], box_sems.at[k], partner)
        for k, (box, ref) in enumerate([(box_a, peer_a_ref), (box_b, peer_b_ref)])
    ]
    sums = [
        PlaneSum(p, part, work[7 * k : 7 * k + 7]) for k, part in enumerate((out_part, gate_part))
    ]

    @pl.when(step_now == 0)
    def _():
        sums[0].begin()
        greet_near(p, False)
        sums[0].start()
        sums[1].begin()

    @pl.when(step_now == 3)
    def _():
        sums[1].plane.finish(0)
        sums[1].plane.start(1)

    @pl.when(step_now == 0)
    def _():
        dstate[...] = jnp.zeros_like(dstate)
        flow[...] = jnp.zeros_like(flow)
        tail[...] = jnp.zeros_like(tail)
        dgain[...] = jnp.zeros_like(dgain)
        dstep_sum[...] = jnp.zeros_like(dstep_sum)
        dtaps_ref[...] = jnp.zeros_like(dtaps_ref)
        dheads_ref[...] = jnp.zeros_like(dheads_ref)

    back = back_ref[...]

    causal = upper()
    ones = causal.astype(F32).astype(BF16)
    row = lax.broadcasted_iota(jnp.int32, (CHUNK, CHUNK), 0)
    col = lax.broadcasted_iota(jnp.int32, (CHUNK, CHUNK), 1)
    ones_back = (row >= col).astype(F32).astype(BF16)

    def chunk(step, carry):
        j = PER - 1 - step
        cols = pl.ds(pl.multiple_of(j * CHUNK, CHUNK), CHUNK)
        raw = raw_ref[0:HEADS, cols]
        steps, logs, columns, grown, to_end, through = rates_of(raw, heads_ref, ones)
        in_turned = silu(c_ref[INNER : INNER + NSTATE, cols])
        out_turned = silu(c_ref[INNER + NSTATE :, cols])
        in_map = in_turned.T
        out_map = out_turned.T
        scores = three_pass(in_map, right_pair(out_turned))
        in_pair = right_pair(in_turned)
        out_pair = right_pair(out_map)
        dscores = jnp.zeros((CHUNK, CHUNK), F32)
        din = jnp.zeros((NSTATE, CHUNK), F32)
        dout = jnp.zeros((NSTATE, CHUNK), F32)
        for g in range(HEADS // GROUP):
            rows = slice(g * GROUP * HEAD_DIM, (g + 1) * GROUP * HEAD_DIM)
            leaving = dstate[rows]
            entering = s_ref[j, rows]
            from_state = three_pass(leaving, in_pair)
            ending, growing, kept = [], [], []
            for q in range(GROUP):
                h = g * GROUP + q
                mine = slice(h * HEAD_DIM, (h + 1) * HEAD_DIM)
                values = silu(c_ref[mine, cols])
                fed = values * steps[h : h + 1]
                dys = dy[mine, cols]
                gaps = logs[h : h + 1] - jnp.broadcast_to(columns[:, h : h + 1], (CHUNK, CHUNK))
                decay = jnp.where(causal, jnp.exp(gaps), 0.0)
                weights = scores * decay
                both = dot_nt(stack_left(dys), beside(*split(weights)))
                du = both[:HEAD_DIM] + both[HEAD_DIM:]
                du = du + from_state[q * HEAD_DIM : (q + 1) * HEAD_DIM] * to_end[h : h + 1]
                fed_high, fed_low = split(fed)
                dy_high, dy_low = split(dys)
                dweights = dot_tn(
                    above(fed_high, fed_low, fed_high), above(dy_high, dy_high, dy_low)
                )
                dscores = dscores + dweights * decay
                vdu_rows[h : h + 1, :] = row_sum(values * du)
                dact[mine, cols] = du * steps[h : h + 1] + heads_ref[2][h : h + 1] * dys
                ending.append(fed * to_end[h : h + 1])
                growing.append(dys * grown[h : h + 1])
                kept.append(jnp.broadcast_to(through[h : h + 1], (HEAD_DIM, CHUNK)))
            ending = above(*ending)
            growing = above(*growing)
            end_high, end_low = split(ending)
            grow_high, grow_low = split(growing)
            leave_high, leave_low = split(leaving)
            enter_high, enter_low = split(entering)
            din = din + dot_tn(
                above(leave_high, leave_low, leave_high), above(end_high, end_high, end_low)
            )
            dout = dout + dot_tn(
                above(enter_high, enter_low, enter_high), above(grow_high, grow_high, grow_low)
            )
            arrived = leaving * above(*kept) + three_pass(growing, out_pair)
            dstate[rows] = arrived
            meet = arrived * entering
            for q in range(GROUP):
                h = g * GROUP + q
                meets[h : h + 1, :] = row_sum(meet[q * HEAD_DIM : (q + 1) * HEAD_DIM])
        vdu = vdu_rows[...]
        dlog = dlogs[:, cols] - steps * vdu
        drate = exact_sum(dlog, ones_back) + flow[...]
        flow[...] = jnp.broadcast_to(
            jnp.sum(meets[...], axis=1, keepdims=True), (HEADS, CHUNK)
        )
        dsteps = vdu + heads_ref[1] * drate
        draw = dsteps * jax.nn.sigmoid(raw + heads_ref[0])
        dheads_ref[0] += draw
        dheads_ref[1] += drate * steps * heads_ref[1]
        dstep_ref[:, cols] = above(draw, jnp.zeros((STEP - HEADS, CHUNK), F32)).astype(BF16)
        score_high, score_low = split(dscores)
        both = dot_nt(stack_left(out_turned), beside(score_high, score_low))
        dact[INNER : INNER + NSTATE, cols] = din + both[:NSTATE] + both[NSTATE:]
        both = dot(stack_left(in_turned), above(score_high, score_low))
        dact[INNER + NSTATE :, cols] = dout + both[:NSTATE] + both[NSTATE:]
        return carry

    lax.fori_loop(0, PER, chunk, 0)

    @pl.when(step_now == 0)
    def _():
        sums[1].start()

    @pl.when(step_now == 2)
    def _():
        sums[0].plane.finish(0)
        sums[0].plane.start(1)

    lane = lax.broadcasted_iota(jnp.int32, (64, CHUNK), 1)

    def conv_tile(target, start, i):
        rows = slice(start + 64 * i, start + 64 * i + 64)
        c = c_ref[rows]
        sig = jax.nn.sigmoid(c)
        dpre = dact[rows] * (sig * (1.0 + c * (1.0 - sig)))
        cin = cin_ref[rows]
        cols = [dpre[:, CHUNK * j : CHUNK * j + CHUNK] for j in range(PER)]
        dcin = dpre * wide(taps_ref[KCONV - 1, rows])
        grad = cin * dpre
        dtaps_ref[KCONV - 1, rows] += grad[:, :CHUNK] + grad[:, CHUNK:]
        dtaps_ref[KCONV, rows] += dpre[:, :CHUNK] + dpre[:, CHUNK:]
        for k in range(KCONV - 1):
            ahead = KCONV - 1 - k
            turned = [pltpu.roll(col, CHUNK - ahead, 1) for col in cols] + [tail[k, rows]]
            tail[k, rows] = turned[0]
            pairs = zip(turned[:-1], turned[1:])
            shifted = beside(*[jnp.where(lane < CHUNK - ahead, a, b) for a, b in pairs])
            dcin = dcin + shifted * wide(taps_ref[k, rows])
            grad = cin * shifted
            dtaps_ref[k, rows] += grad[:, :CHUNK] + grad[:, CHUNK:]
        target[64 * i : 64 * i + 64] = dcin.astype(BF16)

    thirds = [slice(256 * i, 256 * i + 256) for i in range(D // 256)]
    conv_at = INNER + CONV_A
    tiles = CONV_A // 64
    for i in range(tiles):
        conv_tile(dconv_a_ref, 0, i)
        if i % 4 == 0:
            part = thirds[i // 4]
            dscaled_turned[part] = dot(w_in_ref[part, :INNER], dgate_ref[...])
    for i in range((CONVCH - CONV_A) // 64):
        conv_tile(dconv_b_ref, CONV_A, i)
        if i % 4 == 0 and i // 4 < len(thirds):
            part = thirds[i // 4]
            dscaled_turned[part] += dot(w_in_ref[part, INNER:conv_at], dconv_a_ref[...])
    for box, own, ref in (
        (boxes[0], own_a_ref, dconv_a_ref), (boxes[1], own_b_ref, dconv_b_ref),
    ):
        own[...] = ref[half_rows(ref.shape[0], p.c), :]
        box.fill(strip, ref[half_rows(ref.shape[0], 1 - p.c), :], True)
    x = x_ref[...].astype(F32)
    r = lax.rsqrt(jnp.mean(x * x, axis=-1, keepdims=True) + EPSILON)
    parts = []
    for part in thirds:
        total = dscaled_turned[part] + dot(w_in_ref[part, conv_at:], dconv_b_ref[...])
        parts.append((total + dot(step_in_ref[part, :STEP], dstep_ref[...])).T)
    dscaled = beside(*parts)
    plain = x * r
    dgain[...] += fold(dscaled * plain)
    dstep_sum[...] += dot(dstep_ref[...], (plain * gain_ref[...]).astype(BF16))
    gained = dscaled * gain_ref[...]
    inner = jnp.mean(gained * plain, axis=-1, keepdims=True)
    dx_ref[...] = back.astype(F32) + (gained - plain * inner) * r

    @pl.when(step_now == STRIPS - 1)
    def _():
        for part, column in zip(sums, (out_column, gate_column)):
            part.plane.finish(1)
            column[...] = part.column()
        for box in boxes:
            box.finish(True)
        store_flat(flat_ref, dstep_sum, dgain, dtaps_ref, dheads_ref, tail_sums_ref)


def store_flat(flat_ref, dstep_sum, dgain, dtaps, dheads, tail_sums_ref):
    flat_ref[...] = jnp.zeros_like(flat_ref)
    for j in range(D // 128):
        flat_ref[HEADS * j : HEADS * j + HEADS] = dstep_sum[:HEADS, 128 * j : 128 * j + 128]
    last = beside(
        lane_sums(dheads[0])[:1], lane_sums(dheads[1])[:1], tail_sums_ref[:1],
    )
    rows = [jnp.sum(dgain[...], axis=0, keepdims=True)]
    rows += [lane_sums(dtaps[k])[:1] for k in range(KCONV + 1)]
    at = HEADS * (D // 128)
    for row in rows + [last]:
        for j in range(row.shape[1] // 128):
            flat_ref[at + j : at + j + 1] = row[:, 128 * j : 128 * j + 128]
        at += row.shape[1] // 128


def whole(shape):
    return pl.BlockSpec(shape, lambda i: (0,) * len(shape), pipeline_mode=pl.Buffered(1))


def strip_rows(width):
    return pl.BlockSpec((STRIP, width), lambda i: (i, 0))


def strip_cols(height):
    return pl.BlockSpec((height, STRIP), lambda i: (0, i))


def shape(*dims, dtype=F32):
    return jax.ShapeDtypeStruct(dims, dtype)


def columns(width, at):
    return pl.BlockSpec((D, width), lambda i: (0, at), pipeline_mode=pl.Buffered(1))


def forward_call(x, back, weights, gain, taps, heads, inner, blocks, sizes, collective_id):
    count = sizes[0] * sizes[1]
    dma = pltpu.SemaphoreType.DMA
    hbm = pl.BlockSpec(memory_space=pl.ANY)
    return pl.pallas_call(
        functools.partial(forward_kernel, sizes),
        grid=(STRIPS,),
        in_specs=[
            strip_rows(D), strip_rows(D), columns(HALF, 0), columns(HALF, 1), whole((1, D)),
            hbm, whole((3, HEADS, CHUNK)), hbm, hbm, hbm,
        ],
        out_specs=[
            strip_rows(D), strip_rows(D), strip_cols(CONVCH), strip_cols(CONVCH),
            strip_cols(STEP), pl.BlockSpec((PER, INNER, NSTATE), lambda i: (i, 0, 0)),
            strip_cols(INNER // 2), strip_cols(INNER), strip_cols(INNER), strip_cols(INNER // 2),
            strip_cols(HEADS), whole((8, TAIL_SUMS)), hbm, hbm, hbm, hbm, hbm,
        ],
        out_shape=[
            shape(LEN, D, dtype=BF16), shape(LEN, D, dtype=BF16), shape(CONVCH, LEN),
            shape(CONVCH, LEN), shape(STEP, LEN), shape(LEN // CHUNK, INNER, NSTATE),
            shape(INNER // 2, LEN, dtype=BF16), shape(INNER, LEN), shape(INNER, LEN, dtype=BF16),
            shape(INNER // 2, LEN, dtype=BF16), shape(HEADS, LEN), shape(8, TAIL_SUMS),
            shape(*blocks.shape), shape(INNER // 2, LEN, dtype=BF16),
            shape(INNER // 2, LEN, dtype=BF16), shape(LEN, D, dtype=BF16),
            shape(LEN, D, dtype=BF16),
        ],
        scratch_shapes=[
            pltpu.VMEM((CONVCH, STRIP), F32), pltpu.VMEM((INNER, STRIP), F32),
            pltpu.VMEM((INNER, STRIP), F32), pltpu.VMEM((INNER, STRIP), F32),
            pltpu.VMEM((INNER, NSTATE), F32), pltpu.VMEM((2, CONVCH, CHUNK), F32),
            pltpu.VMEM((2, HALF, D), BF16), pltpu.VMEM((HEADS, CHUNK), F32),
            pltpu.VMEM((INNER, CHUNK), F32), pltpu.VMEM((INNER, STRIP), BF16),
            pltpu.VMEM((KCONV + 1, CONVCH, CHUNK), F32), pltpu.VMEM((INNER, CHUNK), F32), dma((2,)),
            pltpu.VMEM((2, INNER // 2, STRIP), BF16), pltpu.VMEM((2, INNER // 2, STRIP), BF16),
            pltpu.VMEM((2, STRIP, D), BF16), dma((3, STRIPS, 2)), dma((2,)),
            dma((count,)), dma((count,)), dma,
        ],
        compiler_params=pltpu.CompilerParams(
            vmem_limit_bytes=60 * 2**20, collective_id=collective_id, has_side_effects=True
        ),
        name="mixer_forward",
    )(x, back, weights, weights, gain, taps, heads, inner, blocks, back)


def backward_call(x, back, weights, gain, taps, heads, kept, tail_sums, parts, sizes,
                  collective_id):
    last = STRIPS - 1

    def rows(width):
        return pl.BlockSpec((STRIP, width), lambda i: (last - i, 0))

    def cols(height):
        return pl.BlockSpec((height, STRIP), lambda i: (0, last - i))

    Z = sizes[0]
    lines = flat_lines(sizes[0] * sizes[1])
    size = (parts[0].shape[1], D)
    dma = pltpu.SemaphoreType.DMA
    hbm = pl.BlockSpec(memory_space=pl.ANY)
    return pl.pallas_call(
        functools.partial(backward_kernel, sizes),
        grid=(STRIPS,),
        in_specs=[
            rows(D), rows(D), columns(WIDE, 0),
            columns(256, (HALF + STEP_AT) // 256), whole((1, D)),
            whole((KCONV, CONVCH, CHUNK)), whole((3, HEADS, CHUNK)), cols(CONVCH),
            cols(CONVCH), cols(STEP),
            pl.BlockSpec((PER, INNER, NSTATE), lambda i: (last - i, 0, 0)), cols(INNER),
            cols(INNER), cols(HEADS), whole((8, TAIL_SUMS)), hbm, hbm,
        ],
        out_specs=[
            rows(D), cols(CONV_A // 2), cols((CONVCH - CONV_A) // 2), whole((lines, 128)),
            whole((Z,) + size), whole((Z,) + size), hbm, hbm,
        ],
        out_shape=[
            shape(LEN, D), shape(CONV_A // 2, LEN, dtype=BF16),
            shape((CONVCH - CONV_A) // 2, LEN, dtype=BF16), shape(lines, 128),
            shape(Z, *size), shape(Z, *size), shape(CONV_A // 2, LEN, dtype=BF16),
            shape((CONVCH - CONV_A) // 2, LEN, dtype=BF16),
        ],
        scratch_shapes=[
            pltpu.VMEM((CONV_A, STRIP), BF16), pltpu.VMEM((CONVCH - CONV_A, STRIP), BF16),
            pltpu.VMEM((2, CONV_A // 2, STRIP), BF16),
            pltpu.VMEM((2, (CONVCH - CONV_A) // 2, STRIP), BF16), dma((2, STRIPS, 2)),
            pltpu.VMEM((CONVCH, STRIP), F32),
            pltpu.VMEM((INNER, NSTATE), F32), pltpu.VMEM((HEADS, CHUNK), F32),
            pltpu.VMEM((KCONV - 1, CONVCH, CHUNK), F32), pltpu.VMEM((HEADS, CHUNK), F32),
            pltpu.VMEM((HEADS, CHUNK), F32), pltpu.VMEM((STEP, STRIP), BF16),
            pltpu.VMEM((STEP, D), F32), pltpu.VMEM((8, D), F32),
            pltpu.VMEM((KCONV + 1, CONVCH, CHUNK), F32), pltpu.VMEM((2, HEADS, CHUNK), F32),
            pltpu.VMEM((D, STRIP), F32),
        ]
        + 2 * (plane_scratch(sizes, size) + [dma]),
        compiler_params=pltpu.CompilerParams(
            vmem_limit_bytes=63 * 2**20, collective_id=collective_id, has_side_effects=True
        ),
        name="mixer_backward",
    )(
        x, back, weights, weights, gain, taps, heads, *kept, tail_sums,
        *(by_chip(part, sizes) for part in parts),
    )


def grads_kernel(*refs):
    ins, block_in, outs, block_out = refs[:8], refs[8], refs[9:11], refs[11]
    sides, others, results, block, sems, out_sems, block_sems = refs[12:]
    load = pltpu.make_async_copy(block_in, block, block_sems.at[0])
    keep = pltpu.make_async_copy(block, block_out, block_sems.at[1])
    copies = []
    for k in range(4):
        copies.append([
            pltpu.make_async_copy(ins[2 * k], sides.at[k], sems.at[2 * k]),
            pltpu.make_async_copy(ins[2 * k + 1], others.at[k], sems.at[2 * k + 1]),
        ])
        for copy in copies[k]:
            copy.start()
    load.start()
    stores = []
    for k in range(2):
        for half in (0, 1):
            for copy in copies[2 * k + half]:
                copy.wait()
            side, other = sides.at[2 * k + half], others.at[2 * k + half]

            def tile(i, carry, k=k, half=half, side=side, other=other):
                rows = pl.ds(pl.multiple_of(i * GRAD_TILE, GRAD_TILE), GRAD_TILE)
                part = dot(side[rows, :], other[...])
                results[k, rows, :] = part if half == 0 else results[k, rows, :] + part
                return carry

            lax.fori_loop(0, INNER // 2 // GRAD_TILE, tile, 0)
        if k == 0:
            load.wait()
            keep.start()
        stores.append(pltpu.make_async_copy(results.at[k], outs[k], out_sems.at[k]))
        stores[k].start()
    for store in stores + [keep]:
        store.wait()


def grads_call(own_normed, peer_normed, own_dgate, peer_dgate, backs, hbs, block):
    rows = INNER // 2
    hbm = pl.BlockSpec(memory_space=pl.ANY)
    return pl.pallas_call(
        grads_kernel,
        in_specs=[hbm] * 9,
        out_specs=[hbm] * 3,
        out_shape=[shape(rows, D)] * 2 + [shape(LEN, D, dtype=BF16)],
        scratch_shapes=[
            pltpu.VMEM((4, rows, LEN), BF16), pltpu.VMEM((4, LEN, D), BF16),
            pltpu.VMEM((2, rows, D), F32), pltpu.VMEM((LEN, D), BF16),
            pltpu.SemaphoreType.DMA((8,)), pltpu.SemaphoreType.DMA((2,)),
            pltpu.SemaphoreType.DMA((2,)),
        ],
        compiler_params=pltpu.CompilerParams(vmem_limit_bytes=60 * 2**20),
        name="grads",
    )(own_normed, backs[0], peer_normed, backs[1], own_dgate, hbs[0], peer_dgate, hbs[1], block)


def flat_lines(count):
    return -(-(HEADS * D + SMALL) // (1024 * count)) * 8 * count


def block_and_gradients(x, back, weights, vectors, blocks, sizes, collective_ids):
    count = sizes[0] * sizes[1]
    gain, taps, heads, inner = vectors
    (
        out, hb, cin, c, raw, states, own_normed, dy, dgate, own_dgate, dlogs, tail_sums, moved,
        peer_normed, peer_dgate, peer_hb, peer_back,
    ) = forward_call(
        x, back, weights, gain, taps, heads, inner, blocks, sizes, collective_ids[0]
    )
    *parts, out = grads_call(
        own_normed, peer_normed, own_dgate, peer_dgate, (back, peer_back), (hb, peer_hb), out
    )
    parts = [part.reshape(count // 2, -1, D) for part in parts]
    dx, own_a, own_b, flat, out_column, gate_column, peer_a, peer_b = backward_call(
        x, back, weights, gain, taps, heads, (cin, c, raw, states, dy, dgate, dlogs), tail_sums,
        parts, sizes, collective_ids[1],
    )
    factors = (own_a, peer_a, own_b, peer_b, hb, peer_hb)
    return out, dx, [out_column, gate_column], factors, flat.reshape(count, -1, 128), moved


MESH = pl.DeviceIdType.MESH


class Place:
    def __init__(self, sizes):
        self.Z, self.F = sizes
        self.C, self.Y = 2, 2
        self.X = self.F // 4
        f = lax.axis_index("fsdp")
        self.z = lax.axis_index("dp")
        self.c = lax.rem(f, 2)
        self.x = lax.rem(f // 2, self.X)
        self.y = f // (2 * self.X)
        self.f = f

    def at(self, z=None, y=None, x=None, c=None):
        z = self.z if z is None else z
        y = self.y if y is None else y
        x = self.x if x is None else x
        c = self.c if c is None else c
        return (z, (y * self.X + x) * 2 + c)

    def other_x(self, step):
        return lax.rem(self.x + step, self.X)


def signal(device):
    pl.semaphore_signal(
        pltpu.get_barrier_semaphore(), inc=1, device_id=device, device_id_type=MESH
    )


def greet_all(place, wait=True):
    count = place.Z * place.F
    me = place.z * place.F + place.f

    def step(i, carry):
        peer = lax.rem(me + i, count)
        signal((peer // place.F, lax.rem(peer, place.F)))
        return carry

    lax.fori_loop(1, count, step, 0)
    if wait:
        await_all(place)


def await_all(place):
    pl.semaphore_wait(pltpu.get_barrier_semaphore(), place.Z * place.F - 1)


def remote(src, dst, send, recv, device):
    return pltpu.make_async_remote_copy(
        src_ref=src, dst_ref=dst, send_sem=send, recv_sem=recv, device_id=device,
        device_id_type=MESH,
    )


def add_blocks(dst, src, count):
    def step(i, carry):
        target = dst(i)
        target[...] = target[...] + src(i)[...]
        return carry

    lax.fori_loop(0, count, step, 0)


class Swap:
    def __init__(self, place, src, dst, send, recv, local, same=False, narrow=None):
        self.place, self.src, self.dst, self.same, self.narrow = place, src, dst, same, narrow
        self.send, self.recv, self.local = send, recv, local
        self.count = place.Z * place.F
        self.me = place.z * place.F + place.f

    def block(self, peer):
        return self.src if self.same else self.src.at[peer]

    def cut(self, ref, odd):
        return ref.at[:, pl.ds(0, self.narrow)] if odd else ref

    def each(self, sender, act):
        if self.narrow is None:
            act(False)
        else:
            @pl.when(lax.rem(sender, 2) == 0)
            def _():
                act(False)

            @pl.when(lax.rem(sender, 2) == 1)
            def _():
                act(True)

    def to(self, i, odd):
        peer = lax.rem(self.me + i, self.count)
        return remote(
            self.cut(self.block(peer), odd), self.cut(self.dst.at[self.me], odd),
            self.send.at[i], self.recv.at[i],
            (peer // self.place.F, lax.rem(peer, self.place.F)),
        )

    def keep(self):
        return pltpu.make_async_copy(self.block(self.me), self.dst.at[self.me], self.local)

    def start(self):
        self.keep().start()

        def step(i, carry):
            self.each(self.me, lambda odd: self.to(i, odd).start())
            return carry

        lax.fori_loop(1, self.count, step, 0)

    def wait(self):
        self.keep().wait()

        def step(i, carry):
            sender = lax.rem(self.me + self.count - i, self.count)
            self.each(self.me, lambda odd: self.to(i, odd).wait_send())
            self.each(sender, lambda odd: remote(
                self.cut(self.block(sender), odd), self.cut(self.dst.at[sender], odd),
                self.send.at[i], self.recv.at[i],
                (sender // self.place.F, lax.rem(sender, self.place.F)),
            ).wait_recv())
            return carry

        lax.fori_loop(1, self.count, step, 0)


def greet_near(place, along_z, wait=True):
    signal(place.at(c=1 - place.c))
    signal(place.at(y=1 - place.y))
    for s in range(1, place.X):
        signal(place.at(x=place.other_x(s)))
    if along_z:
        for s in range(1, place.Z):
            signal(place.at(z=lax.rem(place.z + s, place.Z)))
    if wait:
        await_near(place, along_z)


def await_near(place, along_z):
    pl.semaphore_wait(
        pltpu.get_barrier_semaphore(), place.X + 1 + (place.Z - 1 if along_z else 0)
    )


class Plane:
    def __init__(self, place, acc, x1, y1, x2, y2, sems):
        self.p, self.acc = place, acc
        self.x1, self.y1, self.x2, self.y2, self.sems = x1, y1, x2, y2, sems
        self.h = place.Z // 2

    def copies(self, stage):
        p, acc, h = self.p, self.acc, self.h
        low, high = pl.ds(0, h), pl.ds(h, p.Z - h)
        out = []
        base = stage * p.X
        for s in range(1, p.X):
            x = p.other_x(s)
            if stage == 0:
                src, dst = acc.at[low, :, x], self.x1.at[s - 1]
            else:
                src, dst = acc.at[high, p.y, x], self.x2.at[s - 1]
            sem = self.sems.at[base + s]
            out.append(remote(src, dst, sem.at[0], sem.at[1], p.at(x=x)))
        if stage == 0:
            src, dst = acc.at[high, 1 - p.y], self.y1
        else:
            src, dst = acc.at[low, 1 - p.y, p.x], self.y2
        sem = self.sems.at[base]
        out.append(remote(src, dst, sem.at[0], sem.at[1], p.at(y=1 - p.y)))
        return out

    def start(self, stage):
        for copy in self.copies(stage):
            copy.start()

    def finish(self, stage):
        p, acc, h = self.p, self.acc, self.h
        for copy in self.copies(stage):
            copy.wait()
        for s in range(p.X - 1):
            if stage == 0:
                add_blocks(
                    lambda i: acc.at[i // p.Y, lax.rem(i, p.Y), p.x],
                    lambda i: self.x1.at[s, i // p.Y, lax.rem(i, p.Y)],
                    h * p.Y,
                )
            else:
                add_blocks(
                    lambda i: acc.at[h + i, p.y, p.x], lambda i: self.x2.at[s, i], p.Z - h
                )
        if stage == 0:
            add_blocks(
                lambda i: acc.at[h + i // p.X, p.y, lax.rem(i, p.X)],
                lambda i: self.y1.at[i // p.X, lax.rem(i, p.X)],
                (p.Z - h) * p.X,
            )
        else:
            add_blocks(lambda i: acc.at[i, p.y, p.x], lambda i: self.y2.at[i], h)


def plane_scratch(sizes, block):
    Z, X, Y = sizes[0], sizes[1] // 4, 2
    h = Z // 2
    return [
        pltpu.VMEM((Z, Y, X) + block, F32), pltpu.VMEM((X - 1, h, Y) + block, F32),
        pltpu.VMEM((Z - h, X) + block, F32), pltpu.VMEM((X - 1, Z - h) + block, F32),
        pltpu.VMEM((h,) + block, F32), pltpu.SemaphoreType.DMA((2 * X, 2)),
    ]


def by_place(blocks, sizes):
    return blocks.reshape((sizes[0], 2, sizes[1] // 4, 2) + blocks.shape[1:])


def by_chip(blocks, sizes):
    return blocks.reshape((sizes[0], 2, sizes[1] // 4) + blocks.shape[1:])


class PlaneSum:
    def __init__(self, place, part, work):
        self.p, self.part, self.acc, self.sem = place, part, work[0], work[6]
        self.plane = Plane(place, *work[:6])

    def copy(self):
        return pltpu.make_async_copy(self.part, self.acc, self.sem)

    def begin(self):
        self.copy().start()

    def start(self):
        self.copy().wait()
        self.plane.start(0)

    def block(self, z):
        return self.acc.at[z, self.p.y, self.p.x]

    def column(self):
        return self.acc[:, self.p.y, self.p.x]


class Product(PlaneSum):
    def __init__(self, place, factors, work):
        super().__init__(place, None, work)
        self.factors, self.formed = factors, False

    def begin(self):
        pass

    def start(self):
        if not self.formed:
            self.form()
        self.plane.start(0)

    def form(self):
        self.formed = True
        own, peer, right, peer_right = self.factors
        Z, Y, X, per, _ = self.acc.shape
        h = Z // 2
        size = h * Y * X * per

        def half(k, carry):
            rows = pl.ds(pl.multiple_of(k * size, size), size)
            value = dot(own[rows, :], right[...]) + dot(peer[rows, :], peer_right[...])
            for i in range(h * Y * X):
                place = (k * h + i // (Y * X), i // X % Y, i % X)
                self.acc[place] = value[per * i : per * i + per]
            return carry

        lax.fori_loop(0, Z // h, half, 0)


class PairSum(PlaneSum):
    def __init__(self, place, part, work):
        super().__init__(place, part, work)
        self.core, self.sems = work[7], work[8]

    def copies(self):
        p = self.p
        return (
            remote(
                self.part.at[:, :, :, 1 - p.c], self.core, self.sems.at[0], self.sems.at[1],
                p.at(c=1 - p.c),
            ),
            pltpu.make_async_copy(self.part.at[:, :, :, p.c], self.acc, self.sem),
        )

    def begin(self):
        for copy in self.copies():
            copy.start()

    def start(self):
        p = self.p
        for copy in self.copies():
            copy.wait()

        def place_of(i):
            return i // (p.Y * p.X), lax.rem(i // p.X, p.Y), lax.rem(i, p.X)

        add_blocks(
            lambda i: self.acc.at[place_of(i)], lambda i: self.core.at[place_of(i)],
            p.Z * p.Y * p.X,
        )
        self.plane.start(0)


class Column:
    def __init__(self, part, acc, sem):
        self.copy = pltpu.make_async_copy(part, acc, sem)
        self.acc = acc

    def block(self, z):
        return self.acc.at[z]


class Chain:
    def __init__(self, place, part, held, sems):
        self.p, self.part, self.held, self.sems = place, part, held, sems

    def flow(self, t, side):
        p = self.p
        sem = self.sems.at[side, t]
        target = p.at(z=p.z + 1 - 2 * side)
        return remote(self.part.block(t), self.held.at[side, t], sem.at[0], sem.at[1], target)

    def first(self):
        p = self.p
        for j in range(p.Z - 1):
            @pl.when(p.z == 0)
            def _():
                self.flow(p.Z - 1 - j, 0).start()

            @pl.when(p.z == p.Z - 1)
            def _():
                self.flow(j, 1).start()

    def receive(self, t, side):
        self.flow(t, side).wait_recv()
        mine = self.part.block(t)
        mine[...] = mine[...] + self.held[side, t]

    def forward(self, j):
        p = self.p

        def turn(k, carry):
            side = lax.rem(k + p.z // (p.Z // 2), 2)
            t = (1 - side) * (p.Z - 1 - j) + side * j
            inside = jnp.logical_and(p.z > 0, p.z < p.Z - 1)

            @pl.when(jnp.logical_and(inside, (1 - 2 * side) * (t - p.z) > 0))
            def _():
                self.receive(t, side)
                self.flow(t, side).start()

            return carry

        lax.fori_loop(0, 2, turn, 0)

    def last(self):
        p = self.p

        @pl.when(p.z > 0)
        def _():
            self.receive(p.z, 0)

        @pl.when(p.z < p.Z - 1)
        def _():
            self.receive(p.z, 1)

    def finish(self):
        p = self.p
        for t in range(p.Z):
            for side in (0, 1):
                @pl.when(p.z < t if side == 0 else p.z > t)
                def _():
                    self.flow(t, side).wait_send()


class Direct:
    def __init__(self, place, part, held, sems):
        self.p, self.part, self.held, self.sems = place, part, held, sems

    def over(self, s):
        p = self.p
        z = lax.rem(p.z + s, p.Z)
        sem = self.sems.at[s]
        return remote(self.part.block(z), self.held.at[s - 1], sem.at[0], sem.at[1], p.at(z=z))

    def start(self):
        for s in range(1, self.p.Z):
            self.over(s).start()

    def last(self):
        mine = self.part.block(self.p.z)
        total = mine[...]
        for s in range(1, self.p.Z):
            self.over(s).wait()
            total = total + self.held[s - 1]
        mine[...] = total


def scatter_kernel(sizes, *refs):
    columns_in, factors, small_in, outs, rest = (
        refs[:2], refs[2:8], refs[8], refs[9:14], list(refs[14:])
    )

    def take(n):
        taken = rest[:n]
        del rest[:n]
        return taken

    p = Place(sizes)
    columns = [Column(ref, *take(2)) for ref in columns_in]
    chains = [Chain(p, column, *take(2)) for column in columns]
    own_a, peer_a, own_b, peer_b, hb, peer_hb = factors
    queue = [
        Product(p, (own_a, peer_a, hb, peer_hb), take(7)),
        Product(p, (own_b, peer_b, hb, peer_hb), take(7)),
        PairSum(p, small_in, take(9)),
    ]
    queue = [(part, Direct(p, part, *take(2))) for part in queue]
    greet_near(p, True, False)
    for column in columns:
        column.copy.start()
    queue[0][0].form()
    await_near(p, True)
    for part, _ in queue:
        part.begin()
    for column, chain in zip(columns, chains):
        column.copy.wait()
        chain.first()
    hops = p.Z - 2

    def forward(j):
        if j < hops:
            for chain in chains:
                chain.forward(j)

    stages = [
        lambda part, direct: part.start(),
        lambda part, direct: (part.plane.finish(0), part.plane.start(1)),
        lambda part, direct: (part.plane.finish(1), direct.start()),
    ]
    for k, stage in enumerate(stages):
        for part, direct in queue:
            stage(part, direct)
        forward(k)
    for k in range(len(stages), hops):
        forward(k)
    for chain in chains:
        chain.last()
        chain.finish()
    for _, direct in queue:
        direct.last()
    for part, out in zip(columns + [part for part, _ in queue], outs):
        out[...] = part.block(p.z)[...]


def scatter_call(columns, factors, small, sizes, collective_id):
    Z, F = sizes
    X, Y = F // 4, 2
    chips = Z * X * Y
    dma = pltpu.SemaphoreType.DMA
    parts = [(factors[0].shape[0] // chips, D), (factors[2].shape[0] // chips, D)]
    parts.append(small.shape[1:])
    scratch = []
    for column in columns:
        scratch += [pltpu.VMEM(column.shape, F32), dma]
    for column in columns:
        scratch += [pltpu.VMEM((2, Z) + column.shape[1:], F32), dma((2, Z, 2))]
    for block in parts:
        scratch += plane_scratch(sizes, block) + [dma]
    scratch += [pltpu.VMEM((Z, Y, X) + parts[2], F32), dma((2,))]
    for block in parts:
        scratch += [pltpu.VMEM((Z - 1,) + block, F32), dma((Z, 2))]
    hbm = pl.BlockSpec(memory_space=pl.ANY)
    vmem = pl.BlockSpec(memory_space=pltpu.VMEM)
    return pl.pallas_call(
        functools.partial(scatter_kernel, sizes),
        out_shape=[shape(*block) for block in [column.shape[1:] for column in columns] + parts],
        in_specs=[hbm] * 2 + [vmem] * 6 + [hbm],
        out_specs=[vmem] * 5,
        scratch_shapes=scratch,
        compiler_params=pltpu.CompilerParams(
            collective_id=collective_id, has_side_effects=True, vmem_limit_bytes=60 * 2**20
        ),
        name="scatter",
    )(*columns, *factors, by_place(small, sizes))


def gather_kernel(
    sizes, w_in_ref, w_out_ref, m_in_ref, m_out_ref, params_ref,
    all_ref, blocks_ref, gain_ref, taps_ref, heads_ref, inner_ref,
    mine, keep_sem, z_sems, near, far, across,
):
    p = Place(sizes)
    Z, h = p.Z, p.Z // 2
    greet_near(p, True)
    own = mine.shape[0]
    partner = p.at(c=1 - p.c)
    mine[:, :WIDE] = w_in_ref[:, :WIDE].astype(BF16)
    mine[:, WIDE : WIDE + INNER] = w_out_ref[...].astype(BF16)
    mine[:, WIDE + INNER :] = jnp.concatenate(
        [w_in_ref[:, WIDE:], jnp.zeros((own, 2 * HALF - IN_W - INNER), F32)], axis=1
    ).astype(BF16)
    keep = pltpu.make_async_copy(mine, all_ref.at[p.z, p.y, p.x, p.c], keep_sem)
    keep.start()

    def spot(z, y, x):
        return all_ref.at[z, y, x, p.c]

    def copy(src, dst, sem, device):
        return remote(src, dst, sem.at[0], sem.at[1], device)

    def along_z(z, right, src=None):
        here = spot(z, p.y, p.x)
        target = p.at(z=p.z + 1 if right else p.z - 1)
        return copy(here if src is None else src, here, z_sems.at[0 if right else 1, z], target)

    def near_copies(z, src=None):
        here = spot(z, p.y, p.x)
        src = here if src is None else src
        found = [copy(src, here, near.at[z, 0], p.at(y=1 - p.y))]
        for s in range(1, p.X):
            found.append(copy(src, here, near.at[z, s], p.at(x=p.other_x(s))))
        return found

    def near_arrivals(z):
        found = [(z, 1 - p.y, p.x, near.at[z, 0])]
        for s in range(1, p.X):
            found.append((z, p.y, lax.rem(p.x + p.X - s, p.X), near.at[z, s]))
        return found

    def far_copies(z):
        low, high = [], []
        for s in range(1, p.X):
            x = p.other_x(s)
            there = spot(z, p.y, x)
            low.append(copy(there, there, far.at[z, s], p.at(y=1 - p.y)))
            there = spot(z, 1 - p.y, p.x)
            high.append(copy(there, there, far.at[z, s], p.at(x=x)))
        return low, high

    def far_arrivals(z):
        low = [(z, 1 - p.y, p.other_x(s), far.at[z, s]) for s in range(1, p.X)]
        high = [
            (z, 1 - p.y, lax.rem(p.x + p.X - s, p.X), far.at[z, s]) for s in range(1, p.X)
        ]
        return low, high

    def to_partner(z, y, x, src=None):
        here = spot(z, y, x)
        return copy(here if src is None else src, here, across.at[z, y, x], partner)

    def await_block(z, y, x, sem):
        here = spot(z, y, x)
        copy(here, here, sem, partner).wait_recv()
        to_partner(z, y, x).start()

    def start_all(copies):
        for c in copies:
            c.start()

    @pl.when(p.z < Z - 1)
    def _():
        along_z(p.z, True, mine).start()

    @pl.when(p.z > 0)
    def _():
        along_z(p.z, False, mine).start()

    start_all(near_copies(p.z, mine))
    to_partner(p.z, p.y, p.x, mine).start()
    spread_vectors(params_ref, gain_ref, taps_ref, heads_ref, inner_ref)
    spread_moments(m_in_ref, m_out_ref, blocks_ref)

    def visit(right, z):
        await_block(z, p.y, p.x, z_sems.at[0 if right else 1, z])

        @pl.when(p.z < Z - 1 if right else p.z > 0)
        def _():
            along_z(z, right).start()

        start_all(near_copies(z))

    def by_distance(low, high):
        for j in range(1, Z):
            @pl.when(p.z - j >= 0)
            def _():
                low(p.z - j)

            @pl.when(p.z + j < Z)
            def _():
                high(p.z + j)

    by_distance(lambda z: visit(True, z), lambda z: visit(False, z))

    def relay(z):
        for block in near_arrivals(z):
            await_block(*block)
        low, high = far_copies(z)

        @pl.when(z < h)
        def _():
            start_all(low)

        @pl.when(z >= h)
        def _():
            start_all(high)

    relay(p.z)
    by_distance(relay, relay)

    def settle(z):
        low, high = far_arrivals(z)

        @pl.when(z < h)
        def _():
            for block in low:
                await_block(*block)

        @pl.when(z >= h)
        def _():
            for block in high:
                await_block(*block)

    settle(p.z)
    by_distance(settle, settle)
    keep.wait()

    def finish(z, carry):
        for c in near_copies(z):
            c.wait_send()
        low, high = far_copies(z)

        @pl.when(z < h)
        def _():
            for c in low:
                c.wait_send()

        @pl.when(z >= h)
        def _():
            for c in high:
                c.wait_send()

        @pl.when(jnp.logical_and(z <= p.z, p.z < Z - 1))
        def _():
            along_z(z, True).wait_send()

        @pl.when(jnp.logical_and(z >= p.z, p.z > 0))
        def _():
            along_z(z, False).wait_send()

        for y in range(p.Y):
            for x in range(p.X):
                to_partner(z, y, x).wait_send()
                theirs = all_ref.at[z, y, x, 1 - p.c]
                copy(theirs, theirs, across.at[z, y, x], partner).wait_recv()

        return carry

    lax.fori_loop(0, Z, finish, 0)


def column_of(row):
    return jnp.broadcast_to(row, (128, 128)).T


def spread_vectors(params_ref, gain_ref, taps_ref, heads_ref, inner_ref):
    row = D // 128
    gain_ref[...] = beside(*[params_ref[j : j + 1] for j in range(row)])
    for k in range(KCONV + 1):
        for j in range(CONVCH // 128):
            taps_ref[k, 128 * j : 128 * j + 128] = column_of(params_ref[row : row + 1])
            row += 1
    heads = column_of(params_ref[row : row + 1])
    heads_ref[0] = heads[:HEADS]
    heads_ref[1] = -jnp.exp(heads[HEADS : 2 * HEADS])
    heads_ref[2] = heads[2 * HEADS : 3 * HEADS]
    row = params_ref.shape[0] - INNER // 128
    for j in range(INNER // 128):
        inner_ref[128 * j : 128 * j + 128] = column_of(params_ref[row + j : row + j + 1])


def cuts_of(count):
    widths = [(0, INNER), (INNER, CONV_A), (INNER + CONV_A, CONVCH - CONV_A)]
    return [(start, width, width // count) for start, width in widths], INNER // count


def first_of(d, width, count):
    return d % 2 * (width // 2) + d // 2 * (width // count)


def spread_moments(m_in_ref, m_out_ref, blocks_ref):
    count, own, lanes_in_block = blocks_ref.shape
    ins, outs = cuts_of(count)
    step = m_in_ref[:, WIDE:]
    used = sum(each for _, _, each in ins) + outs + HEADS
    for d in range(count):
        pieces = []
        for start, width, each in ins:
            at = start + first_of(d, width, count)
            pieces.append(m_in_ref[:, at : at + each])
        at = first_of(d, INNER, count)
        pieces += [m_out_ref[:, at : at + outs], step]
        blocks_ref[d] = beside(*pieces, jnp.zeros((own, lanes_in_block - used), F32))


def gather_call(weight_in, weight_out, moment_in, moment_out, params, sizes, collective_id):
    Z, F = sizes
    X, Y = F // 4, 2
    own = weight_in.shape[0]
    count = Z * F
    gap = jnp.zeros((-params.shape[0] % 128,), F32)
    params = jnp.concatenate([params, gap, params[-INNER:]]).reshape(-1, 128)
    vmem = pl.BlockSpec(memory_space=pltpu.VMEM)
    hbm = pl.BlockSpec(memory_space=pl.ANY)
    whole_weights, blocks, *vectors = pl.pallas_call(
        functools.partial(gather_kernel, sizes),
        out_shape=[
            shape(Z, Y, X, 2, own, 2 * HALF, dtype=BF16), shape(count, own, 256), shape(1, D),
            shape(KCONV + 1, CONVCH, CHUNK), shape(3, HEADS, CHUNK), shape(INNER, CHUNK),
        ],
        in_specs=[vmem] * 5,
        out_specs=[hbm] + [vmem] * 5,
        scratch_shapes=[
            pltpu.VMEM((own, 2 * HALF), BF16), pltpu.SemaphoreType.DMA, pltpu.SemaphoreType.DMA((2, Z, 2)),
            pltpu.SemaphoreType.DMA((Z, X, 2)), pltpu.SemaphoreType.DMA((Z, X, 2)),
            pltpu.SemaphoreType.DMA((Z, Y, X, 2)),
        ],
        compiler_params=pltpu.CompilerParams(
            collective_id=collective_id, has_side_effects=True, vmem_limit_bytes=60 * 2**20
        ),
        name="weights_gather",
    )(weight_in, weight_out, moment_in, moment_out, params)
    return whole_weights.reshape(D, 2 * HALF), blocks, vectors


def gram_rows(slab, row):
    high, low = split(slab)
    left = above(high, low, high)[:, 128 * row : 128 * row + 128]
    return dot_tn(left, above(high, high, low)[:, 128 * row :])


def pack_gram(targets, slab):
    Z, Y, X, per, _ = targets[0].shape
    rows = above(*[
        beside(gram_rows(slab, i), gram_rows(slab, D // 128 - 1 - i)) for i in range(D // 256)
    ])
    if Z * Y * X * per > rows.shape[0]:
        rows = above(rows, jnp.zeros((Z * Y * X * per - rows.shape[0], rows.shape[1]), F32))
    at = 0
    for target in targets:
        cols = slice(at, at + target.shape[4])
        for i in range(Z * Y * X):
            target[i // (Y * X), i // X % Y, i % X] = rows[per * i : per * i + per, cols]
        at += target.shape[4]


def unpack_gram(gram, packed):
    Z, Y, X, _, _ = packed[0].shape
    rows = beside(*[
        above(*[part[i // (Y * X), i // X % Y, i % X] for i in range(Z * Y * X)])
        for part in packed
    ])
    for i in range(D // 256):
        pair = rows[128 * i : 128 * i + 128]
        wide_part, j = D - 128 * i, D // 128 - 1 - i
        for row, part in ((i, pair[:, :wide_part]), (j, pair[:, wide_part:])):
            gram[128 * row : 128 * row + 128, 128 * row :] = part
            for k in range(row + 1, D // 128):
                at = 128 * (k - row)
                gram[128 * k : 128 * k + 128, 128 * row : 128 * row + 128] = part[
                    :, at : at + 128
                ].T


BEHIND = 2


class AllSum:
    def __init__(self, place, work):
        self.p = place
        self.total, self.acc, self.core, self.core_sems = work[0], work[1], work[7], work[8]
        self.held, self.z_sems, self.back_sems = work[9:12]
        self.plane = Plane(place, *work[1:7])
        self.steps = [
            self.pair, self.second, self.cross, self.turn, self.spread, self.spread_on, self.done,
        ]

    def to_core(self):
        p = self.p
        return remote(
            self.total, self.core, self.core_sems.at[0], self.core_sems.at[1], p.at(c=1 - p.c)
        )

    def pair(self):
        p = self.p
        self.to_core().wait()

        def place_of(i):
            return i // (p.Y * p.X), lax.rem(i // p.X, p.Y), lax.rem(i, p.X)

        add_blocks(
            lambda i: self.acc.at[place_of(i)], lambda i: self.core.at[place_of(i)],
            p.Z * p.Y * p.X,
        )
        self.plane.start(0)

    def second(self):
        self.plane.finish(0)
        self.plane.start(1)

    def over(self, s):
        p = self.p
        z = lax.rem(p.z + s, p.Z)
        sem = self.z_sems.at[0, s]
        return remote(
            self.acc.at[z, p.y, p.x], self.held.at[s - 1], sem.at[0], sem.at[1], p.at(z=z)
        )

    def cross(self):
        self.plane.finish(1)
        for s in range(1, self.p.Z):
            self.over(s).start()

    def back(self, s, mine):
        p = self.p
        sem = self.z_sems.at[1, s]
        z = p.z if mine else lax.rem(p.z + p.Z - s, p.Z)
        ref = self.total.at[z, p.y, p.x]
        return remote(ref, ref, sem.at[0], sem.at[1], p.at(z=lax.rem(p.z + s, p.Z)))

    def turn(self):
        p = self.p
        for s in range(1, p.Z):
            self.over(s).wait()
        result = self.acc[p.z, p.y, p.x]
        for s in range(1, p.Z):
            result = result + self.held[s - 1]
        self.total[p.z, p.y, p.x] = result
        for s in range(1, p.Z):
            self.back(s, True).start()

    def planes(self, stage, mine):
        p, total, h = self.p, self.total, self.p.Z // 2
        low, high = pl.ds(0, h), pl.ds(h, p.Z - h)
        found = []
        for s in range(1, p.X):
            sem = self.back_sems.at[stage * p.X + s]
            x = p.x if mine else lax.rem(p.x + p.X - s, p.X)
            ref = total.at[high, p.y, x] if stage == 0 else total.at[low, :, x]
            found.append(remote(ref, ref, sem.at[0], sem.at[1], p.at(x=p.other_x(s))))
        sem = self.back_sems.at[stage * p.X]
        y = p.y if mine else 1 - p.y
        ref = total.at[low, y, p.x] if stage == 0 else total.at[high, y]
        found.append(remote(ref, ref, sem.at[0], sem.at[1], p.at(y=1 - p.y)))
        return found

    def arrive(self, copies):
        for mine, theirs in copies:
            mine.wait_send()
            theirs.wait_recv()

    def spread(self):
        self.arrive([(self.back(s, True), self.back(s, False)) for s in range(1, self.p.Z)])
        for copy in self.planes(0, True):
            copy.start()

    def spread_on(self):
        self.arrive(zip(self.planes(0, True), self.planes(0, False)))
        for copy in self.planes(1, True):
            copy.start()

    def done(self):
        self.arrive(zip(self.planes(1, True), self.planes(1, False)))


def all_sum_scratch(sizes, block):
    Z, X, Y = sizes[0], sizes[1] // 4, 2
    dma = pltpu.SemaphoreType.DMA
    return [pltpu.VMEM((Z, Y, X) + block, F32)] + plane_scratch(sizes, block) + [
        pltpu.VMEM((Z, Y, X) + block, F32), dma((2,)), pltpu.VMEM((Z - 1,) + block, F32),
        dma((2, Z, 2)), dma((2 * X, 2)),
    ]


def put_left(left, value, rows):
    high, low = split(value)
    left[rows] = beside(high, low, high)


def put_right(right, value, row):
    high, low = split(value)
    size = value.shape[0]
    right[row : row + size] = high
    right[D + row : D + row + size] = high
    right[2 * D + row : 2 * D + row + size] = low


TILE = 256


def symmetric_product(target, left, right):
    for i in range(D // TILE):
        rows = slice(TILE * i, TILE * i + TILE)
        part = dot(left[rows], right[:, TILE * i :])
        target[rows, TILE * i :] = part
        for j in range(i + 1, D // TILE):
            at = TILE * (j - i)
            target[TILE * j : TILE * j + TILE, rows] = part[:, at : at + TILE].T


def iterate(gram, square, factor, left, right, slab, slab_left):
    tiles = [slice(TILE * i, TILE * i + TILE) for i in range(D // TILE)]
    row = lax.broadcasted_iota(jnp.int32, (TILE, D), 0)
    col = lax.broadcasted_iota(jnp.int32, (TILE, D), 1)
    diagonals = [(row + TILE * i == col) for i in range(D // TILE)]
    trace = jnp.zeros((8, D), F32)
    for rows, diagonal in zip(tiles, diagonals):
        trace = trace + fold(jnp.where(diagonal, gram[rows], 0.0))
    trace = jnp.sum(jnp.sum(trace, axis=0, keepdims=True), axis=1, keepdims=True)
    scale = 1.0 / (jnp.sqrt(trace) + 1e-07)
    for rows in tiles:
        gram[rows] = gram[rows] * (scale * scale)
    slab[...] = slab[...] * scale

    def step(iteration, carry):
        for i, rows in enumerate(tiles):
            value = gram[rows]
            put_left(left, value, rows)
            put_right(right, value, TILE * i)
        symmetric_product(square, left, right)
        for i, rows in enumerate(tiles):
            value = COEF_B * gram[rows] + COEF_C * square[rows]
            put_right(right, value + jnp.where(diagonals[i], COEF_A, 0.0), TILE * i)
        put_left(slab_left, slab[...], slice(None))
        slab[...] = dot(slab_left[...], right[...])
        symmetric_product(factor, left, right)
        for rows in tiles:
            put_left(left, factor[rows], rows)
        symmetric_product(gram, left, right)
        return carry

    lax.fori_loop(0, ITERS - 1, step, 0)
    for i, rows in enumerate(tiles):
        put_right(right, gram[rows], TILE * i)
    first = slab[...]
    put_left(slab_left, first, slice(None))
    once = dot(slab_left[...], right[...])
    put_left(slab_left, once, slice(None))
    slab[...] = COEF_A * first + COEF_B * once + COEF_C * dot(slab_left[...], right[...])


def exact_pick(chosen, rows):
    high = rows.astype(BF16)
    rest = rows - high.astype(F32)
    mid = rest.astype(BF16)
    low = (rest - mid.astype(F32)).astype(BF16)
    return dot_nt(chosen, high) + dot_nt(chosen, mid) + dot_nt(chosen, low)


def update_kernel(
    sizes, gate_ref, conv_a_ref, conv_b_ref, out_ref, small_ref, old_ref, moved_ref, smalls_ref, spread_ref, step_ref,
    give, given, give_sems, messages, smalls, mats, left, right, slab, slab_left,
    swap_send, swap_recv, local, *work,
):
    p = Place(sizes)
    count = p.Z * p.F
    own = D // count
    gates = gate_ref.shape[0]
    ins = gates + conv_a_ref.shape[0] + conv_b_ref.shape[0]
    greet_all(p, False)
    swaps = [
        Swap(p, src, dst, swap_send.at[k], swap_recv.at[k], local.at[k], same, narrow)
        for k, (src, dst, same, narrow) in enumerate([
            (small_ref, smalls, True, None), (messages.at[0], moved_ref, False, None),
            (messages.at[1], spread_ref, False, -(-2 * gates // 128) * 128),
        ])
    ]
    old = old_ref[...].T
    new_in = above(gate_ref[...], conv_a_ref[...], conv_b_ref[...])
    new_out = out_ref[...]

    def push(gradient, moment):
        return gradient + MOMENTUM * (MOMENTUM * moment + gradient)

    push_in = push(new_in, old[:ins])
    push_out = above(push(new_out, old[ins : ins + gates]), jnp.zeros((ins - gates, D), F32))
    in_core = p.c == 0
    give[...] = jnp.where(in_core, push_out, push_in)
    slab[:ins] = jnp.where(in_core, push_in, push_out)
    partner = p.at(c=1 - p.c)
    pieces = [AllSum(p, work[:12]), AllSum(p, work[12:])]
    pack_gram([piece.total for piece in pieces], give[...])
    await_all(p)
    for piece in pieces:
        piece.to_core().start()
    exchange = remote(give, given, give_sems.at[0], give_sems.at[1], partner)
    exchange.start()
    swaps[0].start()
    pack_gram([piece.acc for piece in pieces], slab[:ins])

    def store_messages(k, turned):
        turned = beside(turned, jnp.zeros((D, 256 - turned.shape[1]), F32)) if (
            turned.shape[1] < 256) else turned
        for d in range(count):
            messages[k, d] = turned[own * d : own * d + own]

    steps = len(pieces[0].steps)
    for k in range(steps + BEHIND):
        for which, piece in enumerate(pieces):
            if 0 <= k - BEHIND * which < steps:
                piece.steps[k - BEHIND * which]()
        if k == 0:
            store_messages(0, above(new_in, new_out).T)
    exchange.wait()
    swaps[0].wait()
    swaps[1].start()
    smalls_ref[...] = smalls[...]
    rows = smalls[...].reshape(-1, 128)
    new_step = beside(*[rows[HEADS * j : HEADS * j + HEADS] for j in range(D // 128)])
    mine_at = lax.broadcasted_iota(jnp.int32, (own, D), 0) + own * (p.z * p.F + p.f)
    chosen = (lax.broadcasted_iota(jnp.int32, (own, D), 1) == mine_at).astype(F32).astype(BF16)
    step_ref[...] = exact_pick(chosen, new_step)
    push_step = push(new_step, old_ref[...].T[ins + gates : ins + gates + HEADS])
    push_step = jnp.where(in_core, push_step, 0.0)
    mine, theirs = slab[:ins], given[...]
    slab_in = above(mine, theirs, push_step)
    slab_out = above(theirs[:gates], mine[:gates], jnp.zeros((2 * (ins - gates) + HEADS, D), F32))
    slab[: 2 * ins + HEADS] = jnp.where(in_core, slab_in, slab_out)
    slab[2 * ins + HEADS :] = jnp.zeros((slab.shape[0] - 2 * ins - HEADS, D), F32)
    gram = mats.at[0]
    unpack_gram(gram, [piece.total for piece in pieces])
    step_high, step_low = split(push_step)
    step_left = above(step_high, step_low, step_high)
    gram[...] = gram[...] + dot_tn(step_left, above(step_high, step_high, step_low))
    iterate(gram, mats.at[1], mats.at[2], left, right, slab, slab_left)
    store_messages(1, slab[...].T)
    swaps[2].start()
    swaps[1].wait()
    swaps[2].wait()


def update_call(parts, small, old, sizes, collective_id):
    count = sizes[0] * sizes[1]
    own = D // count
    chips = count // 2
    ins = sum(part.shape[0] for part in parts[:3])
    per = -(-(D // 2) // (8 * chips)) * 8
    blocks = [(per, 512), (per, D + 128 - 512)]
    vmem = pl.BlockSpec(memory_space=pltpu.VMEM)
    hbm = pl.BlockSpec(memory_space=pl.ANY)
    dma = pltpu.SemaphoreType.DMA
    return pl.pallas_call(
        functools.partial(update_kernel, sizes),
        out_shape=[
            shape(count, own, 256), shape(count, *small.shape), shape(count, own, 256),
            shape(own, HEADS),
        ],
        in_specs=[vmem] * 6,
        out_specs=[hbm, vmem, hbm, vmem],
        scratch_shapes=[
            pltpu.VMEM((ins, D), F32), pltpu.VMEM((ins, D), F32), dma((2,)),
            pltpu.VMEM((2, count, own, 256), F32), pltpu.VMEM((count,) + small.shape, F32),
            pltpu.VMEM((3, D, D), F32),
            pltpu.VMEM((D, 3 * D), BF16), pltpu.VMEM((3 * D, D), BF16),
            pltpu.VMEM((256, D), F32), pltpu.VMEM((256, 3 * D), BF16),
            dma((3, count)), dma((3, count)), dma((3,)),
        ]
        + all_sum_scratch(sizes, blocks[0])
        + all_sum_scratch(sizes, blocks[1]),
        compiler_params=pltpu.CompilerParams(
            collective_id=collective_id, has_side_effects=True, vmem_limit_bytes=56 * 2**20
        ),
        name="update",
    )(*parts, small, old)


def finish_kernel(
    moved_ref, spread_ref, step_ref, w_in_ref, w_out_ref, m_in_ref, m_out_ref, dx_ref,
    g_in_ref, g_out_ref, new_m_in_ref, new_m_out_ref, new_w_in_ref, new_w_out_ref, dx_out_ref,
    held, sems,
):
    load = pltpu.make_async_copy(dx_ref, held, sems.at[0])
    store = pltpu.make_async_copy(held, dx_out_ref, sems.at[1])
    load.start()
    count = moved_ref.shape[0]
    cuts, outs = cuts_of(count)
    ins = sum(each for _, _, each in cuts)
    decay = 1.0 - MATRIX_RATE * WEIGHT_DECAY
    order = [(2 * chip + core, core) for core in range(2) for chip in range(count // 2)]
    at = 0
    for start, width, each in cuts:
        cols = slice(start, start + width)
        g_in_ref[:, cols] = beside(*[moved_ref[d, :, at : at + each] for d, _ in order])
        new_w_in_ref[:, cols] = beside(*[
            spread_ref[d - core, :, ins * core + at : ins * core + at + each] for d, core in order
        ])
        at += each
    load.wait()
    store.start()
    g_in_ref[:, WIDE:] = step_ref[...]
    new_w_in_ref[:, WIDE:] = spread_ref[0, :, 2 * ins : 2 * ins + HEADS]
    g_out_ref[...] = beside(*[moved_ref[d, :, ins : ins + outs] for d, _ in order])
    new_w_out_ref[...] = beside(*[
        spread_ref[d - core + 1, :, outs * core : outs * core + outs] for d, core in order
    ])
    for wide_side, g_ref, m_ref, w_ref, new_m_ref, new_w_ref in (
        (IN_W, g_in_ref, m_in_ref, w_in_ref, new_m_in_ref, new_w_in_ref),
        (INNER, g_out_ref, m_out_ref, w_out_ref, new_m_out_ref, new_w_out_ref),
    ):
        new_m_ref[...] = MOMENTUM * m_ref[...] + g_ref[...]
        rate = MATRIX_RATE * 0.2 * math.sqrt(max(D, wide_side))
        new_w_ref[...] = w_ref[...] * decay - rate * new_w_ref[...]
    store.wait()


def finish_call(moved, spread, step_rows, matrices, dx):
    vmem = pl.BlockSpec(memory_space=pltpu.VMEM)
    hbm = pl.BlockSpec(memory_space=pl.ANY)
    return pl.pallas_call(
        finish_kernel,
        out_shape=[shape(*matrix.shape) for matrix in matrices[:2]] * 3 + [shape(*dx.shape)],
        in_specs=[vmem] * 7 + [hbm],
        out_specs=[vmem] * 6 + [hbm],
        scratch_shapes=[pltpu.VMEM(dx.shape, F32), pltpu.SemaphoreType.DMA((2,))],
        compiler_params=pltpu.CompilerParams(vmem_limit_bytes=60 * 2**20),
        name="finish",
    )(moved, spread, step_rows, *matrices, dx)


def shards(
    inputs, cotangent, weight_in, weight_out, small_params, moment_in, moment_out, moment_small
):
    sizes = (lax.axis_size("dp"), lax.axis_size("fsdp"))
    weights, blocks, vectors = gather_call(
        weight_in, weight_out, moment_in, moment_out, small_params, sizes, 0
    )
    output, dx, columns, factors, small, old = block_and_gradients(
        inputs[0], cotangent[0], weights, vectors, blocks, sizes, (3, 4)
    )
    new_out, new_gate, new_conv_a, new_conv_b, new_small = scatter_call(
        columns, factors, small, sizes, 1
    )
    moved, smalls, spread, step_rows = update_call(
        (new_gate, new_conv_a, new_conv_b, new_out), new_small, old.reshape(D, 256), sizes, 2
    )
    smalls = smalls.reshape(-1)
    grad_small = smalls[HEADS * D : HEADS * D + SMALL]
    grad_in, grad_out, new_moment_in, new_moment_out, new_weight_in, new_weight_out, dx = (
        finish_call(
            moved, spread, step_rows, (weight_in, weight_out, moment_in, moment_out), dx
        )
    )
    new_moment_small = MOMENTUM * moment_small + grad_small
    new_small_params = small_params - SMALL_RATE * new_moment_small
    return (
        output[None],
        dx[None],
        grad_in,
        grad_out,
        grad_small,
        new_moment_in,
        new_moment_out,
        new_moment_small,
        new_weight_in,
        new_weight_out,
        new_small_params,
    )


def solution(mesh):
    return jax.shard_map(
        shards,
        mesh=mesh,
        in_specs=(
            P(("dp", "fsdp"), None, None),
            P(("dp", "fsdp"), None, None),
            P(("dp", "fsdp"), None),
            P(("dp", "fsdp"), None),
            P(),
            P(("dp", "fsdp"), None),
            P(("dp", "fsdp"), None),
            P(),
        ),
        out_specs=(
            P(("dp", "fsdp"), None, None),
            P(("dp", "fsdp"), None, None),
            P(("dp", "fsdp"), None),
            P(("dp", "fsdp"), None),
            P(),
            P(("dp", "fsdp"), None),
            P(("dp", "fsdp"), None),
            P(),
            P(("dp", "fsdp"), None),
            P(("dp", "fsdp"), None),
            P(),
        ),
        check_vma=False,
    )
```

```python
import functools
import math

import jax
import jax.numpy as jnp
from jax import lax
from jax.experimental import pallas as pl
from jax.experimental.pallas import tpu as pltpu
from jax.sharding import PartitionSpec as P

D = 768
HEADS = 24
HEAD_DIM = 64
NSTATE = 128
KCONV = 4
LEN = 1024
ITERS = 5
INNER = 1536
CONVCH = 1792
IN_W = 3352
SMALL = 11336
WIDE = INNER + CONVCH
TAIL_SUMS = 1664 - 2 * HEADS
STEP = 32
CONV_A = 768
HALF = 2560
OUT_AT = WIDE - HALF
STEP_AT = OUT_AT + INNER

MOMENTUM = 0.95
MATRIX_RATE = 0.15
WEIGHT_DECAY = 0.1
SMALL_RATE = 0.01
EPSILON = 1e-05
COEF_A = 3.4445
COEF_B = -4.775
COEF_C = 2.0315

F32 = jnp.float32
BF16 = jnp.bfloat16
CHUNK = 128
STRIP = 256
PER = STRIP // CHUNK
STRIPS = LEN // STRIP
GRAD_TILE = 256
GROUP = 4


def dot(a, b):
    return lax.dot_general(a, b, (((1,), (0,)), ((), ())), preferred_element_type=F32)


def dot_nt(a, b):
    return lax.dot_general(a, b, (((1,), (1,)), ((), ())), preferred_element_type=F32)


def dot_tn(a, b):
    return lax.dot_general(a, b, (((0,), (0,)), ((), ())), preferred_element_type=F32)


def split(v):
    high = v.astype(BF16)
    return high, (v - high.astype(F32)).astype(BF16)


def beside(*parts):
    return jnp.concatenate(parts, axis=1)


def above(*parts):
    return jnp.concatenate(parts, axis=0)


def right_pair(b):
    high, low = split(b)
    return above(beside(high, low), beside(high, jnp.zeros_like(low)))


def three_pass(a, pair):
    high, low = split(a)
    both = dot(beside(high, low), pair)
    half = both.shape[1] // 2
    return both[:, :half] + both[:, half:]


def exact_sum(a, ones):
    high = a.astype(BF16)
    rest = a - high.astype(F32)
    mid = rest.astype(BF16)
    low = (rest - mid.astype(F32)).astype(BF16)
    return dot(beside(high, mid, low), above(ones, ones, ones))


def lane_sums(a):
    high = a.astype(BF16)
    rest = a - high.astype(F32)
    mid = rest.astype(BF16)
    low = (rest - mid.astype(F32)).astype(BF16)
    parts = beside(high, mid, low)
    return dot_nt(jnp.ones((8, parts.shape[1]), BF16), parts)


def stack_left(a):
    high, low = split(a)
    return above(beside(high, high), beside(low, jnp.zeros_like(low)))


def fold(rows):
    total = rows[0:8]
    for i in range(1, rows.shape[0] // 8):
        total = total + rows[8 * i : 8 * i + 8]
    return total


def row_sum(rows):
    return jnp.sum(fold(rows), axis=0, keepdims=True)


def upper():
    row = lax.broadcasted_iota(jnp.int32, (CHUNK, CHUNK), 0)
    col = lax.broadcasted_iota(jnp.int32, (CHUNK, CHUNK), 1)
    return col >= row


def softplus(v):
    return jnp.maximum(v, 0.0) + jnp.log1p(jnp.exp(-jnp.abs(v)))


def rates_of(raw, heads_ref, ones):
    steps = softplus(raw + heads_ref[0])
    logs = exact_sum(steps * heads_ref[1], ones)
    last = jnp.broadcast_to(logs[:, CHUNK - 1 : CHUNK], logs.shape)
    columns = above(logs, jnp.zeros((CHUNK - HEADS, CHUNK), F32)).T
    return steps, logs, columns, jnp.exp(logs), jnp.exp(last - logs), jnp.exp(last)


def silu(v):
    return v * jax.nn.sigmoid(v)


def wide(v):
    return beside(*([v] * PER))


def strip_at(s):
    return pl.ds(pl.multiple_of(s * STRIP, STRIP), STRIP)


def half_rows(rows, c):
    return pl.ds(pl.multiple_of(c * (rows // 2), rows // 2), rows // 2)


class Box:
    def __init__(self, box, dst, sems, partner):
        self.box, self.dst, self.sems, self.partner = box, dst, sems, partner

    def copy(self, s):
        sem = self.sems.at[s]
        return remote(
            self.box.at[lax.rem(s, 2)], self.dst(s), sem.at[0], sem.at[1], self.partner
        )

    def fill(self, s, value, back=False):
        @pl.when(pl.program_id(0) > 1)
        def _():
            self.copy(s + 2 if back else s - 2).wait_send()

        self.box[lax.rem(s, 2)] = value
        self.copy(s).start()

    def finish(self, back=False):
        for s in range(2):
            self.copy(s if back else STRIPS - 1 - s).wait_send()
        for s in range(STRIPS):
            self.copy(s).wait_recv()


def forward_kernel(
    sizes, x_ref, back_ref, first_ref, second_ref, gain_ref, taps_in, heads_ref, inner_in,
    blocks_ref, whole_back_ref,
    out_ref, hb_ref, cin_ref, c_ref, raw_ref, s_ref, own_normed_ref,
    dy_ref, dgate_ref, own_dgate_ref, dlogs_ref, tail_sums_ref, moved_ref,
    peer_normed_ref, peer_dgate_ref, peer_hb_ref, peer_back_ref,
    act, z, mixed, dnormed, state, tail, turned, dskip, dinner, normed_ref,
    taps_ref, inner_ref, load_sems, box_normed, box_dgate, box_hb, box_sems, back_sems, *work,
):
    p = Place(sizes)
    swap = Swap(p, blocks_ref, moved_ref, *work)
    partner = p.at(c=1 - p.c)
    strip = pl.program_id(0)
    back_copy = remote(
        whole_back_ref, peer_back_ref, back_sems.at[0], back_sems.at[1], partner
    )
    boxes = [
        Box(box, lambda s, ref=ref: ref.at[:, strip_at(s)], box_sems.at[k], partner)
        for k, (box, ref) in enumerate(
            [(box_normed, peer_normed_ref), (box_dgate, peer_dgate_ref)]
        )
    ]
    boxes.append(Box(box_hb, lambda s: peer_hb_ref.at[strip_at(s)], box_sems.at[2], partner))

    @pl.when(strip == 0)
    def _():
        loads = [
            pltpu.make_async_copy(taps_in, taps_ref, load_sems.at[0]),
            pltpu.make_async_copy(inner_in, inner_ref, load_sems.at[1]),
        ]
        for load in loads:
            load.start()
        greet_all(p, False)
        state[...] = jnp.zeros_like(state)
        tail[...] = jnp.zeros_like(tail)
        dskip[...] = jnp.zeros_like(dskip)
        dinner[...] = jnp.zeros_like(dinner)
        for i in range(HALF // 256):
            part = slice(256 * i, 256 * i + 256)
            turned[0, part] = first_ref[:, part].T
            turned[1, part] = second_ref[:, part].T
        for load in loads:
            load.wait()
        await_all(p)
        back_copy.start()
        swap.start()

    x = x_ref[...].astype(F32)
    scaled = x * lax.rsqrt(jnp.mean(x * x, axis=-1, keepdims=True) + EPSILON) * gain_ref[...]
    hb = scaled.astype(BF16)
    hb_ref[...] = hb
    boxes[2].fill(strip, hb)
    back = back_ref[...]
    raw_ref[...] = dot_nt(turned[1, STEP_AT : STEP_AT + STEP], hb)

    lane = lax.broadcasted_iota(jnp.int32, (64, CHUNK), 1)

    def later(cols, steps, before):
        turned_cols = [before] + [pltpu.roll(col, steps, 1) for col in cols]
        pairs = zip(turned_cols[:-1], turned_cols[1:])
        return [jnp.where(lane < steps, a, b) for a, b in pairs], turned_cols[-1]

    def conv_tile(i):
        rows = slice(64 * i, 64 * i + 64)
        cur = cin_ref[rows]
        cols = [cur[:, CHUNK * j : CHUNK * j + CHUNK] for j in range(PER)]
        taps = [taps_ref[k, rows] for k in range(KCONV + 1)]
        ones_late, tail[0, rows] = later(cols, 1, tail[0, rows])
        early = [taps[1] * a + taps[0] * b for a, b in zip(cols, ones_late)]
        twos_late, tail[1, rows] = later(early, 2, tail[1, rows])
        total = beside(*[
            taps[4] + c + taps[2] * b + taps[3] * a for a, b, c in zip(cols, ones_late, twos_late)
        ])
        c_ref[rows] = total
        act[rows] = total * jax.nn.sigmoid(total)

    def project(i):
        start = INNER + 256 * i
        rows = turned[start // HALF, start % HALF : start % HALF + 256]
        cin_ref[256 * i : 256 * i + 256] = dot_nt(rows, hb)

    project(0)
    for i in range(CONVCH // 256):
        if i + 1 < CONVCH // 256:
            project(i + 1)
        if i < INNER // 256:
            part = slice(256 * i, 256 * i + 256)
            z[part] = dot_nt(turned[0, part], hb)
            dnormed[part] = dot_nt(turned[1, OUT_AT + 256 * i : OUT_AT + 256 * i + 256], back)
        for q in range(4):
            conv_tile(4 * i + q)
    causal = upper()
    ones = causal.astype(F32).astype(BF16)

    def chunk(j, carry):
        cols = pl.ds(pl.multiple_of(j * CHUNK, CHUNK), CHUNK)
        steps, logs, columns, grown, to_end, through = rates_of(
            raw_ref[0:HEADS, cols], heads_ref, ones
        )
        in_map = act[INNER : INNER + NSTATE, cols].T
        in_pair = right_pair(in_map)
        out_pair = right_pair(act[INNER + NSTATE :, cols])
        scores = three_pass(in_map, out_pair)
        for g in range(HEADS // GROUP):
            rows = slice(g * GROUP * HEAD_DIM, (g + 1) * GROUP * HEAD_DIM)
            held = state[rows]
            s_ref[j, rows] = held
            across = three_pass(held, out_pair)
            ending, kept = [], []
            for q in range(GROUP):
                h = g * GROUP + q
                mine = slice(h * HEAD_DIM, (h + 1) * HEAD_DIM)
                values = act[mine, cols]
                fed = values * steps[h : h + 1]
                gaps = logs[h : h + 1] - jnp.broadcast_to(columns[:, h : h + 1], (CHUNK, CHUNK))
                weights = scores * jnp.where(causal, jnp.exp(gaps), 0.0)
                both = dot(stack_left(fed), above(*split(weights)))
                y = both[:HEAD_DIM] + both[HEAD_DIM:]
                y = y + across[q * HEAD_DIM : (q + 1) * HEAD_DIM] * grown[h : h + 1]
                mixed[mine, cols] = y + heads_ref[2][h : h + 1] * values
                ending.append(fed * to_end[h : h + 1])
                kept.append(jnp.broadcast_to(through[h : h + 1], (HEAD_DIM, CHUNK)))
            state[rows] = held * above(*kept) + three_pass(above(*ending), in_pair)
        return carry

    lax.fori_loop(0, PER, chunk, 0)

    def mean_tile(h, totals):
        rows = pl.ds(pl.multiple_of(h * HEAD_DIM, HEAD_DIM), HEAD_DIM)
        gate = z[rows, :]
        opened = mixed[rows, :] * (gate * jax.nn.sigmoid(gate))
        gained = dnormed[rows, :] * wide(inner_ref[rows, :]) * opened
        return totals[0] + fold(opened * opened), totals[1] + fold(gained)

    nothing = jnp.zeros((8, STRIP), F32)
    squares, gains = lax.fori_loop(0, HEADS, mean_tile, (nothing, nothing), unroll=4)
    mean = jnp.sum(squares, axis=0, keepdims=True) * (1.0 / INNER)
    r = lax.rsqrt(mean + EPSILON)
    pulled = jnp.sum(gains, axis=0, keepdims=True) * (1.0 / INNER) * (r * r * r)

    def gate_tile(h, carry):
        rows = pl.ds(pl.multiple_of(h * HEAD_DIM, HEAD_DIM), HEAD_DIM)
        gate = z[rows, :]
        skip = wide(heads_ref[2, pl.ds(h, 1), :])
        mix = mixed[rows, :]
        sig = jax.nn.sigmoid(gate)
        sil = gate * sig
        opened = mix * sil
        normed = opened * r
        inner = wide(inner_ref[rows, :])
        normed_ref[rows, :] = (normed * inner).astype(BF16)
        dn = dnormed[rows, :]
        gained = dn * normed
        dinner[rows, :] += gained[:, :CHUNK] + gained[:, CHUNK:]
        dopened = dn * inner * r - opened * pulled
        dmixed = dopened * sil
        dy_ref[rows, :] = dmixed
        dgate_ref[rows, :] = (dopened * mix * (sig * (1.0 + gate * (1.0 - sig)))).astype(BF16)
        skipped = row_sum(dmixed * act[rows, :])
        dskip[pl.ds(h, 1), :] += skipped[:, :CHUNK] + skipped[:, CHUNK:]
        dlogs_ref[pl.ds(h, 1), :] = row_sum(dmixed * mix) - skip * skipped
        return carry

    lax.fori_loop(0, HEADS, gate_tile, 0)
    for box, own, ref in (
        (boxes[0], own_normed_ref, normed_ref), (boxes[1], own_dgate_ref, dgate_ref),
    ):
        own[...] = ref[half_rows(INNER, p.c), :]
        box.fill(strip, ref[half_rows(INNER, 1 - p.c), :])
    for i in range(D // 256):
        part = slice(256 * i, 256 * i + 256)
        branch = dot(second_ref[part, OUT_AT:STEP_AT], normed_ref[...]).T
        out_ref[:, part] = (x_ref[:, part].astype(F32) + branch).astype(BF16)

    @pl.when(pl.program_id(0) == STRIPS - 1)
    def _():
        tail_sums_ref[...] = beside(
            lane_sums(dskip[...]), lane_sums(dinner[...]),
            jnp.zeros((8, tail_sums_ref.shape[1] - HEADS - INNER), F32),
        )
        swap.wait()
        back_copy.wait()
        for box in boxes:
            box.finish()


def backward_kernel(
    sizes, x_ref, back_ref, w_in_ref, step_in_ref, gain_ref, taps_ref, heads_ref,
    cin_ref, c_ref, raw_ref, s_ref, dy, dgate_ref, dlogs, tail_sums_ref, out_part, gate_part,
    dx_ref, own_a_ref, own_b_ref, flat_ref, out_column, gate_column, peer_a_ref, peer_b_ref,
    dconv_a_ref, dconv_b_ref, box_a, box_b, box_sems, dact, dstate, flow, tail, meets, vdu_rows, dstep_ref, dstep_sum, dgain, dtaps_ref, dheads_ref,
    dscaled_turned, *work,
):
    step_now = pl.program_id(0)
    p = Place(sizes)
    partner = p.at(c=1 - p.c)
    strip = STRIPS - 1 - step_now
    boxes = [
        Box(box, lambda s, ref=ref: ref.at[:, strip_at(s)], box_sems.at[k], partner)
        for k, (box, ref) in enumerate([(box_a, peer_a_ref), (box_b, peer_b_ref)])
    ]
    sums = [
        PlaneSum(p, part, work[7 * k : 7 * k + 7]) for k, part in enumerate((out_part, gate_part))
    ]

    @pl.when(step_now == 0)
    def _():
        sums[0].begin()
        greet_near(p, False, False)

    @pl.when(step_now == 0)
    def _():
        dstate[...] = jnp.zeros_like(dstate)
        flow[...] = jnp.zeros_like(flow)
        tail[...] = jnp.zeros_like(tail)
        dgain[...] = jnp.zeros_like(dgain)
        dstep_sum[...] = jnp.zeros_like(dstep_sum)
        dtaps_ref[...] = jnp.zeros_like(dtaps_ref)
        dheads_ref[...] = jnp.zeros_like(dheads_ref)
        await_near(p, False)
        sums[0].start()
        sums[1].begin()

    @pl.when(step_now == 3)
    def _():
        sums[1].plane.finish(0)
        sums[1].plane.start(1)

    back = back_ref[...]

    causal = upper()
    ones = causal.astype(F32).astype(BF16)
    row = lax.broadcasted_iota(jnp.int32, (CHUNK, CHUNK), 0)
    col = lax.broadcasted_iota(jnp.int32, (CHUNK, CHUNK), 1)
    ones_back = (row >= col).astype(F32).astype(BF16)

    def chunk(step, carry):
        j = PER - 1 - step
        cols = pl.ds(pl.multiple_of(j * CHUNK, CHUNK), CHUNK)
        raw = raw_ref[0:HEADS, cols]
        steps, logs, columns, grown, to_end, through = rates_of(raw, heads_ref, ones)
        in_turned = silu(c_ref[INNER : INNER + NSTATE, cols])
        out_turned = silu(c_ref[INNER + NSTATE :, cols])
        in_map = in_turned.T
        out_map = out_turned.T
        scores = three_pass(in_map, right_pair(out_turned))
        in_pair = right_pair(in_turned)
        out_pair = right_pair(out_map)
        dscores = jnp.zeros((CHUNK, CHUNK), F32)
        din = jnp.zeros((NSTATE, CHUNK), F32)
        dout = jnp.zeros((NSTATE, CHUNK), F32)
        for g in range(HEADS // GROUP):
            rows = slice(g * GROUP * HEAD_DIM, (g + 1) * GROUP * HEAD_DIM)
            leaving = dstate[rows]
            entering = s_ref[j, rows]
            from_state = three_pass(leaving, in_pair)
            ending, growing, kept = [], [], []
            for q in range(GROUP):
                h = g * GROUP + q
                mine = slice(h * HEAD_DIM, (h + 1) * HEAD_DIM)
                values = silu(c_ref[mine, cols])
                fed = values * steps[h : h + 1]
                dys = dy[mine, cols]
                gaps = logs[h : h + 1] - jnp.broadcast_to(columns[:, h : h + 1], (CHUNK, CHUNK))
                decay = jnp.where(causal, jnp.exp(gaps), 0.0)
                weights = scores * decay
                both = dot_nt(stack_left(dys), beside(*split(weights)))
                du = both[:HEAD_DIM] + both[HEAD_DIM:]
                du = du + from_state[q * HEAD_DIM : (q + 1) * HEAD_DIM] * to_end[h : h + 1]
                fed_high, fed_low = split(fed)
                dy_high, dy_low = split(dys)
                dweights = dot_tn(
                    above(fed_high, fed_low, fed_high), above(dy_high, dy_high, dy_low)
                )
                dscores = dscores + dweights * decay
                vdu_rows[h : h + 1, :] = row_sum(values * du)
                dact[mine, cols] = du * steps[h : h + 1] + heads_ref[2][h : h + 1] * dys
                ending.append(fed * to_end[h : h + 1])
                growing.append(dys * grown[h : h + 1])
                kept.append(jnp.broadcast_to(through[h : h + 1], (HEAD_DIM, CHUNK)))
            ending = above(*ending)
            growing = above(*growing)
            end_high, end_low = split(ending)
            grow_high, grow_low = split(growing)
            leave_high, leave_low = split(leaving)
            enter_high, enter_low = split(entering)
            din = din + dot_tn(
                above(leave_high, leave_low, leave_high), above(end_high, end_high, end_low)
            )
            dout = dout + dot_tn(
                above(enter_high, enter_low, enter_high), above(grow_high, grow_high, grow_low)
            )
            arrived = leaving * above(*kept) + three_pass(growing, out_pair)
            dstate[rows] = arrived
            meet = arrived * entering
            for q in range(GROUP):
                h = g * GROUP + q
                meets[h : h + 1, :] = row_sum(meet[q * HEAD_DIM : (q + 1) * HEAD_DIM])
        vdu = vdu_rows[...]
        dlog = dlogs[:, cols] - steps * vdu
        drate = exact_sum(dlog, ones_back) + flow[...]
        flow[...] = jnp.broadcast_to(
            jnp.sum(meets[...], axis=1, keepdims=True), (HEADS, CHUNK)
        )
        dsteps = vdu + heads_ref[1] * drate
        draw = dsteps * jax.nn.sigmoid(raw + heads_ref[0])
        dheads_ref[0] += draw
        dheads_ref[1] += drate * steps * heads_ref[1]
        dstep_ref[:, cols] = above(draw, jnp.zeros((STEP - HEADS, CHUNK), F32)).astype(BF16)
        score_high, score_low = split(dscores)
        both = dot_nt(stack_left(out_turned), beside(score_high, score_low))
        dact[INNER : INNER + NSTATE, cols] = din + both[:NSTATE] + both[NSTATE:]
        both = dot(stack_left(in_turned), above(score_high, score_low))
        dact[INNER + NSTATE :, cols] = dout + both[:NSTATE] + both[NSTATE:]
        return carry

    lax.fori_loop(0, PER, chunk, 0)

    @pl.when(step_now == 0)
    def _():
        sums[1].start()

    @pl.when(step_now == 2)
    def _():
        sums[0].plane.finish(0)
        sums[0].plane.start(1)

    lane = lax.broadcasted_iota(jnp.int32, (64, CHUNK), 1)

    def conv_tile(target, start, i):
        rows = slice(start + 64 * i, start + 64 * i + 64)
        c = c_ref[rows]
        sig = jax.nn.sigmoid(c)
        dpre = dact[rows] * (sig * (1.0 + c * (1.0 - sig)))
        cin = cin_ref[rows]
        cols = [dpre[:, CHUNK * j : CHUNK * j + CHUNK] for j in range(PER)]
        dcin = dpre * wide(taps_ref[KCONV - 1, rows])
        grad = cin * dpre
        dtaps_ref[KCONV - 1, rows] += grad[:, :CHUNK] + grad[:, CHUNK:]
        dtaps_ref[KCONV, rows] += dpre[:, :CHUNK] + dpre[:, CHUNK:]
        for k in range(KCONV - 1):
            ahead = KCONV - 1 - k
            turned = [pltpu.roll(col, CHUNK - ahead, 1) for col in cols] + [tail[k, rows]]
            tail[k, rows] = turned[0]
            pairs = zip(turned[:-1], turned[1:])
            shifted = beside(*[jnp.where(lane < CHUNK - ahead, a, b) for a, b in pairs])
            dcin = dcin + shifted * wide(taps_ref[k, rows])
            grad = cin * shifted
            dtaps_ref[k, rows] += grad[:, :CHUNK] + grad[:, CHUNK:]
        target[64 * i : 64 * i + 64] = dcin.astype(BF16)

    thirds = [slice(256 * i, 256 * i + 256) for i in range(D // 256)]
    conv_at = INNER + CONV_A
    tiles = CONV_A // 64
    for i in range(tiles):
        conv_tile(dconv_a_ref, 0, i)
        if i % 4 == 0:
            part = thirds[i // 4]
            dscaled_turned[part] = dot(w_in_ref[part, :INNER], dgate_ref[...])
    for i in range((CONVCH - CONV_A) // 64):
        conv_tile(dconv_b_ref, CONV_A, i)
        if i % 4 == 0 and i // 4 < len(thirds):
            part = thirds[i // 4]
            dscaled_turned[part] += dot(w_in_ref[part, INNER:conv_at], dconv_a_ref[...])
    for box, own, ref in (
        (boxes[0], own_a_ref, dconv_a_ref), (boxes[1], own_b_ref, dconv_b_ref),
    ):
        own[...] = ref[half_rows(ref.shape[0], p.c), :]
        box.fill(strip, ref[half_rows(ref.shape[0], 1 - p.c), :], True)
    x = x_ref[...].astype(F32)
    r = lax.rsqrt(jnp.mean(x * x, axis=-1, keepdims=True) + EPSILON)
    parts = []
    for part in thirds:
        total = dscaled_turned[part] + dot(w_in_ref[part, conv_at:], dconv_b_ref[...])
        parts.append((total + dot(step_in_ref[part, :STEP], dstep_ref[...])).T)
    dscaled = beside(*parts)
    plain = x * r
    dgain[...] += fold(dscaled * plain)
    dstep_sum[...] += dot(dstep_ref[...], (plain * gain_ref[...]).astype(BF16))
    gained = dscaled * gain_ref[...]
    inner = jnp.mean(gained * plain, axis=-1, keepdims=True)
    dx_ref[...] = back.astype(F32) + (gained - plain * inner) * r

    @pl.when(step_now == STRIPS - 1)
    def _():
        for part, column in zip(sums, (out_column, gate_column)):
            part.plane.finish(1)
            column[...] = part.column()
        for box in boxes:
            box.finish(True)
        store_flat(flat_ref, dstep_sum, dgain, dtaps_ref, dheads_ref, tail_sums_ref)


def store_flat(flat_ref, dstep_sum, dgain, dtaps, dheads, tail_sums_ref):
    flat_ref[...] = jnp.zeros_like(flat_ref)
    for j in range(D // 128):
        flat_ref[HEADS * j : HEADS * j + HEADS] = dstep_sum[:HEADS, 128 * j : 128 * j + 128]
    last = beside(
        lane_sums(dheads[0])[:1], lane_sums(dheads[1])[:1], tail_sums_ref[:1],
    )
    rows = [jnp.sum(dgain[...], axis=0, keepdims=True)]
    rows += [lane_sums(dtaps[k])[:1] for k in range(KCONV + 1)]
    at = HEADS * (D // 128)
    for row in rows + [last]:
        for j in range(row.shape[1] // 128):
            flat_ref[at + j : at + j + 1] = row[:, 128 * j : 128 * j + 128]
        at += row.shape[1] // 128


def whole(shape):
    return pl.BlockSpec(shape, lambda i: (0,) * len(shape), pipeline_mode=pl.Buffered(1))


def strip_rows(width):
    return pl.BlockSpec((STRIP, width), lambda i: (i, 0))


def strip_cols(height):
    return pl.BlockSpec((height, STRIP), lambda i: (0, i))


def shape(*dims, dtype=F32):
    return jax.ShapeDtypeStruct(dims, dtype)


def columns(width, at):
    return pl.BlockSpec((D, width), lambda i: (0, at), pipeline_mode=pl.Buffered(1))


def forward_call(x, back, weights, gain, taps, heads, inner, blocks, sizes, collective_id):
    count = sizes[0] * sizes[1]
    dma = pltpu.SemaphoreType.DMA
    hbm = pl.BlockSpec(memory_space=pl.ANY)
    return pl.pallas_call(
        functools.partial(forward_kernel, sizes),
        grid=(STRIPS,),
        in_specs=[
            strip_rows(D), strip_rows(D), columns(HALF, 0), columns(HALF, 1), whole((1, D)),
            hbm, whole((3, HEADS, CHUNK)), hbm, hbm, hbm,
        ],
        out_specs=[
            strip_rows(D), strip_rows(D), strip_cols(CONVCH), strip_cols(CONVCH),
            strip_cols(STEP), pl.BlockSpec((PER, INNER, NSTATE), lambda i: (i, 0, 0)),
            strip_cols(INNER // 2), strip_cols(INNER), strip_cols(INNER), strip_cols(INNER // 2),
            strip_cols(HEADS), whole((8, TAIL_SUMS)), hbm, hbm, hbm, hbm, hbm,
        ],
        out_shape=[
            shape(LEN, D, dtype=BF16), shape(LEN, D, dtype=BF16), shape(CONVCH, LEN),
            shape(CONVCH, LEN), shape(STEP, LEN), shape(LEN // CHUNK, INNER, NSTATE),
            shape(INNER // 2, LEN, dtype=BF16), shape(INNER, LEN), shape(INNER, LEN, dtype=BF16),
            shape(INNER // 2, LEN, dtype=BF16), shape(HEADS, LEN), shape(8, TAIL_SUMS),
            shape(*blocks.shape), shape(INNER // 2, LEN, dtype=BF16),
            shape(INNER // 2, LEN, dtype=BF16), shape(LEN, D, dtype=BF16),
            shape(LEN, D, dtype=BF16),
        ],
        scratch_shapes=[
            pltpu.VMEM((CONVCH, STRIP), F32), pltpu.VMEM((INNER, STRIP), F32),
            pltpu.VMEM((INNER, STRIP), F32), pltpu.VMEM((INNER, STRIP), F32),
            pltpu.VMEM((INNER, NSTATE), F32), pltpu.VMEM((2, CONVCH, CHUNK), F32),
            pltpu.VMEM((2, HALF, D), BF16), pltpu.VMEM((HEADS, CHUNK), F32),
            pltpu.VMEM((INNER, CHUNK), F32), pltpu.VMEM((INNER, STRIP), BF16),
            pltpu.VMEM((KCONV + 1, CONVCH, CHUNK), F32), pltpu.VMEM((INNER, CHUNK), F32), dma((2,)),
            pltpu.VMEM((2, INNER // 2, STRIP), BF16), pltpu.VMEM((2, INNER // 2, STRIP), BF16),
            pltpu.VMEM((2, STRIP, D), BF16), dma((3, STRIPS, 2)), dma((2,)),
            dma((count,)), dma((count,)), dma,
        ],
        compiler_params=pltpu.CompilerParams(
            vmem_limit_bytes=60 * 2**20, collective_id=collective_id, has_side_effects=True
        ),
        name="mixer_forward",
    )(x, back, weights, weights, gain, taps, heads, inner, blocks, back)


def backward_call(x, back, weights, gain, taps, heads, kept, tail_sums, parts, sizes,
                  collective_id):
    last = STRIPS - 1

    def rows(width):
        return pl.BlockSpec((STRIP, width), lambda i: (last - i, 0))

    def cols(height):
        return pl.BlockSpec((height, STRIP), lambda i: (0, last - i))

    Z = sizes[0]
    lines = flat_lines(sizes[0] * sizes[1])
    size = (parts[0].shape[1], D)
    dma = pltpu.SemaphoreType.DMA
    hbm = pl.BlockSpec(memory_space=pl.ANY)
    return pl.pallas_call(
        functools.partial(backward_kernel, sizes),
        grid=(STRIPS,),
        in_specs=[
            rows(D), rows(D), columns(WIDE, 0),
            columns(256, (HALF + STEP_AT) // 256), whole((1, D)),
            whole((KCONV, CONVCH, CHUNK)), whole((3, HEADS, CHUNK)), cols(CONVCH),
            cols(CONVCH), cols(STEP),
            pl.BlockSpec((PER, INNER, NSTATE), lambda i: (last - i, 0, 0)), cols(INNER),
            cols(INNER), cols(HEADS), whole((8, TAIL_SUMS)), hbm, hbm,
        ],
        out_specs=[
            rows(D), cols(CONV_A // 2), cols((CONVCH - CONV_A) // 2), whole((lines, 128)),
            whole((Z,) + size), whole((Z,) + size), hbm, hbm,
        ],
        out_shape=[
            shape(LEN, D), shape(CONV_A // 2, LEN, dtype=BF16),
            shape((CONVCH - CONV_A) // 2, LEN, dtype=BF16), shape(lines, 128),
            shape(Z, *size), shape(Z, *size), shape(CONV_A // 2, LEN, dtype=BF16),
            shape((CONVCH - CONV_A) // 2, LEN, dtype=BF16),
        ],
        scratch_shapes=[
            pltpu.VMEM((CONV_A, STRIP), BF16), pltpu.VMEM((CONVCH - CONV_A, STRIP), BF16),
            pltpu.VMEM((2, CONV_A // 2, STRIP), BF16),
            pltpu.VMEM((2, (CONVCH - CONV_A) // 2, STRIP), BF16), dma((2, STRIPS, 2)),
            pltpu.VMEM((CONVCH, STRIP), F32),
            pltpu.VMEM((INNER, NSTATE), F32), pltpu.VMEM((HEADS, CHUNK), F32),
            pltpu.VMEM((KCONV - 1, CONVCH, CHUNK), F32), pltpu.VMEM((HEADS, CHUNK), F32),
            pltpu.VMEM((HEADS, CHUNK), F32), pltpu.VMEM((STEP, STRIP), BF16),
            pltpu.VMEM((STEP, D), F32), pltpu.VMEM((8, D), F32),
            pltpu.VMEM((KCONV + 1, CONVCH, CHUNK), F32), pltpu.VMEM((2, HEADS, CHUNK), F32),
            pltpu.VMEM((D, STRIP), F32),
        ]
        + 2 * (plane_scratch(sizes, size) + [dma]),
        compiler_params=pltpu.CompilerParams(
            vmem_limit_bytes=63 * 2**20, collective_id=collective_id, has_side_effects=True
        ),
        name="mixer_backward",
    )(
        x, back, weights, weights, gain, taps, heads, *kept, tail_sums,
        *(by_chip(part, sizes) for part in parts),
    )


def grads_kernel(*refs):
    ins, block_in, outs, block_out = refs[:8], refs[8], refs[9:11], refs[11]
    sides, others, results, block, sems, out_sems, block_sems = refs[12:]
    load = pltpu.make_async_copy(block_in, block, block_sems.at[0])
    keep = pltpu.make_async_copy(block, block_out, block_sems.at[1])
    copies = []
    for k in range(4):
        copies.append([
            pltpu.make_async_copy(ins[2 * k], sides.at[k], sems.at[2 * k]),
            pltpu.make_async_copy(ins[2 * k + 1], others.at[k], sems.at[2 * k + 1]),
        ])
        for copy in copies[k]:
            copy.start()
    load.start()
    stores = []
    for k in range(2):
        for half in (0, 1):
            for copy in copies[2 * k + half]:
                copy.wait()
            side, other = sides.at[2 * k + half], others.at[2 * k + half]

            def tile(i, carry, k=k, half=half, side=side, other=other):
                rows = pl.ds(pl.multiple_of(i * GRAD_TILE, GRAD_TILE), GRAD_TILE)
                part = dot(side[rows, :], other[...])
                results[k, rows, :] = part if half == 0 else results[k, rows, :] + part
                return carry

            lax.fori_loop(0, INNER // 2 // GRAD_TILE, tile, 0)
        if k == 0:
            load.wait()
            keep.start()
        stores.append(pltpu.make_async_copy(results.at[k], outs[k], out_sems.at[k]))
        stores[k].start()
    for store in stores + [keep]:
        store.wait()


def grads_call(own_normed, peer_normed, own_dgate, peer_dgate, backs, hbs, block):
    rows = INNER // 2
    hbm = pl.BlockSpec(memory_space=pl.ANY)
    return pl.pallas_call(
        grads_kernel,
        in_specs=[hbm] * 9,
        out_specs=[hbm] * 3,
        out_shape=[shape(rows, D)] * 2 + [shape(LEN, D, dtype=BF16)],
        scratch_shapes=[
            pltpu.VMEM((4, rows, LEN), BF16), pltpu.VMEM((4, LEN, D), BF16),
            pltpu.VMEM((2, rows, D), F32), pltpu.VMEM((LEN, D), BF16),
            pltpu.SemaphoreType.DMA((8,)), pltpu.SemaphoreType.DMA((2,)),
            pltpu.SemaphoreType.DMA((2,)),
        ],
        compiler_params=pltpu.CompilerParams(vmem_limit_bytes=60 * 2**20),
        name="grads",
    )(own_normed, backs[0], peer_normed, backs[1], own_dgate, hbs[0], peer_dgate, hbs[1], block)


def flat_lines(count):
    return -(-(HEADS * D + SMALL) // (1024 * count)) * 8 * count


def block_and_gradients(x, back, weights, vectors, blocks, sizes, collective_ids):
    count = sizes[0] * sizes[1]
    gain, taps, heads, inner = vectors
    (
        out, hb, cin, c, raw, states, own_normed, dy, dgate, own_dgate, dlogs, tail_sums, moved,
        peer_normed, peer_dgate, peer_hb, peer_back,
    ) = forward_call(
        x, back, weights, gain, taps, heads, inner, blocks, sizes, collective_ids[0]
    )
    *parts, out = grads_call(
        own_normed, peer_normed, own_dgate, peer_dgate, (back, peer_back), (hb, peer_hb), out
    )
    parts = [part.reshape(count // 2, -1, D) for part in parts]
    dx, own_a, own_b, flat, out_column, gate_column, peer_a, peer_b = backward_call(
        x, back, weights, gain, taps, heads, (cin, c, raw, states, dy, dgate, dlogs), tail_sums,
        parts, sizes, collective_ids[1],
    )
    factors = (own_a, peer_a, own_b, peer_b, hb, peer_hb)
    return out, dx, [out_column, gate_column], factors, flat.reshape(count, -1, 128), moved


MESH = pl.DeviceIdType.MESH


class Place:
    def __init__(self, sizes):
        self.Z, self.F = sizes
        self.C, self.Y = 2, 2
        self.X = self.F // 4
        f = lax.axis_index("fsdp")
        self.z = lax.axis_index("dp")
        self.c = lax.rem(f, 2)
        self.x = lax.rem(f // 2, self.X)
        self.y = f // (2 * self.X)
        self.f = f

    def at(self, z=None, y=None, x=None, c=None):
        z = self.z if z is None else z
        y = self.y if y is None else y
        x = self.x if x is None else x
        c = self.c if c is None else c
        return (z, (y * self.X + x) * 2 + c)

    def other_x(self, step):
        return lax.rem(self.x + step, self.X)


def signal(device):
    pl.semaphore_signal(
        pltpu.get_barrier_semaphore(), inc=1, device_id=device, device_id_type=MESH
    )


def greet_all(place, wait=True):
    count = place.Z * place.F
    me = place.z * place.F + place.f

    def step(i, carry):
        peer = lax.rem(me + i, count)
        signal((peer // place.F, lax.rem(peer, place.F)))
        return carry

    lax.fori_loop(1, count, step, 0)
    if wait:
        await_all(place)


def await_all(place):
    pl.semaphore_wait(pltpu.get_barrier_semaphore(), place.Z * place.F - 1)


def remote(src, dst, send, recv, device):
    return pltpu.make_async_remote_copy(
        src_ref=src, dst_ref=dst, send_sem=send, recv_sem=recv, device_id=device,
        device_id_type=MESH,
    )


def add_blocks(dst, src, count):
    def step(i, carry):
        target = dst(i)
        target[...] = target[...] + src(i)[...]
        return carry

    lax.fori_loop(0, count, step, 0)


class Swap:
    def __init__(self, place, src, dst, send, recv, local, same=False, narrow=None):
        self.place, self.src, self.dst, self.same, self.narrow = place, src, dst, same, narrow
        self.send, self.recv, self.local = send, recv, local
        self.count = place.Z * place.F
        self.me = place.z * place.F + place.f

    def block(self, peer):
        return self.src if self.same else self.src.at[peer]

    def cut(self, ref, odd):
        return ref.at[:, pl.ds(0, self.narrow)] if odd else ref

    def each(self, sender, act):
        if self.narrow is None:
            act(False)
        else:
            @pl.when(lax.rem(sender, 2) == 0)
            def _():
                act(False)

            @pl.when(lax.rem(sender, 2) == 1)
            def _():
                act(True)

    def to(self, i, odd):
        peer = lax.rem(self.me + i, self.count)
        return remote(
            self.cut(self.block(peer), odd), self.cut(self.dst.at[self.me], odd),
            self.send.at[i], self.recv.at[i],
            (peer // self.place.F, lax.rem(peer, self.place.F)),
        )

    def keep(self):
        return pltpu.make_async_copy(self.block(self.me), self.dst.at[self.me], self.local)

    def start(self):
        self.keep().start()

        def step(i, carry):
            self.each(self.me, lambda odd: self.to(i, odd).start())
            return carry

        lax.fori_loop(1, self.count, step, 0)

    def wait(self):
        self.keep().wait()

        def step(i, carry):
            sender = lax.rem(self.me + self.count - i, self.count)
            self.each(self.me, lambda odd: self.to(i, odd).wait_send())
            self.each(sender, lambda odd: remote(
                self.cut(self.block(sender), odd), self.cut(self.dst.at[sender], odd),
                self.send.at[i], self.recv.at[i],
                (sender // self.place.F, lax.rem(sender, self.place.F)),
            ).wait_recv())
            return carry

        lax.fori_loop(1, self.count, step, 0)


def greet_near(place, along_z, wait=True):
    signal(place.at(c=1 - place.c))
    signal(place.at(y=1 - place.y))
    for s in range(1, place.X):
        signal(place.at(x=place.other_x(s)))
    if along_z:
        for s in range(1, place.Z):
            signal(place.at(z=lax.rem(place.z + s, place.Z)))
    if wait:
        await_near(place, along_z)


def await_near(place, along_z):
    pl.semaphore_wait(
        pltpu.get_barrier_semaphore(), place.X + 1 + (place.Z - 1 if along_z else 0)
    )


class Plane:
    def __init__(self, place, acc, x1, y1, x2, y2, sems):
        self.p, self.acc = place, acc
        self.x1, self.y1, self.x2, self.y2, self.sems = x1, y1, x2, y2, sems
        self.h = place.Z // 2

    def copies(self, stage):
        p, acc, h = self.p, self.acc, self.h
        low, high = pl.ds(0, h), pl.ds(h, p.Z - h)
        out = []
        base = stage * p.X
        for s in range(1, p.X):
            x = p.other_x(s)
            if stage == 0:
                src, dst = acc.at[low, :, x], self.x1.at[s - 1]
            else:
                src, dst = acc.at[high, p.y, x], self.x2.at[s - 1]
            sem = self.sems.at[base + s]
            out.append(remote(src, dst, sem.at[0], sem.at[1], p.at(x=x)))
        if stage == 0:
            src, dst = acc.at[high, 1 - p.y], self.y1
        else:
            src, dst = acc.at[low, 1 - p.y, p.x], self.y2
        sem = self.sems.at[base]
        out.append(remote(src, dst, sem.at[0], sem.at[1], p.at(y=1 - p.y)))
        return out

    def start(self, stage):
        for copy in self.copies(stage):
            copy.start()

    def finish(self, stage):
        p, acc, h = self.p, self.acc, self.h
        for copy in self.copies(stage):
            copy.wait()
        for s in range(p.X - 1):
            if stage == 0:
                add_blocks(
                    lambda i: acc.at[i // p.Y, lax.rem(i, p.Y), p.x],
                    lambda i: self.x1.at[s, i // p.Y, lax.rem(i, p.Y)],
                    h * p.Y,
                )
            else:
                add_blocks(
                    lambda i: acc.at[h + i, p.y, p.x], lambda i: self.x2.at[s, i], p.Z - h
                )
        if stage == 0:
            add_blocks(
                lambda i: acc.at[h + i // p.X, p.y, lax.rem(i, p.X)],
                lambda i: self.y1.at[i // p.X, lax.rem(i, p.X)],
                (p.Z - h) * p.X,
            )
        else:
            add_blocks(lambda i: acc.at[i, p.y, p.x], lambda i: self.y2.at[i], h)


def plane_scratch(sizes, block):
    Z, X, Y = sizes[0], sizes[1] // 4, 2
    h = Z // 2
    return [
        pltpu.VMEM((Z, Y, X) + block, F32), pltpu.VMEM((X - 1, h, Y) + block, F32),
        pltpu.VMEM((Z - h, X) + block, F32), pltpu.VMEM((X - 1, Z - h) + block, F32),
        pltpu.VMEM((h,) + block, F32), pltpu.SemaphoreType.DMA((2 * X, 2)),
    ]


def by_place(blocks, sizes):
    return blocks.reshape((sizes[0], 2, sizes[1] // 4, 2) + blocks.shape[1:])


def by_chip(blocks, sizes):
    return blocks.reshape((sizes[0], 2, sizes[1] // 4) + blocks.shape[1:])


class PlaneSum:
    def __init__(self, place, part, work):
        self.p, self.part, self.acc, self.sem = place, part, work[0], work[6]
        self.plane = Plane(place, *work[:6])

    def copy(self):
        return pltpu.make_async_copy(self.part, self.acc, self.sem)

    def begin(self):
        self.copy().start()

    def start(self):
        self.copy().wait()
        self.plane.start(0)

    def block(self, z):
        return self.acc.at[z, self.p.y, self.p.x]

    def column(self):
        return self.acc[:, self.p.y, self.p.x]


class Product(PlaneSum):
    def __init__(self, place, factors, work):
        super().__init__(place, None, work)
        self.factors, self.formed = factors, False

    def begin(self):
        pass

    def start(self):
        if not self.formed:
            self.form()
        self.plane.start(0)

    def form(self):
        self.formed = True
        own, peer, right, peer_right = self.factors
        Z, Y, X, per, _ = self.acc.shape
        h = Z // 2
        size = h * Y * X * per

        def half(k, carry):
            rows = pl.ds(pl.multiple_of(k * size, size), size)
            value = dot(own[rows, :], right[...]) + dot(peer[rows, :], peer_right[...])
            for i in range(h * Y * X):
                place = (k * h + i // (Y * X), i // X % Y, i % X)
                self.acc[place] = value[per * i : per * i + per]
            return carry

        lax.fori_loop(0, Z // h, half, 0)


class PairSum(PlaneSum):
    def __init__(self, place, part, work):
        super().__init__(place, part, work)
        self.core, self.sems = work[7], work[8]

    def copies(self):
        p = self.p
        return (
            remote(
                self.part.at[:, :, :, 1 - p.c], self.core, self.sems.at[0], self.sems.at[1],
                p.at(c=1 - p.c),
            ),
            pltpu.make_async_copy(self.part.at[:, :, :, p.c], self.acc, self.sem),
        )

    def begin(self):
        for copy in self.copies():
            copy.start()

    def start(self):
        p = self.p
        for copy in self.copies():
            copy.wait()

        def place_of(i):
            return i // (p.Y * p.X), lax.rem(i // p.X, p.Y), lax.rem(i, p.X)

        add_blocks(
            lambda i: self.acc.at[place_of(i)], lambda i: self.core.at[place_of(i)],
            p.Z * p.Y * p.X,
        )
        self.plane.start(0)


class Column:
    def __init__(self, part, acc, sem):
        self.copy = pltpu.make_async_copy(part, acc, sem)
        self.acc = acc

    def block(self, z):
        return self.acc.at[z]


class Chain:
    def __init__(self, place, part, held, sems):
        self.p, self.part, self.held, self.sems = place, part, held, sems

    def flow(self, t, side):
        p = self.p
        sem = self.sems.at[side, t]
        target = p.at(z=p.z + 1 - 2 * side)
        return remote(self.part.block(t), self.held.at[side, t], sem.at[0], sem.at[1], target)

    def first(self):
        p = self.p
        for j in range(p.Z - 1):
            @pl.when(p.z == 0)
            def _():
                self.flow(p.Z - 1 - j, 0).start()

            @pl.when(p.z == p.Z - 1)
            def _():
                self.flow(j, 1).start()

    def receive(self, t, side):
        self.flow(t, side).wait_recv()
        mine = self.part.block(t)
        mine[...] = mine[...] + self.held[side, t]

    def forward(self, j):
        p = self.p

        def turn(k, carry):
            side = lax.rem(k + p.z // (p.Z // 2), 2)
            t = (1 - side) * (p.Z - 1 - j) + side * j
            inside = jnp.logical_and(p.z > 0, p.z < p.Z - 1)

            @pl.when(jnp.logical_and(inside, (1 - 2 * side) * (t - p.z) > 0))
            def _():
                self.receive(t, side)
                self.flow(t, side).start()

            return carry

        lax.fori_loop(0, 2, turn, 0)

    def last(self):
        p = self.p

        @pl.when(p.z > 0)
        def _():
            self.receive(p.z, 0)

        @pl.when(p.z < p.Z - 1)
        def _():
            self.receive(p.z, 1)

    def finish(self):
        p = self.p
        for t in range(p.Z):
            for side in (0, 1):
                @pl.when(p.z < t if side == 0 else p.z > t)
                def _():
                    self.flow(t, side).wait_send()


class Direct:
    def __init__(self, place, part, held, sems):
        self.p, self.part, self.held, self.sems = place, part, held, sems

    def over(self, s):
        p = self.p
        z = lax.rem(p.z + s, p.Z)
        sem = self.sems.at[s]
        return remote(self.part.block(z), self.held.at[s - 1], sem.at[0], sem.at[1], p.at(z=z))

    def start(self):
        for s in range(1, self.p.Z):
            self.over(s).start()

    def last(self):
        mine = self.part.block(self.p.z)
        total = mine[...]
        for s in range(1, self.p.Z):
            self.over(s).wait()
            total = total + self.held[s - 1]
        mine[...] = total


def scatter_kernel(sizes, *refs):
    columns_in, factors, small_in, outs, rest = (
        refs[:2], refs[2:8], refs[8], refs[9:14], list(refs[14:])
    )

    def take(n):
        taken = rest[:n]
        del rest[:n]
        return taken

    p = Place(sizes)
    columns = [Column(ref, *take(2)) for ref in columns_in]
    chains = [Chain(p, column, *take(2)) for column in columns]
    own_a, peer_a, own_b, peer_b, hb, peer_hb = factors
    queue = [
        Product(p, (own_a, peer_a, hb, peer_hb), take(7)),
        Product(p, (own_b, peer_b, hb, peer_hb), take(7)),
        PairSum(p, small_in, take(9)),
    ]
    queue = [(part, Direct(p, part, *take(2))) for part in queue]
    greet_near(p, True, False)
    for column in columns:
        column.copy.start()
    queue[0][0].form()
    await_near(p, True)
    for part, _ in queue:
        part.begin()
    for column, chain in zip(columns, chains):
        column.copy.wait()
        chain.first()
    hops = p.Z - 2

    def forward(j):
        if j < hops:
            for chain in chains:
                chain.forward(j)

    stages = [
        lambda part, direct: part.start(),
        lambda part, direct: (part.plane.finish(0), part.plane.start(1)),
        lambda part, direct: (part.plane.finish(1), direct.start()),
    ]
    for k, stage in enumerate(stages):
        for part, direct in queue:
            stage(part, direct)
        forward(k)
    for k in range(len(stages), hops):
        forward(k)
    for chain in chains:
        chain.last()
        chain.finish()
    for _, direct in queue:
        direct.last()
    for part, out in zip(columns + [part for part, _ in queue], outs):
        out[...] = part.block(p.z)[...]


def scatter_call(columns, factors, small, sizes, collective_id):
    Z, F = sizes
    X, Y = F // 4, 2
    chips = Z * X * Y
    dma = pltpu.SemaphoreType.DMA
    parts = [(factors[0].shape[0] // chips, D), (factors[2].shape[0] // chips, D)]
    parts.append(small.shape[1:])
    scratch = []
    for column in columns:
        scratch += [pltpu.VMEM(column.shape, F32), dma]
    for column in columns:
        scratch += [pltpu.VMEM((2, Z) + column.shape[1:], F32), dma((2, Z, 2))]
    for block in parts:
        scratch += plane_scratch(sizes, block) + [dma]
    scratch += [pltpu.VMEM((Z, Y, X) + parts[2], F32), dma((2,))]
    for block in parts:
        scratch += [pltpu.VMEM((Z - 1,) + block, F32), dma((Z, 2))]
    hbm = pl.BlockSpec(memory_space=pl.ANY)
    vmem = pl.BlockSpec(memory_space=pltpu.VMEM)
    return pl.pallas_call(
        functools.partial(scatter_kernel, sizes),
        out_shape=[shape(*block) for block in [column.shape[1:] for column in columns] + parts],
        in_specs=[hbm] * 2 + [vmem] * 6 + [hbm],
        out_specs=[vmem] * 5,
        scratch_shapes=scratch,
        compiler_params=pltpu.CompilerParams(
            collective_id=collective_id, has_side_effects=True, vmem_limit_bytes=60 * 2**20
        ),
        name="scatter",
    )(*columns, *factors, by_place(small, sizes))


def gather_kernel(
    sizes, w_in_ref, w_out_ref, m_in_ref, m_out_ref, params_ref,
    all_ref, blocks_ref, gain_ref, taps_ref, heads_ref, inner_ref,
    mine, keep_sem, z_sems, near, far, across,
):
    p = Place(sizes)
    Z, h = p.Z, p.Z // 2
    greet_near(p, True, False)
    own = mine.shape[0]
    partner = p.at(c=1 - p.c)
    mine[:, :WIDE] = w_in_ref[:, :WIDE].astype(BF16)
    mine[:, WIDE : WIDE + INNER] = w_out_ref[...].astype(BF16)
    mine[:, WIDE + INNER :] = jnp.concatenate(
        [w_in_ref[:, WIDE:], jnp.zeros((own, 2 * HALF - IN_W - INNER), F32)], axis=1
    ).astype(BF16)
    keep = pltpu.make_async_copy(mine, all_ref.at[p.z, p.y, p.x, p.c], keep_sem)
    keep.start()
    await_near(p, True)

    def spot(z, y, x):
        return all_ref.at[z, y, x, p.c]

    def copy(src, dst, sem, device):
        return remote(src, dst, sem.at[0], sem.at[1], device)

    def along_z(z, right, src=None):
        here = spot(z, p.y, p.x)
        target = p.at(z=p.z + 1 if right else p.z - 1)
        return copy(here if src is None else src, here, z_sems.at[0 if right else 1, z], target)

    def near_copies(z, src=None):
        here = spot(z, p.y, p.x)
        src = here if src is None else src
        found = [copy(src, here, near.at[z, 0], p.at(y=1 - p.y))]
        for s in range(1, p.X):
            found.append(copy(src, here, near.at[z, s], p.at(x=p.other_x(s))))
        return found

    def near_arrivals(z):
        found = [(z, 1 - p.y, p.x, near.at[z, 0])]
        for s in range(1, p.X):
            found.append((z, p.y, lax.rem(p.x + p.X - s, p.X), near.at[z, s]))
        return found

    def far_copies(z):
        low, high = [], []
        for s in range(1, p.X):
            x = p.other_x(s)
            there = spot(z, p.y, x)
            low.append(copy(there, there, far.at[z, s], p.at(y=1 - p.y)))
            there = spot(z, 1 - p.y, p.x)
            high.append(copy(there, there, far.at[z, s], p.at(x=x)))
        return low, high

    def far_arrivals(z):
        low = [(z, 1 - p.y, p.other_x(s), far.at[z, s]) for s in range(1, p.X)]
        high = [
            (z, 1 - p.y, lax.rem(p.x + p.X - s, p.X), far.at[z, s]) for s in range(1, p.X)
        ]
        return low, high

    def to_partner(z, y, x, src=None):
        here = spot(z, y, x)
        return copy(here if src is None else src, here, across.at[z, y, x], partner)

    def await_block(z, y, x, sem):
        here = spot(z, y, x)
        copy(here, here, sem, partner).wait_recv()
        to_partner(z, y, x).start()

    def start_all(copies):
        for c in copies:
            c.start()

    @pl.when(p.z < Z - 1)
    def _():
        along_z(p.z, True, mine).start()

    @pl.when(p.z > 0)
    def _():
        along_z(p.z, False, mine).start()

    start_all(near_copies(p.z, mine))
    to_partner(p.z, p.y, p.x, mine).start()
    spread_vectors(params_ref, gain_ref, taps_ref, heads_ref, inner_ref)
    spread_moments(m_in_ref, m_out_ref, blocks_ref)

    def visit(right, z):
        await_block(z, p.y, p.x, z_sems.at[0 if right else 1, z])

        @pl.when(p.z < Z - 1 if right else p.z > 0)
        def _():
            along_z(z, right).start()

        start_all(near_copies(z))

    def by_distance(low, high):
        for j in range(1, Z):
            @pl.when(p.z - j >= 0)
            def _():
                low(p.z - j)

            @pl.when(p.z + j < Z)
            def _():
                high(p.z + j)

    by_distance(lambda z: visit(True, z), lambda z: visit(False, z))

    def relay(z):
        for block in near_arrivals(z):
            await_block(*block)
        low, high = far_copies(z)

        @pl.when(z < h)
        def _():
            start_all(low)

        @pl.when(z >= h)
        def _():
            start_all(high)

    relay(p.z)
    by_distance(relay, relay)

    def settle(z):
        low, high = far_arrivals(z)

        @pl.when(z < h)
        def _():
            for block in low:
                await_block(*block)

        @pl.when(z >= h)
        def _():
            for block in high:
                await_block(*block)

    settle(p.z)
    by_distance(settle, settle)
    keep.wait()

    def finish(z, carry):
        for c in near_copies(z):
            c.wait_send()
        low, high = far_copies(z)

        @pl.when(z < h)
        def _():
            for c in low:
                c.wait_send()

        @pl.when(z >= h)
        def _():
            for c in high:
                c.wait_send()

        @pl.when(jnp.logical_and(z <= p.z, p.z < Z - 1))
        def _():
            along_z(z, True).wait_send()

        @pl.when(jnp.logical_and(z >= p.z, p.z > 0))
        def _():
            along_z(z, False).wait_send()

        for y in range(p.Y):
            for x in range(p.X):
                to_partner(z, y, x).wait_send()
                theirs = all_ref.at[z, y, x, 1 - p.c]
                copy(theirs, theirs, across.at[z, y, x], partner).wait_recv()

        return carry

    lax.fori_loop(0, Z, finish, 0)


def column_of(row):
    return jnp.broadcast_to(row, (128, 128)).T


def spread_vectors(params_ref, gain_ref, taps_ref, heads_ref, inner_ref):
    row = D // 128
    gain_ref[...] = beside(*[params_ref[j : j + 1] for j in range(row)])
    for k in range(KCONV + 1):
        for j in range(CONVCH // 128):
            taps_ref[k, 128 * j : 128 * j + 128] = column_of(params_ref[row : row + 1])
            row += 1
    heads = column_of(params_ref[row : row + 1])
    heads_ref[0] = heads[:HEADS]
    heads_ref[1] = -jnp.exp(heads[HEADS : 2 * HEADS])
    heads_ref[2] = heads[2 * HEADS : 3 * HEADS]
    row = params_ref.shape[0] - INNER // 128
    for j in range(INNER // 128):
        inner_ref[128 * j : 128 * j + 128] = column_of(params_ref[row + j : row + j + 1])


def cuts_of(count):
    widths = [(0, INNER), (INNER, CONV_A), (INNER + CONV_A, CONVCH - CONV_A)]
    return [(start, width, width // count) for start, width in widths], INNER // count


def first_of(d, width, count):
    return d % 2 * (width // 2) + d // 2 * (width // count)


def spread_moments(m_in_ref, m_out_ref, blocks_ref):
    count, own, lanes_in_block = blocks_ref.shape
    ins, outs = cuts_of(count)
    step = m_in_ref[:, WIDE:]
    used = sum(each for _, _, each in ins) + outs + HEADS
    for d in range(count):
        pieces = []
        for start, width, each in ins:
            at = start + first_of(d, width, count)
            pieces.append(m_in_ref[:, at : at + each])
        at = first_of(d, INNER, count)
        pieces += [m_out_ref[:, at : at + outs], step]
        blocks_ref[d] = beside(*pieces, jnp.zeros((own, lanes_in_block - used), F32))


def gather_call(weight_in, weight_out, moment_in, moment_out, params, sizes, collective_id):
    Z, F = sizes
    X, Y = F // 4, 2
    own = weight_in.shape[0]
    count = Z * F
    gap = jnp.zeros((-params.shape[0] % 128,), F32)
    params = jnp.concatenate([params, gap, params[-INNER:]]).reshape(-1, 128)
    vmem = pl.BlockSpec(memory_space=pltpu.VMEM)
    hbm = pl.BlockSpec(memory_space=pl.ANY)
    whole_weights, blocks, *vectors = pl.pallas_call(
        functools.partial(gather_kernel, sizes),
        out_shape=[
            shape(Z, Y, X, 2, own, 2 * HALF, dtype=BF16), shape(count, own, 256), shape(1, D),
            shape(KCONV + 1, CONVCH, CHUNK), shape(3, HEADS, CHUNK), shape(INNER, CHUNK),
        ],
        in_specs=[vmem] * 5,
        out_specs=[hbm] + [vmem] * 5,
        scratch_shapes=[
            pltpu.VMEM((own, 2 * HALF), BF16), pltpu.SemaphoreType.DMA, pltpu.SemaphoreType.DMA((2, Z, 2)),
            pltpu.SemaphoreType.DMA((Z, X, 2)), pltpu.SemaphoreType.DMA((Z, X, 2)),
            pltpu.SemaphoreType.DMA((Z, Y, X, 2)),
        ],
        compiler_params=pltpu.CompilerParams(
            collective_id=collective_id, has_side_effects=True, vmem_limit_bytes=60 * 2**20
        ),
        name="weights_gather",
    )(weight_in, weight_out, moment_in, moment_out, params)
    return whole_weights.reshape(D, 2 * HALF), blocks, vectors


def gram_rows(slab, row):
    high, low = split(slab)
    left = above(high, low, high)[:, 128 * row : 128 * row + 128]
    return dot_tn(left, above(high, high, low)[:, 128 * row :])


def pack_gram(targets, slab):
    Z, Y, X, per, _ = targets[0].shape
    rows = above(*[
        beside(gram_rows(slab, i), gram_rows(slab, D // 128 - 1 - i)) for i in range(D // 256)
    ])
    if Z * Y * X * per > rows.shape[0]:
        rows = above(rows, jnp.zeros((Z * Y * X * per - rows.shape[0], rows.shape[1]), F32))
    at = 0
    for target in targets:
        cols = slice(at, at + target.shape[4])
        for i in range(Z * Y * X):
            target[i // (Y * X), i // X % Y, i % X] = rows[per * i : per * i + per, cols]
        at += target.shape[4]


def unpack_gram(gram, packed):
    Z, Y, X, _, _ = packed[0].shape
    rows = beside(*[
        above(*[part[i // (Y * X), i // X % Y, i % X] for i in range(Z * Y * X)])
        for part in packed
    ])
    for i in range(D // 256):
        pair = rows[128 * i : 128 * i + 128]
        wide_part, j = D - 128 * i, D // 128 - 1 - i
        for row, part in ((i, pair[:, :wide_part]), (j, pair[:, wide_part:])):
            gram[128 * row : 128 * row + 128, 128 * row :] = part
            for k in range(row + 1, D // 128):
                at = 128 * (k - row)
                gram[128 * k : 128 * k + 128, 128 * row : 128 * row + 128] = part[
                    :, at : at + 128
                ].T


BEHIND = 2


class AllSum:
    def __init__(self, place, work):
        self.p = place
        self.total, self.acc, self.core, self.core_sems = work[0], work[1], work[7], work[8]
        self.held, self.z_sems, self.back_sems = work[9:12]
        self.plane = Plane(place, *work[1:7])
        self.steps = [
            self.pair, self.second, self.cross, self.turn, self.spread, self.spread_on, self.done,
        ]

    def to_core(self):
        p = self.p
        return remote(
            self.total, self.core, self.core_sems.at[0], self.core_sems.at[1], p.at(c=1 - p.c)
        )

    def pair(self):
        p = self.p
        self.to_core().wait()

        def place_of(i):
            return i // (p.Y * p.X), lax.rem(i // p.X, p.Y), lax.rem(i, p.X)

        add_blocks(
            lambda i: self.acc.at[place_of(i)], lambda i: self.core.at[place_of(i)],
            p.Z * p.Y * p.X,
        )
        self.plane.start(0)

    def second(self):
        self.plane.finish(0)
        self.plane.start(1)

    def over(self, s):
        p = self.p
        z = lax.rem(p.z + s, p.Z)
        sem = self.z_sems.at[0, s]
        return remote(
            self.acc.at[z, p.y, p.x], self.held.at[s - 1], sem.at[0], sem.at[1], p.at(z=z)
        )

    def cross(self):
        self.plane.finish(1)
        for s in range(1, self.p.Z):
            self.over(s).start()

    def back(self, s, mine):
        p = self.p
        sem = self.z_sems.at[1, s]
        z = p.z if mine else lax.rem(p.z + p.Z - s, p.Z)
        ref = self.total.at[z, p.y, p.x]
        return remote(ref, ref, sem.at[0], sem.at[1], p.at(z=lax.rem(p.z + s, p.Z)))

    def turn(self):
        p = self.p
        for s in range(1, p.Z):
            self.over(s).wait()
        result = self.acc[p.z, p.y, p.x]
        for s in range(1, p.Z):
            result = result + self.held[s - 1]
        self.total[p.z, p.y, p.x] = result
        for s in range(1, p.Z):
            self.back(s, True).start()

    def planes(self, stage, mine):
        p, total, h = self.p, self.total, self.p.Z // 2
        low, high = pl.ds(0, h), pl.ds(h, p.Z - h)
        found = []
        for s in range(1, p.X):
            sem = self.back_sems.at[stage * p.X + s]
            x = p.x if mine else lax.rem(p.x + p.X - s, p.X)
            ref = total.at[high, p.y, x] if stage == 0 else total.at[low, :, x]
            found.append(remote(ref, ref, sem.at[0], sem.at[1], p.at(x=p.other_x(s))))
        sem = self.back_sems.at[stage * p.X]
        y = p.y if mine else 1 - p.y
        ref = total.at[low, y, p.x] if stage == 0 else total.at[high, y]
        found.append(remote(ref, ref, sem.at[0], sem.at[1], p.at(y=1 - p.y)))
        return found

    def arrive(self, copies):
        for mine, theirs in copies:
            mine.wait_send()
            theirs.wait_recv()

    def spread(self):
        self.arrive([(self.back(s, True), self.back(s, False)) for s in range(1, self.p.Z)])
        for copy in self.planes(0, True):
            copy.start()

    def spread_on(self):
        self.arrive(zip(self.planes(0, True), self.planes(0, False)))
        for copy in self.planes(1, True):
            copy.start()

    def done(self):
        self.arrive(zip(self.planes(1, True), self.planes(1, False)))


def all_sum_scratch(sizes, block):
    Z, X, Y = sizes[0], sizes[1] // 4, 2
    dma = pltpu.SemaphoreType.DMA
    return [pltpu.VMEM((Z, Y, X) + block, F32)] + plane_scratch(sizes, block) + [
        pltpu.VMEM((Z, Y, X) + block, F32), dma((2,)), pltpu.VMEM((Z - 1,) + block, F32),
        dma((2, Z, 2)), dma((2 * X, 2)),
    ]


def put_left(left, value, rows):
    high, low = split(value)
    left[rows] = beside(high, low, high)


def put_right(right, value, row):
    high, low = split(value)
    size = value.shape[0]
    right[row : row + size] = high
    right[D + row : D + row + size] = high
    right[2 * D + row : 2 * D + row + size] = low


TILE = 256


def symmetric_product(target, left, right):
    for i in range(D // TILE):
        rows = slice(TILE * i, TILE * i + TILE)
        part = dot(left[rows], right[:, TILE * i :])
        target[rows, TILE * i :] = part
        for j in range(i + 1, D // TILE):
            at = TILE * (j - i)
            target[TILE * j : TILE * j + TILE, rows] = part[:, at : at + TILE].T


def iterate(gram, square, factor, left, right, slab, slab_left):
    tiles = [slice(TILE * i, TILE * i + TILE) for i in range(D // TILE)]
    row = lax.broadcasted_iota(jnp.int32, (TILE, D), 0)
    col = lax.broadcasted_iota(jnp.int32, (TILE, D), 1)
    diagonals = [(row + TILE * i == col) for i in range(D // TILE)]
    trace = jnp.zeros((8, D), F32)
    for rows, diagonal in zip(tiles, diagonals):
        trace = trace + fold(jnp.where(diagonal, gram[rows], 0.0))
    trace = jnp.sum(jnp.sum(trace, axis=0, keepdims=True), axis=1, keepdims=True)
    scale = 1.0 / (jnp.sqrt(trace) + 1e-07)
    for rows in tiles:
        gram[rows] = gram[rows] * (scale * scale)
    slab[...] = slab[...] * scale

    def step(iteration, carry):
        for i, rows in enumerate(tiles):
            value = gram[rows]
            put_left(left, value, rows)
            put_right(right, value, TILE * i)
        symmetric_product(square, left, right)
        for i, rows in enumerate(tiles):
            value = COEF_B * gram[rows] + COEF_C * square[rows]
            put_right(right, value + jnp.where(diagonals[i], COEF_A, 0.0), TILE * i)
        put_left(slab_left, slab[...], slice(None))
        slab[...] = dot(slab_left[...], right[...])
        symmetric_product(factor, left, right)
        for rows in tiles:
            put_left(left, factor[rows], rows)
        symmetric_product(gram, left, right)
        return carry

    lax.fori_loop(0, ITERS - 1, step, 0)
    for i, rows in enumerate(tiles):
        put_right(right, gram[rows], TILE * i)
    first = slab[...]
    put_left(slab_left, first, slice(None))
    once = dot(slab_left[...], right[...])
    put_left(slab_left, once, slice(None))
    slab[...] = COEF_A * first + COEF_B * once + COEF_C * dot(slab_left[...], right[...])


def exact_pick(chosen, rows):
    high = rows.astype(BF16)
    rest = rows - high.astype(F32)
    mid = rest.astype(BF16)
    low = (rest - mid.astype(F32)).astype(BF16)
    return dot_nt(chosen, high) + dot_nt(chosen, mid) + dot_nt(chosen, low)


def update_kernel(
    sizes, gate_ref, conv_a_ref, conv_b_ref, out_ref, small_ref, old_ref, moved_ref, smalls_ref, spread_ref, step_ref,
    give, given, give_sems, messages, smalls, mats, left, right, slab, slab_left,
    swap_send, swap_recv, local, *work,
):
    p = Place(sizes)
    count = p.Z * p.F
    own = D // count
    gates = gate_ref.shape[0]
    ins = gates + conv_a_ref.shape[0] + conv_b_ref.shape[0]
    greet_all(p, False)
    swaps = [
        Swap(p, src, dst, swap_send.at[k], swap_recv.at[k], local.at[k], same, narrow)
        for k, (src, dst, same, narrow) in enumerate([
            (small_ref, smalls, True, None), (messages.at[0], moved_ref, False, None),
            (messages.at[1], spread_ref, False, -(-2 * gates // 128) * 128),
        ])
    ]
    old = old_ref[...].T
    new_in = above(gate_ref[...], conv_a_ref[...], conv_b_ref[...])
    new_out = out_ref[...]

    def push(gradient, moment):
        return gradient + MOMENTUM * (MOMENTUM * moment + gradient)

    push_in = push(new_in, old[:ins])
    push_out = above(push(new_out, old[ins : ins + gates]), jnp.zeros((ins - gates, D), F32))
    in_core = p.c == 0
    give[...] = jnp.where(in_core, push_out, push_in)
    slab[:ins] = jnp.where(in_core, push_in, push_out)
    partner = p.at(c=1 - p.c)
    pieces = [AllSum(p, work[:12]), AllSum(p, work[12:])]
    pack_gram([piece.total for piece in pieces], give[...])
    await_all(p)
    for piece in pieces:
        piece.to_core().start()
    exchange = remote(give, given, give_sems.at[0], give_sems.at[1], partner)
    exchange.start()
    swaps[0].start()
    pack_gram([piece.acc for piece in pieces], slab[:ins])

    def store_messages(k, turned):
        turned = beside(turned, jnp.zeros((D, 256 - turned.shape[1]), F32)) if (
            turned.shape[1] < 256) else turned
        for d in range(count):
            messages[k, d] = turned[own * d : own * d + own]

    steps = len(pieces[0].steps)
    for k in range(steps + BEHIND):
        for which, piece in enumerate(pieces):
            if 0 <= k - BEHIND * which < steps:
                piece.steps[k - BEHIND * which]()
        if k == 0:
            store_messages(0, above(new_in, new_out).T)
    exchange.wait()
    swaps[0].wait()
    swaps[1].start()
    smalls_ref[...] = smalls[...]
    rows = smalls[...].reshape(-1, 128)
    new_step = beside(*[rows[HEADS * j : HEADS * j + HEADS] for j in range(D // 128)])
    mine_at = lax.broadcasted_iota(jnp.int32, (own, D), 0) + own * (p.z * p.F + p.f)
    chosen = (lax.broadcasted_iota(jnp.int32, (own, D), 1) == mine_at).astype(F32).astype(BF16)
    step_ref[...] = exact_pick(chosen, new_step)
    push_step = push(new_step, old_ref[...].T[ins + gates : ins + gates + HEADS])
    push_step = jnp.where(in_core, push_step, 0.0)
    mine, theirs = slab[:ins], given[...]
    slab_in = above(mine, theirs, push_step)
    slab_out = above(theirs[:gates], mine[:gates], jnp.zeros((2 * (ins - gates) + HEADS, D), F32))
    slab[: 2 * ins + HEADS] = jnp.where(in_core, slab_in, slab_out)
    slab[2 * ins + HEADS :] = jnp.zeros((slab.shape[0] - 2 * ins - HEADS, D), F32)
    gram = mats.at[0]
    unpack_gram(gram, [piece.total for piece in pieces])
    step_high, step_low = split(push_step)
    step_left = above(step_high, step_low, step_high)
    gram[...] = gram[...] + dot_tn(step_left, above(step_high, step_high, step_low))
    iterate(gram, mats.at[1], mats.at[2], left, right, slab, slab_left)
    store_messages(1, slab[...].T)
    swaps[2].start()
    swaps[1].wait()
    swaps[2].wait()


def update_call(parts, small, old, sizes, collective_id):
    count = sizes[0] * sizes[1]
    own = D // count
    chips = count // 2
    ins = sum(part.shape[0] for part in parts[:3])
    per = -(-(D // 2) // (8 * chips)) * 8
    blocks = [(per, 512), (per, D + 128 - 512)]
    vmem = pl.BlockSpec(memory_space=pltpu.VMEM)
    hbm = pl.BlockSpec(memory_space=pl.ANY)
    dma = pltpu.SemaphoreType.DMA
    return pl.pallas_call(
        functools.partial(update_kernel, sizes),
        out_shape=[
            shape(count, own, 256), shape(count, *small.shape), shape(count, own, 256),
            shape(own, HEADS),
        ],
        in_specs=[vmem] * 6,
        out_specs=[hbm, vmem, hbm, vmem],
        scratch_shapes=[
            pltpu.VMEM((ins, D), F32), pltpu.VMEM((ins, D), F32), dma((2,)),
            pltpu.VMEM((2, count, own, 256), F32), pltpu.VMEM((count,) + small.shape, F32),
            pltpu.VMEM((3, D, D), F32),
            pltpu.VMEM((D, 3 * D), BF16), pltpu.VMEM((3 * D, D), BF16),
            pltpu.VMEM((256, D), F32), pltpu.VMEM((256, 3 * D), BF16),
            dma((3, count)), dma((3, count)), dma((3,)),
        ]
        + all_sum_scratch(sizes, blocks[0])
        + all_sum_scratch(sizes, blocks[1]),
        compiler_params=pltpu.CompilerParams(
            collective_id=collective_id, has_side_effects=True, vmem_limit_bytes=56 * 2**20
        ),
        name="update",
    )(*parts, small, old)


def finish_kernel(
    moved_ref, spread_ref, step_ref, w_in_ref, w_out_ref, m_in_ref, m_out_ref, dx_ref,
    g_in_ref, g_out_ref, new_m_in_ref, new_m_out_ref, new_w_in_ref, new_w_out_ref, dx_out_ref,
    held, sems,
):
    load = pltpu.make_async_copy(dx_ref, held, sems.at[0])
    store = pltpu.make_async_copy(held, dx_out_ref, sems.at[1])
    load.start()
    count = moved_ref.shape[0]
    cuts, outs = cuts_of(count)
    ins = sum(each for _, _, each in cuts)
    decay = 1.0 - MATRIX_RATE * WEIGHT_DECAY
    order = [(2 * chip + core, core) for core in range(2) for chip in range(count // 2)]
    at = 0
    for start, width, each in cuts:
        cols = slice(start, start + width)
        g_in_ref[:, cols] = beside(*[moved_ref[d, :, at : at + each] for d, _ in order])
        new_w_in_ref[:, cols] = beside(*[
            spread_ref[d - core, :, ins * core + at : ins * core + at + each] for d, core in order
        ])
        at += each
    load.wait()
    store.start()
    g_in_ref[:, WIDE:] = step_ref[...]
    new_w_in_ref[:, WIDE:] = spread_ref[0, :, 2 * ins : 2 * ins + HEADS]
    g_out_ref[...] = beside(*[moved_ref[d, :, ins : ins + outs] for d, _ in order])
    new_w_out_ref[...] = beside(*[
        spread_ref[d - core + 1, :, outs * core : outs * core + outs] for d, core in order
    ])
    for wide_side, g_ref, m_ref, w_ref, new_m_ref, new_w_ref in (
        (IN_W, g_in_ref, m_in_ref, w_in_ref, new_m_in_ref, new_w_in_ref),
        (INNER, g_out_ref, m_out_ref, w_out_ref, new_m_out_ref, new_w_out_ref),
    ):
        new_m_ref[...] = MOMENTUM * m_ref[...] + g_ref[...]
        rate = MATRIX_RATE * 0.2 * math.sqrt(max(D, wide_side))
        new_w_ref[...] = w_ref[...] * decay - rate * new_w_ref[...]
    store.wait()


def finish_call(moved, spread, step_rows, matrices, dx):
    vmem = pl.BlockSpec(memory_space=pltpu.VMEM)
    hbm = pl.BlockSpec(memory_space=pl.ANY)
    return pl.pallas_call(
        finish_kernel,
        out_shape=[shape(*matrix.shape) for matrix in matrices[:2]] * 3 + [shape(*dx.shape)],
        in_specs=[vmem] * 7 + [hbm],
        out_specs=[vmem] * 6 + [hbm],
        scratch_shapes=[pltpu.VMEM(dx.shape, F32), pltpu.SemaphoreType.DMA((2,))],
        compiler_params=pltpu.CompilerParams(vmem_limit_bytes=60 * 2**20),
        name="finish",
    )(moved, spread, step_rows, *matrices, dx)


def shards(
    inputs, cotangent, weight_in, weight_out, small_params, moment_in, moment_out, moment_small
):
    sizes = (lax.axis_size("dp"), lax.axis_size("fsdp"))
    weights, blocks, vectors = gather_call(
        weight_in, weight_out, moment_in, moment_out, small_params, sizes, 0
    )
    output, dx, columns, factors, small, old = block_and_gradients(
        inputs[0], cotangent[0], weights, vectors, blocks, sizes, (3, 4)
    )
    new_out, new_gate, new_conv_a, new_conv_b, new_small = scatter_call(
        columns, factors, small, sizes, 1
    )
    moved, smalls, spread, step_rows = update_call(
        (new_gate, new_conv_a, new_conv_b, new_out), new_small, old.reshape(D, 256), sizes, 2
    )
    smalls = smalls.reshape(-1)
    grad_small = smalls[HEADS * D : HEADS * D + SMALL]
    grad_in, grad_out, new_moment_in, new_moment_out, new_weight_in, new_weight_out, dx = (
        finish_call(
            moved, spread, step_rows, (weight_in, weight_out, moment_in, moment_out), dx
        )
    )
    new_moment_small = MOMENTUM * moment_small + grad_small
    new_small_params = small_params - SMALL_RATE * new_moment_small
    return (
        output[None],
        dx[None],
        grad_in,
        grad_out,
        grad_small,
        new_moment_in,
        new_moment_out,
        new_moment_small,
        new_weight_in,
        new_weight_out,
        new_small_params,
    )


def solution(mesh):
    return jax.shard_map(
        shards,
        mesh=mesh,
        in_specs=(
            P(("dp", "fsdp"), None, None),
            P(("dp", "fsdp"), None, None),
            P(("dp", "fsdp"), None),
            P(("dp", "fsdp"), None),
            P(),
            P(("dp", "fsdp"), None),
            P(("dp", "fsdp"), None),
            P(),
        ),
        out_specs=(
            P(("dp", "fsdp"), None, None),
            P(("dp", "fsdp"), None, None),
            P(("dp", "fsdp"), None),
            P(("dp", "fsdp"), None),
            P(),
            P(("dp", "fsdp"), None),
            P(("dp", "fsdp"), None),
            P(),
            P(("dp", "fsdp"), None),
            P(("dp", "fsdp"), None),
            P(),
        ),
        check_vma=False,
    )
```

```python
import functools
import math

import jax
import jax.numpy as jnp
from jax import lax
from jax.experimental import pallas as pl
from jax.experimental.pallas import tpu as pltpu
from jax.sharding import PartitionSpec as P

D = 768
HEADS = 24
HEAD_DIM = 64
NSTATE = 128
KCONV = 4
LEN = 1024
ITERS = 5
INNER = 1536
CONVCH = 1792
IN_W = 3352
SMALL = 11336
WIDE = INNER + CONVCH
TAIL_SUMS = 1664 - 2 * HEADS
STEP = 32
CONV_A = 768
HALF = 2560
OUT_AT = WIDE - HALF
STEP_AT = OUT_AT + INNER

MOMENTUM = 0.95
MATRIX_RATE = 0.15
WEIGHT_DECAY = 0.1
SMALL_RATE = 0.01
EPSILON = 1e-05
COEF_A = 3.4445
COEF_B = -4.775
COEF_C = 2.0315

F32 = jnp.float32
BF16 = jnp.bfloat16
CHUNK = 128
STRIP = 256
PER = STRIP // CHUNK
STRIPS = LEN // STRIP
GRAD_TILE = 256
GROUP = 4


def dot(a, b):
    return lax.dot_general(a, b, (((1,), (0,)), ((), ())), preferred_element_type=F32)


def dot_nt(a, b):
    return lax.dot_general(a, b, (((1,), (1,)), ((), ())), preferred_element_type=F32)


def dot_tn(a, b):
    return lax.dot_general(a, b, (((0,), (0,)), ((), ())), preferred_element_type=F32)


def split(v):
    high = v.astype(BF16)
    return high, (v - high.astype(F32)).astype(BF16)


def beside(*parts):
    return jnp.concatenate(parts, axis=1)


def above(*parts):
    return jnp.concatenate(parts, axis=0)


def right_pair(b):
    high, low = split(b)
    return above(beside(high, low), beside(high, jnp.zeros_like(low)))


def three_pass(a, pair):
    high, low = split(a)
    both = dot(beside(high, low), pair)
    half = both.shape[1] // 2
    return both[:, :half] + both[:, half:]


def exact_sum(a, ones):
    high = a.astype(BF16)
    rest = a - high.astype(F32)
    mid = rest.astype(BF16)
    low = (rest - mid.astype(F32)).astype(BF16)
    return dot(beside(high, mid, low), above(ones, ones, ones))


def lane_sums(a):
    high = a.astype(BF16)
    rest = a - high.astype(F32)
    mid = rest.astype(BF16)
    low = (rest - mid.astype(F32)).astype(BF16)
    parts = beside(high, mid, low)
    return dot_nt(jnp.ones((8, parts.shape[1]), BF16), parts)


def stack_left(a):
    high, low = split(a)
    return above(beside(high, high), beside(low, jnp.zeros_like(low)))


def fold(rows):
    total = rows[0:8]
    for i in range(1, rows.shape[0] // 8):
        total = total + rows[8 * i : 8 * i + 8]
    return total


def row_sum(rows):
    return jnp.sum(fold(rows), axis=0, keepdims=True)


def upper():
    row = lax.broadcasted_iota(jnp.int32, (CHUNK, CHUNK), 0)
    col = lax.broadcasted_iota(jnp.int32, (CHUNK, CHUNK), 1)
    return col >= row


def softplus(v):
    return jnp.maximum(v, 0.0) + jnp.log1p(jnp.exp(-jnp.abs(v)))


def rates_of(raw, heads_ref, ones):
    steps = softplus(raw + heads_ref[0])
    logs = exact_sum(steps * heads_ref[1], ones)
    last = jnp.broadcast_to(logs[:, CHUNK - 1 : CHUNK], logs.shape)
    columns = above(logs, jnp.zeros((CHUNK - HEADS, CHUNK), F32)).T
    return steps, logs, columns, jnp.exp(logs), jnp.exp(last - logs), jnp.exp(last)


def silu(v):
    return v * jax.nn.sigmoid(v)


def wide(v):
    return beside(*([v] * PER))


def strip_at(s):
    return pl.ds(pl.multiple_of(s * STRIP, STRIP), STRIP)


def half_rows(rows, c):
    return pl.ds(pl.multiple_of(c * (rows // 2), rows // 2), rows // 2)


class Box:
    def __init__(self, box, dst, sems, partner):
        self.box, self.dst, self.sems, self.partner = box, dst, sems, partner

    def copy(self, s):
        sem = self.sems.at[s]
        return remote(
            self.box.at[lax.rem(s, 2)], self.dst(s), sem.at[0], sem.at[1], self.partner
        )

    def fill(self, s, value, back=False):
        @pl.when(pl.program_id(0) > 1)
        def _():
            self.copy(s + 2 if back else s - 2).wait_send()

        self.box[lax.rem(s, 2)] = value
        self.copy(s).start()

    def finish(self, back=False):
        for s in range(2):
            self.copy(s if back else STRIPS - 1 - s).wait_send()
        for s in range(STRIPS):
            self.copy(s).wait_recv()


def forward_kernel(
    sizes, x_ref, back_ref, first_ref, second_ref, gain_ref, taps_in, heads_ref, inner_in,
    blocks_ref, whole_back_ref,
    out_ref, hb_ref, cin_ref, c_ref, raw_ref, s_ref, own_normed_ref,
    dy_ref, dgate_ref, own_dgate_ref, dlogs_ref, tail_sums_ref, moved_ref,
    peer_normed_ref, peer_dgate_ref, peer_hb_ref, peer_back_ref,
    act, z, mixed, dnormed, state, tail, turned, dskip, dinner, normed_ref,
    taps_ref, inner_ref, load_sems, box_normed, box_dgate, box_hb, box_sems, back_sems, *work,
):
    p = Place(sizes)
    swap = Swap(p, blocks_ref, moved_ref, *work)
    partner = p.at(c=1 - p.c)
    strip = pl.program_id(0)
    back_copy = remote(
        whole_back_ref, peer_back_ref, back_sems.at[0], back_sems.at[1], partner
    )
    boxes = [
        Box(box, lambda s, ref=ref: ref.at[:, strip_at(s)], box_sems.at[k], partner)
        for k, (box, ref) in enumerate(
            [(box_normed, peer_normed_ref), (box_dgate, peer_dgate_ref)]
        )
    ]
    boxes.append(Box(box_hb, lambda s: peer_hb_ref.at[strip_at(s)], box_sems.at[2], partner))

    @pl.when(strip == 0)
    def _():
        loads = [
            pltpu.make_async_copy(taps_in, taps_ref, load_sems.at[0]),
            pltpu.make_async_copy(inner_in, inner_ref, load_sems.at[1]),
        ]
        for load in loads:
            load.start()
        greet_all(p, False)
        state[...] = jnp.zeros_like(state)
        tail[...] = jnp.zeros_like(tail)
        dskip[...] = jnp.zeros_like(dskip)
        dinner[...] = jnp.zeros_like(dinner)
        for i in range(HALF // 256):
            part = slice(256 * i, 256 * i + 256)
            turned[0, part] = first_ref[:, part].T
            turned[1, part] = second_ref[:, part].T
        for load in loads:
            load.wait()
        await_all(p)
        back_copy.start()
        swap.start()

    x = x_ref[...].astype(F32)
    scaled = x * lax.rsqrt(jnp.mean(x * x, axis=-1, keepdims=True) + EPSILON) * gain_ref[...]
    hb = scaled.astype(BF16)
    hb_ref[...] = hb
    boxes[2].fill(strip, hb)
    back = back_ref[...]
    raw_ref[...] = dot_nt(turned[1, STEP_AT : STEP_AT + STEP], hb)

    lane = lax.broadcasted_iota(jnp.int32, (64, CHUNK), 1)

    def later(cols, steps, before):
        turned_cols = [before] + [pltpu.roll(col, steps, 1) for col in cols]
        pairs = zip(turned_cols[:-1], turned_cols[1:])
        return [jnp.where(lane < steps, a, b) for a, b in pairs], turned_cols[-1]

    def conv_tile(i):
        rows = slice(64 * i, 64 * i + 64)
        cur = cin_ref[rows]
        cols = [cur[:, CHUNK * j : CHUNK * j + CHUNK] for j in range(PER)]
        taps = [taps_ref[k, rows] for k in range(KCONV + 1)]
        ones_late, tail[0, rows] = later(cols, 1, tail[0, rows])
        early = [taps[1] * a + taps[0] * b for a, b in zip(cols, ones_late)]
        twos_late, tail[1, rows] = later(early, 2, tail[1, rows])
        total = beside(*[
            taps[4] + c + taps[2] * b + taps[3] * a for a, b, c in zip(cols, ones_late, twos_late)
        ])
        c_ref[rows] = total
        act[rows] = total * jax.nn.sigmoid(total)

    def project(i):
        start = INNER + 256 * i
        rows = turned[start // HALF, start % HALF : start % HALF + 256]
        cin_ref[256 * i : 256 * i + 256] = dot_nt(rows, hb)

    project(0)
    for i in range(CONVCH // 256):
        if i + 1 < CONVCH // 256:
            project(i + 1)
        if i < INNER // 256:
            part = slice(256 * i, 256 * i + 256)
            z[part] = dot_nt(turned[0, part], hb)
            dnormed[part] = dot_nt(turned[1, OUT_AT + 256 * i : OUT_AT + 256 * i + 256], back)
        for q in range(4):
            conv_tile(4 * i + q)
    causal = upper()
    ones = causal.astype(F32).astype(BF16)

    def chunk(j, carry):
        cols = pl.ds(pl.multiple_of(j * CHUNK, CHUNK), CHUNK)
        steps, logs, columns, grown, to_end, through = rates_of(
            raw_ref[0:HEADS, cols], heads_ref, ones
        )
        in_map = act[INNER : INNER + NSTATE, cols].T
        in_pair = right_pair(in_map)
        out_pair = right_pair(act[INNER + NSTATE :, cols])
        scores = three_pass(in_map, out_pair)
        for g in range(HEADS // GROUP):
            rows = slice(g * GROUP * HEAD_DIM, (g + 1) * GROUP * HEAD_DIM)
            held = state[rows]
            s_ref[j, rows] = held
            across = three_pass(held, out_pair)
            ending, kept = [], []
            for q in range(GROUP):
                h = g * GROUP + q
                mine = slice(h * HEAD_DIM, (h + 1) * HEAD_DIM)
                values = act[mine, cols]
                fed = values * steps[h : h + 1]
                gaps = logs[h : h + 1] - jnp.broadcast_to(columns[:, h : h + 1], (CHUNK, CHUNK))
                weights = scores * jnp.where(causal, jnp.exp(gaps), 0.0)
                both = dot(stack_left(fed), above(*split(weights)))
                y = both[:HEAD_DIM] + both[HEAD_DIM:]
                y = y + across[q * HEAD_DIM : (q + 1) * HEAD_DIM] * grown[h : h + 1]
                mixed[mine, cols] = y + heads_ref[2][h : h + 1] * values
                ending.append(fed * to_end[h : h + 1])
                kept.append(jnp.broadcast_to(through[h : h + 1], (HEAD_DIM, CHUNK)))
            state[rows] = held * above(*kept) + three_pass(above(*ending), in_pair)
        return carry

    lax.fori_loop(0, PER, chunk, 0)

    def mean_tile(h, totals):
        rows = pl.ds(pl.multiple_of(h * HEAD_DIM, HEAD_DIM), HEAD_DIM)
        gate = z[rows, :]
        opened = mixed[rows, :] * (gate * jax.nn.sigmoid(gate))
        gained = dnormed[rows, :] * wide(inner_ref[rows, :]) * opened
        return totals[0] + fold(opened * opened), totals[1] + fold(gained)

    nothing = jnp.zeros((8, STRIP), F32)
    squares, gains = lax.fori_loop(0, HEADS, mean_tile, (nothing, nothing), unroll=4)
    mean = jnp.sum(squares, axis=0, keepdims=True) * (1.0 / INNER)
    r = lax.rsqrt(mean + EPSILON)
    pulled = jnp.sum(gains, axis=0, keepdims=True) * (1.0 / INNER) * (r * r * r)

    def gate_tile(h, carry):
        rows = pl.ds(pl.multiple_of(h * HEAD_DIM, HEAD_DIM), HEAD_DIM)
        gate = z[rows, :]
        skip = wide(heads_ref[2, pl.ds(h, 1), :])
        mix = mixed[rows, :]
        sig = jax.nn.sigmoid(gate)
        sil = gate * sig
        opened = mix * sil
        normed = opened * r
        inner = wide(inner_ref[rows, :])
        normed_ref[rows, :] = (normed * inner).astype(BF16)
        dn = dnormed[rows, :]
        gained = dn * normed
        dinner[rows, :] += gained[:, :CHUNK] + gained[:, CHUNK:]
        dopened = dn * inner * r - opened * pulled
        dmixed = dopened * sil
        dy_ref[rows, :] = dmixed
        dgate_ref[rows, :] = (dopened * mix * (sig * (1.0 + gate * (1.0 - sig)))).astype(BF16)
        skipped = row_sum(dmixed * act[rows, :])
        dskip[pl.ds(h, 1), :] += skipped[:, :CHUNK] + skipped[:, CHUNK:]
        dlogs_ref[pl.ds(h, 1), :] = row_sum(dmixed * mix) - skip * skipped
        return carry

    lax.fori_loop(0, HEADS, gate_tile, 0)
    for box, own, ref in (
        (boxes[0], own_normed_ref, normed_ref), (boxes[1], own_dgate_ref, dgate_ref),
    ):
        own[...] = ref[half_rows(INNER, p.c), :]
        box.fill(strip, ref[half_rows(INNER, 1 - p.c), :])
    for i in range(D // 256):
        part = slice(256 * i, 256 * i + 256)
        branch = dot(second_ref[part, OUT_AT:STEP_AT], normed_ref[...]).T
        out_ref[:, part] = (x_ref[:, part].astype(F32) + branch).astype(BF16)

    @pl.when(pl.program_id(0) == STRIPS - 1)
    def _():
        tail_sums_ref[...] = beside(
            lane_sums(dskip[...]), lane_sums(dinner[...]),
            jnp.zeros((8, tail_sums_ref.shape[1] - HEADS - INNER), F32),
        )
        swap.wait()
        back_copy.wait()
        for box in boxes:
            box.finish()


def backward_kernel(
    sizes, x_ref, back_ref, w_in_ref, step_in_ref, gain_ref, taps_ref, heads_ref,
    cin_ref, c_ref, raw_ref, s_ref, dy, dgate_ref, dlogs, tail_sums_ref, out_part, gate_part,
    dx_ref, own_a_ref, own_b_ref, flat_ref, out_column, gate_column, peer_a_ref, peer_b_ref,
    dconv_a_ref, dconv_b_ref, box_a, box_b, box_sems, dact, dstate, flow, tail, meets, vdu_rows, dstep_ref, dstep_sum, dgain, dtaps_ref, dheads_ref,
    dscaled_turned, *work,
):
    step_now = pl.program_id(0)
    p = Place(sizes)
    partner = p.at(c=1 - p.c)
    strip = STRIPS - 1 - step_now
    boxes = [
        Box(box, lambda s, ref=ref: ref.at[:, strip_at(s)], box_sems.at[k], partner)
        for k, (box, ref) in enumerate([(box_a, peer_a_ref), (box_b, peer_b_ref)])
    ]
    sums = [
        PlaneSum(p, part, work[7 * k : 7 * k + 7]) for k, part in enumerate((out_part, gate_part))
    ]

    @pl.when(step_now == 0)
    def _():
        sums[0].begin()
        greet_near(p, False, False)

    @pl.when(step_now == 0)
    def _():
        dstate[...] = jnp.zeros_like(dstate)
        flow[...] = jnp.zeros_like(flow)
        tail[...] = jnp.zeros_like(tail)
        dgain[...] = jnp.zeros_like(dgain)
        dstep_sum[...] = jnp.zeros_like(dstep_sum)
        dtaps_ref[...] = jnp.zeros_like(dtaps_ref)
        dheads_ref[...] = jnp.zeros_like(dheads_ref)
        await_near(p, False)
        sums[0].start()
        sums[1].begin()

    @pl.when(step_now == 3)
    def _():
        sums[1].plane.finish(0)
        sums[1].plane.start(1)

    back = back_ref[...]

    causal = upper()
    ones = causal.astype(F32).astype(BF16)
    row = lax.broadcasted_iota(jnp.int32, (CHUNK, CHUNK), 0)
    col = lax.broadcasted_iota(jnp.int32, (CHUNK, CHUNK), 1)
    ones_back = (row >= col).astype(F32).astype(BF16)

    def chunk(step, carry):
        j = PER - 1 - step
        cols = pl.ds(pl.multiple_of(j * CHUNK, CHUNK), CHUNK)
        raw = raw_ref[0:HEADS, cols]
        steps, logs, columns, grown, to_end, through = rates_of(raw, heads_ref, ones)
        in_turned = silu(c_ref[INNER : INNER + NSTATE, cols])
        out_turned = silu(c_ref[INNER + NSTATE :, cols])
        in_map = in_turned.T
        out_map = out_turned.T
        scores = three_pass(in_map, right_pair(out_turned))
        in_pair = right_pair(in_turned)
        out_pair = right_pair(out_map)
        dscores = jnp.zeros((CHUNK, CHUNK), F32)
        din = jnp.zeros((NSTATE, CHUNK), F32)
        dout = jnp.zeros((NSTATE, CHUNK), F32)
        for g in range(HEADS // GROUP):
            rows = slice(g * GROUP * HEAD_DIM, (g + 1) * GROUP * HEAD_DIM)
            leaving = dstate[rows]
            entering = s_ref[j, rows]
            from_state = three_pass(leaving, in_pair)
            ending, growing, kept = [], [], []
            for q in range(GROUP):
                h = g * GROUP + q
                mine = slice(h * HEAD_DIM, (h + 1) * HEAD_DIM)
                values = silu(c_ref[mine, cols])
                fed = values * steps[h : h + 1]
                dys = dy[mine, cols]
                gaps = logs[h : h + 1] - jnp.broadcast_to(columns[:, h : h + 1], (CHUNK, CHUNK))
                decay = jnp.where(causal, jnp.exp(gaps), 0.0)
                weights = scores * decay
                both = dot_nt(stack_left(dys), beside(*split(weights)))
                du = both[:HEAD_DIM] + both[HEAD_DIM:]
                du = du + from_state[q * HEAD_DIM : (q + 1) * HEAD_DIM] * to_end[h : h + 1]
                fed_high, fed_low = split(fed)
                dy_high, dy_low = split(dys)
                dweights = dot_tn(
                    above(fed_high, fed_low, fed_high), above(dy_high, dy_high, dy_low)
                )
                dscores = dscores + dweights * decay
                vdu_rows[h : h + 1, :] = row_sum(values * du)
                dact[mine, cols] = du * steps[h : h + 1] + heads_ref[2][h : h + 1] * dys
                ending.append(fed * to_end[h : h + 1])
                growing.append(dys * grown[h : h + 1])
                kept.append(jnp.broadcast_to(through[h : h + 1], (HEAD_DIM, CHUNK)))
            ending = above(*ending)
            growing = above(*growing)
            end_high, end_low = split(ending)
            grow_high, grow_low = split(growing)
            leave_high, leave_low = split(leaving)
            enter_high, enter_low = split(entering)
            din = din + dot_tn(
                above(leave_high, leave_low, leave_high), above(end_high, end_high, end_low)
            )
            dout = dout + dot_tn(
                above(enter_high, enter_low, enter_high), above(grow_high, grow_high, grow_low)
            )
            arrived = leaving * above(*kept) + three_pass(growing, out_pair)
            dstate[rows] = arrived
            meet = arrived * entering
            for q in range(GROUP):
                h = g * GROUP + q
                meets[h : h + 1, :] = row_sum(meet[q * HEAD_DIM : (q + 1) * HEAD_DIM])
        vdu = vdu_rows[...]
        dlog = dlogs[:, cols] - steps * vdu
        drate = exact_sum(dlog, ones_back) + flow[...]
        flow[...] = jnp.broadcast_to(
            jnp.sum(meets[...], axis=1, keepdims=True), (HEADS, CHUNK)
        )
        dsteps = vdu + heads_ref[1] * drate
        draw = dsteps * jax.nn.sigmoid(raw + heads_ref[0])
        dheads_ref[0] += draw
        dheads_ref[1] += drate * steps * heads_ref[1]
        dstep_ref[:, cols] = above(draw, jnp.zeros((STEP - HEADS, CHUNK), F32)).astype(BF16)
        score_high, score_low = split(dscores)
        both = dot_nt(stack_left(out_turned), beside(score_high, score_low))
        dact[INNER : INNER + NSTATE, cols] = din + both[:NSTATE] + both[NSTATE:]
        both = dot(stack_left(in_turned), above(score_high, score_low))
        dact[INNER + NSTATE :, cols] = dout + both[:NSTATE] + both[NSTATE:]
        return carry

    lax.fori_loop(0, PER, chunk, 0)

    @pl.when(step_now == 0)
    def _():
        sums[1].start()

    @pl.when(step_now == 2)
    def _():
        sums[0].plane.finish(0)
        sums[0].plane.start(1)

    lane = lax.broadcasted_iota(jnp.int32, (64, CHUNK), 1)

    def conv_tile(target, start, i):
        rows = slice(start + 64 * i, start + 64 * i + 64)
        c = c_ref[rows]
        sig = jax.nn.sigmoid(c)
        dpre = dact[rows] * (sig * (1.0 + c * (1.0 - sig)))
        cin = cin_ref[rows]
        cols = [dpre[:, CHUNK * j : CHUNK * j + CHUNK] for j in range(PER)]
        dcin = dpre * wide(taps_ref[KCONV - 1, rows])
        grad = cin * dpre
        dtaps_ref[KCONV - 1, rows] += grad[:, :CHUNK] + grad[:, CHUNK:]
        dtaps_ref[KCONV, rows] += dpre[:, :CHUNK] + dpre[:, CHUNK:]
        for k in range(KCONV - 1):
            ahead = KCONV - 1 - k
            turned = [pltpu.roll(col, CHUNK - ahead, 1) for col in cols] + [tail[k, rows]]
            tail[k, rows] = turned[0]
            pairs = zip(turned[:-1], turned[1:])
            shifted = beside(*[jnp.where(lane < CHUNK - ahead, a, b) for a, b in pairs])
            dcin = dcin + shifted * wide(taps_ref[k, rows])
            grad = cin * shifted
            dtaps_ref[k, rows] += grad[:, :CHUNK] + grad[:, CHUNK:]
        target[64 * i : 64 * i + 64] = dcin.astype(BF16)

    thirds = [slice(256 * i, 256 * i + 256) for i in range(D // 256)]
    conv_at = INNER + CONV_A
    tiles = CONV_A // 64
    for i in range(tiles):
        conv_tile(dconv_a_ref, 0, i)
        if i % 4 == 0:
            part = thirds[i // 4]
            dscaled_turned[part] = dot(w_in_ref[part, :INNER], dgate_ref[...])
    for i in range((CONVCH - CONV_A) // 64):
        conv_tile(dconv_b_ref, CONV_A, i)
        if i % 4 == 0 and i // 4 < len(thirds):
            part = thirds[i // 4]
            dscaled_turned[part] += dot(w_in_ref[part, INNER:conv_at], dconv_a_ref[...])
    for box, own, ref in (
        (boxes[0], own_a_ref, dconv_a_ref), (boxes[1], own_b_ref, dconv_b_ref),
    ):
        own[...] = ref[half_rows(ref.shape[0], p.c), :]
        box.fill(strip, ref[half_rows(ref.shape[0], 1 - p.c), :], True)
    x = x_ref[...].astype(F32)
    r = lax.rsqrt(jnp.mean(x * x, axis=-1, keepdims=True) + EPSILON)
    parts = []
    for part in thirds:
        total = dscaled_turned[part] + dot(w_in_ref[part, conv_at:], dconv_b_ref[...])
        parts.append((total + dot(step_in_ref[part, :STEP], dstep_ref[...])).T)
    dscaled = beside(*parts)
    plain = x * r
    dgain[...] += fold(dscaled * plain)
    dstep_sum[...] += dot(dstep_ref[...], (plain * gain_ref[...]).astype(BF16))
    gained = dscaled * gain_ref[...]
    inner = jnp.mean(gained * plain, axis=-1, keepdims=True)
    dx_ref[...] = back.astype(F32) + (gained - plain * inner) * r

    @pl.when(step_now == STRIPS - 1)
    def _():
        for part, column in zip(sums, (out_column, gate_column)):
            part.plane.finish(1)
            column[...] = part.column()
        for box in boxes:
            box.finish(True)
        store_flat(flat_ref, dstep_sum, dgain, dtaps_ref, dheads_ref, tail_sums_ref)


def store_flat(flat_ref, dstep_sum, dgain, dtaps, dheads, tail_sums_ref):
    flat_ref[...] = jnp.zeros_like(flat_ref)
    for j in range(D // 128):
        flat_ref[HEADS * j : HEADS * j + HEADS] = dstep_sum[:HEADS, 128 * j : 128 * j + 128]
    last = beside(
        lane_sums(dheads[0])[:1], lane_sums(dheads[1])[:1], tail_sums_ref[:1],
    )
    rows = [jnp.sum(dgain[...], axis=0, keepdims=True)]
    rows += [lane_sums(dtaps[k])[:1] for k in range(KCONV + 1)]
    at = HEADS * (D // 128)
    for row in rows + [last]:
        for j in range(row.shape[1] // 128):
            flat_ref[at + j : at + j + 1] = row[:, 128 * j : 128 * j + 128]
        at += row.shape[1] // 128


def whole(shape):
    return pl.BlockSpec(shape, lambda i: (0,) * len(shape), pipeline_mode=pl.Buffered(1))


def strip_rows(width):
    return pl.BlockSpec((STRIP, width), lambda i: (i, 0))


def strip_cols(height):
    return pl.BlockSpec((height, STRIP), lambda i: (0, i))


def shape(*dims, dtype=F32):
    return jax.ShapeDtypeStruct(dims, dtype)


def columns(width, at):
    return pl.BlockSpec((D, width), lambda i: (0, at), pipeline_mode=pl.Buffered(1))


def forward_call(x, back, weights, gain, taps, heads, inner, blocks, sizes, collective_id):
    count = sizes[0] * sizes[1]
    dma = pltpu.SemaphoreType.DMA
    hbm = pl.BlockSpec(memory_space=pl.ANY)
    return pl.pallas_call(
        functools.partial(forward_kernel, sizes),
        grid=(STRIPS,),
        in_specs=[
            strip_rows(D), strip_rows(D), columns(HALF, 0), columns(HALF, 1), whole((1, D)),
            hbm, whole((3, HEADS, CHUNK)), hbm, hbm, hbm,
        ],
        out_specs=[
            strip_rows(D), strip_rows(D), strip_cols(CONVCH), strip_cols(CONVCH),
            strip_cols(STEP), pl.BlockSpec((PER, INNER, NSTATE), lambda i: (i, 0, 0)),
            strip_cols(INNER // 2), strip_cols(INNER), strip_cols(INNER), strip_cols(INNER // 2),
            strip_cols(HEADS), whole((8, TAIL_SUMS)), hbm, hbm, hbm, hbm, hbm,
        ],
        out_shape=[
            shape(LEN, D, dtype=BF16), shape(LEN, D, dtype=BF16), shape(CONVCH, LEN),
            shape(CONVCH, LEN), shape(STEP, LEN), shape(LEN // CHUNK, INNER, NSTATE),
            shape(INNER // 2, LEN, dtype=BF16), shape(INNER, LEN), shape(INNER, LEN, dtype=BF16),
            shape(INNER // 2, LEN, dtype=BF16), shape(HEADS, LEN), shape(8, TAIL_SUMS),
            shape(*blocks.shape), shape(INNER // 2, LEN, dtype=BF16),
            shape(INNER // 2, LEN, dtype=BF16), shape(LEN, D, dtype=BF16),
            shape(LEN, D, dtype=BF16),
        ],
        scratch_shapes=[
            pltpu.VMEM((CONVCH, STRIP), F32), pltpu.VMEM((INNER, STRIP), F32),
            pltpu.VMEM((INNER, STRIP), F32), pltpu.VMEM((INNER, STRIP), F32),
            pltpu.VMEM((INNER, NSTATE), F32), pltpu.VMEM((2, CONVCH, CHUNK), F32),
            pltpu.VMEM((2, HALF, D), BF16), pltpu.VMEM((HEADS, CHUNK), F32),
            pltpu.VMEM((INNER, CHUNK), F32), pltpu.VMEM((INNER, STRIP), BF16),
            pltpu.VMEM((KCONV + 1, CONVCH, CHUNK), F32), pltpu.VMEM((INNER, CHUNK), F32), dma((2,)),
            pltpu.VMEM((2, INNER // 2, STRIP), BF16), pltpu.VMEM((2, INNER // 2, STRIP), BF16),
            pltpu.VMEM((2, STRIP, D), BF16), dma((3, STRIPS, 2)), dma((2,)),
            dma((count,)), dma((count,)), dma,
        ],
        compiler_params=pltpu.CompilerParams(
            vmem_limit_bytes=60 * 2**20, collective_id=collective_id, has_side_effects=True
        ),
        name="mixer_forward",
    )(x, back, weights, weights, gain, taps, heads, inner, blocks, back)


def backward_call(x, back, weights, gain, taps, heads, kept, tail_sums, parts, sizes,
                  collective_id):
    last = STRIPS - 1

    def rows(width):
        return pl.BlockSpec((STRIP, width), lambda i: (last - i, 0))

    def cols(height):
        return pl.BlockSpec((height, STRIP), lambda i: (0, last - i))

    Z = sizes[0]
    lines = flat_lines(sizes[0] * sizes[1])
    size = (parts[0].shape[1], D)
    dma = pltpu.SemaphoreType.DMA
    hbm = pl.BlockSpec(memory_space=pl.ANY)
    return pl.pallas_call(
        functools.partial(backward_kernel, sizes),
        grid=(STRIPS,),
        in_specs=[
            rows(D), rows(D), columns(WIDE, 0),
            columns(256, (HALF + STEP_AT) // 256), whole((1, D)),
            whole((KCONV, CONVCH, CHUNK)), whole((3, HEADS, CHUNK)), cols(CONVCH),
            cols(CONVCH), cols(STEP),
            pl.BlockSpec((PER, INNER, NSTATE), lambda i: (last - i, 0, 0)), cols(INNER),
            cols(INNER), cols(HEADS), whole((8, TAIL_SUMS)), hbm, hbm,
        ],
        out_specs=[
            rows(D), cols(CONV_A // 2), cols((CONVCH - CONV_A) // 2), whole((lines, 128)),
            whole((Z,) + size), whole((Z,) + size), hbm, hbm,
        ],
        out_shape=[
            shape(LEN, D), shape(CONV_A // 2, LEN, dtype=BF16),
            shape((CONVCH - CONV_A) // 2, LEN, dtype=BF16), shape(lines, 128),
            shape(Z, *size), shape(Z, *size), shape(CONV_A // 2, LEN, dtype=BF16),
            shape((CONVCH - CONV_A) // 2, LEN, dtype=BF16),
        ],
        scratch_shapes=[
            pltpu.VMEM((CONV_A, STRIP), BF16), pltpu.VMEM((CONVCH - CONV_A, STRIP), BF16),
            pltpu.VMEM((2, CONV_A // 2, STRIP), BF16),
            pltpu.VMEM((2, (CONVCH - CONV_A) // 2, STRIP), BF16), dma((2, STRIPS, 2)),
            pltpu.VMEM((CONVCH, STRIP), F32),
            pltpu.VMEM((INNER, NSTATE), F32), pltpu.VMEM((HEADS, CHUNK), F32),
            pltpu.VMEM((KCONV - 1, CONVCH, CHUNK), F32), pltpu.VMEM((HEADS, CHUNK), F32),
            pltpu.VMEM((HEADS, CHUNK), F32), pltpu.VMEM((STEP, STRIP), BF16),
            pltpu.VMEM((STEP, D), F32), pltpu.VMEM((8, D), F32),
            pltpu.VMEM((KCONV + 1, CONVCH, CHUNK), F32), pltpu.VMEM((2, HEADS, CHUNK), F32),
            pltpu.VMEM((D, STRIP), F32),
        ]
        + 2 * (plane_scratch(sizes, size) + [dma]),
        compiler_params=pltpu.CompilerParams(
            vmem_limit_bytes=63 * 2**20, collective_id=collective_id, has_side_effects=True
        ),
        name="mixer_backward",
    )(
        x, back, weights, weights, gain, taps, heads, *kept, tail_sums,
        *(by_chip(part, sizes) for part in parts),
    )


def grads_kernel(*refs):
    ins, block_in, outs, block_out = refs[:8], refs[8], refs[9:11], refs[11]
    sides, others, results, block, sems, out_sems, block_sems = refs[12:]
    load = pltpu.make_async_copy(block_in, block, block_sems.at[0])
    keep = pltpu.make_async_copy(block, block_out, block_sems.at[1])
    copies = []
    for k in range(4):
        copies.append([
            pltpu.make_async_copy(ins[2 * k], sides.at[k], sems.at[2 * k]),
            pltpu.make_async_copy(ins[2 * k + 1], others.at[k], sems.at[2 * k + 1]),
        ])
        for copy in copies[k]:
            copy.start()
    load.start()
    stores = []
    for k in range(2):
        for half in (0, 1):
            for copy in copies[2 * k + half]:
                copy.wait()
            side, other = sides.at[2 * k + half], others.at[2 * k + half]

            def tile(i, carry, k=k, half=half, side=side, other=other):
                rows = pl.ds(pl.multiple_of(i * GRAD_TILE, GRAD_TILE), GRAD_TILE)
                part = dot(side[rows, :], other[...])
                results[k, rows, :] = part if half == 0 else results[k, rows, :] + part
                return carry

            lax.fori_loop(0, INNER // 2 // GRAD_TILE, tile, 0)
        if k == 0:
            load.wait()
            keep.start()
        stores.append(pltpu.make_async_copy(results.at[k], outs[k], out_sems.at[k]))
        stores[k].start()
    for store in stores + [keep]:
        store.wait()


def grads_call(own_normed, peer_normed, own_dgate, peer_dgate, backs, hbs, block):
    rows = INNER // 2
    hbm = pl.BlockSpec(memory_space=pl.ANY)
    return pl.pallas_call(
        grads_kernel,
        in_specs=[hbm] * 9,
        out_specs=[hbm] * 3,
        out_shape=[shape(rows, D)] * 2 + [shape(LEN, D, dtype=BF16)],
        scratch_shapes=[
            pltpu.VMEM((4, rows, LEN), BF16), pltpu.VMEM((4, LEN, D), BF16),
            pltpu.VMEM((2, rows, D), F32), pltpu.VMEM((LEN, D), BF16),
            pltpu.SemaphoreType.DMA((8,)), pltpu.SemaphoreType.DMA((2,)),
            pltpu.SemaphoreType.DMA((2,)),
        ],
        compiler_params=pltpu.CompilerParams(vmem_limit_bytes=60 * 2**20),
        name="grads",
    )(own_normed, backs[0], peer_normed, backs[1], own_dgate, hbs[0], peer_dgate, hbs[1], block)


def flat_lines(count):
    return -(-(HEADS * D + SMALL) // (1024 * count)) * 8 * count


def block_and_gradients(x, back, weights, vectors, blocks, sizes, collective_ids):
    count = sizes[0] * sizes[1]
    gain, taps, heads, inner = vectors
    (
        out, hb, cin, c, raw, states, own_normed, dy, dgate, own_dgate, dlogs, tail_sums, moved,
        peer_normed, peer_dgate, peer_hb, peer_back,
    ) = forward_call(
        x, back, weights, gain, taps, heads, inner, blocks, sizes, collective_ids[0]
    )
    *parts, out = grads_call(
        own_normed, peer_normed, own_dgate, peer_dgate, (back, peer_back), (hb, peer_hb), out
    )
    parts = [part.reshape(count // 2, -1, D) for part in parts]
    dx, own_a, own_b, flat, out_column, gate_column, peer_a, peer_b = backward_call(
        x, back, weights, gain, taps, heads, (cin, c, raw, states, dy, dgate, dlogs), tail_sums,
        parts, sizes, collective_ids[1],
    )
    factors = (own_a, peer_a, own_b, peer_b, hb, peer_hb)
    return out, dx, [out_column, gate_column], factors, flat.reshape(count, -1, 128), moved


MESH = pl.DeviceIdType.MESH


class Place:
    def __init__(self, sizes):
        self.Z, self.F = sizes
        self.C, self.Y = 2, 2
        self.X = self.F // 4
        f = lax.axis_index("fsdp")
        self.z = lax.axis_index("dp")
        self.c = lax.rem(f, 2)
        self.x = lax.rem(f // 2, self.X)
        self.y = f // (2 * self.X)
        self.f = f

    def at(self, z=None, y=None, x=None, c=None):
        z = self.z if z is None else z
        y = self.y if y is None else y
        x = self.x if x is None else x
        c = self.c if c is None else c
        return (z, (y * self.X + x) * 2 + c)

    def other_x(self, step):
        return lax.rem(self.x + step, self.X)


def signal(device):
    pl.semaphore_signal(
        pltpu.get_barrier_semaphore(), inc=1, device_id=device, device_id_type=MESH
    )


def greet_all(place, wait=True):
    count = place.Z * place.F
    me = place.z * place.F + place.f

    def step(i, carry):
        peer = lax.rem(me + i, count)
        signal((peer // place.F, lax.rem(peer, place.F)))
        return carry

    lax.fori_loop(1, count, step, 0)
    if wait:
        await_all(place)


def await_all(place):
    pl.semaphore_wait(pltpu.get_barrier_semaphore(), place.Z * place.F - 1)


def remote(src, dst, send, recv, device):
    return pltpu.make_async_remote_copy(
        src_ref=src, dst_ref=dst, send_sem=send, recv_sem=recv, device_id=device,
        device_id_type=MESH,
    )


def add_blocks(dst, src, count):
    def step(i, carry):
        target = dst(i)
        target[...] = target[...] + src(i)[...]
        return carry

    lax.fori_loop(0, count, step, 0)


class Swap:
    def __init__(self, place, src, dst, send, recv, local, same=False, narrow=None):
        self.place, self.src, self.dst, self.same, self.narrow = place, src, dst, same, narrow
        self.send, self.recv, self.local = send, recv, local
        self.count = place.Z * place.F
        self.me = place.z * place.F + place.f

    def block(self, peer):
        return self.src if self.same else self.src.at[peer]

    def cut(self, ref, odd):
        return ref.at[:, pl.ds(0, self.narrow)] if odd else ref

    def each(self, sender, act):
        if self.narrow is None:
            act(False)
        else:
            @pl.when(lax.rem(sender, 2) == 0)
            def _():
                act(False)

            @pl.when(lax.rem(sender, 2) == 1)
            def _():
                act(True)

    def to(self, i, odd):
        peer = lax.rem(self.me + i, self.count)
        return remote(
            self.cut(self.block(peer), odd), self.cut(self.dst.at[self.me], odd),
            self.send.at[i], self.recv.at[i],
            (peer // self.place.F, lax.rem(peer, self.place.F)),
        )

    def keep(self):
        return pltpu.make_async_copy(self.block(self.me), self.dst.at[self.me], self.local)

    def start(self):
        self.keep().start()

        def step(i, carry):
            self.each(self.me, lambda odd: self.to(i, odd).start())
            return carry

        lax.fori_loop(1, self.count, step, 0)

    def wait(self):
        self.keep().wait()

        def step(i, carry):
            sender = lax.rem(self.me + self.count - i, self.count)
            self.each(self.me, lambda odd: self.to(i, odd).wait_send())
            self.each(sender, lambda odd: remote(
                self.cut(self.block(sender), odd), self.cut(self.dst.at[sender], odd),
                self.send.at[i], self.recv.at[i],
                (sender // self.place.F, lax.rem(sender, self.place.F)),
            ).wait_recv())
            return carry

        lax.fori_loop(1, self.count, step, 0)


def greet_near(place, along_z, wait=True):
    signal(place.at(c=1 - place.c))
    signal(place.at(y=1 - place.y))
    for s in range(1, place.X):
        signal(place.at(x=place.other_x(s)))
    if along_z:
        for s in range(1, place.Z):
            signal(place.at(z=lax.rem(place.z + s, place.Z)))
    if wait:
        await_near(place, along_z)


def await_near(place, along_z):
    pl.semaphore_wait(
        pltpu.get_barrier_semaphore(), place.X + 1 + (place.Z - 1 if along_z else 0)
    )


class Plane:
    def __init__(self, place, acc, x1, y1, x2, y2, sems):
        self.p, self.acc = place, acc
        self.x1, self.y1, self.x2, self.y2, self.sems = x1, y1, x2, y2, sems
        self.h = place.Z // 2

    def copies(self, stage):
        p, acc, h = self.p, self.acc, self.h
        low, high = pl.ds(0, h), pl.ds(h, p.Z - h)
        out = []
        base = stage * p.X
        for s in range(1, p.X):
            x = p.other_x(s)
            if stage == 0:
                src, dst = acc.at[low, :, x], self.x1.at[s - 1]
            else:
                src, dst = acc.at[high, p.y, x], self.x2.at[s - 1]
            sem = self.sems.at[base + s]
            out.append(remote(src, dst, sem.at[0], sem.at[1], p.at(x=x)))
        if stage == 0:
            src, dst = acc.at[high, 1 - p.y], self.y1
        else:
            src, dst = acc.at[low, 1 - p.y, p.x], self.y2
        sem = self.sems.at[base]
        out.append(remote(src, dst, sem.at[0], sem.at[1], p.at(y=1 - p.y)))
        return out

    def start(self, stage):
        for copy in self.copies(stage):
            copy.start()

    def finish(self, stage):
        p, acc, h = self.p, self.acc, self.h
        for copy in self.copies(stage):
            copy.wait()
        for s in range(p.X - 1):
            if stage == 0:
                add_blocks(
                    lambda i: acc.at[i // p.Y, lax.rem(i, p.Y), p.x],
                    lambda i: self.x1.at[s, i // p.Y, lax.rem(i, p.Y)],
                    h * p.Y,
                )
            else:
                add_blocks(
                    lambda i: acc.at[h + i, p.y, p.x], lambda i: self.x2.at[s, i], p.Z - h
                )
        if stage == 0:
            add_blocks(
                lambda i: acc.at[h + i // p.X, p.y, lax.rem(i, p.X)],
                lambda i: self.y1.at[i // p.X, lax.rem(i, p.X)],
                (p.Z - h) * p.X,
            )
        else:
            add_blocks(lambda i: acc.at[i, p.y, p.x], lambda i: self.y2.at[i], h)


def plane_scratch(sizes, block):
    Z, X, Y = sizes[0], sizes[1] // 4, 2
    h = Z // 2
    return [
        pltpu.VMEM((Z, Y, X) + block, F32), pltpu.VMEM((X - 1, h, Y) + block, F32),
        pltpu.VMEM((Z - h, X) + block, F32), pltpu.VMEM((X - 1, Z - h) + block, F32),
        pltpu.VMEM((h,) + block, F32), pltpu.SemaphoreType.DMA((2 * X, 2)),
    ]


def by_place(blocks, sizes):
    return blocks.reshape((sizes[0], 2, sizes[1] // 4, 2) + blocks.shape[1:])


def by_chip(blocks, sizes):
    return blocks.reshape((sizes[0], 2, sizes[1] // 4) + blocks.shape[1:])


class PlaneSum:
    def __init__(self, place, part, work):
        self.p, self.part, self.acc, self.sem = place, part, work[0], work[6]
        self.plane = Plane(place, *work[:6])

    def copy(self):
        return pltpu.make_async_copy(self.part, self.acc, self.sem)

    def begin(self):
        self.copy().start()

    def start(self):
        self.copy().wait()
        self.plane.start(0)

    def block(self, z):
        return self.acc.at[z, self.p.y, self.p.x]

    def column(self):
        return self.acc[:, self.p.y, self.p.x]


class Product(PlaneSum):
    def __init__(self, place, factors, work):
        super().__init__(place, None, work)
        self.factors, self.formed = factors, False

    def begin(self):
        pass

    def start(self):
        if not self.formed:
            self.form()
        self.plane.start(0)

    def form(self):
        self.formed = True
        own, peer, right, peer_right = self.factors
        Z, Y, X, per, _ = self.acc.shape
        h = Z // 2
        size = h * Y * X * per

        def half(k, carry):
            rows = pl.ds(pl.multiple_of(k * size, size), size)
            value = dot(own[rows, :], right[...]) + dot(peer[rows, :], peer_right[...])
            for i in range(h * Y * X):
                place = (k * h + i // (Y * X), i // X % Y, i % X)
                self.acc[place] = value[per * i : per * i + per]
            return carry

        lax.fori_loop(0, Z // h, half, 0)


class PairSum(PlaneSum):
    def __init__(self, place, part, work):
        super().__init__(place, part, work)
        self.core, self.sems = work[7], work[8]

    def copies(self):
        p = self.p
        return (
            remote(
                self.part.at[:, :, :, 1 - p.c], self.core, self.sems.at[0], self.sems.at[1],
                p.at(c=1 - p.c),
            ),
            pltpu.make_async_copy(self.part.at[:, :, :, p.c], self.acc, self.sem),
        )

    def begin(self):
        for copy in self.copies():
            copy.start()

    def start(self):
        p = self.p
        for copy in self.copies():
            copy.wait()

        def place_of(i):
            return i // (p.Y * p.X), lax.rem(i // p.X, p.Y), lax.rem(i, p.X)

        add_blocks(
            lambda i: self.acc.at[place_of(i)], lambda i: self.core.at[place_of(i)],
            p.Z * p.Y * p.X,
        )
        self.plane.start(0)


class Column:
    def __init__(self, part, acc, sem):
        self.copy = pltpu.make_async_copy(part, acc, sem)
        self.acc = acc

    def block(self, z):
        return self.acc.at[z]


class Chain:
    def __init__(self, place, part, held, sems):
        self.p, self.part, self.held, self.sems = place, part, held, sems

    def flow(self, t, side):
        p = self.p
        sem = self.sems.at[side, t]
        target = p.at(z=lax.rem(p.z + 1 - 2 * side + p.Z, p.Z))
        return remote(self.part.block(t), self.held.at[side, t], sem.at[0], sem.at[1], target)

    def first(self):
        p = self.p
        for j in range(p.Z - 1):
            @pl.when(p.z == 0)
            def _():
                self.flow(p.Z - 1 - j, 0).start()

            @pl.when(p.z == p.Z - 1)
            def _():
                self.flow(j, 1).start()

    def receive(self, t, side):
        self.flow(t, side).wait_recv()
        mine = self.part.block(t)
        mine[...] = mine[...] + self.held[side, t]

    def forward(self, j):
        p = self.p

        def turn(k, carry):
            side = lax.rem(k + p.z // (p.Z // 2), 2)
            t = (1 - side) * (p.Z - 1 - j) + side * j
            inside = jnp.logical_and(p.z > 0, p.z < p.Z - 1)

            @pl.when(jnp.logical_and(inside, (1 - 2 * side) * (t - p.z) > 0))
            def _():
                self.receive(t, side)
                self.flow(t, side).start()

            return carry

        lax.fori_loop(0, 2, turn, 0)

    def last(self):
        p = self.p

        @pl.when(p.z > 0)
        def _():
            self.receive(p.z, 0)

        @pl.when(p.z < p.Z - 1)
        def _():
            self.receive(p.z, 1)

    def finish(self):
        p = self.p
        for t in range(p.Z):
            for side in (0, 1):
                @pl.when(p.z < t if side == 0 else p.z > t)
                def _():
                    self.flow(t, side).wait_send()


class Direct:
    def __init__(self, place, part, held, sems):
        self.p, self.part, self.held, self.sems = place, part, held, sems

    def over(self, s):
        p = self.p
        z = lax.rem(p.z + s, p.Z)
        sem = self.sems.at[s]
        return remote(self.part.block(z), self.held.at[s - 1], sem.at[0], sem.at[1], p.at(z=z))

    def start(self):
        for s in range(1, self.p.Z):
            self.over(s).start()

    def last(self):
        mine = self.part.block(self.p.z)
        total = mine[...]
        for s in range(1, self.p.Z):
            self.over(s).wait()
            total = total + self.held[s - 1]
        mine[...] = total


def scatter_kernel(sizes, *refs):
    columns_in, factors, small_in, outs, rest = (
        refs[:2], refs[2:8], refs[8], refs[9:14], list(refs[14:])
    )

    def take(n):
        taken = rest[:n]
        del rest[:n]
        return taken

    p = Place(sizes)
    columns = [Column(ref, *take(2)) for ref in columns_in]
    chains = [Chain(p, column, *take(2)) for column in columns]
    own_a, peer_a, own_b, peer_b, hb, peer_hb = factors
    queue = [
        Product(p, (own_a, peer_a, hb, peer_hb), take(7)),
        Product(p, (own_b, peer_b, hb, peer_hb), take(7)),
        PairSum(p, small_in, take(9)),
    ]
    queue = [(part, Direct(p, part, *take(2))) for part in queue]
    greet_near(p, True, False)
    for column in columns:
        column.copy.start()
    queue[0][0].form()
    await_near(p, True)
    for part, _ in queue:
        part.begin()
    for column, chain in zip(columns, chains):
        column.copy.wait()
        chain.first()
    hops = p.Z - 2

    def forward(j):
        if j < hops:
            for chain in chains:
                chain.forward(j)

    stages = [
        lambda part, direct: part.start(),
        lambda part, direct: (part.plane.finish(0), part.plane.start(1)),
        lambda part, direct: (part.plane.finish(1), direct.start()),
    ]
    for k, stage in enumerate(stages):
        for part, direct in queue:
            stage(part, direct)
        forward(k)
    for k in range(len(stages), hops):
        forward(k)
    for chain in chains:
        chain.last()
        chain.finish()
    for _, direct in queue:
        direct.last()
    for part, out in zip(columns + [part for part, _ in queue], outs):
        out[...] = part.block(p.z)[...]


def scatter_call(columns, factors, small, sizes, collective_id):
    Z, F = sizes
    X, Y = F // 4, 2
    chips = Z * X * Y
    dma = pltpu.SemaphoreType.DMA
    parts = [(factors[0].shape[0] // chips, D), (factors[2].shape[0] // chips, D)]
    parts.append(small.shape[1:])
    scratch = []
    for column in columns:
        scratch += [pltpu.VMEM(column.shape, F32), dma]
    for column in columns:
        scratch += [pltpu.VMEM((2, Z) + column.shape[1:], F32), dma((2, Z, 2))]
    for block in parts:
        scratch += plane_scratch(sizes, block) + [dma]
    scratch += [pltpu.VMEM((Z, Y, X) + parts[2], F32), dma((2,))]
    for block in parts:
        scratch += [pltpu.VMEM((Z - 1,) + block, F32), dma((Z, 2))]
    hbm = pl.BlockSpec(memory_space=pl.ANY)
    vmem = pl.BlockSpec(memory_space=pltpu.VMEM)
    return pl.pallas_call(
        functools.partial(scatter_kernel, sizes),
        out_shape=[shape(*block) for block in [column.shape[1:] for column in columns] + parts],
        in_specs=[hbm] * 2 + [vmem] * 6 + [hbm],
        out_specs=[vmem] * 5,
        scratch_shapes=scratch,
        compiler_params=pltpu.CompilerParams(
            collective_id=collective_id, has_side_effects=True, vmem_limit_bytes=60 * 2**20
        ),
        name="scatter",
    )(*columns, *factors, by_place(small, sizes))


def gather_kernel(
    sizes, w_in_ref, w_out_ref, m_in_ref, m_out_ref, params_ref,
    all_ref, blocks_ref, gain_ref, taps_ref, heads_ref, inner_ref,
    mine, keep_sem, z_sems, near, far, across,
):
    p = Place(sizes)
    Z, h = p.Z, p.Z // 2
    greet_near(p, True, False)
    own = mine.shape[0]
    partner = p.at(c=1 - p.c)
    mine[:, :WIDE] = w_in_ref[:, :WIDE].astype(BF16)
    mine[:, WIDE : WIDE + INNER] = w_out_ref[...].astype(BF16)
    mine[:, WIDE + INNER :] = jnp.concatenate(
        [w_in_ref[:, WIDE:], jnp.zeros((own, 2 * HALF - IN_W - INNER), F32)], axis=1
    ).astype(BF16)
    keep = pltpu.make_async_copy(mine, all_ref.at[p.z, p.y, p.x, p.c], keep_sem)
    keep.start()
    await_near(p, True)

    def spot(z, y, x):
        return all_ref.at[z, y, x, p.c]

    def copy(src, dst, sem, device):
        return remote(src, dst, sem.at[0], sem.at[1], device)

    def along_z(z, right, src=None):
        here = spot(z, p.y, p.x)
        target = p.at(z=p.z + 1 if right else p.z - 1)
        return copy(here if src is None else src, here, z_sems.at[0 if right else 1, z], target)

    def near_copies(z, src=None):
        here = spot(z, p.y, p.x)
        src = here if src is None else src
        found = [copy(src, here, near.at[z, 0], p.at(y=1 - p.y))]
        for s in range(1, p.X):
            found.append(copy(src, here, near.at[z, s], p.at(x=p.other_x(s))))
        return found

    def near_arrivals(z):
        found = [(z, 1 - p.y, p.x, near.at[z, 0])]
        for s in range(1, p.X):
            found.append((z, p.y, lax.rem(p.x + p.X - s, p.X), near.at[z, s]))
        return found

    def far_copies(z):
        low, high = [], []
        for s in range(1, p.X):
            x = p.other_x(s)
            there = spot(z, p.y, x)
            low.append(copy(there, there, far.at[z, s], p.at(y=1 - p.y)))
            there = spot(z, 1 - p.y, p.x)
            high.append(copy(there, there, far.at[z, s], p.at(x=x)))
        return low, high

    def far_arrivals(z):
        low = [(z, 1 - p.y, p.other_x(s), far.at[z, s]) for s in range(1, p.X)]
        high = [
            (z, 1 - p.y, lax.rem(p.x + p.X - s, p.X), far.at[z, s]) for s in range(1, p.X)
        ]
        return low, high

    def to_partner(z, y, x, src=None):
        here = spot(z, y, x)
        return copy(here if src is None else src, here, across.at[z, y, x], partner)

    def await_block(z, y, x, sem):
        here = spot(z, y, x)
        copy(here, here, sem, partner).wait_recv()
        to_partner(z, y, x).start()

    def start_all(copies):
        for c in copies:
            c.start()

    @pl.when(p.z < Z - 1)
    def _():
        along_z(p.z, True, mine).start()

    @pl.when(p.z > 0)
    def _():
        along_z(p.z, False, mine).start()

    start_all(near_copies(p.z, mine))
    to_partner(p.z, p.y, p.x, mine).start()
    spread_vectors(params_ref, gain_ref, taps_ref, heads_ref, inner_ref)
    spread_moments(m_in_ref, m_out_ref, blocks_ref)

    def visit(right, z):
        await_block(z, p.y, p.x, z_sems.at[0 if right else 1, z])

        @pl.when(p.z < Z - 1 if right else p.z > 0)
        def _():
            along_z(z, right).start()

        start_all(near_copies(z))

    def by_distance(low, high):
        for j in range(1, Z):
            @pl.when(p.z - j >= 0)
            def _():
                low(p.z - j)

            @pl.when(p.z + j < Z)
            def _():
                high(p.z + j)

    by_distance(lambda z: visit(True, z), lambda z: visit(False, z))

    def relay(z):
        for block in near_arrivals(z):
            await_block(*block)
        low, high = far_copies(z)

        @pl.when(z < h)
        def _():
            start_all(low)

        @pl.when(z >= h)
        def _():
            start_all(high)

    relay(p.z)
    by_distance(relay, relay)

    def settle(z):
        low, high = far_arrivals(z)

        @pl.when(z < h)
        def _():
            for block in low:
                await_block(*block)

        @pl.when(z >= h)
        def _():
            for block in high:
                await_block(*block)

    settle(p.z)
    by_distance(settle, settle)
    keep.wait()

    def finish(z, carry):
        for c in near_copies(z):
            c.wait_send()
        low, high = far_copies(z)

        @pl.when(z < h)
        def _():
            for c in low:
                c.wait_send()

        @pl.when(z >= h)
        def _():
            for c in high:
                c.wait_send()

        @pl.when(jnp.logical_and(z <= p.z, p.z < Z - 1))
        def _():
            along_z(z, True).wait_send()

        @pl.when(jnp.logical_and(z >= p.z, p.z > 0))
        def _():
            along_z(z, False).wait_send()

        for y in range(p.Y):
            for x in range(p.X):
                to_partner(z, y, x).wait_send()
                theirs = all_ref.at[z, y, x, 1 - p.c]
                copy(theirs, theirs, across.at[z, y, x], partner).wait_recv()

        return carry

    lax.fori_loop(0, Z, finish, 0)


def column_of(row):
    return jnp.broadcast_to(row, (128, 128)).T


def spread_vectors(params_ref, gain_ref, taps_ref, heads_ref, inner_ref):
    row = D // 128
    gain_ref[...] = beside(*[params_ref[j : j + 1] for j in range(row)])
    for k in range(KCONV + 1):
        for j in range(CONVCH // 128):
            taps_ref[k, 128 * j : 128 * j + 128] = column_of(params_ref[row : row + 1])
            row += 1
    heads = column_of(params_ref[row : row + 1])
    heads_ref[0] = heads[:HEADS]
    heads_ref[1] = -jnp.exp(heads[HEADS : 2 * HEADS])
    heads_ref[2] = heads[2 * HEADS : 3 * HEADS]
    row = params_ref.shape[0] - INNER // 128
    for j in range(INNER // 128):
        inner_ref[128 * j : 128 * j + 128] = column_of(params_ref[row + j : row + j + 1])


def cuts_of(count):
    widths = [(0, INNER), (INNER, CONV_A), (INNER + CONV_A, CONVCH - CONV_A)]
    return [(start, width, width // count) for start, width in widths], INNER // count


def first_of(d, width, count):
    return d % 2 * (width // 2) + d // 2 * (width // count)


def spread_moments(m_in_ref, m_out_ref, blocks_ref):
    count, own, lanes_in_block = blocks_ref.shape
    ins, outs = cuts_of(count)
    step = m_in_ref[:, WIDE:]
    used = sum(each for _, _, each in ins) + outs + HEADS
    for d in range(count):
        pieces = []
        for start, width, each in ins:
            at = start + first_of(d, width, count)
            pieces.append(m_in_ref[:, at : at + each])
        at = first_of(d, INNER, count)
        pieces += [m_out_ref[:, at : at + outs], step]
        blocks_ref[d] = beside(*pieces, jnp.zeros((own, lanes_in_block - used), F32))


def gather_call(weight_in, weight_out, moment_in, moment_out, params, sizes, collective_id):
    Z, F = sizes
    X, Y = F // 4, 2
    own = weight_in.shape[0]
    count = Z * F
    gap = jnp.zeros((-params.shape[0] % 128,), F32)
    params = jnp.concatenate([params, gap, params[-INNER:]]).reshape(-1, 128)
    vmem = pl.BlockSpec(memory_space=pltpu.VMEM)
    hbm = pl.BlockSpec(memory_space=pl.ANY)
    whole_weights, blocks, *vectors = pl.pallas_call(
        functools.partial(gather_kernel, sizes),
        out_shape=[
            shape(Z, Y, X, 2, own, 2 * HALF, dtype=BF16), shape(count, own, 256), shape(1, D),
            shape(KCONV + 1, CONVCH, CHUNK), shape(3, HEADS, CHUNK), shape(INNER, CHUNK),
        ],
        in_specs=[vmem] * 5,
        out_specs=[hbm] + [vmem] * 5,
        scratch_shapes=[
            pltpu.VMEM((own, 2 * HALF), BF16), pltpu.SemaphoreType.DMA, pltpu.SemaphoreType.DMA((2, Z, 2)),
            pltpu.SemaphoreType.DMA((Z, X, 2)), pltpu.SemaphoreType.DMA((Z, X, 2)),
            pltpu.SemaphoreType.DMA((Z, Y, X, 2)),
        ],
        compiler_params=pltpu.CompilerParams(
            collective_id=collective_id, has_side_effects=True, vmem_limit_bytes=60 * 2**20
        ),
        name="weights_gather",
    )(weight_in, weight_out, moment_in, moment_out, params)
    return whole_weights.reshape(D, 2 * HALF), blocks, vectors


def gram_rows(slab, row):
    high, low = split(slab)
    left = above(high, low, high)[:, 128 * row : 128 * row + 128]
    return dot_tn(left, above(high, high, low)[:, 128 * row :])


def pack_gram(targets, slab):
    Z, Y, X, per, _ = targets[0].shape
    rows = above(*[
        beside(gram_rows(slab, i), gram_rows(slab, D // 128 - 1 - i)) for i in range(D // 256)
    ])
    if Z * Y * X * per > rows.shape[0]:
        rows = above(rows, jnp.zeros((Z * Y * X * per - rows.shape[0], rows.shape[1]), F32))
    at = 0
    for target in targets:
        cols = slice(at, at + target.shape[4])
        for i in range(Z * Y * X):
            target[i // (Y * X), i // X % Y, i % X] = rows[per * i : per * i + per, cols]
        at += target.shape[4]


def unpack_gram(gram, packed):
    Z, Y, X, _, _ = packed[0].shape
    rows = beside(*[
        above(*[part[i // (Y * X), i // X % Y, i % X] for i in range(Z * Y * X)])
        for part in packed
    ])
    for i in range(D // 256):
        pair = rows[128 * i : 128 * i + 128]
        wide_part, j = D - 128 * i, D // 128 - 1 - i
        for row, part in ((i, pair[:, :wide_part]), (j, pair[:, wide_part:])):
            gram[128 * row : 128 * row + 128, 128 * row :] = part
            for k in range(row + 1, D // 128):
                at = 128 * (k - row)
                gram[128 * k : 128 * k + 128, 128 * row : 128 * row + 128] = part[
                    :, at : at + 128
                ].T


BEHIND = 2


class AllSum:
    def __init__(self, place, work):
        self.p = place
        self.total, self.acc, self.core, self.core_sems = work[0], work[1], work[7], work[8]
        self.held, self.z_sems, self.back_sems = work[9:12]
        self.plane = Plane(place, *work[1:7])
        self.steps = [
            self.pair, self.second, self.cross, self.turn, self.spread, self.spread_on, self.done,
        ]

    def to_core(self):
        p = self.p
        return remote(
            self.total, self.core, self.core_sems.at[0], self.core_sems.at[1], p.at(c=1 - p.c)
        )

    def pair(self):
        p = self.p
        self.to_core().wait()

        def place_of(i):
            return i // (p.Y * p.X), lax.rem(i // p.X, p.Y), lax.rem(i, p.X)

        add_blocks(
            lambda i: self.acc.at[place_of(i)], lambda i: self.core.at[place_of(i)],
            p.Z * p.Y * p.X,
        )
        self.plane.start(0)

    def second(self):
        self.plane.finish(0)
        self.plane.start(1)

    def over(self, s):
        p = self.p
        z = lax.rem(p.z + s, p.Z)
        sem = self.z_sems.at[0, s]
        return remote(
            self.acc.at[z, p.y, p.x], self.held.at[s - 1], sem.at[0], sem.at[1], p.at(z=z)
        )

    def cross(self):
        self.plane.finish(1)
        for s in range(1, self.p.Z):
            self.over(s).start()

    def back(self, s, mine):
        p = self.p
        sem = self.z_sems.at[1, s]
        z = p.z if mine else lax.rem(p.z + p.Z - s, p.Z)
        ref = self.total.at[z, p.y, p.x]
        return remote(ref, ref, sem.at[0], sem.at[1], p.at(z=lax.rem(p.z + s, p.Z)))

    def turn(self):
        p = self.p
        for s in range(1, p.Z):
            self.over(s).wait()
        result = self.acc[p.z, p.y, p.x]
        for s in range(1, p.Z):
            result = result + self.held[s - 1]
        self.total[p.z, p.y, p.x] = result
        for s in range(1, p.Z):
            self.back(s, True).start()

    def planes(self, stage, mine):
        p, total, h = self.p, self.total, self.p.Z // 2
        low, high = pl.ds(0, h), pl.ds(h, p.Z - h)
        found = []
        for s in range(1, p.X):
            sem = self.back_sems.at[stage * p.X + s]
            x = p.x if mine else lax.rem(p.x + p.X - s, p.X)
            ref = total.at[high, p.y, x] if stage == 0 else total.at[low, :, x]
            found.append(remote(ref, ref, sem.at[0], sem.at[1], p.at(x=p.other_x(s))))
        sem = self.back_sems.at[stage * p.X]
        y = p.y if mine else 1 - p.y
        ref = total.at[low, y, p.x] if stage == 0 else total.at[high, y]
        found.append(remote(ref, ref, sem.at[0], sem.at[1], p.at(y=1 - p.y)))
        return found

    def arrive(self, copies):
        for mine, theirs in copies:
            mine.wait_send()
            theirs.wait_recv()

    def spread(self):
        self.arrive([(self.back(s, True), self.back(s, False)) for s in range(1, self.p.Z)])
        for copy in self.planes(0, True):
            copy.start()

    def spread_on(self):
        self.arrive(zip(self.planes(0, True), self.planes(0, False)))
        for copy in self.planes(1, True):
            copy.start()

    def done(self):
        self.arrive(zip(self.planes(1, True), self.planes(1, False)))


def all_sum_scratch(sizes, block):
    Z, X, Y = sizes[0], sizes[1] // 4, 2
    dma = pltpu.SemaphoreType.DMA
    return [pltpu.VMEM((Z, Y, X) + block, F32)] + plane_scratch(sizes, block) + [
        pltpu.VMEM((Z, Y, X) + block, F32), dma((2,)), pltpu.VMEM((Z - 1,) + block, F32),
        dma((2, Z, 2)), dma((2 * X, 2)),
    ]


def put_left(left, value, rows):
    high, low = split(value)
    left[rows] = beside(high, low, high)


def put_right(right, value, row):
    high, low = split(value)
    size = value.shape[0]
    right[row : row + size] = high
    right[D + row : D + row + size] = high
    right[2 * D + row : 2 * D + row + size] = low


TILE = 256


def symmetric_product(target, left, right):
    for i in range(D // TILE):
        rows = slice(TILE * i, TILE * i + TILE)
        part = dot(left[rows], right[:, TILE * i :])
        target[rows, TILE * i :] = part
        for j in range(i + 1, D // TILE):
            at = TILE * (j - i)
            target[TILE * j : TILE * j + TILE, rows] = part[:, at : at + TILE].T


def iterate(gram, square, factor, left, right, slab, slab_left):
    tiles = [slice(TILE * i, TILE * i + TILE) for i in range(D // TILE)]
    row = lax.broadcasted_iota(jnp.int32, (TILE, D), 0)
    col = lax.broadcasted_iota(jnp.int32, (TILE, D), 1)
    diagonals = [(row + TILE * i == col) for i in range(D // TILE)]
    trace = jnp.zeros((8, D), F32)
    for rows, diagonal in zip(tiles, diagonals):
        trace = trace + fold(jnp.where(diagonal, gram[rows], 0.0))
    trace = jnp.sum(jnp.sum(trace, axis=0, keepdims=True), axis=1, keepdims=True)
    scale = 1.0 / (jnp.sqrt(trace) + 1e-07)
    for rows in tiles:
        gram[rows] = gram[rows] * (scale * scale)
    slab[...] = slab[...] * scale

    def step(iteration, carry):
        for i, rows in enumerate(tiles):
            value = gram[rows]
            put_left(left, value, rows)
            put_right(right, value, TILE * i)
        symmetric_product(square, left, right)
        for i, rows in enumerate(tiles):
            value = COEF_B * gram[rows] + COEF_C * square[rows]
            put_right(right, value + jnp.where(diagonals[i], COEF_A, 0.0), TILE * i)
        put_left(slab_left, slab[...], slice(None))
        slab[...] = dot(slab_left[...], right[...])
        symmetric_product(factor, left, right)
        for rows in tiles:
            put_left(left, factor[rows], rows)
        symmetric_product(gram, left, right)
        return carry

    lax.fori_loop(0, ITERS - 1, step, 0)
    for i, rows in enumerate(tiles):
        put_right(right, gram[rows], TILE * i)
    first = slab[...]
    put_left(slab_left, first, slice(None))
    once = dot(slab_left[...], right[...])
    put_left(slab_left, once, slice(None))
    slab[...] = COEF_A * first + COEF_B * once + COEF_C * dot(slab_left[...], right[...])


def exact_pick(chosen, rows):
    high = rows.astype(BF16)
    rest = rows - high.astype(F32)
    mid = rest.astype(BF16)
    low = (rest - mid.astype(F32)).astype(BF16)
    return dot_nt(chosen, high) + dot_nt(chosen, mid) + dot_nt(chosen, low)


def update_kernel(
    sizes, gate_ref, conv_a_ref, conv_b_ref, out_ref, small_ref, old_ref, moved_ref, smalls_ref, spread_ref, step_ref,
    give, given, give_sems, messages, smalls, mats, left, right, slab, slab_left,
    swap_send, swap_recv, local, *work,
):
    p = Place(sizes)
    count = p.Z * p.F
    own = D // count
    gates = gate_ref.shape[0]
    ins = gates + conv_a_ref.shape[0] + conv_b_ref.shape[0]
    greet_all(p, False)
    swaps = [
        Swap(p, src, dst, swap_send.at[k], swap_recv.at[k], local.at[k], same, narrow)
        for k, (src, dst, same, narrow) in enumerate([
            (small_ref, smalls, True, None), (messages.at[0], moved_ref, False, None),
            (messages.at[1], spread_ref, False, -(-2 * gates // 128) * 128),
        ])
    ]
    old = old_ref[...].T
    new_in = above(gate_ref[...], conv_a_ref[...], conv_b_ref[...])
    new_out = out_ref[...]

    def push(gradient, moment):
        return gradient + MOMENTUM * (MOMENTUM * moment + gradient)

    push_in = push(new_in, old[:ins])
    push_out = above(push(new_out, old[ins : ins + gates]), jnp.zeros((ins - gates, D), F32))
    in_core = p.c == 0
    give[...] = jnp.where(in_core, push_out, push_in)
    slab[:ins] = jnp.where(in_core, push_in, push_out)
    partner = p.at(c=1 - p.c)
    pieces = [AllSum(p, work[:12]), AllSum(p, work[12:])]
    pack_gram([piece.total for piece in pieces], give[...])
    await_all(p)
    for piece in pieces:
        piece.to_core().start()
    exchange = remote(give, given, give_sems.at[0], give_sems.at[1], partner)
    exchange.start()
    swaps[0].start()
    pack_gram([piece.acc for piece in pieces], slab[:ins])

    def store_messages(k, turned):
        turned = beside(turned, jnp.zeros((D, 256 - turned.shape[1]), F32)) if (
            turned.shape[1] < 256) else turned
        for d in range(count):
            messages[k, d] = turned[own * d : own * d + own]

    steps = len(pieces[0].steps)
    for k in range(steps + BEHIND):
        for which, piece in enumerate(pieces):
            if 0 <= k - BEHIND * which < steps:
                piece.steps[k - BEHIND * which]()
        if k == 0:
            store_messages(0, above(new_in, new_out).T)
    exchange.wait()
    swaps[0].wait()
    swaps[1].start()
    smalls_ref[...] = smalls[...]
    rows = smalls[...].reshape(-1, 128)
    new_step = beside(*[rows[HEADS * j : HEADS * j + HEADS] for j in range(D // 128)])
    mine_at = lax.broadcasted_iota(jnp.int32, (own, D), 0) + own * (p.z * p.F + p.f)
    chosen = (lax.broadcasted_iota(jnp.int32, (own, D), 1) == mine_at).astype(F32).astype(BF16)
    step_ref[...] = exact_pick(chosen, new_step)
    push_step = push(new_step, old_ref[...].T[ins + gates : ins + gates + HEADS])
    push_step = jnp.where(in_core, push_step, 0.0)
    mine, theirs = slab[:ins], given[...]
    slab_in = above(mine, theirs, push_step)
    slab_out = above(theirs[:gates], mine[:gates], jnp.zeros((2 * (ins - gates) + HEADS, D), F32))
    slab[: 2 * ins + HEADS] = jnp.where(in_core, slab_in, slab_out)
    slab[2 * ins + HEADS :] = jnp.zeros((slab.shape[0] - 2 * ins - HEADS, D), F32)
    gram = mats.at[0]
    unpack_gram(gram, [piece.total for piece in pieces])
    step_high, step_low = split(push_step)
    step_left = above(step_high, step_low, step_high)
    gram[...] = gram[...] + dot_tn(step_left, above(step_high, step_high, step_low))
    iterate(gram, mats.at[1], mats.at[2], left, right, slab, slab_left)
    store_messages(1, slab[...].T)
    swaps[2].start()
    swaps[1].wait()
    swaps[2].wait()


def update_call(parts, small, old, sizes, collective_id):
    count = sizes[0] * sizes[1]
    own = D // count
    chips = count // 2
    ins = sum(part.shape[0] for part in parts[:3])
    per = -(-(D // 2) // (8 * chips)) * 8
    blocks = [(per, 512), (per, D + 128 - 512)]
    vmem = pl.BlockSpec(memory_space=pltpu.VMEM)
    hbm = pl.BlockSpec(memory_space=pl.ANY)
    dma = pltpu.SemaphoreType.DMA
    return pl.pallas_call(
        functools.partial(update_kernel, sizes),
        out_shape=[
            shape(count, own, 256), shape(count, *small.shape), shape(count, own, 256),
            shape(own, HEADS),
        ],
        in_specs=[vmem] * 6,
        out_specs=[hbm, vmem, hbm, vmem],
        scratch_shapes=[
            pltpu.VMEM((ins, D), F32), pltpu.VMEM((ins, D), F32), dma((2,)),
            pltpu.VMEM((2, count, own, 256), F32), pltpu.VMEM((count,) + small.shape, F32),
            pltpu.VMEM((3, D, D), F32),
            pltpu.VMEM((D, 3 * D), BF16), pltpu.VMEM((3 * D, D), BF16),
            pltpu.VMEM((256, D), F32), pltpu.VMEM((256, 3 * D), BF16),
            dma((3, count)), dma((3, count)), dma((3,)),
        ]
        + all_sum_scratch(sizes, blocks[0])
        + all_sum_scratch(sizes, blocks[1]),
        compiler_params=pltpu.CompilerParams(
            collective_id=collective_id, has_side_effects=True, vmem_limit_bytes=56 * 2**20
        ),
        name="update",
    )(*parts, small, old)


def finish_kernel(
    moved_ref, spread_ref, step_ref, w_in_ref, w_out_ref, m_in_ref, m_out_ref, dx_ref,
    g_in_ref, g_out_ref, new_m_in_ref, new_m_out_ref, new_w_in_ref, new_w_out_ref, dx_out_ref,
    held, sems,
):
    load = pltpu.make_async_copy(dx_ref, held, sems.at[0])
    store = pltpu.make_async_copy(held, dx_out_ref, sems.at[1])
    load.start()
    count = moved_ref.shape[0]
    cuts, outs = cuts_of(count)
    ins = sum(each for _, _, each in cuts)
    decay = 1.0 - MATRIX_RATE * WEIGHT_DECAY
    order = [(2 * chip + core, core) for core in range(2) for chip in range(count // 2)]
    at = 0
    for start, width, each in cuts:
        cols = slice(start, start + width)
        g_in_ref[:, cols] = beside(*[moved_ref[d, :, at : at + each] for d, _ in order])
        new_w_in_ref[:, cols] = beside(*[
            spread_ref[d - core, :, ins * core + at : ins * core + at + each] for d, core in order
        ])
        at += each
    load.wait()
    store.start()
    g_in_ref[:, WIDE:] = step_ref[...]
    new_w_in_ref[:, WIDE:] = spread_ref[0, :, 2 * ins : 2 * ins + HEADS]
    g_out_ref[...] = beside(*[moved_ref[d, :, ins : ins + outs] for d, _ in order])
    new_w_out_ref[...] = beside(*[
        spread_ref[d - core + 1, :, outs * core : outs * core + outs] for d, core in order
    ])
    for wide_side, g_ref, m_ref, w_ref, new_m_ref, new_w_ref in (
        (IN_W, g_in_ref, m_in_ref, w_in_ref, new_m_in_ref, new_w_in_ref),
        (INNER, g_out_ref, m_out_ref, w_out_ref, new_m_out_ref, new_w_out_ref),
    ):
        new_m_ref[...] = MOMENTUM * m_ref[...] + g_ref[...]
        rate = MATRIX_RATE * 0.2 * math.sqrt(max(D, wide_side))
        new_w_ref[...] = w_ref[...] * decay - rate * new_w_ref[...]
    store.wait()


def finish_call(moved, spread, step_rows, matrices, dx):
    vmem = pl.BlockSpec(memory_space=pltpu.VMEM)
    hbm = pl.BlockSpec(memory_space=pl.ANY)
    return pl.pallas_call(
        finish_kernel,
        out_shape=[shape(*matrix.shape) for matrix in matrices[:2]] * 3 + [shape(*dx.shape)],
        in_specs=[vmem] * 7 + [hbm],
        out_specs=[vmem] * 6 + [hbm],
        scratch_shapes=[pltpu.VMEM(dx.shape, F32), pltpu.SemaphoreType.DMA((2,))],
        compiler_params=pltpu.CompilerParams(vmem_limit_bytes=60 * 2**20),
        name="finish",
    )(moved, spread, step_rows, *matrices, dx)


def shards(
    inputs, cotangent, weight_in, weight_out, small_params, moment_in, moment_out, moment_small
):
    sizes = (lax.axis_size("dp"), lax.axis_size("fsdp"))
    weights, blocks, vectors = gather_call(
        weight_in, weight_out, moment_in, moment_out, small_params, sizes, 0
    )
    output, dx, columns, factors, small, old = block_and_gradients(
        inputs[0], cotangent[0], weights, vectors, blocks, sizes, (3, 4)
    )
    new_out, new_gate, new_conv_a, new_conv_b, new_small = scatter_call(
        columns, factors, small, sizes, 1
    )
    moved, smalls, spread, step_rows = update_call(
        (new_gate, new_conv_a, new_conv_b, new_out), new_small, old.reshape(D, 256), sizes, 2
    )
    smalls = smalls.reshape(-1)
    grad_small = smalls[HEADS * D : HEADS * D + SMALL]
    grad_in, grad_out, new_moment_in, new_moment_out, new_weight_in, new_weight_out, dx = (
        finish_call(
            moved, spread, step_rows, (weight_in, weight_out, moment_in, moment_out), dx
        )
    )
    new_moment_small = MOMENTUM * moment_small + grad_small
    new_small_params = small_params - SMALL_RATE * new_moment_small
    return (
        output[None],
        dx[None],
        grad_in,
        grad_out,
        grad_small,
        new_moment_in,
        new_moment_out,
        new_moment_small,
        new_weight_in,
        new_weight_out,
        new_small_params,
    )


def solution(mesh):
    return jax.shard_map(
        shards,
        mesh=mesh,
        in_specs=(
            P(("dp", "fsdp"), None, None),
            P(("dp", "fsdp"), None, None),
            P(("dp", "fsdp"), None),
            P(("dp", "fsdp"), None),
            P(),
            P(("dp", "fsdp"), None),
            P(("dp", "fsdp"), None),
            P(),
        ),
        out_specs=(
            P(("dp", "fsdp"), None, None),
            P(("dp", "fsdp"), None, None),
            P(("dp", "fsdp"), None),
            P(("dp", "fsdp"), None),
            P(),
            P(("dp", "fsdp"), None),
            P(("dp", "fsdp"), None),
            P(),
            P(("dp", "fsdp"), None),
            P(("dp", "fsdp"), None),
            P(),
        ),
        check_vma=False,
    )
```
